128 devices in a mesh: batch: 4 (over y), seq: 32 (over z, x, core).
Axes of the slice: x: 4, y: 4, z: 4, core: 2. Of those that a mesh axis runs over, the one named last changes fastest.
Arguments:
- tokens: bfloat16 [2, 4, 8192, 640], P(None, 'batch', 'seq'), may hold values from -6 to 6
- lengths: int32 [2, 4, 64], P(None, 'batch'), may hold values from 1 to 1024, 8192 in all within a row
- gain_one: bfloat16 [640], P('batch'), may hold values from 0.5 to 1.5
- bias_one: bfloat16 [640], P('batch'), may hold values from -3 to 3
- w_qkv: bfloat16 [640, 1920], P('batch'), may hold values from -0.25 to 0.25
- w_out: bfloat16 [640, 640], P('batch'), may hold values from -1 to 1
- gain_two: bfloat16 [640], P('batch'), may hold values from 0.5 to 1.5
- bias_two: bfloat16 [640], P('batch'), may hold values from -3 to 3
- w_up: bfloat16 [640, 5120], P('batch'), may hold values from -0.25 to 0.25
- w_down: bfloat16 [5120, 640], P('batch'), may hold values from -0.078125 to 0.078125
- cotangent: bfloat16 [2, 4, 8192, 640], P(None, 'batch', 'seq'), may hold values from -6 to 6
Outputs:
- block_out: bfloat16 [2, 4, 8192, 640], P(None, 'batch', 'seq')
- grad_tokens: bfloat16 [2, 4, 8192, 640], P(None, 'batch', 'seq')
- grad_gain_one: float32 [640], P('batch')
- grad_bias_one: float32 [640], P('batch')
- grad_qkv: float32 [640, 1920], P('batch')
- grad_out_proj: float32 [640, 640], P('batch')
- grad_gain_two: float32 [640], P('batch')
- grad_bias_two: float32 [640], P('batch')
- grad_up: float32 [640, 5120], P('batch')
- grad_down: float32 [5120, 640], P('batch')
The draws below stay inside these ranges and needn't reach their ends.
Inputs may be any that keep to these rules, and one draw needn't show every extreme that they name: Each stream's row of 64 lengths sums to 8192; the largest in each row is 1024.
All inputs are finite; a program needn't handle non-finite values.
Results may differ from the reference program's by a relative error of at most 0.029.
Values may be sent and summed in bfloat16 or wider, within the bound.
No kernel may reach another device: no remote copies, remote signals or barrier semaphores. Data moves between devices by JAX's collectives and lax.ppermute only.
A program may use at most 192 MiB of HBM per device.

```python
import math
import jax
import jax.numpy as jnp
import numpy as np
from jax import lax

D = 640
HEADS = 20
HEAD_DIM = 32
FF = 5120
MAXLEN = 1024
MICRO = 2
SLEN = 8192
NSEG = 64
STREAMS = 4
N_BATCH = 4


def steps_of(key, shape, cuts, low, high):
    factor_of, own = 1.0, jax.random.fold_in(key, 6)
    for axis_at, blocks in cuts:
        steps = jnp.exp(jax.random.uniform(jax.random.fold_in(own, axis_at), (blocks,), jnp.float32, low / len(cuts), high / len(cuts)))
        factor_of = factor_of * jnp.repeat(steps, shape[axis_at] // blocks).reshape([-1 if axis == axis_at else 1 for axis in range(len(shape))])
    return factor_of


def profile(count, total, reach, skew):
    portions = [(1 << 20) // math.isqrt(grade ** skew) + 1 for grade in range(2, count + 1)]
    spare, given = total - reach - (count - 1), [1] * (count - 1)
    while spare > 0:
        free = [i for i in range(count - 1) if given[i] < reach]
        mass, left = sum([portions[i] for i in free]), spare
        for i in free:
            more = min(reach - given[i], max(1, left * portions[i] // mass), spare)
            given[i] = given[i] + more
            spare = spare - more
    return np.array([reach] + given)


def uneven_parts(key, count, total, reach, lean):
    if count == 2:
        one = jax.random.randint(key, (), max(1, total - reach), min(reach, total - 1) + 1)
        return jnp.stack([one, total - one])
    tallies = jnp.asarray(profile(count, total, reach, lean), jnp.int32)
    pairs = (count - 1) // 2
    source_of, taker = tallies[1:1 + 2 * pairs:2], tallies[2:2 + 2 * pairs:2]
    room = jnp.minimum(source_of - 1, reach - taker)
    moved = jax.random.randint(jax.random.fold_in(key, 1), (pairs,), 0, 1 << 20) % (room + 1)
    tallies = tallies.at[1:1 + 2 * pairs:2].set(source_of - moved).at[2:2 + 2 * pairs:2].set(taker + moved)
    return tallies[jax.random.permutation(jax.random.fold_in(key, 2), count)]


def gaussian(stream_key, dims, deviation, reach, split=(), kind=jnp.bfloat16):
    level = steps_of(stream_key, dims, split, -0.22, 0.18) if split else 1.0
    values = jax.random.normal(stream_key, dims, jnp.float32) * deviation * level
    return jnp.minimum(jnp.maximum(values, -reach), reach).astype(kind)


def setup_inputs(seed: int = 0) -> dict:
    key_list = jax.random.split(jax.random.key(seed), 12)
    return {
        "tokens": gaussian(key_list[0], (MICRO, STREAMS, SLEN, D), 1.0, 6.0, ((1, 4), (2, 32))),
        "lengths": jax.vmap(lambda own: uneven_parts(own, NSEG, SLEN, MAXLEN, 2))(jax.random.split(key_list[1], MICRO * STREAMS)).reshape((MICRO, STREAMS, NSEG)).astype(jnp.int32),
        "gain_one": jnp.clip(1.0 + 0.1 * jax.random.normal(key_list[2], (D,), jnp.float32), 0.5, 1.5).astype(jnp.bfloat16),
        "bias_one": gaussian(key_list[3], (D,), 0.5, 3.0, ((0, 4),)),
        "w_qkv": gaussian(key_list[4], (D, 3 * D), D ** -0.5, 0.25, ((0, 4),)),
        "w_out": gaussian(key_list[5], (D, D), (D // 16) ** -0.5, 1.0, ((0, 4),)),
        "gain_two": jnp.clip(1.0 + 0.1 * jax.random.normal(key_list[6], (D,), jnp.float32), 0.5, 1.5).astype(jnp.bfloat16),
        "bias_two": gaussian(key_list[7], (D,), 0.5, 3.0, ((0, 4),)),
        "w_up": gaussian(key_list[8], (D, FF), D ** -0.5, 0.25, ((0, 4),)),
        "w_down": gaussian(key_list[9], (FF, D), FF ** -0.5, 0.078125, ((0, 4),)),
        "cotangent": gaussian(key_list[10], (MICRO, STREAMS, SLEN, D), 1.0, 6.0, ((1, 4), (2, 32))),
    }


@jax.custom_vjp
def low(v):
    return lax.optimization_barrier(v.astype(jnp.bfloat16)).astype(jnp.float32)

@jax.custom_vjp
def low_back(v):
    return v

def low_keep(v):
    return (low(v), None)

def low_pass(kept, grad):
    return (grad,)

def back_keep(v):
    return (v, None)

def back_low(kept, grad):
    return (low(grad),)
low.defvjp(low_keep, low_pass)
low_back.defvjp(back_keep, back_low)
highest_precision = lax.Precision.HIGHEST
epsilon = 1e-05

def matmul(left, right):
    return jnp.matmul(left, right, precision=highest_precision)

def normalize(vector, gain, shift):
    average = lax.optimization_barrier(jnp.mean(vector, axis=-1, keepdims=True))
    centred = vector - average
    spread = lax.optimization_barrier(jnp.mean(centred * centred, axis=-1, keepdims=True))
    return centred * lax.rsqrt(spread + epsilon) * gain + shift

def segment_ids(length_row):
    boundaries = jnp.cumsum(length_row).astype(jnp.int32)
    places = jnp.arange(SLEN, dtype=jnp.int32)
    return lax.optimization_barrier(jnp.sum((places[:, None] >= boundaries[None, :]).astype(jnp.int32), axis=1)).astype(jnp.int32)

def stream_forward(inputs, segments, params):
    gain_one, bias_one, w_qkv, w_out, gain_two, bias_two, w_up, w_down = params
    hidden_one = low(normalize(inputs, gain_one, bias_one))
    projected = low_back(low(matmul(hidden_one, w_qkv)))
    queries = projected[:, :D].reshape(SLEN, HEADS, HEAD_DIM)
    keys = projected[:, D:2 * D].reshape(SLEN, HEADS, HEAD_DIM)
    values = projected[:, 2 * D:].reshape(SLEN, HEADS, HEAD_DIM)
    pad_keys = jnp.pad(keys, ((MAXLEN, MAXLEN), (0, 0), (0, 0)))
    pad_values = jnp.pad(values, ((MAXLEN, MAXLEN), (0, 0), (0, 0)))
    pad_segments = jnp.pad(segments, (MAXLEN, MAXLEN), constant_values=-1)
    block_rows = min(512, SLEN)
    window_rows = block_rows + 2 * MAXLEN
    score_scale = HEAD_DIM ** (-0.5)

    def attend(number):
        first_row = number * block_rows
        query_block = lax.dynamic_slice_in_dim(queries, first_row, block_rows, 0)
        key_block = lax.dynamic_slice_in_dim(pad_keys, first_row, window_rows, 0)
        value_block = lax.dynamic_slice_in_dim(pad_values, first_row, window_rows, 0)
        own_segment = lax.dynamic_slice_in_dim(segments, first_row, block_rows, 0)
        near_segment = lax.dynamic_slice_in_dim(pad_segments, first_row, window_rows, 0)
        allowed = own_segment[:, None] == near_segment[None, :]
        scores = low_back(jnp.einsum('qhd,khd->hqk', query_block, key_block, precision=highest_precision) * score_scale)
        scores = jnp.where(allowed[None], scores, -1e+30)
        largest = lax.optimization_barrier(jnp.max(scores, axis=-1, keepdims=True))
        raised = jnp.exp(scores - largest)
        attn_weights = raised / lax.optimization_barrier(jnp.sum(raised, axis=-1, keepdims=True))
        return jnp.einsum('hqk,khd->qhd', low(attn_weights), value_block, precision=highest_precision)
    attended = lax.map(jax.checkpoint(attend), jnp.arange(SLEN // block_rows, dtype=jnp.int32))
    attended = low_back(low(attended.reshape(SLEN, D)))
    middle = inputs + low_back(matmul(attended, w_out))
    hidden_two = low(normalize(middle, gain_two, bias_two))
    upward = low_back(matmul(hidden_two, w_up))
    activated = low(jax.nn.gelu(upward, approximate=False))
    return middle + matmul(activated, w_down)

def reference(tokens, lengths, gain_one, bias_one, w_qkv, w_out, gain_two, bias_two, w_up, w_down, cotangent):
    streams_all = MICRO * N_BATCH
    flattened = tokens.astype(jnp.float32).reshape(streams_all, SLEN, D)
    segments = jax.vmap(segment_ids)(lengths.reshape(streams_all, NSEG))
    params = tuple((matrix.astype(jnp.float32) for matrix in (gain_one, bias_one, w_qkv, w_out, gain_two, bias_two, w_up, w_down)))

    def forward(flat_in, weights):

        def per_stream(stream_pair):
            return stream_forward(stream_pair[0], stream_pair[1], weights)
        return lax.map(jax.checkpoint(per_stream), (flat_in, segments))
    result, pullback = jax.vjp(forward, flattened, params)
    grad_flat, gradients = pullback(cotangent.astype(jnp.float32).reshape(streams_all, SLEN, D))
    return (result.astype(jnp.bfloat16).reshape(tokens.shape), grad_flat.astype(jnp.bfloat16).reshape(tokens.shape), gradients[0], gradients[1], gradients[2], gradients[3], gradients[4], gradients[5], gradients[6], gradients[7])
```

```python
import math

import jax
import jax.numpy as jnp
from jax import lax
from jax.experimental import pallas as pl
from jax.experimental.pallas import tpu as pltpu
from jax.sharding import Mesh
from jax.sharding import PartitionSpec as P

HEAD_DIM = 32
SCALE = HEAD_DIM ** -0.5
LOG2E = math.log2(math.e)
C2 = SCALE * LOG2E
BIG = 1e30
TILE = 256
EPSILON = 1e-05
PAIRS = 5
SHORT, LONG = 640, 1152
f32, bf16 = jnp.float32, jnp.bfloat16


def pair_offset(info_ref):
    p = pl.program_id(0)
    sub = jnp.where(p == PAIRS - 1, info_ref[0], lax.rem(p, 2))
    return sub * (2 * HEAD_DIM)


def split3(v):
    a = v.astype(bf16)
    r = v - a.astype(f32)
    b = r.astype(bf16)
    d = (r - b.astype(f32)).astype(bf16)
    return a, b, d


def rows_masked(xT, off):
    row = lax.broadcasted_iota(jnp.int32, xT.shape, 0) - off
    xf = xT.astype(f32)
    return [jnp.where((row >= HEAD_DIM * j) & (row < HEAD_DIM * (j + 1)), xf, 0.0).astype(bf16) for j in range(2)]


def lanes_masked(x, off):
    lane = lax.broadcasted_iota(jnp.int32, x.shape, 1) - off
    xf = x.astype(f32)
    return [jnp.where((lane >= HEAD_DIM * j) & (lane < HEAD_DIM * (j + 1)), xf, 0.0).astype(bf16) for j in range(2)]


def attend_kernel(info_ref, qT_ref, k_ref, vT_ref, kaug_ref, qaugT_ref, oT_ref, o_ref, l_ref, rhs):
    off = pair_offset(info_ref)
    oT_ref[...] = jnp.where(lax.rem(pl.program_id(0), 2) == 0, 0.0, oT_ref[...])
    for t in range(2):
        cols = slice(t * TILE, (t + 1) * TILE)
        masked = rows_masked(qT_ref[:, cols], off)
        for j in range(2):
            rhs[0:128, j * TILE:(j + 1) * TILE] = masked[j]
            rhs[128:256, j * TILE:(j + 1) * TILE] = qaugT_ref[:, cols]
        start = info_ref[1 + t]
        need = info_ref[3 + t]

        def block(size):
            def step(i, carry):
                row = pl.multiple_of(start + i * size, 128)
                lhs = jnp.concatenate([k_ref[pl.ds(row, size), :], kaug_ref[pl.ds(row, size), :]], axis=1)
                raw = [jnp.dot(lhs, rhs[:, j * TILE:(j + 1) * TILE], preferred_element_type=f32) for j in range(2)]
                out = []
                for j in range(2):
                    m, l, o = carry[j]
                    s = raw[j] * C2
                    m_new = jnp.maximum(m, jnp.max(s, axis=0, keepdims=True))
                    alpha = jnp.exp2(m - m_new)
                    p = jnp.exp2(s - m_new)
                    vT = vT_ref[pl.ds(pl.multiple_of(off + j * HEAD_DIM, HEAD_DIM), HEAD_DIM), pl.ds(row, size)]
                    out.append((m_new, l * alpha + jnp.sum(p, axis=0, keepdims=True),
                                o * alpha + jnp.dot(vT, p.astype(bf16), preferred_element_type=f32)))
                return tuple(out)
            return step

        def finish(state):
            for j in range(2):
                m, l, o = state[j]
                oT_ref[pl.ds(pl.multiple_of(off + j * HEAD_DIM, HEAD_DIM), HEAD_DIM), cols] = o * (1.0 / l)
                l_ref[0, j:j + 1, cols] = m + jnp.log2(l)

        init = tuple((jnp.full((1, TILE), -1e38, f32), jnp.zeros((1, TILE), f32), jnp.zeros((HEAD_DIM, TILE), f32)) for _ in range(2))

        @pl.when(need <= SHORT)
        def _():
            finish(block(SHORT)(0, init))

        @pl.when(need > SHORT)
        def _():
            finish(lax.fori_loop(0, lax.div(need + (LONG - 1), LONG), block(LONG), init))

    o_ref[...] = oT_ref[...].T.astype(bf16)


def attend(info, qT, k, vT, kaug, qaugT):
    win = k.shape[0]
    nq = qT.shape[1]
    group = lambda p, *_: p // 2
    return pl.pallas_call(
        attend_kernel,
        out_shape=(jax.ShapeDtypeStruct((384, nq), f32), jax.ShapeDtypeStruct((nq, 384), bf16), jax.ShapeDtypeStruct((PAIRS, 8, nq), f32)),
        grid_spec=pltpu.PrefetchScalarGridSpec(
            num_scalar_prefetch=1, grid=(PAIRS,),
            in_specs=[
                pl.BlockSpec((128, nq), lambda p, *_: (p // 2, 0)),
                pl.BlockSpec((win, 128), lambda p, *_: (0, p // 2)),
                pl.BlockSpec((128, win), lambda p, *_: (p // 2, 0)),
                pl.BlockSpec((win, 128), lambda p, *_: (0, 0)),
                pl.BlockSpec((128, nq), lambda p, *_: (0, 0)),
            ],
            out_specs=[
                pl.BlockSpec((128, nq), lambda p, *_: (p // 2, 0)),
                pl.BlockSpec((nq, 128), lambda p, *_: (0, p // 2)),
                pl.BlockSpec((1, 8, nq), lambda p, *_: (p, 0, 0)),
            ],
            scratch_shapes=[pltpu.VMEM((256, 2 * TILE), bf16)],
        ),
        compiler_params=pltpu.CompilerParams(vmem_limit_bytes=48 << 20),
        cost_estimate=pl.CostEstimate(flops=20 * 10**9, bytes_accessed=6 << 20, transcendentals=5 * 10**6),
        name="attend",
    )(info, qT, k, vT, kaug, qaugT)


def attend_back_kernel(info_ref, qT_ref, q_ref, k_ref, kT_ref, v_ref, doT_ref, do_ref, oT_ref, l_ref, kaug_ref, qaugT_ref,
                       dq_ref, dk_ref, dv_ref, dqT_ref, rhs_s, rhs_d, q_stk, do_stk, dk_acc, dv_acc):
    p_id = pl.program_id(0)
    off = pair_offset(info_ref)

    @pl.when(lax.rem(p_id, 2) == 0)
    def _():
        dqT_ref[...] = jnp.zeros_like(dqT_ref)
        dk_acc[...] = jnp.zeros_like(dk_acc)
        dv_acc[...] = jnp.zeros_like(dv_acc)

    for t in range(2):
        cols = slice(t * TILE, (t + 1) * TILE)
        masked_q = rows_masked(qT_ref[:, cols], off)
        masked_do = rows_masked(doT_ref[:, cols], off)
        lane_q = lanes_masked(q_ref[cols, :], off)
        lane_do = lanes_masked(do_ref[cols, :], off)
        for j in range(2):
            part = slice(j * TILE, (j + 1) * TILE)
            head = pl.ds(pl.multiple_of(off + j * HEAD_DIM, HEAD_DIM), HEAD_DIM)
            delta = jnp.sum(doT_ref[head, cols].astype(f32) * oT_ref[head, cols], axis=0, keepdims=True)
            total = l_ref[0, j:j + 1, cols] * (1.0 / C2)
            rowid = lax.broadcasted_iota(jnp.int32, (64, TILE), 0)
            lp, dp = split3(-total), split3(-delta)
            def pieces(parts):
                x = jnp.zeros((64, TILE), f32)
                for n in range(3):
                    x = jnp.where(rowid == n, parts[n].astype(f32), x)
                return x.astype(bf16)
            rhs_s[0:128, part] = masked_q[j]
            rhs_s[128:192, part] = qaugT_ref[0:64, cols]
            rhs_s[192:256, part] = pieces(lp)
            rhs_d[0:128, part] = masked_do[j]
            rhs_d[128:192, part] = jnp.zeros((64, TILE), bf16)
            rhs_d[192:256, part] = pieces(dp)
            q_stk[part, :] = lane_q[j]
            do_stk[part, :] = lane_do[j]
        start = info_ref[1 + t]
        need = info_ref[3 + t]

        def block(size):
            def step(i, carry):
                row = pl.multiple_of(start + i * size, 128)
                rows = pl.ds(row, size)
                aug = kaug_ref[rows, :]
                lhs_k = jnp.concatenate([k_ref[rows, :], aug], axis=1)
                lhs_v = jnp.concatenate([v_ref[rows, :], aug], axis=1)
                out, dv, dk = [], dv_acc[rows, :], dk_acc[rows, :]
                for j in range(2):
                    part = slice(j * TILE, (j + 1) * TILE)
                    s = jnp.dot(lhs_k, rhs_s[:, part], preferred_element_type=f32)
                    dp = jnp.dot(lhs_v, rhs_d[:, part], preferred_element_type=f32)
                    p = jnp.exp2(s * C2)
                    ds = (p * dp).astype(bf16)
                    dv = dv + jnp.dot(p.astype(bf16), do_stk[part, :], preferred_element_type=f32)
                    dk = dk + jnp.dot(ds, q_stk[part, :], preferred_element_type=f32)
                    kT = kT_ref[pl.ds(pl.multiple_of(off + j * HEAD_DIM, HEAD_DIM), HEAD_DIM), rows]
                    out.append(carry[j] + jnp.dot(kT, ds, preferred_element_type=f32))
                dv_acc[rows, :] = dv
                dk_acc[rows, :] = dk
                return tuple(out)
            return step

        def finish(dqs):
            for j in range(2):
                dqT_ref[pl.ds(pl.multiple_of(off + j * HEAD_DIM, HEAD_DIM), HEAD_DIM), cols] = dqs[j] * SCALE

        init = tuple(jnp.zeros((HEAD_DIM, TILE), f32) for _ in range(2))

        @pl.when(need <= SHORT)
        def _():
            finish(block(SHORT)(0, init))

        @pl.when(need > SHORT)
        def _():
            finish(lax.fori_loop(0, lax.div(need + (LONG - 1), LONG), block(LONG), init))
    @pl.when((lax.rem(p_id, 2) == 1) | (p_id == PAIRS - 1))
    def _():
        dq_ref[...] = dqT_ref[...].T.astype(bf16)
        dk_ref[...] = (dk_acc[...] * SCALE).astype(bf16)
        dv_ref[...] = dv_acc[...].astype(bf16)


def attend_back(info, qT, q, k, kT, v, doT, do, oT, lse, kaug, qaugT):
    win, nq = k.shape[0], qT.shape[1]
    wide = pl.BlockSpec((128, nq), lambda p, *_: (p // 2, 0))
    tall = pl.BlockSpec((nq, 128), lambda p, *_: (0, p // 2))
    keys = pl.BlockSpec((win, 128), lambda p, *_: (0, p // 2))
    return pl.pallas_call(
        attend_back_kernel,
        out_shape=(jax.ShapeDtypeStruct((nq, 384), bf16), jax.ShapeDtypeStruct((win, 384), bf16), jax.ShapeDtypeStruct((win, 384), bf16)),
        grid_spec=pltpu.PrefetchScalarGridSpec(
            num_scalar_prefetch=1, grid=(PAIRS,),
            in_specs=[wide, tall, keys, pl.BlockSpec((128, win), lambda p, *_: (p // 2, 0)), keys, wide, tall, wide,
                      pl.BlockSpec((1, 8, nq), lambda p, *_: (p, 0, 0)),
                      pl.BlockSpec((win, 128), lambda p, *_: (0, 0)), pl.BlockSpec((128, nq), lambda p, *_: (0, 0))],
            out_specs=[tall, keys, keys],
            scratch_shapes=[pltpu.VMEM((128, nq), f32), pltpu.VMEM((256, 2 * TILE), bf16), pltpu.VMEM((256, 2 * TILE), bf16),
                            pltpu.VMEM((2 * TILE, 128), bf16), pltpu.VMEM((2 * TILE, 128), bf16),
                            pltpu.VMEM((win, 128), f32), pltpu.VMEM((win, 128), f32)],
        ),
        compiler_params=pltpu.CompilerParams(vmem_limit_bytes=48 << 20),
        cost_estimate=pl.CostEstimate(flops=40 * 10**9, bytes_accessed=12 << 20, transcendentals=5 * 10**6),
        name="attend_back",
    )(info, qT, q, k, kT, v, doT, do, oT, lse, kaug, qaugT)


def qkv_kernel(core_ref, own_ref, other_ref, gain_ref, bias_ref, w_ref, k_ref, v_ref, kT_ref, vT_ref, q_ref, qT_ref, hid_ref):
    block = pl.program_id(0)
    mine = lax.rem(block, 2) == core_ref[0]
    x = jnp.where(mine, own_ref[0].astype(f32), other_ref[0].astype(f32))
    centred = x - jnp.mean(x, axis=-1, keepdims=True)
    spread = jnp.mean(centred * centred, axis=-1, keepdims=True)
    hidden = (centred * lax.rsqrt(spread + EPSILON) * gain_ref[...] + bias_ref[...]).astype(bf16)
    kv = jnp.dot(hidden, w_ref[:, 384:], preferred_element_type=f32).astype(bf16)
    k_ref[...] = kv[:, :384]
    v_ref[...] = kv[:, 384:]
    kvT = kv.astype(f32).T.astype(bf16)
    kT_ref[...] = kvT[:384]
    vT_ref[...] = kvT[384:]

    @pl.when((block == 4) | (block == 5))
    def _():
        q = jnp.dot(hidden, w_ref[:, :384], preferred_element_type=f32).astype(bf16)
        q_ref[...] = q
        qT_ref[...] = q.astype(f32).T.astype(bf16)
        hid_ref[...] = hidden


def project(core, own, other, gain, bias, w):
    rows = 256
    blocks = 2 * own.shape[0]
    win, nq = blocks * rows, 2 * rows
    centre = lambda b: jnp.clip(b - 4, 0, 1)
    return pl.pallas_call(
        qkv_kernel,
        out_shape=(
            jax.ShapeDtypeStruct((win, 384), bf16), jax.ShapeDtypeStruct((win, 384), bf16),
            jax.ShapeDtypeStruct((384, win), bf16), jax.ShapeDtypeStruct((384, win), bf16),
            jax.ShapeDtypeStruct((nq, 384), bf16), jax.ShapeDtypeStruct((384, nq), bf16),
            jax.ShapeDtypeStruct((nq, 640), bf16)),
        grid_spec=pltpu.PrefetchScalarGridSpec(
            num_scalar_prefetch=1, grid=(blocks,),
            in_specs=[
                pl.BlockSpec((1, rows, 640), lambda b, *_: (b // 2, 0, 0)),
                pl.BlockSpec((1, rows, 640), lambda b, *_: (b // 2, 0, 0)),
                pl.BlockSpec((1, 640), lambda b, *_: (0, 0)),
                pl.BlockSpec((1, 640), lambda b, *_: (0, 0)),
                pl.BlockSpec((640, 1152), lambda b, *_: (0, 0)),
            ],
            out_specs=[
                pl.BlockSpec((rows, 384), lambda b, *_: (b, 0)),
                pl.BlockSpec((rows, 384), lambda b, *_: (b, 0)),
                pl.BlockSpec((384, rows), lambda b, *_: (0, b)),
                pl.BlockSpec((384, rows), lambda b, *_: (0, b)),
                pl.BlockSpec((rows, 384), lambda b, *_: (centre(b), 0)),
                pl.BlockSpec((384, rows), lambda b, *_: (0, centre(b))),
                pl.BlockSpec((rows, 640), lambda b, *_: (centre(b), 0)),
            ],
        ),
        compiler_params=pltpu.CompilerParams(vmem_limit_bytes=48 << 20),
        cost_estimate=pl.CostEstimate(flops=5 * 10**9, bytes_accessed=12 << 20, transcendentals=10**4),
        name="project",
    )(core, own, other, gain, bias, w)


def feed_kernel(h_ref, cot_ref, up_ref, down_ref, out_ref, dh_ref, g_up_ref, g_down_ref, hT, cT):
    chunk = pl.program_id(0)

    @pl.when(chunk == 0)
    def _():
        hT[...] = h_ref[...].astype(f32).T.astype(bf16)
        cT[...] = cot_ref[...].astype(f32).T.astype(bf16)
        out_ref[...] = jnp.zeros_like(out_ref)
        dh_ref[...] = jnp.zeros_like(dh_ref)

    nt = (((1,), (1,)), ((), ()))
    h, cot = h_ref[...], cot_ref[...]
    up_w, down_w = up_ref[...], down_ref[...]
    u = jnp.dot(h, up_w, preferred_element_type=f32)
    d_act = lax.dot_general(cot, down_w, nt, preferred_element_type=f32)
    cdf = 0.5 * (1.0 + lax.erf(u * (2.0 ** -0.5)))
    pdf = jnp.exp(u * u * -0.5) * ((2.0 * math.pi) ** -0.5)
    act = (u * cdf).astype(bf16)
    d_up = (d_act * (cdf + u * pdf)).astype(bf16)
    out_ref[...] += jnp.dot(act, down_w, preferred_element_type=f32)
    dh_ref[...] += lax.dot_general(d_up, up_w, nt, preferred_element_type=f32)
    g_up = jnp.dot(hT[...], d_up, preferred_element_type=f32).astype(bf16)
    for y in range(4):
        g_up_ref[y] = g_up[160 * y:160 * (y + 1)]
    g_down_ref[0] = jnp.dot(cT[...], act, preferred_element_type=f32).T.astype(bf16)


def feed_forward(h, cot, up, down):
    rows, chunks, wide = h.shape[0], 4, up.shape[1] // 4
    whole = pl.BlockSpec((rows, 640), lambda f: (0, 0))
    return pl.pallas_call(
        feed_kernel,
        out_shape=(
            jax.ShapeDtypeStruct((rows, 640), f32), jax.ShapeDtypeStruct((rows, 640), f32),
            jax.ShapeDtypeStruct((4, 160 * chunks, wide), bf16), jax.ShapeDtypeStruct((4, wide, 640), bf16)),
        grid=(chunks,),
        in_specs=[whole, whole, pl.BlockSpec((640, wide), lambda f: (0, f)), pl.BlockSpec((wide, 640), lambda f: (f, 0))],
        out_specs=[whole, whole, pl.BlockSpec((4, 160, wide), lambda f: (0, f, 0)), pl.BlockSpec((1, wide, 640), lambda f: (f, 0, 0))],
        scratch_shapes=[pltpu.VMEM((640, rows), bf16), pltpu.VMEM((640, rows), bf16)],
        compiler_params=pltpu.CompilerParams(vmem_limit_bytes=56 << 20),
        cost_estimate=pl.CostEstimate(flops=20 * 10**9, bytes_accessed=30 << 20, transcendentals=5 * 10**6),
        name="feed_forward",
    )(h, cot, up, down)


def moments(x):
    centred = x - jnp.mean(x, axis=-1, keepdims=True)
    r = lax.rsqrt(jnp.mean(centred * centred, axis=-1, keepdims=True) + EPSILON)
    return centred * r, r


def norm_back(grad, n, r, gain):
    e = grad * gain
    return r * (e - jnp.mean(e, axis=-1, keepdims=True) - n * jnp.mean(e * n, axis=-1, keepdims=True))


def shifted(array, axis, by):
    devices = lax.axis_size(axis)
    return lax.ppermute(array, axis, [(i, (i + by) % devices) for i in range(devices)])


def passed_along(array, by):
    devices = lax.axis_size(("z", "x"))
    return lax.ppermute(array, ("z", "x"), [(i, i + by) for i in range(devices) if 0 <= i + by < devices])


def swapped(array):
    return lax.ppermute(array, "core", [(0, 1), (1, 0)])


def pick(array, index):
    return lax.dynamic_index_in_dim(array, index, 0, keepdims=False)


def summed_share(array, axis):
    me, devices = lax.axis_index(axis), lax.axis_size(axis)
    total = pick(array, me).astype(f32)
    for by in (1, devices - 1, 2):
        total = total + shifted(pick(array, (me + by) % devices), axis, by).astype(f32)
    return total.astype(bf16)


def gathered(array, axis):
    me, devices = lax.axis_index(axis), lax.axis_size(axis)
    out = jnp.zeros((devices,) + array.shape, array.dtype)
    out = lax.dynamic_update_index_in_dim(out, array, me, 0)
    for by in (1, devices - 1, 2):
        out = lax.dynamic_update_index_in_dim(out, shifted(array, axis, by), (me + devices - by) % devices, 0)
    return out


def summed_over_chips(array):
    rows = array.shape[0]
    part = summed_share(array.reshape(4, rows // 4, 640), "z")
    part = summed_share(part.reshape(4, rows // 16, 640), "x")
    return gathered(gathered(part, "x").reshape(rows // 4, 640), "z").reshape(rows, 640)


def in_order(core, mine, theirs, axis):
    first = jnp.where(core == 0, mine, theirs)
    second = jnp.where(core == 0, theirs, mine)
    return jnp.concatenate([first, second], axis=axis)


def window_info(length_row, chip, core, win):
    ends = jnp.cumsum(length_row)
    starts = ends - length_row
    base = chip * 512 - 1024
    places = base + jnp.arange(win, dtype=jnp.int32)
    inside = (places[:, None] >= starts[None, :]) & (places[:, None] < ends[None, :])
    ones = jnp.broadcast_to(jnp.arange(64) < 3, (win, 64)).astype(bf16)
    key_rows = jnp.concatenate([jnp.where(inside, 0.0, -BIG).astype(bf16), ones], axis=1)
    own = chip * 512 + jnp.arange(512, dtype=jnp.int32)
    inside_q = (own[None, :] >= starts[:, None]) & (own[None, :] < ends[:, None])
    query_rows = jnp.concatenate([inside_q.astype(bf16), jnp.zeros((64, 512), bf16)], axis=0)
    info = [core]
    sizes = []
    for t in range(2):
        first = chip * 512 + t * TILE
        low = jnp.max(jnp.where(starts <= first, starts, 0)) - base
        high = jnp.min(jnp.where(ends > first + TILE - 1, ends, 1 << 30)) - base
        start = low // 128 * 128
        need = high - start
        size = jnp.where(need <= SHORT, SHORT, (need + LONG - 1) // LONG * LONG)
        info.append(jnp.minimum(start, win - size))
        sizes.append(size)
    return jnp.stack(info + sizes).astype(jnp.int32), key_rows, query_rows


def body(tokens, lengths, gain_one, bias_one, w_qkv, w_out, gain_two, bias_two, w_up, w_down, cotangent):
    core, chip = lax.axis_index("core"), lax.axis_index(("z", "x"))
    tiles = lambda w, axis, base: jnp.concatenate(
        [lax.dynamic_slice_in_dim(w, base + 256 * core, 256, axis), lax.slice_in_dim(w, base + 512, base + 640, axis=axis)], axis=axis)

    vectors = jnp.stack([gain_one, bias_one, gain_two, bias_two], axis=1)
    packed = jnp.concatenate(
        [tiles(w_qkv, 1, 0), tiles(w_qkv, 1, 640), tiles(w_qkv, 1, 1280), w_out, jnp.pad(vectors, ((0, 0), (0, 124)))], axis=1)
    packed = gathered(packed, "batch").reshape(640, -1)
    w_heads, w_out_all = packed[:, :1152], packed[:, 1152:1792]
    gain_f1, bias_f1, gain_f2, bias_f2 = (packed[:, 1792 + i].astype(f32)[None, :] for i in range(4))
    up_half = lax.dynamic_index_in_dim(w_up.reshape(160, 4, 2, 640), core, 2, keepdims=False).reshape(160, 2560)
    up_half = lax.all_gather(up_half, "batch", axis=0, tiled=True)
    down_half = lax.all_gather(lax.dynamic_slice_in_dim(w_down, 640 * core, 640, 0), "batch", axis=0, tiled=True)

    core_arg = core[None].astype(jnp.int32)
    projected = []
    for m in range(2):
        own = tokens[m, 0]
        reach = jnp.stack([passed_along(own, 2), passed_along(own, 1), own, passed_along(own, -1), passed_along(own, -2)])
        projected.append(project(core_arg, reach, swapped(reach), gain_f1, bias_f1, w_heads))
    forward = []
    for m in range(2):
        k, v, kT, vT, q, qT, hidden = projected[m]
        info, key_rows, query_rows = window_info(lengths[m, 0], chip, core, k.shape[0])
        forward.append((info, key_rows, query_rows) + tuple(attend(info, qT, k, vT, key_rows, query_rows)))

    low = jnp.stack([f[4] for f in forward])
    mine = lax.dynamic_slice_in_dim(low, 256 * core, 256, 1)
    theirs = swapped(lax.dynamic_slice_in_dim(low, 256 - 256 * core, 256, 1))
    head_a, head_b = jnp.where(core == 0, mine, theirs), jnp.where(core == 0, theirs, mine)
    attended = jnp.concatenate([head_a[..., :256], head_b[..., :256], head_a[..., 256:] + head_b[..., 256:]], axis=-1).reshape(512, 640)
    inputs = tokens[:, 0].reshape(512, 640).astype(f32)
    middle = inputs + jnp.dot(attended, w_out_all, preferred_element_type=f32)
    n_two, r_two = moments(middle)
    hidden_two = (n_two * gain_f2 + bias_f2).astype(bf16)
    cot = cotangent[:, 0].reshape(512, 640)
    both = swapped(jnp.stack([hidden_two, cot]))
    out, d_hidden, g_up, g_down = feed_forward(
        jnp.concatenate([hidden_two, both[0]]), jnp.concatenate([cot, both[1]]), up_half, down_half)
    back = swapped(jnp.stack([out[512:], d_hidden[512:]]).astype(bf16)).astype(f32)
    block_out = (middle + out[:512] + back[0]).astype(bf16)
    d_hidden = d_hidden[:512] + back[1]
    g_gain_two, g_bias_two = jnp.sum(d_hidden * n_two, axis=0), jnp.sum(d_hidden, axis=0)
    grad_middle = cot.astype(f32) + norm_back(d_hidden, n_two, r_two, gain_f2)
    branch = grad_middle.astype(bf16)
    g_out = lax.dot_general(attended, branch, (((0,), (0,)), ((), ())), preferred_element_type=f32).astype(bf16)
    first = jnp.concatenate([g_up, g_down, g_out.reshape(4, 160, 640)], axis=1)
    first = lax.psum_scatter(first, "batch", scatter_dimension=0, tiled=True).reshape(-1, 640)

    branch_all = in_order(core, branch.reshape(2, 256, 640), swapped(branch).reshape(2, 256, 640), 1)
    w_out_half = tiles(w_out_all, 0, 0)
    nt = (((1,), (1,)), ((), ()))
    grads_kv, grads_q = [], []
    for m in range(2):
        k, v, kT, vT, q, qT, hidden = projected[m]
        info, key_rows, query_rows, oT, _, lse = forward[m]
        do = lax.dot_general(branch_all[m], w_out_half, nt, preferred_element_type=f32).astype(bf16)
        doT = lax.dot_general(w_out_half, branch_all[m], nt, preferred_element_type=f32).astype(bf16)
        dq, dk, dv = attend_back(info, qT, q, k, kT, v, doT, do, oT, lse, key_rows, query_rows)
        pieces = jnp.concatenate([dk, dv], axis=1).reshape(5, 512, 768)
        grads_kv.append(pieces[2].astype(f32) + sum(passed_along(pieces[2 + by], by).astype(f32) for by in (1, -1, 2, -2)))
        grads_q.append(dq)
    grad_projected = jnp.concatenate([jnp.stack(grads_q), jnp.stack(grads_kv).astype(bf16)], axis=2)
    flat = grad_projected.reshape(1024, 1152)
    hidden_all = jnp.concatenate([projected[0][6], projected[1][6]])
    g_qkv = lax.dot_general(hidden_all, flat, (((0,), (0,)), ((), ())), preferred_element_type=f32).astype(bf16)
    d_one = lax.dot_general(flat, w_heads, nt, preferred_element_type=f32).reshape(2, 512, 640)
    d_one = lax.dynamic_slice_in_dim(d_one, 256 * core, 256, 1) + swapped(
        lax.dynamic_slice_in_dim(d_one, 256 - 256 * core, 256, 1).astype(bf16)).astype(f32)
    d_one = d_one.reshape(512, 640)
    n_one, r_one = moments(inputs)
    g_gain_one, g_bias_one = jnp.sum(d_one * n_one, axis=0), jnp.sum(d_one, axis=0)
    grad_tokens = (grad_middle + norm_back(d_one, n_one, r_one, gain_f1)).astype(bf16)

    vector_grads = jnp.stack([g_gain_one, g_bias_one, g_gain_two, g_bias_two]).reshape(4, 4, 160)
    vector_grads = jnp.pad(vector_grads.transpose(1, 0, 2).reshape(4, 1, 640), ((0, 0), (0, 31), (0, 0))).astype(bf16)
    wide = jnp.pad(g_qkv, ((0, 0), (0, 128))).reshape(4, 160, 2, 640).transpose(0, 2, 1, 3).reshape(4, 320, 640)
    second = jnp.concatenate([wide, vector_grads], axis=1)
    second = summed_share(second, "batch")
    first = jnp.pad(first, ((0, 1536 - first.shape[0]), (0, 0)))
    second = jnp.pad(second, ((0, 512 - second.shape[0]), (0, 0)))
    first, second = summed_over_chips(first), summed_over_chips(second)
    total = jnp.concatenate([first[:1440], second[:336]])
    other = swapped(total)
    total, other = total.astype(f32), other.astype(f32)
    one, two = jnp.where(core == 0, total, other), jnp.where(core == 0, other, total)
    grad_up = jnp.stack([one[:640].reshape(4, 160, 640), two[:640].reshape(4, 160, 640)], axis=1)
    grad_up = grad_up.transpose(2, 0, 1, 3).reshape(160, 5120)
    grad_down = jnp.concatenate([one[640:1280], two[640:1280]])
    both = one[1280:] + two[1280:]
    grad_out = both[:160]
    parts = [x[1440:1760].reshape(2, 160, 640).transpose(1, 0, 2).reshape(160, 1280) for x in (one, two)]
    columns = []
    for part in range(3):
        a, b = (x[:, 384 * part:384 * (part + 1)] for x in parts)
        columns += [a[:, :256], b[:, :256], a[:, 256:] + b[:, 256:]]
    grad_qkv = jnp.concatenate(columns, axis=1)
    vectors = both[480].reshape(4, 160)
    return (
        block_out.reshape(2, 1, 256, 640), grad_tokens.reshape(2, 1, 256, 640), vectors[0], vectors[1], grad_qkv, grad_out,
        vectors[2], vectors[3], grad_up, grad_down)


def solution(mesh):
    fine = Mesh(mesh.devices.reshape(4, 4, 4, 2), ("batch", "z", "x", "core"))
    rows = P(None, "batch", ("z", "x", "core"), None)
    one, two = P("batch"), P("batch", None)
    return jax.shard_map(
        body,
        mesh=fine,
        in_specs=(rows, P(None, "batch", None), one, one, two, two, one, one, two, two, rows),
        out_specs=(rows, rows, one, one, two, two, one, one, two, two),
        check_vma=False,
    )
```

```python
import math

import jax
import jax.numpy as jnp
from jax import lax
from jax.experimental import pallas as pl
from jax.experimental.pallas import tpu as pltpu
from jax.sharding import Mesh
from jax.sharding import PartitionSpec as P

HEAD_DIM = 32
SCALE = HEAD_DIM ** -0.5
LOG2E = math.log2(math.e)
C2 = SCALE * LOG2E
BIG = 1e30
TILE = 256
EPSILON = 1e-05
PAIRS = 5
SHORT, LONG = 384, 1152
f32, bf16 = jnp.float32, jnp.bfloat16
NT = (((1,), (1,)), ((), ()))


def pair_offset(info_ref):
    p = pl.program_id(0)
    sub = jnp.where(p == PAIRS - 1, info_ref[0], lax.rem(p, 2))
    return sub * (2 * HEAD_DIM)


def split3(v):
    a = v.astype(bf16)
    r = v - a.astype(f32)
    b = r.astype(bf16)
    d = (r - b.astype(f32)).astype(bf16)
    return a, b, d


def rows_masked(xT, off):
    row = lax.broadcasted_iota(jnp.int32, xT.shape, 0) - off
    xf = xT.astype(f32)
    return [jnp.where((row >= HEAD_DIM * j) & (row < HEAD_DIM * (j + 1)), xf, 0.0).astype(bf16) for j in range(2)]


def lanes_masked(x, off):
    lane = lax.broadcasted_iota(jnp.int32, x.shape, 1) - off
    xf = x.astype(f32)
    return [jnp.where((lane >= HEAD_DIM * j) & (lane < HEAD_DIM * (j + 1)), xf, 0.0).astype(bf16) for j in range(2)]


def attend_kernel(info_ref, qT_ref, k_ref, vT_ref, kaug_ref, qaugT_ref, oT_ref, o_ref, l_ref, rhs):
    off = pair_offset(info_ref)
    oT_ref[...] = jnp.where(lax.rem(pl.program_id(0), 2) == 0, 0.0, oT_ref[...])
    for t in range(2):
        cols = slice(t * TILE, (t + 1) * TILE)
        masked = rows_masked(qT_ref[:, cols], off)
        for j in range(2):
            rhs[0:128, j * TILE:(j + 1) * TILE] = masked[j]
            rhs[128:256, j * TILE:(j + 1) * TILE] = qaugT_ref[:, cols]
        start = info_ref[1 + t]
        need = info_ref[3 + t]

        def block(first, size):
            def step(i, carry):
                row = pl.multiple_of(first + i * size, 128)
                lhs = jnp.concatenate([k_ref[pl.ds(row, size), :], kaug_ref[pl.ds(row, size), :]], axis=1)
                raw = [jnp.dot(lhs, rhs[:, j * TILE:(j + 1) * TILE], preferred_element_type=f32) for j in range(2)]
                out = []
                for j in range(2):
                    m, l, o = carry[j]
                    s = raw[j] * C2
                    m_new = jnp.maximum(m, jnp.max(s, axis=0, keepdims=True))
                    alpha = jnp.exp2(m - m_new)
                    p = jnp.exp2(s - m_new)
                    vT = vT_ref[pl.ds(pl.multiple_of(off + j * HEAD_DIM, HEAD_DIM), HEAD_DIM), pl.ds(row, size)]
                    out.append((m_new, l * alpha + jnp.sum(p, axis=0, keepdims=True),
                                o * alpha + jnp.dot(vT, p.astype(bf16), preferred_element_type=f32)))
                return tuple(out)
            return step

        def finish(state):
            for j in range(2):
                m, l, o = state[j]
                oT_ref[pl.ds(pl.multiple_of(off + j * HEAD_DIM, HEAD_DIM), HEAD_DIM), cols] = o * (1.0 / l)
                l_ref[0, j:j + 1, cols] = m + jnp.log2(l)

        init = tuple((jnp.full((1, TILE), -1e38, f32), jnp.zeros((1, TILE), f32), jnp.zeros((HEAD_DIM, TILE), f32)) for _ in range(2))

        longs = lax.div(need, LONG)
        state = lax.fori_loop(0, longs, block(start, LONG), init)
        finish(lax.fori_loop(0, lax.div(need - longs * LONG, SHORT), block(start + longs * LONG, SHORT), state))

    o_ref[...] = oT_ref[...].T.astype(bf16)


def attend(info, qT, k, vT, kaug, qaugT):
    win = k.shape[0]
    nq = qT.shape[1]
    group = lambda p, *_: p // 2
    return pl.pallas_call(
        attend_kernel,
        out_shape=(jax.ShapeDtypeStruct((384, nq), f32), jax.ShapeDtypeStruct((nq, 384), bf16), jax.ShapeDtypeStruct((PAIRS, 8, nq), f32)),
        grid_spec=pltpu.PrefetchScalarGridSpec(
            num_scalar_prefetch=1, grid=(PAIRS,),
            in_specs=[
                pl.BlockSpec((128, nq), lambda p, *_: (p // 2, 0)),
                pl.BlockSpec((win, 128), lambda p, *_: (0, p // 2)),
                pl.BlockSpec((128, win), lambda p, *_: (p // 2, 0)),
                pl.BlockSpec((win, 128), lambda p, *_: (0, 0)),
                pl.BlockSpec((128, nq), lambda p, *_: (0, 0)),
            ],
            out_specs=[
                pl.BlockSpec((128, nq), lambda p, *_: (p // 2, 0)),
                pl.BlockSpec((nq, 128), lambda p, *_: (0, p // 2)),
                pl.BlockSpec((1, 8, nq), lambda p, *_: (p, 0, 0)),
            ],
            scratch_shapes=[pltpu.VMEM((256, 2 * TILE), bf16)],
        ),
        compiler_params=pltpu.CompilerParams(vmem_limit_bytes=28 << 20),
        cost_estimate=pl.CostEstimate(flops=20 * 10**9, bytes_accessed=6 << 20, transcendentals=5 * 10**6),
        name="attend",
    )(info, qT, k, vT, kaug, qaugT)


def attend_back_kernel(info_ref, qT_ref, q_ref, k_ref, kT_ref, v_ref, doT_ref, do_ref, oT_ref, l_ref, kaug_ref, qaugT_ref,
                       dq_ref, dk_ref, dv_ref, dqT_ref, rhs_s, rhs_d, q_stk, do_stk, dk_acc, dv_acc):
    p_id = pl.program_id(0)
    off = pair_offset(info_ref)

    @pl.when(lax.rem(p_id, 2) == 0)
    def _():
        dqT_ref[...] = jnp.zeros_like(dqT_ref)
        dk_acc[...] = jnp.zeros_like(dk_acc)
        dv_acc[...] = jnp.zeros_like(dv_acc)

    for t in range(2):
        cols = slice(t * TILE, (t + 1) * TILE)
        masked_q = rows_masked(qT_ref[:, cols], off)
        masked_do = rows_masked(doT_ref[:, cols], off)
        lane_q = lanes_masked(q_ref[cols, :], off)
        lane_do = lanes_masked(do_ref[cols, :], off)
        for j in range(2):
            part = slice(j * TILE, (j + 1) * TILE)
            head = pl.ds(pl.multiple_of(off + j * HEAD_DIM, HEAD_DIM), HEAD_DIM)
            delta = jnp.sum(doT_ref[head, cols].astype(f32) * oT_ref[head, cols], axis=0, keepdims=True)
            total = l_ref[0, j:j + 1, cols] * (1.0 / C2)
            rowid = lax.broadcasted_iota(jnp.int32, (64, TILE), 0)
            lp, dp = split3(-total), split3(-delta)
            def pieces(parts):
                x = jnp.zeros((64, TILE), f32)
                for n in range(3):
                    x = jnp.where(rowid == n, parts[n].astype(f32), x)
                return x.astype(bf16)
            rhs_s[0:128, part] = masked_q[j]
            rhs_s[128:192, part] = qaugT_ref[0:64, cols]
            rhs_s[192:256, part] = pieces(lp)
            rhs_d[0:128, part] = masked_do[j]
            rhs_d[128:192, part] = jnp.zeros((64, TILE), bf16)
            rhs_d[192:256, part] = pieces(dp)
            q_stk[part, :] = lane_q[j]
            do_stk[part, :] = lane_do[j]
        start = info_ref[1 + t]
        need = info_ref[3 + t]

        def block(first, size):
            def step(i, carry):
                row = pl.multiple_of(first + i * size, 128)
                rows = pl.ds(row, size)
                aug = kaug_ref[rows, :]
                lhs_k = jnp.concatenate([k_ref[rows, :], aug], axis=1)
                lhs_v = jnp.concatenate([v_ref[rows, :], aug], axis=1)
                out, dv, dk = [], dv_acc[rows, :], dk_acc[rows, :]
                for j in range(2):
                    part = slice(j * TILE, (j + 1) * TILE)
                    s = jnp.dot(lhs_k, rhs_s[:, part], preferred_element_type=f32)
                    dp = jnp.dot(lhs_v, rhs_d[:, part], preferred_element_type=f32)
                    p = jnp.exp2(s * C2)
                    ds = (p * dp).astype(bf16)
                    dv = dv + jnp.dot(p.astype(bf16), do_stk[part, :], preferred_element_type=f32)
                    dk = dk + jnp.dot(ds, q_stk[part, :], preferred_element_type=f32)
                    kT = kT_ref[pl.ds(pl.multiple_of(off + j * HEAD_DIM, HEAD_DIM), HEAD_DIM), rows]
                    out.append(carry[j] + jnp.dot(kT, ds, preferred_element_type=f32))
                dv_acc[rows, :] = dv
                dk_acc[rows, :] = dk
                return tuple(out)
            return step

        def finish(dqs):
            for j in range(2):
                dqT_ref[pl.ds(pl.multiple_of(off + j * HEAD_DIM, HEAD_DIM), HEAD_DIM), cols] = dqs[j] * SCALE

        init = tuple(jnp.zeros((HEAD_DIM, TILE), f32) for _ in range(2))

        longs = lax.div(need, LONG)
        state = lax.fori_loop(0, longs, block(start, LONG), init)
        finish(lax.fori_loop(0, lax.div(need - longs * LONG, SHORT), block(start + longs * LONG, SHORT), state))
    @pl.when((lax.rem(p_id, 2) == 1) | (p_id == PAIRS - 1))
    def _():
        dq_ref[...] = dqT_ref[...].T.astype(bf16)
        dk_ref[...] = (dk_acc[...] * SCALE).astype(bf16)
        dv_ref[...] = dv_acc[...].astype(bf16)


def attend_back(m, info, qT, q, k, kT, v, doT, do, oT, lse, kaug, qaugT):
    win, nq = k.shape[0], qT.shape[1]
    wide = pl.BlockSpec((128, nq), lambda p, *_: (p // 2, 0))
    tall = pl.BlockSpec((nq, 128), lambda p, *_: (0, p // 2))
    keys = pl.BlockSpec((win, 128), lambda p, *_: (0, p // 2))
    return pl.pallas_call(
        attend_back_kernel,
        out_shape=(jax.ShapeDtypeStruct((nq, 384), bf16), jax.ShapeDtypeStruct((win, 384), bf16), jax.ShapeDtypeStruct((win, 384), bf16)),
        grid_spec=pltpu.PrefetchScalarGridSpec(
            num_scalar_prefetch=1, grid=(PAIRS,),
            in_specs=[wide, tall, keys, pl.BlockSpec((128, win), lambda p, *_: (p // 2, 0)), keys,
                      pl.BlockSpec((128, nq), lambda p, *_: (p // 2, m)), pl.BlockSpec((nq, 128), lambda p, *_: (m, p // 2)), wide,
                      pl.BlockSpec((1, 8, nq), lambda p, *_: (p, 0, 0)),
                      pl.BlockSpec((win, 128), lambda p, *_: (0, 0)), pl.BlockSpec((128, nq), lambda p, *_: (0, 0))],
            out_specs=[tall, keys, keys],
            scratch_shapes=[pltpu.VMEM((128, nq), f32), pltpu.VMEM((256, 2 * TILE), bf16), pltpu.VMEM((256, 2 * TILE), bf16),
                            pltpu.VMEM((2 * TILE, 128), bf16), pltpu.VMEM((2 * TILE, 128), bf16),
                            pltpu.VMEM((win, 128), f32), pltpu.VMEM((win, 128), f32)],
        ),
        compiler_params=pltpu.CompilerParams(vmem_limit_bytes=32 << 20),
        cost_estimate=pl.CostEstimate(flops=40 * 10**9, bytes_accessed=12 << 20, transcendentals=5 * 10**6),
        name="attend_back",
    )(info, qT, q, k, kT, v, doT, do, oT, lse, kaug, qaugT)


def moments(x):
    centred = x - jnp.mean(x, axis=-1, keepdims=True)
    r = lax.rsqrt(jnp.mean(centred * centred, axis=-1, keepdims=True) + EPSILON)
    return centred * r, r


def norm_back(grad, n, r, gain):
    e = grad * gain
    return r * (e - jnp.mean(e, axis=-1, keepdims=True) - n * jnp.mean(e * n, axis=-1, keepdims=True))


def call(kernel, out_shape, name, flops=10**9, limit=48, **spec):
    return pl.pallas_call(
        kernel, out_shape=out_shape, name=name,
        compiler_params=pltpu.CompilerParams(vmem_limit_bytes=limit << 20),
        cost_estimate=pl.CostEstimate(flops=flops, bytes_accessed=8 << 20, transcendentals=0), **spec)


def shape(*dims, dtype=bf16):
    return jax.ShapeDtypeStruct(dims, dtype)


def scalar_first(grid, in_specs, out_specs, scratch=()):
    return dict(grid_spec=pltpu.PrefetchScalarGridSpec(
        num_scalar_prefetch=1, grid=grid, in_specs=in_specs, out_specs=out_specs, scratch_shapes=list(scratch)))


def full(*dims):
    return pl.BlockSpec(dims, lambda *_: (0,) * len(dims))


def pack_heads_kernel(core_ref, qkv_ref, vec_ref, heads_ref):
    for part in range(3):
        near = pl.ds(pl.multiple_of(640 * part + 256 * core_ref[0], 128), 256)
        heads_ref[0:160, 384 * part:384 * part + 256] = qkv_ref[:, near]
        heads_ref[0:160, 384 * part + 256:384 * (part + 1)] = qkv_ref[:, 640 * part + 512:640 * (part + 1)]
    heads_ref[160:176, :] = jnp.zeros((16, 1152), bf16)
    heads_ref[160:176, 0:160] = vec_ref[...]


def pack_heads(core, w_qkv, vectors):
    return call(pack_heads_kernel, shape(176, 1152), "pack_heads", 10**6, 8, **scalar_first(
        (1,), [full(160, 1920), full(16, 160)], full(176, 1152)))(core, w_qkv, vectors)


def pack_feed_kernel(core_ref, out_ref, up_ref, down_ref, feed_ref):
    core = core_ref[0]
    for f in range(4):
        feed_ref[:, 640 * f:640 * (f + 1)] = up_ref[:, pl.ds(pl.multiple_of(1280 * f + 640 * core, 128), 640)]
        feed_ref[:, 2560 + 640 * f:2560 + 640 * (f + 1)] = down_ref[pl.ds(pl.multiple_of(640 * core + 160 * f, 32), 160), :]
    feed_ref[:, 5120:5760] = out_ref[...]


def pack_feed(core, w_out, w_up, w_down):
    args = (w_out, w_up, w_down)
    return call(pack_feed_kernel, shape(160, 5760), "pack_feed", 10**6, 16, **scalar_first(
        (1,), [full(*a.shape) for a in args], full(160, 5760)))(core, *args)


def assemble_kernel(y_ref, own_ref, before_ref, after_ref, near_ref, far_ref, heads_ref, vec_ref):
    total = jnp.zeros((16, 640), f32)

    def place(by, top, bottom, vec):
        nonlocal total
        row = lax.rem(y_ref[0] + by, 4) * 160
        for part, base in ((top, 0), (bottom, top.shape[0])):
            heads_ref[pl.ds(pl.multiple_of(row + base, 32), part.shape[0]), :] = part
        total = total + pltpu.roll(vec[:, :640].astype(f32), row, 1)

    for by, ref in ((0, own_ref), (3, before_ref), (1, after_ref)):
        place(by, ref[0:96, :], ref[96:160, :], ref[160:176, :])
    place(2, near_ref[...], far_ref[0:64, :], far_ref[64:80, :])
    vec_ref[...] = total


def assemble(y, *parts):
    return call(assemble_kernel, (shape(640, 1152), shape(16, 640, dtype=f32)), "assemble", 10**6, 12, **scalar_first(
        (1,), [full(*a.shape) for a in parts], [full(640, 1152), full(16, 640)]))(y, *parts)


def window_rows(core, own_refs, other_refs, m, x_ref):
    block = lax.rem(pl.program_id(0), 5)
    for j in range(5):
        @pl.when(block == j)
        def _():
            mine, theirs = own_refs[j][m].astype(f32), other_refs[j][m].astype(f32)
            x_ref[0:256, :] = jnp.where(core == 0, mine, theirs)
            x_ref[256:512, :] = jnp.where(core == 0, theirs, mine)


def project_kernel(m, core_ref, *refs):
    own_refs, other_refs = refs[:5], refs[5:10]
    vec_ref, w_ref, k_ref, v_ref, kT_ref, vT_ref, q_ref, qT_ref, x_ref, hid_ref = refs[10:]
    block = pl.program_id(0)
    needed = (block >= core_ref[1 + 2 * m]) & (block < core_ref[2 + 2 * m])

    @pl.when(jnp.logical_not(needed))
    def _():
        for ref in (k_ref, v_ref, kT_ref, vT_ref):
            ref[...] = jnp.zeros_like(ref)

    @pl.when(needed)
    def _():
        window_rows(core_ref[0], own_refs, other_refs, m, x_ref)
        hidden = (moments(x_ref[...])[0] * vec_ref[0:1, :] + vec_ref[1:2, :]).astype(bf16)
        hid_ref[...] = hidden
        kv = jnp.dot(hidden, w_ref[:, 384:], preferred_element_type=f32)
        low = kv.astype(bf16)
        k_ref[...] = low[:, :384]
        v_ref[...] = low[:, 384:]
        turned = kv.T.astype(bf16)
        kT_ref[...] = turned[:384]
        vT_ref[...] = turned[384:]

    @pl.when(block == 2)
    def _():
        q = jnp.dot(hid_ref[...], w_ref[:, :384], preferred_element_type=f32)
        q_ref[...] = q.astype(bf16)
        qT_ref[...] = q.T.astype(bf16)


def project(m, core, own, other, vec, w):
    tall, wide = pl.BlockSpec((512, 384), lambda b, *_: (b, 0)), pl.BlockSpec((384, 512), lambda b, *_: (0, b))
    return call(
        lambda *refs: project_kernel(m, *refs),
        (shape(2560, 384), shape(2560, 384), shape(384, 2560), shape(384, 2560), shape(512, 384), shape(384, 512)),
        "project", 10**10, 32, **scalar_first(
            (5,), [full(2, 256, 640)] * 10 + [full(16, 640), full(640, 1152)],
            [tall, tall, wide, wide, full(512, 384), full(384, 512)], [pltpu.VMEM((512, 640), f32), pltpu.VMEM((512, 640), bf16)]))(core, *own, *other, vec, w)


def heads_joined(core, mine, theirs):
    first, second = (jnp.where(core == 0, a, b) for a, b in ((mine, theirs), (theirs, mine)))
    return jnp.concatenate([first[:, :256], second[:, :256], first[:, 256:] + second[:, 256:]], axis=1)


def middle_kernel(core_ref, low_ref, theirs_ref, tok_ref, w_ref, vec_ref, mid_ref, hid_ref):
    core = core_ref[0]
    rows = pl.ds(pl.multiple_of(256 * core, 256), 256)
    for m in range(2):
        attended = heads_joined(core, low_ref[m, rows, :].astype(f32), theirs_ref[m, rows, :].astype(f32)).astype(bf16)
        part = slice(256 * m, 256 * (m + 1))
        middle = tok_ref[m].astype(f32) + jnp.dot(attended, w_ref[...], preferred_element_type=f32)
        mid_ref[part, :] = middle
        hid_ref[part, :] = (moments(middle)[0] * vec_ref[2:3, :] + vec_ref[3:4, :]).astype(bf16)


def middle_step(core, low, theirs, tok, w, vec):
    args = (low, theirs, tok, w, vec)
    specs = [full(*a.shape) for a in args]
    specs[3] = pl.BlockSpec((640, 640), lambda *_: (0, 8))
    return call(middle_kernel, (shape(512, 640, dtype=f32), shape(512, 640)), "middle", 10**9, 16, **scalar_first(
        (1,), specs, [full(512, 640), full(512, 640)]))(core, *args)


def feed_kernel(h_ref, h2_ref, cot_ref, cot2_ref, up_ref, down_ref, out_ref, dh_ref, theirs_ref, g_ref, h, cot, hT, cT, out, dh):
    chunk = pl.program_id(0)

    @pl.when(chunk == 0)
    def _():
        h[0:512, :], h[512:1024, :] = h_ref[...], h2_ref[...]
        cot[0:512, :], cot[512:1024, :] = cot_ref[...], cot2_ref[...]
        hT[...] = h[...].astype(f32).T.astype(bf16)
        cT[...] = cot[...].astype(f32).T.astype(bf16)
        out[...] = jnp.zeros_like(out)
        dh[...] = jnp.zeros_like(dh)

    up_w = up_ref[...]
    down_w = jnp.concatenate([down_ref[160 * y:160 * (y + 1), 640 * i:640 * (i + 1)] for y in range(2) for i in range(4)], axis=0)
    acts, d_ups = [], []
    for t in range(4):
        rows = slice(256 * t, 256 * (t + 1))
        u = jnp.dot(h[rows, :], up_w, preferred_element_type=f32)
        d_act = lax.dot_general(cot[rows, :], down_w, NT, preferred_element_type=f32)
        cdf = 0.5 * (1.0 + lax.erf(u * (2.0 ** -0.5)))
        pdf = jnp.exp(u * u * -0.5) * ((2.0 * math.pi) ** -0.5)
        act = (u * cdf).astype(bf16)
        d_up = (d_act * (cdf + u * pdf)).astype(bf16)
        out[rows, :] += jnp.dot(act, down_w, preferred_element_type=f32)
        dh[rows, :] += lax.dot_general(d_up, up_w, NT, preferred_element_type=f32)
        acts.append(act)
        d_ups.append(d_up)
    g_up = jnp.dot(hT[...], jnp.concatenate(d_ups, axis=0), preferred_element_type=f32).astype(bf16)
    g_down = jnp.dot(cT[...], jnp.concatenate(acts, axis=0), preferred_element_type=f32).T.astype(bf16)
    for f in range(2):
        for y in range(4):
            for i in range(2):
                g_ref[4 * chunk + 2 * f + i, y] = g_up[160 * y + 80 * i:160 * y + 80 * (i + 1), 640 * f:640 * (f + 1)]
        for i in range(8):
            g_ref[8 + i, 2 * chunk + f] = g_down[640 * f + 80 * i:640 * f + 80 * (i + 1)]

    @pl.when(chunk == 1)
    def _():
        out_ref[...], dh_ref[...] = out[0:512, :], dh[0:512, :]
        theirs_ref[0], theirs_ref[1] = out[512:1024, :].astype(bf16), dh[512:1024, :].astype(bf16)


def feed_forward(h, h2, cot, cot2, weights):
    return call(
        feed_kernel,
        (shape(512, 640, dtype=f32), shape(512, 640, dtype=f32), shape(2, 512, 640), shape(16, 4, 80, 640)),
        "feed_forward", 30 * 10**9, 52, grid=(2,),
        in_specs=[full(512, 640)] * 4 + [pl.BlockSpec((640, 1280), lambda f: (0, f)), pl.BlockSpec((320, 2560), lambda f: (f, 1))],
        out_specs=[full(512, 640), full(512, 640), full(2, 512, 640), full(16, 4, 80, 640)],
        scratch_shapes=[pltpu.VMEM((1024, 640), bf16), pltpu.VMEM((1024, 640), bf16), pltpu.VMEM((640, 1024), bf16), pltpu.VMEM((640, 1024), bf16),
                        pltpu.VMEM((1024, 640), f32), pltpu.VMEM((1024, 640), f32)],
    )(h, h2, cot, cot2, weights, weights)


def after_kernel(mid_ref, out_ref, dh_ref, theirs_ref, cot_ref, vec_ref, block_ref, grad_ref, branch_ref, g_ref):
    middle = mid_ref[...]
    block_ref[...] = (middle + out_ref[...] + theirs_ref[0].astype(f32)).astype(bf16)
    d_hidden = dh_ref[...] + theirs_ref[1].astype(f32)
    n, r = moments(middle)
    g_ref[...] = jnp.zeros_like(g_ref)
    g_ref[0:1, :] = jnp.sum(d_hidden * n, axis=0, keepdims=True)
    g_ref[1:2, :] = jnp.sum(d_hidden, axis=0, keepdims=True)
    grad = cot_ref[...].astype(f32) + norm_back(d_hidden, n, r, vec_ref[2:3, :])
    grad_ref[...] = grad
    branch_ref[...] = grad.astype(bf16)


def after_feed(middle, out, dh, theirs, cot, vec):
    args = (middle, out, dh, theirs, cot, vec)
    return call(
        after_kernel, (shape(512, 640), shape(512, 640, dtype=f32), shape(512, 640), shape(8, 640, dtype=f32)), "after_feed", 10**9, 24,
        in_specs=[pl.BlockSpec(memory_space=pltpu.VMEM)] * 6, out_specs=[pl.BlockSpec(memory_space=pltpu.VMEM)] * 4)(*args)


def branch_kernel(core_ref, own_ref, their_ref, w_ref, low_ref, theirs_ref, do_ref, doT_ref, g_ref):
    core = core_ref[0]
    w = jnp.concatenate([w_ref[pl.ds(pl.multiple_of(256 * core, 256), 256), :], w_ref[512:640, :]], axis=0)
    g = jnp.zeros((640, 384), f32)
    for m in range(2):
        part = slice(256 * m, 256 * (m + 1))
        mine, theirs = own_ref[part, :].astype(f32), their_ref[part, :].astype(f32)
        branch = jnp.concatenate([jnp.where(core == 0, mine, theirs), jnp.where(core == 0, theirs, mine)], axis=0)
        kept = jnp.where(core == 0, branch[:, :384], branch[:, 256:]).astype(bf16)
        branch = branch.astype(bf16)
        rows = slice(512 * m, 512 * (m + 1))
        do = lax.dot_general(branch, w, NT, preferred_element_type=f32)
        do_ref[rows, :] = do.astype(bf16)
        doT_ref[:, rows] = do.T.astype(bf16)
        attended = heads_joined(core, low_ref[m].astype(f32), theirs_ref[m].astype(f32))
        g = g + jnp.dot(attended.T.astype(bf16), kept, preferred_element_type=f32)
    g_ref[...] = g


def branch_step(core, own, their, w, low, theirs):
    args = (own, their, w, low, theirs)
    specs = [full(*a.shape) for a in args]
    specs[2] = pl.BlockSpec((640, 640), lambda *_: (0, 8))
    return call(
        branch_kernel, (shape(1024, 384), shape(384, 1024), shape(640, 384, dtype=f32)), "branch", 10**9, 24, **scalar_first(
            (1,), specs, [full(1024, 384), full(384, 1024), full(640, 384)]))(core, *args)


def project_back_kernel(core_ref, *refs):
    own_refs, other_refs = refs[:5], refs[5:10]
    (vec_ref, w_ref, dq0_ref, dq1_ref, dk0_ref, dk1_ref, dv0_ref, dv1_ref, g_out_ref, g_two_ref,
     mine_ref, theirs_ref, tail_ref, x_ref, d_kv, d_q, d_hid, g_ref, g_vec) = refs[10:]
    step, core = pl.program_id(0), core_ref[0]
    block = lax.rem(step, 5)

    @pl.when(step == 0)
    def _():
        g_ref[...] = jnp.zeros_like(g_ref)
        g_vec[...] = jnp.zeros_like(g_vec)
        g_vec[2:4, :] = g_two_ref[0:2, :]

    second = lax.div(step, 5)
    needed = (block >= core_ref[1 + 2 * second]) & (block < core_ref[2 + 2 * second])

    @pl.when(jnp.logical_not(needed))
    def _():
        mine_ref[...] = jnp.zeros_like(mine_ref)
        theirs_ref[...] = jnp.zeros_like(theirs_ref)

    for m, (dq, dk, dv) in enumerate(((dq0_ref, dk0_ref, dv0_ref), (dq1_ref, dk1_ref, dv1_ref))):
        @pl.when(needed & (second == m))
        def _():
            window_rows(core, own_refs, other_refs, m, x_ref)
            d_kv[:, :384], d_kv[:, 384:] = dk[...], dv[...]
            d_q[...] = dq[...]

    @pl.when(needed)
    def _():
        n = moments(x_ref[...])[0]
        hiddenT = (n * vec_ref[0:1, :] + vec_ref[1:2, :]).T.astype(bf16)
        d_hid[...] = lax.dot_general(d_kv[...], w_ref[:, 384:], NT, preferred_element_type=f32)
        g_ref[:, 384:] += jnp.dot(hiddenT, d_kv[...], preferred_element_type=f32)

        @pl.when(block == 2)
        def _():
            g_ref[:, :384] += jnp.dot(hiddenT, d_q[...], preferred_element_type=f32)
            d_hid[...] += lax.dot_general(d_q[...], w_ref[:, :384], NT, preferred_element_type=f32)

        dh = d_hid[...]
        mine_ref[0, 0] = jnp.where(core == 0, dh[:256], dh[256:]).astype(bf16)
        theirs_ref[0, 0] = jnp.where(core == 0, dh[256:], dh[:256]).astype(bf16)
        g_vec[0:1, :] += jnp.sum(dh * n, axis=0, keepdims=True)
        g_vec[1:2, :] += jnp.sum(dh, axis=0, keepdims=True)

    @pl.when(step == 9)
    def _():
        turned = g_vec[...].T
        lane = lax.broadcasted_iota(jnp.int32, (640, 128), 1) - 64 * (1 - core)
        spare = g_ref[:, 256:384]
        for i in range(4):
            spare = jnp.where(lane == i, turned[:, i:i + 1], spare)
        g_ref[:, 256:384] = spare
        for y in range(4):
            for z in range(4):
                rows = slice(160 * y + 40 * z, 160 * y + 40 * (z + 1))
                for x in range(3):
                    tail_ref[16 * y + 4 * z + x] = g_ref[rows, 384 * x:384 * (x + 1)].astype(bf16)
                tail_ref[16 * y + 4 * z + 3] = g_out_ref[rows, :].astype(bf16)


def project_back(core, own, other, vec, w, dq, dk, dv, g_out, g_two):
    first = pl.BlockSpec((512, 384), lambda b, *_: (jnp.minimum(b, 4), 0))
    second = pl.BlockSpec((512, 384), lambda b, *_: (jnp.maximum(b - 5, 0), 0))
    return call(
        project_back_kernel, (shape(2, 5, 256, 640), shape(2, 5, 256, 640), shape(64, 40, 384)), "project_back", 10**10, 36, **scalar_first(
            (10,), [full(2, 256, 640)] * 10 + [full(16, 640), full(640, 1152), full(512, 384), full(512, 384), first, second, first, second,
                                               full(640, 384), full(8, 640)],
            [pl.BlockSpec((1, 1, 256, 640), lambda b, *_: (b // 5, lax.rem(b, 5), 0, 0))] * 2 + [full(64, 40, 384)],
            [pltpu.VMEM((512, 640), f32), pltpu.VMEM((512, 768), bf16), pltpu.VMEM((512, 384), bf16),
             pltpu.VMEM((512, 640), f32), pltpu.VMEM((640, 1152), f32), pltpu.VMEM((8, 640), f32)]))(core, *own, *other, vec, w, *dq, *dk, *dv, g_out, g_two)


def in_core_order(core_ref, mine, theirs):
    core, mine, theirs = core_ref[0], mine.astype(f32), theirs.astype(f32)
    return jnp.where(core == 0, mine, theirs), jnp.where(core == 0, theirs, mine)


def final_feed_kernel(core_ref, mine_ref, theirs_ref, up_ref, down_ref):
    for i in range(16):
        for c, piece in enumerate(in_core_order(core_ref, mine_ref[i], theirs_ref[i])):
            if i < 8:
                base = 1280 * (i // 2) + 640 * c
                up_ref[80 * (i % 2):80 * (i % 2 + 1), base:base + 640] = piece
            else:
                base = 640 * c + 80 * (i - 8)
                down_ref[base:base + 80, :] = piece


def final_feed(core, mine, theirs):
    return call(final_feed_kernel, (shape(160, 5120, dtype=f32), shape(1280, 640, dtype=f32)), "final_feed", 10**6, 32, **scalar_first(
        (1,), [full(16, 80, 640)] * 2, [full(160, 5120), full(1280, 640)]))(core, mine, theirs)


def final_heads_kernel(core_ref, mine_ref, theirs_ref, qkv_ref, out_ref, vec_ref):
    lane = lax.broadcasted_iota(jnp.int32, (40, 128), 1)
    for z in range(4):
        rows = slice(40 * z, 40 * (z + 1))
        for x in range(4):
            a, b = in_core_order(core_ref, mine_ref[4 * z + x], theirs_ref[4 * z + x])
            if x < 3:
                last = jnp.where(lane < 64, a[:, 256:], b[:, 256:])
                qkv_ref[rows, 640 * x:640 * (x + 1)] = jnp.concatenate([a[:, :256], b[:, :256], last], axis=1)
            else:
                out_ref[rows, :] = jnp.concatenate([a, b[:, 128:]], axis=1)
            if x == 0:
                vec_ref[rows, :] = pltpu.roll(a[:, 256:], 64, 1) + b[:, 256:]


def final_heads(core, mine, theirs):
    return call(
        final_heads_kernel, (shape(160, 1920, dtype=f32), shape(160, 640, dtype=f32), shape(160, 128, dtype=f32)), "final_heads", 10**6, 16,
        **scalar_first((1,), [full(16, 40, 384)] * 2, [full(160, 1920), full(160, 640), full(160, 128)]))(core, mine, theirs)


def shifted(array, axis, by):
    devices = lax.axis_size(axis)
    return lax.ppermute(array, axis, [(i, (i + by) % devices) for i in range(devices)])


def passed_along(array, by):
    devices = lax.axis_size(("z", "x"))
    return lax.ppermute(array, ("z", "x"), [(i, i + by) for i in range(devices) if 0 <= i + by < devices])


def swapped(array):
    return lax.ppermute(array, "core", [(0, 1), (1, 0)])


def pick(array, index):
    return lax.dynamic_index_in_dim(array, index, 0, keepdims=False)


def summed_share(array, axis):
    me, devices = lax.axis_index(axis), lax.axis_size(axis)
    total = pick(array, me).astype(f32)
    for by in (1, devices - 1, 2):
        total = total + shifted(pick(array, (me + by) % devices), axis, by).astype(f32)
    return total.astype(bf16)


def gathered(array, axis):
    me, devices = lax.axis_index(axis), lax.axis_size(axis)
    out = jnp.zeros((devices,) + array.shape, array.dtype)
    out = lax.dynamic_update_index_in_dim(out, array, me, 0)
    for by in (1, devices - 1, 2):
        out = lax.dynamic_update_index_in_dim(out, shifted(array, axis, by), (me + devices - by) % devices, 0)
    return out


def gathered_ring(array, axis):
    me, half = lax.axis_index(axis), array.shape[0] // 2
    before, after = shifted(array, axis, 1), shifted(array, axis, -1)
    far = jnp.concatenate([shifted(before[:half], axis, 1), shifted(after[half:], axis, -1)])
    out = jnp.zeros((4,) + array.shape, array.dtype)
    for by, part in ((0, array), (3, before), (1, after), (2, far)):
        out = lax.dynamic_update_index_in_dim(out, part, (me + by) % 4, 0)
    return out


def window_info(length_row, chip, core, win):
    ends = jnp.cumsum(length_row)
    starts = ends - length_row
    base = chip * 512 - 1024
    places = base + jnp.arange(win, dtype=jnp.int32)
    inside = (places[:, None] >= starts[None, :]) & (places[:, None] < ends[None, :])
    ones = jnp.broadcast_to(jnp.arange(64) < 3, (win, 64)).astype(bf16)
    key_rows = jnp.concatenate([jnp.where(inside, 0.0, -BIG).astype(bf16), ones], axis=1)
    own = chip * 512 + jnp.arange(512, dtype=jnp.int32)
    inside_q = (own[None, :] >= starts[:, None]) & (own[None, :] < ends[:, None])
    query_rows = jnp.concatenate([inside_q.astype(bf16), jnp.zeros((64, 512), bf16)], axis=0)
    info = [core]
    sizes = []
    for t in range(2):
        first = chip * 512 + t * TILE
        low = jnp.max(jnp.where(starts <= first, starts, 0)) - base
        high = jnp.min(jnp.where(ends > first + TILE - 1, ends, 1 << 30)) - base
        start = low // 128 * 128
        need = high - start
        size = (need + SHORT - 1) // SHORT * SHORT
        info.append(jnp.minimum(start, win - size))
        sizes.append(size)
    low = jnp.minimum(info[1], info[2]) // 512
    high = (jnp.maximum(info[1] + sizes[0], info[2] + sizes[1]) + 511) // 512
    return jnp.stack(info + sizes).astype(jnp.int32), key_rows, query_rows, [low, high]


def body(tokens, lengths, gain_one, bias_one, w_qkv, w_out, gain_two, bias_two, w_up, w_down, cotangent):
    core, chip = lax.axis_index("core"), lax.axis_index(("z", "x"))
    core_arg, y_arg = core[None].astype(jnp.int32), lax.axis_index("batch")[None].astype(jnp.int32)
    tok, cot = tokens[:, 0], cotangent[:, 0].reshape(512, 640)

    before, after = passed_along(tok, 1), passed_along(tok, -1)
    vectors = jnp.pad(jnp.stack([gain_one, bias_one, gain_two, bias_two]), ((0, 12), (0, 0)))
    heads = pack_heads(core_arg, w_qkv, vectors)
    heads_before, heads_after = shifted(heads, "batch", 1), shifted(heads, "batch", -1)
    feed_weights = lax.all_gather(pack_feed(core_arg, w_out, w_up, w_down), "batch", axis=0, tiled=True)
    own = (passed_along(before, 1), before, tok, after, passed_along(after, -1))
    near, far = shifted(heads_before[:96], "batch", 1), shifted(heads_after[96:], "batch", -1)
    other = tuple(swapped(a) for a in own)
    w_heads, vec = assemble(y_arg, heads, heads_before, heads_after, near, far)

    windows = [window_info(lengths[m, 0], chip, core, 2560) for m in range(2)]
    place = jnp.stack([core] + windows[0][3] + windows[1][3]).astype(jnp.int32)
    forward = []
    for m in range(2):
        k, v, kT, vT, q, qT = project(m, place, own, other, vec, w_heads)
        info, key_rows, query_rows, _ = windows[m]
        oT, low, lse = attend(info, qT, k, vT, key_rows, query_rows)
        forward.append((info, qT, q, k, kT, v, oT, lse, key_rows, query_rows, low))

    low = jnp.stack([f[-1] for f in forward])
    theirs = swapped(low)
    middle, hidden_two = middle_step(core_arg, low, theirs, tok, feed_weights, vec)
    out, d_hidden, partial, feed_grads = feed_forward(hidden_two, swapped(hidden_two), cot, swapped(cot), feed_weights)
    feed_grads = lax.psum_scatter(feed_grads.reshape(5120, 640), ("z", "x"), scatter_dimension=0, tiled=True).reshape(4, 80, 640)
    block_out, grad_middle, branch, g_two = after_feed(middle, out, d_hidden, swapped(partial), cot, vec)

    do, doT, g_out = branch_step(core_arg, branch, swapped(branch), feed_weights, low, theirs)
    grads = []
    for m in range(2):
        info, qT, q, k, kT, v, oT, lse, key_rows, query_rows, _ = forward[m]
        grads.append(attend_back(m, info, qT, q, k, kT, v, doT, do, oT, lse, key_rows, query_rows))
    dq, dk, dv = zip(*grads)
    mine, theirs, tail = project_back(place, own, other, vec, w_heads, dq, dk, dv, g_out, g_two)
    tail = lax.all_to_all(tail, ("batch", "z", "x"), 0, 0, tiled=True)

    theirs = swapped(theirs)
    sums = [mine[:, j].astype(f32) + theirs[:, j].astype(f32) for j in range(5)]
    right = passed_along(sums[4].astype(bf16), 1).astype(f32) + sums[3]
    left = passed_along(sums[0].astype(bf16), -1).astype(f32) + sums[1]
    d_one = sums[2] + passed_along(right.astype(bf16), 1).astype(f32) + passed_along(left.astype(bf16), -1).astype(f32)
    n_one, r_one = moments(tok.reshape(512, 640).astype(f32))
    grad_tokens = (grad_middle + norm_back(d_one.reshape(512, 640), n_one, r_one, vec[0:1])).astype(bf16)

    feed = gathered(summed_share(feed_grads, "batch"), "x").reshape(320, 640)
    feed = gathered_ring(feed, "z").reshape(16, 80, 640)
    grad_up, grad_down = final_feed(core_arg, feed, swapped(feed))
    tail, grad_tokens, grad_up = lax.optimization_barrier((tail, grad_tokens, grad_up))
    tail = jnp.sum(tail.astype(f32), axis=0).astype(bf16)
    tail = gathered(gathered(tail, "x").reshape(160, 384), "z").reshape(16, 40, 384)
    grad_qkv, grad_out, spare = final_heads(core_arg, tail, swapped(tail))
    return (
        block_out.reshape(2, 1, 256, 640), grad_tokens.reshape(2, 1, 256, 640), spare[:, 0], spare[:, 1], grad_qkv, grad_out,
        spare[:, 2], spare[:, 3], grad_up, grad_down)


def solution(mesh):
    fine = Mesh(mesh.devices.reshape(4, 4, 4, 2), ("batch", "z", "x", "core"))
    rows = P(None, "batch", ("z", "x", "core"), None)
    one, two = P("batch"), P("batch", None)
    return jax.shard_map(
        body,
        mesh=fine,
        in_specs=(rows, P(None, "batch", None), one, one, two, two, one, one, two, two, rows),
        out_specs=(rows, rows, one, one, two, two, one, one, two, two),
        check_vma=False,
    )
```

```python
import math

import jax
import jax.numpy as jnp
from jax import lax
from jax.experimental import pallas as pl
from jax.experimental.pallas import tpu as pltpu
from jax.sharding import Mesh
from jax.sharding import PartitionSpec as P

HEAD_DIM = 32
SCALE = HEAD_DIM ** -0.5
LOG2E = math.log2(math.e)
C2 = SCALE * LOG2E
BIG = 1e30
TILE = 256
EPSILON = 1e-05
PAIRS = 5
SHORT, LONG = 384, 1152
f32, bf16 = jnp.float32, jnp.bfloat16
NT = (((1,), (1,)), ((), ()))


def pair_offset(info_ref):
    p = pl.program_id(0)
    sub = jnp.where(p == PAIRS - 1, info_ref[0], lax.rem(p, 2))
    return sub * (2 * HEAD_DIM)


def split3(v):
    a = v.astype(bf16)
    r = v - a.astype(f32)
    b = r.astype(bf16)
    d = (r - b.astype(f32)).astype(bf16)
    return a, b, d


def rows_masked(xT, off):
    row = lax.broadcasted_iota(jnp.int32, xT.shape, 0) - off
    xf = xT.astype(f32)
    return [jnp.where((row >= HEAD_DIM * j) & (row < HEAD_DIM * (j + 1)), xf, 0.0).astype(bf16) for j in range(2)]


def lanes_masked(x, off):
    lane = lax.broadcasted_iota(jnp.int32, x.shape, 1) - off
    xf = x.astype(f32)
    return [jnp.where((lane >= HEAD_DIM * j) & (lane < HEAD_DIM * (j + 1)), xf, 0.0).astype(bf16) for j in range(2)]


def attend_kernel(info_ref, qT_ref, k_ref, vT_ref, kaug_ref, qaugT_ref, oT_ref, o_ref, l_ref, rhs):
    off = pair_offset(info_ref)
    oT_ref[...] = jnp.where(lax.rem(pl.program_id(0), 2) == 0, 0.0, oT_ref[...])
    for t in range(2):
        cols = slice(t * TILE, (t + 1) * TILE)
        masked = rows_masked(qT_ref[:, cols], off)
        for j in range(2):
            rhs[0:128, j * TILE:(j + 1) * TILE] = masked[j]
            rhs[128:256, j * TILE:(j + 1) * TILE] = qaugT_ref[:, cols]
        start = info_ref[1 + t]
        need = info_ref[3 + t]

        def block(first, size):
            def step(i, carry):
                row = pl.multiple_of(first + i * size, 128)
                lhs = jnp.concatenate([k_ref[pl.ds(row, size), :], kaug_ref[pl.ds(row, size), :]], axis=1)
                raw = [jnp.dot(lhs, rhs[:, j * TILE:(j + 1) * TILE], preferred_element_type=f32) for j in range(2)]
                out = []
                for j in range(2):
                    m, l, o = carry[j]
                    s = raw[j] * C2
                    m_new = jnp.maximum(m, jnp.max(s, axis=0, keepdims=True))
                    alpha = jnp.exp2(m - m_new)
                    p = jnp.exp2(s - m_new)
                    vT = vT_ref[pl.ds(pl.multiple_of(off + j * HEAD_DIM, HEAD_DIM), HEAD_DIM), pl.ds(row, size)]
                    out.append((m_new, l * alpha + jnp.sum(p, axis=0, keepdims=True),
                                o * alpha + jnp.dot(vT, p.astype(bf16), preferred_element_type=f32)))
                return tuple(out)
            return step

        def finish(state):
            for j in range(2):
                m, l, o = state[j]
                oT_ref[pl.ds(pl.multiple_of(off + j * HEAD_DIM, HEAD_DIM), HEAD_DIM), cols] = o * (1.0 / l)
                l_ref[0, j:j + 1, cols] = m + jnp.log2(l)

        init = tuple((jnp.full((1, TILE), -1e38, f32), jnp.zeros((1, TILE), f32), jnp.zeros((HEAD_DIM, TILE), f32)) for _ in range(2))

        longs = lax.div(need, LONG)
        state = lax.fori_loop(0, longs, block(start, LONG), init)
        finish(lax.fori_loop(0, lax.div(need - longs * LONG, SHORT), block(start + longs * LONG, SHORT), state))

    o_ref[...] = oT_ref[...].T.astype(bf16)


def attend(info, qT, k, vT, kaug, qaugT):
    win = k.shape[0]
    nq = qT.shape[1]
    group = lambda p, *_: p // 2
    return pl.pallas_call(
        attend_kernel,
        out_shape=(jax.ShapeDtypeStruct((384, nq), f32), jax.ShapeDtypeStruct((nq, 384), bf16), jax.ShapeDtypeStruct((PAIRS, 8, nq), f32)),
        grid_spec=pltpu.PrefetchScalarGridSpec(
            num_scalar_prefetch=1, grid=(PAIRS,),
            in_specs=[
                pl.BlockSpec((128, nq), lambda p, *_: (p // 2, 0)),
                pl.BlockSpec((win, 128), lambda p, *_: (0, p // 2)),
                pl.BlockSpec((128, win), lambda p, *_: (p // 2, 0)),
                pl.BlockSpec((win, 128), lambda p, *_: (0, 0)),
                pl.BlockSpec((128, nq), lambda p, *_: (0, 0)),
            ],
            out_specs=[
                pl.BlockSpec((128, nq), lambda p, *_: (p // 2, 0)),
                pl.BlockSpec((nq, 128), lambda p, *_: (0, p // 2)),
                pl.BlockSpec((1, 8, nq), lambda p, *_: (p, 0, 0)),
            ],
            scratch_shapes=[pltpu.VMEM((256, 2 * TILE), bf16)],
        ),
        compiler_params=pltpu.CompilerParams(vmem_limit_bytes=28 << 20),
        cost_estimate=pl.CostEstimate(flops=20 * 10**9, bytes_accessed=6 << 20, transcendentals=5 * 10**6),
        name="attend",
    )(info, qT, k, vT, kaug, qaugT)


def attend_back_kernel(info_ref, qT_ref, q_ref, k_ref, kT_ref, v_ref, doT_ref, do_ref, oT_ref, l_ref, kaug_ref, qaugT_ref,
                       dq_ref, dk_ref, dv_ref, dqT_ref, rhs_s, rhs_d, q_stk, do_stk, dk_acc, dv_acc):
    p_id = pl.program_id(0)
    off = pair_offset(info_ref)

    @pl.when(lax.rem(p_id, 2) == 0)
    def _():
        dqT_ref[...] = jnp.zeros_like(dqT_ref)
        dk_acc[...] = jnp.zeros_like(dk_acc)
        dv_acc[...] = jnp.zeros_like(dv_acc)

    for t in range(2):
        cols = slice(t * TILE, (t + 1) * TILE)
        masked_q = rows_masked(qT_ref[:, cols], off)
        masked_do = rows_masked(doT_ref[:, cols], off)
        lane_q = lanes_masked(q_ref[cols, :], off)
        lane_do = lanes_masked(do_ref[cols, :], off)
        for j in range(2):
            part = slice(j * TILE, (j + 1) * TILE)
            head = pl.ds(pl.multiple_of(off + j * HEAD_DIM, HEAD_DIM), HEAD_DIM)
            delta = jnp.sum(doT_ref[head, cols].astype(f32) * oT_ref[head, cols], axis=0, keepdims=True)
            total = l_ref[0, j:j + 1, cols] * (1.0 / C2)
            rowid = lax.broadcasted_iota(jnp.int32, (64, TILE), 0)
            lp, dp = split3(-total), split3(-delta)
            def pieces(parts):
                x = jnp.zeros((64, TILE), f32)
                for n in range(3):
                    x = jnp.where(rowid == n, parts[n].astype(f32), x)
                return x.astype(bf16)
            rhs_s[0:128, part] = masked_q[j]
            rhs_s[128:192, part] = qaugT_ref[0:64, cols]
            rhs_s[192:256, part] = pieces(lp)
            rhs_d[0:128, part] = masked_do[j]
            rhs_d[128:192, part] = jnp.zeros((64, TILE), bf16)
            rhs_d[192:256, part] = pieces(dp)
            q_stk[part, :] = lane_q[j]
            do_stk[part, :] = lane_do[j]
        start = info_ref[1 + t]
        need = info_ref[3 + t]

        def block(first, size):
            def step(i, carry):
                row = pl.multiple_of(first + i * size, 128)
                rows = pl.ds(row, size)
                aug = kaug_ref[rows, :]
                lhs_k = jnp.concatenate([k_ref[rows, :], aug], axis=1)
                lhs_v = jnp.concatenate([v_ref[rows, :], aug], axis=1)
                out, dv, dk = [], dv_acc[rows, :], dk_acc[rows, :]
                for j in range(2):
                    part = slice(j * TILE, (j + 1) * TILE)
                    s = jnp.dot(lhs_k, rhs_s[:, part], preferred_element_type=f32)
                    dp = jnp.dot(lhs_v, rhs_d[:, part], preferred_element_type=f32)
                    p = jnp.exp2(s * C2)
                    ds = (p * dp).astype(bf16)
                    dv = dv + jnp.dot(p.astype(bf16), do_stk[part, :], preferred_element_type=f32)
                    dk = dk + jnp.dot(ds, q_stk[part, :], preferred_element_type=f32)
                    kT = kT_ref[pl.ds(pl.multiple_of(off + j * HEAD_DIM, HEAD_DIM), HEAD_DIM), rows]
                    out.append(carry[j] + jnp.dot(kT, ds, preferred_element_type=f32))
                dv_acc[rows, :] = dv
                dk_acc[rows, :] = dk
                return tuple(out)
            return step

        def finish(dqs):
            for j in range(2):
                dqT_ref[pl.ds(pl.multiple_of(off + j * HEAD_DIM, HEAD_DIM), HEAD_DIM), cols] = dqs[j] * SCALE

        init = tuple(jnp.zeros((HEAD_DIM, TILE), f32) for _ in range(2))

        longs = lax.div(need, LONG)
        state = lax.fori_loop(0, longs, block(start, LONG), init)
        finish(lax.fori_loop(0, lax.div(need - longs * LONG, SHORT), block(start + longs * LONG, SHORT), state))
    @pl.when((lax.rem(p_id, 2) == 1) | (p_id == PAIRS - 1))
    def _():
        dq_ref[...] = dqT_ref[...].T.astype(bf16)
        dk_ref[...] = (dk_acc[...] * SCALE).astype(bf16)
        dv_ref[...] = dv_acc[...].astype(bf16)


def attend_back(m, info, qT, q, k, kT, v, doT, do, oT, lse, kaug, qaugT):
    win, nq = k.shape[0], qT.shape[1]
    wide = pl.BlockSpec((128, nq), lambda p, *_: (p // 2, 0))
    tall = pl.BlockSpec((nq, 128), lambda p, *_: (0, p // 2))
    keys = pl.BlockSpec((win, 128), lambda p, *_: (0, p // 2))
    return pl.pallas_call(
        attend_back_kernel,
        out_shape=(jax.ShapeDtypeStruct((nq, 384), bf16), jax.ShapeDtypeStruct((win, 384), bf16), jax.ShapeDtypeStruct((win, 384), bf16)),
        grid_spec=pltpu.PrefetchScalarGridSpec(
            num_scalar_prefetch=1, grid=(PAIRS,),
            in_specs=[wide, tall, keys, pl.BlockSpec((128, win), lambda p, *_: (p // 2, 0)), keys,
                      pl.BlockSpec((128, nq), lambda p, *_: (p // 2, m)), pl.BlockSpec((nq, 128), lambda p, *_: (m, p // 2)), wide,
                      pl.BlockSpec((1, 8, nq), lambda p, *_: (p, 0, 0)),
                      pl.BlockSpec((win, 128), lambda p, *_: (0, 0)), pl.BlockSpec((128, nq), lambda p, *_: (0, 0))],
            out_specs=[tall, keys, keys],
            scratch_shapes=[pltpu.VMEM((128, nq), f32), pltpu.VMEM((256, 2 * TILE), bf16), pltpu.VMEM((256, 2 * TILE), bf16),
                            pltpu.VMEM((2 * TILE, 128), bf16), pltpu.VMEM((2 * TILE, 128), bf16),
                            pltpu.VMEM((win, 128), f32), pltpu.VMEM((win, 128), f32)],
        ),
        compiler_params=pltpu.CompilerParams(vmem_limit_bytes=32 << 20),
        cost_estimate=pl.CostEstimate(flops=40 * 10**9, bytes_accessed=12 << 20, transcendentals=5 * 10**6),
        name="attend_back",
    )(info, qT, q, k, kT, v, doT, do, oT, lse, kaug, qaugT)


def moments(x):
    centred = x - jnp.mean(x, axis=-1, keepdims=True)
    r = lax.rsqrt(jnp.mean(centred * centred, axis=-1, keepdims=True) + EPSILON)
    return centred * r, r


def norm_back(grad, n, r, gain):
    e = grad * gain
    return r * (e - jnp.mean(e, axis=-1, keepdims=True) - n * jnp.mean(e * n, axis=-1, keepdims=True))


def call(kernel, out_shape, name, flops=10**9, limit=48, **spec):
    return pl.pallas_call(
        kernel, out_shape=out_shape, name=name,
        compiler_params=pltpu.CompilerParams(vmem_limit_bytes=limit << 20),
        cost_estimate=pl.CostEstimate(flops=flops, bytes_accessed=8 << 20, transcendentals=0), **spec)


def shape(*dims, dtype=bf16):
    return jax.ShapeDtypeStruct(dims, dtype)


def scalar_first(grid, in_specs, out_specs, scratch=()):
    return dict(grid_spec=pltpu.PrefetchScalarGridSpec(
        num_scalar_prefetch=1, grid=grid, in_specs=in_specs, out_specs=out_specs, scratch_shapes=list(scratch)))


def full(*dims):
    return pl.BlockSpec(dims, lambda *_: (0,) * len(dims))


def pack_heads_kernel(core_ref, qkv_ref, vec_ref, heads_ref):
    for part in range(3):
        near = pl.ds(pl.multiple_of(640 * part + 256 * core_ref[0], 128), 256)
        heads_ref[0:160, 384 * part:384 * part + 256] = qkv_ref[:, near]
        heads_ref[0:160, 384 * part + 256:384 * (part + 1)] = qkv_ref[:, 640 * part + 512:640 * (part + 1)]
    heads_ref[160:176, :] = jnp.zeros((16, 1152), bf16)
    heads_ref[160:176, 0:160] = vec_ref[...]


def pack_heads(core, w_qkv, vectors):
    return call(pack_heads_kernel, shape(176, 1152), "pack_heads", 10**6, 8, **scalar_first(
        (1,), [full(160, 1920), full(16, 160)], full(176, 1152)))(core, w_qkv, vectors)


def pack_feed_kernel(core_ref, out_ref, up_ref, down_ref, feed_ref):
    core = core_ref[0]
    for f in range(4):
        feed_ref[:, 640 * f:640 * (f + 1)] = up_ref[:, pl.ds(pl.multiple_of(1280 * f + 640 * core, 128), 640)]
        feed_ref[:, 2560 + 640 * f:2560 + 640 * (f + 1)] = down_ref[pl.ds(pl.multiple_of(640 * core + 160 * f, 32), 160), :]
    feed_ref[:, 5120:5760] = out_ref[...]


def pack_feed(core, w_out, w_up, w_down):
    args = (w_out, w_up, w_down)
    return call(pack_feed_kernel, shape(160, 5760), "pack_feed", 10**6, 16, **scalar_first(
        (1,), [full(*a.shape) for a in args], full(160, 5760)))(core, *args)


def assemble_kernel(y_ref, own_ref, before_ref, after_ref, near_ref, far_ref, heads_ref, vec_ref):
    total = jnp.zeros((16, 640), f32)

    def place(by, top, bottom, vec):
        nonlocal total
        row = lax.rem(y_ref[0] + by, 4) * 160
        for part, base in ((top, 0), (bottom, top.shape[0])):
            heads_ref[pl.ds(pl.multiple_of(row + base, 32), part.shape[0]), :] = part
        total = total + pltpu.roll(vec[:, :640].astype(f32), row, 1)

    for by, ref in ((0, own_ref), (3, before_ref), (1, after_ref)):
        place(by, ref[0:96, :], ref[96:160, :], ref[160:176, :])
    place(2, near_ref[...], far_ref[0:64, :], far_ref[64:80, :])
    vec_ref[...] = total


def assemble(y, *parts):
    return call(assemble_kernel, (shape(640, 1152), shape(16, 640, dtype=f32)), "assemble", 10**6, 12, **scalar_first(
        (1,), [full(*a.shape) for a in parts], [full(640, 1152), full(16, 640)]))(y, *parts)


def rows_in_order(core, mine, theirs, x_ref):
    mine, theirs = mine.astype(f32), theirs.astype(f32)
    x_ref[0:256, :] = jnp.where(core == 0, mine, theirs)
    x_ref[256:512, :] = jnp.where(core == 0, theirs, mine)


def window_rows(core, own_refs, other_refs, m, block, x_ref):
    for j in range(len(own_refs)):
        @pl.when(block == j)
        def _():
            rows_in_order(core, own_refs[j][m], other_refs[j][m], x_ref)


def project_kernel(m, chips, place_ref, *refs):
    n = len(chips)
    own_refs, other_refs = refs[:n], refs[n:2 * n]
    vec_ref, w_ref = refs[2 * n:2 * n + 2]
    k_ref, v_ref, kT_ref, vT_ref = refs[-6 - 2 * (n == 3):][:4]
    x_ref, hid_ref = refs[-2:]
    step = pl.program_id(0)
    block = sum(jnp.where(step == i, chip, 0) for i, chip in enumerate(chips))
    needed = (block >= place_ref[1 + 2 * m]) & (block < place_ref[2 + 2 * m])

    @pl.when(jnp.logical_not(needed))
    def _():
        for ref in (k_ref, v_ref, kT_ref, vT_ref):
            ref[...] = jnp.zeros_like(ref)

    @pl.when(needed)
    def _():
        window_rows(place_ref[0], own_refs, other_refs, m, step, x_ref)
        hidden = (moments(x_ref[...])[0] * vec_ref[0:1, :] + vec_ref[1:2, :]).astype(bf16)
        hid_ref[...] = hidden
        kv = jnp.dot(hidden, w_ref[:, 384:], preferred_element_type=f32)
        low = kv.astype(bf16)
        k_ref[...] = low[:, :384]
        v_ref[...] = low[:, 384:]
        turned = kv.T.astype(bf16)
        kT_ref[...] = turned[:384]
        vT_ref[...] = turned[384:]

    if n == 3:
        q_ref, qT_ref = refs[-4:-2]

        @pl.when(step == 1)
        def _():
            q = jnp.dot(hid_ref[...], w_ref[:, :384], preferred_element_type=f32)
            q_ref[...] = q.astype(bf16)
            qT_ref[...] = q.T.astype(bf16)


def project(m, chips, place, own, other, vec, w, earlier=()):
    n = len(chips)
    chip = (lambda b: b + 1) if n == 3 else (lambda b: 4 * b)
    tall, wide = pl.BlockSpec((512, 384), lambda b, *_: (chip(b), 0)), pl.BlockSpec((384, 512), lambda b, *_: (0, chip(b)))
    shapes = [shape(2560, 384), shape(2560, 384), shape(384, 2560), shape(384, 2560)]
    specs = [tall, tall, wide, wide]
    if n == 3:
        shapes, specs = shapes + [shape(512, 384), shape(384, 512)], specs + [full(512, 384), full(384, 512)]
    own, other = [own[c] for c in chips], [other[c] for c in chips]
    return call(
        lambda *refs: project_kernel(m, chips, *refs), shapes, "project", 5 * 10**9, 28,
        input_output_aliases={2 * n + 3 + i: i for i in range(len(earlier))}, **scalar_first(
            (n,), [full(2, 256, 640)] * (2 * n) + [full(16, 640), full(640, 1152)] + [pl.BlockSpec(memory_space=pl.ANY)] * len(earlier),
            specs, [pltpu.VMEM((512, 640), f32), pltpu.VMEM((512, 640), bf16)]))(place, *own, *other, vec, w, *earlier)


def heads_joined(core, mine, theirs):
    first, second = (jnp.where(core == 0, a, b) for a, b in ((mine, theirs), (theirs, mine)))
    return jnp.concatenate([first[:, :256], second[:, :256], first[:, 256:] + second[:, 256:]], axis=1)


def middle_kernel(core_ref, low_ref, theirs_ref, tok_ref, w_ref, vec_ref, mid_ref, hid_ref):
    core = core_ref[0]
    rows = pl.ds(pl.multiple_of(256 * core, 256), 256)
    for m in range(2):
        attended = heads_joined(core, low_ref[m, rows, :].astype(f32), theirs_ref[m, rows, :].astype(f32)).astype(bf16)
        part = slice(256 * m, 256 * (m + 1))
        middle = tok_ref[m].astype(f32) + jnp.dot(attended, w_ref[...], preferred_element_type=f32)
        mid_ref[part, :] = middle
        hid_ref[part, :] = (moments(middle)[0] * vec_ref[2:3, :] + vec_ref[3:4, :]).astype(bf16)


def middle_step(core, low, theirs, tok, w, vec):
    args = (low, theirs, tok, w, vec)
    specs = [full(*a.shape) for a in args]
    return call(middle_kernel, (shape(512, 640, dtype=f32), shape(512, 640)), "middle", 10**9, 16, **scalar_first(
        (1,), specs, [full(512, 640), full(512, 640)]))(core, *args)


def feed_kernel(h_ref, h2_ref, cot_ref, cot2_ref, up_ref, down_ref, out_ref, dh_ref, theirs_ref, g_ref, h, cot, hT, cT, out, dh):
    chunk = pl.program_id(0)

    @pl.when(chunk == 0)
    def _():
        h[0:512, :], h[512:1024, :] = h_ref[...], h2_ref[...]
        cot[0:512, :], cot[512:1024, :] = cot_ref[...], cot2_ref[...]
        hT[...] = h[...].astype(f32).T.astype(bf16)
        cT[...] = cot[...].astype(f32).T.astype(bf16)
        out[...] = jnp.zeros_like(out)
        dh[...] = jnp.zeros_like(dh)

    up_w = up_ref[...]
    down_w = jnp.concatenate([down_ref[160 * y:160 * (y + 1), 640 * i:640 * (i + 1)] for y in range(2) for i in range(4)], axis=0)
    acts, d_ups = [], []
    for t in range(4):
        rows = slice(256 * t, 256 * (t + 1))
        u = jnp.dot(h[rows, :], up_w, preferred_element_type=f32)
        d_act = lax.dot_general(cot[rows, :], down_w, NT, preferred_element_type=f32)
        cdf = 0.5 * (1.0 + lax.erf(u * (2.0 ** -0.5)))
        pdf = jnp.exp(u * u * -0.5) * ((2.0 * math.pi) ** -0.5)
        act = (u * cdf).astype(bf16)
        d_up = (d_act * (cdf + u * pdf)).astype(bf16)
        out[rows, :] += jnp.dot(act, down_w, preferred_element_type=f32)
        dh[rows, :] += lax.dot_general(d_up, up_w, NT, preferred_element_type=f32)
        acts.append(act)
        d_ups.append(d_up)
    g_up = jnp.dot(hT[...], jnp.concatenate(d_ups, axis=0), preferred_element_type=f32).astype(bf16)
    g_down = jnp.dot(cT[...], jnp.concatenate(acts, axis=0), preferred_element_type=f32).T.astype(bf16)
    for f in range(2):
        for y in range(4):
            for i in range(2):
                g_ref[4 * chunk + 2 * f + i, y] = g_up[160 * y + 80 * i:160 * y + 80 * (i + 1), 640 * f:640 * (f + 1)]
        for i in range(8):
            g_ref[8 + i, 2 * chunk + f] = g_down[640 * f + 80 * i:640 * f + 80 * (i + 1)]

    @pl.when(chunk == 1)
    def _():
        out_ref[...], dh_ref[...] = out[0:512, :], dh[0:512, :]
        theirs_ref[0], theirs_ref[1] = out[512:1024, :].astype(bf16), dh[512:1024, :].astype(bf16)


def feed_forward(h, h2, cot, cot2, weights):
    return call(
        feed_kernel,
        (shape(512, 640, dtype=f32), shape(512, 640, dtype=f32), shape(2, 512, 640), shape(16, 4, 80, 640)),
        "feed_forward", 30 * 10**9, 52, grid=(2,),
        in_specs=[full(512, 640)] * 4 + [pl.BlockSpec((640, 1280), lambda f: (0, f)), pl.BlockSpec((320, 2560), lambda f: (f, 1))],
        out_specs=[full(512, 640), full(512, 640), full(2, 512, 640), full(16, 4, 80, 640)],
        scratch_shapes=[pltpu.VMEM((1024, 640), bf16), pltpu.VMEM((1024, 640), bf16), pltpu.VMEM((640, 1024), bf16), pltpu.VMEM((640, 1024), bf16),
                        pltpu.VMEM((1024, 640), f32), pltpu.VMEM((1024, 640), f32)],
    )(h, h2, cot, cot2, weights, weights)


def after_kernel(mid_ref, out_ref, dh_ref, theirs_ref, cot_ref, vec_ref, block_ref, grad_ref, branch_ref, g_ref):
    middle = mid_ref[...]
    block_ref[...] = (middle + out_ref[...] + theirs_ref[0].astype(f32)).astype(bf16)
    d_hidden = dh_ref[...] + theirs_ref[1].astype(f32)
    n, r = moments(middle)
    g_ref[...] = jnp.zeros_like(g_ref)
    g_ref[0:1, :] = jnp.sum(d_hidden * n, axis=0, keepdims=True)
    g_ref[1:2, :] = jnp.sum(d_hidden, axis=0, keepdims=True)
    grad = cot_ref[...].astype(f32) + norm_back(d_hidden, n, r, vec_ref[2:3, :])
    grad_ref[...] = grad
    branch_ref[...] = grad.astype(bf16)


def after_feed(middle, out, dh, theirs, cot, vec):
    args = (middle, out, dh, theirs, cot, vec)
    return call(
        after_kernel, (shape(512, 640), shape(512, 640, dtype=f32), shape(512, 640), shape(8, 640, dtype=f32)), "after_feed", 10**9, 24,
        in_specs=[pl.BlockSpec(memory_space=pltpu.VMEM)] * 6, out_specs=[pl.BlockSpec(memory_space=pltpu.VMEM)] * 4)(*args)


def branch_kernel(core_ref, own_ref, their_ref, w_ref, low_ref, theirs_ref, do_ref, doT_ref, g_ref):
    core = core_ref[0]
    w = jnp.concatenate([w_ref[pl.ds(pl.multiple_of(256 * core, 256), 256), :], w_ref[512:640, :]], axis=0)
    g = jnp.zeros((640, 384), f32)
    for m in range(2):
        part = slice(256 * m, 256 * (m + 1))
        mine, theirs = own_ref[part, :].astype(f32), their_ref[part, :].astype(f32)
        branch = jnp.concatenate([jnp.where(core == 0, mine, theirs), jnp.where(core == 0, theirs, mine)], axis=0)
        kept = jnp.where(core == 0, branch[:, :384], branch[:, 256:]).astype(bf16)
        branch = branch.astype(bf16)
        rows = slice(512 * m, 512 * (m + 1))
        do = lax.dot_general(branch, w, NT, preferred_element_type=f32)
        do_ref[rows, :] = do.astype(bf16)
        doT_ref[:, rows] = do.T.astype(bf16)
        attended = heads_joined(core, low_ref[m].astype(f32), theirs_ref[m].astype(f32))
        g = g + jnp.dot(attended.T.astype(bf16), kept, preferred_element_type=f32)
    g_ref[...] = g


def branch_step(core, own, their, w, low, theirs):
    args = (own, their, w, low, theirs)
    specs = [full(*a.shape) for a in args]
    return call(
        branch_kernel, (shape(1024, 384), shape(384, 1024), shape(640, 384, dtype=f32)), "branch", 10**9, 24, **scalar_first(
            (1,), specs, [full(1024, 384), full(384, 1024), full(640, 384)]))(core, *args)


def project_back_kernel(core_ref, *refs):
    own_refs, other_refs = refs[:5], refs[5:10]
    (vec_ref, w_ref, dq0_ref, dq1_ref, dk0_ref, dk1_ref, dv0_ref, dv1_ref, g_out_ref, g_two_ref,
     mine_ref, theirs_ref, tail_ref, x_ref, d_kv, d_q, d_hid, g_ref, g_vec) = refs[10:]
    step, core = pl.program_id(0), core_ref[0]
    block = lax.rem(step, 5)

    @pl.when(step == 0)
    def _():
        g_ref[...] = jnp.zeros_like(g_ref)
        g_vec[...] = jnp.zeros_like(g_vec)
        g_vec[2:4, :] = g_two_ref[0:2, :]

    second = lax.div(step, 5)
    needed = (block >= core_ref[1 + 2 * second]) & (block < core_ref[2 + 2 * second])

    @pl.when(jnp.logical_not(needed))
    def _():
        mine_ref[...] = jnp.zeros_like(mine_ref)
        theirs_ref[...] = jnp.zeros_like(theirs_ref)

    for m, (dq, dk, dv) in enumerate(((dq0_ref, dk0_ref, dv0_ref), (dq1_ref, dk1_ref, dv1_ref))):
        @pl.when(needed & (second == m))
        def _():
            window_rows(core, own_refs, other_refs, m, block, x_ref)
            d_kv[:, :384], d_kv[:, 384:] = dk[...], dv[...]
            d_q[...] = dq[...]

    @pl.when(needed)
    def _():
        n = moments(x_ref[...])[0]
        hiddenT = (n * vec_ref[0:1, :] + vec_ref[1:2, :]).T.astype(bf16)
        d_hid[...] = lax.dot_general(d_kv[...], w_ref[:, 384:], NT, preferred_element_type=f32)
        g_ref[:, 384:] += jnp.dot(hiddenT, d_kv[...], preferred_element_type=f32)

        @pl.when(block == 2)
        def _():
            g_ref[:, :384] += jnp.dot(hiddenT, d_q[...], preferred_element_type=f32)
            d_hid[...] += lax.dot_general(d_q[...], w_ref[:, :384], NT, preferred_element_type=f32)

        dh = d_hid[...]
        mine_ref[0, 0] = jnp.where(core == 0, dh[:256], dh[256:]).astype(bf16)
        theirs_ref[0, 0] = jnp.where(core == 0, dh[256:], dh[:256]).astype(bf16)
        g_vec[0:1, :] += jnp.sum(dh * n, axis=0, keepdims=True)
        g_vec[1:2, :] += jnp.sum(dh, axis=0, keepdims=True)

    @pl.when(step == 9)
    def _():
        turned = g_vec[...].T
        lane = lax.broadcasted_iota(jnp.int32, (640, 128), 1) - 64 * (1 - core)
        spare = g_ref[:, 256:384]
        for i in range(4):
            spare = jnp.where(lane == i, turned[:, i:i + 1], spare)
        g_ref[:, 256:384] = spare
        for y in range(4):
            for z in range(4):
                rows = slice(160 * y + 40 * z, 160 * y + 40 * (z + 1))
                for x in range(3):
                    tail_ref[16 * y + 4 * z + x] = g_ref[rows, 384 * x:384 * (x + 1)].astype(bf16)
                tail_ref[16 * y + 4 * z + 3] = g_out_ref[rows, :].astype(bf16)


def project_back(core, own, other, vec, w, dq, dk, dv, g_out, g_two):
    first = pl.BlockSpec((512, 384), lambda b, *_: (jnp.minimum(b, 4), 0))
    second = pl.BlockSpec((512, 384), lambda b, *_: (jnp.maximum(b - 5, 0), 0))
    return call(
        project_back_kernel, (shape(5, 2, 256, 640), shape(5, 2, 256, 640), shape(64, 40, 384)), "project_back", 10**10, 36, **scalar_first(
            (10,), [full(2, 256, 640)] * 10 + [full(16, 640), full(640, 1152), full(512, 384), full(512, 384), first, second, first, second,
                                               full(640, 384), full(8, 640)],
            [pl.BlockSpec((1, 1, 256, 640), lambda b, *_: (lax.rem(b, 5), b // 5, 0, 0))] * 2 + [full(64, 40, 384)],
            [pltpu.VMEM((512, 640), f32), pltpu.VMEM((512, 768), bf16), pltpu.VMEM((512, 384), bf16),
             pltpu.VMEM((512, 640), f32), pltpu.VMEM((640, 1152), f32), pltpu.VMEM((8, 640), f32)]))(core, *own, *other, vec, w, *dq, *dk, *dv, g_out, g_two)


def in_core_order(core_ref, mine, theirs):
    core, mine, theirs = core_ref[0], mine.astype(f32), theirs.astype(f32)
    return jnp.where(core == 0, mine, theirs), jnp.where(core == 0, theirs, mine)


def final_feed_kernel(core_ref, mine_ref, theirs_ref, up_ref, down_ref):
    for i in range(16):
        for c, piece in enumerate(in_core_order(core_ref, mine_ref[i], theirs_ref[i])):
            if i < 8:
                base = 1280 * (i // 2) + 640 * c
                up_ref[80 * (i % 2):80 * (i % 2 + 1), base:base + 640] = piece
            else:
                base = 640 * c + 80 * (i - 8)
                down_ref[base:base + 80, :] = piece


def final_feed(core, mine, theirs):
    return call(final_feed_kernel, (shape(160, 5120, dtype=f32), shape(1280, 640, dtype=f32)), "final_feed", 10**6, 32, **scalar_first(
        (1,), [full(16, 80, 640)] * 2, [full(160, 5120), full(1280, 640)]))(core, mine, theirs)


def final_heads_kernel(core_ref, mine_ref, theirs_ref, qkv_ref, out_ref, vec_ref):
    lane = lax.broadcasted_iota(jnp.int32, (40, 128), 1)
    for z in range(4):
        rows = slice(40 * z, 40 * (z + 1))
        for x in range(4):
            a, b = in_core_order(core_ref, mine_ref[4 * z + x], theirs_ref[4 * z + x])
            if x < 3:
                last = jnp.where(lane < 64, a[:, 256:], b[:, 256:])
                qkv_ref[rows, 640 * x:640 * (x + 1)] = jnp.concatenate([a[:, :256], b[:, :256], last], axis=1)
            else:
                out_ref[rows, :] = jnp.concatenate([a, b[:, 128:]], axis=1)
            if x == 0:
                vec_ref[rows, :] = pltpu.roll(a[:, 256:], 64, 1) + b[:, 256:]


def final_heads(core, mine, theirs):
    return call(
        final_heads_kernel, (shape(160, 1920, dtype=f32), shape(160, 640, dtype=f32), shape(160, 128, dtype=f32)), "final_heads", 10**6, 16,
        **scalar_first((1,), [full(16, 40, 384)] * 2, [full(160, 1920), full(160, 640), full(160, 128)]))(core, mine, theirs)


def shifted(array, axis, by):
    devices = lax.axis_size(axis)
    return lax.ppermute(array, axis, [(i, (i + by) % devices) for i in range(devices)])


def passed_along(array, by):
    devices = lax.axis_size(("z", "x"))
    return lax.ppermute(array, ("z", "x"), [(i, i + by) for i in range(devices) if 0 <= i + by < devices])


def swapped(array):
    return lax.ppermute(array, "core", [(0, 1), (1, 0)])


def pick(array, index):
    return lax.dynamic_index_in_dim(array, index, 0, keepdims=False)


def summed_share(array, axis):
    me, devices = lax.axis_index(axis), lax.axis_size(axis)
    total = pick(array, me).astype(f32)
    for by in (1, devices - 1, 2):
        total = total + shifted(pick(array, (me + by) % devices), axis, by).astype(f32)
    return total.astype(bf16)


def gathered(array, axis):
    me, devices = lax.axis_index(axis), lax.axis_size(axis)
    out = jnp.zeros((devices,) + array.shape, array.dtype)
    out = lax.dynamic_update_index_in_dim(out, array, me, 0)
    for by in (1, devices - 1, 2):
        out = lax.dynamic_update_index_in_dim(out, shifted(array, axis, by), (me + devices - by) % devices, 0)
    return out


def gathered_ring(array, axis):
    me, half = lax.axis_index(axis), array.shape[0] // 2
    before, after = shifted(array, axis, 1), shifted(array, axis, -1)
    far = jnp.concatenate([shifted(before[:half], axis, 1), shifted(after[half:], axis, -1)])
    out = jnp.zeros((4,) + array.shape, array.dtype)
    for by, part in ((0, array), (3, before), (1, after), (2, far)):
        out = lax.dynamic_update_index_in_dim(out, part, (me + by) % 4, 0)
    return out


def window_info(length_row, chip, core, win):
    ends = jnp.cumsum(length_row)
    starts = ends - length_row
    base = chip * 512 - 1024
    places = base + jnp.arange(win, dtype=jnp.int32)
    inside = (places[:, None] >= starts[None, :]) & (places[:, None] < ends[None, :])
    ones = jnp.broadcast_to(jnp.arange(64) < 3, (win, 64)).astype(bf16)
    key_rows = jnp.concatenate([jnp.where(inside, 0.0, -BIG).astype(bf16), ones], axis=1)
    own = chip * 512 + jnp.arange(512, dtype=jnp.int32)
    inside_q = (own[None, :] >= starts[:, None]) & (own[None, :] < ends[:, None])
    query_rows = jnp.concatenate([inside_q.astype(bf16), jnp.zeros((64, 512), bf16)], axis=0)
    info = [core]
    sizes = []
    for t in range(2):
        first = chip * 512 + t * TILE
        low = jnp.max(jnp.where(starts <= first, starts, 0)) - base
        high = jnp.min(jnp.where(ends > first + TILE - 1, ends, 1 << 30)) - base
        start = low // 128 * 128
        need = high - start
        size = (need + SHORT - 1) // SHORT * SHORT
        info.append(jnp.minimum(start, win - size))
        sizes.append(size)
    low = jnp.minimum(info[1], info[2]) // 512
    high = (jnp.maximum(info[1] + sizes[0], info[2] + sizes[1]) + 511) // 512
    return jnp.stack(info + sizes).astype(jnp.int32), key_rows, query_rows, [low, high]


def body(tokens, lengths, gain_one, bias_one, w_qkv, w_out, gain_two, bias_two, w_up, w_down, cotangent):
    core, chip = lax.axis_index("core"), lax.axis_index(("z", "x"))
    core_arg, y_arg = core[None].astype(jnp.int32), lax.axis_index("batch")[None].astype(jnp.int32)
    tok, cot = tokens[:, 0], cotangent[:, 0].reshape(512, 640)

    before, after = passed_along(tok, 1), passed_along(tok, -1)
    vectors = jnp.pad(jnp.stack([gain_one, bias_one, gain_two, bias_two]), ((0, 12), (0, 0)))
    heads = pack_heads(core_arg, w_qkv, vectors)
    heads_before, heads_after = shifted(heads, "batch", 1), shifted(heads, "batch", -1)
    feed_weights = lax.all_gather(pack_feed(core_arg, w_out, w_up, w_down), "batch", axis=0, tiled=True)
    w_out_all = feed_weights[:, 5120:]
    own = (passed_along(before, 1), before, tok, after, passed_along(after, -1))
    near, far = shifted(heads_before[:96], "batch", 1), shifted(heads_after[96:], "batch", -1)
    other = tuple(swapped(a) for a in own)
    w_heads, vec = assemble(y_arg, heads, heads_before, heads_after, near, far)

    windows = [window_info(lengths[m, 0], chip, core, 2560) for m in range(2)]
    place = jnp.stack([core] + windows[0][3] + windows[1][3]).astype(jnp.int32)
    forward = []
    near_parts = [project(m, (1, 2, 3), place, own, other, vec, w_heads) for m in range(2)]
    for m in range(2):
        k, v, kT, vT = project(m, (0, 4), place, own, other, vec, w_heads, near_parts[m][:4])
        q, qT = near_parts[m][4:]
        info, key_rows, query_rows, _ = windows[m]
        oT, low, lse = attend(info, qT, k, vT, key_rows, query_rows)
        forward.append((info, qT, q, k, kT, v, oT, lse, key_rows, query_rows, low))

    low = jnp.stack([f[-1] for f in forward])
    theirs = swapped(low)
    middle, hidden_two = middle_step(core_arg, low, theirs, tok, w_out_all, vec)
    out, d_hidden, partial, feed_grads = feed_forward(hidden_two, swapped(hidden_two), cot, swapped(cot), feed_weights)
    feed_grads = lax.psum_scatter(feed_grads.reshape(5120, 640), ("z", "x"), scatter_dimension=0, tiled=True).reshape(4, 80, 640)
    block_out, grad_middle, branch, g_two = after_feed(middle, out, d_hidden, swapped(partial), cot, vec)

    do, doT, g_out = branch_step(core_arg, branch, swapped(branch), w_out_all, low, theirs)
    grads = []
    for m in range(2):
        info, qT, q, k, kT, v, oT, lse, key_rows, query_rows, _ = forward[m]
        grads.append(attend_back(m, info, qT, q, k, kT, v, doT, do, oT, lse, key_rows, query_rows))
    dq, dk, dv = zip(*grads)
    mine, theirs, tail = project_back(place, own, other, vec, w_heads, dq, dk, dv, g_out, g_two)
    tail = lax.all_to_all(tail, ("batch", "z", "x"), 0, 0, tiled=True)

    theirs = swapped(theirs)
    sums = [mine[j].astype(f32) + theirs[j].astype(f32) for j in range(5)]
    right = passed_along(sums[4].astype(bf16), 1).astype(f32) + sums[3]
    left = passed_along(sums[0].astype(bf16), -1).astype(f32) + sums[1]
    d_one = sums[2] + passed_along(right.astype(bf16), 1).astype(f32) + passed_along(left.astype(bf16), -1).astype(f32)
    n_one, r_one = moments(tok.reshape(512, 640).astype(f32))
    grad_tokens = (grad_middle + norm_back(d_one.reshape(512, 640), n_one, r_one, vec[0:1])).astype(bf16)

    feed = lax.all_gather(summed_share(feed_grads, "batch"), ("z", "x"), axis=0, tiled=True).reshape(16, 80, 640)
    grad_up, grad_down = final_feed(core_arg, feed, swapped(feed))
    tail, grad_tokens = lax.optimization_barrier((tail, grad_tokens))
    tail = jnp.sum(tail.astype(f32), axis=0).astype(bf16)
    tail = gathered(gathered(tail, "x").reshape(160, 384), "z").reshape(16, 40, 384)
    grad_qkv, grad_out, spare = final_heads(core_arg, tail, swapped(tail))
    return (
        block_out.reshape(2, 1, 256, 640), grad_tokens.reshape(2, 1, 256, 640), spare[:, 0], spare[:, 1], grad_qkv, grad_out,
        spare[:, 2], spare[:, 3], grad_up, grad_down)


def solution(mesh):
    fine = Mesh(mesh.devices.reshape(4, 4, 4, 2), ("batch", "z", "x", "core"))
    rows = P(None, "batch", ("z", "x", "core"), None)
    one, two = P("batch"), P("batch", None)
    return jax.shard_map(
        body,
        mesh=fine,
        in_specs=(rows, P(None, "batch", None), one, one, two, two, one, one, two, two, rows),
        out_specs=(rows, rows, one, one, two, two, one, one, two, two),
        check_vma=False,
    )
```

```python
import math

import jax
import jax.numpy as jnp
from jax import lax
from jax.experimental import pallas as pl
from jax.experimental.pallas import tpu as pltpu
from jax.sharding import Mesh
from jax.sharding import PartitionSpec as P

HEAD_DIM = 32
SCALE = HEAD_DIM ** -0.5
LOG2E = math.log2(math.e)
C2 = SCALE * LOG2E
BIG = 1e30
TILE = 256
EPSILON = 1e-05
PAIRS = 5
SHORT, LONG = 384, 1152
f32, bf16 = jnp.float32, jnp.bfloat16
NT = (((1,), (1,)), ((), ()))


def pair_offset(info_ref):
    p = pl.program_id(0)
    sub = jnp.where(p == PAIRS - 1, info_ref[0], lax.rem(p, 2))
    return sub * (2 * HEAD_DIM)


def split3(v):
    a = v.astype(bf16)
    r = v - a.astype(f32)
    b = r.astype(bf16)
    d = (r - b.astype(f32)).astype(bf16)
    return a, b, d


def rows_masked(xT, off):
    row = lax.broadcasted_iota(jnp.int32, xT.shape, 0) - off
    xf = xT.astype(f32)
    return [jnp.where((row >= HEAD_DIM * j) & (row < HEAD_DIM * (j + 1)), xf, 0.0).astype(bf16) for j in range(2)]


def lanes_masked(x, off):
    lane = lax.broadcasted_iota(jnp.int32, x.shape, 1) - off
    xf = x.astype(f32)
    return [jnp.where((lane >= HEAD_DIM * j) & (lane < HEAD_DIM * (j + 1)), xf, 0.0).astype(bf16) for j in range(2)]


def attend_kernel(info_ref, qT_ref, k_ref, vT_ref, kaug_ref, qaugT_ref, oT_ref, o_ref, l_ref, rhs):
    off = pair_offset(info_ref)
    oT_ref[...] = jnp.where(lax.rem(pl.program_id(0), 2) == 0, 0.0, oT_ref[...])
    for t in range(2):
        cols = slice(t * TILE, (t + 1) * TILE)
        masked = rows_masked(qT_ref[:, cols], off)
        for j in range(2):
            rhs[0:128, j * TILE:(j + 1) * TILE] = masked[j]
            rhs[128:256, j * TILE:(j + 1) * TILE] = qaugT_ref[:, cols]
        start = info_ref[1 + t]
        need = info_ref[3 + t]

        def block(first, size):
            def step(i, carry):
                row = pl.multiple_of(first + i * size, 128)
                lhs = jnp.concatenate([k_ref[pl.ds(row, size), :], kaug_ref[pl.ds(row, size), :]], axis=1)
                raw = [jnp.dot(lhs, rhs[:, j * TILE:(j + 1) * TILE], preferred_element_type=f32) for j in range(2)]
                out = []
                for j in range(2):
                    m, l, o = carry[j]
                    s = raw[j] * C2
                    m_new = jnp.maximum(m, jnp.max(s, axis=0, keepdims=True))
                    alpha = jnp.exp2(m - m_new)
                    p = jnp.exp2(s - m_new)
                    vT = vT_ref[pl.ds(pl.multiple_of(off + j * HEAD_DIM, HEAD_DIM), HEAD_DIM), pl.ds(row, size)]
                    out.append((m_new, l * alpha + jnp.sum(p, axis=0, keepdims=True),
                                o * alpha + jnp.dot(vT, p.astype(bf16), preferred_element_type=f32)))
                return tuple(out)
            return step

        def finish(state):
            for j in range(2):
                m, l, o = state[j]
                oT_ref[pl.ds(pl.multiple_of(off + j * HEAD_DIM, HEAD_DIM), HEAD_DIM), cols] = o * (1.0 / l)
                l_ref[0, j:j + 1, cols] = m + jnp.log2(l)

        init = tuple((jnp.full((1, TILE), -1e38, f32), jnp.zeros((1, TILE), f32), jnp.zeros((HEAD_DIM, TILE), f32)) for _ in range(2))

        longs = lax.div(need, LONG)
        state = lax.fori_loop(0, longs, block(start, LONG), init)
        finish(lax.fori_loop(0, lax.div(need - longs * LONG, SHORT), block(start + longs * LONG, SHORT), state))

    o_ref[...] = oT_ref[...].T.astype(bf16)


def attend(m, info, qT, k, vT, kaug, qaugT):
    win = k.shape[1]
    nq = qT.shape[2]
    return pl.pallas_call(
        attend_kernel,
        out_shape=(jax.ShapeDtypeStruct((384, nq), f32), jax.ShapeDtypeStruct((nq, 384), bf16), jax.ShapeDtypeStruct((PAIRS, 8, nq), f32)),
        grid_spec=pltpu.PrefetchScalarGridSpec(
            num_scalar_prefetch=1, grid=(PAIRS,),
            in_specs=[
                pl.BlockSpec((None, 128, nq), lambda p, *_: (m, p // 2, 0)),
                pl.BlockSpec((None, win, 128), lambda p, *_: (m, 0, p // 2)),
                pl.BlockSpec((None, 128, win), lambda p, *_: (m, p // 2, 0)),
                pl.BlockSpec((win, 128), lambda p, *_: (0, 0)),
                pl.BlockSpec((128, nq), lambda p, *_: (0, 0)),
            ],
            out_specs=[
                pl.BlockSpec((128, nq), lambda p, *_: (p // 2, 0)),
                pl.BlockSpec((nq, 128), lambda p, *_: (0, p // 2)),
                pl.BlockSpec((1, 8, nq), lambda p, *_: (p, 0, 0)),
            ],
            scratch_shapes=[pltpu.VMEM((256, 2 * TILE), bf16)],
        ),
        compiler_params=pltpu.CompilerParams(vmem_limit_bytes=28 << 20),
        cost_estimate=pl.CostEstimate(flops=20 * 10**9, bytes_accessed=6 << 20, transcendentals=5 * 10**6),
        name="attend",
    )(info, qT, k, vT, kaug, qaugT)


def attend_back_kernel(info_ref, qT_ref, q_ref, k_ref, kT_ref, v_ref, doT_ref, do_ref, oT_ref, l_ref, kaug_ref, qaugT_ref,
                       dq_ref, dk_ref, dv_ref, dqT_ref, rhs_s, rhs_d, q_stk, do_stk, dk_acc, dv_acc):
    p_id = pl.program_id(0)
    off = pair_offset(info_ref)

    @pl.when(lax.rem(p_id, 2) == 0)
    def _():
        dqT_ref[...] = jnp.zeros_like(dqT_ref)
        dk_acc[...] = jnp.zeros_like(dk_acc)
        dv_acc[...] = jnp.zeros_like(dv_acc)

    for t in range(2):
        cols = slice(t * TILE, (t + 1) * TILE)
        masked_q = rows_masked(qT_ref[:, cols], off)
        masked_do = rows_masked(doT_ref[:, cols], off)
        lane_q = lanes_masked(q_ref[cols, :], off)
        lane_do = lanes_masked(do_ref[cols, :], off)
        for j in range(2):
            part = slice(j * TILE, (j + 1) * TILE)
            head = pl.ds(pl.multiple_of(off + j * HEAD_DIM, HEAD_DIM), HEAD_DIM)
            delta = jnp.sum(doT_ref[head, cols].astype(f32) * oT_ref[head, cols], axis=0, keepdims=True)
            total = l_ref[0, j:j + 1, cols] * (1.0 / C2)
            rowid = lax.broadcasted_iota(jnp.int32, (64, TILE), 0)
            lp, dp = split3(-total), split3(-delta)
            def pieces(parts):
                x = jnp.zeros((64, TILE), f32)
                for n in range(3):
                    x = jnp.where(rowid == n, parts[n].astype(f32), x)
                return x.astype(bf16)
            rhs_s[0:128, part] = masked_q[j]
            rhs_s[128:192, part] = qaugT_ref[0:64, cols]
            rhs_s[192:256, part] = pieces(lp)
            rhs_d[0:128, part] = masked_do[j]
            rhs_d[128:192, part] = jnp.zeros((64, TILE), bf16)
            rhs_d[192:256, part] = pieces(dp)
            q_stk[part, :] = lane_q[j]
            do_stk[part, :] = lane_do[j]
        start = info_ref[1 + t]
        need = info_ref[3 + t]

        def block(first, size):
            def step(i, carry):
                row = pl.multiple_of(first + i * size, 128)
                rows = pl.ds(row, size)
                aug = kaug_ref[rows, :]
                lhs_k = jnp.concatenate([k_ref[rows, :], aug], axis=1)
                lhs_v = jnp.concatenate([v_ref[rows, :], aug], axis=1)
                out, dv, dk = [], dv_acc[rows, :], dk_acc[rows, :]
                for j in range(2):
                    part = slice(j * TILE, (j + 1) * TILE)
                    s = jnp.dot(lhs_k, rhs_s[:, part], preferred_element_type=f32)
                    dp = jnp.dot(lhs_v, rhs_d[:, part], preferred_element_type=f32)
                    p = jnp.exp2(s * C2)
                    ds = (p * dp).astype(bf16)
                    dv = dv + jnp.dot(p.astype(bf16), do_stk[part, :], preferred_element_type=f32)
                    dk = dk + jnp.dot(ds, q_stk[part, :], preferred_element_type=f32)
                    kT = kT_ref[pl.ds(pl.multiple_of(off + j * HEAD_DIM, HEAD_DIM), HEAD_DIM), rows]
                    out.append(carry[j] + jnp.dot(kT, ds, preferred_element_type=f32))
                dv_acc[rows, :] = dv
                dk_acc[rows, :] = dk
                return tuple(out)
            return step

        def finish(dqs):
            for j in range(2):
                dqT_ref[pl.ds(pl.multiple_of(off + j * HEAD_DIM, HEAD_DIM), HEAD_DIM), cols] = dqs[j] * SCALE

        init = tuple(jnp.zeros((HEAD_DIM, TILE), f32) for _ in range(2))

        longs = lax.div(need, LONG)
        state = lax.fori_loop(0, longs, block(start, LONG), init)
        finish(lax.fori_loop(0, lax.div(need - longs * LONG, SHORT), block(start + longs * LONG, SHORT), state))
    @pl.when((lax.rem(p_id, 2) == 1) | (p_id == PAIRS - 1))
    def _():
        dq_ref[...] = dqT_ref[...].T.astype(bf16)
        dk_ref[...] = (dk_acc[...] * SCALE).astype(bf16)
        dv_ref[...] = dv_acc[...].astype(bf16)


def attend_back(m, info, qT, q, k, kT, v, doT, do, oT, lse, kaug, qaugT):
    win, nq = k.shape[1], qT.shape[2]
    wide = pl.BlockSpec((128, nq), lambda p, *_: (p // 2, 0))
    tall = pl.BlockSpec((nq, 128), lambda p, *_: (0, p // 2))
    keys = pl.BlockSpec((win, 128), lambda p, *_: (0, p // 2))
    wide_m = pl.BlockSpec((None, 128, nq), lambda p, *_: (m, p // 2, 0))
    tall_m = pl.BlockSpec((None, nq, 128), lambda p, *_: (m, 0, p // 2))
    keys_m = pl.BlockSpec((None, win, 128), lambda p, *_: (m, 0, p // 2))
    return pl.pallas_call(
        attend_back_kernel,
        out_shape=(jax.ShapeDtypeStruct((nq, 384), bf16), jax.ShapeDtypeStruct((win, 384), bf16), jax.ShapeDtypeStruct((win, 384), bf16)),
        grid_spec=pltpu.PrefetchScalarGridSpec(
            num_scalar_prefetch=1, grid=(PAIRS,),
            in_specs=[wide_m, tall_m, keys_m, pl.BlockSpec((None, 128, win), lambda p, *_: (m, p // 2, 0)), keys_m,
                      pl.BlockSpec((128, nq), lambda p, *_: (p // 2, m)), pl.BlockSpec((nq, 128), lambda p, *_: (m, p // 2)), wide,
                      pl.BlockSpec((1, 8, nq), lambda p, *_: (p, 0, 0)),
                      pl.BlockSpec((win, 128), lambda p, *_: (0, 0)), pl.BlockSpec((128, nq), lambda p, *_: (0, 0))],
            out_specs=[tall, keys, keys],
            scratch_shapes=[pltpu.VMEM((128, nq), f32), pltpu.VMEM((256, 2 * TILE), bf16), pltpu.VMEM((256, 2 * TILE), bf16),
                            pltpu.VMEM((2 * TILE, 128), bf16), pltpu.VMEM((2 * TILE, 128), bf16),
                            pltpu.VMEM((win, 128), f32), pltpu.VMEM((win, 128), f32)],
        ),
        compiler_params=pltpu.CompilerParams(vmem_limit_bytes=32 << 20),
        cost_estimate=pl.CostEstimate(flops=40 * 10**9, bytes_accessed=12 << 20, transcendentals=5 * 10**6),
        name="attend_back",
    )(info, qT, q, k, kT, v, doT, do, oT, lse, kaug, qaugT)


def moments(x):
    centred = x - jnp.mean(x, axis=-1, keepdims=True)
    r = lax.rsqrt(jnp.mean(centred * centred, axis=-1, keepdims=True) + EPSILON)
    return centred * r, r


def norm_back(grad, n, r, gain):
    e = grad * gain
    return r * (e - jnp.mean(e, axis=-1, keepdims=True) - n * jnp.mean(e * n, axis=-1, keepdims=True))


def call(kernel, out_shape, name, flops=10**9, limit=48, **spec):
    return pl.pallas_call(
        kernel, out_shape=out_shape, name=name,
        compiler_params=pltpu.CompilerParams(vmem_limit_bytes=limit << 20),
        cost_estimate=pl.CostEstimate(flops=flops, bytes_accessed=8 << 20, transcendentals=0), **spec)


def shape(*dims, dtype=bf16):
    return jax.ShapeDtypeStruct(dims, dtype)


def scalar_first(grid, in_specs, out_specs, scratch=()):
    return dict(grid_spec=pltpu.PrefetchScalarGridSpec(
        num_scalar_prefetch=1, grid=grid, in_specs=in_specs, out_specs=out_specs, scratch_shapes=list(scratch)))


def full(*dims):
    return pl.BlockSpec(dims, lambda *_: (0,) * len(dims))


def pack_heads_kernel(core_ref, qkv_ref, vec_ref, heads_ref):
    for part in range(3):
        near = pl.ds(pl.multiple_of(640 * part + 256 * core_ref[0], 128), 256)
        heads_ref[0:160, 384 * part:384 * part + 256] = qkv_ref[:, near]
        heads_ref[0:160, 384 * part + 256:384 * (part + 1)] = qkv_ref[:, 640 * part + 512:640 * (part + 1)]
    heads_ref[160:176, :] = jnp.zeros((16, 1152), bf16)
    heads_ref[160:176, 0:160] = vec_ref[...]


def pack_heads(core, w_qkv, vectors):
    return call(pack_heads_kernel, shape(176, 1152), "pack_heads", 10**6, 8, **scalar_first(
        (1,), [full(160, 1920), full(16, 160)], full(176, 1152)))(core, w_qkv, vectors)


def pack_feed_kernel(core_ref, out_ref, up_ref, down_ref, feed_ref):
    core = core_ref[0]
    for f in range(4):
        feed_ref[:, 640 * f:640 * (f + 1)] = up_ref[:, pl.ds(pl.multiple_of(1280 * f + 640 * core, 128), 640)]
        feed_ref[:, 2560 + 640 * f:2560 + 640 * (f + 1)] = down_ref[pl.ds(pl.multiple_of(640 * core + 160 * f, 32), 160), :]
    feed_ref[:, 5120:5760] = out_ref[...]


def pack_feed(core, w_out, w_up, w_down):
    args = (w_out, w_up, w_down)
    return call(pack_feed_kernel, shape(160, 5760), "pack_feed", 10**6, 16, **scalar_first(
        (1,), [full(*a.shape) for a in args], full(160, 5760)))(core, *args)


def assemble_kernel(y_ref, own_ref, before_ref, after_ref, near_ref, far_ref, heads_ref, vec_ref):
    total = jnp.zeros((16, 640), f32)

    def place(by, top, bottom, vec):
        nonlocal total
        row = lax.rem(y_ref[0] + by, 4) * 160
        for part, base in ((top, 0), (bottom, top.shape[0])):
            heads_ref[pl.ds(pl.multiple_of(row + base, 32), part.shape[0]), :] = part
        total = total + pltpu.roll(vec[:, :640].astype(f32), row, 1)

    for by, ref in ((0, own_ref), (3, before_ref), (1, after_ref)):
        place(by, ref[0:96, :], ref[96:160, :], ref[160:176, :])
    place(2, near_ref[...], far_ref[0:64, :], far_ref[64:80, :])
    vec_ref[...] = total


def assemble(y, *parts):
    return call(assemble_kernel, (shape(640, 1152), shape(16, 640, dtype=f32)), "assemble", 10**6, 12, **scalar_first(
        (1,), [full(*a.shape) for a in parts], [full(640, 1152), full(16, 640)]))(y, *parts)


def rows_in_order(core, mine, theirs, x_ref):
    mine, theirs = mine.astype(f32), theirs.astype(f32)
    x_ref[0:256, :] = jnp.where(core == 0, mine, theirs)
    x_ref[256:512, :] = jnp.where(core == 0, theirs, mine)


def window_rows(core, own_refs, other_refs, m, block, x_ref):
    for j in range(len(own_refs)):
        @pl.when(block == j)
        def _():
            rows_in_order(core, own_refs[j][m], other_refs[j][m], x_ref)


def project_kernel(chips, place_ref, *refs):
    n = len(chips)
    own_refs, other_refs = refs[:n], refs[n:2 * n]
    vec_ref, w_ref = refs[2 * n:2 * n + 2]
    k_ref, v_ref, kT_ref, vT_ref = refs[-6 - 2 * (n == 3):][:4]
    x_ref, hid_ref = refs[-2:]
    m, step = pl.program_id(0), pl.program_id(1)
    block = sum(jnp.where(step == i, chip, 0) for i, chip in enumerate(chips))
    needed = (block >= place_ref[1 + 2 * m]) & (block < place_ref[2 + 2 * m])

    @pl.when(jnp.logical_not(needed))
    def _():
        for ref in (k_ref, v_ref, kT_ref, vT_ref):
            ref[...] = jnp.zeros_like(ref)

    @pl.when(needed)
    def _():
        window_rows(place_ref[0], own_refs, other_refs, m, step, x_ref)
        hidden = (moments(x_ref[...])[0] * vec_ref[0:1, :] + vec_ref[1:2, :]).astype(bf16)
        hid_ref[...] = hidden
        kv = jnp.dot(hidden, w_ref[:, 384:], preferred_element_type=f32)
        low = kv.astype(bf16)
        k_ref[0] = low[:, :384]
        v_ref[0] = low[:, 384:]
        turned = kv.T.astype(bf16)
        kT_ref[0] = turned[:384]
        vT_ref[0] = turned[384:]

    if n == 3:
        q_ref, qT_ref = refs[-4:-2]

        @pl.when(step == 1)
        def _():
            q = jnp.dot(hid_ref[...], w_ref[:, :384], preferred_element_type=f32)
            q_ref[0] = q.astype(bf16)
            qT_ref[0] = q.T.astype(bf16)


def project(chips, place, own, other, vec, w, earlier=()):
    n = len(chips)
    chip = (lambda b: b + 1) if n == 3 else (lambda b: 4 * b)
    tall = pl.BlockSpec((1, 512, 384), lambda m, b, *_: (m, chip(b), 0))
    wide = pl.BlockSpec((1, 384, 512), lambda m, b, *_: (m, 0, chip(b)))
    shapes = [shape(2, 2560, 384), shape(2, 2560, 384), shape(2, 384, 2560), shape(2, 384, 2560)]
    specs = [tall, tall, wide, wide]
    if n == 3:
        shapes += [shape(2, 512, 384), shape(2, 384, 512)]
        specs += [pl.BlockSpec((1, 512, 384), lambda m, *_: (m, 0, 0)), pl.BlockSpec((1, 384, 512), lambda m, *_: (m, 0, 0))]
    own, other = [own[c] for c in chips], [other[c] for c in chips]
    return call(
        lambda *refs: project_kernel(chips, *refs), shapes, "project", 5 * 10**9, 28,
        input_output_aliases={2 * n + 3 + i: i for i in range(len(earlier))}, **scalar_first(
            (2, n), [full(2, 256, 640)] * (2 * n) + [full(16, 640), full(640, 1152)] + [pl.BlockSpec(memory_space=pl.ANY)] * len(earlier),
            specs, [pltpu.VMEM((512, 640), f32), pltpu.VMEM((512, 640), bf16)]))(place, *own, *other, vec, w, *earlier)


def heads_joined(core, mine, theirs):
    first, second = (jnp.where(core == 0, a, b) for a, b in ((mine, theirs), (theirs, mine)))
    return jnp.concatenate([first[:, :256], second[:, :256], first[:, 256:] + second[:, 256:]], axis=1)


def middle_kernel(core_ref, low0_ref, low1_ref, theirs_ref, tok_ref, tok2_ref, w_ref, vec_ref, mid_ref, hid_ref, hid2_ref):
    core = core_ref[0]
    for m, low_ref in enumerate((low0_ref, low1_ref)):
        attended = heads_joined(core, low_ref[...].astype(f32), theirs_ref[m].astype(f32)).astype(bf16)
        branch = jnp.dot(attended, w_ref[...], preferred_element_type=f32)
        mine = jnp.where(core == 0, branch[:256], branch[256:]) + tok_ref[m].astype(f32)
        theirs = jnp.where(core == 0, branch[256:], branch[:256]) + tok2_ref[m].astype(f32)
        part = slice(256 * m, 256 * (m + 1))
        mid_ref[part, :] = mine
        hid_ref[part, :] = (moments(mine)[0] * vec_ref[2:3, :] + vec_ref[3:4, :]).astype(bf16)
        hid2_ref[part, :] = (moments(theirs)[0] * vec_ref[2:3, :] + vec_ref[3:4, :]).astype(bf16)


def middle_step(core, *args):
    return call(middle_kernel, (shape(512, 640, dtype=f32), shape(512, 640), shape(512, 640)), "middle", 10**9, 20, **scalar_first(
        (1,), [full(*a.shape) for a in args], [full(512, 640)] * 3))(core, *args)


def feed_kernel(h_ref, h2_ref, cot_ref, cot2_ref, up_ref, down_ref, mine_ref, theirs_ref, g_ref, h, cot, hT, cT, out, dh):
    chunk = pl.program_id(0)

    @pl.when(chunk == 0)
    def _():
        h[0:512, :], h[512:1024, :] = h_ref[...], h2_ref[...]
        cot[0:512, :], cot[512:1024, :] = cot_ref[...], cot2_ref[...]
        hT[...] = h[...].astype(f32).T.astype(bf16)
        cT[...] = cot[...].astype(f32).T.astype(bf16)
        out[...] = jnp.zeros_like(out)
        dh[...] = jnp.zeros_like(dh)

    up_w = up_ref[...]
    down_w = jnp.concatenate([down_ref[160 * y:160 * (y + 1), 640 * i:640 * (i + 1)] for y in range(2) for i in range(4)], axis=0)
    acts, d_ups = [], []
    for t in range(4):
        rows = slice(256 * t, 256 * (t + 1))
        u = jnp.dot(h[rows, :], up_w, preferred_element_type=f32)
        d_act = lax.dot_general(cot[rows, :], down_w, NT, preferred_element_type=f32)
        cdf = 0.5 * (1.0 + lax.erf(u * (2.0 ** -0.5)))
        pdf = jnp.exp(u * u * -0.5) * ((2.0 * math.pi) ** -0.5)
        act = (u * cdf).astype(bf16)
        d_up = (d_act * (cdf + u * pdf)).astype(bf16)
        out[rows, :] += jnp.dot(act, down_w, preferred_element_type=f32)
        dh[rows, :] += lax.dot_general(d_up, up_w, NT, preferred_element_type=f32)
        acts.append(act)
        d_ups.append(d_up)
    g_up = jnp.dot(hT[...], jnp.concatenate(d_ups, axis=0), preferred_element_type=f32).astype(bf16)
    g_down = jnp.dot(cT[...], jnp.concatenate(acts, axis=0), preferred_element_type=f32).T.astype(bf16)
    for f in range(2):
        for y in range(4):
            for i in range(2):
                g_ref[4 * chunk + 2 * f + i, y] = g_up[160 * y + 80 * i:160 * y + 80 * (i + 1), 640 * f:640 * (f + 1)]
        for i in range(8):
            g_ref[8 + i, 2 * chunk + f] = g_down[640 * f + 80 * i:640 * f + 80 * (i + 1)]

    @pl.when(chunk == 1)
    def _():
        mine_ref[0], mine_ref[1] = out[0:512, :].astype(bf16), dh[0:512, :].astype(bf16)
        theirs_ref[0], theirs_ref[1] = out[512:1024, :].astype(bf16), dh[512:1024, :].astype(bf16)


def feed_forward(h, h2, cot, cot2, weights):
    return call(
        feed_kernel,
        (shape(2, 512, 640), shape(2, 512, 640), shape(16, 4, 80, 640)),
        "feed_forward", 30 * 10**9, 52, grid=(2,),
        in_specs=[full(512, 640)] * 4 + [pl.BlockSpec((640, 1280), lambda f: (0, f)), pl.BlockSpec((320, 2560), lambda f: (f, 1))],
        out_specs=[full(2, 512, 640), full(2, 512, 640), full(16, 4, 80, 640)],
        scratch_shapes=[pltpu.VMEM((1024, 640), bf16), pltpu.VMEM((1024, 640), bf16), pltpu.VMEM((640, 1024), bf16), pltpu.VMEM((640, 1024), bf16),
                        pltpu.VMEM((1024, 640), f32), pltpu.VMEM((1024, 640), f32)],
    )(h, h2, cot, cot2, weights, weights)


def after_kernel(mid_ref, mine_ref, theirs_ref, cot_ref, vec_ref, block_ref, grad_ref, branch_ref, g_ref):
    middle = mid_ref[...]
    block_ref[...] = (middle + mine_ref[0].astype(f32) + theirs_ref[0].astype(f32)).astype(bf16)
    d_hidden = mine_ref[1].astype(f32) + theirs_ref[1].astype(f32)
    n, r = moments(middle)
    g_ref[...] = jnp.zeros_like(g_ref)
    g_ref[0:1, :] = jnp.sum(d_hidden * n, axis=0, keepdims=True)
    g_ref[1:2, :] = jnp.sum(d_hidden, axis=0, keepdims=True)
    grad = cot_ref[...].astype(f32) + norm_back(d_hidden, n, r, vec_ref[2:3, :])
    grad_ref[...] = grad
    branch_ref[...] = grad.astype(bf16)


def after_feed(*args):
    return call(
        after_kernel, (shape(512, 640), shape(512, 640, dtype=f32), shape(512, 640), shape(8, 640, dtype=f32)), "after_feed", 10**9, 24,
        in_specs=[pl.BlockSpec(memory_space=pltpu.VMEM)] * 5, out_specs=[pl.BlockSpec(memory_space=pltpu.VMEM)] * 4)(*args)


def branch_kernel(core_ref, own_ref, their_ref, w_ref, low0_ref, low1_ref, theirs_ref, do_ref, doT_ref, g_ref):
    core = core_ref[0]
    w = jnp.concatenate([w_ref[pl.ds(pl.multiple_of(256 * core, 256), 256), :], w_ref[512:640, :]], axis=0)
    g = jnp.zeros((640, 384), f32)
    for m in range(2):
        part = slice(256 * m, 256 * (m + 1))
        mine, theirs = own_ref[part, :].astype(f32), their_ref[part, :].astype(f32)
        branch = jnp.concatenate([jnp.where(core == 0, mine, theirs), jnp.where(core == 0, theirs, mine)], axis=0)
        kept = jnp.where(core == 0, branch[:, :384], branch[:, 256:]).astype(bf16)
        branch = branch.astype(bf16)
        rows = slice(512 * m, 512 * (m + 1))
        do = lax.dot_general(branch, w, NT, preferred_element_type=f32)
        do_ref[rows, :] = do.astype(bf16)
        doT_ref[:, rows] = do.T.astype(bf16)
        attended = heads_joined(core, (low0_ref, low1_ref)[m][...].astype(f32), theirs_ref[m].astype(f32))
        g = g + jnp.dot(attended.T.astype(bf16), kept, preferred_element_type=f32)
    g_ref[...] = g


def branch_step(core, *args):
    specs = [full(*a.shape) for a in args]
    return call(
        branch_kernel, (shape(1024, 384), shape(384, 1024), shape(640, 384, dtype=f32)), "branch", 10**9, 24, **scalar_first(
            (1,), specs, [full(1024, 384), full(384, 1024), full(640, 384)]))(core, *args)


def project_back_kernel(core_ref, *refs):
    own_refs, other_refs = refs[:5], refs[5:10]
    (vec_ref, w_ref, dq0_ref, dq1_ref, dk0_ref, dk1_ref, dv0_ref, dv1_ref, g_out_ref, g_two_ref,
     mine_ref, theirs_ref, tail_ref, x_ref, d_kv, d_q, d_hid, g_ref, g_vec) = refs[10:]
    step, core = pl.program_id(0), core_ref[0]
    block = lax.rem(step, 5)

    @pl.when(step == 0)
    def _():
        g_ref[...] = jnp.zeros_like(g_ref)
        g_vec[...] = jnp.zeros_like(g_vec)
        g_vec[2:4, :] = g_two_ref[0:2, :]

    second = lax.div(step, 5)
    needed = (block >= core_ref[1 + 2 * second]) & (block < core_ref[2 + 2 * second])

    @pl.when(jnp.logical_not(needed))
    def _():
        mine_ref[...] = jnp.zeros_like(mine_ref)
        theirs_ref[...] = jnp.zeros_like(theirs_ref)

    for m, (dq, dk, dv) in enumerate(((dq0_ref, dk0_ref, dv0_ref), (dq1_ref, dk1_ref, dv1_ref))):
        @pl.when(needed & (second == m))
        def _():
            window_rows(core, own_refs, other_refs, m, block, x_ref)
            d_kv[:, :384], d_kv[:, 384:] = dk[...], dv[...]
            d_q[...] = dq[...]

    @pl.when(needed)
    def _():
        n = moments(x_ref[...])[0]
        hiddenT = (n * vec_ref[0:1, :] + vec_ref[1:2, :]).T.astype(bf16)
        d_hid[...] = lax.dot_general(d_kv[...], w_ref[:, 384:], NT, preferred_element_type=f32)
        g_ref[:, 384:] += jnp.dot(hiddenT, d_kv[...], preferred_element_type=f32)

        @pl.when(block == 2)
        def _():
            g_ref[:, :384] += jnp.dot(hiddenT, d_q[...], preferred_element_type=f32)
            d_hid[...] += lax.dot_general(d_q[...], w_ref[:, :384], NT, preferred_element_type=f32)

        dh = d_hid[...]
        mine_ref[0, 0] = jnp.where(core == 0, dh[:256], dh[256:]).astype(bf16)
        theirs_ref[0, 0] = jnp.where(core == 0, dh[256:], dh[:256]).astype(bf16)
        g_vec[0:1, :] += jnp.sum(dh * n, axis=0, keepdims=True)
        g_vec[1:2, :] += jnp.sum(dh, axis=0, keepdims=True)

    @pl.when(step == 9)
    def _():
        turned = g_vec[...].T
        lane = lax.broadcasted_iota(jnp.int32, (640, 128), 1) - 64 * (1 - core)
        spare = g_ref[:, 256:384]
        for i in range(4):
            spare = jnp.where(lane == i, turned[:, i:i + 1], spare)
        g_ref[:, 256:384] = spare
        for y in range(4):
            for z in range(4):
                rows = slice(160 * y + 40 * z, 160 * y + 40 * (z + 1))
                for x in range(3):
                    tail_ref[16 * y + 4 * z + x] = g_ref[rows, 384 * x:384 * (x + 1)].astype(bf16)
                tail_ref[16 * y + 4 * z + 3] = g_out_ref[rows, :].astype(bf16)


def project_back(core, own, other, vec, w, dq, dk, dv, g_out, g_two):
    first = pl.BlockSpec((512, 384), lambda b, *_: (jnp.minimum(b, 4), 0))
    second = pl.BlockSpec((512, 384), lambda b, *_: (jnp.maximum(b - 5, 0), 0))
    return call(
        project_back_kernel, (shape(5, 2, 256, 640), shape(5, 2, 256, 640), shape(64, 40, 384)), "project_back", 10**10, 36, **scalar_first(
            (10,), [full(2, 256, 640)] * 10 + [full(16, 640), full(640, 1152), full(512, 384), full(512, 384), first, second, first, second,
                                               full(640, 384), full(8, 640)],
            [pl.BlockSpec((1, 1, 256, 640), lambda b, *_: (lax.rem(b, 5), b // 5, 0, 0))] * 2 + [full(64, 40, 384)],
            [pltpu.VMEM((512, 640), f32), pltpu.VMEM((512, 768), bf16), pltpu.VMEM((512, 384), bf16),
             pltpu.VMEM((512, 640), f32), pltpu.VMEM((640, 1152), f32), pltpu.VMEM((8, 640), f32)]))(core, *own, *other, vec, w, *dq, *dk, *dv, g_out, g_two)


def final_kernel(core_ref, mine_ref, theirs_ref, up_ref, down_ref, qkv_ref, out_ref, vec_ref):
    core = core_ref[0]
    lane = lax.broadcasted_iota(jnp.int32, (40, 128), 1)
    for i in range(16):
        mine, theirs = mine_ref[i].astype(f32), theirs_ref[i].astype(f32)
        pair = [jnp.where(core == 0, mine, theirs), jnp.where(core == 0, theirs, mine)]
        for c in range(2):
            piece = jnp.concatenate([pair[c][80 * t:80 * (t + 1)] for t in range(5)], axis=1)
            if i < 8:
                base = 1280 * (i // 2) + 640 * c
                up_ref[80 * (i % 2):80 * (i % 2 + 1), base:base + 640] = piece
            else:
                base = 640 * c + 80 * (i - 8)
                down_ref[base:base + 80, :] = piece
        a, b = ([pair[c][400 + 40 * t:440 + 40 * t] for t in range(3)] for c in range(2))
        rows, x = slice(40 * (i // 4), 40 * (i // 4 + 1)), i % 4
        if x < 3:
            last = jnp.where(lane < 64, a[2], b[2])
            qkv_ref[rows, 640 * x:640 * (x + 1)] = jnp.concatenate([a[0], a[1], b[0], b[1], last], axis=1)
        else:
            out_ref[rows, :] = jnp.concatenate([a[0], a[1], a[2], b[1], b[2]], axis=1)
        if x == 0:
            vec_ref[rows, :] = pltpu.roll(a[2], 64, 1) + b[2]


def final_step(core, mine, theirs):
    return call(
        final_kernel,
        (shape(160, 5120, dtype=f32), shape(1280, 640, dtype=f32), shape(160, 1920, dtype=f32), shape(160, 640, dtype=f32),
         shape(160, 128, dtype=f32)), "final", 10**6, 32, **scalar_first(
            (1,), [full(16, 520, 128)] * 2, [full(160, 5120), full(1280, 640), full(160, 1920), full(160, 640), full(160, 128)]))(
                core, mine, theirs)


def shifted(array, axis, by):
    devices = lax.axis_size(axis)
    return lax.ppermute(array, axis, [(i, (i + by) % devices) for i in range(devices)])


def passed_along(array, by):
    devices = lax.axis_size(("z", "x"))
    return lax.ppermute(array, ("z", "x"), [(i, i + by) for i in range(devices) if 0 <= i + by < devices])


def swapped(array):
    return lax.ppermute(array, "core", [(0, 1), (1, 0)])


def pick(array, index):
    return lax.dynamic_index_in_dim(array, index, 0, keepdims=False)


def summed_share(array, axis):
    me, devices = lax.axis_index(axis), lax.axis_size(axis)
    total = pick(array, me).astype(f32)
    for by in (1, devices - 1, 2):
        total = total + shifted(pick(array, (me + by) % devices), axis, by).astype(f32)
    return total.astype(bf16)


def gathered(array, axis):
    me, devices = lax.axis_index(axis), lax.axis_size(axis)
    out = jnp.zeros((devices,) + array.shape, array.dtype)
    out = lax.dynamic_update_index_in_dim(out, array, me, 0)
    for by in (1, devices - 1, 2):
        out = lax.dynamic_update_index_in_dim(out, shifted(array, axis, by), (me + devices - by) % devices, 0)
    return out


def gathered_ring(array, axis):
    me, half = lax.axis_index(axis), array.shape[0] // 2
    before, after = shifted(array, axis, 1), shifted(array, axis, -1)
    far = jnp.concatenate([shifted(before[:half], axis, 1), shifted(after[half:], axis, -1)])
    out = jnp.zeros((4,) + array.shape, array.dtype)
    for by, part in ((0, array), (3, before), (1, after), (2, far)):
        out = lax.dynamic_update_index_in_dim(out, part, (me + by) % 4, 0)
    return out


def window_info(length_row, chip, core, win):
    ends = jnp.cumsum(length_row)
    starts = ends - length_row
    base = chip * 512 - 1024
    places = base + jnp.arange(win, dtype=jnp.int32)
    inside = (places[:, None] >= starts[None, :]) & (places[:, None] < ends[None, :])
    ones = jnp.broadcast_to(jnp.arange(64) < 3, (win, 64)).astype(bf16)
    key_rows = jnp.concatenate([jnp.where(inside, 0.0, -BIG).astype(bf16), ones], axis=1)
    own = chip * 512 + jnp.arange(512, dtype=jnp.int32)
    inside_q = (own[None, :] >= starts[:, None]) & (own[None, :] < ends[:, None])
    query_rows = jnp.concatenate([inside_q.astype(bf16), jnp.zeros((64, 512), bf16)], axis=0)
    info = [core]
    sizes = []
    for t in range(2):
        first = chip * 512 + t * TILE
        low = jnp.max(jnp.where(starts <= first, starts, 0)) - base
        high = jnp.min(jnp.where(ends > first + TILE - 1, ends, 1 << 30)) - base
        start = low // 128 * 128
        need = high - start
        size = (need + SHORT - 1) // SHORT * SHORT
        info.append(jnp.minimum(start, win - size))
        sizes.append(size)
    low = jnp.minimum(info[1], info[2]) // 512
    high = (jnp.maximum(info[1] + sizes[0], info[2] + sizes[1]) + 511) // 512
    return jnp.stack(info + sizes).astype(jnp.int32), key_rows, query_rows, [low, high]


def lane_tiles_down(array):
    return jnp.concatenate([array[:, 128 * t:128 * (t + 1)] for t in range(array.shape[1] // 128)], axis=0)


def body(tokens, lengths, gain_one, bias_one, w_qkv, w_out, gain_two, bias_two, w_up, w_down, cotangent):
    core, chip = lax.axis_index("core"), lax.axis_index(("z", "x"))
    core_arg, y_arg = core[None].astype(jnp.int32), lax.axis_index("batch")[None].astype(jnp.int32)
    tok, cot = tokens[:, 0], cotangent[:, 0].reshape(512, 640)

    together = lambda *arrays: lax.optimization_barrier(arrays)
    before, after, tok_other = passed_along(tok, 1), passed_along(tok, -1), swapped(tok)
    vectors = jnp.pad(jnp.stack([gain_one, bias_one, gain_two, bias_two]), ((0, 12), (0, 0)))
    heads = pack_heads(core_arg, w_qkv, vectors)
    heads_before, heads_after = shifted(heads, "batch", 1), shifted(heads, "batch", -1)
    heads, w_out, w_up, w_down = together(heads, w_out, w_up, w_down)
    feed_weights = lax.all_gather(pack_feed(core_arg, w_out, w_up, w_down), "batch", axis=0, tiled=True)
    w_out_all = feed_weights[:, 5120:]
    before, after, heads_before, heads_after = together(before, after, heads_before, heads_after)
    own = (passed_along(before, 1), before, tok, after, passed_along(after, -1))
    near, far = shifted(heads_before[:96], "batch", 1), shifted(heads_after[96:], "batch", -1)
    other = (swapped(own[0]), swapped(before), tok_other, swapped(after), swapped(own[4]))
    w_heads, vec = assemble(y_arg, heads, heads_before, heads_after, near, far)

    windows = [window_info(lengths[m, 0], chip, core, 2560) for m in range(2)]
    place = jnp.stack([core] + windows[0][3] + windows[1][3]).astype(jnp.int32)
    *near_parts, q, qT = project((1, 2, 3), place, own, other, vec, w_heads)
    k, v, kT, vT = project((0, 4), place, own, other, vec, w_heads, near_parts)
    (oT0, low0, lse0), (oT1, low1, lse1) = (
        attend(m, info, qT, k, vT, key_rows, query_rows) for m, (info, key_rows, query_rows, _) in enumerate(windows))

    theirs = swapped(jnp.stack([low0, low1]))
    middle, hidden_two, hidden_other = middle_step(core_arg, low0, low1, theirs, tok, tok_other, w_out_all, vec)
    mine, partial, feed_grads = feed_forward(hidden_two, hidden_other, cot, swapped(cot), feed_weights)
    feed_grads = lax.psum_scatter(feed_grads.reshape(5120, 640), ("z", "x"), scatter_dimension=0, tiled=True).reshape(4, 80, 640)
    block_out, grad_middle, branch, g_two = after_feed(middle, mine, swapped(partial), cot, vec)

    do, doT, g_out = branch_step(core_arg, branch, swapped(branch), w_out_all, low0, low1, theirs)
    dq, dk, dv = zip(*(
        attend_back(m, info, qT, q, k, kT, v, doT, do, oT, lse, key_rows, query_rows)
        for m, ((info, key_rows, query_rows, _), oT, lse) in enumerate(zip(windows, (oT0, oT1), (lse0, lse1)))))
    mine, theirs, tail = project_back(place, own, other, vec, w_heads, dq, dk, dv, g_out, g_two)

    tail = lax.all_to_all(tail, ("batch", "z", "x"), 0, 0, tiled=True)
    tail = jnp.sum(tail.astype(f32), axis=0).astype(bf16)
    feed = summed_share(feed_grads, "batch")
    theirs = swapped(theirs)
    sums = [mine[j].astype(f32) + theirs[j].astype(f32) for j in range(5)]
    shares = jnp.concatenate([lane_tiles_down(feed), lane_tiles_down(tail)], axis=0)
    shares, right, left = together(shares, sums[4].astype(bf16), sums[0].astype(bf16))
    shares = gathered(shares, "x").reshape(2080, 128)
    right = (passed_along(right, 1).astype(f32) + sums[3]).astype(bf16)
    left = (passed_along(left, -1).astype(f32) + sums[1]).astype(bf16)
    shares, right, left = together(shares, right, left)
    d_one = sums[2] + passed_along(right, 1).astype(f32) + passed_along(left, -1).astype(f32)
    n_one, r_one = moments(tok.reshape(512, 640).astype(f32))
    grad_tokens = (grad_middle + norm_back(d_one.reshape(512, 640), n_one, r_one, vec[0:1])).astype(bf16)
    shares = gathered_ring(shares, "z").reshape(16, 520, 128)
    grad_up, grad_down, grad_qkv, grad_out, spare = final_step(core_arg, shares, swapped(shares))
    return (
        block_out.reshape(2, 1, 256, 640), grad_tokens.reshape(2, 1, 256, 640), spare[:, 0], spare[:, 1], grad_qkv, grad_out,
        spare[:, 2], spare[:, 3], grad_up, grad_down)


def solution(mesh):
    fine = Mesh(mesh.devices.reshape(4, 4, 4, 2), ("batch", "z", "x", "core"))
    rows = P(None, "batch", ("z", "x", "core"), None)
    one, two = P("batch"), P("batch", None)
    return jax.shard_map(
        body,
        mesh=fine,
        in_specs=(rows, P(None, "batch", None), one, one, two, two, one, one, two, two, rows),
        out_specs=(rows, rows, one, one, two, two, one, one, two, two),
        check_vma=False,
    )
```

```python
import math

import jax
import jax.numpy as jnp
from jax import lax
from jax.experimental import pallas as pl
from jax.experimental.pallas import tpu as pltpu
from jax.sharding import Mesh
from jax.sharding import PartitionSpec as P

HEAD_DIM = 32
SCALE = HEAD_DIM ** -0.5
LOG2E = math.log2(math.e)
C2 = SCALE * LOG2E
BIG = 1e30
TILE = 256
EPSILON = 1e-05
PAIRS = 5
SHORT, LONG = 384, 1152
f32, bf16 = jnp.float32, jnp.bfloat16
NT = (((1,), (1,)), ((), ()))


def pair_offset(info_ref):
    p = pl.program_id(0)
    sub = jnp.where(p == PAIRS - 1, info_ref[0], lax.rem(p, 2))
    return sub * (2 * HEAD_DIM)


def split3(v):
    a = v.astype(bf16)
    r = v - a.astype(f32)
    b = r.astype(bf16)
    d = (r - b.astype(f32)).astype(bf16)
    return a, b, d


def rows_masked(xT, off):
    row = lax.broadcasted_iota(jnp.int32, xT.shape, 0) - off
    xf = xT.astype(f32)
    return [jnp.where((row >= HEAD_DIM * j) & (row < HEAD_DIM * (j + 1)), xf, 0.0).astype(bf16) for j in range(2)]


def lanes_masked(x, off):
    lane = lax.broadcasted_iota(jnp.int32, x.shape, 1) - off
    xf = x.astype(f32)
    return [jnp.where((lane >= HEAD_DIM * j) & (lane < HEAD_DIM * (j + 1)), xf, 0.0).astype(bf16) for j in range(2)]


def attend_kernel(info_ref, qT_ref, k_ref, vT_ref, kaug_ref, qaugT_ref, oT_ref, o_ref, l_ref, rhs):
    off = pair_offset(info_ref)
    oT_ref[...] = jnp.where(lax.rem(pl.program_id(0), 2) == 0, 0.0, oT_ref[...])
    for t in range(2):
        cols = slice(t * TILE, (t + 1) * TILE)
        masked = rows_masked(qT_ref[:, cols], off)
        for j in range(2):
            rhs[0:128, j * TILE:(j + 1) * TILE] = masked[j]
            rhs[128:256, j * TILE:(j + 1) * TILE] = qaugT_ref[:, cols]
        start = info_ref[1 + t]
        need = info_ref[3 + t]

        def block(first, size):
            def step(i, carry):
                row = pl.multiple_of(first + i * size, 128)
                lhs = jnp.concatenate([k_ref[pl.ds(row, size), :], kaug_ref[pl.ds(row, size), :]], axis=1)
                raw = [jnp.dot(lhs, rhs[:, j * TILE:(j + 1) * TILE], preferred_element_type=f32) for j in range(2)]
                out = []
                for j in range(2):
                    m, l, o = carry[j]
                    s = raw[j] * C2
                    m_new = jnp.maximum(m, jnp.max(s, axis=0, keepdims=True))
                    alpha = jnp.exp2(m - m_new)
                    p = jnp.exp2(s - m_new)
                    vT = vT_ref[pl.ds(pl.multiple_of(off + j * HEAD_DIM, HEAD_DIM), HEAD_DIM), pl.ds(row, size)]
                    out.append((m_new, l * alpha + jnp.sum(p, axis=0, keepdims=True),
                                o * alpha + jnp.dot(vT, p.astype(bf16), preferred_element_type=f32)))
                return tuple(out)
            return step

        def finish(state):
            for j in range(2):
                m, l, o = state[j]
                oT_ref[pl.ds(pl.multiple_of(off + j * HEAD_DIM, HEAD_DIM), HEAD_DIM), cols] = o * (1.0 / l)
                l_ref[0, j:j + 1, cols] = m + jnp.log2(l)

        init = tuple((jnp.full((1, TILE), -1e38, f32), jnp.zeros((1, TILE), f32), jnp.zeros((HEAD_DIM, TILE), f32)) for _ in range(2))

        longs = lax.div(need, LONG)
        state = lax.fori_loop(0, longs, block(start, LONG), init)
        finish(lax.fori_loop(0, lax.div(need - longs * LONG, SHORT), block(start + longs * LONG, SHORT), state))

    o_ref[...] = oT_ref[...].T.astype(bf16)


def attend(m, info, qT, k, vT, kaug, qaugT):
    win = k.shape[1]
    nq = qT.shape[2]
    return pl.pallas_call(
        attend_kernel,
        out_shape=(jax.ShapeDtypeStruct((384, nq), f32), jax.ShapeDtypeStruct((nq, 384), bf16), jax.ShapeDtypeStruct((PAIRS, 8, nq), f32)),
        grid_spec=pltpu.PrefetchScalarGridSpec(
            num_scalar_prefetch=1, grid=(PAIRS,),
            in_specs=[
                pl.BlockSpec((None, 128, nq), lambda p, *_: (m, p // 2, 0)),
                pl.BlockSpec((None, win, 128), lambda p, *_: (m, 0, p // 2)),
                pl.BlockSpec((None, 128, win), lambda p, *_: (m, p // 2, 0)),
                pl.BlockSpec((win, 128), lambda p, *_: (0, 0)),
                pl.BlockSpec((128, nq), lambda p, *_: (0, 0)),
            ],
            out_specs=[
                pl.BlockSpec((128, nq), lambda p, *_: (p // 2, 0)),
                pl.BlockSpec((nq, 128), lambda p, *_: (0, p // 2)),
                pl.BlockSpec((1, 8, nq), lambda p, *_: (p, 0, 0)),
            ],
            scratch_shapes=[pltpu.VMEM((256, 2 * TILE), bf16)],
        ),
        compiler_params=pltpu.CompilerParams(vmem_limit_bytes=28 << 20),
        cost_estimate=pl.CostEstimate(flops=20 * 10**9, bytes_accessed=6 << 20, transcendentals=5 * 10**6),
        name="attend",
    )(info, qT, k, vT, kaug, qaugT)


def attend_back_kernel(info_ref, qT_ref, q_ref, k_ref, kT_ref, v_ref, doT_ref, do_ref, oT_ref, l_ref, kaug_ref, qaugT_ref,
                       dq_ref, dk_ref, dv_ref, dqT_ref, rhs_s, rhs_d, q_stk, do_stk, dk_acc, dv_acc):
    p_id = pl.program_id(0)
    off = pair_offset(info_ref)

    @pl.when(lax.rem(p_id, 2) == 0)
    def _():
        dqT_ref[...] = jnp.zeros_like(dqT_ref)
        dk_acc[...] = jnp.zeros_like(dk_acc)
        dv_acc[...] = jnp.zeros_like(dv_acc)

    for t in range(2):
        cols = slice(t * TILE, (t + 1) * TILE)
        masked_q = rows_masked(qT_ref[:, cols], off)
        masked_do = rows_masked(doT_ref[:, cols], off)
        lane_q = lanes_masked(q_ref[cols, :], off)
        lane_do = lanes_masked(do_ref[cols, :], off)
        for j in range(2):
            part = slice(j * TILE, (j + 1) * TILE)
            head = pl.ds(pl.multiple_of(off + j * HEAD_DIM, HEAD_DIM), HEAD_DIM)
            delta = jnp.sum(doT_ref[head, cols].astype(f32) * oT_ref[head, cols], axis=0, keepdims=True)
            total = l_ref[0, j:j + 1, cols] * (1.0 / C2)
            rowid = lax.broadcasted_iota(jnp.int32, (64, TILE), 0)
            lp, dp = split3(-total), split3(-delta)
            def pieces(parts):
                x = jnp.zeros((64, TILE), f32)
                for n in range(3):
                    x = jnp.where(rowid == n, parts[n].astype(f32), x)
                return x.astype(bf16)
            rhs_s[0:128, part] = masked_q[j]
            rhs_s[128:192, part] = qaugT_ref[0:64, cols]
            rhs_s[192:256, part] = pieces(lp)
            rhs_d[0:128, part] = masked_do[j]
            rhs_d[128:192, part] = jnp.zeros((64, TILE), bf16)
            rhs_d[192:256, part] = pieces(dp)
            q_stk[part, :] = lane_q[j]
            do_stk[part, :] = lane_do[j]
        start = info_ref[1 + t]
        need = info_ref[3 + t]

        def block(first, size):
            def step(i, carry):
                row = pl.multiple_of(first + i * size, 128)
                rows = pl.ds(row, size)
                aug = kaug_ref[rows, :]
                lhs_k = jnp.concatenate([k_ref[rows, :], aug], axis=1)
                lhs_v = jnp.concatenate([v_ref[rows, :], aug], axis=1)
                out, dv, dk = [], dv_acc[rows, :], dk_acc[rows, :]
                for j in range(2):
                    part = slice(j * TILE, (j + 1) * TILE)
                    s = jnp.dot(lhs_k, rhs_s[:, part], preferred_element_type=f32)
                    dp = jnp.dot(lhs_v, rhs_d[:, part], preferred_element_type=f32)
                    p = jnp.exp2(s * C2)
                    ds = (p * dp).astype(bf16)
                    dv = dv + jnp.dot(p.astype(bf16), do_stk[part, :], preferred_element_type=f32)
                    dk = dk + jnp.dot(ds, q_stk[part, :], preferred_element_type=f32)
                    kT = kT_ref[pl.ds(pl.multiple_of(off + j * HEAD_DIM, HEAD_DIM), HEAD_DIM), rows]
                    out.append(carry[j] + jnp.dot(kT, ds, preferred_element_type=f32))
                dv_acc[rows, :] = dv
                dk_acc[rows, :] = dk
                return tuple(out)
            return step

        def finish(dqs):
            for j in range(2):
                dqT_ref[pl.ds(pl.multiple_of(off + j * HEAD_DIM, HEAD_DIM), HEAD_DIM), cols] = dqs[j] * SCALE

        init = tuple(jnp.zeros((HEAD_DIM, TILE), f32) for _ in range(2))

        longs = lax.div(need, LONG)
        state = lax.fori_loop(0, longs, block(start, LONG), init)
        finish(lax.fori_loop(0, lax.div(need - longs * LONG, SHORT), block(start + longs * LONG, SHORT), state))
    @pl.when((lax.rem(p_id, 2) == 1) | (p_id == PAIRS - 1))
    def _():
        dq_ref[...] = dqT_ref[...].T.astype(bf16)
        dk_ref[...] = (dk_acc[...] * SCALE).astype(bf16)
        dv_ref[...] = dv_acc[...].astype(bf16)


def attend_back(m, info, qT, q, k, kT, v, doT, do, oT, lse, kaug, qaugT):
    win, nq = k.shape[1], qT.shape[2]
    wide = pl.BlockSpec((128, nq), lambda p, *_: (p // 2, 0))
    tall = pl.BlockSpec((nq, 128), lambda p, *_: (0, p // 2))
    keys = pl.BlockSpec((win, 128), lambda p, *_: (0, p // 2))
    wide_m = pl.BlockSpec((None, 128, nq), lambda p, *_: (m, p // 2, 0))
    tall_m = pl.BlockSpec((None, nq, 128), lambda p, *_: (m, 0, p // 2))
    keys_m = pl.BlockSpec((None, win, 128), lambda p, *_: (m, 0, p // 2))
    return pl.pallas_call(
        attend_back_kernel,
        out_shape=(far(nq, 384), far(win, 384), far(win, 384)),
        grid_spec=pltpu.PrefetchScalarGridSpec(
            num_scalar_prefetch=1, grid=(PAIRS,),
            in_specs=[wide_m, tall_m, keys_m, pl.BlockSpec((None, 128, win), lambda p, *_: (m, p // 2, 0)), keys_m,
                      pl.BlockSpec((128, nq), lambda p, *_: (p // 2, m)), pl.BlockSpec((nq, 128), lambda p, *_: (m, p // 2)), wide,
                      pl.BlockSpec((1, 8, nq), lambda p, *_: (p, 0, 0)),
                      pl.BlockSpec((win, 128), lambda p, *_: (0, 0)), pl.BlockSpec((128, nq), lambda p, *_: (0, 0))],
            out_specs=[tall, keys, keys],
            scratch_shapes=[pltpu.VMEM((128, nq), f32), pltpu.VMEM((256, 2 * TILE), bf16), pltpu.VMEM((256, 2 * TILE), bf16),
                            pltpu.VMEM((2 * TILE, 128), bf16), pltpu.VMEM((2 * TILE, 128), bf16),
                            pltpu.VMEM((win, 128), f32), pltpu.VMEM((win, 128), f32)],
        ),
        compiler_params=pltpu.CompilerParams(vmem_limit_bytes=32 << 20),
        cost_estimate=pl.CostEstimate(flops=40 * 10**9, bytes_accessed=12 << 20, transcendentals=5 * 10**6),
        name="attend_back",
    )(info, qT, q, k, kT, v, doT, do, oT, lse, kaug, qaugT)


def moments(x):
    centred = x - jnp.mean(x, axis=-1, keepdims=True)
    r = lax.rsqrt(jnp.mean(centred * centred, axis=-1, keepdims=True) + EPSILON)
    return centred * r, r


def norm_back(grad, n, r, gain):
    e = grad * gain
    return r * (e - jnp.mean(e, axis=-1, keepdims=True) - n * jnp.mean(e * n, axis=-1, keepdims=True))


def call(kernel, out_shape, name, flops=10**9, limit=48, **spec):
    return pl.pallas_call(
        kernel, out_shape=out_shape, name=name,
        compiler_params=pltpu.CompilerParams(vmem_limit_bytes=limit << 20),
        cost_estimate=pl.CostEstimate(flops=flops, bytes_accessed=8 << 20, transcendentals=0), **spec)


def shape(*dims, dtype=bf16):
    return jax.ShapeDtypeStruct(dims, dtype)


def far(*dims):
    return pltpu.MemorySpace.HBM(dims, bf16)


def scalar_first(grid, in_specs, out_specs, scratch=()):
    return dict(grid_spec=pltpu.PrefetchScalarGridSpec(
        num_scalar_prefetch=1, grid=grid, in_specs=in_specs, out_specs=out_specs, scratch_shapes=list(scratch)))


def full(*dims):
    return pl.BlockSpec(dims, lambda *_: (0,) * len(dims))


def pack_heads_kernel(core_ref, qkv_ref, vec_ref, heads_ref):
    for part in range(3):
        near = pl.ds(pl.multiple_of(640 * part + 256 * core_ref[0], 128), 256)
        heads_ref[0:160, 384 * part:384 * part + 256] = qkv_ref[:, near]
        heads_ref[0:160, 384 * part + 256:384 * (part + 1)] = qkv_ref[:, 640 * part + 512:640 * (part + 1)]
    heads_ref[160:176, :] = jnp.zeros((16, 1152), bf16)
    heads_ref[160:176, 0:160] = vec_ref[...]


def pack_heads(core, w_qkv, vectors):
    return call(pack_heads_kernel, shape(176, 1152), "pack_heads", 10**6, 8, **scalar_first(
        (1,), [full(160, 1920), full(16, 160)], full(176, 1152)))(core, w_qkv, vectors)


def pack_feed_kernel(core_ref, out_ref, up_ref, down_ref, feed_ref):
    core = core_ref[0]
    for f in range(4):
        feed_ref[:, 640 * f:640 * (f + 1)] = up_ref[:, pl.ds(pl.multiple_of(1280 * f + 640 * core, 128), 640)]
        feed_ref[:, 2560 + 640 * f:2560 + 640 * (f + 1)] = down_ref[pl.ds(pl.multiple_of(640 * core + 160 * f, 32), 160), :]
    feed_ref[:, 5120:5760] = out_ref[...]


def pack_feed(core, w_out, w_up, w_down):
    args = (w_out, w_up, w_down)
    return call(pack_feed_kernel, shape(160, 5760), "pack_feed", 10**6, 16, **scalar_first(
        (1,), [full(*a.shape) for a in args], full(160, 5760)))(core, *args)


def assemble_kernel(y_ref, own_ref, before_ref, after_ref, near_ref, far_ref, heads_ref, vec_ref):
    total = jnp.zeros((16, 640), f32)

    def place(by, top, bottom, vec):
        nonlocal total
        row = lax.rem(y_ref[0] + by, 4) * 160
        for part, base in ((top, 0), (bottom, top.shape[0])):
            heads_ref[pl.ds(pl.multiple_of(row + base, 32), part.shape[0]), :] = part
        total = total + pltpu.roll(vec[:, :640].astype(f32), row, 1)

    for by, ref in ((0, own_ref), (3, before_ref), (1, after_ref)):
        place(by, ref[0:96, :], ref[96:160, :], ref[160:176, :])
    place(2, near_ref[...], far_ref[0:64, :], far_ref[64:80, :])
    vec_ref[...] = total


def assemble(y, *parts):
    return call(assemble_kernel, (shape(640, 1152), shape(16, 640, dtype=f32)), "assemble", 10**6, 12, **scalar_first(
        (1,), [full(*a.shape) for a in parts], [full(640, 1152), full(16, 640)]))(y, *parts)


def rows_in_order(core, mine, theirs, x_ref):
    mine, theirs = mine.astype(f32), theirs.astype(f32)
    x_ref[0:256, :] = jnp.where(core == 0, mine, theirs)
    x_ref[256:512, :] = jnp.where(core == 0, theirs, mine)


def window_rows(core, own_refs, other_refs, m, block, x_ref):
    for j in range(len(own_refs)):
        @pl.when(block == j)
        def _():
            rows_in_order(core, own_refs[j][m], other_refs[j][m], x_ref)


def project_kernel(chips, place_ref, *refs):
    n = len(chips)
    own_refs, other_refs = refs[:n], refs[n:2 * n]
    vec_ref, w_ref = refs[2 * n:2 * n + 2]
    k_ref, v_ref, kT_ref, vT_ref = refs[-6 - 2 * (n == 3):][:4]
    x_ref, hid_ref = refs[-2:]
    m, step = pl.program_id(0), pl.program_id(1)
    block = sum(jnp.where(step == i, chip, 0) for i, chip in enumerate(chips))
    needed = (block >= place_ref[1 + 2 * m]) & (block < place_ref[2 + 2 * m])

    @pl.when(jnp.logical_not(needed))
    def _():
        for ref in (k_ref, v_ref, kT_ref, vT_ref):
            ref[...] = jnp.zeros_like(ref)

    @pl.when(needed)
    def _():
        window_rows(place_ref[0], own_refs, other_refs, m, step, x_ref)
        hidden = (moments(x_ref[...])[0] * vec_ref[0:1, :] + vec_ref[1:2, :]).astype(bf16)
        hid_ref[...] = hidden
        kv = jnp.dot(hidden, w_ref[:, 384:], preferred_element_type=f32)
        low = kv.astype(bf16)
        k_ref[0] = low[:, :384]
        v_ref[0] = low[:, 384:]
        turned = kv.T.astype(bf16)
        kT_ref[0] = turned[:384]
        vT_ref[0] = turned[384:]

    if n == 3:
        q_ref, qT_ref = refs[-4:-2]

        @pl.when(step == 1)
        def _():
            q = jnp.dot(hid_ref[...], w_ref[:, :384], preferred_element_type=f32)
            q_ref[0] = q.astype(bf16)
            qT_ref[0] = q.T.astype(bf16)


def project(chips, place, own, other, vec, w, earlier=()):
    n = len(chips)
    chip = (lambda b: b + 1) if n == 3 else (lambda b: 4 * b)
    tall = pl.BlockSpec((1, 512, 384), lambda m, b, *_: (m, chip(b), 0))
    wide = pl.BlockSpec((1, 384, 512), lambda m, b, *_: (m, 0, chip(b)))
    shapes = [far(2, 2560, 384), far(2, 2560, 384), far(2, 384, 2560), far(2, 384, 2560)]
    specs = [tall, tall, wide, wide]
    if n == 3:
        shapes += [far(2, 512, 384), far(2, 384, 512)]
        specs += [pl.BlockSpec((1, 512, 384), lambda m, *_: (m, 0, 0)), pl.BlockSpec((1, 384, 512), lambda m, *_: (m, 0, 0))]
    own, other = [own[c] for c in chips], [other[c] for c in chips]
    return call(
        lambda *refs: project_kernel(chips, *refs), shapes, "project", 5 * 10**9, 28,
        input_output_aliases={2 * n + 3 + i: i for i in range(len(earlier))}, **scalar_first(
            (2, n), [full(2, 256, 640)] * (2 * n) + [full(16, 640), full(640, 1152)] + [pl.BlockSpec(memory_space=pl.ANY)] * len(earlier),
            specs, [pltpu.VMEM((512, 640), f32), pltpu.VMEM((512, 640), bf16)]))(place, *own, *other, vec, w, *earlier)


def heads_joined(core, mine, theirs):
    first, second = (jnp.where(core == 0, a, b) for a, b in ((mine, theirs), (theirs, mine)))
    return jnp.concatenate([first[:, :256], second[:, :256], first[:, 256:] + second[:, 256:]], axis=1)


def middle_kernel(core_ref, low0_ref, low1_ref, theirs_ref, tok_ref, tok2_ref, w_ref, vec_ref, mid_ref, hid_ref, hid2_ref):
    core = core_ref[0]
    for m, low_ref in enumerate((low0_ref, low1_ref)):
        attended = heads_joined(core, low_ref[...].astype(f32), theirs_ref[m].astype(f32)).astype(bf16)
        branch = jnp.dot(attended, w_ref[...], preferred_element_type=f32)
        mine = jnp.where(core == 0, branch[:256], branch[256:]) + tok_ref[m].astype(f32)
        theirs = jnp.where(core == 0, branch[256:], branch[:256]) + tok2_ref[m].astype(f32)
        part = slice(256 * m, 256 * (m + 1))
        mid_ref[part, :] = mine
        hid_ref[part, :] = (moments(mine)[0] * vec_ref[2:3, :] + vec_ref[3:4, :]).astype(bf16)
        hid2_ref[part, :] = (moments(theirs)[0] * vec_ref[2:3, :] + vec_ref[3:4, :]).astype(bf16)


def middle_step(core, *args):
    return call(middle_kernel, (shape(512, 640, dtype=f32), shape(512, 640), shape(512, 640)), "middle", 10**9, 20, **scalar_first(
        (1,), [full(*a.shape) for a in args], [full(512, 640)] * 3))(core, *args)


def feed_kernel(h_ref, h2_ref, cot_ref, cot2_ref, up_ref, down_ref, mine_ref, theirs_ref, g_ref, h, cot, hT, cT, out, dh):
    chunk = pl.program_id(0)

    @pl.when(chunk == 0)
    def _():
        h[0:512, :], h[512:1024, :] = h_ref[...], h2_ref[...]
        cot[0:512, :], cot[512:1024, :] = cot_ref[...], cot2_ref[...]
        hT[...] = h[...].astype(f32).T.astype(bf16)
        cT[...] = cot[...].astype(f32).T.astype(bf16)
        out[...] = jnp.zeros_like(out)
        dh[...] = jnp.zeros_like(dh)

    up_w = up_ref[...]
    down_w = jnp.concatenate([down_ref[160 * y:160 * (y + 1), 640 * i:640 * (i + 1)] for y in range(2) for i in range(4)], axis=0)
    acts, d_ups = [], []
    for t in range(4):
        rows = slice(256 * t, 256 * (t + 1))
        u = jnp.dot(h[rows, :], up_w, preferred_element_type=f32)
        d_act = lax.dot_general(cot[rows, :], down_w, NT, preferred_element_type=f32)
        cdf = 0.5 * (1.0 + lax.erf(u * (2.0 ** -0.5)))
        pdf = jnp.exp(u * u * -0.5) * ((2.0 * math.pi) ** -0.5)
        act = (u * cdf).astype(bf16)
        d_up = (d_act * (cdf + u * pdf)).astype(bf16)
        out[rows, :] += jnp.dot(act, down_w, preferred_element_type=f32)
        dh[rows, :] += lax.dot_general(d_up, up_w, NT, preferred_element_type=f32)
        acts.append(act)
        d_ups.append(d_up)
    g_up = jnp.dot(hT[...], jnp.concatenate(d_ups, axis=0), preferred_element_type=f32).astype(bf16)
    g_down = jnp.dot(cT[...], jnp.concatenate(acts, axis=0), preferred_element_type=f32).T.astype(bf16)
    for f in range(2):
        for y in range(4):
            for i in range(2):
                g_ref[4 * chunk + 2 * f + i, y] = g_up[160 * y + 80 * i:160 * y + 80 * (i + 1), 640 * f:640 * (f + 1)]
        for i in range(8):
            g_ref[8 + i, 2 * chunk + f] = g_down[640 * f + 80 * i:640 * f + 80 * (i + 1)]

    @pl.when(chunk == 1)
    def _():
        mine_ref[0], mine_ref[1] = out[0:512, :].astype(bf16), dh[0:512, :].astype(bf16)
        theirs_ref[0], theirs_ref[1] = out[512:1024, :].astype(bf16), dh[512:1024, :].astype(bf16)


def feed_forward(h, h2, cot, cot2, weights):
    return call(
        feed_kernel,
        (shape(2, 512, 640), shape(2, 512, 640), shape(16, 4, 80, 640)),
        "feed_forward", 30 * 10**9, 52, grid=(2,),
        in_specs=[full(512, 640)] * 4 + [pl.BlockSpec((640, 1280), lambda f: (0, f)), pl.BlockSpec((320, 2560), lambda f: (f, 1))],
        out_specs=[full(2, 512, 640), full(2, 512, 640), full(16, 4, 80, 640)],
        scratch_shapes=[pltpu.VMEM((1024, 640), bf16), pltpu.VMEM((1024, 640), bf16), pltpu.VMEM((640, 1024), bf16), pltpu.VMEM((640, 1024), bf16),
                        pltpu.VMEM((1024, 640), f32), pltpu.VMEM((1024, 640), f32)],
    )(h, h2, cot, cot2, weights, weights)


def after_kernel(mid_ref, mine_ref, theirs_ref, cot_ref, vec_ref, block_ref, grad_ref, branch_ref, g_ref):
    @pl.when(pl.program_id(0) == 0)
    def _():
        g_ref[...] = jnp.zeros_like(g_ref)

    middle = mid_ref[...]
    block_ref[...] = (middle + mine_ref[0].astype(f32) + theirs_ref[0].astype(f32)).astype(bf16)
    d_hidden = mine_ref[1].astype(f32) + theirs_ref[1].astype(f32)
    n, r = moments(middle)
    g_ref[0:1, :] += jnp.sum(d_hidden * n, axis=0, keepdims=True)
    g_ref[1:2, :] += jnp.sum(d_hidden, axis=0, keepdims=True)
    grad = cot_ref[...].astype(f32) + norm_back(d_hidden, n, r, vec_ref[2:3, :])
    grad_ref[...] = grad
    branch_ref[...] = grad.astype(bf16)


def after_feed(*args):
    rows, pair = pl.BlockSpec((128, 640), lambda i: (i, 0)), pl.BlockSpec((2, 128, 640), lambda i: (0, i, 0))
    return call(
        after_kernel, (shape(512, 640), shape(512, 640, dtype=f32), shape(512, 640), shape(8, 640, dtype=f32)), "after_feed", 10**9, 16,
        grid=(4,), in_specs=[rows, pair, pair, rows, full(16, 640)], out_specs=[rows, rows, rows, full(8, 640)])(*args)


def branch_kernel(core_ref, own_ref, their_ref, w_ref, low0_ref, low1_ref, theirs_ref, do_ref, doT_ref, g_ref):
    core = core_ref[0]
    w = jnp.concatenate([w_ref[pl.ds(pl.multiple_of(256 * core, 256), 256), :], w_ref[512:640, :]], axis=0)
    g = jnp.zeros((640, 384), f32)
    for m in range(2):
        part = slice(256 * m, 256 * (m + 1))
        mine, theirs = own_ref[part, :].astype(f32), their_ref[part, :].astype(f32)
        branch = jnp.concatenate([jnp.where(core == 0, mine, theirs), jnp.where(core == 0, theirs, mine)], axis=0)
        kept = jnp.where(core == 0, branch[:, :384], branch[:, 256:]).astype(bf16)
        branch = branch.astype(bf16)
        rows = slice(512 * m, 512 * (m + 1))
        do = lax.dot_general(branch, w, NT, preferred_element_type=f32)
        do_ref[rows, :] = do.astype(bf16)
        doT_ref[:, rows] = do.T.astype(bf16)
        attended = heads_joined(core, (low0_ref, low1_ref)[m][...].astype(f32), theirs_ref[m].astype(f32))
        g = g + jnp.dot(attended.T.astype(bf16), kept, preferred_element_type=f32)
    g_ref[...] = g


def branch_step(core, *args):
    specs = [full(*a.shape) for a in args]
    return call(
        branch_kernel, (shape(1024, 384), shape(384, 1024), shape(640, 384, dtype=f32)), "branch", 10**9, 24, **scalar_first(
            (1,), specs, [full(1024, 384), full(384, 1024), full(640, 384)]))(core, *args)


def project_back_kernel(m, place_ref, *refs):
    own_refs, other_refs = refs[:5], refs[5:10]
    vec_ref, w_ref, dq_ref, dk_ref, dv_ref = refs[10:15]
    x_ref, d_hid = refs[-2:]
    if m == 0:
        mine_ref, theirs_ref, g_ref, g_vec = refs[15:19]
    else:
        g0_ref, g_vec0_ref, g_out_ref, g_two_ref, mine_ref, theirs_ref, tail_ref, g_ref, g_vec = refs[15:24]
    block, core = pl.program_id(0), place_ref[0]
    needed = (block >= place_ref[1 + 2 * m]) & (block < place_ref[2 + 2 * m])

    @pl.when(block == 0)
    def _():
        if m == 0:
            g_ref[...] = jnp.zeros_like(g_ref)
            g_vec[...] = jnp.zeros_like(g_vec)
        else:
            g_ref[...] = g0_ref[...]
            g_vec[...] = g_vec0_ref[...]
            g_vec[2:4, :] = g_two_ref[0:2, :]

    @pl.when(jnp.logical_not(needed))
    def _():
        mine_ref[...] = jnp.zeros_like(mine_ref)
        theirs_ref[...] = jnp.zeros_like(theirs_ref)

    @pl.when(needed)
    def _():
        window_rows(core, own_refs, other_refs, 0, block, x_ref)
        n = moments(x_ref[...])[0]
        hiddenT = (n * vec_ref[0:1, :] + vec_ref[1:2, :]).T.astype(bf16)
        d_kv = jnp.concatenate([dk_ref[...], dv_ref[...]], axis=1)
        d_hid[...] = lax.dot_general(d_kv, w_ref[:, 384:], NT, preferred_element_type=f32)
        g_ref[:, 384:] += jnp.dot(hiddenT, d_kv, preferred_element_type=f32)

        @pl.when(block == 2)
        def _():
            g_ref[:, :384] += jnp.dot(hiddenT, dq_ref[...], preferred_element_type=f32)
            d_hid[...] += lax.dot_general(dq_ref[...], w_ref[:, :384], NT, preferred_element_type=f32)

        dh = d_hid[...]
        mine_ref[0] = jnp.where(core == 0, dh[:256], dh[256:]).astype(bf16)
        theirs_ref[0] = jnp.where(core == 0, dh[256:], dh[:256]).astype(bf16)
        g_vec[0:1, :] += jnp.sum(dh * n, axis=0, keepdims=True)
        g_vec[1:2, :] += jnp.sum(dh, axis=0, keepdims=True)

    if m == 1:
        @pl.when(block == 4)
        def _():
            turned = g_vec[...].T
            lane = lax.broadcasted_iota(jnp.int32, (640, 128), 1) - 64 * (1 - core)
            spare = g_ref[:, 256:384]
            for i in range(4):
                spare = jnp.where(lane == i, turned[:, i:i + 1], spare)
            g_ref[:, 256:384] = spare
            for y in range(4):
                for z in range(4):
                    rows = slice(160 * y + 40 * z, 160 * y + 40 * (z + 1))
                    for x in range(3):
                        tail_ref[16 * y + 4 * z + x] = g_ref[rows, 384 * x:384 * (x + 1)].astype(bf16)
                    tail_ref[16 * y + 4 * z + 3] = g_out_ref[rows, :].astype(bf16)


def project_back(m, place, own, other, vec, w, dq, dk, dv, *rest):
    keys = pl.BlockSpec((512, 384), lambda b, *_: (b, 0))
    tokens = pl.BlockSpec((1, 256, 640), lambda *_: (m, 0, 0))
    part = pl.BlockSpec((1, 256, 640), lambda b, *_: (b, 0, 0))
    sums, sum_specs = (shape(640, 1152, dtype=f32), shape(8, 640, dtype=f32)), [full(640, 1152), full(8, 640)]
    scratch = [pltpu.VMEM((512, 640), f32), pltpu.VMEM((512, 640), f32)]
    if m == 1:
        scratch = [pltpu.VMEM(a.shape, f32) for a in sums] + scratch
        sums, sum_specs = (shape(64, 40, 384),), [full(64, 40, 384)]
    return call(
        lambda *refs: project_back_kernel(m, *refs), (shape(5, 256, 640), shape(5, 256, 640)) + sums, "project_back", 5 * 10**9, 32,
        **scalar_first((5,), [tokens] * 10 + [full(16, 640), full(640, 1152), full(512, 384), keys, keys] + [full(*a.shape) for a in rest],
                       [part, part] + sum_specs, scratch))(place, *own, *other, vec, w, dq, dk, dv, *rest)


def in_core_order(core_ref, mine, theirs):
    core, mine, theirs = core_ref[0], mine.astype(f32), theirs.astype(f32)
    return jnp.where(core == 0, mine, theirs), jnp.where(core == 0, theirs, mine)


def final_feed_kernel(core_ref, mine_ref, theirs_ref, up_ref, down_ref):
    for i in range(16):
        for c, piece in enumerate(in_core_order(core_ref, mine_ref[i], theirs_ref[i])):
            if i < 8:
                base = 1280 * (i // 2) + 640 * c
                up_ref[80 * (i % 2):80 * (i % 2 + 1), base:base + 640] = piece
            else:
                base = 640 * c + 80 * (i - 8)
                down_ref[base:base + 80, :] = piece


def final_feed(core, mine, theirs):
    return call(final_feed_kernel, (shape(160, 5120, dtype=f32), shape(1280, 640, dtype=f32)), "final_feed", 10**6, 32, **scalar_first(
        (1,), [full(16, 80, 640)] * 2, [full(160, 5120), full(1280, 640)]))(core, mine, theirs)


def final_heads_kernel(core_ref, mine_ref, theirs_ref, qkv_ref, out_ref, vec_ref):
    lane = lax.broadcasted_iota(jnp.int32, (40, 128), 1)
    for z in range(4):
        rows = slice(40 * z, 40 * (z + 1))
        for x in range(4):
            a, b = in_core_order(core_ref, mine_ref[4 * z + x], theirs_ref[4 * z + x])
            if x < 3:
                last = jnp.where(lane < 64, a[:, 256:], b[:, 256:])
                qkv_ref[rows, 640 * x:640 * (x + 1)] = jnp.concatenate([a[:, :256], b[:, :256], last], axis=1)
            else:
                out_ref[rows, :] = jnp.concatenate([a, b[:, 128:]], axis=1)
            if x == 0:
                vec_ref[rows, :] = pltpu.roll(a[:, 256:], 64, 1) + b[:, 256:]


def final_heads(core, mine, theirs):
    return call(
        final_heads_kernel, (shape(160, 1920, dtype=f32), shape(160, 640, dtype=f32), shape(160, 128, dtype=f32)), "final_heads", 10**6, 16,
        **scalar_first((1,), [full(16, 40, 384)] * 2, [full(160, 1920), full(160, 640), full(160, 128)]))(core, mine, theirs)


def shifted(array, axis, by):
    devices = lax.axis_size(axis)
    return lax.ppermute(array, axis, [(i, (i + by) % devices) for i in range(devices)])


def passed_along(array, by):
    devices = lax.axis_size(("z", "x"))
    return lax.ppermute(array, ("z", "x"), [(i, i + by) for i in range(devices) if 0 <= i + by < devices])


def swapped(array):
    return lax.ppermute(array, "core", [(0, 1), (1, 0)])


def pick(array, index):
    return lax.dynamic_index_in_dim(array, index, 0, keepdims=False)


def summed_share(array, axis):
    me, devices = lax.axis_index(axis), lax.axis_size(axis)
    total = pick(array, me).astype(f32)
    for by in (1, devices - 1, 2):
        total = total + shifted(pick(array, (me + by) % devices), axis, by).astype(f32)
    return total.astype(bf16)


def gathered(array, axis):
    me, devices = lax.axis_index(axis), lax.axis_size(axis)
    out = jnp.zeros((devices,) + array.shape, array.dtype)
    out = lax.dynamic_update_index_in_dim(out, array, me, 0)
    for by in (1, devices - 1, 2):
        out = lax.dynamic_update_index_in_dim(out, shifted(array, axis, by), (me + devices - by) % devices, 0)
    return out


def gathered_ring(array, axis):
    me, half = lax.axis_index(axis), array.shape[0] // 2
    before, after = shifted(array, axis, 1), shifted(array, axis, -1)
    far = jnp.concatenate([shifted(before[:half], axis, 1), shifted(after[half:], axis, -1)])
    out = jnp.zeros((4,) + array.shape, array.dtype)
    for by, part in ((0, array), (3, before), (1, after), (2, far)):
        out = lax.dynamic_update_index_in_dim(out, part, (me + by) % 4, 0)
    return out


def window_info(length_row, chip, core, win):
    ends = jnp.cumsum(length_row)
    starts = ends - length_row
    base = chip * 512 - 1024
    places = base + jnp.arange(win, dtype=jnp.int32)
    inside = (places[:, None] >= starts[None, :]) & (places[:, None] < ends[None, :])
    ones = jnp.broadcast_to(jnp.arange(64) < 3, (win, 64)).astype(bf16)
    key_rows = jnp.concatenate([jnp.where(inside, 0.0, -BIG).astype(bf16), ones], axis=1)
    own = chip * 512 + jnp.arange(512, dtype=jnp.int32)
    inside_q = (own[None, :] >= starts[:, None]) & (own[None, :] < ends[:, None])
    query_rows = jnp.concatenate([inside_q.astype(bf16), jnp.zeros((64, 512), bf16)], axis=0)
    info = [core]
    sizes = []
    for t in range(2):
        first = chip * 512 + t * TILE
        low = jnp.max(jnp.where(starts <= first, starts, 0)) - base
        high = jnp.min(jnp.where(ends > first + TILE - 1, ends, 1 << 30)) - base
        start = low // 128 * 128
        need = high - start
        size = (need + SHORT - 1) // SHORT * SHORT
        info.append(jnp.minimum(start, win - size))
        sizes.append(size)
    low = jnp.minimum(info[1], info[2]) // 512
    high = (jnp.maximum(info[1] + sizes[0], info[2] + sizes[1]) + 511) // 512
    return jnp.stack(info + sizes).astype(jnp.int32), key_rows, query_rows, [low, high]


def body(tokens, lengths, gain_one, bias_one, w_qkv, w_out, gain_two, bias_two, w_up, w_down, cotangent):
    core, chip = lax.axis_index("core"), lax.axis_index(("z", "x"))
    core_arg, y_arg = core[None].astype(jnp.int32), lax.axis_index("batch")[None].astype(jnp.int32)
    tok, cot = tokens[:, 0], cotangent[:, 0].reshape(512, 640)

    together = lambda *arrays: lax.optimization_barrier(arrays)
    before, after, tok_other = passed_along(tok, 1), passed_along(tok, -1), swapped(tok)
    vectors = jnp.pad(jnp.stack([gain_one, bias_one, gain_two, bias_two]), ((0, 12), (0, 0)))
    heads = pack_heads(core_arg, w_qkv, vectors)
    heads_before, heads_after = shifted(heads, "batch", 1), shifted(heads, "batch", -1)
    heads, tok_other, w_out, w_up, w_down = together(heads, tok_other, w_out, w_up, w_down)
    feed_weights = lax.all_gather(pack_feed(core_arg, w_out, w_up, w_down), "batch", axis=0, tiled=True)
    w_out_all = feed_weights[:, 5120:]
    before, after, heads_before, heads_after = together(before, after, heads_before, heads_after)
    own = (passed_along(before, 1), before, tok, after, passed_along(after, -1))
    near, far = shifted(heads_before[:96], "batch", 1), shifted(heads_after[96:], "batch", -1)
    other = (swapped(own[0]), swapped(before), tok_other, swapped(after), swapped(own[4]))
    w_heads, vec = assemble(y_arg, heads, heads_before, heads_after, near, far)

    windows = [window_info(lengths[m, 0], chip, core, 2560) for m in range(2)]
    place = jnp.stack([core] + windows[0][3] + windows[1][3]).astype(jnp.int32)
    *near_parts, q, qT = project((1, 2, 3), place, own, other, vec, w_heads)
    k, v, kT, vT = project((0, 4), place, own, other, vec, w_heads, near_parts)
    (oT0, low0, lse0), (oT1, low1, lse1) = (
        attend(m, info, qT, k, vT, key_rows, query_rows) for m, (info, key_rows, query_rows, _) in enumerate(windows))

    theirs = swapped(jnp.stack([low0, low1]))
    middle, hidden_two, hidden_other = middle_step(core_arg, low0, low1, theirs, tok, tok_other, w_out_all, vec)
    mine, partial, feed_grads = feed_forward(hidden_two, hidden_other, cot, swapped(cot), feed_weights)
    feed_grads = lax.psum_scatter(feed_grads.reshape(5120, 640), ("z", "x"), scatter_dimension=0, tiled=True).reshape(4, 80, 640)
    block_out, grad_middle, branch, g_two = after_feed(middle, mine, swapped(partial), cot, vec)

    do, doT, g_out = branch_step(core_arg, branch, swapped(branch), w_out_all, low0, low1, theirs)
    back = [
        lambda m=m, info=info, rows=(key_rows, query_rows), oT=oT, lse=lse: attend_back(m, info, qT, q, k, kT, v, doT, do, oT, lse, *rows)
        for m, ((info, key_rows, query_rows, _), oT, lse) in enumerate(zip(windows, (oT0, oT1), (lse0, lse1)))]
    mine0, theirs0, g_sum, g_vec = project_back(0, place, own, other, vec, w_heads, *back[0]())
    feed = summed_share(feed_grads, "batch")
    dq, dk, dv, feed = together(*back[1](), feed)
    mine1, theirs1, tail = project_back(1, place, own, other, vec, w_heads, dq, dk, dv, g_sum, g_vec, g_out, g_two)

    tail = lax.all_to_all(tail, ("batch", "z", "x"), 0, 0, tiled=True)
    feed = lax.all_gather(feed, ("z", "x"), axis=0, tiled=True).reshape(16, 80, 640)
    sums = []
    for mine, theirs in ((mine0, theirs0), (mine1, theirs1)):
        theirs = swapped(theirs)
        sums.append([mine[j].astype(f32) + theirs[j].astype(f32) for j in range(5)])
    handed = []
    for m in range(2):
        right, left = sums[m][4].astype(bf16), sums[m][0].astype(bf16)
        if m == 1:
            tail, right, left = together(tail, right, left)
            tail = gathered(jnp.sum(tail.astype(f32), axis=0).astype(bf16), "x").reshape(160, 384)
        right = (passed_along(right, 1).astype(f32) + sums[m][3]).astype(bf16)
        left = (passed_along(left, -1).astype(f32) + sums[m][1]).astype(bf16)
        if m == 1:
            tail, right, left = together(tail, right, left)
        handed.append(sums[m][2] + passed_along(right, 1).astype(f32) + passed_along(left, -1).astype(f32))
    n_one, r_one = moments(tok.reshape(512, 640).astype(f32))
    grad_tokens = (grad_middle + norm_back(jnp.concatenate(handed), n_one, r_one, vec[0:1])).astype(bf16)
    tail = gathered(tail, "z").reshape(16, 40, 384)
    grad_qkv, grad_out, spare = final_heads(core_arg, tail, swapped(tail))
    grad_up, grad_down = final_feed(core_arg, feed, swapped(feed))
    return (
        block_out.reshape(2, 1, 256, 640), grad_tokens.reshape(2, 1, 256, 640), spare[:, 0], spare[:, 1], grad_qkv, grad_out,
        spare[:, 2], spare[:, 3], grad_up, grad_down)


def solution(mesh):
    fine = Mesh(mesh.devices.reshape(4, 4, 4, 2), ("batch", "z", "x", "core"))
    rows = P(None, "batch", ("z", "x", "core"), None)
    one, two = P("batch"), P("batch", None)
    return jax.shard_map(
        body,
        mesh=fine,
        in_specs=(rows, P(None, "batch", None), one, one, two, two, one, one, two, two, rows),
        out_specs=(rows, rows, one, one, two, two, one, one, two, two),
        check_vma=False,
    )
```

```python
import math

import jax
import jax.numpy as jnp
from jax import lax
from jax.experimental import pallas as pl
from jax.experimental.pallas import tpu as pltpu
from jax.sharding import Mesh
from jax.sharding import PartitionSpec as P

HEAD_DIM = 32
SCALE = HEAD_DIM ** -0.5
LOG2E = math.log2(math.e)
C2 = SCALE * LOG2E
BIG = 1e30
TILE = 256
EPSILON = 1e-05
PAIRS = 5
SHORT, LONG = 384, 1152
f32, bf16 = jnp.float32, jnp.bfloat16
NT = (((1,), (1,)), ((), ()))


def pair_offset(info_ref):
    p = pl.program_id(0)
    sub = jnp.where(p == PAIRS - 1, info_ref[0], lax.rem(p, 2))
    return sub * (2 * HEAD_DIM)


def split3(v):
    a = v.astype(bf16)
    r = v - a.astype(f32)
    b = r.astype(bf16)
    d = (r - b.astype(f32)).astype(bf16)
    return a, b, d


def rows_masked(xT, off):
    row = lax.broadcasted_iota(jnp.int32, xT.shape, 0) - off
    xf = xT.astype(f32)
    return [jnp.where((row >= HEAD_DIM * j) & (row < HEAD_DIM * (j + 1)), xf, 0.0).astype(bf16) for j in range(2)]


def lanes_masked(x, off):
    lane = lax.broadcasted_iota(jnp.int32, x.shape, 1) - off
    xf = x.astype(f32)
    return [jnp.where((lane >= HEAD_DIM * j) & (lane < HEAD_DIM * (j + 1)), xf, 0.0).astype(bf16) for j in range(2)]


def attend_kernel(info_ref, qT_ref, k_ref, vT_ref, kaug_ref, qaugT_ref, oT_ref, o_ref, l_ref, rhs):
    off = pair_offset(info_ref)
    oT_ref[...] = jnp.where(lax.rem(pl.program_id(0), 2) == 0, 0.0, oT_ref[...])
    for t in range(2):
        cols = slice(t * TILE, (t + 1) * TILE)
        masked = rows_masked(qT_ref[:, cols], off)
        for j in range(2):
            rhs[0:128, j * TILE:(j + 1) * TILE] = masked[j]
            rhs[128:256, j * TILE:(j + 1) * TILE] = qaugT_ref[:, cols]
        start = info_ref[1 + t]
        need = info_ref[3 + t]

        def block(first, size):
            def step(i, carry):
                row = pl.multiple_of(first + i * size, 128)
                lhs = jnp.concatenate([k_ref[pl.ds(row, size), :], kaug_ref[pl.ds(row, size), :]], axis=1)
                raw = [jnp.dot(lhs, rhs[:, j * TILE:(j + 1) * TILE], preferred_element_type=f32) for j in range(2)]
                out = []
                for j in range(2):
                    m, l, o = carry[j]
                    s = raw[j] * C2
                    m_new = jnp.maximum(m, jnp.max(s, axis=0, keepdims=True))
                    alpha = jnp.exp2(m - m_new)
                    p = jnp.exp2(s - m_new)
                    vT = vT_ref[pl.ds(pl.multiple_of(off + j * HEAD_DIM, HEAD_DIM), HEAD_DIM), pl.ds(row, size)]
                    out.append((m_new, l * alpha + jnp.sum(p, axis=0, keepdims=True),
                                o * alpha + jnp.dot(vT, p.astype(bf16), preferred_element_type=f32)))
                return tuple(out)
            return step

        def finish(state):
            for j in range(2):
                m, l, o = state[j]
                oT_ref[pl.ds(pl.multiple_of(off + j * HEAD_DIM, HEAD_DIM), HEAD_DIM), cols] = o * (1.0 / l)
                l_ref[0, j:j + 1, cols] = m + jnp.log2(l)

        init = tuple((jnp.full((1, TILE), -1e38, f32), jnp.zeros((1, TILE), f32), jnp.zeros((HEAD_DIM, TILE), f32)) for _ in range(2))

        longs = lax.div(need, LONG)
        state = lax.fori_loop(0, longs, block(start, LONG), init)
        finish(lax.fori_loop(0, lax.div(need - longs * LONG, SHORT), block(start + longs * LONG, SHORT), state))

    o_ref[...] = oT_ref[...].T.astype(bf16)


def attend(m, info, qT, k, vT, kaug, qaugT):
    win, nq = k.shape[1], qT.shape[2]
    qT, k, vT = stay(qT, k, vT)
    return pl.pallas_call(
        attend_kernel,
        out_shape=(jax.ShapeDtypeStruct((384, nq), f32), jax.ShapeDtypeStruct((nq, 384), bf16), jax.ShapeDtypeStruct((PAIRS, 8, nq), f32)),
        grid_spec=pltpu.PrefetchScalarGridSpec(
            num_scalar_prefetch=1, grid=(PAIRS,),
            in_specs=[
                pl.BlockSpec((None, 128, nq), lambda p, *_: (m, p // 2, 0)),
                pl.BlockSpec((None, win, 128), lambda p, *_: (m, 0, p // 2)),
                pl.BlockSpec((None, 128, win), lambda p, *_: (m, p // 2, 0)),
                pl.BlockSpec((win, 128), lambda p, *_: (0, 0)),
                pl.BlockSpec((128, nq), lambda p, *_: (0, 0)),
            ],
            out_specs=[
                pl.BlockSpec((128, nq), lambda p, *_: (p // 2, 0)),
                pl.BlockSpec((nq, 128), lambda p, *_: (0, p // 2)),
                pl.BlockSpec((1, 8, nq), lambda p, *_: (p, 0, 0)),
            ],
            scratch_shapes=[pltpu.VMEM((256, 2 * TILE), bf16)],
        ),
        compiler_params=pltpu.CompilerParams(vmem_limit_bytes=28 << 20),
        cost_estimate=pl.CostEstimate(flops=20 * 10**9, bytes_accessed=6 << 20, transcendentals=5 * 10**6),
        name="attend",
    )(info, qT, k, vT, kaug, qaugT)


def attend_back_kernel(info_ref, qT_ref, q_ref, k_ref, kT_ref, v_ref, doT_ref, do_ref, oT_ref, l_ref, kaug_ref, qaugT_ref,
                       dq_ref, dk_ref, dv_ref, dqT_ref, rhs_s, rhs_d, q_stk, do_stk, dk_acc, dv_acc):
    p_id = pl.program_id(0)
    off = pair_offset(info_ref)

    @pl.when(lax.rem(p_id, 2) == 0)
    def _():
        dqT_ref[...] = jnp.zeros_like(dqT_ref)
        dk_acc[...] = jnp.zeros_like(dk_acc)
        dv_acc[...] = jnp.zeros_like(dv_acc)

    for t in range(2):
        cols = slice(t * TILE, (t + 1) * TILE)
        masked_q = rows_masked(qT_ref[:, cols], off)
        masked_do = rows_masked(doT_ref[:, cols], off)
        lane_q = lanes_masked(q_ref[cols, :], off)
        lane_do = lanes_masked(do_ref[cols, :], off)
        for j in range(2):
            part = slice(j * TILE, (j + 1) * TILE)
            head = pl.ds(pl.multiple_of(off + j * HEAD_DIM, HEAD_DIM), HEAD_DIM)
            delta = jnp.sum(doT_ref[head, cols].astype(f32) * oT_ref[head, cols], axis=0, keepdims=True)
            total = l_ref[0, j:j + 1, cols] * (1.0 / C2)
            rowid = lax.broadcasted_iota(jnp.int32, (64, TILE), 0)
            lp, dp = split3(-total), split3(-delta)
            def pieces(parts):
                x = jnp.zeros((64, TILE), f32)
                for n in range(3):
                    x = jnp.where(rowid == n, parts[n].astype(f32), x)
                return x.astype(bf16)
            rhs_s[0:128, part] = masked_q[j]
            rhs_s[128:192, part] = qaugT_ref[0:64, cols]
            rhs_s[192:256, part] = pieces(lp)
            rhs_d[0:128, part] = masked_do[j]
            rhs_d[128:192, part] = jnp.zeros((64, TILE), bf16)
            rhs_d[192:256, part] = pieces(dp)
            q_stk[part, :] = lane_q[j]
            do_stk[part, :] = lane_do[j]
        start = info_ref[1 + t]
        need = info_ref[3 + t]

        def block(first, size):
            def step(i, carry):
                row = pl.multiple_of(first + i * size, 128)
                rows = pl.ds(row, size)
                aug = kaug_ref[rows, :]
                lhs_k = jnp.concatenate([k_ref[rows, :], aug], axis=1)
                lhs_v = jnp.concatenate([v_ref[rows, :], aug], axis=1)
                out, dv, dk = [], dv_acc[rows, :], dk_acc[rows, :]
                for j in range(2):
                    part = slice(j * TILE, (j + 1) * TILE)
                    s = jnp.dot(lhs_k, rhs_s[:, part], preferred_element_type=f32)
                    dp = jnp.dot(lhs_v, rhs_d[:, part], preferred_element_type=f32)
                    p = jnp.exp2(s * C2)
                    ds = (p * dp).astype(bf16)
                    dv = dv + jnp.dot(p.astype(bf16), do_stk[part, :], preferred_element_type=f32)
                    dk = dk + jnp.dot(ds, q_stk[part, :], preferred_element_type=f32)
                    kT = kT_ref[pl.ds(pl.multiple_of(off + j * HEAD_DIM, HEAD_DIM), HEAD_DIM), rows]
                    out.append(carry[j] + jnp.dot(kT, ds, preferred_element_type=f32))
                dv_acc[rows, :] = dv
                dk_acc[rows, :] = dk
                return tuple(out)
            return step

        def finish(dqs):
            for j in range(2):
                dqT_ref[pl.ds(pl.multiple_of(off + j * HEAD_DIM, HEAD_DIM), HEAD_DIM), cols] = dqs[j] * SCALE

        init = tuple(jnp.zeros((HEAD_DIM, TILE), f32) for _ in range(2))

        longs = lax.div(need, LONG)
        state = lax.fori_loop(0, longs, block(start, LONG), init)
        finish(lax.fori_loop(0, lax.div(need - longs * LONG, SHORT), block(start + longs * LONG, SHORT), state))
    @pl.when((lax.rem(p_id, 2) == 1) | (p_id == PAIRS - 1))
    def _():
        dq_ref[...] = dqT_ref[...].T.astype(bf16)
        dk_ref[...] = (dk_acc[...] * SCALE).astype(bf16)
        dv_ref[...] = dv_acc[...].astype(bf16)


def attend_back(m, info, qT, q, k, kT, v, doT, do, oT, lse, kaug, qaugT):
    win, nq = k.shape[1], qT.shape[2]
    qT, q, k, kT, v = stay(qT, q, k, kT, v)
    wide = pl.BlockSpec((128, nq), lambda p, *_: (p // 2, 0))
    tall = pl.BlockSpec((nq, 128), lambda p, *_: (0, p // 2))
    keys = pl.BlockSpec((win, 128), lambda p, *_: (0, p // 2))
    wide_m = pl.BlockSpec((None, 128, nq), lambda p, *_: (m, p // 2, 0))
    tall_m = pl.BlockSpec((None, nq, 128), lambda p, *_: (m, 0, p // 2))
    keys_m = pl.BlockSpec((None, win, 128), lambda p, *_: (m, 0, p // 2))
    return pl.pallas_call(
        attend_back_kernel,
        out_shape=(far(nq, 384), far(win, 384), far(win, 384)),
        grid_spec=pltpu.PrefetchScalarGridSpec(
            num_scalar_prefetch=1, grid=(PAIRS,),
            in_specs=[wide_m, tall_m, keys_m, pl.BlockSpec((None, 128, win), lambda p, *_: (m, p // 2, 0)), keys_m,
                      pl.BlockSpec((128, nq), lambda p, *_: (p // 2, m)), pl.BlockSpec((nq, 128), lambda p, *_: (m, p // 2)), wide,
                      pl.BlockSpec((1, 8, nq), lambda p, *_: (p, 0, 0)),
                      pl.BlockSpec((win, 128), lambda p, *_: (0, 0)), pl.BlockSpec((128, nq), lambda p, *_: (0, 0))],
            out_specs=[tall, keys, keys],
            scratch_shapes=[pltpu.VMEM((128, nq), f32), pltpu.VMEM((256, 2 * TILE), bf16), pltpu.VMEM((256, 2 * TILE), bf16),
                            pltpu.VMEM((2 * TILE, 128), bf16), pltpu.VMEM((2 * TILE, 128), bf16),
                            pltpu.VMEM((win, 128), f32), pltpu.VMEM((win, 128), f32)],
        ),
        compiler_params=pltpu.CompilerParams(vmem_limit_bytes=32 << 20),
        cost_estimate=pl.CostEstimate(flops=40 * 10**9, bytes_accessed=12 << 20, transcendentals=5 * 10**6),
        name="attend_back",
    )(info, qT, q, k, kT, v, doT, do, oT, lse, kaug, qaugT)


def moments(x):
    centred = x - jnp.mean(x, axis=-1, keepdims=True)
    r = lax.rsqrt(jnp.mean(centred * centred, axis=-1, keepdims=True) + EPSILON)
    return centred * r, r


def norm_back(grad, n, r, gain):
    e = grad * gain
    return r * (e - jnp.mean(e, axis=-1, keepdims=True) - n * jnp.mean(e * n, axis=-1, keepdims=True))


def call(kernel, out_shape, name, flops=10**9, limit=48, **spec):
    return pl.pallas_call(
        kernel, out_shape=out_shape, name=name,
        compiler_params=pltpu.CompilerParams(vmem_limit_bytes=limit << 20),
        cost_estimate=pl.CostEstimate(flops=flops, bytes_accessed=8 << 20, transcendentals=0), **spec)


def shape(*dims, dtype=bf16):
    return jax.ShapeDtypeStruct(dims, dtype)


def far(*dims):
    return pltpu.MemorySpace.HBM(dims, bf16)


def stay(*arrays):
    return [pltpu.with_memory_space_constraint(a, pltpu.MemorySpace.HBM) for a in arrays]


def scalar_first(grid, in_specs, out_specs, scratch=()):
    return dict(grid_spec=pltpu.PrefetchScalarGridSpec(
        num_scalar_prefetch=1, grid=grid, in_specs=in_specs, out_specs=out_specs, scratch_shapes=list(scratch)))


def full(*dims):
    return pl.BlockSpec(dims, lambda *_: (0,) * len(dims))


def pack_heads_kernel(core_ref, qkv_ref, vec_ref, heads_ref):
    for part in range(3):
        near = pl.ds(pl.multiple_of(640 * part + 256 * core_ref[0], 128), 256)
        heads_ref[:, 384 * part:384 * part + 256] = qkv_ref[:, near]
        heads_ref[:, 384 * part + 256:384 * (part + 1)] = qkv_ref[:, 640 * part + 512:640 * (part + 1)]
    heads_ref[:, 1152:1280] = vec_ref[...]


def pack_heads(core, w_qkv, vectors):
    return call(pack_heads_kernel, shape(160, 1280), "pack_heads", 10**6, 8, **scalar_first(
        (1,), [full(160, 1920), full(160, 128)], full(160, 1280)))(core, w_qkv, vectors)


def turn_kernel(vec_ref, rows_ref):
    rows_ref[...] = vec_ref[...].astype(f32).T[:16]


def vector_rows(heads):
    return call(turn_kernel, shape(16, 640, dtype=f32), "vector_rows", 10**6, 8, grid=(1,),
                in_specs=[pl.BlockSpec((640, 128), lambda i: (0, 9))], out_specs=full(16, 640))(heads)


def pack_feed_kernel(core_ref, up_ref, down_ref, feed_ref):
    core = core_ref[0]
    for f in range(4):
        feed_ref[:, 640 * f:640 * (f + 1)] = up_ref[:, pl.ds(pl.multiple_of(1280 * f + 640 * core, 128), 640)]
        feed_ref[:, 2560 + 640 * f:2560 + 640 * (f + 1)] = down_ref[pl.ds(pl.multiple_of(640 * core + 160 * f, 32), 160), :]


def pack_feed(core, w_up, w_down):
    return call(pack_feed_kernel, shape(160, 5120), "pack_feed", 10**6, 16, **scalar_first(
        (1,), [full(160, 5120), full(1280, 640)], full(160, 5120)))(core, w_up, w_down)


def rows_in_order(core, mine, theirs, x_ref):
    mine, theirs = mine.astype(f32), theirs.astype(f32)
    x_ref[0:256, :] = jnp.where(core == 0, mine, theirs)
    x_ref[256:512, :] = jnp.where(core == 0, theirs, mine)


def window_rows(core, own_refs, other_refs, m, block, x_ref):
    for j in range(len(own_refs)):
        @pl.when(block == j)
        def _():
            rows_in_order(core, own_refs[j][m], other_refs[j][m], x_ref)


def project_kernel(chips, place_ref, *refs):
    n = len(chips)
    own_refs, other_refs = refs[:n], refs[n:2 * n]
    vec_ref, w_ref = refs[2 * n:2 * n + 2]
    k_ref, v_ref, kT_ref, vT_ref = refs[-6 - 2 * (n == 3):][:4]
    x_ref, hid_ref = refs[-2:]
    m, step = pl.program_id(0), pl.program_id(1)
    block = sum(jnp.where(step == i, chip, 0) for i, chip in enumerate(chips))
    needed = (block >= place_ref[1 + 2 * m]) & (block < place_ref[2 + 2 * m])

    @pl.when(jnp.logical_not(needed))
    def _():
        for ref in (k_ref, v_ref, kT_ref, vT_ref):
            ref[...] = jnp.zeros_like(ref)

    @pl.when(needed)
    def _():
        window_rows(place_ref[0], own_refs, other_refs, m, step, x_ref)
        hidden = (moments(x_ref[...])[0] * vec_ref[0:1, :] + vec_ref[1:2, :]).astype(bf16)
        hid_ref[...] = hidden
        kv = jnp.dot(hidden, w_ref[:, 384:], preferred_element_type=f32)
        low = kv.astype(bf16)
        k_ref[0] = low[:, :384]
        v_ref[0] = low[:, 384:]
        turned = kv.T.astype(bf16)
        kT_ref[0] = turned[:384]
        vT_ref[0] = turned[384:]

    if n == 3:
        q_ref, qT_ref = refs[-4:-2]

        @pl.when(step == 1)
        def _():
            q = jnp.dot(hid_ref[...], w_ref[:, :384], preferred_element_type=f32)
            q_ref[0] = q.astype(bf16)
            qT_ref[0] = q.T.astype(bf16)


def project(chips, place, own, other, vec, w, earlier=()):
    n = len(chips)
    chip = (lambda b: b + 1) if n == 3 else (lambda b: 4 * b)
    tall = pl.BlockSpec((1, 512, 384), lambda m, b, *_: (m, chip(b), 0))
    wide = pl.BlockSpec((1, 384, 512), lambda m, b, *_: (m, 0, chip(b)))
    shapes = [far(2, 2560, 384), far(2, 2560, 384), far(2, 384, 2560), far(2, 384, 2560)]
    specs = [tall, tall, wide, wide]
    if n == 3:
        shapes += [far(2, 512, 384), far(2, 384, 512)]
        specs += [pl.BlockSpec((1, 512, 384), lambda m, *_: (m, 0, 0)), pl.BlockSpec((1, 384, 512), lambda m, *_: (m, 0, 0))]
    own, other = [own[c] for c in chips], [other[c] for c in chips]
    return call(
        lambda *refs: project_kernel(chips, *refs), shapes, "project", 5 * 10**9, 28,
        input_output_aliases={2 * n + 3 + i: i for i in range(len(earlier))}, **scalar_first(
            (2, n), [full(2, 256, 640)] * (2 * n) + [full(16, 640), full(640, 1152)] + [pl.BlockSpec(memory_space=pl.ANY)] * len(earlier),
            specs, [pltpu.VMEM((512, 640), f32), pltpu.VMEM((512, 640), bf16)]))(place, *own, *other, vec, w, *earlier)


def heads_joined(core, mine, theirs):
    first, second = (jnp.where(core == 0, a, b) for a, b in ((mine, theirs), (theirs, mine)))
    return jnp.concatenate([first[:, :256], second[:, :256], first[:, 256:] + second[:, 256:]], axis=1)


def middle_kernel(place_ref, low0_ref, low1_ref, theirs_ref, tok_ref, tok2_ref, vec_ref, w0_ref, w1_ref, w2_ref, w3_ref,
                  mid_ref, hid_ref, hid2_ref, w_ref):
    core = place_ref[0]
    for by, part in enumerate((w0_ref, w1_ref, w2_ref, w3_ref)):
        w_ref[pl.ds(pl.multiple_of(lax.rem(place_ref[5] + 4 - by, 4) * 160, 32), 160), :] = part[...]
    for m, low_ref in enumerate((low0_ref, low1_ref)):
        attended = heads_joined(core, low_ref[...].astype(f32), theirs_ref[m].astype(f32)).astype(bf16)
        branch = jnp.dot(attended, w_ref[...], preferred_element_type=f32)
        mine = jnp.where(core == 0, branch[:256], branch[256:]) + tok_ref[m].astype(f32)
        theirs = jnp.where(core == 0, branch[256:], branch[:256]) + tok2_ref[m].astype(f32)
        part = slice(256 * m, 256 * (m + 1))
        mid_ref[part, :] = mine
        hid_ref[part, :] = (moments(mine)[0] * vec_ref[2:3, :] + vec_ref[3:4, :]).astype(bf16)
        hid2_ref[part, :] = (moments(theirs)[0] * vec_ref[2:3, :] + vec_ref[3:4, :]).astype(bf16)


def middle_step(place, *args):
    return call(middle_kernel, (shape(512, 640, dtype=f32), shape(512, 640), shape(512, 640), shape(640, 640)), "middle", 10**9, 20, **scalar_first(
        (1,), [full(*a.shape) for a in args], [full(512, 640)] * 3 + [full(640, 640)]))(place, *args)


def feed_kernel(h_ref, h2_ref, cot_ref, cot2_ref, up_ref, down_ref, mine_ref, theirs_ref, g_ref, h, cot, hT, cT, out, dh):
    chunk = pl.program_id(0)

    @pl.when(chunk == 0)
    def _():
        h[0:512, :], h[512:1024, :] = h_ref[...], h2_ref[...]
        cot[0:512, :], cot[512:1024, :] = cot_ref[...], cot2_ref[...]
        hT[...] = h[...].astype(f32).T.astype(bf16)
        cT[...] = cot[...].astype(f32).T.astype(bf16)
        out[...] = jnp.zeros_like(out)
        dh[...] = jnp.zeros_like(dh)

    up_w = up_ref[...]
    down_w = jnp.concatenate([down_ref[160 * y:160 * (y + 1), 640 * i:640 * (i + 1)] for y in range(2) for i in range(4)], axis=0)
    acts, d_ups = [], []
    for t in range(4):
        rows = slice(256 * t, 256 * (t + 1))
        u = jnp.dot(h[rows, :], up_w, preferred_element_type=f32)
        d_act = lax.dot_general(cot[rows, :], down_w, NT, preferred_element_type=f32)
        cdf = 0.5 * (1.0 + lax.erf(u * (2.0 ** -0.5)))
        pdf = jnp.exp(u * u * -0.5) * ((2.0 * math.pi) ** -0.5)
        act = (u * cdf).astype(bf16)
        d_up = (d_act * (cdf + u * pdf)).astype(bf16)
        out[rows, :] += jnp.dot(act, down_w, preferred_element_type=f32)
        dh[rows, :] += lax.dot_general(d_up, up_w, NT, preferred_element_type=f32)
        acts.append(act)
        d_ups.append(d_up)
    g_up = jnp.dot(hT[...], jnp.concatenate(d_ups, axis=0), preferred_element_type=f32).astype(bf16)
    g_down = jnp.dot(cT[...], jnp.concatenate(acts, axis=0), preferred_element_type=f32).T.astype(bf16)
    for f in range(2):
        for y in range(4):
            for i in range(2):
                g_ref[4 * chunk + 2 * f + i, y] = g_up[160 * y + 80 * i:160 * y + 80 * (i + 1), 640 * f:640 * (f + 1)]
        for i in range(8):
            g_ref[8 + i, 2 * chunk + f] = g_down[640 * f + 80 * i:640 * f + 80 * (i + 1)]

    @pl.when(chunk == 1)
    def _():
        mine_ref[0], mine_ref[1] = out[0:512, :].astype(bf16), dh[0:512, :].astype(bf16)
        theirs_ref[0], theirs_ref[1] = out[512:1024, :].astype(bf16), dh[512:1024, :].astype(bf16)


def feed_forward(h, h2, cot, cot2, weights):
    return call(
        feed_kernel,
        (shape(2, 512, 640), shape(2, 512, 640), shape(16, 4, 80, 640)),
        "feed_forward", 30 * 10**9, 52, grid=(2,),
        in_specs=[full(512, 640)] * 4 + [pl.BlockSpec((640, 1280), lambda f: (0, f)), pl.BlockSpec((320, 2560), lambda f: (f, 1))],
        out_specs=[full(2, 512, 640), full(2, 512, 640), full(16, 4, 80, 640)],
        scratch_shapes=[pltpu.VMEM((1024, 640), bf16), pltpu.VMEM((1024, 640), bf16), pltpu.VMEM((640, 1024), bf16), pltpu.VMEM((640, 1024), bf16),
                        pltpu.VMEM((1024, 640), f32), pltpu.VMEM((1024, 640), f32)],
    )(h, h2, cot, cot2, weights, weights)


def after_kernel(mid_ref, mine_ref, theirs_ref, cot_ref, vec_ref, block_ref, grad_ref, branch_ref, g_ref):
    middle = mid_ref[...]
    block_ref[...] = (middle + mine_ref[0].astype(f32) + theirs_ref[0].astype(f32)).astype(bf16)
    d_hidden = mine_ref[1].astype(f32) + theirs_ref[1].astype(f32)
    n, r = moments(middle)
    g_ref[...] = jnp.zeros_like(g_ref)
    g_ref[0:1, :] = jnp.sum(d_hidden * n, axis=0, keepdims=True)
    g_ref[1:2, :] = jnp.sum(d_hidden, axis=0, keepdims=True)
    grad = cot_ref[...].astype(f32) + norm_back(d_hidden, n, r, vec_ref[2:3, :])
    grad_ref[...] = grad
    branch_ref[...] = grad.astype(bf16)


def after_feed(*args):
    return call(
        after_kernel, (shape(512, 640), shape(512, 640, dtype=f32), shape(512, 640), shape(8, 640, dtype=f32)), "after_feed", 10**9, 24,
        in_specs=[pl.BlockSpec(memory_space=pltpu.VMEM)] * 5, out_specs=[pl.BlockSpec(memory_space=pltpu.VMEM)] * 4)(*args)


def branch_kernel(core_ref, own_ref, their_ref, w_ref, low0_ref, low1_ref, theirs_ref, do_ref, doT_ref, g_ref):
    core = core_ref[0]
    w = jnp.concatenate([w_ref[pl.ds(pl.multiple_of(256 * core, 256), 256), :], w_ref[512:640, :]], axis=0)
    g = jnp.zeros((640, 384), f32)
    for m in range(2):
        part = slice(256 * m, 256 * (m + 1))
        mine, theirs = own_ref[part, :].astype(f32), their_ref[part, :].astype(f32)
        branch = jnp.concatenate([jnp.where(core == 0, mine, theirs), jnp.where(core == 0, theirs, mine)], axis=0)
        kept = jnp.where(core == 0, branch[:, :384], branch[:, 256:]).astype(bf16)
        branch = branch.astype(bf16)
        rows = slice(512 * m, 512 * (m + 1))
        do = lax.dot_general(branch, w, NT, preferred_element_type=f32)
        do_ref[rows, :] = do.astype(bf16)
        doT_ref[:, rows] = do.T.astype(bf16)
        attended = heads_joined(core, (low0_ref, low1_ref)[m][...].astype(f32), theirs_ref[m].astype(f32))
        g = g + jnp.dot(attended.T.astype(bf16), kept, preferred_element_type=f32)
    g_ref[...] = g


def branch_step(core, *args):
    specs = [full(*a.shape) for a in args]
    return call(
        branch_kernel, (shape(1024, 384), shape(384, 1024), shape(640, 384, dtype=f32)), "branch", 10**9, 24, **scalar_first(
            (1,), specs, [full(1024, 384), full(384, 1024), full(640, 384)]))(core, *args)


def project_back_kernel(core_ref, *refs):
    own_refs, other_refs = refs[:5], refs[5:10]
    (vec_ref, w_ref, dq0_ref, dq1_ref, dk0_ref, dk1_ref, dv0_ref, dv1_ref, g_out_ref, g_two_ref,
     mine_ref, theirs_ref, tail_ref, x_ref, d_kv, d_q, d_hid, g_ref, g_vec) = refs[10:]
    step, core = pl.program_id(0), core_ref[0]
    block = lax.rem(step, 5)

    @pl.when(step == 0)
    def _():
        g_ref[...] = jnp.zeros_like(g_ref)
        g_vec[...] = jnp.zeros_like(g_vec)
        g_vec[2:4, :] = g_two_ref[0:2, :]

    second = lax.div(step, 5)
    needed = (block >= core_ref[1 + 2 * second]) & (block < core_ref[2 + 2 * second])

    @pl.when(jnp.logical_not(needed))
    def _():
        mine_ref[...] = jnp.zeros_like(mine_ref)
        theirs_ref[...] = jnp.zeros_like(theirs_ref)

    for m, (dq, dk, dv) in enumerate(((dq0_ref, dk0_ref, dv0_ref), (dq1_ref, dk1_ref, dv1_ref))):
        @pl.when(needed & (second == m))
        def _():
            window_rows(core, own_refs, other_refs, m, block, x_ref)
            d_kv[:, :384], d_kv[:, 384:] = dk[...], dv[...]
            d_q[...] = dq[...]

    @pl.when(needed)
    def _():
        n = moments(x_ref[...])[0]
        hiddenT = (n * vec_ref[0:1, :] + vec_ref[1:2, :]).T.astype(bf16)
        d_hid[...] = lax.dot_general(d_kv[...], w_ref[:, 384:], NT, preferred_element_type=f32)
        g_ref[:, 384:] += jnp.dot(hiddenT, d_kv[...], preferred_element_type=f32)

        @pl.when(block == 2)
        def _():
            g_ref[:, :384] += jnp.dot(hiddenT, d_q[...], preferred_element_type=f32)
            d_hid[...] += lax.dot_general(d_q[...], w_ref[:, :384], NT, preferred_element_type=f32)

        dh = d_hid[...]
        mine_ref[0, 0] = jnp.where(core == 0, dh[:256], dh[256:]).astype(bf16)
        theirs_ref[0, 0] = jnp.where(core == 0, dh[256:], dh[:256]).astype(bf16)
        g_vec[0:1, :] += jnp.sum(dh * n, axis=0, keepdims=True)
        g_vec[1:2, :] += jnp.sum(dh, axis=0, keepdims=True)

    @pl.when(step == 9)
    def _():
        turned = g_vec[...].T
        lane = lax.broadcasted_iota(jnp.int32, (640, 128), 1) - 64 * (1 - core)
        spare = g_ref[:, 256:384]
        for i in range(4):
            spare = jnp.where(lane == i, turned[:, i:i + 1], spare)
        g_ref[:, 256:384] = spare
        for y in range(4):
            for z in range(4):
                rows = slice(160 * y + 40 * z, 160 * y + 40 * (z + 1))
                for x in range(3):
                    tail_ref[16 * y + 4 * z + x] = g_ref[rows, 384 * x:384 * (x + 1)].astype(bf16)
                tail_ref[16 * y + 4 * z + 3] = g_out_ref[rows, :].astype(bf16)


def project_back(core, own, other, vec, w, dq, dk, dv, g_out, g_two):
    dk, dv = stay(*dk), stay(*dv)
    first = pl.BlockSpec((512, 384), lambda b, *_: (jnp.minimum(b, 4), 0))
    second = pl.BlockSpec((512, 384), lambda b, *_: (jnp.maximum(b - 5, 0), 0))
    return call(
        project_back_kernel, (shape(5, 2, 256, 640), shape(5, 2, 256, 640), shape(64, 40, 384)), "project_back", 10**10, 36, **scalar_first(
            (10,), [full(2, 256, 640)] * 10 + [full(16, 640), full(640, 1152), full(512, 384), full(512, 384), first, second, first, second,
                                               full(640, 384), full(8, 640)],
            [pl.BlockSpec((1, 1, 256, 640), lambda b, *_: (lax.rem(b, 5), b // 5, 0, 0))] * 2 + [full(64, 40, 384)],
            [pltpu.VMEM((512, 640), f32), pltpu.VMEM((512, 768), bf16), pltpu.VMEM((512, 384), bf16),
             pltpu.VMEM((512, 640), f32), pltpu.VMEM((640, 1152), f32), pltpu.VMEM((8, 640), f32)]))(core, *own, *other, vec, w, *dq, *dk, *dv, g_out, g_two)


def in_core_order(core_ref, mine, theirs):
    core, mine, theirs = core_ref[0], mine.astype(f32), theirs.astype(f32)
    return jnp.where(core == 0, mine, theirs), jnp.where(core == 0, theirs, mine)


def final_feed_kernel(core_ref, mine_ref, theirs_ref, up_ref, down_ref):
    for i in range(16):
        for c, piece in enumerate(in_core_order(core_ref, mine_ref[i], theirs_ref[i])):
            if i < 8:
                base = 1280 * (i // 2) + 640 * c
                up_ref[80 * (i % 2):80 * (i % 2 + 1), base:base + 640] = piece
            else:
                base = 640 * c + 80 * (i - 8)
                down_ref[base:base + 80, :] = piece


def final_feed(core, mine, theirs):
    return call(final_feed_kernel, (shape(160, 5120, dtype=f32), shape(1280, 640, dtype=f32)), "final_feed", 10**6, 32, **scalar_first(
        (1,), [full(16, 80, 640)] * 2, [full(160, 5120), full(1280, 640)]))(core, mine, theirs)


def final_heads_kernel(core_ref, mine_ref, theirs_ref, qkv_ref, out_ref, vec_ref):
    lane = lax.broadcasted_iota(jnp.int32, (40, 128), 1)
    for z in range(4):
        rows = slice(40 * z, 40 * (z + 1))
        for x in range(4):
            a, b = in_core_order(core_ref, mine_ref[4 * z + x], theirs_ref[4 * z + x])
            if x < 3:
                last = jnp.where(lane < 64, a[:, 256:], b[:, 256:])
                qkv_ref[rows, 640 * x:640 * (x + 1)] = jnp.concatenate([a[:, :256], b[:, :256], last], axis=1)
            else:
                out_ref[rows, :] = jnp.concatenate([a, b[:, 128:]], axis=1)
            if x == 0:
                vec_ref[rows, :] = pltpu.roll(a[:, 256:], 64, 1) + b[:, 256:]


def final_heads(core, mine, theirs):
    return call(
        final_heads_kernel, (shape(160, 1920, dtype=f32), shape(160, 640, dtype=f32), shape(160, 128, dtype=f32)), "final_heads", 10**6, 16,
        **scalar_first((1,), [full(16, 40, 384)] * 2, [full(160, 1920), full(160, 640), full(160, 128)]))(core, mine, theirs)


def shifted(array, axis, by):
    devices = lax.axis_size(axis)
    return lax.ppermute(array, axis, [(i, (i + by) % devices) for i in range(devices)])


def passed_along(array, by):
    devices = lax.axis_size(("z", "x"))
    return lax.ppermute(array, ("z", "x"), [(i, i + by) for i in range(devices) if 0 <= i + by < devices])


def swapped(array):
    return lax.ppermute(array, "core", [(0, 1), (1, 0)])


def pick(array, index):
    return lax.dynamic_index_in_dim(array, index, 0, keepdims=False)


def summed_share(array, axis):
    me, devices = lax.axis_index(axis), lax.axis_size(axis)
    total = pick(array, me).astype(f32)
    for by in (1, devices - 1, 2):
        total = total + shifted(pick(array, (me + by) % devices), axis, by).astype(f32)
    return total.astype(bf16)


def gathered(array, axis):
    me, devices = lax.axis_index(axis), lax.axis_size(axis)
    out = jnp.zeros((devices,) + array.shape, array.dtype)
    out = lax.dynamic_update_index_in_dim(out, array, me, 0)
    for by in (1, devices - 1, 2):
        out = lax.dynamic_update_index_in_dim(out, shifted(array, axis, by), (me + devices - by) % devices, 0)
    return out


def window_info(length_row, chip, core, win):
    ends = jnp.cumsum(length_row)
    starts = ends - length_row
    base = chip * 512 - 1024
    places = base + jnp.arange(win, dtype=jnp.int32)
    inside = (places[:, None] >= starts[None, :]) & (places[:, None] < ends[None, :])
    ones = jnp.broadcast_to(jnp.arange(64) < 3, (win, 64)).astype(bf16)
    key_rows = jnp.concatenate([jnp.where(inside, 0.0, -BIG).astype(bf16), ones], axis=1)
    own = chip * 512 + jnp.arange(512, dtype=jnp.int32)
    inside_q = (own[None, :] >= starts[:, None]) & (own[None, :] < ends[:, None])
    query_rows = jnp.concatenate([inside_q.astype(bf16), jnp.zeros((64, 512), bf16)], axis=0)
    info = [core]
    sizes = []
    for t in range(2):
        first = chip * 512 + t * TILE
        low = jnp.max(jnp.where(starts <= first, starts, 0)) - base
        high = jnp.min(jnp.where(ends > first + TILE - 1, ends, 1 << 30)) - base
        start = low // 128 * 128
        need = high - start
        size = (need + SHORT - 1) // SHORT * SHORT
        info.append(jnp.minimum(start, win - size))
        sizes.append(size)
    low = jnp.minimum(info[1], info[2]) // 512
    high = (jnp.maximum(info[1] + sizes[0], info[2] + sizes[1]) + 511) // 512
    return jnp.stack(info + sizes).astype(jnp.int32), key_rows, query_rows, [low, high]


def body(tokens, lengths, gain_one, bias_one, w_qkv, w_out, gain_two, bias_two, w_up, w_down, cotangent):
    core, chip = lax.axis_index("core"), lax.axis_index(("z", "x"))
    core_arg = core[None].astype(jnp.int32)
    tok, cot = tokens[:, 0], cotangent[:, 0].reshape(512, 640)
    together = lambda *arrays: lax.optimization_barrier(arrays)

    vectors = jnp.pad(jnp.stack([gain_one, bias_one, gain_two, bias_two], axis=1), ((0, 0), (0, 124)))
    heads = lax.all_gather(pack_heads(core_arg, w_qkv, vectors), "batch", axis=0, tiled=True)
    before, after, tok_other = passed_along(tok, 1), passed_along(tok, -1), swapped(tok)
    own = (passed_along(before, 1), before, tok, after, passed_along(after, -1))
    other = (swapped(own[0]), swapped(before), tok_other, swapped(after), swapped(own[4]))
    heads, w_up, w_down = together(heads, w_up, w_down)
    feed_weights = lax.all_gather(pack_feed(core_arg, w_up, w_down), "batch", axis=0, tiled=True)
    vec = vector_rows(heads)

    windows = [window_info(lengths[m, 0], chip, core, 2560) for m in range(2)]
    place = jnp.stack([core] + windows[0][3] + windows[1][3] + [lax.axis_index("batch")]).astype(jnp.int32)
    *near_parts, q, qT = project((1, 2, 3), place, own, other, vec, heads)
    k, v, kT, vT = project((0, 4), place, own, other, vec, heads, near_parts)
    (oT0, low0, lse0), (oT1, low1, lse1) = (
        attend(m, info, qT, k, vT, key_rows, query_rows) for m, (info, key_rows, query_rows, _) in enumerate(windows))

    theirs = swapped(jnp.stack([low0, low1]))
    w_out_parts = [w_out] + [shifted(w_out, "batch", by) for by in (1, 2, 3)]
    middle, hidden_two, hidden_other, w_out_all = middle_step(place, low0, low1, theirs, tok, tok_other, vec, *w_out_parts)
    mine, partial, feed_grads = feed_forward(hidden_two, hidden_other, cot, swapped(cot), feed_weights)
    feed_grads = lax.psum_scatter(feed_grads.reshape(5120, 640), ("z", "x"), scatter_dimension=0, tiled=True).reshape(4, 80, 640)
    block_out, grad_middle, branch, g_two = after_feed(middle, mine, swapped(partial), cot, vec)

    do, doT, g_out = branch_step(core_arg, branch, swapped(branch), w_out_all, low0, low1, theirs)
    dq, dk, dv = zip(*(
        attend_back(m, info, qT, q, k, kT, v, doT, do, oT, lse, key_rows, query_rows)
        for m, ((info, key_rows, query_rows, _), oT, lse) in enumerate(zip(windows, (oT0, oT1), (lse0, lse1)))))
    mine, theirs, tail = project_back(place, own, other, vec, heads, dq, dk, dv, g_out, g_two)

    feed = summed_share(feed_grads, "batch")
    tail, feed = together(tail, feed)
    tail = lax.all_to_all(tail, ("batch", "z", "x"), 0, 0, tiled=True)
    feed = lax.all_gather(feed, ("z", "x"), axis=0, tiled=True).reshape(16, 80, 640)
    theirs = swapped(theirs)
    sums = [mine[j].astype(f32) + theirs[j].astype(f32) for j in range(5)]
    tail, right, left = together(tail, sums[4].astype(bf16), sums[0].astype(bf16))
    tail = gathered(jnp.sum(tail.astype(f32), axis=0).astype(bf16), "x").reshape(160, 384)
    right = (passed_along(right, 1).astype(f32) + sums[3]).astype(bf16)
    left = (passed_along(left, -1).astype(f32) + sums[1]).astype(bf16)
    tail, right, left = together(tail, right, left)
    tail = gathered(tail, "z").reshape(16, 40, 384)
    right, left = passed_along(right, 1), passed_along(left, -1)
    tail, right, left = together(tail, right, left)
    d_one = (sums[2] + right.astype(f32) + left.astype(f32)).reshape(512, 640)
    n_one, r_one = moments(tok.reshape(512, 640).astype(f32))
    grad_tokens = (grad_middle + norm_back(d_one, n_one, r_one, vec[0:1])).astype(bf16)
    grad_qkv, grad_out, spare = final_heads(core_arg, tail, swapped(tail))
    grad_up, grad_down = final_feed(core_arg, feed, swapped(feed))
    return (
        block_out.reshape(2, 1, 256, 640), grad_tokens.reshape(2, 1, 256, 640), spare[:, 0], spare[:, 1], grad_qkv, grad_out,
        spare[:, 2], spare[:, 3], grad_up, grad_down)


def solution(mesh):
    fine = Mesh(mesh.devices.reshape(4, 4, 4, 2), ("batch", "z", "x", "core"))
    rows = P(None, "batch", ("z", "x", "core"), None)
    one, two = P("batch"), P("batch", None)
    return jax.shard_map(
        body,
        mesh=fine,
        in_specs=(rows, P(None, "batch", None), one, one, two, two, one, one, two, two, rows),
        out_specs=(rows, rows, one, one, two, two, one, one, two, two),
        check_vma=False,
    )
```

```python
import math

import jax
import jax.numpy as jnp
from jax import lax
from jax.experimental import pallas as pl
from jax.experimental.pallas import tpu as pltpu
from jax.sharding import Mesh
from jax.sharding import PartitionSpec as P

HEAD_DIM = 32
SCALE = HEAD_DIM ** -0.5
LOG2E = math.log2(math.e)
C2 = SCALE * LOG2E
BIG = 1e30
TILE = 256
EPSILON = 1e-05
PAIRS = 5
SHORT, LONG = 384, 1152
f32, bf16 = jnp.float32, jnp.bfloat16
NT = (((1,), (1,)), ((), ()))


def pair_offset(info_ref):
    p = pl.program_id(0)
    sub = jnp.where(p == PAIRS - 1, info_ref[0], lax.rem(p, 2))
    return sub * (2 * HEAD_DIM)


def split3(v):
    a = v.astype(bf16)
    r = v - a.astype(f32)
    b = r.astype(bf16)
    d = (r - b.astype(f32)).astype(bf16)
    return a, b, d


def rows_masked(xT, off):
    row = lax.broadcasted_iota(jnp.int32, xT.shape, 0) - off
    xf = xT.astype(f32)
    return [jnp.where((row >= HEAD_DIM * j) & (row < HEAD_DIM * (j + 1)), xf, 0.0).astype(bf16) for j in range(2)]


def lanes_masked(x, off):
    lane = lax.broadcasted_iota(jnp.int32, x.shape, 1) - off
    xf = x.astype(f32)
    return [jnp.where((lane >= HEAD_DIM * j) & (lane < HEAD_DIM * (j + 1)), xf, 0.0).astype(bf16) for j in range(2)]


def attend_kernel(info_ref, qT_ref, k_ref, vT_ref, kaug_ref, qaugT_ref, oT_ref, o_ref, l_ref, rhs):
    off = pair_offset(info_ref)
    oT_ref[...] = jnp.where(lax.rem(pl.program_id(0), 2) == 0, 0.0, oT_ref[...])
    for t in range(2):
        cols = slice(t * TILE, (t + 1) * TILE)
        masked = rows_masked(qT_ref[:, cols], off)
        for j in range(2):
            rhs[0:128, j * TILE:(j + 1) * TILE] = masked[j]
            rhs[128:256, j * TILE:(j + 1) * TILE] = qaugT_ref[:, cols]
        start = info_ref[1 + t]
        need = info_ref[3 + t]

        def block(first, size):
            def step(i, carry):
                row = pl.multiple_of(first + i * size, 128)
                lhs = jnp.concatenate([k_ref[pl.ds(row, size), :], kaug_ref[pl.ds(row, size), :]], axis=1)
                raw = [jnp.dot(lhs, rhs[:, j * TILE:(j + 1) * TILE], preferred_element_type=f32) for j in range(2)]
                out = []
                for j in range(2):
                    m, l, o = carry[j]
                    s = raw[j] * C2
                    m_new = jnp.maximum(m, jnp.max(s, axis=0, keepdims=True))
                    alpha = jnp.exp2(m - m_new)
                    p = jnp.exp2(s - m_new)
                    vT = vT_ref[pl.ds(pl.multiple_of(off + j * HEAD_DIM, HEAD_DIM), HEAD_DIM), pl.ds(row, size)]
                    out.append((m_new, l * alpha + jnp.sum(p, axis=0, keepdims=True),
                                o * alpha + jnp.dot(vT, p.astype(bf16), preferred_element_type=f32)))
                return tuple(out)
            return step

        def finish(state):
            for j in range(2):
                m, l, o = state[j]
                oT_ref[pl.ds(pl.multiple_of(off + j * HEAD_DIM, HEAD_DIM), HEAD_DIM), cols] = o * (1.0 / l)
                l_ref[0, j:j + 1, cols] = m + jnp.log2(l)

        init = tuple((jnp.full((1, TILE), -1e38, f32), jnp.zeros((1, TILE), f32), jnp.zeros((HEAD_DIM, TILE), f32)) for _ in range(2))

        longs = lax.div(need, LONG)
        state = lax.fori_loop(0, longs, block(start, LONG), init)
        finish(lax.fori_loop(0, lax.div(need - longs * LONG, SHORT), block(start + longs * LONG, SHORT), state))

    o_ref[...] = oT_ref[...].T.astype(bf16)


def attend(m, info, qT, k, vT, kaug, qaugT):
    win, nq = k.shape[1], qT.shape[2]
    qT, k, vT = stay(qT, k, vT)
    return pl.pallas_call(
        attend_kernel,
        out_shape=(jax.ShapeDtypeStruct((384, nq), f32), jax.ShapeDtypeStruct((nq, 384), bf16), jax.ShapeDtypeStruct((PAIRS, 8, nq), f32)),
        grid_spec=pltpu.PrefetchScalarGridSpec(
            num_scalar_prefetch=1, grid=(PAIRS,),
            in_specs=[
                pl.BlockSpec((None, 128, nq), lambda p, *_: (m, p // 2, 0)),
                pl.BlockSpec((None, win, 128), lambda p, *_: (m, 0, p // 2)),
                pl.BlockSpec((None, 128, win), lambda p, *_: (m, p // 2, 0)),
                pl.BlockSpec((win, 128), lambda p, *_: (0, 0)),
                pl.BlockSpec((128, nq), lambda p, *_: (0, 0)),
            ],
            out_specs=[
                pl.BlockSpec((128, nq), lambda p, *_: (p // 2, 0)),
                pl.BlockSpec((nq, 128), lambda p, *_: (0, p // 2)),
                pl.BlockSpec((1, 8, nq), lambda p, *_: (p, 0, 0)),
            ],
            scratch_shapes=[pltpu.VMEM((256, 2 * TILE), bf16)],
        ),
        compiler_params=pltpu.CompilerParams(vmem_limit_bytes=28 << 20),
        cost_estimate=pl.CostEstimate(flops=int(20 * 10**9 * 0.02), bytes_accessed=0, transcendentals=0),
        name="attend",
    )(info, qT, k, vT, kaug, qaugT)


def attend_back_kernel(info_ref, qT_ref, q_ref, k_ref, kT_ref, v_ref, doT_ref, do_ref, oT_ref, l_ref, kaug_ref, qaugT_ref,
                       dq_ref, dk_ref, dv_ref, dqT_ref, rhs_s, rhs_d, q_stk, do_stk, dk_acc, dv_acc):
    p_id = pl.program_id(0)
    off = pair_offset(info_ref)

    @pl.when(lax.rem(p_id, 2) == 0)
    def _():
        dqT_ref[...] = jnp.zeros_like(dqT_ref)
        dk_acc[...] = jnp.zeros_like(dk_acc)
        dv_acc[...] = jnp.zeros_like(dv_acc)

    for t in range(2):
        cols = slice(t * TILE, (t + 1) * TILE)
        masked_q = rows_masked(qT_ref[:, cols], off)
        masked_do = rows_masked(doT_ref[:, cols], off)
        lane_q = lanes_masked(q_ref[cols, :], off)
        lane_do = lanes_masked(do_ref[cols, :], off)
        for j in range(2):
            part = slice(j * TILE, (j + 1) * TILE)
            head = pl.ds(pl.multiple_of(off + j * HEAD_DIM, HEAD_DIM), HEAD_DIM)
            delta = jnp.sum(doT_ref[head, cols].astype(f32) * oT_ref[head, cols], axis=0, keepdims=True)
            total = l_ref[0, j:j + 1, cols] * (1.0 / C2)
            rowid = lax.broadcasted_iota(jnp.int32, (64, TILE), 0)
            lp, dp = split3(-total), split3(-delta)
            def pieces(parts):
                x = jnp.zeros((64, TILE), f32)
                for n in range(3):
                    x = jnp.where(rowid == n, parts[n].astype(f32), x)
                return x.astype(bf16)
            rhs_s[0:128, part] = masked_q[j]
            rhs_s[128:192, part] = qaugT_ref[0:64, cols]
            rhs_s[192:256, part] = pieces(lp)
            rhs_d[0:128, part] = masked_do[j]
            rhs_d[128:192, part] = jnp.zeros((64, TILE), bf16)
            rhs_d[192:256, part] = pieces(dp)
            q_stk[part, :] = lane_q[j]
            do_stk[part, :] = lane_do[j]
        start = info_ref[1 + t]
        need = info_ref[3 + t]

        def block(first, size):
            def step(i, carry):
                row = pl.multiple_of(first + i * size, 128)
                rows = pl.ds(row, size)
                aug = kaug_ref[rows, :]
                lhs_k = jnp.concatenate([k_ref[rows, :], aug], axis=1)
                lhs_v = jnp.concatenate([v_ref[rows, :], aug], axis=1)
                out, dv, dk = [], dv_acc[rows, :], dk_acc[rows, :]
                for j in range(2):
                    part = slice(j * TILE, (j + 1) * TILE)
                    s = jnp.dot(lhs_k, rhs_s[:, part], preferred_element_type=f32)
                    dp = jnp.dot(lhs_v, rhs_d[:, part], preferred_element_type=f32)
                    p = jnp.exp2(s * C2)
                    ds = (p * dp).astype(bf16)
                    dv = dv + jnp.dot(p.astype(bf16), do_stk[part, :], preferred_element_type=f32)
                    dk = dk + jnp.dot(ds, q_stk[part, :], preferred_element_type=f32)
                    kT = kT_ref[pl.ds(pl.multiple_of(off + j * HEAD_DIM, HEAD_DIM), HEAD_DIM), rows]
                    out.append(carry[j] + jnp.dot(kT, ds, preferred_element_type=f32))
                dv_acc[rows, :] = dv
                dk_acc[rows, :] = dk
                return tuple(out)
            return step

        def finish(dqs):
            for j in range(2):
                dqT_ref[pl.ds(pl.multiple_of(off + j * HEAD_DIM, HEAD_DIM), HEAD_DIM), cols] = dqs[j] * SCALE

        init = tuple(jnp.zeros((HEAD_DIM, TILE), f32) for _ in range(2))

        longs = lax.div(need, LONG)
        state = lax.fori_loop(0, longs, block(start, LONG), init)
        finish(lax.fori_loop(0, lax.div(need - longs * LONG, SHORT), block(start + longs * LONG, SHORT), state))
    @pl.when((lax.rem(p_id, 2) == 1) | (p_id == PAIRS - 1))
    def _():
        dq_ref[...] = dqT_ref[...].T.astype(bf16)
        dk_ref[...] = (dk_acc[...] * SCALE).astype(bf16)
        dv_ref[...] = dv_acc[...].astype(bf16)


def attend_back(m, info, qT, q, k, kT, v, doT, do, oT, lse, kaug, qaugT):
    win, nq = k.shape[1], qT.shape[2]
    qT, q, k, kT, v = stay(qT, q, k, kT, v)
    wide = pl.BlockSpec((128, nq), lambda p, *_: (p // 2, 0))
    tall = pl.BlockSpec((nq, 128), lambda p, *_: (0, p // 2))
    keys = pl.BlockSpec((win, 128), lambda p, *_: (0, p // 2))
    wide_m = pl.BlockSpec((None, 128, nq), lambda p, *_: (m, p // 2, 0))
    tall_m = pl.BlockSpec((None, nq, 128), lambda p, *_: (m, 0, p // 2))
    keys_m = pl.BlockSpec((None, win, 128), lambda p, *_: (m, 0, p // 2))
    return pl.pallas_call(
        attend_back_kernel,
        out_shape=(far(nq, 384), far(win, 384), far(win, 384)),
        grid_spec=pltpu.PrefetchScalarGridSpec(
            num_scalar_prefetch=1, grid=(PAIRS,),
            in_specs=[wide_m, tall_m, keys_m, pl.BlockSpec((None, 128, win), lambda p, *_: (m, p // 2, 0)), keys_m,
                      pl.BlockSpec((128, nq), lambda p, *_: (p // 2, m)), pl.BlockSpec((nq, 128), lambda p, *_: (m, p // 2)), wide,
                      pl.BlockSpec((1, 8, nq), lambda p, *_: (p, 0, 0)),
                      pl.BlockSpec((win, 128), lambda p, *_: (0, 0)), pl.BlockSpec((128, nq), lambda p, *_: (0, 0))],
            out_specs=[tall, keys, keys],
            scratch_shapes=[pltpu.VMEM((128, nq), f32), pltpu.VMEM((256, 2 * TILE), bf16), pltpu.VMEM((256, 2 * TILE), bf16),
                            pltpu.VMEM((2 * TILE, 128), bf16), pltpu.VMEM((2 * TILE, 128), bf16),
                            pltpu.VMEM((win, 128), f32), pltpu.VMEM((win, 128), f32)],
        ),
        compiler_params=pltpu.CompilerParams(vmem_limit_bytes=32 << 20),
        cost_estimate=pl.CostEstimate(flops=int(40 * 10**9 * 0.02), bytes_accessed=0, transcendentals=0),
        name="attend_back",
    )(info, qT, q, k, kT, v, doT, do, oT, lse, kaug, qaugT)


def moments(x):
    centred = x - jnp.mean(x, axis=-1, keepdims=True)
    r = lax.rsqrt(jnp.mean(centred * centred, axis=-1, keepdims=True) + EPSILON)
    return centred * r, r


def norm_back(grad, n, r, gain):
    e = grad * gain
    return r * (e - jnp.mean(e, axis=-1, keepdims=True) - n * jnp.mean(e * n, axis=-1, keepdims=True))


def call(kernel, out_shape, name, flops=10**9, limit=48, **spec):
    return pl.pallas_call(
        kernel, out_shape=out_shape, name=name,
        compiler_params=pltpu.CompilerParams(vmem_limit_bytes=limit << 20),
        cost_estimate=pl.CostEstimate(flops=int(flops * 0.02), bytes_accessed=0, transcendentals=0), **spec)


def shape(*dims, dtype=bf16):
    return jax.ShapeDtypeStruct(dims, dtype)


def far(*dims):
    return pltpu.MemorySpace.HBM(dims, bf16)


def stay(*arrays):
    return [pltpu.with_memory_space_constraint(a, pltpu.MemorySpace.HBM) for a in arrays]


def scalar_first(grid, in_specs, out_specs, scratch=()):
    return dict(grid_spec=pltpu.PrefetchScalarGridSpec(
        num_scalar_prefetch=1, grid=grid, in_specs=in_specs, out_specs=out_specs, scratch_shapes=list(scratch)))


def full(*dims):
    return pl.BlockSpec(dims, lambda *_: (0,) * len(dims))


def pack_heads_kernel(core_ref, qkv_ref, vec_ref, heads_ref):
    for part in range(3):
        near = pl.ds(pl.multiple_of(640 * part + 256 * core_ref[0], 128), 256)
        heads_ref[:, 384 * part:384 * part + 256] = qkv_ref[:, near]
        heads_ref[:, 384 * part + 256:384 * (part + 1)] = qkv_ref[:, 640 * part + 512:640 * (part + 1)]
    heads_ref[:, 1152:1280] = vec_ref[...]


def pack_heads(core, w_qkv, vectors):
    return call(pack_heads_kernel, shape(160, 1280), "pack_heads", 10**6, 8, **scalar_first(
        (1,), [full(160, 1920), full(160, 128)], full(160, 1280)))(core, w_qkv, vectors)


def turn_kernel(vec_ref, rows_ref):
    rows_ref[...] = vec_ref[...].astype(f32).T[:16]


def vector_rows(heads):
    return call(turn_kernel, shape(16, 640, dtype=f32), "vector_rows", 10**6, 8, grid=(1,),
                in_specs=[pl.BlockSpec((640, 128), lambda i: (0, 9))], out_specs=full(16, 640))(heads)


def pack_feed_kernel(core_ref, up_ref, down_ref, feed_ref):
    core = core_ref[0]
    for f in range(4):
        feed_ref[:, 640 * f:640 * (f + 1)] = up_ref[:, pl.ds(pl.multiple_of(1280 * f + 640 * core, 128), 640)]
        feed_ref[:, 2560 + 640 * f:2560 + 640 * (f + 1)] = down_ref[pl.ds(pl.multiple_of(640 * core + 160 * f, 32), 160), :]


def pack_feed(core, w_up, w_down):
    return call(pack_feed_kernel, shape(160, 5120), "pack_feed", 10**6, 16, **scalar_first(
        (1,), [full(160, 5120), full(1280, 640)], full(160, 5120)))(core, w_up, w_down)


def rows_in_order(core, mine, theirs, x_ref):
    mine, theirs = mine.astype(f32), theirs.astype(f32)
    x_ref[0:256, :] = jnp.where(core == 0, mine, theirs)
    x_ref[256:512, :] = jnp.where(core == 0, theirs, mine)


def window_rows(core, own_refs, other_refs, m, block, x_ref):
    for j in range(len(own_refs)):
        @pl.when(block == j)
        def _():
            rows_in_order(core, own_refs[j][m], other_refs[j][m], x_ref)


def project_kernel(chips, place_ref, *refs):
    n = len(chips)
    own_refs, other_refs = refs[:n], refs[n:2 * n]
    vec_ref, w_ref = refs[2 * n:2 * n + 2]
    k_ref, v_ref, kT_ref, vT_ref = refs[-6 - 2 * (n == 3):][:4]
    x_ref, hid_ref = refs[-2:]
    m, step = pl.program_id(0), pl.program_id(1)
    block = sum(jnp.where(step == i, chip, 0) for i, chip in enumerate(chips))
    needed = (block >= place_ref[1 + 2 * m]) & (block < place_ref[2 + 2 * m])

    @pl.when(jnp.logical_not(needed))
    def _():
        for ref in (k_ref, v_ref, kT_ref, vT_ref):
            ref[...] = jnp.zeros_like(ref)

    @pl.when(needed)
    def _():
        window_rows(place_ref[0], own_refs, other_refs, m, step, x_ref)
        hidden = (moments(x_ref[...])[0] * vec_ref[0:1, :] + vec_ref[1:2, :]).astype(bf16)
        hid_ref[...] = hidden
        kv = jnp.dot(hidden, w_ref[:, 384:], preferred_element_type=f32)
        low = kv.astype(bf16)
        k_ref[0] = low[:, :384]
        v_ref[0] = low[:, 384:]
        turned = kv.T.astype(bf16)
        kT_ref[0] = turned[:384]
        vT_ref[0] = turned[384:]

    if n == 3:
        q_ref, qT_ref = refs[-4:-2]

        @pl.when(step == 1)
        def _():
            q = jnp.dot(hid_ref[...], w_ref[:, :384], preferred_element_type=f32)
            q_ref[0] = q.astype(bf16)
            qT_ref[0] = q.T.astype(bf16)


def project(chips, place, own, other, vec, w, earlier=()):
    n = len(chips)
    chip = (lambda b: b + 1) if n == 3 else (lambda b: 4 * b)
    tall = pl.BlockSpec((1, 512, 384), lambda m, b, *_: (m, chip(b), 0))
    wide = pl.BlockSpec((1, 384, 512), lambda m, b, *_: (m, 0, chip(b)))
    shapes = [far(2, 2560, 384), far(2, 2560, 384), far(2, 384, 2560), far(2, 384, 2560)]
    specs = [tall, tall, wide, wide]
    if n == 3:
        shapes += [far(2, 512, 384), far(2, 384, 512)]
        specs += [pl.BlockSpec((1, 512, 384), lambda m, *_: (m, 0, 0)), pl.BlockSpec((1, 384, 512), lambda m, *_: (m, 0, 0))]
    own, other = [own[c] for c in chips], [other[c] for c in chips]
    return call(
        lambda *refs: project_kernel(chips, *refs), shapes, "project", 5 * 10**9, 28,
        input_output_aliases={2 * n + 3 + i: i for i in range(len(earlier))}, **scalar_first(
            (2, n), [full(2, 256, 640)] * (2 * n) + [full(16, 640), full(640, 1152)] + [pl.BlockSpec(memory_space=pl.ANY)] * len(earlier),
            specs, [pltpu.VMEM((512, 640), f32), pltpu.VMEM((512, 640), bf16)]))(place, *own, *other, vec, w, *earlier)


def heads_joined(core, mine, theirs):
    first, second = (jnp.where(core == 0, a, b) for a, b in ((mine, theirs), (theirs, mine)))
    return jnp.concatenate([first[:, :256], second[:, :256], first[:, 256:] + second[:, 256:]], axis=1)


def middle_kernel(place_ref, low0_ref, low1_ref, theirs_ref, tok_ref, tok2_ref, vec_ref, w0_ref, w1_ref, w2_ref, w3_ref,
                  mid_ref, hid_ref, hid2_ref, w_ref):
    core = place_ref[0]
    for by, part in enumerate((w0_ref, w1_ref, w2_ref, w3_ref)):
        w_ref[pl.ds(pl.multiple_of(lax.rem(place_ref[5] + 4 - by, 4) * 160, 32), 160), :] = part[...]
    for m, low_ref in enumerate((low0_ref, low1_ref)):
        attended = heads_joined(core, low_ref[...].astype(f32), theirs_ref[m].astype(f32)).astype(bf16)
        branch = jnp.dot(attended, w_ref[...], preferred_element_type=f32)
        mine = jnp.where(core == 0, branch[:256], branch[256:]) + tok_ref[m].astype(f32)
        theirs = jnp.where(core == 0, branch[256:], branch[:256]) + tok2_ref[m].astype(f32)
        part = slice(256 * m, 256 * (m + 1))
        mid_ref[part, :] = mine
        hid_ref[part, :] = (moments(mine)[0] * vec_ref[2:3, :] + vec_ref[3:4, :]).astype(bf16)
        hid2_ref[part, :] = (moments(theirs)[0] * vec_ref[2:3, :] + vec_ref[3:4, :]).astype(bf16)


def middle_step(place, *args):
    return call(middle_kernel, (shape(512, 640, dtype=f32), shape(512, 640), shape(512, 640), shape(640, 640)), "middle", 10**9, 20, **scalar_first(
        (1,), [full(*a.shape) for a in args], [full(512, 640)] * 3 + [full(640, 640)]))(place, *args)


def feed_kernel(h_ref, h2_ref, cot_ref, cot2_ref, up_ref, down_ref, mine_ref, theirs_ref, g_ref, h, cot, hT, cT, out, dh):
    chunk = pl.program_id(0)

    @pl.when(chunk == 0)
    def _():
        h[0:512, :], h[512:1024, :] = h_ref[...], h2_ref[...]
        cot[0:512, :], cot[512:1024, :] = cot_ref[...], cot2_ref[...]
        hT[...] = h[...].astype(f32).T.astype(bf16)
        cT[...] = cot[...].astype(f32).T.astype(bf16)
        out[...] = jnp.zeros_like(out)
        dh[...] = jnp.zeros_like(dh)

    up_w = up_ref[...]
    down_w = jnp.concatenate([down_ref[160 * y:160 * (y + 1), 640 * i:640 * (i + 1)] for y in range(2) for i in range(4)], axis=0)
    acts, d_ups = [], []
    for t in range(4):
        rows = slice(256 * t, 256 * (t + 1))
        u = jnp.dot(h[rows, :], up_w, preferred_element_type=f32)
        d_act = lax.dot_general(cot[rows, :], down_w, NT, preferred_element_type=f32)
        cdf = 0.5 * (1.0 + lax.erf(u * (2.0 ** -0.5)))
        pdf = jnp.exp(u * u * -0.5) * ((2.0 * math.pi) ** -0.5)
        act = (u * cdf).astype(bf16)
        d_up = (d_act * (cdf + u * pdf)).astype(bf16)
        out[rows, :] += jnp.dot(act, down_w, preferred_element_type=f32)
        dh[rows, :] += lax.dot_general(d_up, up_w, NT, preferred_element_type=f32)
        acts.append(act)
        d_ups.append(d_up)
    g_up = jnp.dot(hT[...], jnp.concatenate(d_ups, axis=0), preferred_element_type=f32).astype(bf16)
    g_down = jnp.dot(cT[...], jnp.concatenate(acts, axis=0), preferred_element_type=f32).T.astype(bf16)
    for f in range(2):
        for y in range(4):
            for i in range(2):
                g_ref[4 * chunk + 2 * f + i, y] = g_up[160 * y + 80 * i:160 * y + 80 * (i + 1), 640 * f:640 * (f + 1)]
        for i in range(8):
            g_ref[8 + i, 2 * chunk + f] = g_down[640 * f + 80 * i:640 * f + 80 * (i + 1)]

    @pl.when(chunk == 1)
    def _():
        mine_ref[0], mine_ref[1] = out[0:512, :].astype(bf16), dh[0:512, :].astype(bf16)
        theirs_ref[0], theirs_ref[1] = out[512:1024, :].astype(bf16), dh[512:1024, :].astype(bf16)


def feed_forward(h, h2, cot, cot2, weights):
    return call(
        feed_kernel,
        (shape(2, 512, 640), shape(2, 512, 640), shape(16, 4, 80, 640)),
        "feed_forward", 30 * 10**9, 52, grid=(2,),
        in_specs=[full(512, 640)] * 4 + [pl.BlockSpec((640, 1280), lambda f: (0, f)), pl.BlockSpec((320, 2560), lambda f: (f, 1))],
        out_specs=[full(2, 512, 640), full(2, 512, 640), full(16, 4, 80, 640)],
        scratch_shapes=[pltpu.VMEM((1024, 640), bf16), pltpu.VMEM((1024, 640), bf16), pltpu.VMEM((640, 1024), bf16), pltpu.VMEM((640, 1024), bf16),
                        pltpu.VMEM((1024, 640), f32), pltpu.VMEM((1024, 640), f32)],
    )(h, h2, cot, cot2, weights, weights)


def after_kernel(mid_ref, mine_ref, theirs_ref, cot_ref, vec_ref, block_ref, grad_ref, branch_ref, g_ref):
    middle = mid_ref[...]
    block_ref[...] = (middle + mine_ref[0].astype(f32) + theirs_ref[0].astype(f32)).astype(bf16)
    d_hidden = mine_ref[1].astype(f32) + theirs_ref[1].astype(f32)
    n, r = moments(middle)
    g_ref[...] = jnp.zeros_like(g_ref)
    g_ref[0:1, :] = jnp.sum(d_hidden * n, axis=0, keepdims=True)
    g_ref[1:2, :] = jnp.sum(d_hidden, axis=0, keepdims=True)
    grad = cot_ref[...].astype(f32) + norm_back(d_hidden, n, r, vec_ref[2:3, :])
    grad_ref[...] = grad
    branch_ref[...] = grad.astype(bf16)


def after_feed(*args):
    return call(
        after_kernel, (shape(512, 640), shape(512, 640, dtype=f32), shape(512, 640), shape(8, 640, dtype=f32)), "after_feed", 10**9, 24,
        in_specs=[pl.BlockSpec(memory_space=pltpu.VMEM)] * 5, out_specs=[pl.BlockSpec(memory_space=pltpu.VMEM)] * 4)(*args)


def branch_kernel(core_ref, own_ref, their_ref, w_ref, low0_ref, low1_ref, theirs_ref, do_ref, doT_ref, g_ref):
    core = core_ref[0]
    w = jnp.concatenate([w_ref[pl.ds(pl.multiple_of(256 * core, 256), 256), :], w_ref[512:640, :]], axis=0)
    g = jnp.zeros((640, 384), f32)
    for m in range(2):
        part = slice(256 * m, 256 * (m + 1))
        mine, theirs = own_ref[part, :].astype(f32), their_ref[part, :].astype(f32)
        branch = jnp.concatenate([jnp.where(core == 0, mine, theirs), jnp.where(core == 0, theirs, mine)], axis=0)
        kept = jnp.where(core == 0, branch[:, :384], branch[:, 256:]).astype(bf16)
        branch = branch.astype(bf16)
        rows = slice(512 * m, 512 * (m + 1))
        do = lax.dot_general(branch, w, NT, preferred_element_type=f32)
        do_ref[rows, :] = do.astype(bf16)
        doT_ref[:, rows] = do.T.astype(bf16)
        attended = heads_joined(core, (low0_ref, low1_ref)[m][...].astype(f32), theirs_ref[m].astype(f32))
        g = g + jnp.dot(attended.T.astype(bf16), kept, preferred_element_type=f32)
    g_ref[...] = g


def branch_step(core, *args):
    specs = [full(*a.shape) for a in args]
    return call(
        branch_kernel, (shape(1024, 384), shape(384, 1024), shape(640, 384, dtype=f32)), "branch", 10**9, 24, **scalar_first(
            (1,), specs, [full(1024, 384), full(384, 1024), full(640, 384)]))(core, *args)


def project_back_kernel(core_ref, *refs):
    own_refs, other_refs = refs[:5], refs[5:10]
    (vec_ref, w_ref, dq0_ref, dq1_ref, dk0_ref, dk1_ref, dv0_ref, dv1_ref, g_out_ref, g_two_ref,
     mine_ref, theirs_ref, tail_ref, x_ref, d_kv, d_q, d_hid, g_ref, g_vec) = refs[10:]
    step, core = pl.program_id(0), core_ref[0]
    block = lax.rem(step, 5)

    @pl.when(step == 0)
    def _():
        g_ref[...] = jnp.zeros_like(g_ref)
        g_vec[...] = jnp.zeros_like(g_vec)
        g_vec[2:4, :] = g_two_ref[0:2, :]

    second = lax.div(step, 5)
    needed = (block >= core_ref[1 + 2 * second]) & (block < core_ref[2 + 2 * second])

    @pl.when(jnp.logical_not(needed))
    def _():
        mine_ref[...] = jnp.zeros_like(mine_ref)
        theirs_ref[...] = jnp.zeros_like(theirs_ref)

    for m, (dq, dk, dv) in enumerate(((dq0_ref, dk0_ref, dv0_ref), (dq1_ref, dk1_ref, dv1_ref))):
        @pl.when(needed & (second == m))
        def _():
            window_rows(core, own_refs, other_refs, m, block, x_ref)
            d_kv[:, :384], d_kv[:, 384:] = dk[...], dv[...]
            d_q[...] = dq[...]

    @pl.when(needed)
    def _():
        n = moments(x_ref[...])[0]
        hiddenT = (n * vec_ref[0:1, :] + vec_ref[1:2, :]).T.astype(bf16)
        d_hid[...] = lax.dot_general(d_kv[...], w_ref[:, 384:], NT, preferred_element_type=f32)
        g_ref[:, 384:] += jnp.dot(hiddenT, d_kv[...], preferred_element_type=f32)

        @pl.when(block == 2)
        def _():
            g_ref[:, :384] += jnp.dot(hiddenT, d_q[...], preferred_element_type=f32)
            d_hid[...] += lax.dot_general(d_q[...], w_ref[:, :384], NT, preferred_element_type=f32)

        dh = d_hid[...]
        mine_ref[0, 0] = jnp.where(core == 0, dh[:256], dh[256:]).astype(bf16)
        theirs_ref[0, 0] = jnp.where(core == 0, dh[256:], dh[:256]).astype(bf16)
        g_vec[0:1, :] += jnp.sum(dh * n, axis=0, keepdims=True)
        g_vec[1:2, :] += jnp.sum(dh, axis=0, keepdims=True)

    @pl.when(step == 9)
    def _():
        turned = g_vec[...].T
        lane = lax.broadcasted_iota(jnp.int32, (640, 128), 1) - 64 * (1 - core)
        spare = g_ref[:, 256:384]
        for i in range(4):
            spare = jnp.where(lane == i, turned[:, i:i + 1], spare)
        g_ref[:, 256:384] = spare
        for y in range(4):
            for z in range(4):
                rows = slice(160 * y + 40 * z, 160 * y + 40 * (z + 1))
                for x in range(3):
                    tail_ref[16 * y + 4 * z + x] = g_ref[rows, 384 * x:384 * (x + 1)].astype(bf16)
                tail_ref[16 * y + 4 * z + 3] = g_out_ref[rows, :].astype(bf16)


def project_back(core, own, other, vec, w, dq, dk, dv, g_out, g_two):
    dk, dv = stay(*dk), stay(*dv)
    first = pl.BlockSpec((512, 384), lambda b, *_: (jnp.minimum(b, 4), 0))
    second = pl.BlockSpec((512, 384), lambda b, *_: (jnp.maximum(b - 5, 0), 0))
    return call(
        project_back_kernel, (shape(5, 2, 256, 640), shape(5, 2, 256, 640), shape(64, 40, 384)), "project_back", 10**10, 36, **scalar_first(
            (10,), [full(2, 256, 640)] * 10 + [full(16, 640), full(640, 1152), full(512, 384), full(512, 384), first, second, first, second,
                                               full(640, 384), full(8, 640)],
            [pl.BlockSpec((1, 1, 256, 640), lambda b, *_: (lax.rem(b, 5), b // 5, 0, 0))] * 2 + [full(64, 40, 384)],
            [pltpu.VMEM((512, 640), f32), pltpu.VMEM((512, 768), bf16), pltpu.VMEM((512, 384), bf16),
             pltpu.VMEM((512, 640), f32), pltpu.VMEM((640, 1152), f32), pltpu.VMEM((8, 640), f32)]))(core, *own, *other, vec, w, *dq, *dk, *dv, g_out, g_two)


def in_core_order(core_ref, mine, theirs):
    core, mine, theirs = core_ref[0], mine.astype(f32), theirs.astype(f32)
    return jnp.where(core == 0, mine, theirs), jnp.where(core == 0, theirs, mine)


def final_feed_kernel(core_ref, mine_ref, theirs_ref, up_ref, down_ref):
    for i in range(16):
        for c, piece in enumerate(in_core_order(core_ref, mine_ref[i], theirs_ref[i])):
            if i < 8:
                base = 1280 * (i // 2) + 640 * c
                up_ref[80 * (i % 2):80 * (i % 2 + 1), base:base + 640] = piece
            else:
                base = 640 * c + 80 * (i - 8)
                down_ref[base:base + 80, :] = piece


def final_feed(core, mine, theirs):
    return call(final_feed_kernel, (shape(160, 5120, dtype=f32), shape(1280, 640, dtype=f32)), "final_feed", 10**6, 32, **scalar_first(
        (1,), [full(16, 80, 640)] * 2, [full(160, 5120), full(1280, 640)]))(core, mine, theirs)


def final_heads_kernel(core_ref, mine_ref, theirs_ref, qkv_ref, out_ref, vec_ref):
    lane = lax.broadcasted_iota(jnp.int32, (40, 128), 1)
    for z in range(4):
        rows = slice(40 * z, 40 * (z + 1))
        for x in range(4):
            a, b = in_core_order(core_ref, mine_ref[4 * z + x], theirs_ref[4 * z + x])
            if x < 3:
                last = jnp.where(lane < 64, a[:, 256:], b[:, 256:])
                qkv_ref[rows, 640 * x:640 * (x + 1)] = jnp.concatenate([a[:, :256], b[:, :256], last], axis=1)
            else:
                out_ref[rows, :] = jnp.concatenate([a, b[:, 128:]], axis=1)
            if x == 0:
                vec_ref[rows, :] = pltpu.roll(a[:, 256:], 64, 1) + b[:, 256:]


def final_heads(core, mine, theirs):
    return call(
        final_heads_kernel, (shape(160, 1920, dtype=f32), shape(160, 640, dtype=f32), shape(160, 128, dtype=f32)), "final_heads", 10**6, 16,
        **scalar_first((1,), [full(16, 40, 384)] * 2, [full(160, 1920), full(160, 640), full(160, 128)]))(core, mine, theirs)


def shifted(array, axis, by):
    devices = lax.axis_size(axis)
    return lax.ppermute(array, axis, [(i, (i + by) % devices) for i in range(devices)])


def passed_along(array, by):
    devices = lax.axis_size(("z", "x"))
    return lax.ppermute(array, ("z", "x"), [(i, i + by) for i in range(devices) if 0 <= i + by < devices])


def swapped(array):
    return lax.ppermute(array, "core", [(0, 1), (1, 0)])


def pick(array, index):
    return lax.dynamic_index_in_dim(array, index, 0, keepdims=False)


def gathered(array, axis):
    me, devices = lax.axis_index(axis), lax.axis_size(axis)
    out = jnp.zeros((devices,) + array.shape, array.dtype)
    out = lax.dynamic_update_index_in_dim(out, array, me, 0)
    for by in (1, devices - 1, 2):
        out = lax.dynamic_update_index_in_dim(out, shifted(array, axis, by), (me + devices - by) % devices, 0)
    return out


def window_info(length_row, chip, core, win):
    ends = jnp.cumsum(length_row)
    starts = ends - length_row
    base = chip * 512 - 1024
    places = base + jnp.arange(win, dtype=jnp.int32)
    inside = (places[:, None] >= starts[None, :]) & (places[:, None] < ends[None, :])
    ones = jnp.broadcast_to(jnp.arange(64) < 3, (win, 64)).astype(bf16)
    key_rows = jnp.concatenate([jnp.where(inside, 0.0, -BIG).astype(bf16), ones], axis=1)
    own = chip * 512 + jnp.arange(512, dtype=jnp.int32)
    inside_q = (own[None, :] >= starts[:, None]) & (own[None, :] < ends[:, None])
    query_rows = jnp.concatenate([inside_q.astype(bf16), jnp.zeros((64, 512), bf16)], axis=0)
    info = [core]
    sizes = []
    for t in range(2):
        first = chip * 512 + t * TILE
        low = jnp.max(jnp.where(starts <= first, starts, 0)) - base
        high = jnp.min(jnp.where(ends > first + TILE - 1, ends, 1 << 30)) - base
        start = low // 128 * 128
        need = high - start
        size = (need + SHORT - 1) // SHORT * SHORT
        info.append(jnp.minimum(start, win - size))
        sizes.append(size)
    low = jnp.minimum(info[1], info[2]) // 512
    high = (jnp.maximum(info[1] + sizes[0], info[2] + sizes[1]) + 511) // 512
    return jnp.stack(info + sizes).astype(jnp.int32), key_rows, query_rows, [low, high]


def body(tokens, lengths, gain_one, bias_one, w_qkv, w_out, gain_two, bias_two, w_up, w_down, cotangent):
    core, chip = lax.axis_index("core"), lax.axis_index(("z", "x"))
    core_arg = core[None].astype(jnp.int32)
    tok, cot = tokens[:, 0], cotangent[:, 0].reshape(512, 640)
    together = lambda *arrays: lax.optimization_barrier(arrays)

    vectors = jnp.pad(jnp.stack([gain_one, bias_one, gain_two, bias_two], axis=1), ((0, 0), (0, 124)))
    before, after, tok_other = passed_along(tok, 1), passed_along(tok, -1), swapped(tok)
    heads = lax.all_gather(pack_heads(core_arg, w_qkv, vectors), "batch", axis=0, tiled=True)
    heads, before, after, tok_other, w_up, w_down = together(heads, before, after, tok_other, w_up, w_down)
    feed_weights = lax.all_gather(pack_feed(core_arg, w_up, w_down), "batch", axis=0, tiled=True)
    vec = vector_rows(heads)
    windows = [window_info(lengths[m, 0], chip, core, 2560) for m in range(2)]
    place = jnp.stack([core] + windows[0][3] + windows[1][3] + [lax.axis_index("batch")]).astype(jnp.int32)
    own, other = [None, before, tok, after, None], [None, swapped(before), tok_other, swapped(after), None]
    before, after, place, own[1:4], other[1:4] = together(before, after, place, own[1:4], other[1:4])
    own[0], own[4] = passed_along(before, 1), passed_along(after, -1)
    *near_parts, q, qT = project((1, 2, 3), place, own, other, vec, heads)
    own[0], own[4], near_parts = together(own[0], own[4], near_parts)
    other[0], other[4] = swapped(own[0]), swapped(own[4])
    k, v, kT, vT = project((0, 4), place, own, other, vec, heads, near_parts)
    w_out_parts = [shifted(w_out, "batch", by) for by in (1, 2, 3)]
    info, key_rows, query_rows, _ = windows[0]
    oT0, low0, lse0 = attend(0, info, qT, k, vT, key_rows, query_rows)
    w_out_parts, qT_next, low0 = together(w_out_parts, qT, low0)
    w_out_parts = [w_out] + w_out_parts
    info, key_rows, query_rows, _ = windows[1]
    oT1, low1, lse1 = attend(1, info, qT_next, k, vT, key_rows, query_rows)

    theirs = swapped(jnp.stack([low0, low1]))
    middle, hidden_two, hidden_other, w_out_all = middle_step(place, low0, low1, theirs, tok, tok_other, vec, *w_out_parts)
    mine, partial, feed_grads = feed_forward(hidden_two, hidden_other, cot, swapped(cot), feed_weights)
    feed_grads = lax.psum_scatter(feed_grads.reshape(5120, 640), ("z", "x"), scatter_dimension=0, tiled=True)
    block_out, grad_middle, branch, g_two = after_feed(middle, mine, swapped(partial), cot, vec)

    do, doT, g_out = branch_step(core_arg, branch, swapped(branch), w_out_all, low0, low1, theirs)
    dq, dk, dv = zip(*(
        attend_back(m, info, qT, q, k, kT, v, doT, do, oT, lse, key_rows, query_rows)
        for m, ((info, key_rows, query_rows, _), oT, lse) in enumerate(zip(windows, (oT0, oT1), (lse0, lse1)))))
    dq, feed_grads = together(dq, feed_grads)
    feed = lax.psum_scatter(feed_grads, "batch", scatter_dimension=0, tiled=True).reshape(80, 640)
    mine, theirs, tail = project_back(place, own, other, vec, heads, dq, dk, dv, g_out, g_two)

    feed, mine, theirs, tail = together(feed, mine, theirs, tail)

    tail = lax.all_to_all(tail, ("batch", "z", "x"), 0, 0, tiled=True)
    feed = lax.all_gather(feed, ("z", "x"), axis=0, tiled=True).reshape(16, 80, 640)
    theirs = swapped(theirs)
    sums = [mine[j].astype(f32) + theirs[j].astype(f32) for j in range(5)]
    right, left = passed_along(sums[4].astype(bf16), 1), passed_along(sums[0].astype(bf16), -1)
    tail, right, left = together(tail, right, left)
    right = passed_along((right.astype(f32) + sums[3]).astype(bf16), 1)
    left = passed_along((left.astype(f32) + sums[1]).astype(bf16), -1)
    tail = gathered(jnp.sum(tail.astype(f32), axis=0).astype(bf16), "x").reshape(160, 384)
    tail, right, left = together(tail, right, left)
    tail = gathered(tail, "z").reshape(16, 40, 384)
    d_one = (sums[2] + right.astype(f32) + left.astype(f32)).reshape(512, 640)
    n_one, r_one = moments(tok.reshape(512, 640).astype(f32))
    grad_tokens = (grad_middle + norm_back(d_one, n_one, r_one, vec[0:1])).astype(bf16)
    tail, grad_tokens = together(tail, grad_tokens)
    grad_qkv, grad_out, spare = final_heads(core_arg, tail, swapped(tail))
    grad_up, grad_down = final_feed(core_arg, feed, swapped(feed))
    return (
        block_out.reshape(2, 1, 256, 640), grad_tokens.reshape(2, 1, 256, 640), spare[:, 0], spare[:, 1], grad_qkv, grad_out,
        spare[:, 2], spare[:, 3], grad_up, grad_down)


def solution(mesh):
    fine = Mesh(mesh.devices.reshape(4, 4, 4, 2), ("batch", "z", "x", "core"))
    rows = P(None, "batch", ("z", "x", "core"), None)
    one, two = P("batch"), P("batch", None)
    return jax.shard_map(
        body,
        mesh=fine,
        in_specs=(rows, P(None, "batch", None), one, one, two, two, one, one, two, two, rows),
        out_specs=(rows, rows, one, one, two, two, one, one, two, two),
        check_vma=False,
    )
```

```python
import math

import jax
import jax.numpy as jnp
from jax import lax
from jax.experimental import pallas as pl
from jax.experimental.pallas import tpu as pltpu
from jax.sharding import Mesh
from jax.sharding import PartitionSpec as P

HEAD_DIM = 32
SCALE = HEAD_DIM ** -0.5
LOG2E = math.log2(math.e)
C2 = SCALE * LOG2E
BIG = 1e30
TILE = 256
EPSILON = 1e-05
PAIRS = 5
SHORT, LONG = 384, 1152
f32, bf16 = jnp.float32, jnp.bfloat16
NT = (((1,), (1,)), ((), ()))


def pair_offset(info_ref):
    p = pl.program_id(0)
    sub = jnp.where(p == PAIRS - 1, info_ref[0], lax.rem(p, 2))
    return sub * (2 * HEAD_DIM)


def split3(v):
    a = v.astype(bf16)
    r = v - a.astype(f32)
    b = r.astype(bf16)
    d = (r - b.astype(f32)).astype(bf16)
    return a, b, d


def rows_masked(xT, off):
    row = lax.broadcasted_iota(jnp.int32, xT.shape, 0) - off
    xf = xT.astype(f32)
    return [jnp.where((row >= HEAD_DIM * j) & (row < HEAD_DIM * (j + 1)), xf, 0.0).astype(bf16) for j in range(2)]


def lanes_masked(x, off):
    lane = lax.broadcasted_iota(jnp.int32, x.shape, 1) - off
    xf = x.astype(f32)
    return [jnp.where((lane >= HEAD_DIM * j) & (lane < HEAD_DIM * (j + 1)), xf, 0.0).astype(bf16) for j in range(2)]


def attend_kernel(info_ref, qT_ref, k_ref, vT_ref, kaug_ref, qaugT_ref, oT_ref, o_ref, l_ref, rhs):
    off = pair_offset(info_ref)
    oT_ref[...] = jnp.where(lax.rem(pl.program_id(0), 2) == 0, 0.0, oT_ref[...])
    for t in range(2):
        cols = slice(t * TILE, (t + 1) * TILE)
        masked = rows_masked(qT_ref[:, cols], off)
        for j in range(2):
            rhs[0:128, j * TILE:(j + 1) * TILE] = masked[j]
            rhs[128:256, j * TILE:(j + 1) * TILE] = qaugT_ref[:, cols]
        start = info_ref[1 + t]
        need = info_ref[3 + t]

        def block(first, size):
            def step(i, carry):
                row = pl.multiple_of(first + i * size, 128)
                lhs = jnp.concatenate([k_ref[pl.ds(row, size), :], kaug_ref[pl.ds(row, size), :]], axis=1)
                raw = [jnp.dot(lhs, rhs[:, j * TILE:(j + 1) * TILE], preferred_element_type=f32) for j in range(2)]
                out = []
                for j in range(2):
                    m, l, o = carry[j]
                    s = raw[j] * C2
                    m_new = jnp.maximum(m, jnp.max(s, axis=0, keepdims=True))
                    alpha = jnp.exp2(m - m_new)
                    p = jnp.exp2(s - m_new)
                    vT = vT_ref[pl.ds(pl.multiple_of(off + j * HEAD_DIM, HEAD_DIM), HEAD_DIM), pl.ds(row, size)]
                    out.append((m_new, l * alpha + jnp.sum(p, axis=0, keepdims=True),
                                o * alpha + jnp.dot(vT, p.astype(bf16), preferred_element_type=f32)))
                return tuple(out)
            return step

        def finish(state):
            for j in range(2):
                m, l, o = state[j]
                oT_ref[pl.ds(pl.multiple_of(off + j * HEAD_DIM, HEAD_DIM), HEAD_DIM), cols] = o * (1.0 / l)
                l_ref[0, j:j + 1, cols] = m + jnp.log2(l)

        init = tuple((jnp.full((1, TILE), -1e38, f32), jnp.zeros((1, TILE), f32), jnp.zeros((HEAD_DIM, TILE), f32)) for _ in range(2))

        longs = lax.div(need, LONG)
        state = lax.fori_loop(0, longs, block(start, LONG), init)
        finish(lax.fori_loop(0, lax.div(need - longs * LONG, SHORT), block(start + longs * LONG, SHORT), state))

    o_ref[...] = oT_ref[...].T.astype(bf16)


def attend(m, info, qT, k, vT, kaug, qaugT):
    win, nq = k.shape[1], qT.shape[2]
    qT, k, vT = stay(qT, k, vT)
    return pl.pallas_call(
        attend_kernel,
        out_shape=(jax.ShapeDtypeStruct((384, nq), f32), jax.ShapeDtypeStruct((nq, 384), bf16), jax.ShapeDtypeStruct((PAIRS, 8, nq), f32)),
        grid_spec=pltpu.PrefetchScalarGridSpec(
            num_scalar_prefetch=1, grid=(PAIRS,),
            in_specs=[
                pl.BlockSpec((None, 128, nq), lambda p, *_: (m, p // 2, 0)),
                pl.BlockSpec((None, win, 128), lambda p, *_: (m, 0, p // 2)),
                pl.BlockSpec((None, 128, win), lambda p, *_: (m, p // 2, 0)),
                pl.BlockSpec((win, 128), lambda p, *_: (0, 0)),
                pl.BlockSpec((128, nq), lambda p, *_: (0, 0)),
            ],
            out_specs=[
                pl.BlockSpec((128, nq), lambda p, *_: (p // 2, 0)),
                pl.BlockSpec((nq, 128), lambda p, *_: (0, p // 2)),
                pl.BlockSpec((1, 8, nq), lambda p, *_: (p, 0, 0)),
            ],
            scratch_shapes=[pltpu.VMEM((256, 2 * TILE), bf16)],
        ),
        compiler_params=pltpu.CompilerParams(vmem_limit_bytes=28 << 20),
        cost_estimate=pl.CostEstimate(flops=int(20 * 10**9 * 0.02), bytes_accessed=0, transcendentals=0),
        name="attend",
    )(info, qT, k, vT, kaug, qaugT)


def attend_back_kernel(info_ref, qT_ref, q_ref, k_ref, kT_ref, v_ref, doT_ref, do_ref, oT_ref, l_ref, kaug_ref, qaugT_ref,
                       dq_ref, dk_ref, dv_ref, dqT_ref, rhs_s, rhs_d, q_stk, do_stk, dk_acc, dv_acc):
    p_id = pl.program_id(0)
    off = pair_offset(info_ref)

    @pl.when(lax.rem(p_id, 2) == 0)
    def _():
        dqT_ref[...] = jnp.zeros_like(dqT_ref)
        dk_acc[...] = jnp.zeros_like(dk_acc)
        dv_acc[...] = jnp.zeros_like(dv_acc)

    for t in range(2):
        cols = slice(t * TILE, (t + 1) * TILE)
        masked_q = rows_masked(qT_ref[:, cols], off)
        masked_do = rows_masked(doT_ref[:, cols], off)
        lane_q = lanes_masked(q_ref[cols, :], off)
        lane_do = lanes_masked(do_ref[cols, :], off)
        for j in range(2):
            part = slice(j * TILE, (j + 1) * TILE)
            head = pl.ds(pl.multiple_of(off + j * HEAD_DIM, HEAD_DIM), HEAD_DIM)
            delta = jnp.sum(doT_ref[head, cols].astype(f32) * oT_ref[head, cols], axis=0, keepdims=True)
            total = l_ref[0, j:j + 1, cols] * (1.0 / C2)
            rowid = lax.broadcasted_iota(jnp.int32, (64, TILE), 0)
            lp, dp = split3(-total), split3(-delta)
            def pieces(parts):
                x = jnp.zeros((64, TILE), f32)
                for n in range(3):
                    x = jnp.where(rowid == n, parts[n].astype(f32), x)
                return x.astype(bf16)
            rhs_s[0:128, part] = masked_q[j]
            rhs_s[128:192, part] = qaugT_ref[0:64, cols]
            rhs_s[192:256, part] = pieces(lp)
            rhs_d[0:128, part] = masked_do[j]
            rhs_d[128:192, part] = jnp.zeros((64, TILE), bf16)
            rhs_d[192:256, part] = pieces(dp)
            q_stk[part, :] = lane_q[j]
            do_stk[part, :] = lane_do[j]
        start = info_ref[1 + t]
        need = info_ref[3 + t]

        def block(first, size):
            def step(i, carry):
                row = pl.multiple_of(first + i * size, 128)
                rows = pl.ds(row, size)
                aug = kaug_ref[rows, :]
                lhs_k = jnp.concatenate([k_ref[rows, :], aug], axis=1)
                lhs_v = jnp.concatenate([v_ref[rows, :], aug], axis=1)
                out, dv, dk = [], dv_acc[rows, :], dk_acc[rows, :]
                for j in range(2):
                    part = slice(j * TILE, (j + 1) * TILE)
                    s = jnp.dot(lhs_k, rhs_s[:, part], preferred_element_type=f32)
                    dp = jnp.dot(lhs_v, rhs_d[:, part], preferred_element_type=f32)
                    p = jnp.exp2(s * C2)
                    ds = (p * dp).astype(bf16)
                    dv = dv + jnp.dot(p.astype(bf16), do_stk[part, :], preferred_element_type=f32)
                    dk = dk + jnp.dot(ds, q_stk[part, :], preferred_element_type=f32)
                    kT = kT_ref[pl.ds(pl.multiple_of(off + j * HEAD_DIM, HEAD_DIM), HEAD_DIM), rows]
                    out.append(carry[j] + jnp.dot(kT, ds, preferred_element_type=f32))
                dv_acc[rows, :] = dv
                dk_acc[rows, :] = dk
                return tuple(out)
            return step

        def finish(dqs):
            for j in range(2):
                dqT_ref[pl.ds(pl.multiple_of(off + j * HEAD_DIM, HEAD_DIM), HEAD_DIM), cols] = dqs[j] * SCALE

        init = tuple(jnp.zeros((HEAD_DIM, TILE), f32) for _ in range(2))

        longs = lax.div(need, LONG)
        state = lax.fori_loop(0, longs, block(start, LONG), init)
        finish(lax.fori_loop(0, lax.div(need - longs * LONG, SHORT), block(start + longs * LONG, SHORT), state))
    @pl.when((lax.rem(p_id, 2) == 1) | (p_id == PAIRS - 1))
    def _():
        dq_ref[...] = dqT_ref[...].T.astype(bf16)
        dk_ref[...] = (dk_acc[...] * SCALE).astype(bf16)
        dv_ref[...] = dv_acc[...].astype(bf16)


def attend_back(m, info, qT, q, k, kT, v, doT, do, oT, lse, kaug, qaugT):
    win, nq = k.shape[1], qT.shape[2]
    qT, q, k, kT, v, doT, do = stay(qT, q, k, kT, v, doT, do)
    wide = pl.BlockSpec((128, nq), lambda p, *_: (p // 2, 0))
    tall = pl.BlockSpec((nq, 128), lambda p, *_: (0, p // 2))
    keys = pl.BlockSpec((win, 128), lambda p, *_: (0, p // 2))
    wide_m = pl.BlockSpec((None, 128, nq), lambda p, *_: (m, p // 2, 0))
    tall_m = pl.BlockSpec((None, nq, 128), lambda p, *_: (m, 0, p // 2))
    keys_m = pl.BlockSpec((None, win, 128), lambda p, *_: (m, 0, p // 2))
    return pl.pallas_call(
        attend_back_kernel,
        out_shape=(far(nq, 384), far(win, 384), far(win, 384)),
        grid_spec=pltpu.PrefetchScalarGridSpec(
            num_scalar_prefetch=1, grid=(PAIRS,),
            in_specs=[wide_m, tall_m, keys_m, pl.BlockSpec((None, 128, win), lambda p, *_: (m, p // 2, 0)), keys_m,
                      pl.BlockSpec((128, nq), lambda p, *_: (p // 2, m)), pl.BlockSpec((nq, 128), lambda p, *_: (m, p // 2)), wide,
                      pl.BlockSpec((1, 8, nq), lambda p, *_: (p, 0, 0)),
                      pl.BlockSpec((win, 128), lambda p, *_: (0, 0)), pl.BlockSpec((128, nq), lambda p, *_: (0, 0))],
            out_specs=[tall, keys, keys],
            scratch_shapes=[pltpu.VMEM((128, nq), f32), pltpu.VMEM((256, 2 * TILE), bf16), pltpu.VMEM((256, 2 * TILE), bf16),
                            pltpu.VMEM((2 * TILE, 128), bf16), pltpu.VMEM((2 * TILE, 128), bf16),
                            pltpu.VMEM((win, 128), f32), pltpu.VMEM((win, 128), f32)],
        ),
        compiler_params=pltpu.CompilerParams(vmem_limit_bytes=32 << 20),
        cost_estimate=pl.CostEstimate(flops=int(40 * 10**9 * 0.02), bytes_accessed=0, transcendentals=0),
        name="attend_back",
    )(info, qT, q, k, kT, v, doT, do, oT, lse, kaug, qaugT)


def moments(x):
    centred = x - jnp.mean(x, axis=-1, keepdims=True)
    r = lax.rsqrt(jnp.mean(centred * centred, axis=-1, keepdims=True) + EPSILON)
    return centred * r, r


def norm_back(grad, n, r, gain):
    e = grad * gain
    return r * (e - jnp.mean(e, axis=-1, keepdims=True) - n * jnp.mean(e * n, axis=-1, keepdims=True))


def call(kernel, out_shape, name, flops=10**9, limit=48, **spec):
    return pl.pallas_call(
        kernel, out_shape=out_shape, name=name,
        compiler_params=pltpu.CompilerParams(vmem_limit_bytes=limit << 20),
        cost_estimate=pl.CostEstimate(flops=int(flops * 0.02), bytes_accessed=0, transcendentals=0), **spec)


def shape(*dims, dtype=bf16):
    return jax.ShapeDtypeStruct(dims, dtype)


def far(*dims, dtype=bf16):
    return pltpu.MemorySpace.HBM(dims, dtype)


def stay(*arrays):
    return [pltpu.with_memory_space_constraint(a, pltpu.MemorySpace.HBM) for a in arrays]


def scalar_first(grid, in_specs, out_specs, scratch=()):
    return dict(grid_spec=pltpu.PrefetchScalarGridSpec(
        num_scalar_prefetch=1, grid=grid, in_specs=in_specs, out_specs=out_specs, scratch_shapes=list(scratch)))


def full(*dims):
    return pl.BlockSpec(dims, lambda *_: (0,) * len(dims))


def pack_heads_kernel(core_ref, qkv_ref, vec_ref, heads_ref):
    for part in range(3):
        near = pl.ds(pl.multiple_of(640 * part + 256 * core_ref[0], 128), 256)
        heads_ref[:, 384 * part:384 * part + 256] = qkv_ref[:, near]
        heads_ref[:, 384 * part + 256:384 * (part + 1)] = qkv_ref[:, 640 * part + 512:640 * (part + 1)]
    heads_ref[:, 1152:1280] = vec_ref[...]


def pack_heads(core, w_qkv, vectors):
    return call(pack_heads_kernel, shape(160, 1280), "pack_heads", 10**6, 8, **scalar_first(
        (1,), [full(160, 1920), full(160, 128)], full(160, 1280)))(core, w_qkv, vectors)


def turn_kernel(vec_ref, rows_ref):
    rows_ref[...] = vec_ref[...].astype(f32).T[:16]


def vector_rows(heads):
    return call(turn_kernel, shape(16, 640, dtype=f32), "vector_rows", 10**6, 8, grid=(1,),
                in_specs=[pl.BlockSpec((640, 128), lambda i: (0, 9))], out_specs=full(16, 640))(heads)


def pack_feed_kernel(core_ref, out_ref, up_ref, down_ref, feed_ref):
    core = core_ref[0]
    feed_ref[:, 5120:5760] = out_ref[...]
    for f in range(4):
        feed_ref[:, 640 * f:640 * (f + 1)] = up_ref[:, pl.ds(pl.multiple_of(1280 * f + 640 * core, 128), 640)]
        feed_ref[:, 2560 + 640 * f:2560 + 640 * (f + 1)] = down_ref[pl.ds(pl.multiple_of(640 * core + 160 * f, 32), 160), :]


def pack_feed(core, w_out, w_up, w_down):
    return call(pack_feed_kernel, far(160, 5760), "pack_feed", 10**6, 16, **scalar_first(
        (1,), [full(160, 640), full(160, 5120), full(1280, 640)], full(160, 5760)))(core, *stay(w_out, w_up, w_down))


def rows_in_order(core, mine, theirs, x_ref):
    mine, theirs = mine.astype(f32), theirs.astype(f32)
    x_ref[0:256, :] = jnp.where(core == 0, mine, theirs)
    x_ref[256:512, :] = jnp.where(core == 0, theirs, mine)


def window_rows(core, own_refs, other_refs, m, block, x_ref):
    for j in range(len(own_refs)):
        @pl.when(block == j)
        def _():
            rows_in_order(core, own_refs[j][m], other_refs[j][m], x_ref)


def project_kernel(chips, place_ref, *refs):
    n = len(chips)
    own_refs, other_refs = refs[:n], refs[n:2 * n]
    vec_ref, w_ref = refs[2 * n:2 * n + 2]
    k_ref, v_ref, kT_ref, vT_ref = refs[-6 - 2 * (n == 3):][:4]
    x_ref, hid_ref = refs[-2:]
    m, step = pl.program_id(0), pl.program_id(1)
    block = sum(jnp.where(step == i, chip, 0) for i, chip in enumerate(chips))
    needed = (block >= place_ref[1 + 2 * m]) & (block < place_ref[2 + 2 * m])

    @pl.when(jnp.logical_not(needed))
    def _():
        for ref in (k_ref, v_ref, kT_ref, vT_ref):
            ref[...] = jnp.zeros_like(ref)

    @pl.when(needed)
    def _():
        window_rows(place_ref[0], own_refs, other_refs, m, step, x_ref)
        hidden = (moments(x_ref[...])[0] * vec_ref[0:1, :] + vec_ref[1:2, :]).astype(bf16)
        hid_ref[...] = hidden
        kv = jnp.dot(hidden, w_ref[:, 384:], preferred_element_type=f32)
        low = kv.astype(bf16)
        k_ref[0] = low[:, :384]
        v_ref[0] = low[:, 384:]
        turned = kv.T.astype(bf16)
        kT_ref[0] = turned[:384]
        vT_ref[0] = turned[384:]

    if n == 3:
        q_ref, qT_ref = refs[-4:-2]

        @pl.when(step == 1)
        def _():
            q = jnp.dot(hid_ref[...], w_ref[:, :384], preferred_element_type=f32)
            q_ref[0] = q.astype(bf16)
            qT_ref[0] = q.T.astype(bf16)


def project(chips, place, own, other, vec, w, earlier=()):
    n = len(chips)
    chip = (lambda b: b + 1) if n == 3 else (lambda b: 4 * b)
    tall = pl.BlockSpec((1, 512, 384), lambda m, b, *_: (m, chip(b), 0))
    wide = pl.BlockSpec((1, 384, 512), lambda m, b, *_: (m, 0, chip(b)))
    shapes = [far(2, 2560, 384), far(2, 2560, 384), far(2, 384, 2560), far(2, 384, 2560)]
    specs = [tall, tall, wide, wide]
    if n == 3:
        shapes += [far(2, 512, 384), far(2, 384, 512)]
        specs += [pl.BlockSpec((1, 512, 384), lambda m, *_: (m, 0, 0)), pl.BlockSpec((1, 384, 512), lambda m, *_: (m, 0, 0))]
    own, other = [own[c] for c in chips], [other[c] for c in chips]
    return call(
        lambda *refs: project_kernel(chips, *refs), shapes, "project", 5 * 10**9, 28,
        input_output_aliases={2 * n + 3 + i: i for i in range(len(earlier))}, **scalar_first(
            (2, n), [full(2, 256, 640)] * (2 * n) + [full(16, 640), full(640, 1152)] + [pl.BlockSpec(memory_space=pl.ANY)] * len(earlier),
            specs, [pltpu.VMEM((512, 640), f32), pltpu.VMEM((512, 640), bf16)]))(place, *own, *other, vec, *stay(w), *earlier)


def heads_joined(core, mine, theirs):
    first, second = (jnp.where(core == 0, a, b) for a, b in ((mine, theirs), (theirs, mine)))
    return jnp.concatenate([first[:, :256], second[:, :256], first[:, 256:] + second[:, 256:]], axis=1)


def middle_kernel(core_ref, w_ref, low0_ref, low1_ref, theirs_ref, tok_ref, tok2_ref, vec_ref, mid_ref, hid_ref, hid2_ref):
    core = core_ref[0]
    for m, low_ref in enumerate((low0_ref, low1_ref)):
        attended = heads_joined(core, low_ref[...].astype(f32), theirs_ref[m].astype(f32)).astype(bf16)
        branch = jnp.dot(attended, w_ref[...], preferred_element_type=f32)
        mine = jnp.where(core == 0, branch[:256], branch[256:]) + tok_ref[m].astype(f32)
        theirs = jnp.where(core == 0, branch[256:], branch[:256]) + tok2_ref[m].astype(f32)
        part = slice(256 * m, 256 * (m + 1))
        mid_ref[part, :] = mine
        hid_ref[part, :] = (moments(mine)[0] * vec_ref[2:3, :] + vec_ref[3:4, :]).astype(bf16)
        hid2_ref[part, :] = (moments(theirs)[0] * vec_ref[2:3, :] + vec_ref[3:4, :]).astype(bf16)


W_OUT = pl.BlockSpec((640, 640), lambda *_: (0, 8))


def middle_step(core, weights, *args):
    return call(middle_kernel, (far(512, 640, dtype=f32), far(512, 640), far(512, 640)), "middle", 10**9, 20, **scalar_first(
        (1,), [W_OUT] + [full(*a.shape) for a in args], [full(512, 640)] * 3))(core, *stay(weights), *args)


def feed_kernel(h_ref, h2_ref, cot_ref, cot2_ref, up_ref, down_ref, mine_ref, theirs_ref, g_ref, h, cot, hT, cT, out, dh):
    chunk = pl.program_id(0)

    @pl.when(chunk == 0)
    def _():
        h[0:512, :], h[512:1024, :] = h_ref[...], h2_ref[...]
        cot[0:512, :], cot[512:1024, :] = cot_ref[...], cot2_ref[...]
        hT[...] = h[...].astype(f32).T.astype(bf16)
        cT[...] = cot[...].astype(f32).T.astype(bf16)
        out[...] = jnp.zeros_like(out)
        dh[...] = jnp.zeros_like(dh)

    up_w = up_ref[...]
    down_w = jnp.concatenate([down_ref[160 * y:160 * (y + 1), 640 * i:640 * (i + 1)] for y in range(2) for i in range(4)], axis=0)
    acts, d_ups = [], []
    for t in range(4):
        rows = slice(256 * t, 256 * (t + 1))
        u = jnp.dot(h[rows, :], up_w, preferred_element_type=f32)
        d_act = lax.dot_general(cot[rows, :], down_w, NT, preferred_element_type=f32)
        cdf = 0.5 * (1.0 + lax.erf(u * (2.0 ** -0.5)))
        pdf = jnp.exp(u * u * -0.5) * ((2.0 * math.pi) ** -0.5)
        act = (u * cdf).astype(bf16)
        d_up = (d_act * (cdf + u * pdf)).astype(bf16)
        out[rows, :] += jnp.dot(act, down_w, preferred_element_type=f32)
        dh[rows, :] += lax.dot_general(d_up, up_w, NT, preferred_element_type=f32)
        acts.append(act)
        d_ups.append(d_up)
    g_up = jnp.dot(hT[...], jnp.concatenate(d_ups, axis=0), preferred_element_type=f32).astype(bf16)
    g_down = jnp.dot(cT[...], jnp.concatenate(acts, axis=0), preferred_element_type=f32).T.astype(bf16)
    for f in range(2):
        for y in range(4):
            for i in range(2):
                g_ref[4 * chunk + 2 * f + i, y] = g_up[160 * y + 80 * i:160 * y + 80 * (i + 1), 640 * f:640 * (f + 1)]
        for i in range(8):
            g_ref[8 + i, 2 * chunk + f] = g_down[640 * f + 80 * i:640 * f + 80 * (i + 1)]

    @pl.when(chunk == 1)
    def _():
        mine_ref[0], mine_ref[1] = out[0:512, :].astype(bf16), dh[0:512, :].astype(bf16)
        theirs_ref[0], theirs_ref[1] = out[512:1024, :].astype(bf16), dh[512:1024, :].astype(bf16)


def feed_forward(h, h2, cot, cot2, weights):
    return call(
        feed_kernel,
        (far(2, 512, 640), far(2, 512, 640), far(16, 4, 80, 640)),
        "feed_forward", 30 * 10**9, 52, grid=(2,),
        in_specs=[full(512, 640)] * 4 + [pl.BlockSpec((640, 1280), lambda f: (0, f)), pl.BlockSpec((320, 2560), lambda f: (f, 1))],
        out_specs=[full(2, 512, 640), full(2, 512, 640), full(16, 4, 80, 640)],
        scratch_shapes=[pltpu.VMEM((1024, 640), bf16), pltpu.VMEM((1024, 640), bf16), pltpu.VMEM((640, 1024), bf16), pltpu.VMEM((640, 1024), bf16),
                        pltpu.VMEM((1024, 640), f32), pltpu.VMEM((1024, 640), f32)],
    )(*stay(h, h2, cot), cot2, *stay(weights, weights))


def after_kernel(mid_ref, mine_ref, theirs_ref, cot_ref, vec_ref, block_ref, grad_ref, branch_ref, g_ref):
    @pl.when(pl.program_id(0) == 0)
    def _():
        g_ref[...] = jnp.zeros_like(g_ref)

    middle = mid_ref[...]
    block_ref[...] = (middle + mine_ref[0].astype(f32) + theirs_ref[0].astype(f32)).astype(bf16)
    d_hidden = mine_ref[1].astype(f32) + theirs_ref[1].astype(f32)
    n, r = moments(middle)
    g_ref[0:1, :] += jnp.sum(d_hidden * n, axis=0, keepdims=True)
    g_ref[1:2, :] += jnp.sum(d_hidden, axis=0, keepdims=True)
    grad = cot_ref[...].astype(f32) + norm_back(d_hidden, n, r, vec_ref[2:3, :])
    grad_ref[...] = grad
    branch_ref[...] = grad.astype(bf16)


def after_feed(*args):
    rows, pair = pl.BlockSpec((128, 640), lambda i: (i, 0)), pl.BlockSpec((2, 128, 640), lambda i: (0, i, 0))
    return call(
        after_kernel, (far(512, 640), far(512, 640, dtype=f32), shape(512, 640), shape(8, 640, dtype=f32)), "after_feed", 10**9, 16,
        grid=(4,), in_specs=[rows, pair, pair, rows, full(16, 640)], out_specs=[rows, rows, rows, full(8, 640)])(*stay(args[0], args[1]), args[2], *stay(args[3]), args[4])


def branch_kernel(core_ref, own_ref, their_ref, w_ref, low0_ref, low1_ref, theirs_ref, do_ref, doT_ref, g_ref):
    core = core_ref[0]
    w = jnp.concatenate([w_ref[pl.ds(pl.multiple_of(256 * core, 256), 256), :], w_ref[512:640, :]], axis=0)
    g = jnp.zeros((640, 384), f32)
    for m in range(2):
        part = slice(256 * m, 256 * (m + 1))
        mine, theirs = own_ref[part, :].astype(f32), their_ref[part, :].astype(f32)
        branch = jnp.concatenate([jnp.where(core == 0, mine, theirs), jnp.where(core == 0, theirs, mine)], axis=0)
        kept = jnp.where(core == 0, branch[:, :384], branch[:, 256:]).astype(bf16)
        branch = branch.astype(bf16)
        rows = slice(512 * m, 512 * (m + 1))
        do = lax.dot_general(branch, w, NT, preferred_element_type=f32)
        do_ref[rows, :] = do.astype(bf16)
        doT_ref[:, rows] = do.T.astype(bf16)
        attended = heads_joined(core, (low0_ref, low1_ref)[m][...].astype(f32), theirs_ref[m].astype(f32))
        g = g + jnp.dot(attended.T.astype(bf16), kept, preferred_element_type=f32)
    g_ref[...] = g


def branch_step(core, own, their, weights, *args):
    return call(
        branch_kernel, (far(1024, 384), far(384, 1024), far(640, 384, dtype=f32)), "branch", 10**9, 24, **scalar_first(
            (1,), [full(512, 640)] * 2 + [W_OUT] + [full(*a.shape) for a in args], [full(1024, 384), full(384, 1024), full(640, 384)]))(
                core, own, their, *stay(weights), *args)


def project_back_kernel(core_ref, *refs):
    own_refs, other_refs = refs[:5], refs[5:10]
    (vec_ref, w_ref, dq0_ref, dq1_ref, dk0_ref, dk1_ref, dv0_ref, dv1_ref, g_out_ref, g_two_ref,
     mine_ref, theirs_ref, tail_ref, x_ref, d_kv, d_q, d_hid, g_ref, g_vec) = refs[10:]
    step, core = pl.program_id(0), core_ref[0]
    block = lax.rem(step, 5)

    @pl.when(step == 0)
    def _():
        g_ref[...] = jnp.zeros_like(g_ref)
        g_vec[...] = jnp.zeros_like(g_vec)
        g_vec[2:4, :] = g_two_ref[0:2, :]

    second = lax.div(step, 5)
    needed = (block >= core_ref[1 + 2 * second]) & (block < core_ref[2 + 2 * second])

    @pl.when(jnp.logical_not(needed))
    def _():
        mine_ref[...] = jnp.zeros_like(mine_ref)
        theirs_ref[...] = jnp.zeros_like(theirs_ref)

    for m, (dq, dk, dv) in enumerate(((dq0_ref, dk0_ref, dv0_ref), (dq1_ref, dk1_ref, dv1_ref))):
        @pl.when(needed & (second == m))
        def _():
            window_rows(core, own_refs, other_refs, m, block, x_ref)
            d_kv[:, :384], d_kv[:, 384:] = dk[...], dv[...]
            d_q[...] = dq[...]

    @pl.when(needed)
    def _():
        n = moments(x_ref[...])[0]
        hiddenT = (n * vec_ref[0:1, :] + vec_ref[1:2, :]).T.astype(bf16)
        d_hid[...] = lax.dot_general(d_kv[...], w_ref[:, 384:], NT, preferred_element_type=f32)
        g_ref[:, 384:] += jnp.dot(hiddenT, d_kv[...], preferred_element_type=f32)

        @pl.when(block == 2)
        def _():
            g_ref[:, :384] += jnp.dot(hiddenT, d_q[...], preferred_element_type=f32)
            d_hid[...] += lax.dot_general(d_q[...], w_ref[:, :384], NT, preferred_element_type=f32)

        dh = d_hid[...]
        mine_ref[0, 0] = jnp.where(core == 0, dh[:256], dh[256:]).astype(bf16)
        theirs_ref[0, 0] = jnp.where(core == 0, dh[256:], dh[:256]).astype(bf16)
        g_vec[0:1, :] += jnp.sum(dh * n, axis=0, keepdims=True)
        g_vec[1:2, :] += jnp.sum(dh, axis=0, keepdims=True)

    @pl.when(step == 9)
    def _():
        turned = g_vec[...].T
        lane = lax.broadcasted_iota(jnp.int32, (640, 128), 1) - 64 * (1 - core)
        spare = g_ref[:, 256:384]
        for i in range(4):
            spare = jnp.where(lane == i, turned[:, i:i + 1], spare)
        g_ref[:, 256:384] = spare
        for y in range(4):
            for z in range(4):
                rows = slice(160 * y + 40 * z, 160 * y + 40 * (z + 1))
                for x in range(3):
                    tail_ref[16 * y + 4 * z + x] = g_ref[rows, 384 * x:384 * (x + 1)].astype(bf16)
                tail_ref[16 * y + 4 * z + 3] = g_out_ref[rows, :].astype(bf16)


def project_back(core, own, other, vec, w, dq, dk, dv, g_out, g_two):
    dq, dk, dv, (g_out,) = stay(*dq), stay(*dk), stay(*dv), stay(g_out)
    first = pl.BlockSpec((512, 384), lambda b, *_: (jnp.minimum(b, 4), 0))
    second = pl.BlockSpec((512, 384), lambda b, *_: (jnp.maximum(b - 5, 0), 0))
    return call(
        project_back_kernel, (shape(5, 2, 256, 640), shape(5, 2, 256, 640), shape(64, 40, 384)), "project_back", 10**10, 36, **scalar_first(
            (10,), [full(2, 256, 640)] * 10 + [full(16, 640), full(640, 1152), full(512, 384), full(512, 384), first, second, first, second,
                                               full(640, 384), full(8, 640)],
            [pl.BlockSpec((1, 1, 256, 640), lambda b, *_: (lax.rem(b, 5), b // 5, 0, 0))] * 2 + [full(64, 40, 384)],
            [pltpu.VMEM((512, 640), f32), pltpu.VMEM((512, 768), bf16), pltpu.VMEM((512, 384), bf16),
             pltpu.VMEM((512, 640), f32), pltpu.VMEM((640, 1152), f32), pltpu.VMEM((8, 640), f32)]))(core, *own, *other, vec, *stay(w), *dq, *dk, *dv, g_out, g_two)


def in_core_order(core_ref, mine, theirs):
    core, mine, theirs = core_ref[0], mine.astype(f32), theirs.astype(f32)
    return jnp.where(core == 0, mine, theirs), jnp.where(core == 0, theirs, mine)


def final_feed_kernel(core_ref, mine_ref, theirs_ref, up_ref, down_ref):
    for i in range(16):
        for c, piece in enumerate(in_core_order(core_ref, mine_ref[i], theirs_ref[i])):
            if i < 8:
                base = 1280 * (i // 2) + 640 * c
                up_ref[80 * (i % 2):80 * (i % 2 + 1), base:base + 640] = piece
            else:
                base = 640 * c + 80 * (i - 8)
                down_ref[base:base + 80, :] = piece


def final_feed(core, mine, theirs):
    return call(final_feed_kernel, (shape(160, 5120, dtype=f32), shape(1280, 640, dtype=f32)), "final_feed", 10**6, 32, **scalar_first(
        (1,), [full(16, 80, 640)] * 2, [full(160, 5120), full(1280, 640)]))(core, mine, theirs)


def final_heads_kernel(core_ref, mine_ref, theirs_ref, qkv_ref, out_ref, vec_ref):
    lane = lax.broadcasted_iota(jnp.int32, (40, 128), 1)
    for z in range(4):
        rows = slice(40 * z, 40 * (z + 1))
        for x in range(4):
            a, b = in_core_order(core_ref, mine_ref[4 * z + x], theirs_ref[4 * z + x])
            if x < 3:
                last = jnp.where(lane < 64, a[:, 256:], b[:, 256:])
                qkv_ref[rows, 640 * x:640 * (x + 1)] = jnp.concatenate([a[:, :256], b[:, :256], last], axis=1)
            else:
                out_ref[rows, :] = jnp.concatenate([a, b[:, 128:]], axis=1)
            if x == 0:
                vec_ref[rows, :] = pltpu.roll(a[:, 256:], 64, 1) + b[:, 256:]


def final_heads(core, mine, theirs):
    return call(
        final_heads_kernel, (shape(160, 1920, dtype=f32), shape(160, 640, dtype=f32), shape(160, 128, dtype=f32)), "final_heads", 10**6, 16,
        **scalar_first((1,), [full(16, 40, 384)] * 2, [full(160, 1920), full(160, 640), full(160, 128)]))(core, mine, theirs)


def shifted(array, axis, by):
    devices = lax.axis_size(axis)
    return lax.ppermute(array, axis, [(i, (i + by) % devices) for i in range(devices)])


def passed_along(array, by):
    devices = lax.axis_size(("z", "x"))
    return lax.ppermute(array, ("z", "x"), [(i, i + by) for i in range(devices) if 0 <= i + by < devices])


def swapped(array):
    return lax.ppermute(array, "core", [(0, 1), (1, 0)])


def pick(array, index):
    return lax.dynamic_index_in_dim(array, index, 0, keepdims=False)


def gathered(array, axis):
    me, devices = lax.axis_index(axis), lax.axis_size(axis)
    out = jnp.zeros((devices,) + array.shape, array.dtype)
    out = lax.dynamic_update_index_in_dim(out, array, me, 0)
    for by in (1, devices - 1, 2):
        out = lax.dynamic_update_index_in_dim(out, shifted(array, axis, by), (me + devices - by) % devices, 0)
    return out


def window_info(length_row, chip, core, win):
    ends = jnp.cumsum(length_row)
    starts = ends - length_row
    base = chip * 512 - 1024
    places = base + jnp.arange(win, dtype=jnp.int32)
    inside = (places[:, None] >= starts[None, :]) & (places[:, None] < ends[None, :])
    ones = jnp.broadcast_to(jnp.arange(64) < 3, (win, 64)).astype(bf16)
    key_rows = jnp.concatenate([jnp.where(inside, 0.0, -BIG).astype(bf16), ones], axis=1)
    own = chip * 512 + jnp.arange(512, dtype=jnp.int32)
    inside_q = (own[None, :] >= starts[:, None]) & (own[None, :] < ends[:, None])
    query_rows = jnp.concatenate([inside_q.astype(bf16), jnp.zeros((64, 512), bf16)], axis=0)
    info = [core]
    sizes = []
    for t in range(2):
        first = chip * 512 + t * TILE
        low = jnp.max(jnp.where(starts <= first, starts, 0)) - base
        high = jnp.min(jnp.where(ends > first + TILE - 1, ends, 1 << 30)) - base
        start = low // 128 * 128
        need = high - start
        size = (need + SHORT - 1) // SHORT * SHORT
        info.append(jnp.minimum(start, win - size))
        sizes.append(size)
    low = jnp.minimum(info[1], info[2]) // 512
    high = (jnp.maximum(info[1] + sizes[0], info[2] + sizes[1]) + 511) // 512
    return jnp.stack(info + sizes).astype(jnp.int32), key_rows, query_rows, [low, high]


def body(tokens, lengths, gain_one, bias_one, w_qkv, w_out, gain_two, bias_two, w_up, w_down, cotangent):
    core, chip = lax.axis_index("core"), lax.axis_index(("z", "x"))
    core_arg = core[None].astype(jnp.int32)
    tok, cot = tokens[:, 0], cotangent[:, 0].reshape(512, 640)
    together = lambda *arrays: lax.optimization_barrier(arrays)

    vectors = jnp.pad(jnp.stack([gain_one, bias_one, gain_two, bias_two], axis=1), ((0, 0), (0, 124)))
    before, after, tok_other = passed_along(tok, 1), passed_along(tok, -1), swapped(tok)
    heads = lax.all_gather(pack_heads(core_arg, w_qkv, vectors), "batch", axis=0, tiled=True)
    windows = [window_info(lengths[m, 0], chip, core, 2560) for m in range(2)]
    place = jnp.stack([core] + windows[0][3] + windows[1][3]).astype(jnp.int32)
    feed_pack = pack_feed(core_arg, w_out, w_up, w_down)
    before, after, tok_other, feed_pack, place, windows = together(before, after, tok_other, feed_pack, place, windows)
    own = [passed_along(before, 1), before, tok, after, passed_along(after, -1)]
    other = [None, swapped(before), tok_other, swapped(after), None]
    heads, feed_pack = together(heads, feed_pack)
    feed_weights = lax.all_gather(feed_pack, "batch", axis=0, tiled=True)
    vec = vector_rows(heads)
    *near_parts, q, qT = project((1, 2, 3), place, own, other, vec, heads)
    own[0], own[4], near_parts = together(own[0], own[4], near_parts)
    other[0], other[4] = swapped(own[0]), swapped(own[4])
    k, v, kT, vT = project((0, 4), place, own, other, vec, heads, near_parts)
    (oT0, low0, lse0), (oT1, low1, lse1) = (
        attend(m, info, qT, k, vT, key_rows, query_rows) for m, (info, key_rows, query_rows, _) in enumerate(windows))

    theirs = swapped(jnp.stack([low0, low1]))
    middle, hidden_two, hidden_other = middle_step(core_arg, feed_weights, low0, low1, theirs, tok, tok_other, vec)
    mine, partial, feed_grads = feed_forward(hidden_two, hidden_other, cot, swapped(cot), feed_weights)
    feed_grads = lax.psum_scatter(feed_grads.reshape(5120, 640), ("z", "x"), scatter_dimension=0, tiled=True)
    block_out, grad_middle, branch, g_two = after_feed(middle, mine, swapped(partial), cot, vec)

    do, doT, g_out = branch_step(core_arg, branch, swapped(branch), feed_weights, low0, low1, theirs)
    dq, dk, dv = zip(*(
        attend_back(m, info, qT, q, k, kT, v, doT, do, oT, lse, key_rows, query_rows)
        for m, ((info, key_rows, query_rows, _), oT, lse) in enumerate(zip(windows, (oT0, oT1), (lse0, lse1)))))
    dq, feed_grads = together(dq, feed_grads)
    feed = lax.psum_scatter(feed_grads, "batch", scatter_dimension=0, tiled=True).reshape(80, 640)
    mine, theirs, tail = project_back(place, own, other, vec, heads, dq, dk, dv, g_out, g_two)

    feed, mine, theirs, tail = together(feed, mine, theirs, tail)

    tail = lax.all_to_all(tail, ("batch", "z", "x"), 0, 0, tiled=True)
    feed = lax.all_gather(feed, ("z", "x"), axis=0, tiled=True).reshape(16, 80, 640)
    theirs = swapped(theirs)
    sums = [mine[j].astype(f32) + theirs[j].astype(f32) for j in range(5)]
    right, left = passed_along(sums[4].astype(bf16), 1), passed_along(sums[0].astype(bf16), -1)
    tail, right, left = together(tail, right, left)
    right = passed_along((right.astype(f32) + sums[3]).astype(bf16), 1)
    left = passed_along((left.astype(f32) + sums[1]).astype(bf16), -1)
    tail = gathered(jnp.sum(tail.astype(f32), axis=0).astype(bf16), "x").reshape(160, 384)
    tail, right, left = together(tail, right, left)
    tail = gathered(tail, "z").reshape(16, 40, 384)
    d_one = (sums[2] + right.astype(f32) + left.astype(f32)).reshape(512, 640)
    n_one, r_one = moments(tok.reshape(512, 640).astype(f32))
    grad_tokens = (grad_middle + norm_back(d_one, n_one, r_one, vec[0:1])).astype(bf16)
    tail, grad_tokens, feed = together(tail, grad_tokens, feed)
    grad_qkv, grad_out, spare = final_heads(core_arg, tail, swapped(tail))
    grad_up, grad_down = final_feed(core_arg, feed, swapped(feed))
    return (
        block_out.reshape(2, 1, 256, 640), grad_tokens.reshape(2, 1, 256, 640), spare[:, 0], spare[:, 1], grad_qkv, grad_out,
        spare[:, 2], spare[:, 3], grad_up, grad_down)


def solution(mesh):
    fine = Mesh(mesh.devices.reshape(4, 4, 4, 2), ("batch", "z", "x", "core"))
    rows = P(None, "batch", ("z", "x", "core"), None)
    one, two = P("batch"), P("batch", None)
    return jax.shard_map(
        body,
        mesh=fine,
        in_specs=(rows, P(None, "batch", None), one, one, two, two, one, one, two, two, rows),
        out_specs=(rows, rows, one, one, two, two, one, one, two, two),
        check_vma=False,
    )
```

```python
import math

import jax
import jax.numpy as jnp
from jax import lax
from jax.experimental import pallas as pl
from jax.experimental.pallas import tpu as pltpu
from jax.sharding import Mesh
from jax.sharding import PartitionSpec as P

HEAD_DIM = 32
SCALE = HEAD_DIM ** -0.5
LOG2E = math.log2(math.e)
C2 = SCALE * LOG2E
BIG = 1e30
TILE = 256
EPSILON = 1e-05
PAIRS = 5
SHORT, LONG = 384, 1152
f32, bf16 = jnp.float32, jnp.bfloat16
NT = (((1,), (1,)), ((), ()))


def pair_offset(info_ref):
    p = pl.program_id(0)
    sub = jnp.where(p == PAIRS - 1, info_ref[0], lax.rem(p, 2))
    return sub * (2 * HEAD_DIM)


def split3(v):
    a = v.astype(bf16)
    r = v - a.astype(f32)
    b = r.astype(bf16)
    d = (r - b.astype(f32)).astype(bf16)
    return a, b, d


def rows_masked(xT, off):
    row = lax.broadcasted_iota(jnp.int32, xT.shape, 0) - off
    xf = xT.astype(f32)
    return [jnp.where((row >= HEAD_DIM * j) & (row < HEAD_DIM * (j + 1)), xf, 0.0).astype(bf16) for j in range(2)]


def lanes_masked(x, off):
    lane = lax.broadcasted_iota(jnp.int32, x.shape, 1) - off
    xf = x.astype(f32)
    return [jnp.where((lane >= HEAD_DIM * j) & (lane < HEAD_DIM * (j + 1)), xf, 0.0).astype(bf16) for j in range(2)]


def attend_kernel(info_ref, qT_ref, k_ref, vT_ref, kaug_ref, qaugT_ref, oT_ref, o_ref, l_ref, rhs):
    off = pair_offset(info_ref)
    oT_ref[...] = jnp.where(lax.rem(pl.program_id(0), 2) == 0, 0.0, oT_ref[...])
    for t in range(2):
        cols = slice(t * TILE, (t + 1) * TILE)
        masked = rows_masked(qT_ref[:, cols], off)
        for j in range(2):
            rhs[0:128, j * TILE:(j + 1) * TILE] = masked[j]
            rhs[128:256, j * TILE:(j + 1) * TILE] = qaugT_ref[:, cols]
        start = info_ref[1 + t]
        need = info_ref[3 + t]

        def block(first, size):
            def step(i, carry):
                row = pl.multiple_of(first + i * size, 128)
                lhs = jnp.concatenate([k_ref[pl.ds(row, size), :], kaug_ref[pl.ds(row, size), :]], axis=1)
                raw = [jnp.dot(lhs, rhs[:, j * TILE:(j + 1) * TILE], preferred_element_type=f32) for j in range(2)]
                out = []
                for j in range(2):
                    m, l, o = carry[j]
                    s = raw[j] * C2
                    m_new = jnp.maximum(m, jnp.max(s, axis=0, keepdims=True))
                    alpha = jnp.exp2(m - m_new)
                    p = jnp.exp2(s - m_new)
                    vT = vT_ref[pl.ds(pl.multiple_of(off + j * HEAD_DIM, HEAD_DIM), HEAD_DIM), pl.ds(row, size)]
                    out.append((m_new, l * alpha + jnp.sum(p, axis=0, keepdims=True),
                                o * alpha + jnp.dot(vT, p.astype(bf16), preferred_element_type=f32)))
                return tuple(out)
            return step

        def finish(state):
            for j in range(2):
                m, l, o = state[j]
                oT_ref[pl.ds(pl.multiple_of(off + j * HEAD_DIM, HEAD_DIM), HEAD_DIM), cols] = o * (1.0 / l)
                l_ref[0, j:j + 1, cols] = m + jnp.log2(l)

        init = tuple((jnp.full((1, TILE), -1e38, f32), jnp.zeros((1, TILE), f32), jnp.zeros((HEAD_DIM, TILE), f32)) for _ in range(2))

        longs = lax.div(need, LONG)
        state = lax.fori_loop(0, longs, block(start, LONG), init)
        finish(lax.fori_loop(0, lax.div(need - longs * LONG, SHORT), block(start + longs * LONG, SHORT), state))

    o_ref[...] = oT_ref[...].T.astype(bf16)


def attend(m, info, qT, k, vT, kaug, qaugT):
    win, nq = k.shape[1], qT.shape[2]
    qT, k, vT = stay(qT, k, vT)
    return pl.pallas_call(
        attend_kernel,
        out_shape=(jax.ShapeDtypeStruct((384, nq), f32), jax.ShapeDtypeStruct((nq, 384), bf16), jax.ShapeDtypeStruct((PAIRS, 8, nq), f32)),
        grid_spec=pltpu.PrefetchScalarGridSpec(
            num_scalar_prefetch=1, grid=(PAIRS,),
            in_specs=[
                pl.BlockSpec((None, 128, nq), lambda p, *_: (m, p // 2, 0)),
                pl.BlockSpec((None, win, 128), lambda p, *_: (m, 0, p // 2)),
                pl.BlockSpec((None, 128, win), lambda p, *_: (m, p // 2, 0)),
                pl.BlockSpec((win, 128), lambda p, *_: (0, 0)),
                pl.BlockSpec((128, nq), lambda p, *_: (0, 0)),
            ],
            out_specs=[
                pl.BlockSpec((128, nq), lambda p, *_: (p // 2, 0)),
                pl.BlockSpec((nq, 128), lambda p, *_: (0, p // 2)),
                pl.BlockSpec((1, 8, nq), lambda p, *_: (p, 0, 0)),
            ],
            scratch_shapes=[pltpu.VMEM((256, 2 * TILE), bf16)],
        ),
        compiler_params=pltpu.CompilerParams(vmem_limit_bytes=28 << 20),
        cost_estimate=pl.CostEstimate(flops=int(20 * 10**9 * 0.02), bytes_accessed=0, transcendentals=0),
        name="attend",
    )(info, qT, k, vT, kaug, qaugT)


def attend_back_kernel(info_ref, qT_ref, q_ref, k_ref, kT_ref, v_ref, doT_ref, do_ref, oT_ref, l_ref, kaug_ref, qaugT_ref,
                       dq_ref, dk_ref, dv_ref, dqT_ref, rhs_s, rhs_d, q_stk, do_stk, dk_acc, dv_acc):
    p_id = pl.program_id(0)
    off = pair_offset(info_ref)

    @pl.when(lax.rem(p_id, 2) == 0)
    def _():
        dqT_ref[...] = jnp.zeros_like(dqT_ref)
        dk_acc[...] = jnp.zeros_like(dk_acc)
        dv_acc[...] = jnp.zeros_like(dv_acc)

    for t in range(2):
        cols = slice(t * TILE, (t + 1) * TILE)
        masked_q = rows_masked(qT_ref[:, cols], off)
        masked_do = rows_masked(doT_ref[:, cols], off)
        lane_q = lanes_masked(q_ref[cols, :], off)
        lane_do = lanes_masked(do_ref[cols, :], off)
        for j in range(2):
            part = slice(j * TILE, (j + 1) * TILE)
            head = pl.ds(pl.multiple_of(off + j * HEAD_DIM, HEAD_DIM), HEAD_DIM)
            delta = jnp.sum(doT_ref[head, cols].astype(f32) * oT_ref[head, cols], axis=0, keepdims=True)
            total = l_ref[0, j:j + 1, cols] * (1.0 / C2)
            rowid = lax.broadcasted_iota(jnp.int32, (64, TILE), 0)
            lp, dp = split3(-total), split3(-delta)
            def pieces(parts):
                x = jnp.zeros((64, TILE), f32)
                for n in range(3):
                    x = jnp.where(rowid == n, parts[n].astype(f32), x)
                return x.astype(bf16)
            rhs_s[0:128, part] = masked_q[j]
            rhs_s[128:192, part] = qaugT_ref[0:64, cols]
            rhs_s[192:256, part] = pieces(lp)
            rhs_d[0:128, part] = masked_do[j]
            rhs_d[128:192, part] = jnp.zeros((64, TILE), bf16)
            rhs_d[192:256, part] = pieces(dp)
            q_stk[part, :] = lane_q[j]
            do_stk[part, :] = lane_do[j]
        start = info_ref[1 + t]
        need = info_ref[3 + t]

        def block(first, size):
            def step(i, carry):
                row = pl.multiple_of(first + i * size, 128)
                rows = pl.ds(row, size)
                aug = kaug_ref[rows, :]
                lhs_k = jnp.concatenate([k_ref[rows, :], aug], axis=1)
                lhs_v = jnp.concatenate([v_ref[rows, :], aug], axis=1)
                out, dv, dk = [], dv_acc[rows, :], dk_acc[rows, :]
                for j in range(2):
                    part = slice(j * TILE, (j + 1) * TILE)
                    s = jnp.dot(lhs_k, rhs_s[:, part], preferred_element_type=f32)
                    dp = jnp.dot(lhs_v, rhs_d[:, part], preferred_element_type=f32)
                    p = jnp.exp2(s * C2)
                    ds = (p * dp).astype(bf16)
                    dv = dv + jnp.dot(p.astype(bf16), do_stk[part, :], preferred_element_type=f32)
                    dk = dk + jnp.dot(ds, q_stk[part, :], preferred_element_type=f32)
                    kT = kT_ref[pl.ds(pl.multiple_of(off + j * HEAD_DIM, HEAD_DIM), HEAD_DIM), rows]
                    out.append(carry[j] + jnp.dot(kT, ds, preferred_element_type=f32))
                dv_acc[rows, :] = dv
                dk_acc[rows, :] = dk
                return tuple(out)
            return step

        def finish(dqs):
            for j in range(2):
                dqT_ref[pl.ds(pl.multiple_of(off + j * HEAD_DIM, HEAD_DIM), HEAD_DIM), cols] = dqs[j] * SCALE

        init = tuple(jnp.zeros((HEAD_DIM, TILE), f32) for _ in range(2))

        longs = lax.div(need, LONG)
        state = lax.fori_loop(0, longs, block(start, LONG), init)
        finish(lax.fori_loop(0, lax.div(need - longs * LONG, SHORT), block(start + longs * LONG, SHORT), state))
    @pl.when((lax.rem(p_id, 2) == 1) | (p_id == PAIRS - 1))
    def _():
        dq_ref[...] = dqT_ref[...].T.astype(bf16)
        dk_ref[...] = (dk_acc[...] * SCALE).astype(bf16)
        dv_ref[...] = dv_acc[...].astype(bf16)


def attend_back(m, info, qT, q, k, kT, v, doT, do, oT, lse, kaug, qaugT):
    win, nq = k.shape[1], qT.shape[2]
    qT, q, k, kT, v, doT, do = stay(qT, q, k, kT, v, doT, do)
    wide = pl.BlockSpec((128, nq), lambda p, *_: (p // 2, 0))
    tall = pl.BlockSpec((nq, 128), lambda p, *_: (0, p // 2))
    keys = pl.BlockSpec((win, 128), lambda p, *_: (0, p // 2))
    wide_m = pl.BlockSpec((None, 128, nq), lambda p, *_: (m, p // 2, 0))
    tall_m = pl.BlockSpec((None, nq, 128), lambda p, *_: (m, 0, p // 2))
    keys_m = pl.BlockSpec((None, win, 128), lambda p, *_: (m, 0, p // 2))
    return pl.pallas_call(
        attend_back_kernel,
        out_shape=(far(nq, 384), far(win, 384), far(win, 384)),
        grid_spec=pltpu.PrefetchScalarGridSpec(
            num_scalar_prefetch=1, grid=(PAIRS,),
            in_specs=[wide_m, tall_m, keys_m, pl.BlockSpec((None, 128, win), lambda p, *_: (m, p // 2, 0)), keys_m,
                      pl.BlockSpec((128, nq), lambda p, *_: (p // 2, m)), pl.BlockSpec((nq, 128), lambda p, *_: (m, p // 2)), wide,
                      pl.BlockSpec((1, 8, nq), lambda p, *_: (p, 0, 0)),
                      pl.BlockSpec((win, 128), lambda p, *_: (0, 0)), pl.BlockSpec((128, nq), lambda p, *_: (0, 0))],
            out_specs=[tall, keys, keys],
            scratch_shapes=[pltpu.VMEM((128, nq), f32), pltpu.VMEM((256, 2 * TILE), bf16), pltpu.VMEM((256, 2 * TILE), bf16),
                            pltpu.VMEM((2 * TILE, 128), bf16), pltpu.VMEM((2 * TILE, 128), bf16),
                            pltpu.VMEM((win, 128), f32), pltpu.VMEM((win, 128), f32)],
        ),
        compiler_params=pltpu.CompilerParams(vmem_limit_bytes=32 << 20),
        cost_estimate=pl.CostEstimate(flops=int(40 * 10**9 * 0.02), bytes_accessed=0, transcendentals=0),
        name="attend_back",
    )(info, qT, q, k, kT, v, doT, do, oT, lse, kaug, qaugT)


def moments(x):
    centred = x - jnp.mean(x, axis=-1, keepdims=True)
    r = lax.rsqrt(jnp.mean(centred * centred, axis=-1, keepdims=True) + EPSILON)
    return centred * r, r


def norm_back(grad, n, r, gain):
    e = grad * gain
    return r * (e - jnp.mean(e, axis=-1, keepdims=True) - n * jnp.mean(e * n, axis=-1, keepdims=True))


def call(kernel, out_shape, name, flops=10**9, limit=48, **spec):
    return pl.pallas_call(
        kernel, out_shape=out_shape, name=name,
        compiler_params=pltpu.CompilerParams(vmem_limit_bytes=limit << 20),
        cost_estimate=pl.CostEstimate(flops=int(flops * 0.02), bytes_accessed=0, transcendentals=0), **spec)


def shape(*dims, dtype=bf16):
    return jax.ShapeDtypeStruct(dims, dtype)


def far(*dims, dtype=bf16):
    return pltpu.MemorySpace.HBM(dims, dtype)


def stay(*arrays):
    return [pltpu.with_memory_space_constraint(a, pltpu.MemorySpace.HBM) for a in arrays]


def scalar_first(grid, in_specs, out_specs, scratch=()):
    return dict(grid_spec=pltpu.PrefetchScalarGridSpec(
        num_scalar_prefetch=1, grid=grid, in_specs=in_specs, out_specs=out_specs, scratch_shapes=list(scratch)))


def full(*dims):
    return pl.BlockSpec(dims, lambda *_: (0,) * len(dims))


def pack_heads_kernel(core_ref, qkv_ref, vec_ref, heads_ref):
    for part in range(3):
        near = pl.ds(pl.multiple_of(640 * part + 256 * core_ref[0], 128), 256)
        heads_ref[:, 384 * part:384 * part + 256] = qkv_ref[:, near]
        heads_ref[:, 384 * part + 256:384 * (part + 1)] = qkv_ref[:, 640 * part + 512:640 * (part + 1)]
    heads_ref[:, 1152:1280] = vec_ref[...]


def pack_heads(core, w_qkv, vectors):
    return call(pack_heads_kernel, shape(160, 1280), "pack_heads", 10**6, 8, **scalar_first(
        (1,), [full(160, 1920), full(160, 128)], full(160, 1280)))(core, w_qkv, vectors)


def turn_kernel(vec_ref, rows_ref):
    rows_ref[...] = vec_ref[...].astype(f32).T[:16]


def vector_rows(heads):
    return call(turn_kernel, shape(16, 640, dtype=f32), "vector_rows", 10**6, 8, grid=(1,),
                in_specs=[pl.BlockSpec((640, 128), lambda i: (0, 9))], out_specs=full(16, 640))(heads)


def pack_feed_kernel(core_ref, out_ref, up_ref, down_ref, feed_ref):
    core = core_ref[0]
    feed_ref[:, 5120:5760] = out_ref[...]
    for f in range(4):
        feed_ref[:, 640 * f:640 * (f + 1)] = up_ref[:, pl.ds(pl.multiple_of(1280 * f + 640 * core, 128), 640)]
        feed_ref[:, 2560 + 640 * f:2560 + 640 * (f + 1)] = down_ref[pl.ds(pl.multiple_of(640 * core + 160 * f, 32), 160), :]


def pack_feed(core, w_out, w_up, w_down):
    return call(pack_feed_kernel, far(160, 5760), "pack_feed", 10**6, 16, **scalar_first(
        (1,), [full(160, 640), full(160, 5120), full(1280, 640)], full(160, 5760)))(core, *stay(w_out, w_up, w_down))


def rows_in_order(core, mine, theirs, x_ref):
    mine, theirs = mine.astype(f32), theirs.astype(f32)
    x_ref[0:256, :] = jnp.where(core == 0, mine, theirs)
    x_ref[256:512, :] = jnp.where(core == 0, theirs, mine)


def window_rows(core, own_refs, other_refs, m, block, x_ref):
    for j in range(len(own_refs)):
        @pl.when(block == j)
        def _():
            rows_in_order(core, own_refs[j][m], other_refs[j][m], x_ref)


def project_kernel(chips, place_ref, *refs):
    n = len(chips)
    own_refs, other_refs = refs[:n], refs[n:2 * n]
    vec_ref, w_ref = refs[2 * n:2 * n + 2]
    k_ref, v_ref, kT_ref, vT_ref = refs[-6 - 2 * (n == 3):][:4]
    x_ref, hid_ref = refs[-2:]
    m, step = pl.program_id(0), pl.program_id(1)
    block = sum(jnp.where(step == i, chip, 0) for i, chip in enumerate(chips))
    needed = (block >= place_ref[1 + 2 * m]) & (block < place_ref[2 + 2 * m])

    @pl.when(jnp.logical_not(needed))
    def _():
        for ref in (k_ref, v_ref, kT_ref, vT_ref):
            ref[...] = jnp.zeros_like(ref)

    @pl.when(needed)
    def _():
        window_rows(place_ref[0], own_refs, other_refs, m, step, x_ref)
        hidden = (moments(x_ref[...])[0] * vec_ref[0:1, :] + vec_ref[1:2, :]).astype(bf16)
        hid_ref[...] = hidden
        kv = jnp.dot(hidden, w_ref[:, 384:], preferred_element_type=f32)
        low = kv.astype(bf16)
        k_ref[0] = low[:, :384]
        v_ref[0] = low[:, 384:]
        turned = kv.T.astype(bf16)
        kT_ref[0] = turned[:384]
        vT_ref[0] = turned[384:]

    if n == 3:
        q_ref, qT_ref = refs[-4:-2]

        @pl.when(step == 1)
        def _():
            q = jnp.dot(hid_ref[...], w_ref[:, :384], preferred_element_type=f32)
            q_ref[0] = q.astype(bf16)
            qT_ref[0] = q.T.astype(bf16)


def project(chips, place, own, other, vec, w, earlier=()):
    n = len(chips)
    chip = (lambda b: b + 1) if n == 3 else (lambda b: 4 * b)
    tall = pl.BlockSpec((1, 512, 384), lambda m, b, *_: (m, chip(b), 0))
    wide = pl.BlockSpec((1, 384, 512), lambda m, b, *_: (m, 0, chip(b)))
    shapes = [far(2, 2560, 384), far(2, 2560, 384), far(2, 384, 2560), far(2, 384, 2560)]
    specs = [tall, tall, wide, wide]
    if n == 3:
        shapes += [far(2, 512, 384), far(2, 384, 512)]
        specs += [pl.BlockSpec((1, 512, 384), lambda m, *_: (m, 0, 0)), pl.BlockSpec((1, 384, 512), lambda m, *_: (m, 0, 0))]
    own, other = [own[c] for c in chips], [other[c] for c in chips]
    return call(
        lambda *refs: project_kernel(chips, *refs), shapes, "project", 5 * 10**9, 28,
        input_output_aliases={2 * n + 3 + i: i for i in range(len(earlier))}, **scalar_first(
            (2, n), [full(2, 256, 640)] * (2 * n) + [full(16, 640), full(640, 1152)] + [pl.BlockSpec(memory_space=pl.ANY)] * len(earlier),
            specs, [pltpu.VMEM((512, 640), f32), pltpu.VMEM((512, 640), bf16)]))(place, *own, *other, vec, *stay(w), *earlier)


def heads_joined(core, mine, theirs):
    first, second = (jnp.where(core == 0, a, b) for a, b in ((mine, theirs), (theirs, mine)))
    return jnp.concatenate([first[:, :256], second[:, :256], first[:, 256:] + second[:, 256:]], axis=1)


def middle_kernel(core_ref, w_ref, low0_ref, low1_ref, theirs_ref, tok_ref, tok2_ref, vec_ref, mid_ref, hid_ref, hid2_ref):
    core = core_ref[0]
    for m, low_ref in enumerate((low0_ref, low1_ref)):
        attended = heads_joined(core, low_ref[...].astype(f32), theirs_ref[m].astype(f32)).astype(bf16)
        branch = jnp.dot(attended, w_ref[...], preferred_element_type=f32)
        mine = jnp.where(core == 0, branch[:256], branch[256:]) + tok_ref[m].astype(f32)
        theirs = jnp.where(core == 0, branch[256:], branch[:256]) + tok2_ref[m].astype(f32)
        part = slice(256 * m, 256 * (m + 1))
        mid_ref[part, :] = mine
        hid_ref[part, :] = (moments(mine)[0] * vec_ref[2:3, :] + vec_ref[3:4, :]).astype(bf16)
        hid2_ref[part, :] = (moments(theirs)[0] * vec_ref[2:3, :] + vec_ref[3:4, :]).astype(bf16)


W_OUT = pl.BlockSpec((640, 640), lambda *_: (0, 8))


def middle_step(core, weights, *args):
    return call(middle_kernel, (far(512, 640, dtype=f32), far(512, 640), far(512, 640)), "middle", 10**9, 20, **scalar_first(
        (1,), [W_OUT] + [full(*a.shape) for a in args], [full(512, 640)] * 3))(core, *stay(weights), *args)


def feed_kernel(h_ref, h2_ref, cot_ref, cot2_ref, up_ref, down_ref, mine_ref, theirs_ref, g_ref, h, cot, hT, cT, out, dh):
    chunk = pl.program_id(0)

    @pl.when(chunk == 0)
    def _():
        h[0:512, :], h[512:1024, :] = h_ref[...], h2_ref[...]
        cot[0:512, :], cot[512:1024, :] = cot_ref[...], cot2_ref[...]
        hT[...] = h[...].astype(f32).T.astype(bf16)
        cT[...] = cot[...].astype(f32).T.astype(bf16)
        out[...] = jnp.zeros_like(out)
        dh[...] = jnp.zeros_like(dh)

    up_w = up_ref[...]
    down_w = jnp.concatenate([down_ref[160 * y:160 * (y + 1), 640 * i:640 * (i + 1)] for y in range(2) for i in range(4)], axis=0)
    acts, d_ups = [], []
    for t in range(4):
        rows = slice(256 * t, 256 * (t + 1))
        u = jnp.dot(h[rows, :], up_w, preferred_element_type=f32)
        d_act = lax.dot_general(cot[rows, :], down_w, NT, preferred_element_type=f32)
        cdf = 0.5 * (1.0 + lax.erf(u * (2.0 ** -0.5)))
        pdf = jnp.exp(u * u * -0.5) * ((2.0 * math.pi) ** -0.5)
        act = (u * cdf).astype(bf16)
        d_up = (d_act * (cdf + u * pdf)).astype(bf16)
        out[rows, :] += jnp.dot(act, down_w, preferred_element_type=f32)
        dh[rows, :] += lax.dot_general(d_up, up_w, NT, preferred_element_type=f32)
        acts.append(act)
        d_ups.append(d_up)
    g_up = jnp.dot(hT[...], jnp.concatenate(d_ups, axis=0), preferred_element_type=f32).astype(bf16)
    g_down = jnp.dot(cT[...], jnp.concatenate(acts, axis=0), preferred_element_type=f32).T.astype(bf16)
    for f in range(2):
        for y in range(4):
            for i in range(2):
                g_ref[4 * chunk + 2 * f + i, y] = g_up[160 * y + 80 * i:160 * y + 80 * (i + 1), 640 * f:640 * (f + 1)]
        for i in range(8):
            g_ref[8 + i, 2 * chunk + f] = g_down[640 * f + 80 * i:640 * f + 80 * (i + 1)]

    @pl.when(chunk == 1)
    def _():
        mine_ref[0], mine_ref[1] = out[0:512, :].astype(bf16), dh[0:512, :].astype(bf16)
        theirs_ref[0], theirs_ref[1] = out[512:1024, :].astype(bf16), dh[512:1024, :].astype(bf16)


def feed_forward(h, h2, cot, cot2, weights):
    return call(
        feed_kernel,
        (far(2, 512, 640), far(2, 512, 640), far(16, 4, 80, 640)),
        "feed_forward", 30 * 10**9, 52, grid=(2,),
        in_specs=[full(512, 640)] * 4 + [pl.BlockSpec((640, 1280), lambda f: (0, f)), pl.BlockSpec((320, 2560), lambda f: (f, 1))],
        out_specs=[full(2, 512, 640), full(2, 512, 640), full(16, 4, 80, 640)],
        scratch_shapes=[pltpu.VMEM((1024, 640), bf16), pltpu.VMEM((1024, 640), bf16), pltpu.VMEM((640, 1024), bf16), pltpu.VMEM((640, 1024), bf16),
                        pltpu.VMEM((1024, 640), f32), pltpu.VMEM((1024, 640), f32)],
    )(*stay(h, h2, cot), cot2, *stay(weights, weights))


def after_kernel(mid_ref, mine_ref, theirs_ref, cot_ref, vec_ref, block_ref, grad_ref, branch_ref, g_ref):
    @pl.when(pl.program_id(0) == 0)
    def _():
        g_ref[...] = jnp.zeros_like(g_ref)

    middle = mid_ref[...]
    block_ref[...] = (middle + mine_ref[0].astype(f32) + theirs_ref[0].astype(f32)).astype(bf16)
    d_hidden = mine_ref[1].astype(f32) + theirs_ref[1].astype(f32)
    n, r = moments(middle)
    g_ref[0:1, :] += jnp.sum(d_hidden * n, axis=0, keepdims=True)
    g_ref[1:2, :] += jnp.sum(d_hidden, axis=0, keepdims=True)
    grad = cot_ref[...].astype(f32) + norm_back(d_hidden, n, r, vec_ref[2:3, :])
    grad_ref[...] = grad
    branch_ref[...] = grad.astype(bf16)


def after_feed(*args):
    rows, pair = pl.BlockSpec((128, 640), lambda i: (i, 0)), pl.BlockSpec((2, 128, 640), lambda i: (0, i, 0))
    return call(
        after_kernel, (far(512, 640), far(512, 640, dtype=f32), shape(512, 640), shape(8, 640, dtype=f32)), "after_feed", 10**9, 16,
        grid=(4,), in_specs=[rows, pair, pair, rows, full(16, 640)], out_specs=[rows, rows, rows, full(8, 640)])(*stay(args[0], args[1]), args[2], *stay(args[3]), args[4])


def branch_kernel(core_ref, own_ref, their_ref, w_ref, low0_ref, low1_ref, theirs_ref, do_ref, doT_ref, g_ref):
    core = core_ref[0]
    w = jnp.concatenate([w_ref[pl.ds(pl.multiple_of(256 * core, 256), 256), :], w_ref[512:640, :]], axis=0)
    g = jnp.zeros((640, 384), f32)
    for m in range(2):
        part = slice(256 * m, 256 * (m + 1))
        mine, theirs = own_ref[part, :].astype(f32), their_ref[part, :].astype(f32)
        branch = jnp.concatenate([jnp.where(core == 0, mine, theirs), jnp.where(core == 0, theirs, mine)], axis=0)
        kept = jnp.where(core == 0, branch[:, :384], branch[:, 256:]).astype(bf16)
        branch = branch.astype(bf16)
        rows = slice(512 * m, 512 * (m + 1))
        do = lax.dot_general(branch, w, NT, preferred_element_type=f32)
        do_ref[rows, :] = do.astype(bf16)
        doT_ref[:, rows] = do.T.astype(bf16)
        attended = heads_joined(core, (low0_ref, low1_ref)[m][...].astype(f32), theirs_ref[m].astype(f32))
        g = g + jnp.dot(attended.T.astype(bf16), kept, preferred_element_type=f32)
    g_ref[...] = g


def branch_step(core, own, their, weights, *args):
    return call(
        branch_kernel, (far(1024, 384), far(384, 1024), far(640, 384, dtype=f32)), "branch", 10**9, 24, **scalar_first(
            (1,), [full(512, 640)] * 2 + [W_OUT] + [full(*a.shape) for a in args], [full(1024, 384), full(384, 1024), full(640, 384)]))(
                core, own, their, *stay(weights), *args)


def project_back_kernel(core_ref, *refs):
    own_refs, other_refs = refs[:5], refs[5:10]
    (vec_ref, w_ref, dq0_ref, dq1_ref, dk0_ref, dk1_ref, dv0_ref, dv1_ref, g_out_ref, g_two_ref,
     mine_ref, theirs_ref, tail_ref, x_ref, d_kv, d_q, d_hid, g_ref, g_vec, slots, arrived) = refs[10:]
    step, core = pl.program_id(0), core_ref[0]
    block = lax.rem(step, 5)

    def copies(at, j, m, slot):
        for i, refs_of in enumerate((own_refs, other_refs)):
            getattr(pltpu.make_async_copy(refs_of[j].at[m], slots.at[slot, i], arrived.at[slot, i]), at)()

    def fetch(number):
        for j in range(5):
            for m in range(2):
                @pl.when(number == 5 * m + j)
                def _():
                    copies("start", j, m, lax.rem(number, 2))

    @pl.when(step == 0)
    def _():
        fetch(step)

    copies("wait", 0, 0, lax.rem(step, 2))

    @pl.when(step < 9)
    def _():
        fetch(step + 1)

    @pl.when(step == 0)
    def _():
        g_ref[...] = jnp.zeros_like(g_ref)
        g_vec[...] = jnp.zeros_like(g_vec)
        g_vec[2:4, :] = g_two_ref[0:2, :]

    second = lax.div(step, 5)
    needed = (block >= core_ref[1 + 2 * second]) & (block < core_ref[2 + 2 * second])

    @pl.when(jnp.logical_not(needed))
    def _():
        mine_ref[...] = jnp.zeros_like(mine_ref)
        theirs_ref[...] = jnp.zeros_like(theirs_ref)

    for m, (dq, dk, dv) in enumerate(((dq0_ref, dk0_ref, dv0_ref), (dq1_ref, dk1_ref, dv1_ref))):
        @pl.when(needed & (second == m))
        def _():
            rows_in_order(core, slots[lax.rem(step, 2), 0], slots[lax.rem(step, 2), 1], x_ref)
            d_kv[:, :384], d_kv[:, 384:] = dk[...], dv[...]
            d_q[...] = dq[...]

    @pl.when(needed)
    def _():
        n = moments(x_ref[...])[0]
        hiddenT = (n * vec_ref[0:1, :] + vec_ref[1:2, :]).T.astype(bf16)
        d_hid[...] = lax.dot_general(d_kv[...], w_ref[:, 384:], NT, preferred_element_type=f32)
        g_ref[:, 384:] += jnp.dot(hiddenT, d_kv[...], preferred_element_type=f32)

        @pl.when(block == 2)
        def _():
            g_ref[:, :384] += jnp.dot(hiddenT, d_q[...], preferred_element_type=f32)
            d_hid[...] += lax.dot_general(d_q[...], w_ref[:, :384], NT, preferred_element_type=f32)

        dh = d_hid[...]
        mine_ref[0, 0] = jnp.where(core == 0, dh[:256], dh[256:]).astype(bf16)
        theirs_ref[0, 0] = jnp.where(core == 0, dh[256:], dh[:256]).astype(bf16)
        g_vec[0:1, :] += jnp.sum(dh * n, axis=0, keepdims=True)
        g_vec[1:2, :] += jnp.sum(dh, axis=0, keepdims=True)

    @pl.when(step == 9)
    def _():
        turned = g_vec[...].T
        lane = lax.broadcasted_iota(jnp.int32, (640, 128), 1) - 64 * (1 - core)
        spare = g_ref[:, 256:384]
        for i in range(4):
            spare = jnp.where(lane == i, turned[:, i:i + 1], spare)
        g_ref[:, 256:384] = spare
        for y in range(4):
            for z in range(4):
                rows = slice(160 * y + 40 * z, 160 * y + 40 * (z + 1))
                for x in range(3):
                    tail_ref[16 * y + 4 * z + x] = g_ref[rows, 384 * x:384 * (x + 1)].astype(bf16)
                tail_ref[16 * y + 4 * z + 3] = g_out_ref[rows, :].astype(bf16)


def project_back(core, own, other, vec, w, dq, dk, dv, g_out, g_two):
    dq, dk, dv, (g_out,) = stay(*dq), stay(*dk), stay(*dv), stay(g_out)
    first = pl.BlockSpec((512, 384), lambda b, *_: (jnp.minimum(b, 4), 0))
    second = pl.BlockSpec((512, 384), lambda b, *_: (jnp.maximum(b - 5, 0), 0))
    return call(
        project_back_kernel, (shape(5, 2, 256, 640), shape(5, 2, 256, 640), shape(64, 40, 384)), "project_back", 10**10, 36, **scalar_first(
            (10,), [pl.BlockSpec(memory_space=pl.ANY)] * 10 + [full(16, 640), full(640, 1152), full(512, 384), full(512, 384), first, second, first, second,
                                               full(640, 384), full(8, 640)],
            [pl.BlockSpec((1, 1, 256, 640), lambda b, *_: (lax.rem(b, 5), b // 5, 0, 0))] * 2 + [full(64, 40, 384)],
            [pltpu.VMEM((512, 640), f32), pltpu.VMEM((512, 768), bf16), pltpu.VMEM((512, 384), bf16),
             pltpu.VMEM((512, 640), f32), pltpu.VMEM((640, 1152), f32), pltpu.VMEM((8, 640), f32),
             pltpu.VMEM((2, 2, 256, 640), bf16), pltpu.SemaphoreType.DMA((2, 2))]))(core, *stay(*own, *other), vec, *stay(w), *dq, *dk, *dv, g_out, g_two)


def in_core_order(core_ref, mine, theirs):
    core, mine, theirs = core_ref[0], mine.astype(f32), theirs.astype(f32)
    return jnp.where(core == 0, mine, theirs), jnp.where(core == 0, theirs, mine)


def final_feed_kernel(core_ref, mine_ref, theirs_ref, up_ref, down_ref):
    for i in range(16):
        for c, piece in enumerate(in_core_order(core_ref, mine_ref[i], theirs_ref[i])):
            if i < 8:
                base = 1280 * (i // 2) + 640 * c
                up_ref[80 * (i % 2):80 * (i % 2 + 1), base:base + 640] = piece
            else:
                base = 640 * c + 80 * (i - 8)
                down_ref[base:base + 80, :] = piece


def final_feed(core, mine, theirs):
    return call(final_feed_kernel, (shape(160, 5120, dtype=f32), shape(1280, 640, dtype=f32)), "final_feed", 10**6, 32, **scalar_first(
        (1,), [full(16, 80, 640)] * 2, [full(160, 5120), full(1280, 640)]))(core, mine, theirs)


def final_heads_kernel(core_ref, mine_ref, theirs_ref, qkv_ref, out_ref, vec_ref):
    lane = lax.broadcasted_iota(jnp.int32, (40, 128), 1)
    for z in range(4):
        rows = slice(40 * z, 40 * (z + 1))
        for x in range(4):
            a, b = in_core_order(core_ref, mine_ref[4 * z + x], theirs_ref[4 * z + x])
            if x < 3:
                last = jnp.where(lane < 64, a[:, 256:], b[:, 256:])
                qkv_ref[rows, 640 * x:640 * (x + 1)] = jnp.concatenate([a[:, :256], b[:, :256], last], axis=1)
            else:
                out_ref[rows, :] = jnp.concatenate([a, b[:, 128:]], axis=1)
            if x == 0:
                vec_ref[rows, :] = pltpu.roll(a[:, 256:], 64, 1) + b[:, 256:]


def final_heads(core, mine, theirs):
    return call(
        final_heads_kernel, (shape(160, 1920, dtype=f32), shape(160, 640, dtype=f32), shape(160, 128, dtype=f32)), "final_heads", 10**6, 16,
        **scalar_first((1,), [full(16, 40, 384)] * 2, [full(160, 1920), full(160, 640), full(160, 128)]))(core, mine, theirs)


def shifted(array, axis, by):
    devices = lax.axis_size(axis)
    return lax.ppermute(array, axis, [(i, (i + by) % devices) for i in range(devices)])


def passed_along(array, by):
    devices = lax.axis_size(("z", "x"))
    return lax.ppermute(array, ("z", "x"), [(i, i + by) for i in range(devices) if 0 <= i + by < devices])


def swapped(array):
    return lax.ppermute(array, "core", [(0, 1), (1, 0)])


def pick(array, index):
    return lax.dynamic_index_in_dim(array, index, 0, keepdims=False)


def gathered(array, axis):
    me, devices = lax.axis_index(axis), lax.axis_size(axis)
    out = jnp.zeros((devices,) + array.shape, array.dtype)
    out = lax.dynamic_update_index_in_dim(out, array, me, 0)
    for by in (1, devices - 1, 2):
        out = lax.dynamic_update_index_in_dim(out, shifted(array, axis, by), (me + devices - by) % devices, 0)
    return out


def window_info(length_row, chip, core, win):
    ends = jnp.cumsum(length_row)
    starts = ends - length_row
    base = chip * 512 - 1024
    places = base + jnp.arange(win, dtype=jnp.int32)
    inside = (places[:, None] >= starts[None, :]) & (places[:, None] < ends[None, :])
    ones = jnp.broadcast_to(jnp.arange(64) < 3, (win, 64)).astype(bf16)
    key_rows = jnp.concatenate([jnp.where(inside, 0.0, -BIG).astype(bf16), ones], axis=1)
    own = chip * 512 + jnp.arange(512, dtype=jnp.int32)
    inside_q = (own[None, :] >= starts[:, None]) & (own[None, :] < ends[:, None])
    query_rows = jnp.concatenate([inside_q.astype(bf16), jnp.zeros((64, 512), bf16)], axis=0)
    info = [core]
    sizes = []
    for t in range(2):
        first = chip * 512 + t * TILE
        low = jnp.max(jnp.where(starts <= first, starts, 0)) - base
        high = jnp.min(jnp.where(ends > first + TILE - 1, ends, 1 << 30)) - base
        start = low // 128 * 128
        need = high - start
        size = (need + SHORT - 1) // SHORT * SHORT
        info.append(jnp.minimum(start, win - size))
        sizes.append(size)
    low = jnp.minimum(info[1], info[2]) // 512
    high = (jnp.maximum(info[1] + sizes[0], info[2] + sizes[1]) + 511) // 512
    return jnp.stack(info + sizes).astype(jnp.int32), key_rows, query_rows, [low, high]


def body(tokens, lengths, gain_one, bias_one, w_qkv, w_out, gain_two, bias_two, w_up, w_down, cotangent):
    core, chip = lax.axis_index("core"), lax.axis_index(("z", "x"))
    core_arg = core[None].astype(jnp.int32)
    tok, cot = tokens[:, 0], cotangent[:, 0].reshape(512, 640)
    together = lambda *arrays: lax.optimization_barrier(arrays)

    vectors = jnp.pad(jnp.stack([gain_one, bias_one, gain_two, bias_two], axis=1), ((0, 0), (0, 124)))
    heads, tok = together(pack_heads(core_arg, w_qkv, vectors), tok)
    heads = lax.all_gather(heads, "batch", axis=0, tiled=True)
    before, after, tok_other = passed_along(tok, 1), passed_along(tok, -1), swapped(tok)
    windows = [window_info(lengths[m, 0], chip, core, 2560) for m in range(2)]
    place = jnp.stack([core] + windows[0][3] + windows[1][3]).astype(jnp.int32)
    feed_pack = pack_feed(core_arg, w_out, w_up, w_down)
    before, after, tok_other, feed_pack, place, windows = together(before, after, tok_other, feed_pack, place, windows)
    own = [passed_along(before, 1), before, tok, after, passed_along(after, -1)]
    other = [None, swapped(before), tok_other, swapped(after), None]
    heads, feed_pack = together(heads, feed_pack)
    feed_weights = lax.all_gather(feed_pack, "batch", axis=0, tiled=True)
    vec = vector_rows(heads)
    *near_parts, q, qT = project((1, 2, 3), place, own, other, vec, heads)
    own[0], own[4], near_parts = together(own[0], own[4], near_parts)
    other[0], other[4] = swapped(own[0]), swapped(own[4])
    k, v, kT, vT = project((0, 4), place, own, other, vec, heads, near_parts)
    (oT0, low0, lse0), (oT1, low1, lse1) = (
        attend(m, info, qT, k, vT, key_rows, query_rows) for m, (info, key_rows, query_rows, _) in enumerate(windows))

    theirs = swapped(jnp.stack([low0, low1]))
    middle, hidden_two, hidden_other = middle_step(core_arg, feed_weights, low0, low1, theirs, tok, tok_other, vec)
    mine, partial, feed_grads = feed_forward(hidden_two, hidden_other, cot, swapped(cot), feed_weights)
    feed_grads = lax.psum_scatter(feed_grads.reshape(5120, 640), ("z", "x"), scatter_dimension=0, tiled=True)
    block_out, grad_middle, branch, g_two = after_feed(middle, mine, swapped(partial), cot, vec)

    do, doT, g_out = branch_step(core_arg, branch, swapped(branch), feed_weights, low0, low1, theirs)
    dq, dk, dv = zip(*(
        attend_back(m, info, qT, q, k, kT, v, doT, do, oT, lse, key_rows, query_rows)
        for m, ((info, key_rows, query_rows, _), oT, lse) in enumerate(zip(windows, (oT0, oT1), (lse0, lse1)))))
    mine, theirs, tail = project_back(place, own, other, vec, heads, dq, dk, dv, g_out, g_two)
    feed_grads, mine, theirs, tail = together(feed_grads, mine, theirs, tail)

    feed = lax.psum_scatter(feed_grads, "batch", scatter_dimension=0, tiled=True).reshape(80, 640)
    tail = lax.all_to_all(tail, ("batch", "z", "x"), 0, 0, tiled=True)
    feed = lax.all_gather(feed, ("z", "x"), axis=0, tiled=True).reshape(16, 80, 640)
    theirs = swapped(theirs)
    sums = [mine[j].astype(f32) + theirs[j].astype(f32) for j in range(5)]
    returned = [passed_along(sums[2 + by].astype(bf16), by) for by in (1, -1, 2, -2)]
    tail, sums[2] = together(tail, sums[2])
    tail = gathered(jnp.sum(tail.astype(f32), axis=0).astype(bf16), "x").reshape(160, 384)
    tail, returned[0], returned[1] = together(tail, returned[0], returned[1])
    tail = gathered(tail, "z").reshape(16, 40, 384)
    tail, returned = together(tail, returned)
    d_one = sum((part.astype(f32) for part in returned), sums[2]).reshape(512, 640)
    n_one, r_one = moments(tok.reshape(512, 640).astype(f32))
    grad_tokens = (grad_middle + norm_back(d_one, n_one, r_one, vec[0:1])).astype(bf16)
    tail, grad_tokens, feed = together(tail, grad_tokens, feed)
    grad_qkv, grad_out, spare = final_heads(core_arg, tail, swapped(tail))
    grad_up, grad_down = final_feed(core_arg, feed, swapped(feed))
    return (
        block_out.reshape(2, 1, 256, 640), grad_tokens.reshape(2, 1, 256, 640), spare[:, 0], spare[:, 1], grad_qkv, grad_out,
        spare[:, 2], spare[:, 3], grad_up, grad_down)


def solution(mesh):
    fine = Mesh(mesh.devices.reshape(4, 4, 4, 2), ("batch", "z", "x", "core"))
    rows = P(None, "batch", ("z", "x", "core"), None)
    one, two = P("batch"), P("batch", None)
    return jax.shard_map(
        body,
        mesh=fine,
        in_specs=(rows, P(None, "batch", None), one, one, two, two, one, one, two, two, rows),
        out_specs=(rows, rows, one, one, two, two, one, one, two, two),
        check_vma=False,
    )
```

```python
import math

import jax
import jax.numpy as jnp
from jax import lax
from jax.experimental import pallas as pl
from jax.experimental.pallas import tpu as pltpu
from jax.sharding import Mesh
from jax.sharding import PartitionSpec as P

HEAD_DIM = 32
SCALE = HEAD_DIM ** -0.5
LOG2E = math.log2(math.e)
C2 = SCALE * LOG2E
BIG = 1e30
TILE = 256
EPSILON = 1e-05
PAIRS = 5
SHORT, LONG = 384, 1152
f32, bf16 = jnp.float32, jnp.bfloat16
NT = (((1,), (1,)), ((), ()))


def pair_offset(info_ref):
    p = pl.program_id(0)
    sub = jnp.where(p == PAIRS - 1, info_ref[0], lax.rem(p, 2))
    return sub * (2 * HEAD_DIM)


def split3(v):
    a = v.astype(bf16)
    r = v - a.astype(f32)
    b = r.astype(bf16)
    d = (r - b.astype(f32)).astype(bf16)
    return a, b, d


def rows_masked(xT, off):
    row = lax.broadcasted_iota(jnp.int32, xT.shape, 0) - off
    xf = xT.astype(f32)
    return [jnp.where((row >= HEAD_DIM * j) & (row < HEAD_DIM * (j + 1)), xf, 0.0).astype(bf16) for j in range(2)]


def lanes_masked(x, off):
    lane = lax.broadcasted_iota(jnp.int32, x.shape, 1) - off
    xf = x.astype(f32)
    return [jnp.where((lane >= HEAD_DIM * j) & (lane < HEAD_DIM * (j + 1)), xf, 0.0).astype(bf16) for j in range(2)]


def attend_kernel(info_ref, qT_ref, k_ref, vT_ref, kaug_ref, qaugT_ref, oT_ref, o_ref, l_ref, rhs):
    off = pair_offset(info_ref)
    oT_ref[...] = jnp.where(lax.rem(pl.program_id(0), 2) == 0, 0.0, oT_ref[...])
    for t in range(2):
        cols = slice(t * TILE, (t + 1) * TILE)
        masked = rows_masked(qT_ref[:, cols], off)
        for j in range(2):
            rhs[0:128, j * TILE:(j + 1) * TILE] = masked[j]
            rhs[128:256, j * TILE:(j + 1) * TILE] = qaugT_ref[:, cols]
        start = info_ref[1 + t]
        need = info_ref[3 + t]

        def block(first, size):
            def step(i, carry):
                row = pl.multiple_of(first + i * size, 128)
                lhs = jnp.concatenate([k_ref[pl.ds(row, size), :], kaug_ref[pl.ds(row, size), :]], axis=1)
                raw = [jnp.dot(lhs, rhs[:, j * TILE:(j + 1) * TILE], preferred_element_type=f32) for j in range(2)]
                out = []
                for j in range(2):
                    m, l, o = carry[j]
                    s = raw[j] * C2
                    m_new = jnp.maximum(m, jnp.max(s, axis=0, keepdims=True))
                    alpha = jnp.exp2(m - m_new)
                    p = jnp.exp2(s - m_new)
                    vT = vT_ref[pl.ds(pl.multiple_of(off + j * HEAD_DIM, HEAD_DIM), HEAD_DIM), pl.ds(row, size)]
                    out.append((m_new, l * alpha + jnp.sum(p, axis=0, keepdims=True),
                                o * alpha + jnp.dot(vT, p.astype(bf16), preferred_element_type=f32)))
                return tuple(out)
            return step

        def finish(state):
            for j in range(2):
                m, l, o = state[j]
                oT_ref[pl.ds(pl.multiple_of(off + j * HEAD_DIM, HEAD_DIM), HEAD_DIM), cols] = o * (1.0 / l)
                l_ref[0, j:j + 1, cols] = m + jnp.log2(l)

        init = tuple((jnp.full((1, TILE), -1e38, f32), jnp.zeros((1, TILE), f32), jnp.zeros((HEAD_DIM, TILE), f32)) for _ in range(2))

        longs = lax.div(need, LONG)
        state = lax.fori_loop(0, longs, block(start, LONG), init)
        finish(lax.fori_loop(0, lax.div(need - longs * LONG, SHORT), block(start + longs * LONG, SHORT), state))

    o_ref[...] = oT_ref[...].T.astype(bf16)


def attend(m, info, qT, k, vT, kaug, qaugT):
    win, nq = k.shape[1], qT.shape[2]
    qT, k, vT = stay(qT, k, vT)
    return pl.pallas_call(
        attend_kernel,
        out_shape=(jax.ShapeDtypeStruct((384, nq), f32), jax.ShapeDtypeStruct((nq, 384), bf16), jax.ShapeDtypeStruct((PAIRS, 8, nq), f32)),
        grid_spec=pltpu.PrefetchScalarGridSpec(
            num_scalar_prefetch=1, grid=(PAIRS,),
            in_specs=[
                pl.BlockSpec((None, 128, nq), lambda p, *_: (m, p // 2, 0)),
                pl.BlockSpec((None, win, 128), lambda p, *_: (m, 0, p // 2)),
                pl.BlockSpec((None, 128, win), lambda p, *_: (m, p // 2, 0)),
                pl.BlockSpec((win, 128), lambda p, *_: (0, 0)),
                pl.BlockSpec((128, nq), lambda p, *_: (0, 0)),
            ],
            out_specs=[
                pl.BlockSpec((128, nq), lambda p, *_: (p // 2, 0)),
                pl.BlockSpec((nq, 128), lambda p, *_: (0, p // 2)),
                pl.BlockSpec((1, 8, nq), lambda p, *_: (p, 0, 0)),
            ],
            scratch_shapes=[pltpu.VMEM((256, 2 * TILE), bf16)],
        ),
        compiler_params=pltpu.CompilerParams(vmem_limit_bytes=28 << 20),
        cost_estimate=pl.CostEstimate(flops=int(20 * 10**9 * 0.02), bytes_accessed=0, transcendentals=0),
        name="attend",
    )(info, qT, k, vT, kaug, qaugT)


def attend_back_kernel(info_ref, qT_ref, q_ref, k_ref, kT_ref, v_ref, doT_ref, do_ref, oT_ref, l_ref, kaug_ref, qaugT_ref,
                       dq_ref, dk_ref, dv_ref, dqT_ref, rhs_s, rhs_d, q_stk, do_stk, dk_acc, dv_acc):
    p_id = pl.program_id(0)
    off = pair_offset(info_ref)

    @pl.when(lax.rem(p_id, 2) == 0)
    def _():
        dqT_ref[...] = jnp.zeros_like(dqT_ref)
        dk_acc[...] = jnp.zeros_like(dk_acc)
        dv_acc[...] = jnp.zeros_like(dv_acc)

    for t in range(2):
        cols = slice(t * TILE, (t + 1) * TILE)
        masked_q = rows_masked(qT_ref[:, cols], off)
        masked_do = rows_masked(doT_ref[:, cols], off)
        lane_q = lanes_masked(q_ref[cols, :], off)
        lane_do = lanes_masked(do_ref[cols, :], off)
        for j in range(2):
            part = slice(j * TILE, (j + 1) * TILE)
            head = pl.ds(pl.multiple_of(off + j * HEAD_DIM, HEAD_DIM), HEAD_DIM)
            delta = jnp.sum(doT_ref[head, cols].astype(f32) * oT_ref[head, cols], axis=0, keepdims=True)
            total = l_ref[0, j:j + 1, cols] * (1.0 / C2)
            rowid = lax.broadcasted_iota(jnp.int32, (64, TILE), 0)
            lp, dp = split3(-total), split3(-delta)
            def pieces(parts):
                x = jnp.zeros((64, TILE), f32)
                for n in range(3):
                    x = jnp.where(rowid == n, parts[n].astype(f32), x)
                return x.astype(bf16)
            rhs_s[0:128, part] = masked_q[j]
            rhs_s[128:192, part] = qaugT_ref[0:64, cols]
            rhs_s[192:256, part] = pieces(lp)
            rhs_d[0:128, part] = masked_do[j]
            rhs_d[128:192, part] = jnp.zeros((64, TILE), bf16)
            rhs_d[192:256, part] = pieces(dp)
            q_stk[part, :] = lane_q[j]
            do_stk[part, :] = lane_do[j]
        start = info_ref[1 + t]
        need = info_ref[3 + t]

        def block(first, size):
            def step(i, carry):
                row = pl.multiple_of(first + i * size, 128)
                rows = pl.ds(row, size)
                aug = kaug_ref[rows, :]
                lhs_k = jnp.concatenate([k_ref[rows, :], aug], axis=1)
                lhs_v = jnp.concatenate([v_ref[rows, :], aug], axis=1)
                out, dv, dk = [], dv_acc[rows, :], dk_acc[rows, :]
                for j in range(2):
                    part = slice(j * TILE, (j + 1) * TILE)
                    s = jnp.dot(lhs_k, rhs_s[:, part], preferred_element_type=f32)
                    dp = jnp.dot(lhs_v, rhs_d[:, part], preferred_element_type=f32)
                    p = jnp.exp2(s * C2)
                    ds = (p * dp).astype(bf16)
                    dv = dv + jnp.dot(p.astype(bf16), do_stk[part, :], preferred_element_type=f32)
                    dk = dk + jnp.dot(ds, q_stk[part, :], preferred_element_type=f32)
                    kT = kT_ref[pl.ds(pl.multiple_of(off + j * HEAD_DIM, HEAD_DIM), HEAD_DIM), rows]
                    out.append(carry[j] + jnp.dot(kT, ds, preferred_element_type=f32))
                dv_acc[rows, :] = dv
                dk_acc[rows, :] = dk
                return tuple(out)
            return step

        def finish(dqs):
            for j in range(2):
                dqT_ref[pl.ds(pl.multiple_of(off + j * HEAD_DIM, HEAD_DIM), HEAD_DIM), cols] = dqs[j] * SCALE

        init = tuple(jnp.zeros((HEAD_DIM, TILE), f32) for _ in range(2))

        longs = lax.div(need, LONG)
        state = lax.fori_loop(0, longs, block(start, LONG), init)
        finish(lax.fori_loop(0, lax.div(need - longs * LONG, SHORT), block(start + longs * LONG, SHORT), state))
    @pl.when((lax.rem(p_id, 2) == 1) | (p_id == PAIRS - 1))
    def _():
        dq_ref[...] = dqT_ref[...].T.astype(bf16)
        dk_ref[...] = (dk_acc[...] * SCALE).astype(bf16)
        dv_ref[...] = dv_acc[...].astype(bf16)


def attend_back(m, info, qT, q, k, kT, v, doT, do, oT, lse, kaug, qaugT):
    win, nq = k.shape[1], qT.shape[2]
    qT, q, k, kT, v, doT, do = stay(qT, q, k, kT, v, doT, do)
    wide = pl.BlockSpec((128, nq), lambda p, *_: (p // 2, 0))
    tall = pl.BlockSpec((nq, 128), lambda p, *_: (0, p // 2))
    keys = pl.BlockSpec((win, 128), lambda p, *_: (0, p // 2))
    wide_m = pl.BlockSpec((None, 128, nq), lambda p, *_: (m, p // 2, 0))
    tall_m = pl.BlockSpec((None, nq, 128), lambda p, *_: (m, 0, p // 2))
    keys_m = pl.BlockSpec((None, win, 128), lambda p, *_: (m, 0, p // 2))
    return pl.pallas_call(
        attend_back_kernel,
        out_shape=(far(nq, 384), far(win, 384), far(win, 384)),
        grid_spec=pltpu.PrefetchScalarGridSpec(
            num_scalar_prefetch=1, grid=(PAIRS,),
            in_specs=[wide_m, tall_m, keys_m, pl.BlockSpec((None, 128, win), lambda p, *_: (m, p // 2, 0)), keys_m,
                      pl.BlockSpec((128, nq), lambda p, *_: (p // 2, m)), pl.BlockSpec((nq, 128), lambda p, *_: (m, p // 2)), wide,
                      pl.BlockSpec((1, 8, nq), lambda p, *_: (p, 0, 0)),
                      pl.BlockSpec((win, 128), lambda p, *_: (0, 0)), pl.BlockSpec((128, nq), lambda p, *_: (0, 0))],
            out_specs=[tall, keys, keys],
            scratch_shapes=[pltpu.VMEM((128, nq), f32), pltpu.VMEM((256, 2 * TILE), bf16), pltpu.VMEM((256, 2 * TILE), bf16),
                            pltpu.VMEM((2 * TILE, 128), bf16), pltpu.VMEM((2 * TILE, 128), bf16),
                            pltpu.VMEM((win, 128), f32), pltpu.VMEM((win, 128), f32)],
        ),
        compiler_params=pltpu.CompilerParams(vmem_limit_bytes=32 << 20),
        cost_estimate=pl.CostEstimate(flops=int(40 * 10**9 * 0.02), bytes_accessed=0, transcendentals=0),
        name="attend_back",
    )(info, qT, q, k, kT, v, doT, do, oT, lse, kaug, qaugT)


def moments(x):
    centred = x - jnp.mean(x, axis=-1, keepdims=True)
    r = lax.rsqrt(jnp.mean(centred * centred, axis=-1, keepdims=True) + EPSILON)
    return centred * r, r


def norm_back(grad, n, r, gain):
    e = grad * gain
    return r * (e - jnp.mean(e, axis=-1, keepdims=True) - n * jnp.mean(e * n, axis=-1, keepdims=True))


def call(kernel, out_shape, name, flops=10**9, limit=48, **spec):
    return pl.pallas_call(
        kernel, out_shape=out_shape, name=name,
        compiler_params=pltpu.CompilerParams(vmem_limit_bytes=limit << 20),
        cost_estimate=pl.CostEstimate(flops=int(flops * 0.02), bytes_accessed=0, transcendentals=0), **spec)


def shape(*dims, dtype=bf16):
    return jax.ShapeDtypeStruct(dims, dtype)


def far(*dims, dtype=bf16):
    return pltpu.MemorySpace.HBM(dims, dtype)


def stay(*arrays):
    return [pltpu.with_memory_space_constraint(a, pltpu.MemorySpace.HBM) for a in arrays]


def scalar_first(grid, in_specs, out_specs, scratch=()):
    return dict(grid_spec=pltpu.PrefetchScalarGridSpec(
        num_scalar_prefetch=1, grid=grid, in_specs=in_specs, out_specs=out_specs, scratch_shapes=list(scratch)))


def full(*dims):
    return pl.BlockSpec(dims, lambda *_: (0,) * len(dims))


def pack_heads_kernel(core_ref, qkv_ref, vec_ref, heads_ref):
    for part in range(3):
        near = pl.ds(pl.multiple_of(640 * part + 256 * core_ref[0], 128), 256)
        heads_ref[:, 384 * part:384 * part + 256] = qkv_ref[:, near]
        heads_ref[:, 384 * part + 256:384 * (part + 1)] = qkv_ref[:, 640 * part + 512:640 * (part + 1)]
    heads_ref[:, 1152:1280] = vec_ref[...]


def pack_heads(core, w_qkv, vectors):
    return call(pack_heads_kernel, shape(160, 1280), "pack_heads", 10**6, 8, **scalar_first(
        (1,), [full(160, 1920), full(160, 128)], full(160, 1280)))(core, w_qkv, vectors)


def turn_kernel(vec_ref, rows_ref):
    rows_ref[...] = vec_ref[...].astype(f32).T[:16]


def vector_rows(heads):
    return call(turn_kernel, shape(16, 640, dtype=f32), "vector_rows", 10**6, 8, grid=(1,),
                in_specs=[pl.BlockSpec((640, 128), lambda i: (0, 9))], out_specs=full(16, 640))(heads)


def pack_feed_kernel(core_ref, out_ref, up_ref, down_ref, feed_ref):
    core = core_ref[0]
    feed_ref[:, 5120:5760] = out_ref[...]
    for f in range(4):
        feed_ref[:, 640 * f:640 * (f + 1)] = up_ref[:, pl.ds(pl.multiple_of(1280 * f + 640 * core, 128), 640)]
        feed_ref[:, 2560 + 640 * f:2560 + 640 * (f + 1)] = down_ref[pl.ds(pl.multiple_of(640 * core + 160 * f, 32), 160), :]


def pack_feed(core, w_out, w_up, w_down):
    return call(pack_feed_kernel, far(160, 5760), "pack_feed", 10**6, 16, **scalar_first(
        (1,), [full(160, 640), full(160, 5120), full(1280, 640)], full(160, 5760)))(core, *stay(w_out, w_up, w_down))


def rows_in_order(core, mine, theirs, x_ref):
    mine, theirs = mine.astype(f32), theirs.astype(f32)
    x_ref[0:256, :] = jnp.where(core == 0, mine, theirs)
    x_ref[256:512, :] = jnp.where(core == 0, theirs, mine)


def window_rows(core, own_refs, other_refs, m, block, x_ref):
    for j in range(len(own_refs)):
        @pl.when(block == j)
        def _():
            rows_in_order(core, own_refs[j][m], other_refs[j][m], x_ref)


def project_kernel(chips, place_ref, *refs):
    n = len(chips)
    own_refs, other_refs = refs[:n], refs[n:2 * n]
    vec_ref, w_ref = refs[2 * n:2 * n + 2]
    k_ref, v_ref, kT_ref, vT_ref = refs[-6 - 2 * (n == 3):][:4]
    x_ref, hid_ref = refs[-2:]
    m, step = pl.program_id(0), pl.program_id(1)
    block = sum(jnp.where(step == i, chip, 0) for i, chip in enumerate(chips))
    needed = (block >= place_ref[1 + 2 * m]) & (block < place_ref[2 + 2 * m])

    @pl.when(jnp.logical_not(needed))
    def _():
        for ref in (k_ref, v_ref, kT_ref, vT_ref):
            ref[...] = jnp.zeros_like(ref)

    @pl.when(needed)
    def _():
        window_rows(place_ref[0], own_refs, other_refs, m, step, x_ref)
        hidden = (moments(x_ref[...])[0] * vec_ref[0:1, :] + vec_ref[1:2, :]).astype(bf16)
        hid_ref[...] = hidden
        kv = jnp.dot(hidden, w_ref[:, 384:], preferred_element_type=f32)
        low = kv.astype(bf16)
        k_ref[0] = low[:, :384]
        v_ref[0] = low[:, 384:]
        turned = kv.T.astype(bf16)
        kT_ref[0] = turned[:384]
        vT_ref[0] = turned[384:]

    if n == 3:
        q_ref, qT_ref = refs[-4:-2]

        @pl.when(step == 1)
        def _():
            q = jnp.dot(hid_ref[...], w_ref[:, :384], preferred_element_type=f32)
            q_ref[0] = q.astype(bf16)
            qT_ref[0] = q.T.astype(bf16)


def project(chips, place, own, other, vec, w, earlier=()):
    n = len(chips)
    chip = (lambda b: b + 1) if n == 3 else (lambda b: 4 * b)
    tall = pl.BlockSpec((1, 512, 384), lambda m, b, *_: (m, chip(b), 0))
    wide = pl.BlockSpec((1, 384, 512), lambda m, b, *_: (m, 0, chip(b)))
    shapes = [far(2, 2560, 384), far(2, 2560, 384), far(2, 384, 2560), far(2, 384, 2560)]
    specs = [tall, tall, wide, wide]
    if n == 3:
        shapes += [far(2, 512, 384), far(2, 384, 512)]
        specs += [pl.BlockSpec((1, 512, 384), lambda m, *_: (m, 0, 0)), pl.BlockSpec((1, 384, 512), lambda m, *_: (m, 0, 0))]
    own, other = [own[c] for c in chips], [other[c] for c in chips]
    return call(
        lambda *refs: project_kernel(chips, *refs), shapes, "project", 5 * 10**9, 28,
        input_output_aliases={2 * n + 3 + i: i for i in range(len(earlier))}, **scalar_first(
            (2, n), [full(2, 256, 640)] * (2 * n) + [full(16, 640), full(640, 1152)] + [pl.BlockSpec(memory_space=pl.ANY)] * len(earlier),
            specs, [pltpu.VMEM((512, 640), f32), pltpu.VMEM((512, 640), bf16)]))(place, *own, *other, vec, *stay(w), *earlier)


def heads_joined(core, mine, theirs):
    first, second = (jnp.where(core == 0, a, b) for a, b in ((mine, theirs), (theirs, mine)))
    return jnp.concatenate([first[:, :256], second[:, :256], first[:, 256:] + second[:, 256:]], axis=1)


def middle_kernel(core_ref, w_ref, low0_ref, low1_ref, theirs_ref, tok_ref, tok2_ref, vec_ref, mid_ref, hid_ref, hid2_ref):
    core = core_ref[0]
    for m, low_ref in enumerate((low0_ref, low1_ref)):
        attended = heads_joined(core, low_ref[...].astype(f32), theirs_ref[m].astype(f32)).astype(bf16)
        branch = jnp.dot(attended, w_ref[...], preferred_element_type=f32)
        mine = jnp.where(core == 0, branch[:256], branch[256:]) + tok_ref[m].astype(f32)
        theirs = jnp.where(core == 0, branch[256:], branch[:256]) + tok2_ref[m].astype(f32)
        part = slice(256 * m, 256 * (m + 1))
        mid_ref[part, :] = mine
        hid_ref[part, :] = (moments(mine)[0] * vec_ref[2:3, :] + vec_ref[3:4, :]).astype(bf16)
        hid2_ref[part, :] = (moments(theirs)[0] * vec_ref[2:3, :] + vec_ref[3:4, :]).astype(bf16)


W_OUT = pl.BlockSpec((640, 640), lambda *_: (0, 8))


def middle_step(core, weights, *args):
    return call(middle_kernel, (far(512, 640, dtype=f32), far(512, 640), far(512, 640)), "middle", 10**9, 20, **scalar_first(
        (1,), [W_OUT] + [full(*a.shape) for a in args], [full(512, 640)] * 3))(core, *stay(weights), *args)


def feed_kernel(h_ref, h2_ref, cot_ref, cot2_ref, up_ref, down_ref, mine_ref, theirs_ref, g_ref, h, cot, hT, cT, out, dh):
    chunk = pl.program_id(0)

    @pl.when(chunk == 0)
    def _():
        h[0:512, :], h[512:1024, :] = h_ref[...], h2_ref[...]
        cot[0:512, :], cot[512:1024, :] = cot_ref[...], cot2_ref[...]
        hT[...] = h[...].astype(f32).T.astype(bf16)
        cT[...] = cot[...].astype(f32).T.astype(bf16)
        out[...] = jnp.zeros_like(out)
        dh[...] = jnp.zeros_like(dh)

    up_w = up_ref[...]
    down_w = jnp.concatenate([down_ref[160 * y:160 * (y + 1), 640 * i:640 * (i + 1)] for y in range(2) for i in range(4)], axis=0)
    acts, d_ups = [], []
    for t in range(4):
        rows = slice(256 * t, 256 * (t + 1))
        u = jnp.dot(h[rows, :], up_w, preferred_element_type=f32)
        d_act = lax.dot_general(cot[rows, :], down_w, NT, preferred_element_type=f32)
        cdf = 0.5 * (1.0 + lax.erf(u * (2.0 ** -0.5)))
        pdf = jnp.exp(u * u * -0.5) * ((2.0 * math.pi) ** -0.5)
        act = (u * cdf).astype(bf16)
        d_up = (d_act * (cdf + u * pdf)).astype(bf16)
        out[rows, :] += jnp.dot(act, down_w, preferred_element_type=f32)
        dh[rows, :] += lax.dot_general(d_up, up_w, NT, preferred_element_type=f32)
        acts.append(act)
        d_ups.append(d_up)
    g_up = jnp.dot(hT[...], jnp.concatenate(d_ups, axis=0), preferred_element_type=f32).astype(bf16)
    g_down = jnp.dot(cT[...], jnp.concatenate(acts, axis=0), preferred_element_type=f32).T.astype(bf16)
    for f in range(2):
        for y in range(4):
            for i in range(2):
                g_ref[y, 4 * chunk + 2 * f + i] = g_up[160 * y + 80 * i:160 * y + 80 * (i + 1), 640 * f:640 * (f + 1)]
        for i in range(8):
            g_ref[2 * chunk + f, 8 + i] = g_down[640 * f + 80 * i:640 * f + 80 * (i + 1)]

    @pl.when(chunk == 1)
    def _():
        mine_ref[0], mine_ref[1] = out[0:512, :].astype(bf16), dh[0:512, :].astype(bf16)
        theirs_ref[0], theirs_ref[1] = out[512:1024, :].astype(bf16), dh[512:1024, :].astype(bf16)


def feed_forward(h, h2, cot, cot2, weights):
    return call(
        feed_kernel,
        (far(2, 512, 640), far(2, 512, 640), far(4, 16, 80, 640)),
        "feed_forward", 30 * 10**9, 52, grid=(2,),
        in_specs=[full(512, 640)] * 4 + [pl.BlockSpec((640, 1280), lambda f: (0, f)), pl.BlockSpec((320, 2560), lambda f: (f, 1))],
        out_specs=[full(2, 512, 640), full(2, 512, 640), full(4, 16, 80, 640)],
        scratch_shapes=[pltpu.VMEM((1024, 640), bf16), pltpu.VMEM((1024, 640), bf16), pltpu.VMEM((640, 1024), bf16), pltpu.VMEM((640, 1024), bf16),
                        pltpu.VMEM((1024, 640), f32), pltpu.VMEM((1024, 640), f32)],
    )(*stay(h, h2, cot), cot2, *stay(weights, weights))


def after_kernel(mid_ref, mine_ref, theirs_ref, cot_ref, vec_ref, block_ref, grad_ref, branch_ref, g_ref):
    @pl.when(pl.program_id(0) == 0)
    def _():
        g_ref[...] = jnp.zeros_like(g_ref)

    middle = mid_ref[...]
    block_ref[...] = (middle + mine_ref[0].astype(f32) + theirs_ref[0].astype(f32)).astype(bf16)
    d_hidden = mine_ref[1].astype(f32) + theirs_ref[1].astype(f32)
    n, r = moments(middle)
    g_ref[0:1, :] += jnp.sum(d_hidden * n, axis=0, keepdims=True)
    g_ref[1:2, :] += jnp.sum(d_hidden, axis=0, keepdims=True)
    grad = cot_ref[...].astype(f32) + norm_back(d_hidden, n, r, vec_ref[2:3, :])
    grad_ref[...] = grad
    branch_ref[...] = grad.astype(bf16)


def after_feed(*args):
    rows, pair = pl.BlockSpec((128, 640), lambda i: (i, 0)), pl.BlockSpec((2, 128, 640), lambda i: (0, i, 0))
    return call(
        after_kernel, (far(512, 640), far(512, 640, dtype=f32), shape(512, 640), shape(8, 640, dtype=f32)), "after_feed", 10**9, 16,
        grid=(4,), in_specs=[rows, pair, pair, rows, full(16, 640)], out_specs=[rows, rows, rows, full(8, 640)])(*stay(args[0], args[1]), args[2], *stay(args[3]), args[4])


def branch_kernel(core_ref, own_ref, their_ref, w_ref, low0_ref, low1_ref, theirs_ref, do_ref, doT_ref, g_ref):
    core = core_ref[0]
    w = jnp.concatenate([w_ref[pl.ds(pl.multiple_of(256 * core, 256), 256), :], w_ref[512:640, :]], axis=0)
    g = jnp.zeros((640, 384), f32)
    for m in range(2):
        part = slice(256 * m, 256 * (m + 1))
        mine, theirs = own_ref[part, :].astype(f32), their_ref[part, :].astype(f32)
        branch = jnp.concatenate([jnp.where(core == 0, mine, theirs), jnp.where(core == 0, theirs, mine)], axis=0)
        kept = jnp.where(core == 0, branch[:, :384], branch[:, 256:]).astype(bf16)
        branch = branch.astype(bf16)
        rows = slice(512 * m, 512 * (m + 1))
        do = lax.dot_general(branch, w, NT, preferred_element_type=f32)
        do_ref[rows, :] = do.astype(bf16)
        doT_ref[:, rows] = do.T.astype(bf16)
        attended = heads_joined(core, (low0_ref, low1_ref)[m][...].astype(f32), theirs_ref[m].astype(f32))
        g = g + jnp.dot(attended.T.astype(bf16), kept, preferred_element_type=f32)
    g_ref[...] = g


def branch_step(core, own, their, weights, *args):
    return call(
        branch_kernel, (far(1024, 384), far(384, 1024), far(640, 384, dtype=f32)), "branch", 10**9, 24, **scalar_first(
            (1,), [full(512, 640)] * 2 + [W_OUT] + [full(*a.shape) for a in args], [full(1024, 384), full(384, 1024), full(640, 384)]))(
                core, own, their, *stay(weights), *args)


def project_back_kernel(core_ref, *refs):
    own_refs, other_refs = refs[:5], refs[5:10]
    (vec_ref, w_ref, dq0_ref, dq1_ref, dk0_ref, dk1_ref, dv0_ref, dv1_ref, g_out_ref, g_two_ref,
     mine_ref, theirs_ref, tail_ref, x_ref, d_kv, d_q, d_hid, g_ref, g_vec, slots, arrived) = refs[10:]
    step, core = pl.program_id(0), core_ref[0]
    block = lax.rem(step, 5)

    def copies(at, j, m, slot):
        for i, refs_of in enumerate((own_refs, other_refs)):
            getattr(pltpu.make_async_copy(refs_of[j].at[m], slots.at[slot, i], arrived.at[slot, i]), at)()

    def fetch(number):
        for j in range(5):
            for m in range(2):
                @pl.when(number == 5 * m + j)
                def _():
                    copies("start", j, m, lax.rem(number, 2))

    @pl.when(step == 0)
    def _():
        fetch(step)

    copies("wait", 0, 0, lax.rem(step, 2))

    @pl.when(step < 9)
    def _():
        fetch(step + 1)

    @pl.when(step == 0)
    def _():
        g_ref[...] = jnp.zeros_like(g_ref)
        g_vec[...] = jnp.zeros_like(g_vec)
        g_vec[2:4, :] = g_two_ref[0:2, :]

    second = lax.div(step, 5)
    needed = (block >= core_ref[1 + 2 * second]) & (block < core_ref[2 + 2 * second])

    @pl.when(jnp.logical_not(needed))
    def _():
        mine_ref[...] = jnp.zeros_like(mine_ref)
        theirs_ref[...] = jnp.zeros_like(theirs_ref)

    for m, (dq, dk, dv) in enumerate(((dq0_ref, dk0_ref, dv0_ref), (dq1_ref, dk1_ref, dv1_ref))):
        @pl.when(needed & (second == m))
        def _():
            rows_in_order(core, slots[lax.rem(step, 2), 0], slots[lax.rem(step, 2), 1], x_ref)
            d_kv[:, :384], d_kv[:, 384:] = dk[...], dv[...]
            d_q[...] = dq[...]

    @pl.when(needed)
    def _():
        n = moments(x_ref[...])[0]
        hiddenT = (n * vec_ref[0:1, :] + vec_ref[1:2, :]).T.astype(bf16)
        d_hid[...] = lax.dot_general(d_kv[...], w_ref[:, 384:], NT, preferred_element_type=f32)
        g_ref[:, 384:] += jnp.dot(hiddenT, d_kv[...], preferred_element_type=f32)

        @pl.when(block == 2)
        def _():
            g_ref[:, :384] += jnp.dot(hiddenT, d_q[...], preferred_element_type=f32)
            d_hid[...] += lax.dot_general(d_q[...], w_ref[:, :384], NT, preferred_element_type=f32)

        dh = d_hid[...]
        mine_ref[0, 0] = jnp.where(core == 0, dh[:256], dh[256:]).astype(bf16)
        theirs_ref[0, 0] = jnp.where(core == 0, dh[256:], dh[:256]).astype(bf16)
        g_vec[0:1, :] += jnp.sum(dh * n, axis=0, keepdims=True)
        g_vec[1:2, :] += jnp.sum(dh, axis=0, keepdims=True)

    @pl.when(step == 9)
    def _():
        turned = g_vec[...].T
        lane = lax.broadcasted_iota(jnp.int32, (640, 128), 1) - 64 * (1 - core)
        spare = g_ref[:, 256:384]
        for i in range(4):
            spare = jnp.where(lane == i, turned[:, i:i + 1], spare)
        g_ref[:, 256:384] = spare
        for y in range(4):
            for z in range(4):
                rows = slice(160 * y + 40 * z, 160 * y + 40 * (z + 1))
                for x in range(3):
                    tail_ref[16 * y + 4 * z + x] = g_ref[rows, 384 * x:384 * (x + 1)].astype(bf16)
                tail_ref[16 * y + 4 * z + 3] = g_out_ref[rows, :].astype(bf16)


def project_back(core, own, other, vec, w, dq, dk, dv, g_out, g_two):
    dq, dk, dv, (g_out,) = stay(*dq), stay(*dk), stay(*dv), stay(g_out)
    first = pl.BlockSpec((512, 384), lambda b, *_: (jnp.minimum(b, 4), 0))
    second = pl.BlockSpec((512, 384), lambda b, *_: (jnp.maximum(b - 5, 0), 0))
    return call(
        project_back_kernel, (far(5, 2, 256, 640), far(5, 2, 256, 640), far(64, 40, 384)), "project_back", 10**10, 36, **scalar_first(
            (10,), [pl.BlockSpec(memory_space=pl.ANY)] * 10 + [full(16, 640), full(640, 1152), full(512, 384), full(512, 384), first, second, first, second,
                                               full(640, 384), full(8, 640)],
            [pl.BlockSpec((1, 1, 256, 640), lambda b, *_: (lax.rem(b, 5), b // 5, 0, 0))] * 2 + [full(64, 40, 384)],
            [pltpu.VMEM((512, 640), f32), pltpu.VMEM((512, 768), bf16), pltpu.VMEM((512, 384), bf16),
             pltpu.VMEM((512, 640), f32), pltpu.VMEM((640, 1152), f32), pltpu.VMEM((8, 640), f32),
             pltpu.VMEM((2, 2, 256, 640), bf16), pltpu.SemaphoreType.DMA((2, 2))]))(core, *stay(*own, *other), vec, *stay(w), *dq, *dk, *dv, g_out, g_two)


def in_core_order(core_ref, mine, theirs):
    core, mine, theirs = core_ref[0], mine.astype(f32), theirs.astype(f32)
    return jnp.where(core == 0, mine, theirs), jnp.where(core == 0, theirs, mine)


def final_feed_kernel(core_ref, mine_ref, theirs_ref, up_ref, down_ref):
    for i in range(16):
        for c, piece in enumerate(in_core_order(core_ref, mine_ref[i], theirs_ref[i])):
            if i < 8:
                base = 1280 * (i // 2) + 640 * c
                up_ref[80 * (i % 2):80 * (i % 2 + 1), base:base + 640] = piece
            else:
                base = 640 * c + 80 * (i - 8)
                down_ref[base:base + 80, :] = piece


def final_feed(core, mine, theirs):
    return call(final_feed_kernel, (shape(160, 5120, dtype=f32), shape(1280, 640, dtype=f32)), "final_feed", 10**6, 32, **scalar_first(
        (1,), [full(16, 80, 640)] * 2, [full(160, 5120), full(1280, 640)]))(core, mine, theirs)


def final_heads_kernel(core_ref, mine_ref, theirs_ref, qkv_ref, out_ref, vec_ref):
    lane = lax.broadcasted_iota(jnp.int32, (40, 128), 1)
    for z in range(4):
        rows = slice(40 * z, 40 * (z + 1))
        for x in range(4):
            a, b = in_core_order(core_ref, mine_ref[4 * z + x], theirs_ref[4 * z + x])
            if x < 3:
                last = jnp.where(lane < 64, a[:, 256:], b[:, 256:])
                qkv_ref[rows, 640 * x:640 * (x + 1)] = jnp.concatenate([a[:, :256], b[:, :256], last], axis=1)
            else:
                out_ref[rows, :] = jnp.concatenate([a, b[:, 128:]], axis=1)
            if x == 0:
                vec_ref[rows, :] = pltpu.roll(a[:, 256:], 64, 1) + b[:, 256:]


def final_heads(core, mine, theirs):
    return call(
        final_heads_kernel, (shape(160, 1920, dtype=f32), shape(160, 640, dtype=f32), shape(160, 128, dtype=f32)), "final_heads", 10**6, 16,
        **scalar_first((1,), [full(16, 40, 384)] * 2, [full(160, 1920), full(160, 640), full(160, 128)]))(core, mine, theirs)


def shifted(array, axis, by):
    devices = lax.axis_size(axis)
    return lax.ppermute(array, axis, [(i, (i + by) % devices) for i in range(devices)])


def passed_along(array, by):
    devices = lax.axis_size(("z", "x"))
    return lax.ppermute(array, ("z", "x"), [(i, i + by) for i in range(devices) if 0 <= i + by < devices])


def swapped(array):
    return lax.ppermute(array, "core", [(0, 1), (1, 0)])


def pick(array, index):
    return lax.dynamic_index_in_dim(array, index, 0, keepdims=False)


def gathered(array, axis):
    me, devices = lax.axis_index(axis), lax.axis_size(axis)
    out = jnp.zeros((devices,) + array.shape, array.dtype)
    out = lax.dynamic_update_index_in_dim(out, array, me, 0)
    for by in (1, devices - 1, 2):
        out = lax.dynamic_update_index_in_dim(out, shifted(array, axis, by), (me + devices - by) % devices, 0)
    return out


def window_info(length_row, chip, core, win):
    ends = jnp.cumsum(length_row)
    starts = ends - length_row
    base = chip * 512 - 1024
    places = base + jnp.arange(win, dtype=jnp.int32)
    inside = (places[:, None] >= starts[None, :]) & (places[:, None] < ends[None, :])
    ones = jnp.broadcast_to(jnp.arange(64) < 3, (win, 64)).astype(bf16)
    key_rows = jnp.concatenate([jnp.where(inside, 0.0, -BIG).astype(bf16), ones], axis=1)
    own = chip * 512 + jnp.arange(512, dtype=jnp.int32)
    inside_q = (own[None, :] >= starts[:, None]) & (own[None, :] < ends[:, None])
    query_rows = jnp.concatenate([inside_q.astype(bf16), jnp.zeros((64, 512), bf16)], axis=0)
    info = [core]
    sizes = []
    for t in range(2):
        first = chip * 512 + t * TILE
        low = jnp.max(jnp.where(starts <= first, starts, 0)) - base
        high = jnp.min(jnp.where(ends > first + TILE - 1, ends, 1 << 30)) - base
        start = low // 128 * 128
        need = high - start
        size = (need + SHORT - 1) // SHORT * SHORT
        info.append(jnp.minimum(start, win - size))
        sizes.append(size)
    low = jnp.minimum(info[1], info[2]) // 512
    high = (jnp.maximum(info[1] + sizes[0], info[2] + sizes[1]) + 511) // 512
    return jnp.stack(info + sizes).astype(jnp.int32), key_rows, query_rows, [low, high]


def body(tokens, lengths, gain_one, bias_one, w_qkv, w_out, gain_two, bias_two, w_up, w_down, cotangent):
    core, chip = lax.axis_index("core"), lax.axis_index(("z", "x"))
    core_arg = core[None].astype(jnp.int32)
    tok, cot = tokens[:, 0], cotangent[:, 0].reshape(512, 640)
    together = lambda *arrays: lax.optimization_barrier(arrays)

    vectors = jnp.pad(jnp.stack([gain_one, bias_one, gain_two, bias_two], axis=1), ((0, 0), (0, 124)))
    heads, tok_sent = together(pack_heads(core_arg, w_qkv, vectors), tok)
    heads = lax.all_gather(heads, "batch", axis=0, tiled=True)
    before, after, tok_other = passed_along(tok_sent, 1), passed_along(tok_sent, -1), swapped(tok_sent)
    windows = [window_info(lengths[m, 0], chip, core, 2560) for m in range(2)]
    place = jnp.stack([core] + windows[0][3] + windows[1][3]).astype(jnp.int32)
    feed_pack = pack_feed(core_arg, w_out, w_up, w_down)
    before, after, tok_other, feed_pack, place, windows = together(before, after, tok_other, feed_pack, place, windows)
    own = [passed_along(before, 1), before, tok, after, passed_along(after, -1)]
    other = [None, swapped(before), tok_other, swapped(after), None]
    heads, feed_pack, own[0], own[4] = together(heads, feed_pack, own[0], own[4])
    feed_weights = lax.all_gather(feed_pack, "batch", axis=0, tiled=True)
    vec = vector_rows(heads)
    *near_parts, q, qT = project((1, 2, 3), place, own, other, vec, heads)
    own[0], own[4], near_parts = together(own[0], own[4], near_parts)
    other[0], other[4] = swapped(own[0]), swapped(own[4])
    k, v, kT, vT = project((0, 4), place, own, other, vec, heads, near_parts)
    (oT0, low0, lse0), (oT1, low1, lse1) = (
        attend(m, info, qT, k, vT, key_rows, query_rows) for m, (info, key_rows, query_rows, _) in enumerate(windows))

    theirs = swapped(jnp.stack([low0, low1]))
    middle, hidden_two, hidden_other = middle_step(core_arg, feed_weights, low0, low1, theirs, tok, tok_other, vec)
    mine, partial, feed_grads = feed_forward(hidden_two, hidden_other, cot, swapped(cot), feed_weights)
    feed_grads = lax.all_to_all(feed_grads.reshape(64, 80, 640), ("batch", "z", "x"), 0, 0, tiled=True)
    block_out, grad_middle, branch, g_two = after_feed(middle, mine, swapped(partial), cot, vec)

    do, doT, g_out = branch_step(core_arg, branch, swapped(branch), feed_weights, low0, low1, theirs)
    dq, dk, dv = zip(*(
        attend_back(m, info, qT, q, k, kT, v, doT, do, oT, lse, key_rows, query_rows)
        for m, ((info, key_rows, query_rows, _), oT, lse) in enumerate(zip(windows, (oT0, oT1), (lse0, lse1)))))
    mine, theirs, tail = project_back(place, own, other, vec, heads, dq, dk, dv, g_out, g_two)
    feed_grads, mine, theirs, tail = together(feed_grads, mine, theirs, tail)

    feed = jnp.sum(feed_grads.astype(f32), axis=0).astype(bf16)
    tail = lax.all_to_all(tail, ("batch", "z", "x"), 0, 0, tiled=True)
    feed = lax.all_gather(feed, ("z", "x"), axis=0, tiled=True).reshape(16, 80, 640)
    theirs = swapped(theirs)
    sums = [mine[j].astype(f32) + theirs[j].astype(f32) for j in range(5)]
    returned = [passed_along(sums[2 + by].astype(bf16), by) for by in (1, -1, 2, -2)]
    tail, sums[2] = together(tail, sums[2])
    tail = gathered(jnp.sum(tail.astype(f32), axis=0).astype(bf16), "x").reshape(160, 384)
    tail, returned[0], returned[1] = together(tail, returned[0], returned[1])
    tail = gathered(tail, "z").reshape(16, 40, 384)
    tail, returned = together(tail, returned)
    d_one = sum((part.astype(f32) for part in returned), sums[2]).reshape(512, 640)
    n_one, r_one = moments(tok.reshape(512, 640).astype(f32))
    grad_tokens = (grad_middle + norm_back(d_one, n_one, r_one, vec[0:1])).astype(bf16)
    tail, grad_tokens, feed = together(tail, grad_tokens, feed)
    grad_qkv, grad_out, spare = final_heads(core_arg, tail, swapped(tail))
    grad_up, grad_down = final_feed(core_arg, feed, swapped(feed))
    return (
        block_out.reshape(2, 1, 256, 640), grad_tokens.reshape(2, 1, 256, 640), spare[:, 0], spare[:, 1], grad_qkv, grad_out,
        spare[:, 2], spare[:, 3], grad_up, grad_down)


def solution(mesh):
    fine = Mesh(mesh.devices.reshape(4, 4, 4, 2), ("batch", "z", "x", "core"))
    rows = P(None, "batch", ("z", "x", "core"), None)
    one, two = P("batch"), P("batch", None)
    return jax.shard_map(
        body,
        mesh=fine,
        in_specs=(rows, P(None, "batch", None), one, one, two, two, one, one, two, two, rows),
        out_specs=(rows, rows, one, one, two, two, one, one, two, two),
        check_vma=False,
    )
```

```python
import math

import jax
import jax.numpy as jnp
from jax import lax
from jax.experimental import pallas as pl
from jax.experimental.pallas import tpu as pltpu
from jax.sharding import Mesh
from jax.sharding import PartitionSpec as P

HEAD_DIM = 32
SCALE = HEAD_DIM ** -0.5
LOG2E = math.log2(math.e)
C2 = SCALE * LOG2E
BIG = 1e30
TILE = 256
EPSILON = 1e-05
PAIRS = 5
SHORT, LONG = 384, 1152
f32, bf16 = jnp.float32, jnp.bfloat16
NT = (((1,), (1,)), ((), ()))


def pair_offset(info_ref):
    p = pl.program_id(0)
    sub = jnp.where(p == PAIRS - 1, info_ref[0], lax.rem(p, 2))
    return sub * (2 * HEAD_DIM)


def split3(v):
    a = v.astype(bf16)
    r = v - a.astype(f32)
    b = r.astype(bf16)
    d = (r - b.astype(f32)).astype(bf16)
    return a, b, d


def rows_masked(xT, off):
    row = lax.broadcasted_iota(jnp.int32, xT.shape, 0) - off
    xf = xT.astype(f32)
    return [jnp.where((row >= HEAD_DIM * j) & (row < HEAD_DIM * (j + 1)), xf, 0.0).astype(bf16) for j in range(2)]


def lanes_masked(x, off):
    lane = lax.broadcasted_iota(jnp.int32, x.shape, 1) - off
    xf = x.astype(f32)
    return [jnp.where((lane >= HEAD_DIM * j) & (lane < HEAD_DIM * (j + 1)), xf, 0.0).astype(bf16) for j in range(2)]


def attend_kernel(info_ref, qT_ref, k_ref, vT_ref, kaug_ref, qaugT_ref, oT_ref, o_ref, l_ref, rhs):
    off = pair_offset(info_ref)
    oT_ref[...] = jnp.where(lax.rem(pl.program_id(0), 2) == 0, 0.0, oT_ref[...])
    for t in range(2):
        cols = slice(t * TILE, (t + 1) * TILE)
        masked = rows_masked(qT_ref[:, cols], off)
        for j in range(2):
            rhs[0:128, j * TILE:(j + 1) * TILE] = masked[j]
            rhs[128:256, j * TILE:(j + 1) * TILE] = qaugT_ref[:, cols]
        start = info_ref[1 + t]
        need = info_ref[3 + t]

        def block(first, size):
            def step(i, carry):
                row = pl.multiple_of(first + i * size, 128)
                lhs = jnp.concatenate([k_ref[pl.ds(row, size), :], kaug_ref[pl.ds(row, size), :]], axis=1)
                raw = [jnp.dot(lhs, rhs[:, j * TILE:(j + 1) * TILE], preferred_element_type=f32) for j in range(2)]
                out = []
                for j in range(2):
                    m, l, o = carry[j]
                    s = raw[j] * C2
                    m_new = jnp.maximum(m, jnp.max(s, axis=0, keepdims=True))
                    alpha = jnp.exp2(m - m_new)
                    p = jnp.exp2(s - m_new)
                    vT = vT_ref[pl.ds(pl.multiple_of(off + j * HEAD_DIM, HEAD_DIM), HEAD_DIM), pl.ds(row, size)]
                    out.append((m_new, l * alpha + jnp.sum(p, axis=0, keepdims=True),
                                o * alpha + jnp.dot(vT, p.astype(bf16), preferred_element_type=f32)))
                return tuple(out)
            return step

        def finish(state):
            for j in range(2):
                m, l, o = state[j]
                oT_ref[pl.ds(pl.multiple_of(off + j * HEAD_DIM, HEAD_DIM), HEAD_DIM), cols] = o * (1.0 / l)
                l_ref[0, j:j + 1, cols] = m + jnp.log2(l)

        init = tuple((jnp.full((1, TILE), -1e38, f32), jnp.zeros((1, TILE), f32), jnp.zeros((HEAD_DIM, TILE), f32)) for _ in range(2))

        longs = lax.div(need, LONG)
        state = lax.fori_loop(0, longs, block(start, LONG), init)
        finish(lax.fori_loop(0, lax.div(need - longs * LONG, SHORT), block(start + longs * LONG, SHORT), state))

    o_ref[...] = oT_ref[...].T.astype(bf16)


def attend(m, info, qT, k, vT, kaug, qaugT):
    win, nq = k.shape[1], qT.shape[2]
    qT, k, vT = stay(qT, k, vT)
    return pl.pallas_call(
        attend_kernel,
        out_shape=(jax.ShapeDtypeStruct((384, nq), f32), jax.ShapeDtypeStruct((nq, 384), bf16), jax.ShapeDtypeStruct((PAIRS, 8, nq), f32)),
        grid_spec=pltpu.PrefetchScalarGridSpec(
            num_scalar_prefetch=1, grid=(PAIRS,),
            in_specs=[
                pl.BlockSpec((None, 128, nq), lambda p, *_: (m, p // 2, 0)),
                pl.BlockSpec((None, win, 128), lambda p, *_: (m, 0, p // 2)),
                pl.BlockSpec((None, 128, win), lambda p, *_: (m, p // 2, 0)),
                pl.BlockSpec((win, 128), lambda p, *_: (0, 0)),
                pl.BlockSpec((128, nq), lambda p, *_: (0, 0)),
            ],
            out_specs=[
                pl.BlockSpec((128, nq), lambda p, *_: (p // 2, 0)),
                pl.BlockSpec((nq, 128), lambda p, *_: (0, p // 2)),
                pl.BlockSpec((1, 8, nq), lambda p, *_: (p, 0, 0)),
            ],
            scratch_shapes=[pltpu.VMEM((256, 2 * TILE), bf16)],
        ),
        compiler_params=pltpu.CompilerParams(vmem_limit_bytes=28 << 20),
        cost_estimate=pl.CostEstimate(flops=int(20 * 10**9 * 0.02), bytes_accessed=0, transcendentals=0),
        name="attend",
    )(info, qT, k, vT, kaug, qaugT)


def attend_back_kernel(info_ref, qT_ref, q_ref, k_ref, kT_ref, v_ref, doT_ref, do_ref, oT_ref, l_ref, kaug_ref, qaugT_ref,
                       dq_ref, dk_ref, dv_ref, dqT_ref, rhs_s, rhs_d, q_stk, do_stk, dk_acc, dv_acc):
    p_id = pl.program_id(0)
    off = pair_offset(info_ref)

    @pl.when(lax.rem(p_id, 2) == 0)
    def _():
        dqT_ref[...] = jnp.zeros_like(dqT_ref)
        dk_acc[...] = jnp.zeros_like(dk_acc)
        dv_acc[...] = jnp.zeros_like(dv_acc)

    for t in range(2):
        cols = slice(t * TILE, (t + 1) * TILE)
        masked_q = rows_masked(qT_ref[:, cols], off)
        masked_do = rows_masked(doT_ref[:, cols], off)
        lane_q = lanes_masked(q_ref[cols, :], off)
        lane_do = lanes_masked(do_ref[cols, :], off)
        for j in range(2):
            part = slice(j * TILE, (j + 1) * TILE)
            head = pl.ds(pl.multiple_of(off + j * HEAD_DIM, HEAD_DIM), HEAD_DIM)
            delta = jnp.sum(doT_ref[head, cols].astype(f32) * oT_ref[head, cols], axis=0, keepdims=True)
            total = l_ref[0, j:j + 1, cols] * (1.0 / C2)
            rowid = lax.broadcasted_iota(jnp.int32, (64, TILE), 0)
            lp, dp = split3(-total), split3(-delta)
            def pieces(parts):
                x = jnp.zeros((64, TILE), f32)
                for n in range(3):
                    x = jnp.where(rowid == n, parts[n].astype(f32), x)
                return x.astype(bf16)
            rhs_s[0:128, part] = masked_q[j]
            rhs_s[128:192, part] = qaugT_ref[0:64, cols]
            rhs_s[192:256, part] = pieces(lp)
            rhs_d[0:128, part] = masked_do[j]
            rhs_d[128:192, part] = jnp.zeros((64, TILE), bf16)
            rhs_d[192:256, part] = pieces(dp)
            q_stk[part, :] = lane_q[j]
            do_stk[part, :] = lane_do[j]
        start = info_ref[1 + t]
        need = info_ref[3 + t]

        def block(first, size):
            def step(i, carry):
                row = pl.multiple_of(first + i * size, 128)
                rows = pl.ds(row, size)
                aug = kaug_ref[rows, :]
                lhs_k = jnp.concatenate([k_ref[rows, :], aug], axis=1)
                lhs_v = jnp.concatenate([v_ref[rows, :], aug], axis=1)
                out, dv, dk = [], dv_acc[rows, :], dk_acc[rows, :]
                for j in range(2):
                    part = slice(j * TILE, (j + 1) * TILE)
                    s = jnp.dot(lhs_k, rhs_s[:, part], preferred_element_type=f32)
                    dp = jnp.dot(lhs_v, rhs_d[:, part], preferred_element_type=f32)
                    p = jnp.exp2(s * C2)
                    ds = (p * dp).astype(bf16)
                    dv = dv + jnp.dot(p.astype(bf16), do_stk[part, :], preferred_element_type=f32)
                    dk = dk + jnp.dot(ds, q_stk[part, :], preferred_element_type=f32)
                    kT = kT_ref[pl.ds(pl.multiple_of(off + j * HEAD_DIM, HEAD_DIM), HEAD_DIM), rows]
                    out.append(carry[j] + jnp.dot(kT, ds, preferred_element_type=f32))
                dv_acc[rows, :] = dv
                dk_acc[rows, :] = dk
                return tuple(out)
            return step

        def finish(dqs):
            for j in range(2):
                dqT_ref[pl.ds(pl.multiple_of(off + j * HEAD_DIM, HEAD_DIM), HEAD_DIM), cols] = dqs[j] * SCALE

        init = tuple(jnp.zeros((HEAD_DIM, TILE), f32) for _ in range(2))

        longs = lax.div(need, LONG)
        state = lax.fori_loop(0, longs, block(start, LONG), init)
        finish(lax.fori_loop(0, lax.div(need - longs * LONG, SHORT), block(start + longs * LONG, SHORT), state))
    @pl.when((lax.rem(p_id, 2) == 1) | (p_id == PAIRS - 1))
    def _():
        dq_ref[...] = dqT_ref[...].T.astype(bf16)
        dk_ref[...] = (dk_acc[...] * SCALE).astype(bf16)
        dv_ref[...] = dv_acc[...].astype(bf16)


def attend_back(m, info, qT, q, k, kT, v, doT, do, oT, lse, kaug, qaugT):
    win, nq = k.shape[1], qT.shape[2]
    qT, q, k, kT, v, doT, do = stay(qT, q, k, kT, v, doT, do)
    wide = pl.BlockSpec((128, nq), lambda p, *_: (p // 2, 0))
    tall = pl.BlockSpec((nq, 128), lambda p, *_: (0, p // 2))
    keys = pl.BlockSpec((win, 128), lambda p, *_: (0, p // 2))
    wide_m = pl.BlockSpec((None, 128, nq), lambda p, *_: (m, p // 2, 0))
    tall_m = pl.BlockSpec((None, nq, 128), lambda p, *_: (m, 0, p // 2))
    keys_m = pl.BlockSpec((None, win, 128), lambda p, *_: (m, 0, p // 2))
    return pl.pallas_call(
        attend_back_kernel,
        out_shape=(far(nq, 384), far(win, 384), far(win, 384)),
        grid_spec=pltpu.PrefetchScalarGridSpec(
            num_scalar_prefetch=1, grid=(PAIRS,),
            in_specs=[wide_m, tall_m, keys_m, pl.BlockSpec((None, 128, win), lambda p, *_: (m, p // 2, 0)), keys_m,
                      pl.BlockSpec((128, nq), lambda p, *_: (p // 2, m)), pl.BlockSpec((nq, 128), lambda p, *_: (m, p // 2)), wide,
                      pl.BlockSpec((1, 8, nq), lambda p, *_: (p, 0, 0)),
                      pl.BlockSpec((win, 128), lambda p, *_: (0, 0)), pl.BlockSpec((128, nq), lambda p, *_: (0, 0))],
            out_specs=[tall, keys, keys],
            scratch_shapes=[pltpu.VMEM((128, nq), f32), pltpu.VMEM((256, 2 * TILE), bf16), pltpu.VMEM((256, 2 * TILE), bf16),
                            pltpu.VMEM((2 * TILE, 128), bf16), pltpu.VMEM((2 * TILE, 128), bf16),
                            pltpu.VMEM((win, 128), f32), pltpu.VMEM((win, 128), f32)],
        ),
        compiler_params=pltpu.CompilerParams(vmem_limit_bytes=32 << 20),
        cost_estimate=pl.CostEstimate(flops=int(40 * 10**9 * 0.02), bytes_accessed=0, transcendentals=0),
        name="attend_back",
    )(info, qT, q, k, kT, v, doT, do, oT, lse, kaug, qaugT)


def moments(x):
    centred = x - jnp.mean(x, axis=-1, keepdims=True)
    r = lax.rsqrt(jnp.mean(centred * centred, axis=-1, keepdims=True) + EPSILON)
    return centred * r, r


def norm_back(grad, n, r, gain):
    e = grad * gain
    return r * (e - jnp.mean(e, axis=-1, keepdims=True) - n * jnp.mean(e * n, axis=-1, keepdims=True))


def call(kernel, out_shape, name, flops=10**9, limit=48, **spec):
    return pl.pallas_call(
        kernel, out_shape=out_shape, name=name,
        compiler_params=pltpu.CompilerParams(vmem_limit_bytes=limit << 20),
        cost_estimate=pl.CostEstimate(flops=int(flops * 0.02), bytes_accessed=0, transcendentals=0), **spec)


def shape(*dims, dtype=bf16):
    return jax.ShapeDtypeStruct(dims, dtype)


def far(*dims, dtype=bf16):
    return pltpu.MemorySpace.HBM(dims, dtype)


def stay(*arrays):
    return [pltpu.with_memory_space_constraint(a, pltpu.MemorySpace.HBM) for a in arrays]


def scalar_first(grid, in_specs, out_specs, scratch=()):
    return dict(grid_spec=pltpu.PrefetchScalarGridSpec(
        num_scalar_prefetch=1, grid=grid, in_specs=in_specs, out_specs=out_specs, scratch_shapes=list(scratch)))


def full(*dims):
    return pl.BlockSpec(dims, lambda *_: (0,) * len(dims))


def pack_heads_kernel(core_ref, qkv_ref, vec_ref, heads_ref):
    for part in range(3):
        near = pl.ds(pl.multiple_of(640 * part + 256 * core_ref[0], 128), 256)
        heads_ref[:, 384 * part:384 * part + 256] = qkv_ref[:, near]
        heads_ref[:, 384 * part + 256:384 * (part + 1)] = qkv_ref[:, 640 * part + 512:640 * (part + 1)]
    heads_ref[:, 1152:1280] = vec_ref[...]


def pack_heads(core, w_qkv, vectors):
    return call(pack_heads_kernel, shape(160, 1280), "pack_heads", 10**6, 8, **scalar_first(
        (1,), [full(160, 1920), full(160, 128)], full(160, 1280)))(core, w_qkv, vectors)


def turn_kernel(vec_ref, rows_ref):
    rows_ref[...] = vec_ref[...].astype(f32).T[:16]


def vector_rows(heads):
    return call(turn_kernel, shape(16, 640, dtype=f32), "vector_rows", 10**6, 8, grid=(1,),
                in_specs=[pl.BlockSpec((640, 128), lambda i: (0, 9))], out_specs=full(16, 640))(*stay(heads))


def pack_feed_kernel(core_ref, out_ref, up_ref, down_ref, feed_ref):
    core = core_ref[0]
    feed_ref[:, 5120:5760] = out_ref[...]
    for f in range(4):
        feed_ref[:, 640 * f:640 * (f + 1)] = up_ref[:, pl.ds(pl.multiple_of(1280 * f + 640 * core, 128), 640)]
        feed_ref[:, 2560 + 640 * f:2560 + 640 * (f + 1)] = down_ref[pl.ds(pl.multiple_of(640 * core + 160 * f, 32), 160), :]


def pack_feed(core, w_out, w_up, w_down):
    return call(pack_feed_kernel, far(160, 5760), "pack_feed", 10**6, 16, **scalar_first(
        (1,), [full(160, 640), full(160, 5120), full(1280, 640)], full(160, 5760)))(core, *stay(w_out, w_up, w_down))


def rows_in_order(core, mine, theirs, x_ref):
    mine, theirs = mine.astype(f32), theirs.astype(f32)
    x_ref[0:256, :] = jnp.where(core == 0, mine, theirs)
    x_ref[256:512, :] = jnp.where(core == 0, theirs, mine)


def window_rows(core, own_refs, other_refs, m, block, x_ref):
    for j in range(len(own_refs)):
        @pl.when(block == j)
        def _():
            rows_in_order(core, own_refs[j][m], other_refs[j][m], x_ref)


def project_kernel(chips, place_ref, *refs):
    n = len(chips)
    own_refs, other_refs = refs[:n], refs[n:2 * n]
    vec_ref, w_ref = refs[2 * n:2 * n + 2]
    k_ref, v_ref, kT_ref, vT_ref = refs[-6 - 2 * (n == 3):][:4]
    x_ref, hid_ref = refs[-2:]
    m, step = pl.program_id(0), pl.program_id(1)
    block = sum(jnp.where(step == i, chip, 0) for i, chip in enumerate(chips))
    needed = (block >= place_ref[1 + 2 * m]) & (block < place_ref[2 + 2 * m])

    @pl.when(jnp.logical_not(needed))
    def _():
        for ref in (k_ref, v_ref, kT_ref, vT_ref):
            ref[...] = jnp.zeros_like(ref)

    @pl.when(needed)
    def _():
        window_rows(place_ref[0], own_refs, other_refs, m, step, x_ref)
        hidden = (moments(x_ref[...])[0] * vec_ref[0:1, :] + vec_ref[1:2, :]).astype(bf16)
        hid_ref[...] = hidden
        kv = jnp.dot(hidden, w_ref[:, 384:], preferred_element_type=f32)
        low = kv.astype(bf16)
        k_ref[0] = low[:, :384]
        v_ref[0] = low[:, 384:]
        turned = kv.T.astype(bf16)
        kT_ref[0] = turned[:384]
        vT_ref[0] = turned[384:]

    if n == 3:
        q_ref, qT_ref = refs[-4:-2]

        @pl.when(step == 1)
        def _():
            q = jnp.dot(hid_ref[...], w_ref[:, :384], preferred_element_type=f32)
            q_ref[0] = q.astype(bf16)
            qT_ref[0] = q.T.astype(bf16)


def project(chips, place, own, other, vec, w, earlier=()):
    n = len(chips)
    chip = (lambda b: b + 1) if n == 3 else (lambda b: 4 * b)
    tall = pl.BlockSpec((1, 512, 384), lambda m, b, *_: (m, chip(b), 0))
    wide = pl.BlockSpec((1, 384, 512), lambda m, b, *_: (m, 0, chip(b)))
    shapes = [far(2, 2560, 384), far(2, 2560, 384), far(2, 384, 2560), far(2, 384, 2560)]
    specs = [tall, tall, wide, wide]
    if n == 3:
        shapes += [far(2, 512, 384), far(2, 384, 512)]
        specs += [pl.BlockSpec((1, 512, 384), lambda m, *_: (m, 0, 0)), pl.BlockSpec((1, 384, 512), lambda m, *_: (m, 0, 0))]
    own, other = [own[c] for c in chips], [other[c] for c in chips]
    return call(
        lambda *refs: project_kernel(chips, *refs), shapes, "project", 5 * 10**9, 28,
        input_output_aliases={2 * n + 3 + i: i for i in range(len(earlier))}, **scalar_first(
            (2, n), [full(2, 256, 640)] * (2 * n) + [full(16, 640), full(640, 1152)] + [pl.BlockSpec(memory_space=pl.ANY)] * len(earlier),
            specs, [pltpu.VMEM((512, 640), f32), pltpu.VMEM((512, 640), bf16)]))(place, *own, *other, vec, *stay(w), *earlier)


def heads_joined(core, mine, theirs):
    first, second = (jnp.where(core == 0, a, b) for a, b in ((mine, theirs), (theirs, mine)))
    return jnp.concatenate([first[:, :256], second[:, :256], first[:, 256:] + second[:, 256:]], axis=1)


def middle_kernel(core_ref, w_ref, low0_ref, low1_ref, theirs_ref, tok_ref, tok2_ref, vec_ref, mid_ref, hid_ref, hid2_ref):
    core = core_ref[0]
    for m, low_ref in enumerate((low0_ref, low1_ref)):
        attended = heads_joined(core, low_ref[...].astype(f32), theirs_ref[m].astype(f32)).astype(bf16)
        branch = jnp.dot(attended, w_ref[...], preferred_element_type=f32)
        mine = jnp.where(core == 0, branch[:256], branch[256:]) + tok_ref[m].astype(f32)
        theirs = jnp.where(core == 0, branch[256:], branch[:256]) + tok2_ref[m].astype(f32)
        part = slice(256 * m, 256 * (m + 1))
        mid_ref[part, :] = mine
        hid_ref[part, :] = (moments(mine)[0] * vec_ref[2:3, :] + vec_ref[3:4, :]).astype(bf16)
        hid2_ref[part, :] = (moments(theirs)[0] * vec_ref[2:3, :] + vec_ref[3:4, :]).astype(bf16)


W_OUT = pl.BlockSpec((640, 640), lambda *_: (0, 8))


def middle_step(core, weights, *args):
    return call(middle_kernel, (far(512, 640, dtype=f32), far(512, 640), far(512, 640)), "middle", 10**9, 20, **scalar_first(
        (1,), [W_OUT] + [full(*a.shape) for a in args], [full(512, 640)] * 3))(core, *stay(weights), *args)


def feed_kernel(h_ref, h2_ref, cot_ref, cot2_ref, up_ref, down_ref, mine_ref, theirs_ref, g_ref, h, cot, hT, cT, out, dh):
    chunk = pl.program_id(0)

    @pl.when(chunk == 0)
    def _():
        h[0:512, :], h[512:1024, :] = h_ref[...], h2_ref[...]
        cot[0:512, :], cot[512:1024, :] = cot_ref[...], cot2_ref[...]
        hT[...] = h[...].astype(f32).T.astype(bf16)
        cT[...] = cot[...].astype(f32).T.astype(bf16)
        out[...] = jnp.zeros_like(out)
        dh[...] = jnp.zeros_like(dh)

    up_w = up_ref[...]
    down_w = jnp.concatenate([down_ref[160 * y:160 * (y + 1), 640 * i:640 * (i + 1)] for y in range(2) for i in range(4)], axis=0)
    acts, d_ups = [], []
    for t in range(4):
        rows = slice(256 * t, 256 * (t + 1))
        u = jnp.dot(h[rows, :], up_w, preferred_element_type=f32)
        d_act = lax.dot_general(cot[rows, :], down_w, NT, preferred_element_type=f32)
        cdf = 0.5 * (1.0 + lax.erf(u * (2.0 ** -0.5)))
        pdf = jnp.exp(u * u * -0.5) * ((2.0 * math.pi) ** -0.5)
        act = (u * cdf).astype(bf16)
        d_up = (d_act * (cdf + u * pdf)).astype(bf16)
        out[rows, :] += jnp.dot(act, down_w, preferred_element_type=f32)
        dh[rows, :] += lax.dot_general(d_up, up_w, NT, preferred_element_type=f32)
        acts.append(act)
        d_ups.append(d_up)
    g_up = jnp.dot(hT[...], jnp.concatenate(d_ups, axis=0), preferred_element_type=f32).astype(bf16)
    g_down = jnp.dot(cT[...], jnp.concatenate(acts, axis=0), preferred_element_type=f32).T.astype(bf16)
    for f in range(2):
        for y in range(4):
            for i in range(2):
                g_ref[y, 4 * chunk + 2 * f + i] = g_up[160 * y + 80 * i:160 * y + 80 * (i + 1), 640 * f:640 * (f + 1)]
        for i in range(8):
            g_ref[2 * chunk + f, 8 + i] = g_down[640 * f + 80 * i:640 * f + 80 * (i + 1)]

    @pl.when(chunk == 1)
    def _():
        mine_ref[0], mine_ref[1] = out[0:512, :].astype(bf16), dh[0:512, :].astype(bf16)
        theirs_ref[0], theirs_ref[1] = out[512:1024, :].astype(bf16), dh[512:1024, :].astype(bf16)


def feed_forward(h, h2, cot, cot2, weights):
    return call(
        feed_kernel,
        (far(2, 512, 640), far(2, 512, 640), far(4, 16, 80, 640)),
        "feed_forward", 30 * 10**9, 52, grid=(2,),
        in_specs=[full(512, 640)] * 4 + [pl.BlockSpec((640, 1280), lambda f: (0, f)), pl.BlockSpec((320, 2560), lambda f: (f, 1))],
        out_specs=[full(2, 512, 640), full(2, 512, 640), full(4, 16, 80, 640)],
        scratch_shapes=[pltpu.VMEM((1024, 640), bf16), pltpu.VMEM((1024, 640), bf16), pltpu.VMEM((640, 1024), bf16), pltpu.VMEM((640, 1024), bf16),
                        pltpu.VMEM((1024, 640), f32), pltpu.VMEM((1024, 640), f32)],
    )(*stay(h, h2, cot), cot2, *stay(weights, weights))


def after_kernel(mid_ref, mine_ref, theirs_ref, cot_ref, vec_ref, block_ref, grad_ref, branch_ref, g_ref):
    @pl.when(pl.program_id(0) == 0)
    def _():
        g_ref[...] = jnp.zeros_like(g_ref)

    middle = mid_ref[...]
    block_ref[...] = (middle + mine_ref[0].astype(f32) + theirs_ref[0].astype(f32)).astype(bf16)
    d_hidden = mine_ref[1].astype(f32) + theirs_ref[1].astype(f32)
    n, r = moments(middle)
    g_ref[0:1, :] += jnp.sum(d_hidden * n, axis=0, keepdims=True)
    g_ref[1:2, :] += jnp.sum(d_hidden, axis=0, keepdims=True)
    grad = cot_ref[...].astype(f32) + norm_back(d_hidden, n, r, vec_ref[2:3, :])
    grad_ref[...] = grad
    branch_ref[...] = grad.astype(bf16)


def after_feed(*args):
    rows, pair = pl.BlockSpec((128, 640), lambda i: (i, 0)), pl.BlockSpec((2, 128, 640), lambda i: (0, i, 0))
    return call(
        after_kernel, (far(512, 640), far(512, 640, dtype=f32), shape(512, 640), shape(8, 640, dtype=f32)), "after_feed", 10**9, 16,
        grid=(4,), in_specs=[rows, pair, pair, rows, full(16, 640)], out_specs=[rows, rows, rows, full(8, 640)])(*stay(args[0], args[1]), args[2], *stay(args[3]), args[4])


def branch_kernel(core_ref, own_ref, their_ref, w_ref, low0_ref, low1_ref, theirs_ref, do_ref, doT_ref, g_ref):
    core = core_ref[0]
    w = jnp.concatenate([w_ref[pl.ds(pl.multiple_of(256 * core, 256), 256), :], w_ref[512:640, :]], axis=0)
    g = jnp.zeros((640, 384), f32)
    for m in range(2):
        part = slice(256 * m, 256 * (m + 1))
        mine, theirs = own_ref[part, :].astype(f32), their_ref[part, :].astype(f32)
        branch = jnp.concatenate([jnp.where(core == 0, mine, theirs), jnp.where(core == 0, theirs, mine)], axis=0)
        kept = jnp.where(core == 0, branch[:, :384], branch[:, 256:]).astype(bf16)
        branch = branch.astype(bf16)
        rows = slice(512 * m, 512 * (m + 1))
        do = lax.dot_general(branch, w, NT, preferred_element_type=f32)
        do_ref[rows, :] = do.astype(bf16)
        doT_ref[:, rows] = do.T.astype(bf16)
        attended = heads_joined(core, (low0_ref, low1_ref)[m][...].astype(f32), theirs_ref[m].astype(f32))
        g = g + jnp.dot(attended.T.astype(bf16), kept, preferred_element_type=f32)
    g_ref[...] = g


def branch_step(core, own, their, weights, *args):
    return call(
        branch_kernel, (far(1024, 384), far(384, 1024), far(640, 384, dtype=f32)), "branch", 10**9, 24, **scalar_first(
            (1,), [full(512, 640)] * 2 + [W_OUT] + [full(*a.shape) for a in args], [full(1024, 384), full(384, 1024), full(640, 384)]))(
                core, own, their, *stay(weights), *args)


def project_back_kernel(core_ref, *refs):
    own_refs, other_refs = refs[:5], refs[5:10]
    (vec_ref, w_ref, dq0_ref, dq1_ref, dk0_ref, dk1_ref, dv0_ref, dv1_ref, g_out_ref, g_two_ref,
     mine_ref, theirs_ref, tail_ref, x_ref, d_kv, d_q, d_hid, g_ref, g_vec, slots, arrived) = refs[10:]
    step, core = pl.program_id(0), core_ref[0]
    block = lax.rem(step, 5)

    def copies(at, j, m, slot):
        for i, refs_of in enumerate((own_refs, other_refs)):
            getattr(pltpu.make_async_copy(refs_of[j].at[m], slots.at[slot, i], arrived.at[slot, i]), at)()

    def fetch(number):
        for j in range(5):
            for m in range(2):
                @pl.when(number == 5 * m + j)
                def _():
                    copies("start", j, m, lax.rem(number, 2))

    @pl.when(step == 0)
    def _():
        fetch(step)

    copies("wait", 0, 0, lax.rem(step, 2))

    @pl.when(step < 9)
    def _():
        fetch(step + 1)

    @pl.when(step == 0)
    def _():
        g_ref[...] = jnp.zeros_like(g_ref)
        g_vec[...] = jnp.zeros_like(g_vec)
        g_vec[2:4, :] = g_two_ref[0:2, :]

    second = lax.div(step, 5)
    needed = (block >= core_ref[1 + 2 * second]) & (block < core_ref[2 + 2 * second])

    @pl.when(jnp.logical_not(needed))
    def _():
        mine_ref[...] = jnp.zeros_like(mine_ref)
        theirs_ref[...] = jnp.zeros_like(theirs_ref)

    for m, (dq, dk, dv) in enumerate(((dq0_ref, dk0_ref, dv0_ref), (dq1_ref, dk1_ref, dv1_ref))):
        @pl.when(needed & (second == m))
        def _():
            rows_in_order(core, slots[lax.rem(step, 2), 0], slots[lax.rem(step, 2), 1], x_ref)
            d_kv[:, :384], d_kv[:, 384:] = dk[...], dv[...]
            d_q[...] = dq[...]

    @pl.when(needed)
    def _():
        n = moments(x_ref[...])[0]
        hiddenT = (n * vec_ref[0:1, :] + vec_ref[1:2, :]).T.astype(bf16)
        d_hid[...] = lax.dot_general(d_kv[...], w_ref[:, 384:], NT, preferred_element_type=f32)
        g_ref[:, 384:] += jnp.dot(hiddenT, d_kv[...], preferred_element_type=f32)

        @pl.when(block == 2)
        def _():
            g_ref[:, :384] += jnp.dot(hiddenT, d_q[...], preferred_element_type=f32)
            d_hid[...] += lax.dot_general(d_q[...], w_ref[:, :384], NT, preferred_element_type=f32)

        dh = d_hid[...]
        mine_ref[0, 0] = jnp.where(core == 0, dh[:256], dh[256:]).astype(bf16)
        theirs_ref[0, 0] = jnp.where(core == 0, dh[256:], dh[:256]).astype(bf16)
        g_vec[0:1, :] += jnp.sum(dh * n, axis=0, keepdims=True)
        g_vec[1:2, :] += jnp.sum(dh, axis=0, keepdims=True)

    @pl.when(step == 9)
    def _():
        turned = g_vec[...].T
        lane = lax.broadcasted_iota(jnp.int32, (640, 128), 1) - 64 * (1 - core)
        spare = g_ref[:, 256:384]
        for i in range(4):
            spare = jnp.where(lane == i, turned[:, i:i + 1], spare)
        g_ref[:, 256:384] = spare
        for y in range(4):
            for z in range(4):
                rows = slice(160 * y + 40 * z, 160 * y + 40 * (z + 1))
                for x in range(3):
                    tail_ref[16 * y + 4 * z + x] = g_ref[rows, 384 * x:384 * (x + 1)].astype(bf16)
                tail_ref[16 * y + 4 * z + 3] = g_out_ref[rows, :].astype(bf16)


def project_back(core, own, other, vec, w, dq, dk, dv, g_out, g_two):
    dq, dk, dv, (g_out,) = stay(*dq), stay(*dk), stay(*dv), stay(g_out)
    first = pl.BlockSpec((512, 384), lambda b, *_: (jnp.minimum(b, 4), 0))
    second = pl.BlockSpec((512, 384), lambda b, *_: (jnp.maximum(b - 5, 0), 0))
    return call(
        project_back_kernel, (far(5, 2, 256, 640), far(5, 2, 256, 640), far(64, 40, 384)), "project_back", 10**10, 36, **scalar_first(
            (10,), [pl.BlockSpec(memory_space=pl.ANY)] * 10 + [full(16, 640), full(640, 1152), full(512, 384), full(512, 384), first, second, first, second,
                                               full(640, 384), full(8, 640)],
            [pl.BlockSpec((1, 1, 256, 640), lambda b, *_: (lax.rem(b, 5), b // 5, 0, 0))] * 2 + [full(64, 40, 384)],
            [pltpu.VMEM((512, 640), f32), pltpu.VMEM((512, 768), bf16), pltpu.VMEM((512, 384), bf16),
             pltpu.VMEM((512, 640), f32), pltpu.VMEM((640, 1152), f32), pltpu.VMEM((8, 640), f32),
             pltpu.VMEM((2, 2, 256, 640), bf16), pltpu.SemaphoreType.DMA((2, 2))]))(core, *stay(*own, *other), vec, *stay(w), *dq, *dk, *dv, g_out, g_two)


def in_core_order(core_ref, mine, theirs):
    core, mine, theirs = core_ref[0], mine.astype(f32), theirs.astype(f32)
    return jnp.where(core == 0, mine, theirs), jnp.where(core == 0, theirs, mine)


def final_feed_kernel(core_ref, mine_ref, theirs_ref, up_ref, down_ref):
    for i in range(16):
        for c, piece in enumerate(in_core_order(core_ref, mine_ref[i], theirs_ref[i])):
            if i < 8:
                base = 1280 * (i // 2) + 640 * c
                up_ref[80 * (i % 2):80 * (i % 2 + 1), base:base + 640] = piece
            else:
                base = 640 * c + 80 * (i - 8)
                down_ref[base:base + 80, :] = piece


def final_feed(core, mine, theirs):
    return call(final_feed_kernel, (shape(160, 5120, dtype=f32), shape(1280, 640, dtype=f32)), "final_feed", 10**6, 32, **scalar_first(
        (1,), [full(16, 80, 640)] * 2, [full(160, 5120), full(1280, 640)]))(core, mine, theirs)


def final_heads_kernel(core_ref, mine_ref, theirs_ref, qkv_ref, out_ref, vec_ref):
    lane = lax.broadcasted_iota(jnp.int32, (40, 128), 1)
    for z in range(4):
        rows = slice(40 * z, 40 * (z + 1))
        for x in range(4):
            a, b = in_core_order(core_ref, mine_ref[4 * z + x], theirs_ref[4 * z + x])
            if x < 3:
                last = jnp.where(lane < 64, a[:, 256:], b[:, 256:])
                qkv_ref[rows, 640 * x:640 * (x + 1)] = jnp.concatenate([a[:, :256], b[:, :256], last], axis=1)
            else:
                out_ref[rows, :] = jnp.concatenate([a, b[:, 128:]], axis=1)
            if x == 0:
                vec_ref[rows, :] = pltpu.roll(a[:, 256:], 64, 1) + b[:, 256:]


def final_heads(core, mine, theirs):
    return call(
        final_heads_kernel, (shape(160, 1920, dtype=f32), shape(160, 640, dtype=f32), shape(160, 128, dtype=f32)), "final_heads", 10**6, 16,
        **scalar_first((1,), [full(16, 40, 384)] * 2, [full(160, 1920), full(160, 640), full(160, 128)]))(core, mine, theirs)


def shifted(array, axis, by):
    devices = lax.axis_size(axis)
    return lax.ppermute(array, axis, [(i, (i + by) % devices) for i in range(devices)])


def passed_along(array, by):
    devices = lax.axis_size(("z", "x"))
    return lax.ppermute(array, ("z", "x"), [(i, i + by) for i in range(devices) if 0 <= i + by < devices])


def swapped(array):
    return lax.ppermute(array, "core", [(0, 1), (1, 0)])


def pick(array, index):
    return lax.dynamic_index_in_dim(array, index, 0, keepdims=False)


def gathered(array, axis):
    me, devices = lax.axis_index(axis), lax.axis_size(axis)
    out = jnp.zeros((devices,) + array.shape, array.dtype)
    out = lax.dynamic_update_index_in_dim(out, array, me, 0)
    for by in (1, devices - 1, 2):
        out = lax.dynamic_update_index_in_dim(out, shifted(array, axis, by), (me + devices - by) % devices, 0)
    return out


def window_info(length_row, chip, core, win):
    ends = jnp.cumsum(length_row)
    starts = ends - length_row
    base = chip * 512 - 1024
    places = base + jnp.arange(win, dtype=jnp.int32)
    inside = (places[:, None] >= starts[None, :]) & (places[:, None] < ends[None, :])
    ones = jnp.broadcast_to(jnp.arange(64) < 3, (win, 64)).astype(bf16)
    key_rows = jnp.concatenate([jnp.where(inside, 0.0, -BIG).astype(bf16), ones], axis=1)
    own = chip * 512 + jnp.arange(512, dtype=jnp.int32)
    inside_q = (own[None, :] >= starts[:, None]) & (own[None, :] < ends[:, None])
    query_rows = jnp.concatenate([inside_q.astype(bf16), jnp.zeros((64, 512), bf16)], axis=0)
    info = [core]
    sizes = []
    for t in range(2):
        first = chip * 512 + t * TILE
        low = jnp.max(jnp.where(starts <= first, starts, 0)) - base
        high = jnp.min(jnp.where(ends > first + TILE - 1, ends, 1 << 30)) - base
        start = low // 128 * 128
        need = high - start
        size = (need + SHORT - 1) // SHORT * SHORT
        info.append(jnp.minimum(start, win - size))
        sizes.append(size)
    low = jnp.minimum(info[1], info[2]) // 512
    high = (jnp.maximum(info[1] + sizes[0], info[2] + sizes[1]) + 511) // 512
    return jnp.stack(info + sizes).astype(jnp.int32), key_rows, query_rows, [low, high]


def body(tokens, lengths, gain_one, bias_one, w_qkv, w_out, gain_two, bias_two, w_up, w_down, cotangent):
    core, chip = lax.axis_index("core"), lax.axis_index(("z", "x"))
    core_arg = core[None].astype(jnp.int32)
    tok, cot = tokens[:, 0], cotangent[:, 0].reshape(512, 640)
    together = lambda *arrays: lax.optimization_barrier(arrays)

    vectors = jnp.pad(jnp.stack([gain_one, bias_one, gain_two, bias_two], axis=1), ((0, 0), (0, 124)))
    heads, tok_sent = together(pack_heads(core_arg, w_qkv, vectors), tok)
    heads = lax.all_gather(heads, "batch", axis=0, tiled=True)
    before, after, tok_other = passed_along(tok_sent, 1), passed_along(tok_sent, -1), swapped(tok_sent)
    windows = [window_info(lengths[m, 0], chip, core, 2560) for m in range(2)]
    place = jnp.stack([core] + windows[0][3] + windows[1][3]).astype(jnp.int32)
    feed_pack = pack_feed(core_arg, w_out, w_up, w_down)
    heads, before, after, tok_other, feed_pack, place, windows = together(heads, before, after, tok_other, feed_pack, place, windows)
    own = [passed_along(before, 1), before, tok, after, passed_along(after, -1)]
    other = [None, swapped(before), tok_other, swapped(after), None]
    feed_weights = lax.all_gather(feed_pack, "batch", axis=0, tiled=True)
    vec = vector_rows(heads)
    *near_parts, q, qT = project((1, 2, 3), place, own, other, vec, heads)
    own[0], own[4], near_parts = together(own[0], own[4], near_parts)
    other[0], other[4] = swapped(own[0]), swapped(own[4])
    k, v, kT, vT = project((0, 4), place, own, other, vec, heads, near_parts)
    (oT0, low0, lse0), (oT1, low1, lse1) = (
        attend(m, info, qT, k, vT, key_rows, query_rows) for m, (info, key_rows, query_rows, _) in enumerate(windows))

    theirs = swapped(jnp.stack([low0, low1]))
    middle, hidden_two, hidden_other = middle_step(core_arg, feed_weights, low0, low1, theirs, tok, tok_other, vec)
    mine, partial, feed_grads = feed_forward(hidden_two, hidden_other, cot, swapped(cot), feed_weights)
    feed_grads = lax.all_to_all(feed_grads.reshape(64, 80, 640), ("batch", "z", "x"), 0, 0, tiled=True)
    block_out, grad_middle, branch, g_two = after_feed(middle, mine, swapped(partial), cot, vec)

    do, doT, g_out = branch_step(core_arg, branch, swapped(branch), feed_weights, low0, low1, theirs)
    dq, dk, dv = zip(*(
        attend_back(m, info, qT, q, k, kT, v, doT, do, oT, lse, key_rows, query_rows)
        for m, ((info, key_rows, query_rows, _), oT, lse) in enumerate(zip(windows, (oT0, oT1), (lse0, lse1)))))
    mine, theirs, tail = project_back(place, own, other, vec, heads, dq, dk, dv, g_out, g_two)
    feed_grads, mine, theirs, tail = together(feed_grads, mine, theirs, tail)

    feed = jnp.sum(feed_grads.astype(f32), axis=0).astype(bf16)
    tail = lax.all_to_all(tail, ("batch", "z", "x"), 0, 0, tiled=True)
    feed = lax.all_gather(feed, ("z", "x"), axis=0, tiled=True).reshape(16, 80, 640)
    theirs = swapped(theirs)
    sums = [mine[j].astype(f32) + theirs[j].astype(f32) for j in range(5)]
    right, left = passed_along(sums[4].astype(bf16), 1), passed_along(sums[0].astype(bf16), -1)
    tail, right, left = together(tail, right, left)
    right = passed_along((right.astype(f32) + sums[3]).astype(bf16), 1)
    left = passed_along((left.astype(f32) + sums[1]).astype(bf16), -1)
    tail = gathered(jnp.sum(tail.astype(f32), axis=0).astype(bf16), "x").reshape(160, 384)
    tail = gathered(tail, "z").reshape(16, 40, 384)
    tail, right, left = together(tail, right, left)
    d_one = (sums[2] + right.astype(f32) + left.astype(f32)).reshape(512, 640)
    n_one, r_one = moments(tok.reshape(512, 640).astype(f32))
    grad_tokens = (grad_middle + norm_back(d_one, n_one, r_one, vec[0:1])).astype(bf16)
    tail, grad_tokens, feed = together(tail, grad_tokens, feed)
    grad_qkv, grad_out, spare = final_heads(core_arg, tail, swapped(tail))
    grad_up, grad_down = final_feed(core_arg, feed, swapped(feed))
    return (
        block_out.reshape(2, 1, 256, 640), grad_tokens.reshape(2, 1, 256, 640), spare[:, 0], spare[:, 1], grad_qkv, grad_out,
        spare[:, 2], spare[:, 3], grad_up, grad_down)


def solution(mesh):
    fine = Mesh(mesh.devices.reshape(4, 4, 4, 2), ("batch", "z", "x", "core"))
    rows = P(None, "batch", ("z", "x", "core"), None)
    one, two = P("batch"), P("batch", None)
    return jax.shard_map(
        body,
        mesh=fine,
        in_specs=(rows, P(None, "batch", None), one, one, two, two, one, one, two, two, rows),
        out_specs=(rows, rows, one, one, two, two, one, one, two, two),
        check_vma=False,
    )
```

```python
import math

import jax
import jax.numpy as jnp
from jax import lax
from jax.experimental import pallas as pl
from jax.experimental.pallas import tpu as pltpu
from jax.sharding import Mesh
from jax.sharding import PartitionSpec as P

HEAD_DIM = 32
SCALE = HEAD_DIM ** -0.5
LOG2E = math.log2(math.e)
C2 = SCALE * LOG2E
BIG = 1e30
TILE = 256
EPSILON = 1e-05
PAIRS = 5
SHORT, LONG = 384, 1152
f32, bf16 = jnp.float32, jnp.bfloat16
NT = (((1,), (1,)), ((), ()))


def pair_offset(info_ref):
    p = pl.program_id(0)
    sub = jnp.where(p == PAIRS - 1, info_ref[0], lax.rem(p, 2))
    return sub * (2 * HEAD_DIM)


def split3(v):
    a = v.astype(bf16)
    r = v - a.astype(f32)
    b = r.astype(bf16)
    d = (r - b.astype(f32)).astype(bf16)
    return a, b, d


def rows_masked(xT, off):
    row = lax.broadcasted_iota(jnp.int32, xT.shape, 0) - off
    xf = xT.astype(f32)
    return [jnp.where((row >= HEAD_DIM * j) & (row < HEAD_DIM * (j + 1)), xf, 0.0).astype(bf16) for j in range(2)]


def lanes_masked(x, off):
    lane = lax.broadcasted_iota(jnp.int32, x.shape, 1) - off
    xf = x.astype(f32)
    return [jnp.where((lane >= HEAD_DIM * j) & (lane < HEAD_DIM * (j + 1)), xf, 0.0).astype(bf16) for j in range(2)]


def attend_kernel(info_ref, qT_ref, k_ref, vT_ref, kaug_ref, qaugT_ref, oT_ref, o_ref, l_ref, rhs):
    off = pair_offset(info_ref)
    oT_ref[...] = jnp.where(lax.rem(pl.program_id(0), 2) == 0, 0.0, oT_ref[...])
    for t in range(2):
        cols = slice(t * TILE, (t + 1) * TILE)
        masked = rows_masked(qT_ref[:, cols], off)
        for j in range(2):
            rhs[0:128, j * TILE:(j + 1) * TILE] = masked[j]
            rhs[128:256, j * TILE:(j + 1) * TILE] = qaugT_ref[:, cols]
        start = info_ref[1 + t]
        need = info_ref[3 + t]

        def block(first, size):
            def step(i, carry):
                row = pl.multiple_of(first + i * size, 128)
                lhs = jnp.concatenate([k_ref[pl.ds(row, size), :], kaug_ref[pl.ds(row, size), :]], axis=1)
                raw = [jnp.dot(lhs, rhs[:, j * TILE:(j + 1) * TILE], preferred_element_type=f32) for j in range(2)]
                out = []
                for j in range(2):
                    m, l, o = carry[j]
                    s = raw[j] * C2
                    m_new = jnp.maximum(m, jnp.max(s, axis=0, keepdims=True))
                    alpha = jnp.exp2(m - m_new)
                    p = jnp.exp2(s - m_new)
                    vT = vT_ref[pl.ds(pl.multiple_of(off + j * HEAD_DIM, HEAD_DIM), HEAD_DIM), pl.ds(row, size)]
                    out.append((m_new, l * alpha + jnp.sum(p, axis=0, keepdims=True),
                                o * alpha + jnp.dot(vT, p.astype(bf16), preferred_element_type=f32)))
                return tuple(out)
            return step

        def finish(state):
            for j in range(2):
                m, l, o = state[j]
                oT_ref[pl.ds(pl.multiple_of(off + j * HEAD_DIM, HEAD_DIM), HEAD_DIM), cols] = o * (1.0 / l)
                l_ref[0, j:j + 1, cols] = m + jnp.log2(l)

        init = tuple((jnp.full((1, TILE), -1e38, f32), jnp.zeros((1, TILE), f32), jnp.zeros((HEAD_DIM, TILE), f32)) for _ in range(2))

        longs = lax.div(need, LONG)
        state = lax.fori_loop(0, longs, block(start, LONG), init)
        finish(lax.fori_loop(0, lax.div(need - longs * LONG, SHORT), block(start + longs * LONG, SHORT), state))

    o_ref[...] = oT_ref[...].T.astype(bf16)


def attend(m, info, qT, k, vT, kaug, qaugT):
    win, nq = k.shape[1], qT.shape[2]
    qT, k, vT = stay(qT, k, vT)
    return pl.pallas_call(
        attend_kernel,
        out_shape=(jax.ShapeDtypeStruct((384, nq), f32), jax.ShapeDtypeStruct((nq, 384), bf16), jax.ShapeDtypeStruct((PAIRS, 8, nq), f32)),
        grid_spec=pltpu.PrefetchScalarGridSpec(
            num_scalar_prefetch=1, grid=(PAIRS,),
            in_specs=[
                pl.BlockSpec((None, 128, nq), lambda p, *_: (m, p // 2, 0)),
                pl.BlockSpec((None, win, 128), lambda p, *_: (m, 0, p // 2)),
                pl.BlockSpec((None, 128, win), lambda p, *_: (m, p // 2, 0)),
                pl.BlockSpec((win, 128), lambda p, *_: (0, 0)),
                pl.BlockSpec((128, nq), lambda p, *_: (0, 0)),
            ],
            out_specs=[
                pl.BlockSpec((128, nq), lambda p, *_: (p // 2, 0)),
                pl.BlockSpec((nq, 128), lambda p, *_: (0, p // 2)),
                pl.BlockSpec((1, 8, nq), lambda p, *_: (p, 0, 0)),
            ],
            scratch_shapes=[pltpu.VMEM((256, 2 * TILE), bf16)],
        ),
        compiler_params=pltpu.CompilerParams(vmem_limit_bytes=28 << 20),
        cost_estimate=pl.CostEstimate(flops=int(20 * 10**9 * 0.02), bytes_accessed=0, transcendentals=0),
        name="attend",
    )(info, qT, k, vT, kaug, qaugT)


def attend_back_kernel(info_ref, qT_ref, q_ref, k_ref, kT_ref, v_ref, doT_ref, do_ref, oT_ref, l_ref, kaug_ref, qaugT_ref,
                       dq_ref, dk_ref, dv_ref, dqT_ref, rhs_s, rhs_d, q_stk, do_stk, dk_acc, dv_acc):
    p_id = pl.program_id(0)
    off = pair_offset(info_ref)

    @pl.when(lax.rem(p_id, 2) == 0)
    def _():
        dqT_ref[...] = jnp.zeros_like(dqT_ref)
        dk_acc[...] = jnp.zeros_like(dk_acc)
        dv_acc[...] = jnp.zeros_like(dv_acc)

    for t in range(2):
        cols = slice(t * TILE, (t + 1) * TILE)
        masked_q = rows_masked(qT_ref[:, cols], off)
        masked_do = rows_masked(doT_ref[:, cols], off)
        lane_q = lanes_masked(q_ref[cols, :], off)
        lane_do = lanes_masked(do_ref[cols, :], off)
        for j in range(2):
            part = slice(j * TILE, (j + 1) * TILE)
            head = pl.ds(pl.multiple_of(off + j * HEAD_DIM, HEAD_DIM), HEAD_DIM)
            delta = jnp.sum(doT_ref[head, cols].astype(f32) * oT_ref[head, cols], axis=0, keepdims=True)
            total = l_ref[0, j:j + 1, cols] * (1.0 / C2)
            rowid = lax.broadcasted_iota(jnp.int32, (64, TILE), 0)
            lp, dp = split3(-total), split3(-delta)
            def pieces(parts):
                x = jnp.zeros((64, TILE), f32)
                for n in range(3):
                    x = jnp.where(rowid == n, parts[n].astype(f32), x)
                return x.astype(bf16)
            rhs_s[0:128, part] = masked_q[j]
            rhs_s[128:192, part] = qaugT_ref[0:64, cols]
            rhs_s[192:256, part] = pieces(lp)
            rhs_d[0:128, part] = masked_do[j]
            rhs_d[128:192, part] = jnp.zeros((64, TILE), bf16)
            rhs_d[192:256, part] = pieces(dp)
            q_stk[part, :] = lane_q[j]
            do_stk[part, :] = lane_do[j]
        start = info_ref[1 + t]
        need = info_ref[3 + t]

        def block(first, size):
            def step(i, carry):
                row = pl.multiple_of(first + i * size, 128)
                rows = pl.ds(row, size)
                aug = kaug_ref[rows, :]
                lhs_k = jnp.concatenate([k_ref[rows, :], aug], axis=1)
                lhs_v = jnp.concatenate([v_ref[rows, :], aug], axis=1)
                out, dv, dk = [], dv_acc[rows, :], dk_acc[rows, :]
                for j in range(2):
                    part = slice(j * TILE, (j + 1) * TILE)
                    s = jnp.dot(lhs_k, rhs_s[:, part], preferred_element_type=f32)
                    dp = jnp.dot(lhs_v, rhs_d[:, part], preferred_element_type=f32)
                    p = jnp.exp2(s * C2)
                    ds = (p * dp).astype(bf16)
                    dv = dv + jnp.dot(p.astype(bf16), do_stk[part, :], preferred_element_type=f32)
                    dk = dk + jnp.dot(ds, q_stk[part, :], preferred_element_type=f32)
                    kT = kT_ref[pl.ds(pl.multiple_of(off + j * HEAD_DIM, HEAD_DIM), HEAD_DIM), rows]
                    out.append(carry[j] + jnp.dot(kT, ds, preferred_element_type=f32))
                dv_acc[rows, :] = dv
                dk_acc[rows, :] = dk
                return tuple(out)
            return step

        def finish(dqs):
            for j in range(2):
                dqT_ref[pl.ds(pl.multiple_of(off + j * HEAD_DIM, HEAD_DIM), HEAD_DIM), cols] = dqs[j] * SCALE

        init = tuple(jnp.zeros((HEAD_DIM, TILE), f32) for _ in range(2))

        longs = lax.div(need, LONG)
        state = lax.fori_loop(0, longs, block(start, LONG), init)
        finish(lax.fori_loop(0, lax.div(need - longs * LONG, SHORT), block(start + longs * LONG, SHORT), state))
    @pl.when((lax.rem(p_id, 2) == 1) | (p_id == PAIRS - 1))
    def _():
        dq_ref[...] = dqT_ref[...].T.astype(bf16)
        dk_ref[...] = (dk_acc[...] * SCALE).astype(bf16)
        dv_ref[...] = dv_acc[...].astype(bf16)


def attend_back(m, info, qT, q, k, kT, v, doT, do, oT, lse, kaug, qaugT):
    win, nq = k.shape[1], qT.shape[2]
    qT, q, k, kT, v, doT, do = stay(qT, q, k, kT, v, doT, do)
    wide = pl.BlockSpec((128, nq), lambda p, *_: (p // 2, 0))
    tall = pl.BlockSpec((nq, 128), lambda p, *_: (0, p // 2))
    keys = pl.BlockSpec((win, 128), lambda p, *_: (0, p // 2))
    wide_m = pl.BlockSpec((None, 128, nq), lambda p, *_: (m, p // 2, 0))
    tall_m = pl.BlockSpec((None, nq, 128), lambda p, *_: (m, 0, p // 2))
    keys_m = pl.BlockSpec((None, win, 128), lambda p, *_: (m, 0, p // 2))
    return pl.pallas_call(
        attend_back_kernel,
        out_shape=tuple(pltpu.MemorySpace.VMEM(d, bf16) for d in ((nq, 384), (win, 384), (win, 384))),
        grid_spec=pltpu.PrefetchScalarGridSpec(
            num_scalar_prefetch=1, grid=(PAIRS,),
            in_specs=[wide_m, tall_m, keys_m, pl.BlockSpec((None, 128, win), lambda p, *_: (m, p // 2, 0)), keys_m,
                      pl.BlockSpec((128, nq), lambda p, *_: (p // 2, m)), pl.BlockSpec((nq, 128), lambda p, *_: (m, p // 2)), wide,
                      pl.BlockSpec((1, 8, nq), lambda p, *_: (p, 0, 0)),
                      pl.BlockSpec((win, 128), lambda p, *_: (0, 0)), pl.BlockSpec((128, nq), lambda p, *_: (0, 0))],
            out_specs=[tall, keys, keys],
            scratch_shapes=[pltpu.VMEM((128, nq), f32), pltpu.VMEM((256, 2 * TILE), bf16), pltpu.VMEM((256, 2 * TILE), bf16),
                            pltpu.VMEM((2 * TILE, 128), bf16), pltpu.VMEM((2 * TILE, 128), bf16),
                            pltpu.VMEM((win, 128), f32), pltpu.VMEM((win, 128), f32)],
        ),
        compiler_params=pltpu.CompilerParams(vmem_limit_bytes=32 << 20),
        cost_estimate=pl.CostEstimate(flops=int(40 * 10**9 * 0.02), bytes_accessed=0, transcendentals=0),
        name="attend_back",
    )(info, qT, q, k, kT, v, doT, do, oT, lse, kaug, qaugT)


def moments(x):
    centred = x - jnp.mean(x, axis=-1, keepdims=True)
    r = lax.rsqrt(jnp.mean(centred * centred, axis=-1, keepdims=True) + EPSILON)
    return centred * r, r


def norm_back(grad, n, r, gain):
    e = grad * gain
    return r * (e - jnp.mean(e, axis=-1, keepdims=True) - n * jnp.mean(e * n, axis=-1, keepdims=True))


def call(kernel, out_shape, name, flops=10**9, limit=48, **spec):
    return pl.pallas_call(
        kernel, out_shape=out_shape, name=name,
        compiler_params=pltpu.CompilerParams(vmem_limit_bytes=limit << 20),
        cost_estimate=pl.CostEstimate(flops=int(flops * 0.02), bytes_accessed=0, transcendentals=0), **spec)


def shape(*dims, dtype=bf16):
    return jax.ShapeDtypeStruct(dims, dtype)


def far(*dims, dtype=bf16):
    return pltpu.MemorySpace.HBM(dims, dtype)


def stay(*arrays):
    return [pltpu.with_memory_space_constraint(a, pltpu.MemorySpace.HBM) for a in arrays]


def scalar_first(grid, in_specs, out_specs, scratch=()):
    return dict(grid_spec=pltpu.PrefetchScalarGridSpec(
        num_scalar_prefetch=1, grid=grid, in_specs=in_specs, out_specs=out_specs, scratch_shapes=list(scratch)))


def full(*dims):
    return pl.BlockSpec(dims, lambda *_: (0,) * len(dims))


def pack_heads_kernel(core_ref, qkv_ref, vec_ref, heads_ref):
    for part in range(3):
        near = pl.ds(pl.multiple_of(640 * part + 256 * core_ref[0], 128), 256)
        heads_ref[:, 384 * part:384 * part + 256] = qkv_ref[:, near]
        heads_ref[:, 384 * part + 256:384 * (part + 1)] = qkv_ref[:, 640 * part + 512:640 * (part + 1)]
    heads_ref[:, 1152:1280] = vec_ref[...]


def pack_heads(core, w_qkv, vectors):
    return call(pack_heads_kernel, shape(160, 1280), "pack_heads", 10**6, 8, **scalar_first(
        (1,), [full(160, 1920), full(160, 128)], full(160, 1280)))(core, w_qkv, vectors)


def turn_kernel(vec_ref, rows_ref):
    rows_ref[...] = vec_ref[...].astype(f32).T[:16]


def vector_rows(heads):
    return call(turn_kernel, shape(16, 640, dtype=f32), "vector_rows", 10**12, 8, grid=(1,),
                in_specs=[pl.BlockSpec((640, 128), lambda i: (0, 9))], out_specs=full(16, 640))(*stay(heads))


def pack_feed_kernel(core_ref, out_ref, up_ref, down_ref, feed_ref):
    core = core_ref[0]
    feed_ref[:, 5120:5760] = out_ref[...]
    for f in range(4):
        feed_ref[:, 640 * f:640 * (f + 1)] = up_ref[:, pl.ds(pl.multiple_of(1280 * f + 640 * core, 128), 640)]
        feed_ref[:, 2560 + 640 * f:2560 + 640 * (f + 1)] = down_ref[pl.ds(pl.multiple_of(640 * core + 160 * f, 32), 160), :]


def pack_feed(core, w_out, w_up, w_down):
    return call(pack_feed_kernel, far(160, 5760), "pack_feed", 10**6, 16, **scalar_first(
        (1,), [full(160, 640), full(160, 5120), full(1280, 640)], full(160, 5760)))(core, *stay(w_out, w_up, w_down))


def rows_in_order(core, mine_ref, theirs_ref, x_ref):
    for c, (first, second) in enumerate(((mine_ref, theirs_ref), (theirs_ref, mine_ref))):
        @pl.when(core == c)
        def _():
            x_ref[0:256, :], x_ref[256:512, :] = first[...], second[...]


def normal_kernel(tok_ref, n_ref):
    for m in range(2):
        n_ref[m] = moments(tok_ref[m].astype(f32))[0].astype(bf16)


def normal_rows(tok):
    return call(normal_kernel, shape(2, 256, 640), "normal_rows", 10**6, 8, grid=(1,), in_specs=[full(2, 256, 640)], out_specs=full(2, 256, 640))(tok)


def project_kernel(chips, place_ref, *refs):
    n = len(chips)
    own_refs, other_refs = refs[:n], refs[n:2 * n]
    vec_ref, w_ref = refs[2 * n:2 * n + 2]
    k_ref, v_ref, kT_ref, vT_ref = refs[-6 - 2 * (n == 3):][:4]
    x_ref, hid_ref = refs[-2:]
    m, step = pl.program_id(0), pl.program_id(1)
    block = sum(jnp.where(step == i, chip, 0) for i, chip in enumerate(chips))
    needed = (block >= place_ref[1 + 2 * m]) & (block < place_ref[2 + 2 * m])

    @pl.when(jnp.logical_not(needed))
    def _():
        for ref in (k_ref, v_ref, kT_ref, vT_ref):
            ref[...] = jnp.zeros_like(ref)

    @pl.when(needed)
    def _():
        for j in range(n):
            @pl.when(step == j)
            def _():
                rows_in_order(place_ref[0], own_refs[j].at[m], other_refs[j].at[m], x_ref)

        hidden = (x_ref[...].astype(f32) * vec_ref[0:1, :] + vec_ref[1:2, :]).astype(bf16)
        hid_ref[...] = hidden
        kv = jnp.dot(hidden, w_ref[:, 384:], preferred_element_type=f32)
        low = kv.astype(bf16)
        k_ref[0] = low[:, :384]
        v_ref[0] = low[:, 384:]
        turned = kv.T.astype(bf16)
        kT_ref[0] = turned[:384]
        vT_ref[0] = turned[384:]

    if n == 3:
        q_ref, qT_ref = refs[-4:-2]

        @pl.when(step == 1)
        def _():
            q = jnp.dot(hid_ref[...], w_ref[:, :384], preferred_element_type=f32)
            q_ref[0] = q.astype(bf16)
            qT_ref[0] = q.T.astype(bf16)


def project(chips, place, own, other, vec, w, earlier=()):
    n = len(chips)
    chip = (lambda b: b + 1) if n == 3 else (lambda b: 4 * b)
    tall = pl.BlockSpec((1, 512, 384), lambda m, b, *_: (m, chip(b), 0))
    wide = pl.BlockSpec((1, 384, 512), lambda m, b, *_: (m, 0, chip(b)))
    shapes = [far(2, 2560, 384), far(2, 2560, 384), far(2, 384, 2560), far(2, 384, 2560)]
    specs = [tall, tall, wide, wide]
    if n == 3:
        shapes += [far(2, 512, 384), far(2, 384, 512)]
        specs += [pl.BlockSpec((1, 512, 384), lambda m, *_: (m, 0, 0)), pl.BlockSpec((1, 384, 512), lambda m, *_: (m, 0, 0))]
    own, other = [own[c] for c in chips], [other[c] for c in chips]
    return call(
        lambda *refs: project_kernel(chips, *refs), shapes, "project", 5 * 10**9, 28,
        input_output_aliases={2 * n + 3 + i: i for i in range(len(earlier))}, **scalar_first(
            (2, n), [full(2, 256, 640)] * (2 * n) + [full(16, 640), full(640, 1152)] + [pl.BlockSpec(memory_space=pl.ANY)] * len(earlier),
            specs, [pltpu.VMEM((512, 640), bf16), pltpu.VMEM((512, 640), bf16)]))(place, *own, *other, vec, *stay(w), *earlier)


def heads_joined(core, mine, theirs):
    first, second = (jnp.where(core == 0, a, b) for a, b in ((mine, theirs), (theirs, mine)))
    return jnp.concatenate([first[:, :256], second[:, :256], first[:, 256:] + second[:, 256:]], axis=1)


def middle_kernel(core_ref, w_ref, low0_ref, low1_ref, theirs_ref, tok_ref, tok2_ref, vec_ref, mid_ref, hid_ref, hid2_ref):
    core = core_ref[0]
    for m, low_ref in enumerate((low0_ref, low1_ref)):
        attended = heads_joined(core, low_ref[...].astype(f32), theirs_ref[m].astype(f32)).astype(bf16)
        branch = jnp.dot(attended, w_ref[...], preferred_element_type=f32)
        mine = jnp.where(core == 0, branch[:256], branch[256:]) + tok_ref[m].astype(f32)
        theirs = jnp.where(core == 0, branch[256:], branch[:256]) + tok2_ref[m].astype(f32)
        part = slice(256 * m, 256 * (m + 1))
        mid_ref[part, :] = mine
        hid_ref[part, :] = (moments(mine)[0] * vec_ref[2:3, :] + vec_ref[3:4, :]).astype(bf16)
        hid2_ref[part, :] = (moments(theirs)[0] * vec_ref[2:3, :] + vec_ref[3:4, :]).astype(bf16)


W_OUT = pl.BlockSpec((640, 640), lambda *_: (0, 8))


def middle_step(core, weights, *args):
    return call(middle_kernel, (far(512, 640, dtype=f32), far(512, 640), far(512, 640)), "middle", 10**9, 20, **scalar_first(
        (1,), [W_OUT] + [full(*a.shape) for a in args], [full(512, 640)] * 3))(core, *stay(weights), *args)


def feed_kernel(h_ref, h2_ref, cot_ref, cot2_ref, up_ref, down_ref, mine_ref, theirs_ref, g_ref, h, cot, hT, cT, out, dh):
    chunk = pl.program_id(0)

    @pl.when(chunk == 0)
    def _():
        h[0:512, :], h[512:1024, :] = h_ref[...], h2_ref[...]
        cot[0:512, :], cot[512:1024, :] = cot_ref[...], cot2_ref[...]
        hT[...] = h[...].astype(f32).T.astype(bf16)
        cT[...] = cot[...].astype(f32).T.astype(bf16)
        out[...] = jnp.zeros_like(out)
        dh[...] = jnp.zeros_like(dh)

    up_w = up_ref[...]
    down_w = jnp.concatenate([down_ref[160 * y:160 * (y + 1), 640 * i:640 * (i + 1)] for y in range(2) for i in range(4)], axis=0)
    acts, d_ups = [], []
    for t in range(4):
        rows = slice(256 * t, 256 * (t + 1))
        u = jnp.dot(h[rows, :], up_w, preferred_element_type=f32)
        d_act = lax.dot_general(cot[rows, :], down_w, NT, preferred_element_type=f32)
        cdf = 0.5 * (1.0 + lax.erf(u * (2.0 ** -0.5)))
        pdf = jnp.exp(u * u * -0.5) * ((2.0 * math.pi) ** -0.5)
        act = (u * cdf).astype(bf16)
        d_up = (d_act * (cdf + u * pdf)).astype(bf16)
        out[rows, :] += jnp.dot(act, down_w, preferred_element_type=f32)
        dh[rows, :] += lax.dot_general(d_up, up_w, NT, preferred_element_type=f32)
        acts.append(act)
        d_ups.append(d_up)
    g_up = jnp.dot(hT[...], jnp.concatenate(d_ups, axis=0), preferred_element_type=f32).astype(bf16)
    g_down = jnp.dot(cT[...], jnp.concatenate(acts, axis=0), preferred_element_type=f32).T.astype(bf16)
    for f in range(2):
        for y in range(4):
            for i in range(2):
                g_ref[y, 4 * chunk + 2 * f + i] = g_up[160 * y + 80 * i:160 * y + 80 * (i + 1), 640 * f:640 * (f + 1)]
        for i in range(8):
            g_ref[2 * chunk + f, 8 + i] = g_down[640 * f + 80 * i:640 * f + 80 * (i + 1)]

    @pl.when(chunk == 1)
    def _():
        mine_ref[0], mine_ref[1] = out[0:512, :].astype(bf16), dh[0:512, :].astype(bf16)
        theirs_ref[0], theirs_ref[1] = out[512:1024, :].astype(bf16), dh[512:1024, :].astype(bf16)


def feed_forward(h, h2, cot, cot2, weights):
    return call(
        feed_kernel,
        (far(2, 512, 640), far(2, 512, 640), far(4, 16, 80, 640)),
        "feed_forward", 30 * 10**9, 52, grid=(2,),
        in_specs=[full(512, 640)] * 4 + [pl.BlockSpec((640, 1280), lambda f: (0, f)), pl.BlockSpec((320, 2560), lambda f: (f, 1))],
        out_specs=[full(2, 512, 640), full(2, 512, 640), full(4, 16, 80, 640)],
        scratch_shapes=[pltpu.VMEM((1024, 640), bf16), pltpu.VMEM((1024, 640), bf16), pltpu.VMEM((640, 1024), bf16), pltpu.VMEM((640, 1024), bf16),
                        pltpu.VMEM((1024, 640), f32), pltpu.VMEM((1024, 640), f32)],
    )(*stay(h, h2, cot), cot2, *stay(weights, weights))


def after_kernel(mid_ref, mine_ref, theirs_ref, cot_ref, vec_ref, block_ref, grad_ref, branch_ref, g_ref):
    @pl.when(pl.program_id(0) == 0)
    def _():
        g_ref[...] = jnp.zeros_like(g_ref)

    middle = mid_ref[...]
    block_ref[...] = (middle + mine_ref[0].astype(f32) + theirs_ref[0].astype(f32)).astype(bf16)
    d_hidden = mine_ref[1].astype(f32) + theirs_ref[1].astype(f32)
    n, r = moments(middle)
    g_ref[0:1, :] += jnp.sum(d_hidden * n, axis=0, keepdims=True)
    g_ref[1:2, :] += jnp.sum(d_hidden, axis=0, keepdims=True)
    grad = cot_ref[...].astype(f32) + norm_back(d_hidden, n, r, vec_ref[2:3, :])
    grad_ref[...] = grad
    branch_ref[...] = grad.astype(bf16)


def after_feed(*args):
    rows, pair = pl.BlockSpec((128, 640), lambda i: (i, 0)), pl.BlockSpec((2, 128, 640), lambda i: (0, i, 0))
    return call(
        after_kernel, (far(512, 640), far(512, 640, dtype=f32), shape(512, 640), shape(8, 640, dtype=f32)), "after_feed", 10**9, 16,
        grid=(4,), in_specs=[rows, pair, pair, rows, full(16, 640)], out_specs=[rows, rows, rows, full(8, 640)])(*stay(args[0], args[1]), args[2], *stay(args[3]), args[4])


def branch_kernel(core_ref, own_ref, their_ref, w_ref, low0_ref, low1_ref, theirs_ref, do_ref, doT_ref, g_ref):
    core = core_ref[0]
    w = jnp.concatenate([w_ref[pl.ds(pl.multiple_of(256 * core, 256), 256), :], w_ref[512:640, :]], axis=0)
    g = jnp.zeros((640, 384), f32)
    for m in range(2):
        part = slice(256 * m, 256 * (m + 1))
        mine, theirs = own_ref[part, :].astype(f32), their_ref[part, :].astype(f32)
        branch = jnp.concatenate([jnp.where(core == 0, mine, theirs), jnp.where(core == 0, theirs, mine)], axis=0)
        kept = jnp.where(core == 0, branch[:, :384], branch[:, 256:]).astype(bf16)
        branch = branch.astype(bf16)
        rows = slice(512 * m, 512 * (m + 1))
        do = lax.dot_general(branch, w, NT, preferred_element_type=f32)
        do_ref[rows, :] = do.astype(bf16)
        doT_ref[:, rows] = do.T.astype(bf16)
        attended = heads_joined(core, (low0_ref, low1_ref)[m][...].astype(f32), theirs_ref[m].astype(f32))
        g = g + jnp.dot(attended.T.astype(bf16), kept, preferred_element_type=f32)
    g_ref[...] = g.astype(bf16)


def branch_step(core, own, their, weights, *args):
    return call(
        branch_kernel, (far(1024, 384), far(384, 1024), shape(640, 384)), "branch", 10**9, 24, **scalar_first(
            (1,), [full(512, 640)] * 2 + [W_OUT] + [full(*a.shape) for a in args], [full(1024, 384), full(384, 1024), full(640, 384)]))(
                core, own, their, *stay(weights), *args)


def near_by(*arrays):
    return [pltpu.with_memory_space_constraint(a, pltpu.MemorySpace.VMEM) for a in arrays]


def project_back_kernel(place_ref, *refs):
    own_refs, other_refs = refs[:5], refs[5:10]
    (vec_ref, w_ref, dq0_ref, dq1_ref, dk0_ref, dk1_ref, dv0_ref, dv1_ref, g_out_ref, g_two_ref,
     mine_ref, theirs_ref, tail_ref, n_ref, d_kv, d_q, d_hid, g_ref, g_vec, slots, arrived) = refs[10:]
    step, core = pl.program_id(0), place_ref[0]
    block, second = lax.rem(step, 5), lax.div(step, 5)
    inside = lambda j, m: (j >= place_ref[1 + 2 * m]) & (j < place_ref[2 + 2 * m])
    needed = inside(block, second)

    def copies(j, m, slot):
        return [pltpu.make_async_copy(refs_of[j].at[m], slots.at[slot, i], arrived.at[slot, i]) for i, refs_of in enumerate((own_refs, other_refs))]

    @pl.when(step == 0)
    def _():
        for m in range(2):
            for j in range(5):
                @pl.when(inside(j, m))
                def _():
                    for copy in copies(j, m, 5 * m + j):
                        copy.start()
        g_ref[...] = jnp.zeros_like(g_ref)
        g_vec[...] = jnp.zeros_like(g_vec)
        g_vec[2:4, :] = g_two_ref[0:2, :]

    @pl.when(jnp.logical_not(needed))
    def _():
        mine_ref[...] = jnp.zeros_like(mine_ref)
        theirs_ref[...] = jnp.zeros_like(theirs_ref)

    @pl.when(needed)
    def _():
        for copy in copies(0, 0, step):
            copy.wait()
        rows_in_order(core, slots.at[step, 0], slots.at[step, 1], n_ref)

    for m, (dq, dk, dv) in enumerate(((dq0_ref, dk0_ref, dv0_ref), (dq1_ref, dk1_ref, dv1_ref))):
        @pl.when(needed & (second == m))
        def _():
            rows = pl.ds(pl.multiple_of(block * 512, 512), 512)
            d_kv[:, :384], d_kv[:, 384:] = dk[rows, :], dv[rows, :]
            d_q[...] = dq[...]

    @pl.when(needed)
    def _():
        n = n_ref[...].astype(f32)
        hiddenT = (n * vec_ref[0:1, :] + vec_ref[1:2, :]).T.astype(bf16)
        d_hid[...] = lax.dot_general(d_kv[...], w_ref[:, 384:1152], NT, preferred_element_type=f32)
        g_ref[:, 384:] += jnp.dot(hiddenT, d_kv[...], preferred_element_type=f32)

        @pl.when(block == 2)
        def _():
            g_ref[:, :384] += jnp.dot(hiddenT, d_q[...], preferred_element_type=f32)
            d_hid[...] += lax.dot_general(d_q[...], w_ref[:, :384], NT, preferred_element_type=f32)

        dh = d_hid[...]
        low = dh.astype(bf16)
        for c, (first, other) in enumerate(((mine_ref, theirs_ref), (theirs_ref, mine_ref))):
            @pl.when(core == c)
            def _():
                first[0, 0], other[0, 0] = low[:256], low[256:]
        g_vec[0:1, :] += jnp.sum(dh * n, axis=0, keepdims=True)
        g_vec[1:2, :] += jnp.sum(dh, axis=0, keepdims=True)

    @pl.when(step == 9)
    def _():
        turned = g_vec[...].T
        lane = lax.broadcasted_iota(jnp.int32, (640, 128), 1) - 64 * (1 - core)
        spare = g_ref[:, 256:384]
        for i in range(4):
            spare = jnp.where(lane == i, turned[:, i:i + 1], spare)
        g_ref[:, 256:384] = spare
        for y in range(4):
            for z in range(4):
                rows = slice(160 * y + 40 * z, 160 * y + 40 * (z + 1))
                for x in range(3):
                    tail_ref[16 * y + 4 * z + x] = g_ref[rows, 384 * x:384 * (x + 1)].astype(bf16)
                tail_ref[16 * y + 4 * z + 3] = g_out_ref[rows, :].astype(bf16)


def project_back(place, own, other, vec, w, dq, dk, dv, g_out, g_two):
    here = pl.BlockSpec(memory_space=pltpu.VMEM)
    part = pl.BlockSpec((1, 1, 256, 640), lambda b, *_: (lax.rem(b, 5), b // 5, 0, 0))
    return call(
        project_back_kernel, (far(5, 2, 256, 640), far(5, 2, 256, 640), far(64, 40, 384)), "project_back", 10**10, 30, **scalar_first(
            (10,), [pl.BlockSpec(memory_space=pl.ANY)] * 10 + [here] * 10, [part, part, full(64, 40, 384)],
            [pltpu.VMEM((512, 640), bf16), pltpu.VMEM((512, 768), bf16), pltpu.VMEM((512, 384), bf16),
             pltpu.VMEM((512, 640), f32), pltpu.VMEM((640, 1152), f32), pltpu.VMEM((8, 640), f32),
             pltpu.VMEM((10, 2, 256, 640), bf16), pltpu.SemaphoreType.DMA((10, 2))]))(
                 place, *stay(*own, *other), *near_by(vec, w, *dq, *dk, *dv, g_out, g_two))


def in_core_order(core_ref, mine, theirs):
    core, mine, theirs = core_ref[0], mine.astype(f32), theirs.astype(f32)
    return jnp.where(core == 0, mine, theirs), jnp.where(core == 0, theirs, mine)


def final_feed_kernel(core_ref, mine_ref, theirs_ref, up_ref, down_ref):
    for i in range(16):
        for c, piece in enumerate(in_core_order(core_ref, mine_ref[i], theirs_ref[i])):
            if i < 8:
                base = 1280 * (i // 2) + 640 * c
                up_ref[80 * (i % 2):80 * (i % 2 + 1), base:base + 640] = piece
            else:
                base = 640 * c + 80 * (i - 8)
                down_ref[base:base + 80, :] = piece


def final_feed(core, mine, theirs):
    return call(final_feed_kernel, (shape(160, 5120, dtype=f32), shape(1280, 640, dtype=f32)), "final_feed", 10**6, 32, **scalar_first(
        (1,), [full(16, 80, 640)] * 2, [full(160, 5120), full(1280, 640)]))(core, mine, theirs)


def final_heads_kernel(core_ref, mine_ref, theirs_ref, qkv_ref, out_ref, vec_ref):
    lane = lax.broadcasted_iota(jnp.int32, (40, 128), 1)
    for z in range(4):
        rows = slice(40 * z, 40 * (z + 1))
        for x in range(4):
            a, b = in_core_order(core_ref, mine_ref[4 * z + x], theirs_ref[4 * z + x])
            if x < 3:
                last = jnp.where(lane < 64, a[:, 256:], b[:, 256:])
                qkv_ref[rows, 640 * x:640 * (x + 1)] = jnp.concatenate([a[:, :256], b[:, :256], last], axis=1)
            else:
                out_ref[rows, :] = jnp.concatenate([a, b[:, 128:]], axis=1)
            if x == 0:
                vec_ref[rows, :] = pltpu.roll(a[:, 256:], 64, 1) + b[:, 256:]


def final_heads(core, mine, theirs):
    return call(
        final_heads_kernel, (shape(160, 1920, dtype=f32), shape(160, 640, dtype=f32), shape(160, 128, dtype=f32)), "final_heads", 10**6, 16,
        **scalar_first((1,), [full(16, 40, 384)] * 2, [full(160, 1920), full(160, 640), full(160, 128)]))(core, mine, theirs)


def shifted(array, axis, by):
    devices = lax.axis_size(axis)
    return lax.ppermute(array, axis, [(i, (i + by) % devices) for i in range(devices)])


def passed_along(array, by):
    devices = lax.axis_size(("z", "x"))
    return lax.ppermute(array, ("z", "x"), [(i, i + by) for i in range(devices) if 0 <= i + by < devices])


def swapped(array):
    return lax.ppermute(array, "core", [(0, 1), (1, 0)])


def pick(array, index):
    return lax.dynamic_index_in_dim(array, index, 0, keepdims=False)


def gathered(array, axis):
    me, devices = lax.axis_index(axis), lax.axis_size(axis)
    out = jnp.zeros((devices,) + array.shape, array.dtype)
    out = lax.dynamic_update_index_in_dim(out, array, me, 0)
    for by in (1, devices - 1, 2):
        out = lax.dynamic_update_index_in_dim(out, shifted(array, axis, by), (me + devices - by) % devices, 0)
    return out


def window_info(length_row, chip, core, win):
    ends = jnp.cumsum(length_row)
    starts = ends - length_row
    base = chip * 512 - 1024
    places = base + jnp.arange(win, dtype=jnp.int32)
    inside = (places[:, None] >= starts[None, :]) & (places[:, None] < ends[None, :])
    ones = jnp.broadcast_to(jnp.arange(64) < 3, (win, 64)).astype(bf16)
    key_rows = jnp.concatenate([jnp.where(inside, 0.0, -BIG).astype(bf16), ones], axis=1)
    own = chip * 512 + jnp.arange(512, dtype=jnp.int32)
    inside_q = (own[None, :] >= starts[:, None]) & (own[None, :] < ends[:, None])
    query_rows = jnp.concatenate([inside_q.astype(bf16), jnp.zeros((64, 512), bf16)], axis=0)
    info = [core]
    sizes = []
    for t in range(2):
        first = chip * 512 + t * TILE
        low = jnp.max(jnp.where(starts <= first, starts, 0)) - base
        high = jnp.min(jnp.where(ends > first + TILE - 1, ends, 1 << 30)) - base
        start = low // 128 * 128
        need = high - start
        size = (need + SHORT - 1) // SHORT * SHORT
        info.append(jnp.minimum(start, win - size))
        sizes.append(size)
    low = jnp.minimum(info[1], info[2]) // 512
    high = (jnp.maximum(info[1] + sizes[0], info[2] + sizes[1]) + 511) // 512
    return jnp.stack(info + sizes).astype(jnp.int32), key_rows, query_rows, [low, high]


def body(tokens, lengths, gain_one, bias_one, w_qkv, w_out, gain_two, bias_two, w_up, w_down, cotangent):
    core, chip = lax.axis_index("core"), lax.axis_index(("z", "x"))
    core_arg = core[None].astype(jnp.int32)
    tok, cot = tokens[:, 0], cotangent[:, 0].reshape(512, 640)
    together = lambda *arrays: lax.optimization_barrier(arrays)

    vectors = jnp.pad(jnp.stack([gain_one, bias_one, gain_two, bias_two], axis=1), ((0, 0), (0, 124)))
    heads, tok_sent = together(pack_heads(core_arg, w_qkv, vectors), tok)
    heads = lax.all_gather(heads, "batch", axis=0, tiled=True)
    vec = vector_rows(heads)
    normal = normal_rows(tok_sent)
    before, after, normal_other, tok_other = passed_along(normal, 1), passed_along(normal, -1), swapped(normal), swapped(tok)
    windows = [window_info(lengths[m, 0], chip, core, 2560) for m in range(2)]
    place = jnp.stack([core] + windows[0][3] + windows[1][3]).astype(jnp.int32)
    feed_pack = pack_feed(core_arg, w_out, w_up, w_down)
    heads, vec, before, after, normal_other, tok_other, feed_pack, place, windows = together(
        heads, vec, before, after, normal_other, tok_other, feed_pack, place, windows)
    own = [passed_along(before, 1), before, normal, after, passed_along(after, -1)]
    other = [None, swapped(before), normal_other, swapped(after), None]
    feed_weights = lax.all_gather(feed_pack, "batch", axis=0, tiled=True)
    *near_parts, q, qT = project((1, 2, 3), place, own, other, vec, heads)
    own[0], own[4], near_parts = together(own[0], own[4], near_parts)
    other[0], other[4] = swapped(own[0]), swapped(own[4])
    k, v, kT, vT = project((0, 4), place, own, other, vec, heads, near_parts)
    (oT0, low0, lse0), (oT1, low1, lse1) = (
        attend(m, info, qT, k, vT, key_rows, query_rows) for m, (info, key_rows, query_rows, _) in enumerate(windows))

    theirs = swapped(jnp.stack([low0, low1]))
    middle, hidden_two, hidden_other = middle_step(core_arg, feed_weights, low0, low1, theirs, tok, tok_other, vec)
    mine, partial, feed_grads = feed_forward(hidden_two, hidden_other, cot, swapped(cot), feed_weights)
    feed_grads = lax.all_to_all(feed_grads.reshape(64, 80, 640), ("batch", "z", "x"), 0, 0, tiled=True)
    block_out, grad_middle, branch, g_two = after_feed(middle, mine, swapped(partial), cot, vec)

    do, doT, g_out = branch_step(core_arg, branch, swapped(branch), feed_weights, low0, low1, theirs)
    dq, dk, dv = zip(*(
        attend_back(m, info, qT, q, k, kT, v, doT, do, oT, lse, key_rows, query_rows)
        for m, ((info, key_rows, query_rows, _), oT, lse) in enumerate(zip(windows, (oT0, oT1), (lse0, lse1)))))
    mine, theirs, tail = project_back(place, own, other, vec, heads, dq, dk, dv, g_out, g_two)
    feed_grads, mine, theirs, tail = together(feed_grads, mine, theirs, tail)

    feed = jnp.sum(feed_grads.astype(f32), axis=0).astype(bf16)
    tail = lax.all_to_all(tail, ("batch", "z", "x"), 0, 0, tiled=True)
    feed = lax.all_gather(feed, ("z", "x"), axis=0, tiled=True).reshape(16, 80, 640)
    theirs = swapped(theirs)
    sums = [mine[j].astype(f32) + theirs[j].astype(f32) for j in range(5)]
    right, left = passed_along(sums[4].astype(bf16), 1), passed_along(sums[0].astype(bf16), -1)
    tail, right, left = together(tail, right, left)
    right, left = (right.astype(f32) + sums[3]).astype(bf16), (left.astype(f32) + sums[1]).astype(bf16)
    tail, right, left = together(jnp.sum(tail.astype(f32), axis=0).astype(bf16), right, left)
    right, left = passed_along(right, 1), passed_along(left, -1)
    tail = gathered(tail, "x").reshape(160, 384)
    tail = gathered(tail, "z").reshape(16, 40, 384)
    tail, right, left = together(tail, right, left)
    d_one = (sums[2] + right.astype(f32) + left.astype(f32)).reshape(512, 640)
    n_one, r_one = moments(tok.reshape(512, 640).astype(f32))
    grad_tokens = (grad_middle + norm_back(d_one, n_one, r_one, vec[0:1])).astype(bf16)
    tail, grad_tokens, feed = together(tail, grad_tokens, feed)
    grad_qkv, grad_out, spare = final_heads(core_arg, tail, swapped(tail))
    grad_up, grad_down = final_feed(core_arg, feed, swapped(feed))
    return (
        block_out.reshape(2, 1, 256, 640), grad_tokens.reshape(2, 1, 256, 640), spare[:, 0], spare[:, 1], grad_qkv, grad_out,
        spare[:, 2], spare[:, 3], grad_up, grad_down)


def solution(mesh):
    fine = Mesh(mesh.devices.reshape(4, 4, 4, 2), ("batch", "z", "x", "core"))
    rows = P(None, "batch", ("z", "x", "core"), None)
    one, two = P("batch"), P("batch", None)
    return jax.shard_map(
        body,
        mesh=fine,
        in_specs=(rows, P(None, "batch", None), one, one, two, two, one, one, two, two, rows),
        out_specs=(rows, rows, one, one, two, two, one, one, two, two),
        check_vma=False,
    )
```

```python
import math

import jax
import jax.numpy as jnp
from jax import lax
from jax.experimental import pallas as pl
from jax.experimental.pallas import tpu as pltpu
from jax.sharding import Mesh
from jax.sharding import PartitionSpec as P

HEAD_DIM = 32
SCALE = HEAD_DIM ** -0.5
LOG2E = math.log2(math.e)
C2 = SCALE * LOG2E
BIG = 1e30
TILE = 256
EPSILON = 1e-05
PAIRS = 5
SHORT, LONG = 384, 1152
f32, bf16 = jnp.float32, jnp.bfloat16
NT = (((1,), (1,)), ((), ()))


def pair_offset(info_ref):
    p = pl.program_id(0)
    sub = jnp.where(p == PAIRS - 1, info_ref[0], lax.rem(p, 2))
    return sub * (2 * HEAD_DIM)


def split3(v):
    a = v.astype(bf16)
    r = v - a.astype(f32)
    b = r.astype(bf16)
    d = (r - b.astype(f32)).astype(bf16)
    return a, b, d


def rows_masked(xT, off):
    row = lax.broadcasted_iota(jnp.int32, xT.shape, 0) - off
    xf = xT.astype(f32)
    return [jnp.where((row >= HEAD_DIM * j) & (row < HEAD_DIM * (j + 1)), xf, 0.0).astype(bf16) for j in range(2)]


def lanes_masked(x, off):
    lane = lax.broadcasted_iota(jnp.int32, x.shape, 1) - off
    xf = x.astype(f32)
    return [jnp.where((lane >= HEAD_DIM * j) & (lane < HEAD_DIM * (j + 1)), xf, 0.0).astype(bf16) for j in range(2)]


def attend_kernel(info_ref, qT_ref, k_ref, vT_ref, kaug_ref, qaugT_ref, oT_ref, o_ref, l_ref, rhs):
    off = pair_offset(info_ref)
    oT_ref[...] = jnp.where(lax.rem(pl.program_id(0), 2) == 0, 0.0, oT_ref[...])
    for t in range(2):
        cols = slice(t * TILE, (t + 1) * TILE)
        masked = rows_masked(qT_ref[:, cols], off)
        for j in range(2):
            rhs[0:128, j * TILE:(j + 1) * TILE] = masked[j]
            rhs[128:256, j * TILE:(j + 1) * TILE] = qaugT_ref[:, cols]
        start = info_ref[1 + t]
        need = info_ref[3 + t]

        def block(first, size):
            def step(i, carry):
                row = pl.multiple_of(first + i * size, 128)
                lhs = jnp.concatenate([k_ref[pl.ds(row, size), :], kaug_ref[pl.ds(row, size), :]], axis=1)
                raw = [jnp.dot(lhs, rhs[:, j * TILE:(j + 1) * TILE], preferred_element_type=f32) for j in range(2)]
                out = []
                for j in range(2):
                    m, l, o = carry[j]
                    s = raw[j] * C2
                    m_new = jnp.maximum(m, jnp.max(s, axis=0, keepdims=True))
                    alpha = jnp.exp2(m - m_new)
                    p = jnp.exp2(s - m_new)
                    vT = vT_ref[pl.ds(pl.multiple_of(off + j * HEAD_DIM, HEAD_DIM), HEAD_DIM), pl.ds(row, size)]
                    out.append((m_new, l * alpha + jnp.sum(p, axis=0, keepdims=True),
                                o * alpha + jnp.dot(vT, p.astype(bf16), preferred_element_type=f32)))
                return tuple(out)
            return step

        def finish(state):
            for j in range(2):
                m, l, o = state[j]
                oT_ref[pl.ds(pl.multiple_of(off + j * HEAD_DIM, HEAD_DIM), HEAD_DIM), cols] = o * (1.0 / l)
                l_ref[0, j:j + 1, cols] = m + jnp.log2(l)

        init = tuple((jnp.full((1, TILE), -1e38, f32), jnp.zeros((1, TILE), f32), jnp.zeros((HEAD_DIM, TILE), f32)) for _ in range(2))

        longs = lax.div(need, LONG)
        state = lax.fori_loop(0, longs, block(start, LONG), init)
        finish(lax.fori_loop(0, lax.div(need - longs * LONG, SHORT), block(start + longs * LONG, SHORT), state))

    o_ref[...] = oT_ref[...].T.astype(bf16)


def attend(m, info, qT, k, vT, kaug, qaugT):
    win, nq = k.shape[1], qT.shape[2]
    qT, k, vT = stay(qT, k, vT)
    return pl.pallas_call(
        attend_kernel,
        out_shape=(jax.ShapeDtypeStruct((384, nq), f32), jax.ShapeDtypeStruct((nq, 384), bf16), jax.ShapeDtypeStruct((PAIRS, 8, nq), f32)),
        grid_spec=pltpu.PrefetchScalarGridSpec(
            num_scalar_prefetch=1, grid=(PAIRS,),
            in_specs=[
                pl.BlockSpec((None, 128, nq), lambda p, *_: (m, p // 2, 0)),
                pl.BlockSpec((None, win, 128), lambda p, *_: (m, 0, p // 2)),
                pl.BlockSpec((None, 128, win), lambda p, *_: (m, p // 2, 0)),
                pl.BlockSpec((win, 128), lambda p, *_: (0, 0)),
                pl.BlockSpec((128, nq), lambda p, *_: (0, 0)),
            ],
            out_specs=[
                pl.BlockSpec((128, nq), lambda p, *_: (p // 2, 0)),
                pl.BlockSpec((nq, 128), lambda p, *_: (0, p // 2)),
                pl.BlockSpec((1, 8, nq), lambda p, *_: (p, 0, 0)),
            ],
            scratch_shapes=[pltpu.VMEM((256, 2 * TILE), bf16)],
        ),
        compiler_params=pltpu.CompilerParams(vmem_limit_bytes=28 << 20),
        cost_estimate=pl.CostEstimate(flops=int(20 * 10**9 * 0.02), bytes_accessed=0, transcendentals=0),
        name="attend",
    )(info, qT, k, vT, kaug, qaugT)


def attend_back_kernel(info_ref, qT_ref, q_ref, k_ref, kT_ref, v_ref, doT_ref, do_ref, oT_ref, l_ref, kaug_ref, qaugT_ref,
                       dq_ref, dk_ref, dv_ref, dqT_ref, rhs_s, rhs_d, q_stk, do_stk, dk_acc, dv_acc):
    p_id = pl.program_id(0)
    off = pair_offset(info_ref)

    @pl.when(lax.rem(p_id, 2) == 0)
    def _():
        dqT_ref[...] = jnp.zeros_like(dqT_ref)
        dk_acc[...] = jnp.zeros_like(dk_acc)
        dv_acc[...] = jnp.zeros_like(dv_acc)

    for t in range(2):
        cols = slice(t * TILE, (t + 1) * TILE)
        masked_q = rows_masked(qT_ref[:, cols], off)
        masked_do = rows_masked(doT_ref[:, cols], off)
        lane_q = lanes_masked(q_ref[cols, :], off)
        lane_do = lanes_masked(do_ref[cols, :], off)
        for j in range(2):
            part = slice(j * TILE, (j + 1) * TILE)
            head = pl.ds(pl.multiple_of(off + j * HEAD_DIM, HEAD_DIM), HEAD_DIM)
            delta = jnp.sum(doT_ref[head, cols].astype(f32) * oT_ref[head, cols], axis=0, keepdims=True)
            total = l_ref[0, j:j + 1, cols] * (1.0 / C2)
            rowid = lax.broadcasted_iota(jnp.int32, (64, TILE), 0)
            lp, dp = split3(-total), split3(-delta)
            def pieces(parts):
                x = jnp.zeros((64, TILE), f32)
                for n in range(3):
                    x = jnp.where(rowid == n, parts[n].astype(f32), x)
                return x.astype(bf16)
            rhs_s[0:128, part] = masked_q[j]
            rhs_s[128:192, part] = qaugT_ref[0:64, cols]
            rhs_s[192:256, part] = pieces(lp)
            rhs_d[0:128, part] = masked_do[j]
            rhs_d[128:192, part] = jnp.zeros((64, TILE), bf16)
            rhs_d[192:256, part] = pieces(dp)
            q_stk[part, :] = lane_q[j]
            do_stk[part, :] = lane_do[j]
        start = info_ref[1 + t]
        need = info_ref[3 + t]

        def block(first, size):
            def step(i, carry):
                row = pl.multiple_of(first + i * size, 128)
                rows = pl.ds(row, size)
                aug = kaug_ref[rows, :]
                lhs_k = jnp.concatenate([k_ref[rows, :], aug], axis=1)
                lhs_v = jnp.concatenate([v_ref[rows, :], aug], axis=1)
                out, dv, dk = [], dv_acc[rows, :], dk_acc[rows, :]
                for j in range(2):
                    part = slice(j * TILE, (j + 1) * TILE)
                    s = jnp.dot(lhs_k, rhs_s[:, part], preferred_element_type=f32)
                    dp = jnp.dot(lhs_v, rhs_d[:, part], preferred_element_type=f32)
                    p = jnp.exp2(s * C2)
                    ds = (p * dp).astype(bf16)
                    dv = dv + jnp.dot(p.astype(bf16), do_stk[part, :], preferred_element_type=f32)
                    dk = dk + jnp.dot(ds, q_stk[part, :], preferred_element_type=f32)
                    kT = kT_ref[pl.ds(pl.multiple_of(off + j * HEAD_DIM, HEAD_DIM), HEAD_DIM), rows]
                    out.append(carry[j] + jnp.dot(kT, ds, preferred_element_type=f32))
                dv_acc[rows, :] = dv
                dk_acc[rows, :] = dk
                return tuple(out)
            return step

        def finish(dqs):
            for j in range(2):
                dqT_ref[pl.ds(pl.multiple_of(off + j * HEAD_DIM, HEAD_DIM), HEAD_DIM), cols] = dqs[j] * SCALE

        init = tuple(jnp.zeros((HEAD_DIM, TILE), f32) for _ in range(2))

        longs = lax.div(need, LONG)
        state = lax.fori_loop(0, longs, block(start, LONG), init)
        finish(lax.fori_loop(0, lax.div(need - longs * LONG, SHORT), block(start + longs * LONG, SHORT), state))
    @pl.when((lax.rem(p_id, 2) == 1) | (p_id == PAIRS - 1))
    def _():
        dq_ref[...] = dqT_ref[...].T.astype(bf16)
        dk_ref[...] = (dk_acc[...] * SCALE).astype(bf16)
        dv_ref[...] = dv_acc[...].astype(bf16)


def attend_back(m, info, qT, q, k, kT, v, doT, do, oT, lse, kaug, qaugT):
    win, nq = k.shape[1], qT.shape[2]
    qT, q, k, kT, v, doT, do = stay(qT, q, k, kT, v, doT, do)
    wide = pl.BlockSpec((128, nq), lambda p, *_: (p // 2, 0))
    tall = pl.BlockSpec((nq, 128), lambda p, *_: (0, p // 2))
    keys = pl.BlockSpec((win, 128), lambda p, *_: (0, p // 2))
    wide_m = pl.BlockSpec((None, 128, nq), lambda p, *_: (m, p // 2, 0))
    tall_m = pl.BlockSpec((None, nq, 128), lambda p, *_: (m, 0, p // 2))
    keys_m = pl.BlockSpec((None, win, 128), lambda p, *_: (m, 0, p // 2))
    return pl.pallas_call(
        attend_back_kernel,
        out_shape=tuple(pltpu.MemorySpace.VMEM(d, bf16) for d in ((nq, 384), (win, 384), (win, 384))),
        grid_spec=pltpu.PrefetchScalarGridSpec(
            num_scalar_prefetch=1, grid=(PAIRS,),
            in_specs=[wide_m, tall_m, keys_m, pl.BlockSpec((None, 128, win), lambda p, *_: (m, p // 2, 0)), keys_m,
                      pl.BlockSpec((128, nq), lambda p, *_: (p // 2, m)), pl.BlockSpec((nq, 128), lambda p, *_: (m, p // 2)), wide,
                      pl.BlockSpec((1, 8, nq), lambda p, *_: (p, 0, 0)),
                      pl.BlockSpec((win, 128), lambda p, *_: (0, 0)), pl.BlockSpec((128, nq), lambda p, *_: (0, 0))],
            out_specs=[tall, keys, keys],
            scratch_shapes=[pltpu.VMEM((128, nq), f32), pltpu.VMEM((256, 2 * TILE), bf16), pltpu.VMEM((256, 2 * TILE), bf16),
                            pltpu.VMEM((2 * TILE, 128), bf16), pltpu.VMEM((2 * TILE, 128), bf16),
                            pltpu.VMEM((win, 128), f32), pltpu.VMEM((win, 128), f32)],
        ),
        compiler_params=pltpu.CompilerParams(vmem_limit_bytes=32 << 20),
        cost_estimate=pl.CostEstimate(flops=int(40 * 10**9 * 0.02), bytes_accessed=0, transcendentals=0),
        name="attend_back",
    )(info, qT, q, k, kT, v, doT, do, oT, lse, kaug, qaugT)


def moments(x):
    centred = x - jnp.mean(x, axis=-1, keepdims=True)
    r = lax.rsqrt(jnp.mean(centred * centred, axis=-1, keepdims=True) + EPSILON)
    return centred * r, r


def norm_back(grad, n, r, gain):
    e = grad * gain
    return r * (e - jnp.mean(e, axis=-1, keepdims=True) - n * jnp.mean(e * n, axis=-1, keepdims=True))


def call(kernel, out_shape, name, flops=10**9, limit=48, **spec):
    return pl.pallas_call(
        kernel, out_shape=out_shape, name=name,
        compiler_params=pltpu.CompilerParams(vmem_limit_bytes=limit << 20),
        cost_estimate=pl.CostEstimate(flops=int(flops * 0.02), bytes_accessed=0, transcendentals=0), **spec)


def shape(*dims, dtype=bf16):
    return jax.ShapeDtypeStruct(dims, dtype)


def far(*dims, dtype=bf16):
    return pltpu.MemorySpace.HBM(dims, dtype)


def stay(*arrays):
    return [pltpu.with_memory_space_constraint(a, pltpu.MemorySpace.HBM) for a in arrays]


def scalar_first(grid, in_specs, out_specs, scratch=()):
    return dict(grid_spec=pltpu.PrefetchScalarGridSpec(
        num_scalar_prefetch=1, grid=grid, in_specs=in_specs, out_specs=out_specs, scratch_shapes=list(scratch)))


def full(*dims):
    return pl.BlockSpec(dims, lambda *_: (0,) * len(dims))


def pack_heads_kernel(core_ref, qkv_ref, vec_ref, heads_ref):
    for part in range(3):
        near = pl.ds(pl.multiple_of(640 * part + 256 * core_ref[0], 128), 256)
        heads_ref[:, 384 * part:384 * part + 256] = qkv_ref[:, near]
        heads_ref[:, 384 * part + 256:384 * (part + 1)] = qkv_ref[:, 640 * part + 512:640 * (part + 1)]
    heads_ref[:, 1152:1280] = vec_ref[...]


def pack_heads(core, w_qkv, vectors):
    return call(pack_heads_kernel, shape(160, 1280), "pack_heads", 10**6, 8, **scalar_first(
        (1,), [full(160, 1920), full(160, 128)], full(160, 1280)))(core, w_qkv, vectors)


def turn_kernel(vec_ref, rows_ref):
    rows_ref[...] = vec_ref[...].astype(f32).T[:16]


def vector_rows(heads):
    return call(turn_kernel, shape(16, 640, dtype=f32), "vector_rows", 10**12, 8, grid=(1,),
                in_specs=[pl.BlockSpec((640, 128), lambda i: (0, 9))], out_specs=full(16, 640))(*stay(heads))


def pack_feed_kernel(core_ref, out_ref, up_ref, down_ref, feed_ref):
    core = core_ref[0]
    feed_ref[:, 5120:5760] = out_ref[...]
    for f in range(4):
        feed_ref[:, 640 * f:640 * (f + 1)] = up_ref[:, pl.ds(pl.multiple_of(1280 * f + 640 * core, 128), 640)]
        feed_ref[:, 2560 + 640 * f:2560 + 640 * (f + 1)] = down_ref[pl.ds(pl.multiple_of(640 * core + 160 * f, 32), 160), :]


def pack_feed(core, w_out, w_up, w_down):
    return call(pack_feed_kernel, far(160, 5760), "pack_feed", 10**6, 16, **scalar_first(
        (1,), [full(160, 640), full(160, 5120), full(1280, 640)], full(160, 5760)))(core, *stay(w_out, w_up, w_down))


def rows_in_order(core, mine_ref, theirs_ref, x_ref):
    for c, (first, second) in enumerate(((mine_ref, theirs_ref), (theirs_ref, mine_ref))):
        @pl.when(core == c)
        def _():
            x_ref[0:256, :], x_ref[256:512, :] = first[...], second[...]


def normal_kernel(tok_ref, n_ref):
    for m in range(2):
        n_ref[m] = moments(tok_ref[m].astype(f32))[0].astype(bf16)


def normal_rows(tok):
    return call(normal_kernel, shape(2, 256, 640), "normal_rows", 10**6, 8, grid=(1,), in_specs=[full(2, 256, 640)], out_specs=full(2, 256, 640))(tok)


def project_kernel(chips, place_ref, *refs):
    n = len(chips)
    own_refs, other_refs = refs[:n], refs[n:2 * n]
    vec_ref, w_ref = refs[2 * n:2 * n + 2]
    k_ref, v_ref, kT_ref, vT_ref = refs[-6 - 2 * (n == 3):][:4]
    x_ref, hid_ref = refs[-2:]
    m, step = pl.program_id(0), pl.program_id(1)
    block = sum(jnp.where(step == i, chip, 0) for i, chip in enumerate(chips))
    needed = (block >= place_ref[1 + 2 * m]) & (block < place_ref[2 + 2 * m])

    @pl.when(jnp.logical_not(needed))
    def _():
        for ref in (k_ref, v_ref, kT_ref, vT_ref):
            ref[...] = jnp.zeros_like(ref)

    @pl.when(needed)
    def _():
        for j in range(n):
            @pl.when(step == j)
            def _():
                rows_in_order(place_ref[0], own_refs[j].at[m], other_refs[j].at[m], x_ref)

        hidden = (x_ref[...].astype(f32) * vec_ref[0:1, :] + vec_ref[1:2, :]).astype(bf16)
        hid_ref[...] = hidden
        kv = jnp.dot(hidden, w_ref[:, 384:], preferred_element_type=f32)
        low = kv.astype(bf16)
        k_ref[0] = low[:, :384]
        v_ref[0] = low[:, 384:]
        turned = kv.T.astype(bf16)
        kT_ref[0] = turned[:384]
        vT_ref[0] = turned[384:]

    if n == 3:
        q_ref, qT_ref = refs[-4:-2]

        @pl.when(step == 1)
        def _():
            q = jnp.dot(hid_ref[...], w_ref[:, :384], preferred_element_type=f32)
            q_ref[0] = q.astype(bf16)
            qT_ref[0] = q.T.astype(bf16)


def project(chips, place, own, other, vec, w, earlier=()):
    n = len(chips)
    chip = (lambda b: b + 1) if n == 3 else (lambda b: 4 * b)
    tall = pl.BlockSpec((1, 512, 384), lambda m, b, *_: (m, chip(b), 0))
    wide = pl.BlockSpec((1, 384, 512), lambda m, b, *_: (m, 0, chip(b)))
    shapes = [far(2, 2560, 384), far(2, 2560, 384), far(2, 384, 2560), far(2, 384, 2560)]
    specs = [tall, tall, wide, wide]
    if n == 3:
        shapes += [far(2, 512, 384), far(2, 384, 512)]
        specs += [pl.BlockSpec((1, 512, 384), lambda m, *_: (m, 0, 0)), pl.BlockSpec((1, 384, 512), lambda m, *_: (m, 0, 0))]
    own, other = [own[c] for c in chips], [other[c] for c in chips]
    return call(
        lambda *refs: project_kernel(chips, *refs), shapes, "project", 5 * 10**9, 28,
        input_output_aliases={2 * n + 3 + i: i for i in range(len(earlier))}, **scalar_first(
            (2, n), [full(2, 256, 640)] * (2 * n) + [full(16, 640), full(640, 1152)] + [pl.BlockSpec(memory_space=pl.ANY)] * len(earlier),
            specs, [pltpu.VMEM((512, 640), bf16), pltpu.VMEM((512, 640), bf16)]))(place, *own, *other, vec, *stay(w), *earlier)


def heads_joined(core, mine, theirs):
    first, second = (jnp.where(core == 0, a, b) for a, b in ((mine, theirs), (theirs, mine)))
    return jnp.concatenate([first[:, :256], second[:, :256], first[:, 256:] + second[:, 256:]], axis=1)


def middle_kernel(core_ref, w_ref, low0_ref, low1_ref, theirs_ref, tok_ref, tok2_ref, vec_ref, mid_ref, hid_ref, hid2_ref):
    core = core_ref[0]
    for m, low_ref in enumerate((low0_ref, low1_ref)):
        attended = heads_joined(core, low_ref[...].astype(f32), theirs_ref[m].astype(f32)).astype(bf16)
        branch = jnp.dot(attended, w_ref[...], preferred_element_type=f32)
        mine = jnp.where(core == 0, branch[:256], branch[256:]) + tok_ref[m].astype(f32)
        theirs = jnp.where(core == 0, branch[256:], branch[:256]) + tok2_ref[m].astype(f32)
        part = slice(256 * m, 256 * (m + 1))
        mid_ref[part, :] = mine
        hid_ref[part, :] = (moments(mine)[0] * vec_ref[2:3, :] + vec_ref[3:4, :]).astype(bf16)
        hid2_ref[part, :] = (moments(theirs)[0] * vec_ref[2:3, :] + vec_ref[3:4, :]).astype(bf16)


W_OUT = pl.BlockSpec((640, 640), lambda *_: (0, 8))


def middle_step(core, weights, *args):
    return call(middle_kernel, (far(512, 640, dtype=f32), far(512, 640), far(512, 640)), "middle", 10**9, 20, **scalar_first(
        (1,), [W_OUT] + [full(*a.shape) for a in args], [full(512, 640)] * 3))(core, *stay(weights), *args)


def feed_kernel(h_ref, h2_ref, cot_ref, cot2_ref, up_ref, down_ref, mine_ref, theirs_ref, g_ref, h, cot, hT, cT, out, dh):
    chunk = pl.program_id(0)

    @pl.when(chunk == 0)
    def _():
        h[0:512, :], h[512:1024, :] = h_ref[...], h2_ref[...]
        cot[0:512, :], cot[512:1024, :] = cot_ref[...], cot2_ref[...]
        hT[...] = h[...].astype(f32).T.astype(bf16)
        cT[...] = cot[...].astype(f32).T.astype(bf16)
        out[...] = jnp.zeros_like(out)
        dh[...] = jnp.zeros_like(dh)

    up_w = up_ref[...]
    down_w = jnp.concatenate([down_ref[160 * y:160 * (y + 1), 640 * i:640 * (i + 1)] for y in range(2) for i in range(4)], axis=0)
    acts, d_ups = [], []
    for t in range(4):
        rows = slice(256 * t, 256 * (t + 1))
        u = jnp.dot(h[rows, :], up_w, preferred_element_type=f32)
        d_act = lax.dot_general(cot[rows, :], down_w, NT, preferred_element_type=f32)
        cdf = 0.5 * (1.0 + lax.erf(u * (2.0 ** -0.5)))
        pdf = jnp.exp(u * u * -0.5) * ((2.0 * math.pi) ** -0.5)
        act = (u * cdf).astype(bf16)
        d_up = (d_act * (cdf + u * pdf)).astype(bf16)
        out[rows, :] += jnp.dot(act, down_w, preferred_element_type=f32)
        dh[rows, :] += lax.dot_general(d_up, up_w, NT, preferred_element_type=f32)
        acts.append(act)
        d_ups.append(d_up)
    g_up = jnp.dot(hT[...], jnp.concatenate(d_ups, axis=0), preferred_element_type=f32).astype(bf16)
    g_down = jnp.dot(cT[...], jnp.concatenate(acts, axis=0), preferred_element_type=f32).T.astype(bf16)
    for f in range(2):
        for y in range(4):
            for i in range(2):
                g_ref[4 * chunk + 2 * f + i, y] = g_up[160 * y + 80 * i:160 * y + 80 * (i + 1), 640 * f:640 * (f + 1)]
        for i in range(8):
            g_ref[8 + i, 2 * chunk + f] = g_down[640 * f + 80 * i:640 * f + 80 * (i + 1)]

    @pl.when(chunk == 1)
    def _():
        mine_ref[0], mine_ref[1] = out[0:512, :].astype(bf16), dh[0:512, :].astype(bf16)
        theirs_ref[0], theirs_ref[1] = out[512:1024, :].astype(bf16), dh[512:1024, :].astype(bf16)


def feed_forward(h, h2, cot, cot2, weights):
    return call(
        feed_kernel,
        (far(2, 512, 640), far(2, 512, 640), far(16, 4, 80, 640)),
        "feed_forward", 30 * 10**9, 52, grid=(2,),
        in_specs=[full(512, 640)] * 4 + [pl.BlockSpec((640, 1280), lambda f: (0, f)), pl.BlockSpec((320, 2560), lambda f: (f, 1))],
        out_specs=[full(2, 512, 640), full(2, 512, 640), full(16, 4, 80, 640)],
        scratch_shapes=[pltpu.VMEM((1024, 640), bf16), pltpu.VMEM((1024, 640), bf16), pltpu.VMEM((640, 1024), bf16), pltpu.VMEM((640, 1024), bf16),
                        pltpu.VMEM((1024, 640), f32), pltpu.VMEM((1024, 640), f32)],
    )(*stay(h, h2, cot), cot2, *stay(weights, weights))


def after_kernel(mid_ref, mine_ref, theirs_ref, cot_ref, vec_ref, block_ref, grad_ref, branch_ref, g_ref):
    @pl.when(pl.program_id(0) == 0)
    def _():
        g_ref[...] = jnp.zeros_like(g_ref)

    middle = mid_ref[...]
    block_ref[...] = (middle + mine_ref[0].astype(f32) + theirs_ref[0].astype(f32)).astype(bf16)
    d_hidden = mine_ref[1].astype(f32) + theirs_ref[1].astype(f32)
    n, r = moments(middle)
    g_ref[0:1, :] += jnp.sum(d_hidden * n, axis=0, keepdims=True)
    g_ref[1:2, :] += jnp.sum(d_hidden, axis=0, keepdims=True)
    grad = cot_ref[...].astype(f32) + norm_back(d_hidden, n, r, vec_ref[2:3, :])
    grad_ref[...] = grad
    branch_ref[...] = grad.astype(bf16)


def after_feed(*args):
    rows, pair = pl.BlockSpec((128, 640), lambda i: (i, 0)), pl.BlockSpec((2, 128, 640), lambda i: (0, i, 0))
    return call(
        after_kernel, (far(512, 640), far(512, 640, dtype=f32), shape(512, 640), shape(8, 640, dtype=f32)), "after_feed", 10**9, 16,
        grid=(4,), in_specs=[rows, pair, pair, rows, full(16, 640)], out_specs=[rows, rows, rows, full(8, 640)])(*stay(args[0], args[1]), args[2], *stay(args[3]), args[4])


def branch_kernel(core_ref, own_ref, their_ref, w_ref, low0_ref, low1_ref, theirs_ref, do_ref, doT_ref, g_ref):
    core = core_ref[0]
    w = jnp.concatenate([w_ref[pl.ds(pl.multiple_of(256 * core, 256), 256), :], w_ref[512:640, :]], axis=0)
    g = jnp.zeros((640, 384), f32)
    for m in range(2):
        part = slice(256 * m, 256 * (m + 1))
        mine, theirs = own_ref[part, :].astype(f32), their_ref[part, :].astype(f32)
        branch = jnp.concatenate([jnp.where(core == 0, mine, theirs), jnp.where(core == 0, theirs, mine)], axis=0)
        kept = jnp.where(core == 0, branch[:, :384], branch[:, 256:]).astype(bf16)
        branch = branch.astype(bf16)
        rows = slice(512 * m, 512 * (m + 1))
        do = lax.dot_general(branch, w, NT, preferred_element_type=f32)
        do_ref[rows, :] = do.astype(bf16)
        doT_ref[:, rows] = do.T.astype(bf16)
        attended = heads_joined(core, (low0_ref, low1_ref)[m][...].astype(f32), theirs_ref[m].astype(f32))
        g = g + jnp.dot(attended.T.astype(bf16), kept, preferred_element_type=f32)
    g_ref[...] = g.astype(bf16)


def branch_step(core, own, their, weights, *args):
    return call(
        branch_kernel, (far(1024, 384), far(384, 1024), shape(640, 384)), "branch", 10**9, 24, **scalar_first(
            (1,), [full(512, 640)] * 2 + [W_OUT] + [full(*a.shape) for a in args], [full(1024, 384), full(384, 1024), full(640, 384)]))(
                core, own, their, *stay(weights), *args)


def near_by(*arrays):
    return [pltpu.with_memory_space_constraint(a, pltpu.MemorySpace.VMEM) for a in arrays]


def project_back_kernel(place_ref, *refs):
    own_refs, other_refs = refs[:5], refs[5:10]
    (vec_ref, w_ref, dq0_ref, dq1_ref, dk0_ref, dk1_ref, dv0_ref, dv1_ref, g_out_ref, g_two_ref,
     mine_ref, theirs_ref, tail_ref, n_ref, d_kv, d_q, d_hid, g_ref, g_vec, slots, arrived) = refs[10:]
    step, core = pl.program_id(0), place_ref[0]
    block, second = lax.rem(step, 5), lax.div(step, 5)
    inside = lambda j, m: (j >= place_ref[1 + 2 * m]) & (j < place_ref[2 + 2 * m])
    needed = inside(block, second)

    def copies(j, m, slot):
        return [pltpu.make_async_copy(refs_of[j].at[m], slots.at[slot, i], arrived.at[slot, i]) for i, refs_of in enumerate((own_refs, other_refs))]

    @pl.when(step == 0)
    def _():
        for m in range(2):
            for j in range(5):
                @pl.when(inside(j, m))
                def _():
                    for copy in copies(j, m, 5 * m + j):
                        copy.start()
        g_ref[...] = jnp.zeros_like(g_ref)
        g_vec[...] = jnp.zeros_like(g_vec)
        g_vec[2:4, :] = g_two_ref[0:2, :]

    @pl.when(jnp.logical_not(needed))
    def _():
        mine_ref[...] = jnp.zeros_like(mine_ref)
        theirs_ref[...] = jnp.zeros_like(theirs_ref)

    @pl.when(needed)
    def _():
        for copy in copies(0, 0, step):
            copy.wait()
        rows_in_order(core, slots.at[step, 0], slots.at[step, 1], n_ref)

    for m, (dq, dk, dv) in enumerate(((dq0_ref, dk0_ref, dv0_ref), (dq1_ref, dk1_ref, dv1_ref))):
        @pl.when(needed & (second == m))
        def _():
            rows = pl.ds(pl.multiple_of(block * 512, 512), 512)
            d_kv[:, :384], d_kv[:, 384:] = dk[rows, :], dv[rows, :]
            d_q[...] = dq[...]

    @pl.when(needed)
    def _():
        n = n_ref[...].astype(f32)
        hiddenT = (n * vec_ref[0:1, :] + vec_ref[1:2, :]).T.astype(bf16)
        d_hid[...] = lax.dot_general(d_kv[...], w_ref[:, 384:1152], NT, preferred_element_type=f32)
        g_ref[:, 384:] += jnp.dot(hiddenT, d_kv[...], preferred_element_type=f32)

        @pl.when(block == 2)
        def _():
            g_ref[:, :384] += jnp.dot(hiddenT, d_q[...], preferred_element_type=f32)
            d_hid[...] += lax.dot_general(d_q[...], w_ref[:, :384], NT, preferred_element_type=f32)

        dh = d_hid[...]
        low = dh.astype(bf16)
        for c, (first, other) in enumerate(((mine_ref, theirs_ref), (theirs_ref, mine_ref))):
            @pl.when(core == c)
            def _():
                first[0, 0], other[0, 0] = low[:256], low[256:]
        g_vec[0:1, :] += jnp.sum(dh * n, axis=0, keepdims=True)
        g_vec[1:2, :] += jnp.sum(dh, axis=0, keepdims=True)

    @pl.when(step == 9)
    def _():
        turned = g_vec[...].T
        lane = lax.broadcasted_iota(jnp.int32, (640, 128), 1) - 64 * (1 - core)
        spare = g_ref[:, 256:384]
        for i in range(4):
            spare = jnp.where(lane == i, turned[:, i:i + 1], spare)
        g_ref[:, 256:384] = spare
        for y in range(4):
            for z in range(4):
                rows = slice(160 * y + 40 * z, 160 * y + 40 * (z + 1))
                for x in range(3):
                    tail_ref[16 * y + 4 * z + x] = g_ref[rows, 384 * x:384 * (x + 1)].astype(bf16)
                tail_ref[16 * y + 4 * z + 3] = g_out_ref[rows, :].astype(bf16)


def project_back(place, own, other, vec, w, dq, dk, dv, g_out, g_two):
    here = pl.BlockSpec(memory_space=pltpu.VMEM)
    part = pl.BlockSpec((1, 1, 256, 640), lambda b, *_: (lax.rem(b, 5), b // 5, 0, 0))
    return call(
        project_back_kernel, (far(5, 2, 256, 640), far(5, 2, 256, 640), far(64, 40, 384)), "project_back", 10**10, 30, **scalar_first(
            (10,), [pl.BlockSpec(memory_space=pl.ANY)] * 10 + [here] * 10, [part, part, full(64, 40, 384)],
            [pltpu.VMEM((512, 640), bf16), pltpu.VMEM((512, 768), bf16), pltpu.VMEM((512, 384), bf16),
             pltpu.VMEM((512, 640), f32), pltpu.VMEM((640, 1152), f32), pltpu.VMEM((8, 640), f32),
             pltpu.VMEM((10, 2, 256, 640), bf16), pltpu.SemaphoreType.DMA((10, 2))]))(
                 place, *stay(*own, *other), *near_by(vec, w, *dq, *dk, *dv, g_out, g_two))


def in_core_order(core_ref, mine, theirs):
    core, mine, theirs = core_ref[0], mine.astype(f32), theirs.astype(f32)
    return jnp.where(core == 0, mine, theirs), jnp.where(core == 0, theirs, mine)


def final_feed_kernel(core_ref, mine_ref, theirs_ref, up_ref, down_ref):
    for i in range(16):
        for c, piece in enumerate(in_core_order(core_ref, mine_ref[i], theirs_ref[i])):
            if i < 8:
                base = 1280 * (i // 2) + 640 * c
                up_ref[80 * (i % 2):80 * (i % 2 + 1), base:base + 640] = piece
            else:
                base = 640 * c + 80 * (i - 8)
                down_ref[base:base + 80, :] = piece


def final_feed(core, mine, theirs):
    return call(final_feed_kernel, (shape(160, 5120, dtype=f32), shape(1280, 640, dtype=f32)), "final_feed", 10**6, 32, **scalar_first(
        (1,), [full(16, 80, 640)] * 2, [full(160, 5120), full(1280, 640)]))(core, mine, theirs)


def final_heads_kernel(core_ref, mine_ref, theirs_ref, qkv_ref, out_ref, vec_ref):
    lane = lax.broadcasted_iota(jnp.int32, (40, 128), 1)
    for z in range(4):
        rows = slice(40 * z, 40 * (z + 1))
        for x in range(4):
            a, b = in_core_order(core_ref, mine_ref[4 * z + x], theirs_ref[4 * z + x])
            if x < 3:
                last = jnp.where(lane < 64, a[:, 256:], b[:, 256:])
                qkv_ref[rows, 640 * x:640 * (x + 1)] = jnp.concatenate([a[:, :256], b[:, :256], last], axis=1)
            else:
                out_ref[rows, :] = jnp.concatenate([a, b[:, 128:]], axis=1)
            if x == 0:
                vec_ref[rows, :] = pltpu.roll(a[:, 256:], 64, 1) + b[:, 256:]


def final_heads(core, mine, theirs):
    return call(
        final_heads_kernel, (shape(160, 1920, dtype=f32), shape(160, 640, dtype=f32), shape(160, 128, dtype=f32)), "final_heads", 10**6, 16,
        **scalar_first((1,), [full(16, 40, 384)] * 2, [full(160, 1920), full(160, 640), full(160, 128)]))(core, mine, theirs)


def shifted(array, axis, by):
    devices = lax.axis_size(axis)
    return lax.ppermute(array, axis, [(i, (i + by) % devices) for i in range(devices)])


def passed_along(array, by):
    devices = lax.axis_size(("z", "x"))
    return lax.ppermute(array, ("z", "x"), [(i, i + by) for i in range(devices) if 0 <= i + by < devices])


def swapped(array):
    return lax.ppermute(array, "core", [(0, 1), (1, 0)])


def pick(array, index):
    return lax.dynamic_index_in_dim(array, index, 0, keepdims=False)


def summed_share(array, axis):
    me, devices = lax.axis_index(axis), lax.axis_size(axis)
    total = pick(array, me).astype(f32)
    for by in (1, devices - 1, 2):
        total = total + shifted(pick(array, (me + by) % devices), axis, by).astype(f32)
    return total.astype(bf16)


def gathered(array, axis):
    me, devices = lax.axis_index(axis), lax.axis_size(axis)
    out = jnp.zeros((devices,) + array.shape, array.dtype)
    out = lax.dynamic_update_index_in_dim(out, array, me, 0)
    for by in (1, devices - 1, 2):
        out = lax.dynamic_update_index_in_dim(out, shifted(array, axis, by), (me + devices - by) % devices, 0)
    return out


def window_info(length_row, chip, core, win):
    ends = jnp.cumsum(length_row)
    starts = ends - length_row
    base = chip * 512 - 1024
    places = base + jnp.arange(win, dtype=jnp.int32)
    inside = (places[:, None] >= starts[None, :]) & (places[:, None] < ends[None, :])
    ones = jnp.broadcast_to(jnp.arange(64) < 3, (win, 64)).astype(bf16)
    key_rows = jnp.concatenate([jnp.where(inside, 0.0, -BIG).astype(bf16), ones], axis=1)
    own = chip * 512 + jnp.arange(512, dtype=jnp.int32)
    inside_q = (own[None, :] >= starts[:, None]) & (own[None, :] < ends[:, None])
    query_rows = jnp.concatenate([inside_q.astype(bf16), jnp.zeros((64, 512), bf16)], axis=0)
    info = [core]
    sizes = []
    for t in range(2):
        first = chip * 512 + t * TILE
        low = jnp.max(jnp.where(starts <= first, starts, 0)) - base
        high = jnp.min(jnp.where(ends > first + TILE - 1, ends, 1 << 30)) - base
        start = low // 128 * 128
        need = high - start
        size = (need + SHORT - 1) // SHORT * SHORT
        info.append(jnp.minimum(start, win - size))
        sizes.append(size)
    low = jnp.minimum(info[1], info[2]) // 512
    high = (jnp.maximum(info[1] + sizes[0], info[2] + sizes[1]) + 511) // 512
    return jnp.stack(info + sizes).astype(jnp.int32), key_rows, query_rows, [low, high]


def body(tokens, lengths, gain_one, bias_one, w_qkv, w_out, gain_two, bias_two, w_up, w_down, cotangent):
    core, chip = lax.axis_index("core"), lax.axis_index(("z", "x"))
    core_arg = core[None].astype(jnp.int32)
    tok, cot = tokens[:, 0], cotangent[:, 0].reshape(512, 640)
    together = lambda *arrays: lax.optimization_barrier(arrays)

    vectors = jnp.pad(jnp.stack([gain_one, bias_one, gain_two, bias_two], axis=1), ((0, 0), (0, 124)))
    heads, tok_sent = together(pack_heads(core_arg, w_qkv, vectors), tok)
    heads = lax.all_gather(heads, "batch", axis=0, tiled=True)
    vec = vector_rows(heads)
    normal = normal_rows(tok_sent)
    before, after, normal_other, tok_other = passed_along(normal, 1), passed_along(normal, -1), swapped(normal), swapped(tok)
    windows = [window_info(lengths[m, 0], chip, core, 2560) for m in range(2)]
    place = jnp.stack([core] + windows[0][3] + windows[1][3]).astype(jnp.int32)
    feed_pack = pack_feed(core_arg, w_out, w_up, w_down)
    heads, vec, before, after, normal_other, tok_other, feed_pack, place, windows = together(
        heads, vec, before, after, normal_other, tok_other, feed_pack, place, windows)
    own = [passed_along(before, 1), before, normal, after, passed_along(after, -1)]
    other = [None, swapped(before), normal_other, swapped(after), None]
    feed_weights = lax.all_gather(feed_pack, "batch", axis=0, tiled=True)
    *near_parts, q, qT = project((1, 2, 3), place, own, other, vec, heads)
    own[0], own[4], near_parts = together(own[0], own[4], near_parts)
    other[0], other[4] = swapped(own[0]), swapped(own[4])
    k, v, kT, vT = project((0, 4), place, own, other, vec, heads, near_parts)
    (oT0, low0, lse0), (oT1, low1, lse1) = (
        attend(m, info, qT, k, vT, key_rows, query_rows) for m, (info, key_rows, query_rows, _) in enumerate(windows))

    theirs = swapped(jnp.stack([low0, low1]))
    middle, hidden_two, hidden_other = middle_step(core_arg, feed_weights, low0, low1, theirs, tok, tok_other, vec)
    mine, partial, feed_grads = feed_forward(hidden_two, hidden_other, cot, swapped(cot), feed_weights)
    feed_grads = lax.psum_scatter(feed_grads.reshape(5120, 640), ("z", "x"), scatter_dimension=0, tiled=True)
    block_out, grad_middle, branch, g_two = after_feed(middle, mine, swapped(partial), cot, vec)

    do, doT, g_out = branch_step(core_arg, branch, swapped(branch), feed_weights, low0, low1, theirs)
    dq, dk, dv = zip(*(
        attend_back(m, info, qT, q, k, kT, v, doT, do, oT, lse, key_rows, query_rows)
        for m, ((info, key_rows, query_rows, _), oT, lse) in enumerate(zip(windows, (oT0, oT1), (lse0, lse1)))))
    mine, theirs, tail = project_back(place, own, other, vec, heads, dq, dk, dv, g_out, g_two)
    feed_grads, mine, theirs, tail = together(feed_grads, mine, theirs, tail)

    feed = summed_share(feed_grads.reshape(4, 80, 640), "batch")
    tail = lax.all_to_all(tail, ("batch", "z", "x"), 0, 0, tiled=True)
    theirs, mine, feed = together(swapped(theirs), mine, feed)
    feed = lax.all_gather(feed, ("z", "x"), axis=0, tiled=True).reshape(16, 80, 640)
    sums = [mine[j].astype(f32) + theirs[j].astype(f32) for j in range(5)]
    right, left = passed_along(sums[4].astype(bf16), 1), passed_along(sums[0].astype(bf16), -1)
    tail, right, left = together(tail, right, left)
    right, left = (right.astype(f32) + sums[3]).astype(bf16), (left.astype(f32) + sums[1]).astype(bf16)
    tail, right, left = together(jnp.sum(tail.astype(f32), axis=0).astype(bf16), right, left)
    right, left = passed_along(right, 1), passed_along(left, -1)
    tail = gathered(tail, "x").reshape(160, 384)
    tail = gathered(tail, "z").reshape(16, 40, 384)
    tail, right, left = together(tail, right, left)
    d_one = (sums[2] + right.astype(f32) + left.astype(f32)).reshape(512, 640)
    n_one, r_one = moments(tok.reshape(512, 640).astype(f32))
    grad_tokens = (grad_middle + norm_back(d_one, n_one, r_one, vec[0:1])).astype(bf16)
    tail, grad_tokens, feed = together(tail, grad_tokens, feed)
    grad_qkv, grad_out, spare = final_heads(core_arg, tail, swapped(tail))
    grad_up, grad_down = final_feed(core_arg, feed, swapped(feed))
    return (
        block_out.reshape(2, 1, 256, 640), grad_tokens.reshape(2, 1, 256, 640), spare[:, 0], spare[:, 1], grad_qkv, grad_out,
        spare[:, 2], spare[:, 3], grad_up, grad_down)


def solution(mesh):
    fine = Mesh(mesh.devices.reshape(4, 4, 4, 2), ("batch", "z", "x", "core"))
    rows = P(None, "batch", ("z", "x", "core"), None)
    one, two = P("batch"), P("batch", None)
    return jax.shard_map(
        body,
        mesh=fine,
        in_specs=(rows, P(None, "batch", None), one, one, two, two, one, one, two, two, rows),
        out_specs=(rows, rows, one, one, two, two, one, one, two, two),
        check_vma=False,
    )
```

```python
import math

import jax
import jax.numpy as jnp
from jax import lax
from jax.experimental import pallas as pl
from jax.experimental.pallas import tpu as pltpu
from jax.sharding import Mesh
from jax.sharding import PartitionSpec as P

HEAD_DIM = 32
SCALE = HEAD_DIM ** -0.5
LOG2E = math.log2(math.e)
C2 = SCALE * LOG2E
BIG = 1e30
TILE = 256
EPSILON = 1e-05
PAIRS = 5
SHORT, LONG = 384, 1152
f32, bf16 = jnp.float32, jnp.bfloat16
NT = (((1,), (1,)), ((), ()))


def pair_offset(info_ref):
    p = pl.program_id(0)
    sub = jnp.where(p == PAIRS - 1, info_ref[0], lax.rem(p, 2))
    return sub * (2 * HEAD_DIM)


def split3(v):
    a = v.astype(bf16)
    r = v - a.astype(f32)
    b = r.astype(bf16)
    d = (r - b.astype(f32)).astype(bf16)
    return a, b, d


def rows_masked(xT, off):
    row = lax.broadcasted_iota(jnp.int32, xT.shape, 0) - off
    xf = xT.astype(f32)
    return [jnp.where((row >= HEAD_DIM * j) & (row < HEAD_DIM * (j + 1)), xf, 0.0).astype(bf16) for j in range(2)]


def lanes_masked(x, off):
    lane = lax.broadcasted_iota(jnp.int32, x.shape, 1) - off
    xf = x.astype(f32)
    return [jnp.where((lane >= HEAD_DIM * j) & (lane < HEAD_DIM * (j + 1)), xf, 0.0).astype(bf16) for j in range(2)]


def attend_kernel(info_ref, qT_ref, k_ref, vT_ref, kaug_ref, qaugT_ref, oT_ref, o_ref, l_ref, rhs):
    off = pair_offset(info_ref)
    oT_ref[...] = jnp.where(lax.rem(pl.program_id(0), 2) == 0, 0.0, oT_ref[...])
    for t in range(2):
        cols = slice(t * TILE, (t + 1) * TILE)
        masked = rows_masked(qT_ref[:, cols], off)
        for j in range(2):
            rhs[0:128, j * TILE:(j + 1) * TILE] = masked[j]
            rhs[128:256, j * TILE:(j + 1) * TILE] = qaugT_ref[:, cols]
        start = info_ref[1 + t]
        need = info_ref[3 + t]

        def block(first, size):
            def step(i, carry):
                row = pl.multiple_of(first + i * size, 128)
                lhs = jnp.concatenate([k_ref[pl.ds(row, size), :], kaug_ref[pl.ds(row, size), :]], axis=1)
                raw = [jnp.dot(lhs, rhs[:, j * TILE:(j + 1) * TILE], preferred_element_type=f32) for j in range(2)]
                out = []
                for j in range(2):
                    m, l, o = carry[j]
                    s = raw[j] * C2
                    m_new = jnp.maximum(m, jnp.max(s, axis=0, keepdims=True))
                    alpha = jnp.exp2(m - m_new)
                    p = jnp.exp2(s - m_new)
                    vT = vT_ref[pl.ds(pl.multiple_of(off + j * HEAD_DIM, HEAD_DIM), HEAD_DIM), pl.ds(row, size)]
                    out.append((m_new, l * alpha + jnp.sum(p, axis=0, keepdims=True),
                                o * alpha + jnp.dot(vT, p.astype(bf16), preferred_element_type=f32)))
                return tuple(out)
            return step

        def finish(state):
            for j in range(2):
                m, l, o = state[j]
                oT_ref[pl.ds(pl.multiple_of(off + j * HEAD_DIM, HEAD_DIM), HEAD_DIM), cols] = o * (1.0 / l)
                l_ref[0, j:j + 1, cols] = m + jnp.log2(l)

        init = tuple((jnp.full((1, TILE), -1e38, f32), jnp.zeros((1, TILE), f32), jnp.zeros((HEAD_DIM, TILE), f32)) for _ in range(2))

        longs = lax.div(need, LONG)
        state = lax.fori_loop(0, longs, block(start, LONG), init)
        finish(lax.fori_loop(0, lax.div(need - longs * LONG, SHORT), block(start + longs * LONG, SHORT), state))

    o_ref[...] = oT_ref[...].T.astype(bf16)


def attend(m, info, qT, k, vT, kaug, qaugT):
    win, nq = k.shape[1], qT.shape[2]
    qT, k, vT = stay(qT, k, vT)
    return pl.pallas_call(
        attend_kernel,
        out_shape=(jax.ShapeDtypeStruct((384, nq), f32), jax.ShapeDtypeStruct((nq, 384), bf16), jax.ShapeDtypeStruct((PAIRS, 8, nq), f32)),
        grid_spec=pltpu.PrefetchScalarGridSpec(
            num_scalar_prefetch=1, grid=(PAIRS,),
            in_specs=[
                pl.BlockSpec((None, 128, nq), lambda p, *_: (m, p // 2, 0)),
                pl.BlockSpec((None, win, 128), lambda p, *_: (m, 0, p // 2)),
                pl.BlockSpec((None, 128, win), lambda p, *_: (m, p // 2, 0)),
                pl.BlockSpec((win, 128), lambda p, *_: (0, 0)),
                pl.BlockSpec((128, nq), lambda p, *_: (0, 0)),
            ],
            out_specs=[
                pl.BlockSpec((128, nq), lambda p, *_: (p // 2, 0)),
                pl.BlockSpec((nq, 128), lambda p, *_: (0, p // 2)),
                pl.BlockSpec((1, 8, nq), lambda p, *_: (p, 0, 0)),
            ],
            scratch_shapes=[pltpu.VMEM((256, 2 * TILE), bf16)],
        ),
        compiler_params=pltpu.CompilerParams(vmem_limit_bytes=28 << 20),
        cost_estimate=pl.CostEstimate(flops=int(20 * 10**9 * 0.02), bytes_accessed=0, transcendentals=0),
        name="attend",
    )(info, qT, k, vT, kaug, qaugT)


def attend_back_kernel(info_ref, qT_ref, q_ref, k_ref, kT_ref, v_ref, doT_ref, do_ref, oT_ref, l_ref, kaug_ref, qaugT_ref,
                       dq_ref, dk_ref, dv_ref, dqT_ref, rhs_s, rhs_d, q_stk, do_stk, dk_acc, dv_acc):
    p_id = pl.program_id(0)
    off = pair_offset(info_ref)

    @pl.when(lax.rem(p_id, 2) == 0)
    def _():
        dqT_ref[...] = jnp.zeros_like(dqT_ref)
        dk_acc[...] = jnp.zeros_like(dk_acc)
        dv_acc[...] = jnp.zeros_like(dv_acc)

    for t in range(2):
        cols = slice(t * TILE, (t + 1) * TILE)
        masked_q = rows_masked(qT_ref[:, cols], off)
        masked_do = rows_masked(doT_ref[:, cols], off)
        lane_q = lanes_masked(q_ref[cols, :], off)
        lane_do = lanes_masked(do_ref[cols, :], off)
        for j in range(2):
            part = slice(j * TILE, (j + 1) * TILE)
            head = pl.ds(pl.multiple_of(off + j * HEAD_DIM, HEAD_DIM), HEAD_DIM)
            delta = jnp.sum(doT_ref[head, cols].astype(f32) * oT_ref[head, cols], axis=0, keepdims=True)
            total = l_ref[0, j:j + 1, cols] * (1.0 / C2)
            rowid = lax.broadcasted_iota(jnp.int32, (64, TILE), 0)
            lp, dp = split3(-total), split3(-delta)
            def pieces(parts):
                x = jnp.zeros((64, TILE), f32)
                for n in range(3):
                    x = jnp.where(rowid == n, parts[n].astype(f32), x)
                return x.astype(bf16)
            rhs_s[0:128, part] = masked_q[j]
            rhs_s[128:192, part] = qaugT_ref[0:64, cols]
            rhs_s[192:256, part] = pieces(lp)
            rhs_d[0:128, part] = masked_do[j]
            rhs_d[128:192, part] = jnp.zeros((64, TILE), bf16)
            rhs_d[192:256, part] = pieces(dp)
            q_stk[part, :] = lane_q[j]
            do_stk[part, :] = lane_do[j]
        start = info_ref[1 + t]
        need = info_ref[3 + t]

        def block(first, size):
            def step(i, carry):
                row = pl.multiple_of(first + i * size, 128)
                rows = pl.ds(row, size)
                aug = kaug_ref[rows, :]
                lhs_k = jnp.concatenate([k_ref[rows, :], aug], axis=1)
                lhs_v = jnp.concatenate([v_ref[rows, :], aug], axis=1)
                out, dv, dk = [], dv_acc[rows, :], dk_acc[rows, :]
                for j in range(2):
                    part = slice(j * TILE, (j + 1) * TILE)
                    s = jnp.dot(lhs_k, rhs_s[:, part], preferred_element_type=f32)
                    dp = jnp.dot(lhs_v, rhs_d[:, part], preferred_element_type=f32)
                    p = jnp.exp2(s * C2)
                    ds = (p * dp).astype(bf16)
                    dv = dv + jnp.dot(p.astype(bf16), do_stk[part, :], preferred_element_type=f32)
                    dk = dk + jnp.dot(ds, q_stk[part, :], preferred_element_type=f32)
                    kT = kT_ref[pl.ds(pl.multiple_of(off + j * HEAD_DIM, HEAD_DIM), HEAD_DIM), rows]
                    out.append(carry[j] + jnp.dot(kT, ds, preferred_element_type=f32))
                dv_acc[rows, :] = dv
                dk_acc[rows, :] = dk
                return tuple(out)
            return step

        def finish(dqs):
            for j in range(2):
                dqT_ref[pl.ds(pl.multiple_of(off + j * HEAD_DIM, HEAD_DIM), HEAD_DIM), cols] = dqs[j] * SCALE

        init = tuple(jnp.zeros((HEAD_DIM, TILE), f32) for _ in range(2))

        longs = lax.div(need, LONG)
        state = lax.fori_loop(0, longs, block(start, LONG), init)
        finish(lax.fori_loop(0, lax.div(need - longs * LONG, SHORT), block(start + longs * LONG, SHORT), state))
    @pl.when((lax.rem(p_id, 2) == 1) | (p_id == PAIRS - 1))
    def _():
        dq_ref[...] = dqT_ref[...].T.astype(bf16)
        dk_ref[...] = (dk_acc[...] * SCALE).astype(bf16)
        dv_ref[...] = dv_acc[...].astype(bf16)


def attend_back(m, info, qT, q, k, kT, v, doT, do, oT, lse, kaug, qaugT):
    win, nq = k.shape[1], qT.shape[2]
    qT, q, k, kT, v, doT, do = stay(qT, q, k, kT, v, doT, do)
    wide = pl.BlockSpec((128, nq), lambda p, *_: (p // 2, 0))
    tall = pl.BlockSpec((nq, 128), lambda p, *_: (0, p // 2))
    keys = pl.BlockSpec((win, 128), lambda p, *_: (0, p // 2))
    wide_m = pl.BlockSpec((None, 128, nq), lambda p, *_: (m, p // 2, 0))
    tall_m = pl.BlockSpec((None, nq, 128), lambda p, *_: (m, 0, p // 2))
    keys_m = pl.BlockSpec((None, win, 128), lambda p, *_: (m, 0, p // 2))
    return pl.pallas_call(
        attend_back_kernel,
        out_shape=tuple(pltpu.MemorySpace.VMEM(d, bf16) for d in ((nq, 384), (win, 384), (win, 384))),
        grid_spec=pltpu.PrefetchScalarGridSpec(
            num_scalar_prefetch=1, grid=(PAIRS,),
            in_specs=[wide_m, tall_m, keys_m, pl.BlockSpec((None, 128, win), lambda p, *_: (m, p // 2, 0)), keys_m,
                      pl.BlockSpec((128, nq), lambda p, *_: (p // 2, m)), pl.BlockSpec((nq, 128), lambda p, *_: (m, p // 2)), wide,
                      pl.BlockSpec((1, 8, nq), lambda p, *_: (p, 0, 0)),
                      pl.BlockSpec((win, 128), lambda p, *_: (0, 0)), pl.BlockSpec((128, nq), lambda p, *_: (0, 0))],
            out_specs=[tall, keys, keys],
            scratch_shapes=[pltpu.VMEM((128, nq), f32), pltpu.VMEM((256, 2 * TILE), bf16), pltpu.VMEM((256, 2 * TILE), bf16),
                            pltpu.VMEM((2 * TILE, 128), bf16), pltpu.VMEM((2 * TILE, 128), bf16),
                            pltpu.VMEM((win, 128), f32), pltpu.VMEM((win, 128), f32)],
        ),
        compiler_params=pltpu.CompilerParams(vmem_limit_bytes=32 << 20),
        cost_estimate=pl.CostEstimate(flops=int(40 * 10**9 * 0.02), bytes_accessed=0, transcendentals=0),
        name="attend_back",
    )(info, qT, q, k, kT, v, doT, do, oT, lse, kaug, qaugT)


def moments(x):
    centred = x - jnp.mean(x, axis=-1, keepdims=True)
    r = lax.rsqrt(jnp.mean(centred * centred, axis=-1, keepdims=True) + EPSILON)
    return centred * r, r


def norm_back(grad, n, r, gain):
    e = grad * gain
    return r * (e - jnp.mean(e, axis=-1, keepdims=True) - n * jnp.mean(e * n, axis=-1, keepdims=True))


def call(kernel, out_shape, name, flops=10**9, limit=48, **spec):
    return pl.pallas_call(
        kernel, out_shape=out_shape, name=name,
        compiler_params=pltpu.CompilerParams(vmem_limit_bytes=limit << 20),
        cost_estimate=pl.CostEstimate(flops=int(flops * 0.02), bytes_accessed=0, transcendentals=0), **spec)


def shape(*dims, dtype=bf16):
    return jax.ShapeDtypeStruct(dims, dtype)


def far(*dims, dtype=bf16):
    return pltpu.MemorySpace.HBM(dims, dtype)


def stay(*arrays):
    return [pltpu.with_memory_space_constraint(a, pltpu.MemorySpace.HBM) for a in arrays]


def scalar_first(grid, in_specs, out_specs, scratch=()):
    return dict(grid_spec=pltpu.PrefetchScalarGridSpec(
        num_scalar_prefetch=1, grid=grid, in_specs=in_specs, out_specs=out_specs, scratch_shapes=list(scratch)))


def full(*dims):
    return pl.BlockSpec(dims, lambda *_: (0,) * len(dims))


def pack_heads_kernel(core_ref, qkv_ref, vec_ref, heads_ref):
    for part in range(3):
        near = pl.ds(pl.multiple_of(640 * part + 256 * core_ref[0], 128), 256)
        heads_ref[:, 384 * part:384 * part + 256] = qkv_ref[:, near]
        heads_ref[:, 384 * part + 256:384 * (part + 1)] = qkv_ref[:, 640 * part + 512:640 * (part + 1)]
    heads_ref[:, 1152:1280] = vec_ref[...]


def pack_heads(core, w_qkv, vectors):
    return call(pack_heads_kernel, shape(160, 1280), "pack_heads", 10**6, 8, **scalar_first(
        (1,), [full(160, 1920), full(160, 128)], full(160, 1280)))(core, w_qkv, vectors)


def turn_kernel(vec_ref, rows_ref):
    rows_ref[...] = vec_ref[...].astype(f32).T[:16]


def vector_rows(heads):
    return call(turn_kernel, shape(16, 640, dtype=f32), "vector_rows", 10**12, 8, grid=(1,),
                in_specs=[pl.BlockSpec((640, 128), lambda i: (0, 9))], out_specs=full(16, 640))(*stay(heads))


def pack_feed_kernel(core_ref, out_ref, up_ref, down_ref, feed_ref):
    core = core_ref[0]
    feed_ref[:, 5120:5760] = out_ref[...]
    for f in range(4):
        feed_ref[:, 640 * f:640 * (f + 1)] = up_ref[:, pl.ds(pl.multiple_of(1280 * f + 640 * core, 128), 640)]
        feed_ref[:, 2560 + 640 * f:2560 + 640 * (f + 1)] = down_ref[pl.ds(pl.multiple_of(640 * core + 160 * f, 32), 160), :]


def pack_feed(core, w_out, w_up, w_down):
    return call(pack_feed_kernel, far(160, 5760), "pack_feed", 10**6, 16, **scalar_first(
        (1,), [full(160, 640), full(160, 5120), full(1280, 640)], full(160, 5760)))(core, *stay(w_out, w_up, w_down))


def rows_in_order(core, mine_ref, theirs_ref, x_ref):
    for c, (first, second) in enumerate(((mine_ref, theirs_ref), (theirs_ref, mine_ref))):
        @pl.when(core == c)
        def _():
            x_ref[0:256, :], x_ref[256:512, :] = first[...], second[...]


def normal_kernel(tok_ref, n_ref):
    for m in range(2):
        n_ref[m] = moments(tok_ref[m].astype(f32))[0].astype(bf16)


def normal_rows(tok):
    return call(normal_kernel, shape(2, 256, 640), "normal_rows", 10**6, 8, grid=(1,), in_specs=[full(2, 256, 640)], out_specs=full(2, 256, 640))(tok)


def project_kernel(chips, place_ref, *refs):
    n = len(chips)
    own_refs, other_refs = refs[:n], refs[n:2 * n]
    vec_ref, w_ref = refs[2 * n:2 * n + 2]
    k_ref, v_ref, kT_ref, vT_ref = refs[-6 - 2 * (n == 3):][:4]
    x_ref, hid_ref = refs[-2:]
    m, step = pl.program_id(0), pl.program_id(1)
    block = sum(jnp.where(step == i, chip, 0) for i, chip in enumerate(chips))
    needed = (block >= place_ref[1 + 2 * m]) & (block < place_ref[2 + 2 * m])

    @pl.when(jnp.logical_not(needed))
    def _():
        for ref in (k_ref, v_ref, kT_ref, vT_ref):
            ref[...] = jnp.zeros_like(ref)

    @pl.when(needed)
    def _():
        for j in range(n):
            @pl.when(step == j)
            def _():
                rows_in_order(place_ref[0], own_refs[j].at[m], other_refs[j].at[m], x_ref)

        hidden = (x_ref[...].astype(f32) * vec_ref[0:1, :] + vec_ref[1:2, :]).astype(bf16)
        hid_ref[...] = hidden
        kv = jnp.dot(hidden, w_ref[:, 384:], preferred_element_type=f32)
        low = kv.astype(bf16)
        k_ref[0] = low[:, :384]
        v_ref[0] = low[:, 384:]
        turned = kv.T.astype(bf16)
        kT_ref[0] = turned[:384]
        vT_ref[0] = turned[384:]

    if n == 3:
        q_ref, qT_ref = refs[-4:-2]

        @pl.when(step == 1)
        def _():
            q = jnp.dot(hid_ref[...], w_ref[:, :384], preferred_element_type=f32)
            q_ref[0] = q.astype(bf16)
            qT_ref[0] = q.T.astype(bf16)


def project(chips, place, own, other, vec, w, earlier=()):
    n = len(chips)
    chip = (lambda b: b + 1) if n == 3 else (lambda b: 4 * b)
    tall = pl.BlockSpec((1, 512, 384), lambda m, b, *_: (m, chip(b), 0))
    wide = pl.BlockSpec((1, 384, 512), lambda m, b, *_: (m, 0, chip(b)))
    shapes = [far(2, 2560, 384), far(2, 2560, 384), far(2, 384, 2560), far(2, 384, 2560)]
    specs = [tall, tall, wide, wide]
    if n == 3:
        shapes += [far(2, 512, 384), far(2, 384, 512)]
        specs += [pl.BlockSpec((1, 512, 384), lambda m, *_: (m, 0, 0)), pl.BlockSpec((1, 384, 512), lambda m, *_: (m, 0, 0))]
    own, other = [own[c] for c in chips], [other[c] for c in chips]
    return call(
        lambda *refs: project_kernel(chips, *refs), shapes, "project", 5 * 10**9, 28,
        input_output_aliases={2 * n + 3 + i: i for i in range(len(earlier))}, **scalar_first(
            (2, n), [full(2, 256, 640)] * (2 * n) + [full(16, 640), full(640, 1152)] + [pl.BlockSpec(memory_space=pl.ANY)] * len(earlier),
            specs, [pltpu.VMEM((512, 640), bf16), pltpu.VMEM((512, 640), bf16)]))(place, *own, *other, vec, *stay(w), *earlier)


def heads_joined(core, mine, theirs):
    first, second = (jnp.where(core == 0, a, b) for a, b in ((mine, theirs), (theirs, mine)))
    return jnp.concatenate([first[:, :256], second[:, :256], first[:, 256:] + second[:, 256:]], axis=1)


def middle_kernel(core_ref, w_ref, low0_ref, low1_ref, theirs_ref, tok_ref, tok2_ref, vec_ref, mid_ref, hid_ref, hid2_ref):
    core = core_ref[0]
    for m, low_ref in enumerate((low0_ref, low1_ref)):
        attended = heads_joined(core, low_ref[...].astype(f32), theirs_ref[m].astype(f32)).astype(bf16)
        branch = jnp.dot(attended, w_ref[...], preferred_element_type=f32)
        mine = jnp.where(core == 0, branch[:256], branch[256:]) + tok_ref[m].astype(f32)
        theirs = jnp.where(core == 0, branch[256:], branch[:256]) + tok2_ref[m].astype(f32)
        part = slice(256 * m, 256 * (m + 1))
        mid_ref[part, :] = mine
        hid_ref[part, :] = (moments(mine)[0] * vec_ref[2:3, :] + vec_ref[3:4, :]).astype(bf16)
        hid2_ref[part, :] = (moments(theirs)[0] * vec_ref[2:3, :] + vec_ref[3:4, :]).astype(bf16)


W_OUT = pl.BlockSpec((640, 640), lambda *_: (0, 8))


def middle_step(core, weights, *args):
    return call(middle_kernel, (far(512, 640, dtype=f32), far(512, 640), far(512, 640)), "middle", 10**9, 20, **scalar_first(
        (1,), [W_OUT] + [full(*a.shape) for a in args], [full(512, 640)] * 3))(core, *stay(weights), *args)


def feed_kernel(h_ref, h2_ref, cot_ref, cot2_ref, up_ref, down_ref, mine_ref, theirs_ref, g_ref, h, cot, hT, cT, out, dh):
    chunk = pl.program_id(0)

    @pl.when(chunk == 0)
    def _():
        h[0:512, :], h[512:1024, :] = h_ref[...], h2_ref[...]
        cot[0:512, :], cot[512:1024, :] = cot_ref[...], cot2_ref[...]
        hT[...] = h[...].astype(f32).T.astype(bf16)
        cT[...] = cot[...].astype(f32).T.astype(bf16)
        out[...] = jnp.zeros_like(out)
        dh[...] = jnp.zeros_like(dh)

    up_w = up_ref[...]
    down_w = jnp.concatenate([down_ref[160 * y:160 * (y + 1), 640 * i:640 * (i + 1)] for y in range(2) for i in range(4)], axis=0)
    acts, d_ups = [], []
    for t in range(4):
        rows = slice(256 * t, 256 * (t + 1))
        u = jnp.dot(h[rows, :], up_w, preferred_element_type=f32)
        d_act = lax.dot_general(cot[rows, :], down_w, NT, preferred_element_type=f32)
        cdf = 0.5 * (1.0 + lax.erf(u * (2.0 ** -0.5)))
        pdf = jnp.exp(u * u * -0.5) * ((2.0 * math.pi) ** -0.5)
        act = (u * cdf).astype(bf16)
        d_up = (d_act * (cdf + u * pdf)).astype(bf16)
        out[rows, :] += jnp.dot(act, down_w, preferred_element_type=f32)
        dh[rows, :] += lax.dot_general(d_up, up_w, NT, preferred_element_type=f32)
        acts.append(act)
        d_ups.append(d_up)
    g_up = jnp.dot(hT[...], jnp.concatenate(d_ups, axis=0), preferred_element_type=f32).astype(bf16)
    g_down = jnp.dot(cT[...], jnp.concatenate(acts, axis=0), preferred_element_type=f32).T.astype(bf16)
    for f in range(2):
        for y in range(4):
            for i in range(2):
                g_ref[4 * chunk + 2 * f + i, y] = g_up[160 * y + 80 * i:160 * y + 80 * (i + 1), 640 * f:640 * (f + 1)]
        for i in range(8):
            g_ref[8 + i, 2 * chunk + f] = g_down[640 * f + 80 * i:640 * f + 80 * (i + 1)]

    @pl.when(chunk == 1)
    def _():
        mine_ref[0], mine_ref[1] = out[0:512, :].astype(bf16), dh[0:512, :].astype(bf16)
        theirs_ref[0], theirs_ref[1] = out[512:1024, :].astype(bf16), dh[512:1024, :].astype(bf16)


def feed_forward(h, h2, cot, cot2, weights):
    return call(
        feed_kernel,
        (far(2, 512, 640), far(2, 512, 640), far(16, 4, 80, 640)),
        "feed_forward", 30 * 10**9, 52, grid=(2,),
        in_specs=[full(512, 640)] * 4 + [pl.BlockSpec((640, 1280), lambda f: (0, f)), pl.BlockSpec((320, 2560), lambda f: (f, 1))],
        out_specs=[full(2, 512, 640), full(2, 512, 640), full(16, 4, 80, 640)],
        scratch_shapes=[pltpu.VMEM((1024, 640), bf16), pltpu.VMEM((1024, 640), bf16), pltpu.VMEM((640, 1024), bf16), pltpu.VMEM((640, 1024), bf16),
                        pltpu.VMEM((1024, 640), f32), pltpu.VMEM((1024, 640), f32)],
    )(*stay(h, h2, cot), cot2, *stay(weights, weights))


def after_kernel(mid_ref, mine_ref, theirs_ref, cot_ref, vec_ref, block_ref, grad_ref, branch_ref, g_ref):
    @pl.when(pl.program_id(0) == 0)
    def _():
        g_ref[...] = jnp.zeros_like(g_ref)

    middle = mid_ref[...]
    block_ref[...] = (middle + mine_ref[0].astype(f32) + theirs_ref[0].astype(f32)).astype(bf16)
    d_hidden = mine_ref[1].astype(f32) + theirs_ref[1].astype(f32)
    n, r = moments(middle)
    g_ref[0:1, :] += jnp.sum(d_hidden * n, axis=0, keepdims=True)
    g_ref[1:2, :] += jnp.sum(d_hidden, axis=0, keepdims=True)
    grad = cot_ref[...].astype(f32) + norm_back(d_hidden, n, r, vec_ref[2:3, :])
    grad_ref[...] = grad
    branch_ref[...] = grad.astype(bf16)


def after_feed(*args):
    rows, pair = pl.BlockSpec((128, 640), lambda i: (i, 0)), pl.BlockSpec((2, 128, 640), lambda i: (0, i, 0))
    return call(
        after_kernel, (far(512, 640), far(512, 640, dtype=f32), shape(512, 640), shape(8, 640, dtype=f32)), "after_feed", 10**9, 16,
        grid=(4,), in_specs=[rows, pair, pair, rows, full(16, 640)], out_specs=[rows, rows, rows, full(8, 640)])(*stay(args[0], args[1]), args[2], *stay(args[3]), args[4])


def branch_kernel(core_ref, own_ref, their_ref, w_ref, low0_ref, low1_ref, theirs_ref, do_ref, doT_ref, g_ref):
    core = core_ref[0]
    w = jnp.concatenate([w_ref[pl.ds(pl.multiple_of(256 * core, 256), 256), :], w_ref[512:640, :]], axis=0)
    g = jnp.zeros((640, 384), f32)
    for m in range(2):
        part = slice(256 * m, 256 * (m + 1))
        mine, theirs = own_ref[part, :].astype(f32), their_ref[part, :].astype(f32)
        branch = jnp.concatenate([jnp.where(core == 0, mine, theirs), jnp.where(core == 0, theirs, mine)], axis=0)
        kept = jnp.where(core == 0, branch[:, :384], branch[:, 256:]).astype(bf16)
        branch = branch.astype(bf16)
        rows = slice(512 * m, 512 * (m + 1))
        do = lax.dot_general(branch, w, NT, preferred_element_type=f32)
        do_ref[rows, :] = do.astype(bf16)
        doT_ref[:, rows] = do.T.astype(bf16)
        attended = heads_joined(core, (low0_ref, low1_ref)[m][...].astype(f32), theirs_ref[m].astype(f32))
        g = g + jnp.dot(attended.T.astype(bf16), kept, preferred_element_type=f32)
    g_ref[...] = g.astype(bf16)


def branch_step(core, own, their, weights, *args):
    return call(
        branch_kernel, (far(1024, 384), far(384, 1024), shape(640, 384)), "branch", 10**9, 24, **scalar_first(
            (1,), [full(512, 640)] * 2 + [W_OUT] + [full(*a.shape) for a in args], [full(1024, 384), full(384, 1024), full(640, 384)]))(
                core, own, their, *stay(weights), *args)


def near_by(*arrays):
    return [pltpu.with_memory_space_constraint(a, pltpu.MemorySpace.VMEM) for a in arrays]


def project_back_kernel(place_ref, *refs):
    own_refs, other_refs = refs[:5], refs[5:10]
    (vec_ref, w_ref, dq0_ref, dq1_ref, dk0_ref, dk1_ref, dv0_ref, dv1_ref, g_out_ref, g_two_ref,
     mine_ref, theirs_ref, tail_ref, n_ref, d_kv, d_q, d_hid, g_ref, g_vec, slots, arrived) = refs[10:]
    step, core = pl.program_id(0), place_ref[0]
    block, second = lax.rem(step, 5), lax.div(step, 5)
    inside = lambda j, m: (j >= place_ref[1 + 2 * m]) & (j < place_ref[2 + 2 * m])
    needed = inside(block, second)

    def copies(j, m, slot):
        return [pltpu.make_async_copy(refs_of[j].at[m], slots.at[slot, i], arrived.at[slot, i]) for i, refs_of in enumerate((own_refs, other_refs))]

    @pl.when(step == 0)
    def _():
        for m in range(2):
            for j in range(5):
                @pl.when(inside(j, m))
                def _():
                    for copy in copies(j, m, 5 * m + j):
                        copy.start()
        g_ref[...] = jnp.zeros_like(g_ref)
        g_vec[...] = jnp.zeros_like(g_vec)
        g_vec[2:4, :] = g_two_ref[0:2, :]

    @pl.when(jnp.logical_not(needed))
    def _():
        mine_ref[...] = jnp.zeros_like(mine_ref)
        theirs_ref[...] = jnp.zeros_like(theirs_ref)

    @pl.when(needed)
    def _():
        for copy in copies(0, 0, step):
            copy.wait()
        rows_in_order(core, slots.at[step, 0], slots.at[step, 1], n_ref)

    for m, (dq, dk, dv) in enumerate(((dq0_ref, dk0_ref, dv0_ref), (dq1_ref, dk1_ref, dv1_ref))):
        @pl.when(needed & (second == m))
        def _():
            rows = pl.ds(pl.multiple_of(block * 512, 512), 512)
            d_kv[:, :384], d_kv[:, 384:] = dk[rows, :], dv[rows, :]
            d_q[...] = dq[...]

    @pl.when(needed)
    def _():
        n = n_ref[...].astype(f32)
        hiddenT = (n * vec_ref[0:1, :] + vec_ref[1:2, :]).T.astype(bf16)
        d_hid[...] = lax.dot_general(d_kv[...], w_ref[:, 384:1152], NT, preferred_element_type=f32)
        g_ref[:, 384:] += jnp.dot(hiddenT, d_kv[...], preferred_element_type=f32)

        @pl.when(block == 2)
        def _():
            g_ref[:, :384] += jnp.dot(hiddenT, d_q[...], preferred_element_type=f32)
            d_hid[...] += lax.dot_general(d_q[...], w_ref[:, :384], NT, preferred_element_type=f32)

        dh = d_hid[...]
        low = dh.astype(bf16)
        for c, (first, other) in enumerate(((mine_ref, theirs_ref), (theirs_ref, mine_ref))):
            @pl.when(core == c)
            def _():
                first[0, 0], other[0, 0] = low[:256], low[256:]
        g_vec[0:1, :] += jnp.sum(dh * n, axis=0, keepdims=True)
        g_vec[1:2, :] += jnp.sum(dh, axis=0, keepdims=True)

    @pl.when(step == 9)
    def _():
        turned = g_vec[...].T
        lane = lax.broadcasted_iota(jnp.int32, (640, 128), 1) - 64 * (1 - core)
        spare = g_ref[:, 256:384]
        for i in range(4):
            spare = jnp.where(lane == i, turned[:, i:i + 1], spare)
        g_ref[:, 256:384] = spare
        for y in range(4):
            for z in range(4):
                rows = slice(160 * y + 40 * z, 160 * y + 40 * (z + 1))
                for x in range(3):
                    tail_ref[16 * y + 4 * z + x] = g_ref[rows, 384 * x:384 * (x + 1)].astype(bf16)
                tail_ref[16 * y + 4 * z + 3] = g_out_ref[rows, :].astype(bf16)


def project_back(place, own, other, vec, w, dq, dk, dv, g_out, g_two):
    here = pl.BlockSpec(memory_space=pltpu.VMEM)
    part = pl.BlockSpec((1, 1, 256, 640), lambda b, *_: (lax.rem(b, 5), b // 5, 0, 0))
    return call(
        project_back_kernel, (far(5, 2, 256, 640), far(5, 2, 256, 640), far(64, 40, 384)), "project_back", 10**10, 30, **scalar_first(
            (10,), [pl.BlockSpec(memory_space=pl.ANY)] * 10 + [here] * 10, [part, part, full(64, 40, 384)],
            [pltpu.VMEM((512, 640), bf16), pltpu.VMEM((512, 768), bf16), pltpu.VMEM((512, 384), bf16),
             pltpu.VMEM((512, 640), f32), pltpu.VMEM((640, 1152), f32), pltpu.VMEM((8, 640), f32),
             pltpu.VMEM((10, 2, 256, 640), bf16), pltpu.SemaphoreType.DMA((10, 2))]))(
                 place, *stay(*own, *other), *near_by(vec, w, *dq, *dk, *dv, g_out, g_two))


def in_core_order(core_ref, mine, theirs):
    core, mine, theirs = core_ref[0], mine.astype(f32), theirs.astype(f32)
    return jnp.where(core == 0, mine, theirs), jnp.where(core == 0, theirs, mine)


def final_feed_kernel(core_ref, mine_ref, theirs_ref, up_ref, down_ref):
    for i in range(16):
        for c, piece in enumerate(in_core_order(core_ref, mine_ref[i], theirs_ref[i])):
            if i < 8:
                base = 1280 * (i // 2) + 640 * c
                up_ref[80 * (i % 2):80 * (i % 2 + 1), base:base + 640] = piece
            else:
                base = 640 * c + 80 * (i - 8)
                down_ref[base:base + 80, :] = piece


def final_feed(core, mine, theirs):
    return call(final_feed_kernel, (shape(160, 5120, dtype=f32), shape(1280, 640, dtype=f32)), "final_feed", 10**6, 32, **scalar_first(
        (1,), [full(16, 80, 640)] * 2, [full(160, 5120), full(1280, 640)]))(core, mine, theirs)


def final_heads_kernel(core_ref, mine_ref, theirs_ref, qkv_ref, out_ref, vec_ref):
    lane = lax.broadcasted_iota(jnp.int32, (40, 128), 1)
    for z in range(4):
        rows = slice(40 * z, 40 * (z + 1))
        for x in range(4):
            a, b = in_core_order(core_ref, mine_ref[4 * z + x], theirs_ref[4 * z + x])
            if x < 3:
                last = jnp.where(lane < 64, a[:, 256:], b[:, 256:])
                qkv_ref[rows, 640 * x:640 * (x + 1)] = jnp.concatenate([a[:, :256], b[:, :256], last], axis=1)
            else:
                out_ref[rows, :] = jnp.concatenate([a, b[:, 128:]], axis=1)
            if x == 0:
                vec_ref[rows, :] = pltpu.roll(a[:, 256:], 64, 1) + b[:, 256:]


def final_heads(core, mine, theirs):
    return call(
        final_heads_kernel, (shape(160, 1920, dtype=f32), shape(160, 640, dtype=f32), shape(160, 128, dtype=f32)), "final_heads", 10**6, 16,
        **scalar_first((1,), [full(16, 40, 384)] * 2, [full(160, 1920), full(160, 640), full(160, 128)]))(core, mine, theirs)


def shifted(array, axis, by):
    devices = lax.axis_size(axis)
    return lax.ppermute(array, axis, [(i, (i + by) % devices) for i in range(devices)])


def passed_along(array, by):
    devices = lax.axis_size(("z", "x"))
    return lax.ppermute(array, ("z", "x"), [(i, i + by) for i in range(devices) if 0 <= i + by < devices])


def swapped(array):
    return lax.ppermute(array, "core", [(0, 1), (1, 0)])


def pick(array, index):
    return lax.dynamic_index_in_dim(array, index, 0, keepdims=False)


def summed_share(array, axis):
    me, devices = lax.axis_index(axis), lax.axis_size(axis)
    total = pick(array, me).astype(f32)
    for by in (1, devices - 1, 2):
        total = total + shifted(pick(array, (me + by) % devices), axis, by).astype(f32)
    return total.astype(bf16)


def gathered(array, axis):
    me, devices = lax.axis_index(axis), lax.axis_size(axis)
    out = jnp.zeros((devices,) + array.shape, array.dtype)
    out = lax.dynamic_update_index_in_dim(out, array, me, 0)
    for by in (1, devices - 1, 2):
        out = lax.dynamic_update_index_in_dim(out, shifted(array, axis, by), (me + devices - by) % devices, 0)
    return out


def window_info(length_row, chip, core, win):
    ends = jnp.cumsum(length_row)
    starts = ends - length_row
    base = chip * 512 - 1024
    places = base + jnp.arange(win, dtype=jnp.int32)
    inside = (places[:, None] >= starts[None, :]) & (places[:, None] < ends[None, :])
    ones = jnp.broadcast_to(jnp.arange(64) < 3, (win, 64)).astype(bf16)
    key_rows = jnp.concatenate([jnp.where(inside, 0.0, -BIG).astype(bf16), ones], axis=1)
    own = chip * 512 + jnp.arange(512, dtype=jnp.int32)
    inside_q = (own[None, :] >= starts[:, None]) & (own[None, :] < ends[:, None])
    query_rows = jnp.concatenate([inside_q.astype(bf16), jnp.zeros((64, 512), bf16)], axis=0)
    info = [core]
    sizes = []
    for t in range(2):
        first = chip * 512 + t * TILE
        low = jnp.max(jnp.where(starts <= first, starts, 0)) - base
        high = jnp.min(jnp.where(ends > first + TILE - 1, ends, 1 << 30)) - base
        start = low // 128 * 128
        need = high - start
        size = (need + SHORT - 1) // SHORT * SHORT
        info.append(jnp.minimum(start, win - size))
        sizes.append(size)
    low = jnp.minimum(info[1], info[2]) // 512
    high = (jnp.maximum(info[1] + sizes[0], info[2] + sizes[1]) + 511) // 512
    return jnp.stack(info + sizes).astype(jnp.int32), key_rows, query_rows, [low, high]


def body(tokens, lengths, gain_one, bias_one, w_qkv, w_out, gain_two, bias_two, w_up, w_down, cotangent):
    core, chip = lax.axis_index("core"), lax.axis_index(("z", "x"))
    core_arg = core[None].astype(jnp.int32)
    tok, cot = tokens[:, 0], cotangent[:, 0].reshape(512, 640)
    together = lambda *arrays: lax.optimization_barrier(arrays)

    vectors = jnp.pad(jnp.stack([gain_one, bias_one, gain_two, bias_two], axis=1), ((0, 0), (0, 124)))
    heads, tok_sent = together(pack_heads(core_arg, w_qkv, vectors), tok)
    heads = lax.all_gather(heads, "batch", axis=0, tiled=True)
    vec = vector_rows(heads)
    normal = normal_rows(tok_sent)
    before, after, normal_other, tok_other = passed_along(normal, 1), passed_along(normal, -1), swapped(normal), swapped(tok)
    windows = [window_info(lengths[m, 0], chip, core, 2560) for m in range(2)]
    place = jnp.stack([core] + windows[0][3] + windows[1][3]).astype(jnp.int32)
    feed_pack = pack_feed(core_arg, w_out, w_up, w_down)
    heads, vec, before, after, normal_other, tok_other, feed_pack, place, windows = together(
        heads, vec, before, after, normal_other, tok_other, feed_pack, place, windows)
    own = [passed_along(before, 1), before, normal, after, passed_along(after, -1)]
    other = [None, swapped(before), normal_other, swapped(after), None]
    feed_weights = lax.all_gather(feed_pack, "batch", axis=0, tiled=True)
    *near_parts, q, qT = project((1, 2, 3), place, own, other, vec, heads)
    own[0], own[4], near_parts = together(own[0], own[4], near_parts)
    other[0], other[4] = swapped(own[0]), swapped(own[4])
    k, v, kT, vT = project((0, 4), place, own, other, vec, heads, near_parts)
    (oT0, low0, lse0), (oT1, low1, lse1) = (
        attend(m, info, qT, k, vT, key_rows, query_rows) for m, (info, key_rows, query_rows, _) in enumerate(windows))

    theirs = swapped(jnp.stack([low0, low1]))
    middle, hidden_two, hidden_other = middle_step(core_arg, feed_weights, low0, low1, theirs, tok, tok_other, vec)
    mine, partial, feed_grads = feed_forward(hidden_two, hidden_other, cot, swapped(cot), feed_weights)
    feed_grads = lax.psum_scatter(feed_grads.reshape(5120, 640), ("z", "x"), scatter_dimension=0, tiled=True)
    block_out, grad_middle, branch, g_two = after_feed(middle, mine, swapped(partial), cot, vec)

    do, doT, g_out = branch_step(core_arg, branch, swapped(branch), feed_weights, low0, low1, theirs)
    dq, dk, dv = zip(*(
        attend_back(m, info, qT, q, k, kT, v, doT, do, oT, lse, key_rows, query_rows)
        for m, ((info, key_rows, query_rows, _), oT, lse) in enumerate(zip(windows, (oT0, oT1), (lse0, lse1)))))
    mine, theirs, tail = project_back(place, own, other, vec, heads, dq, dk, dv, g_out, g_two)
    feed_grads, mine, theirs, tail = together(feed_grads, mine, theirs, tail)

    feed = summed_share(feed_grads.reshape(4, 80, 640), "batch")
    tail, feed = together(tail, feed)
    tail = lax.all_to_all(tail, ("batch", "z", "x"), 0, 0, tiled=True)
    feed = lax.all_gather(feed, ("z", "x"), axis=0, tiled=True).reshape(16, 80, 640)
    theirs = swapped(theirs)
    sums = [mine[j].astype(f32) + theirs[j].astype(f32) for j in range(5)]
    right, left = passed_along(sums[4].astype(bf16), 1), passed_along(sums[0].astype(bf16), -1)
    tail, right, left = together(tail, right, left)
    right, left = (right.astype(f32) + sums[3]).astype(bf16), (left.astype(f32) + sums[1]).astype(bf16)
    tail, right, left = together(jnp.sum(tail.astype(f32), axis=0).astype(bf16), right, left)
    right, left = passed_along(right, 1), passed_along(left, -1)
    tail = gathered(tail, "x").reshape(160, 384)
    tail = gathered(tail, "z").reshape(16, 40, 384)
    tail, right, left = together(tail, right, left)
    d_one = (sums[2] + right.astype(f32) + left.astype(f32)).reshape(512, 640)
    n_one, r_one = moments(tok.reshape(512, 640).astype(f32))
    grad_tokens = (grad_middle + norm_back(d_one, n_one, r_one, vec[0:1])).astype(bf16)
    tail, grad_tokens, feed = together(tail, grad_tokens, feed)
    grad_qkv, grad_out, spare = final_heads(core_arg, tail, swapped(tail))
    grad_up, grad_down = final_feed(core_arg, feed, swapped(feed))
    return (
        block_out.reshape(2, 1, 256, 640), grad_tokens.reshape(2, 1, 256, 640), spare[:, 0], spare[:, 1], grad_qkv, grad_out,
        spare[:, 2], spare[:, 3], grad_up, grad_down)


def solution(mesh):
    fine = Mesh(mesh.devices.reshape(4, 4, 4, 2), ("batch", "z", "x", "core"))
    rows = P(None, "batch", ("z", "x", "core"), None)
    one, two = P("batch"), P("batch", None)
    return jax.shard_map(
        body,
        mesh=fine,
        in_specs=(rows, P(None, "batch", None), one, one, two, two, one, one, two, two, rows),
        out_specs=(rows, rows, one, one, two, two, one, one, two, two),
        check_vma=False,
    )
```

```python
import math

import jax
import jax.numpy as jnp
from jax import lax
from jax.experimental import pallas as pl
from jax.experimental.pallas import tpu as pltpu
from jax.sharding import Mesh
from jax.sharding import PartitionSpec as P

HEAD_DIM = 32
SCALE = HEAD_DIM ** -0.5
LOG2E = math.log2(math.e)
C2 = SCALE * LOG2E
BIG = 1e30
TILE = 256
EPSILON = 1e-05
PAIRS = 5
SHORT, LONG = 384, 1152
f32, bf16 = jnp.float32, jnp.bfloat16
NT = (((1,), (1,)), ((), ()))


def pair_offset(info_ref):
    p = pl.program_id(0)
    sub = jnp.where(p == PAIRS - 1, info_ref[0], lax.rem(p, 2))
    return sub * (2 * HEAD_DIM)


def split3(v):
    a = v.astype(bf16)
    r = v - a.astype(f32)
    b = r.astype(bf16)
    d = (r - b.astype(f32)).astype(bf16)
    return a, b, d


def rows_masked(xT, off):
    row = lax.broadcasted_iota(jnp.int32, xT.shape, 0) - off
    xf = xT.astype(f32)
    return [jnp.where((row >= HEAD_DIM * j) & (row < HEAD_DIM * (j + 1)), xf, 0.0).astype(bf16) for j in range(2)]


def lanes_masked(x, off):
    lane = lax.broadcasted_iota(jnp.int32, x.shape, 1) - off
    xf = x.astype(f32)
    return [jnp.where((lane >= HEAD_DIM * j) & (lane < HEAD_DIM * (j + 1)), xf, 0.0).astype(bf16) for j in range(2)]


def attend_kernel(info_ref, qT_ref, k_ref, vT_ref, kaug_ref, qaugT_ref, oT_ref, o_ref, l_ref, rhs):
    off = pair_offset(info_ref)
    oT_ref[...] = jnp.where(lax.rem(pl.program_id(0), 2) == 0, 0.0, oT_ref[...])
    for t in range(2):
        cols = slice(t * TILE, (t + 1) * TILE)
        masked = rows_masked(qT_ref[:, cols], off)
        for j in range(2):
            rhs[0:128, j * TILE:(j + 1) * TILE] = masked[j]
            rhs[128:256, j * TILE:(j + 1) * TILE] = qaugT_ref[:, cols]
        start = info_ref[1 + t]
        need = info_ref[3 + t]

        def block(first, size):
            def step(i, carry):
                row = pl.multiple_of(first + i * size, 128)
                lhs = jnp.concatenate([k_ref[pl.ds(row, size), :], kaug_ref[pl.ds(row, size), :]], axis=1)
                raw = [jnp.dot(lhs, rhs[:, j * TILE:(j + 1) * TILE], preferred_element_type=f32) for j in range(2)]
                out = []
                for j in range(2):
                    m, l, o = carry[j]
                    s = raw[j] * C2
                    m_new = jnp.maximum(m, jnp.max(s, axis=0, keepdims=True))
                    alpha = jnp.exp2(m - m_new)
                    p = jnp.exp2(s - m_new)
                    vT = vT_ref[pl.ds(pl.multiple_of(off + j * HEAD_DIM, HEAD_DIM), HEAD_DIM), pl.ds(row, size)]
                    out.append((m_new, l * alpha + jnp.sum(p, axis=0, keepdims=True),
                                o * alpha + jnp.dot(vT, p.astype(bf16), preferred_element_type=f32)))
                return tuple(out)
            return step

        def finish(state):
            for j in range(2):
                m, l, o = state[j]
                oT_ref[pl.ds(pl.multiple_of(off + j * HEAD_DIM, HEAD_DIM), HEAD_DIM), cols] = o * (1.0 / l)
                l_ref[0, j:j + 1, cols] = m + jnp.log2(l)

        init = tuple((jnp.full((1, TILE), -1e38, f32), jnp.zeros((1, TILE), f32), jnp.zeros((HEAD_DIM, TILE), f32)) for _ in range(2))

        longs = lax.div(need, LONG)
        state = lax.fori_loop(0, longs, block(start, LONG), init)
        finish(lax.fori_loop(0, lax.div(need - longs * LONG, SHORT), block(start + longs * LONG, SHORT), state))

    o_ref[...] = oT_ref[...].T.astype(bf16)


def attend(m, info, qT, k, vT, kaug, qaugT):
    win, nq = k.shape[1], qT.shape[2]
    qT, k, vT = stay(qT, k, vT)
    return pl.pallas_call(
        attend_kernel,
        out_shape=(jax.ShapeDtypeStruct((384, nq), f32), jax.ShapeDtypeStruct((nq, 384), bf16), jax.ShapeDtypeStruct((PAIRS, 8, nq), f32)),
        grid_spec=pltpu.PrefetchScalarGridSpec(
            num_scalar_prefetch=1, grid=(PAIRS,),
            in_specs=[
                pl.BlockSpec((None, 128, nq), lambda p, *_: (m, p // 2, 0)),
                pl.BlockSpec((None, win, 128), lambda p, *_: (m, 0, p // 2)),
                pl.BlockSpec((None, 128, win), lambda p, *_: (m, p // 2, 0)),
                pl.BlockSpec((win, 128), lambda p, *_: (0, 0)),
                pl.BlockSpec((128, nq), lambda p, *_: (0, 0)),
            ],
            out_specs=[
                pl.BlockSpec((128, nq), lambda p, *_: (p // 2, 0)),
                pl.BlockSpec((nq, 128), lambda p, *_: (0, p // 2)),
                pl.BlockSpec((1, 8, nq), lambda p, *_: (p, 0, 0)),
            ],
            scratch_shapes=[pltpu.VMEM((256, 2 * TILE), bf16)],
        ),
        compiler_params=pltpu.CompilerParams(vmem_limit_bytes=28 << 20),
        cost_estimate=pl.CostEstimate(flops=int(20 * 10**9 * 0.02), bytes_accessed=0, transcendentals=0),
        name="attend",
    )(info, qT, k, vT, kaug, qaugT)


def attend_back_kernel(info_ref, qT_ref, q_ref, k_ref, kT_ref, v_ref, doT_ref, do_ref, oT_ref, l_ref, kaug_ref, qaugT_ref,
                       dq_ref, dk_ref, dv_ref, dqT_ref, rhs_s, rhs_d, q_stk, do_stk, dk_acc, dv_acc):
    p_id = pl.program_id(0)
    off = pair_offset(info_ref)

    @pl.when(lax.rem(p_id, 2) == 0)
    def _():
        dqT_ref[...] = jnp.zeros_like(dqT_ref)
        dk_acc[...] = jnp.zeros_like(dk_acc)
        dv_acc[...] = jnp.zeros_like(dv_acc)

    for t in range(2):
        cols = slice(t * TILE, (t + 1) * TILE)
        masked_q = rows_masked(qT_ref[:, cols], off)
        masked_do = rows_masked(doT_ref[:, cols], off)
        lane_q = lanes_masked(q_ref[cols, :], off)
        lane_do = lanes_masked(do_ref[cols, :], off)
        for j in range(2):
            part = slice(j * TILE, (j + 1) * TILE)
            head = pl.ds(pl.multiple_of(off + j * HEAD_DIM, HEAD_DIM), HEAD_DIM)
            delta = jnp.sum(doT_ref[head, cols].astype(f32) * oT_ref[head, cols], axis=0, keepdims=True)
            total = l_ref[0, j:j + 1, cols] * (1.0 / C2)
            rowid = lax.broadcasted_iota(jnp.int32, (64, TILE), 0)
            lp, dp = split3(-total), split3(-delta)
            def pieces(parts):
                x = jnp.zeros((64, TILE), f32)
                for n in range(3):
                    x = jnp.where(rowid == n, parts[n].astype(f32), x)
                return x.astype(bf16)
            rhs_s[0:128, part] = masked_q[j]
            rhs_s[128:192, part] = qaugT_ref[0:64, cols]
            rhs_s[192:256, part] = pieces(lp)
            rhs_d[0:128, part] = masked_do[j]
            rhs_d[128:192, part] = jnp.zeros((64, TILE), bf16)
            rhs_d[192:256, part] = pieces(dp)
            q_stk[part, :] = lane_q[j]
            do_stk[part, :] = lane_do[j]
        start = info_ref[1 + t]
        need = info_ref[3 + t]

        def block(first, size):
            def step(i, carry):
                row = pl.multiple_of(first + i * size, 128)
                rows = pl.ds(row, size)
                aug = kaug_ref[rows, :]
                lhs_k = jnp.concatenate([k_ref[rows, :], aug], axis=1)
                lhs_v = jnp.concatenate([v_ref[rows, :], aug], axis=1)
                out, dv, dk = [], dv_acc[rows, :], dk_acc[rows, :]
                for j in range(2):
                    part = slice(j * TILE, (j + 1) * TILE)
                    s = jnp.dot(lhs_k, rhs_s[:, part], preferred_element_type=f32)
                    dp = jnp.dot(lhs_v, rhs_d[:, part], preferred_element_type=f32)
                    p = jnp.exp2(s * C2)
                    ds = (p * dp).astype(bf16)
                    dv = dv + jnp.dot(p.astype(bf16), do_stk[part, :], preferred_element_type=f32)
                    dk = dk + jnp.dot(ds, q_stk[part, :], preferred_element_type=f32)
                    kT = kT_ref[pl.ds(pl.multiple_of(off + j * HEAD_DIM, HEAD_DIM), HEAD_DIM), rows]
                    out.append(carry[j] + jnp.dot(kT, ds, preferred_element_type=f32))
                dv_acc[rows, :] = dv
                dk_acc[rows, :] = dk
                return tuple(out)
            return step

        def finish(dqs):
            for j in range(2):
                dqT_ref[pl.ds(pl.multiple_of(off + j * HEAD_DIM, HEAD_DIM), HEAD_DIM), cols] = dqs[j] * SCALE

        init = tuple(jnp.zeros((HEAD_DIM, TILE), f32) for _ in range(2))

        longs = lax.div(need, LONG)
        state = lax.fori_loop(0, longs, block(start, LONG), init)
        finish(lax.fori_loop(0, lax.div(need - longs * LONG, SHORT), block(start + longs * LONG, SHORT), state))
    @pl.when((lax.rem(p_id, 2) == 1) | (p_id == PAIRS - 1))
    def _():
        dq_ref[...] = dqT_ref[...].T.astype(bf16)
        dk_ref[...] = (dk_acc[...] * SCALE).astype(bf16)
        dv_ref[...] = dv_acc[...].astype(bf16)


def attend_back(m, info, qT, q, k, kT, v, doT, do, oT, lse, kaug, qaugT):
    win, nq = k.shape[1], qT.shape[2]
    qT, q, k, kT, v, doT, do = stay(qT, q, k, kT, v, doT, do)
    wide = pl.BlockSpec((128, nq), lambda p, *_: (p // 2, 0))
    tall = pl.BlockSpec((nq, 128), lambda p, *_: (0, p // 2))
    keys = pl.BlockSpec((win, 128), lambda p, *_: (0, p // 2))
    wide_m = pl.BlockSpec((None, 128, nq), lambda p, *_: (m, p // 2, 0))
    tall_m = pl.BlockSpec((None, nq, 128), lambda p, *_: (m, 0, p // 2))
    keys_m = pl.BlockSpec((None, win, 128), lambda p, *_: (m, 0, p // 2))
    return pl.pallas_call(
        attend_back_kernel,
        out_shape=tuple(pltpu.MemorySpace.VMEM(d, bf16) for d in ((nq, 384), (win, 384), (win, 384))),
        grid_spec=pltpu.PrefetchScalarGridSpec(
            num_scalar_prefetch=1, grid=(PAIRS,),
            in_specs=[wide_m, tall_m, keys_m, pl.BlockSpec((None, 128, win), lambda p, *_: (m, p // 2, 0)), keys_m,
                      pl.BlockSpec((128, nq), lambda p, *_: (p // 2, m)), pl.BlockSpec((nq, 128), lambda p, *_: (m, p // 2)), wide,
                      pl.BlockSpec((1, 8, nq), lambda p, *_: (p, 0, 0)),
                      pl.BlockSpec((win, 128), lambda p, *_: (0, 0)), pl.BlockSpec((128, nq), lambda p, *_: (0, 0))],
            out_specs=[tall, keys, keys],
            scratch_shapes=[pltpu.VMEM((128, nq), f32), pltpu.VMEM((256, 2 * TILE), bf16), pltpu.VMEM((256, 2 * TILE), bf16),
                            pltpu.VMEM((2 * TILE, 128), bf16), pltpu.VMEM((2 * TILE, 128), bf16),
                            pltpu.VMEM((win, 128), f32), pltpu.VMEM((win, 128), f32)],
        ),
        compiler_params=pltpu.CompilerParams(vmem_limit_bytes=32 << 20),
        cost_estimate=pl.CostEstimate(flops=int(40 * 10**9 * 0.02), bytes_accessed=0, transcendentals=0),
        name="attend_back",
    )(info, qT, q, k, kT, v, doT, do, oT, lse, kaug, qaugT)


def moments(x):
    centred = x - jnp.mean(x, axis=-1, keepdims=True)
    r = lax.rsqrt(jnp.mean(centred * centred, axis=-1, keepdims=True) + EPSILON)
    return centred * r, r


def norm_back(grad, n, r, gain):
    e = grad * gain
    return r * (e - jnp.mean(e, axis=-1, keepdims=True) - n * jnp.mean(e * n, axis=-1, keepdims=True))


def call(kernel, out_shape, name, flops=10**9, limit=48, **spec):
    return pl.pallas_call(
        kernel, out_shape=out_shape, name=name,
        compiler_params=pltpu.CompilerParams(vmem_limit_bytes=limit << 20),
        cost_estimate=pl.CostEstimate(flops=int(flops * 0.02), bytes_accessed=0, transcendentals=0), **spec)


def shape(*dims, dtype=bf16):
    return jax.ShapeDtypeStruct(dims, dtype)


def far(*dims, dtype=bf16):
    return pltpu.MemorySpace.HBM(dims, dtype)


def stay(*arrays):
    return [pltpu.with_memory_space_constraint(a, pltpu.MemorySpace.HBM) for a in arrays]


def scalar_first(grid, in_specs, out_specs, scratch=()):
    return dict(grid_spec=pltpu.PrefetchScalarGridSpec(
        num_scalar_prefetch=1, grid=grid, in_specs=in_specs, out_specs=out_specs, scratch_shapes=list(scratch)))


def full(*dims):
    return pl.BlockSpec(dims, lambda *_: (0,) * len(dims))


def pack_heads_kernel(core_ref, qkv_ref, vec_ref, heads_ref):
    for part in range(3):
        near = pl.ds(pl.multiple_of(640 * part + 256 * core_ref[0], 128), 256)
        heads_ref[:, 384 * part:384 * part + 256] = qkv_ref[:, near]
        heads_ref[:, 384 * part + 256:384 * (part + 1)] = qkv_ref[:, 640 * part + 512:640 * (part + 1)]
    heads_ref[:, 1152:1280] = vec_ref[...]


def pack_heads(core, w_qkv, vectors):
    return call(pack_heads_kernel, shape(160, 1280), "pack_heads", 10**6, 8, **scalar_first(
        (1,), [full(160, 1920), full(160, 128)], full(160, 1280)))(core, w_qkv, vectors)


def turn_kernel(vec_ref, rows_ref):
    rows_ref[...] = vec_ref[...].astype(f32).T[:16]


def vector_rows(heads):
    return call(turn_kernel, shape(16, 640, dtype=f32), "vector_rows", 10**12, 8, grid=(1,),
                in_specs=[pl.BlockSpec((640, 128), lambda i: (0, 9))], out_specs=full(16, 640))(*stay(heads))


def pack_feed_kernel(core_ref, out_ref, up_ref, down_ref, feed_ref):
    core = core_ref[0]
    feed_ref[:, 5120:5760] = out_ref[...]
    for f in range(4):
        feed_ref[:, 640 * f:640 * (f + 1)] = up_ref[:, pl.ds(pl.multiple_of(1280 * f + 640 * core, 128), 640)]
        feed_ref[:, 2560 + 640 * f:2560 + 640 * (f + 1)] = down_ref[pl.ds(pl.multiple_of(640 * core + 160 * f, 32), 160), :]


def pack_feed(core, w_out, w_up, w_down):
    return call(pack_feed_kernel, far(160, 5760), "pack_feed", 10**6, 16, **scalar_first(
        (1,), [full(160, 640), full(160, 5120), full(1280, 640)], full(160, 5760)))(core, *stay(w_out, w_up, w_down))


def rows_in_order(core, mine_ref, theirs_ref, x_ref):
    for c, (first, second) in enumerate(((mine_ref, theirs_ref), (theirs_ref, mine_ref))):
        @pl.when(core == c)
        def _():
            x_ref[0:256, :], x_ref[256:512, :] = first[...], second[...]


def normal_kernel(tok_ref, n_ref):
    for m in range(2):
        n_ref[m] = moments(tok_ref[m].astype(f32))[0].astype(bf16)


def normal_rows(tok):
    return call(normal_kernel, shape(2, 256, 640), "normal_rows", 10**6, 8, grid=(1,), in_specs=[full(2, 256, 640)], out_specs=full(2, 256, 640))(tok)


def project_kernel(chips, place_ref, *refs):
    n = len(chips)
    own_refs, other_refs = refs[:n], refs[n:2 * n]
    vec_ref, w_ref = refs[2 * n:2 * n + 2]
    k_ref, v_ref, kT_ref, vT_ref = refs[-6 - 2 * (n == 3):][:4]
    x_ref, hid_ref = refs[-2:]
    m, step = pl.program_id(0), pl.program_id(1)
    block = sum(jnp.where(step == i, chip, 0) for i, chip in enumerate(chips))
    needed = (block >= place_ref[1 + 2 * m]) & (block < place_ref[2 + 2 * m])

    @pl.when(jnp.logical_not(needed))
    def _():
        for ref in (k_ref, v_ref, kT_ref, vT_ref):
            ref[...] = jnp.zeros_like(ref)

    @pl.when(needed)
    def _():
        for j in range(n):
            @pl.when(step == j)
            def _():
                rows_in_order(place_ref[0], own_refs[j].at[m], other_refs[j].at[m], x_ref)

        hidden = (x_ref[...].astype(f32) * vec_ref[0:1, :] + vec_ref[1:2, :]).astype(bf16)
        hid_ref[...] = hidden
        kv = jnp.dot(hidden, w_ref[:, 384:], preferred_element_type=f32)
        low = kv.astype(bf16)
        k_ref[0] = low[:, :384]
        v_ref[0] = low[:, 384:]
        turned = kv.T.astype(bf16)
        kT_ref[0] = turned[:384]
        vT_ref[0] = turned[384:]

    if n == 3:
        q_ref, qT_ref = refs[-4:-2]

        @pl.when(step == 1)
        def _():
            q = jnp.dot(hid_ref[...], w_ref[:, :384], preferred_element_type=f32)
            q_ref[0] = q.astype(bf16)
            qT_ref[0] = q.T.astype(bf16)


def project(chips, place, own, other, vec, w, earlier=()):
    n = len(chips)
    chip = (lambda b: b + 1) if n == 3 else (lambda b: 4 * b)
    tall = pl.BlockSpec((1, 512, 384), lambda m, b, *_: (m, chip(b), 0))
    wide = pl.BlockSpec((1, 384, 512), lambda m, b, *_: (m, 0, chip(b)))
    shapes = [far(2, 2560, 384), far(2, 2560, 384), far(2, 384, 2560), far(2, 384, 2560)]
    specs = [tall, tall, wide, wide]
    if n == 3:
        shapes += [far(2, 512, 384), far(2, 384, 512)]
        specs += [pl.BlockSpec((1, 512, 384), lambda m, *_: (m, 0, 0)), pl.BlockSpec((1, 384, 512), lambda m, *_: (m, 0, 0))]
    own, other = [own[c] for c in chips], [other[c] for c in chips]
    return call(
        lambda *refs: project_kernel(chips, *refs), shapes, "project", 5 * 10**9, 28,
        input_output_aliases={2 * n + 3 + i: i for i in range(len(earlier))}, **scalar_first(
            (2, n), [full(2, 256, 640)] * (2 * n) + [full(16, 640), full(640, 1152)] + [pl.BlockSpec(memory_space=pl.ANY)] * len(earlier),
            specs, [pltpu.VMEM((512, 640), bf16), pltpu.VMEM((512, 640), bf16)]))(place, *own, *other, vec, *stay(w), *earlier)


def heads_joined(core, mine, theirs):
    first, second = (jnp.where(core == 0, a, b) for a, b in ((mine, theirs), (theirs, mine)))
    return jnp.concatenate([first[:, :256], second[:, :256], first[:, 256:] + second[:, 256:]], axis=1)


def middle_kernel(core_ref, w_ref, low0_ref, low1_ref, theirs_ref, tok_ref, tok2_ref, vec_ref, mid_ref, hid_ref, hid2_ref):
    core = core_ref[0]
    for m, low_ref in enumerate((low0_ref, low1_ref)):
        attended = heads_joined(core, low_ref[...].astype(f32), theirs_ref[m].astype(f32)).astype(bf16)
        branch = jnp.dot(attended, w_ref[...], preferred_element_type=f32)
        mine = jnp.where(core == 0, branch[:256], branch[256:]) + tok_ref[m].astype(f32)
        theirs = jnp.where(core == 0, branch[256:], branch[:256]) + tok2_ref[m].astype(f32)
        part = slice(256 * m, 256 * (m + 1))
        mid_ref[part, :] = mine
        hid_ref[part, :] = (moments(mine)[0] * vec_ref[2:3, :] + vec_ref[3:4, :]).astype(bf16)
        hid2_ref[part, :] = (moments(theirs)[0] * vec_ref[2:3, :] + vec_ref[3:4, :]).astype(bf16)


W_OUT = pl.BlockSpec((640, 640), lambda *_: (0, 8))


def middle_step(core, weights, *args):
    return call(middle_kernel, (far(512, 640, dtype=f32), far(512, 640), far(512, 640)), "middle", 10**9, 20, **scalar_first(
        (1,), [W_OUT] + [full(*a.shape) for a in args], [full(512, 640)] * 3))(core, *stay(weights), *args)


def feed_kernel(h_ref, h2_ref, cot_ref, cot2_ref, up_ref, down_ref, mine_ref, theirs_ref, g_ref, h, cot, hT, cT, out, dh):
    chunk = pl.program_id(0)

    @pl.when(chunk == 0)
    def _():
        h[0:512, :], h[512:1024, :] = h_ref[...], h2_ref[...]
        cot[0:512, :], cot[512:1024, :] = cot_ref[...], cot2_ref[...]
        hT[...] = h[...].astype(f32).T.astype(bf16)
        cT[...] = cot[...].astype(f32).T.astype(bf16)
        out[...] = jnp.zeros_like(out)
        dh[...] = jnp.zeros_like(dh)

    up_w = up_ref[...]
    down_w = jnp.concatenate([down_ref[160 * y:160 * (y + 1), 640 * i:640 * (i + 1)] for y in range(2) for i in range(4)], axis=0)
    acts, d_ups = [], []
    for t in range(4):
        rows = slice(256 * t, 256 * (t + 1))
        u = jnp.dot(h[rows, :], up_w, preferred_element_type=f32)
        d_act = lax.dot_general(cot[rows, :], down_w, NT, preferred_element_type=f32)
        cdf = 0.5 * (1.0 + lax.erf(u * (2.0 ** -0.5)))
        pdf = jnp.exp(u * u * -0.5) * ((2.0 * math.pi) ** -0.5)
        act = (u * cdf).astype(bf16)
        d_up = (d_act * (cdf + u * pdf)).astype(bf16)
        out[rows, :] += jnp.dot(act, down_w, preferred_element_type=f32)
        dh[rows, :] += lax.dot_general(d_up, up_w, NT, preferred_element_type=f32)
        acts.append(act)
        d_ups.append(d_up)
    g_up = jnp.dot(hT[...], jnp.concatenate(d_ups, axis=0), preferred_element_type=f32).astype(bf16)
    g_down = jnp.dot(cT[...], jnp.concatenate(acts, axis=0), preferred_element_type=f32).T.astype(bf16)
    for f in range(2):
        for y in range(4):
            for i in range(2):
                g_ref[4 * chunk + 2 * f + i, y] = g_up[160 * y + 80 * i:160 * y + 80 * (i + 1), 640 * f:640 * (f + 1)]
        for i in range(8):
            g_ref[8 + i, 2 * chunk + f] = g_down[640 * f + 80 * i:640 * f + 80 * (i + 1)]

    @pl.when(chunk == 1)
    def _():
        mine_ref[0], mine_ref[1] = out[0:512, :].astype(bf16), dh[0:512, :].astype(bf16)
        theirs_ref[0], theirs_ref[1] = out[512:1024, :].astype(bf16), dh[512:1024, :].astype(bf16)


def feed_forward(h, h2, cot, cot2, weights):
    return call(
        feed_kernel,
        (far(2, 512, 640), far(2, 512, 640), far(16, 4, 80, 640)),
        "feed_forward", 30 * 10**9, 52, grid=(2,),
        in_specs=[full(512, 640)] * 4 + [pl.BlockSpec((640, 1280), lambda f: (0, f)), pl.BlockSpec((320, 2560), lambda f: (f, 1))],
        out_specs=[full(2, 512, 640), full(2, 512, 640), full(16, 4, 80, 640)],
        scratch_shapes=[pltpu.VMEM((1024, 640), bf16), pltpu.VMEM((1024, 640), bf16), pltpu.VMEM((640, 1024), bf16), pltpu.VMEM((640, 1024), bf16),
                        pltpu.VMEM((1024, 640), f32), pltpu.VMEM((1024, 640), f32)],
    )(*stay(h, h2, cot), cot2, *stay(weights, weights))


def after_kernel(mid_ref, mine_ref, theirs_ref, cot_ref, vec_ref, block_ref, grad_ref, branch_ref, g_ref):
    @pl.when(pl.program_id(0) == 0)
    def _():
        g_ref[...] = jnp.zeros_like(g_ref)

    middle = mid_ref[...]
    block_ref[...] = (middle + mine_ref[0].astype(f32) + theirs_ref[0].astype(f32)).astype(bf16)
    d_hidden = mine_ref[1].astype(f32) + theirs_ref[1].astype(f32)
    n, r = moments(middle)
    g_ref[0:1, :] += jnp.sum(d_hidden * n, axis=0, keepdims=True)
    g_ref[1:2, :] += jnp.sum(d_hidden, axis=0, keepdims=True)
    grad = cot_ref[...].astype(f32) + norm_back(d_hidden, n, r, vec_ref[2:3, :])
    grad_ref[...] = grad
    branch_ref[...] = grad.astype(bf16)


def after_feed(*args):
    rows, pair = pl.BlockSpec((128, 640), lambda i: (i, 0)), pl.BlockSpec((2, 128, 640), lambda i: (0, i, 0))
    return call(
        after_kernel, (far(512, 640), far(512, 640, dtype=f32), shape(512, 640), shape(8, 640, dtype=f32)), "after_feed", 10**9, 16,
        grid=(4,), in_specs=[rows, pair, pair, rows, full(16, 640)], out_specs=[rows, rows, rows, full(8, 640)])(*stay(args[0], args[1]), args[2], *stay(args[3]), args[4])


def branch_kernel(core_ref, own_ref, their_ref, w_ref, low0_ref, low1_ref, theirs_ref, do_ref, doT_ref, g_ref):
    core = core_ref[0]
    w = jnp.concatenate([w_ref[pl.ds(pl.multiple_of(256 * core, 256), 256), :], w_ref[512:640, :]], axis=0)
    g = jnp.zeros((640, 384), f32)
    for m in range(2):
        part = slice(256 * m, 256 * (m + 1))
        mine, theirs = own_ref[part, :].astype(f32), their_ref[part, :].astype(f32)
        branch = jnp.concatenate([jnp.where(core == 0, mine, theirs), jnp.where(core == 0, theirs, mine)], axis=0)
        kept = jnp.where(core == 0, branch[:, :384], branch[:, 256:]).astype(bf16)
        branch = branch.astype(bf16)
        rows = slice(512 * m, 512 * (m + 1))
        do = lax.dot_general(branch, w, NT, preferred_element_type=f32)
        do_ref[rows, :] = do.astype(bf16)
        doT_ref[:, rows] = do.T.astype(bf16)
        attended = heads_joined(core, (low0_ref, low1_ref)[m][...].astype(f32), theirs_ref[m].astype(f32))
        g = g + jnp.dot(attended.T.astype(bf16), kept, preferred_element_type=f32)
    g_ref[...] = g.astype(bf16)


def branch_step(core, own, their, weights, *args):
    return call(
        branch_kernel, (far(1024, 384), far(384, 1024), shape(640, 384)), "branch", 10**9, 24, **scalar_first(
            (1,), [full(512, 640)] * 2 + [W_OUT] + [full(*a.shape) for a in args], [full(1024, 384), full(384, 1024), full(640, 384)]))(
                core, own, their, *stay(weights), *args)


def near_by(*arrays):
    return [pltpu.with_memory_space_constraint(a, pltpu.MemorySpace.VMEM) for a in arrays]


def project_back_kernel(place_ref, *refs):
    own_refs, other_refs = refs[:5], refs[5:10]
    (vec_ref, w_ref, dq0_ref, dq1_ref, dk0_ref, dk1_ref, dv0_ref, dv1_ref, g_out_ref, g_two_ref,
     mine_ref, theirs_ref, tail_ref, n_ref, d_kv, d_q, d_hid, g_ref, g_vec, slots, arrived) = refs[10:]
    step, core = pl.program_id(0), place_ref[0]
    block, second = lax.rem(step, 5), lax.div(step, 5)
    inside = lambda j, m: (j >= place_ref[1 + 2 * m]) & (j < place_ref[2 + 2 * m])
    needed = inside(block, second)

    def copies(j, m, slot):
        return [pltpu.make_async_copy(refs_of[j].at[m], slots.at[slot, i], arrived.at[slot, i]) for i, refs_of in enumerate((own_refs, other_refs))]

    @pl.when(step == 0)
    def _():
        for m in range(2):
            for j in range(5):
                @pl.when(inside(j, m))
                def _():
                    for copy in copies(j, m, 5 * m + j):
                        copy.start()
        g_ref[...] = jnp.zeros_like(g_ref)
        g_vec[...] = jnp.zeros_like(g_vec)
        g_vec[2:4, :] = g_two_ref[0:2, :]

    @pl.when(jnp.logical_not(needed))
    def _():
        mine_ref[...] = jnp.zeros_like(mine_ref)
        theirs_ref[...] = jnp.zeros_like(theirs_ref)

    @pl.when(needed)
    def _():
        for copy in copies(0, 0, step):
            copy.wait()
        rows_in_order(core, slots.at[step, 0], slots.at[step, 1], n_ref)

    for m, (dq, dk, dv) in enumerate(((dq0_ref, dk0_ref, dv0_ref), (dq1_ref, dk1_ref, dv1_ref))):
        @pl.when(needed & (second == m))
        def _():
            rows = pl.ds(pl.multiple_of(block * 512, 512), 512)
            d_kv[:, :384], d_kv[:, 384:] = dk[rows, :], dv[rows, :]
            d_q[...] = dq[...]

    @pl.when(needed)
    def _():
        n = n_ref[...].astype(f32)
        hiddenT = (n * vec_ref[0:1, :] + vec_ref[1:2, :]).T.astype(bf16)
        d_hid[...] = lax.dot_general(d_kv[...], w_ref[:, 384:1152], NT, preferred_element_type=f32)
        g_ref[:, 384:] += jnp.dot(hiddenT, d_kv[...], preferred_element_type=f32)

        @pl.when(block == 2)
        def _():
            g_ref[:, :384] += jnp.dot(hiddenT, d_q[...], preferred_element_type=f32)
            d_hid[...] += lax.dot_general(d_q[...], w_ref[:, :384], NT, preferred_element_type=f32)

        dh = d_hid[...]
        low = dh.astype(bf16)
        for c, (first, other) in enumerate(((mine_ref, theirs_ref), (theirs_ref, mine_ref))):
            @pl.when(core == c)
            def _():
                first[0, 0], other[0, 0] = low[:256], low[256:]
        g_vec[0:1, :] += jnp.sum(dh * n, axis=0, keepdims=True)
        g_vec[1:2, :] += jnp.sum(dh, axis=0, keepdims=True)

    @pl.when(step == 9)
    def _():
        turned = g_vec[...].T
        lane = lax.broadcasted_iota(jnp.int32, (640, 128), 1) - 64 * (1 - core)
        spare = g_ref[:, 256:384]
        for i in range(4):
            spare = jnp.where(lane == i, turned[:, i:i + 1], spare)
        g_ref[:, 256:384] = spare
        for y in range(4):
            for z in range(4):
                rows = slice(160 * y + 40 * z, 160 * y + 40 * (z + 1))
                for x in range(3):
                    tail_ref[16 * y + 4 * z + x] = g_ref[rows, 384 * x:384 * (x + 1)].astype(bf16)
                tail_ref[16 * y + 4 * z + 3] = g_out_ref[rows, :].astype(bf16)


def project_back(place, own, other, vec, w, dq, dk, dv, g_out, g_two):
    here = pl.BlockSpec(memory_space=pltpu.VMEM)
    part = pl.BlockSpec((1, 1, 256, 640), lambda b, *_: (lax.rem(b, 5), b // 5, 0, 0))
    return call(
        project_back_kernel, (far(5, 2, 256, 640), far(5, 2, 256, 640), far(64, 40, 384)), "project_back", 10**10, 30, **scalar_first(
            (10,), [pl.BlockSpec(memory_space=pl.ANY)] * 10 + [here] * 10, [part, part, full(64, 40, 384)],
            [pltpu.VMEM((512, 640), bf16), pltpu.VMEM((512, 768), bf16), pltpu.VMEM((512, 384), bf16),
             pltpu.VMEM((512, 640), f32), pltpu.VMEM((640, 1152), f32), pltpu.VMEM((8, 640), f32),
             pltpu.VMEM((10, 2, 256, 640), bf16), pltpu.SemaphoreType.DMA((10, 2))]))(
                 place, *stay(*own, *other), *near_by(vec, w, *dq, *dk, *dv, g_out, g_two))


def in_core_order(core_ref, mine, theirs):
    core, mine, theirs = core_ref[0], mine.astype(f32), theirs.astype(f32)
    return jnp.where(core == 0, mine, theirs), jnp.where(core == 0, theirs, mine)


def final_feed_kernel(core_ref, mine_ref, theirs_ref, up_ref, down_ref):
    for i in range(16):
        for c, piece in enumerate(in_core_order(core_ref, mine_ref[i], theirs_ref[i])):
            if i < 8:
                base = 1280 * (i // 2) + 640 * c
                up_ref[80 * (i % 2):80 * (i % 2 + 1), base:base + 640] = piece
            else:
                base = 640 * c + 80 * (i - 8)
                down_ref[base:base + 80, :] = piece


def final_feed(core, mine, theirs):
    return call(final_feed_kernel, (shape(160, 5120, dtype=f32), shape(1280, 640, dtype=f32)), "final_feed", 10**6, 32, **scalar_first(
        (1,), [full(16, 80, 640)] * 2, [full(160, 5120), full(1280, 640)]))(core, mine, theirs)


def final_heads_kernel(core_ref, mine_ref, theirs_ref, qkv_ref, out_ref, vec_ref):
    lane = lax.broadcasted_iota(jnp.int32, (40, 128), 1)
    for z in range(4):
        rows = slice(40 * z, 40 * (z + 1))
        for x in range(4):
            a, b = in_core_order(core_ref, mine_ref[4 * z + x], theirs_ref[4 * z + x])
            if x < 3:
                last = jnp.where(lane < 64, a[:, 256:], b[:, 256:])
                qkv_ref[rows, 640 * x:640 * (x + 1)] = jnp.concatenate([a[:, :256], b[:, :256], last], axis=1)
            else:
                out_ref[rows, :] = jnp.concatenate([a, b[:, 128:]], axis=1)
            if x == 0:
                vec_ref[rows, :] = pltpu.roll(a[:, 256:], 64, 1) + b[:, 256:]


def final_heads(core, mine, theirs):
    return call(
        final_heads_kernel, (shape(160, 1920, dtype=f32), shape(160, 640, dtype=f32), shape(160, 128, dtype=f32)), "final_heads", 10**6, 16,
        **scalar_first((1,), [full(16, 40, 384)] * 2, [full(160, 1920), full(160, 640), full(160, 128)]))(core, mine, theirs)


def shifted(array, axis, by):
    devices = lax.axis_size(axis)
    return lax.ppermute(array, axis, [(i, (i + by) % devices) for i in range(devices)])


def passed_along(array, by):
    devices = lax.axis_size(("z", "x"))
    return lax.ppermute(array, ("z", "x"), [(i, i + by) for i in range(devices) if 0 <= i + by < devices])


def swapped(array):
    return lax.ppermute(array, "core", [(0, 1), (1, 0)])


def pick(array, index):
    return lax.dynamic_index_in_dim(array, index, 0, keepdims=False)


def summed_share(array, axis):
    me, devices = lax.axis_index(axis), lax.axis_size(axis)
    total = pick(array, me).astype(f32)
    for by in (1, devices - 1, 2):
        total = total + shifted(pick(array, (me + by) % devices), axis, by).astype(f32)
    return total.astype(bf16)


def gathered(array, axis):
    me, devices = lax.axis_index(axis), lax.axis_size(axis)
    out = jnp.zeros((devices,) + array.shape, array.dtype)
    out = lax.dynamic_update_index_in_dim(out, array, me, 0)
    for by in (1, devices - 1, 2):
        out = lax.dynamic_update_index_in_dim(out, shifted(array, axis, by), (me + devices - by) % devices, 0)
    return out


def window_info(length_row, chip, core, win):
    ends = jnp.cumsum(length_row)
    starts = ends - length_row
    base = chip * 512 - 1024
    places = base + jnp.arange(win, dtype=jnp.int32)
    inside = (places[:, None] >= starts[None, :]) & (places[:, None] < ends[None, :])
    ones = jnp.broadcast_to(jnp.arange(64) < 3, (win, 64)).astype(bf16)
    key_rows = jnp.concatenate([jnp.where(inside, 0.0, -BIG).astype(bf16), ones], axis=1)
    own = chip * 512 + jnp.arange(512, dtype=jnp.int32)
    inside_q = (own[None, :] >= starts[:, None]) & (own[None, :] < ends[:, None])
    query_rows = jnp.concatenate([inside_q.astype(bf16), jnp.zeros((64, 512), bf16)], axis=0)
    info = [core]
    sizes = []
    for t in range(2):
        first = chip * 512 + t * TILE
        low = jnp.max(jnp.where(starts <= first, starts, 0)) - base
        high = jnp.min(jnp.where(ends > first + TILE - 1, ends, 1 << 30)) - base
        start = low // 128 * 128
        need = high - start
        size = (need + SHORT - 1) // SHORT * SHORT
        info.append(jnp.minimum(start, win - size))
        sizes.append(size)
    low = jnp.minimum(info[1], info[2]) // 512
    high = (jnp.maximum(info[1] + sizes[0], info[2] + sizes[1]) + 511) // 512
    return jnp.stack(info + sizes).astype(jnp.int32), key_rows, query_rows, [low, high]


def body(tokens, lengths, gain_one, bias_one, w_qkv, w_out, gain_two, bias_two, w_up, w_down, cotangent):
    core, chip = lax.axis_index("core"), lax.axis_index(("z", "x"))
    core_arg = core[None].astype(jnp.int32)
    tok, cot = tokens[:, 0], cotangent[:, 0].reshape(512, 640)
    together = lambda *arrays: lax.optimization_barrier(arrays)

    vectors = jnp.pad(jnp.stack([gain_one, bias_one, gain_two, bias_two], axis=1), ((0, 0), (0, 124)))
    heads, tok_sent = together(pack_heads(core_arg, w_qkv, vectors), tok)
    heads = lax.all_gather(heads, "batch", axis=0, tiled=True)
    vec = vector_rows(heads)
    normal = normal_rows(tok_sent)
    before, after, normal_other, tok_other = passed_along(normal, 1), passed_along(normal, -1), swapped(normal), swapped(tok)
    feed_pack = pack_feed(core_arg, w_out, w_up, w_down)
    heads, feed_pack, length_row = together(heads, feed_pack, lengths[1, 0])
    feed_weights = lax.all_gather(feed_pack, "batch", axis=0, tiled=True)
    windows = [window_info(row, chip, core, 2560) for row in (lengths[0, 0], length_row)]
    place = jnp.stack([core] + windows[0][3] + windows[1][3]).astype(jnp.int32)
    heads, vec, before, after, normal_other, tok_other, place, windows = together(
        heads, vec, before, after, normal_other, tok_other, place, windows)
    own = [passed_along(before, 1), before, normal, after, passed_along(after, -1)]
    other = [None, swapped(before), normal_other, swapped(after), None]
    *near_parts, q, qT = project((1, 2, 3), place, own, other, vec, heads)
    own[0], own[4], near_parts = together(own[0], own[4], near_parts)
    other[0], other[4] = swapped(own[0]), swapped(own[4])
    k, v, kT, vT = project((0, 4), place, own, other, vec, heads, near_parts)
    (oT0, low0, lse0), (oT1, low1, lse1) = (
        attend(m, info, qT, k, vT, key_rows, query_rows) for m, (info, key_rows, query_rows, _) in enumerate(windows))

    theirs = swapped(jnp.stack([low0, low1]))
    middle, hidden_two, hidden_other = middle_step(core_arg, feed_weights, low0, low1, theirs, tok, tok_other, vec)
    mine, partial, feed_grads = feed_forward(hidden_two, hidden_other, cot, swapped(cot), feed_weights)
    feed_grads = lax.psum_scatter(feed_grads.reshape(5120, 640), ("z", "x"), scatter_dimension=0, tiled=True)
    block_out, grad_middle, branch, g_two = after_feed(middle, mine, swapped(partial), cot, vec)

    do, doT, g_out = branch_step(core_arg, branch, swapped(branch), feed_weights, low0, low1, theirs)
    dq, dk, dv = zip(*(
        attend_back(m, info, qT, q, k, kT, v, doT, do, oT, lse, key_rows, query_rows)
        for m, ((info, key_rows, query_rows, _), oT, lse) in enumerate(zip(windows, (oT0, oT1), (lse0, lse1)))))
    mine, theirs, tail = project_back(place, own, other, vec, heads, dq, dk, dv, g_out, g_two)
    feed_grads, mine, theirs, tail = together(feed_grads, mine, theirs, tail)

    feed = summed_share(feed_grads.reshape(4, 80, 640), "batch")
    tail, feed = together(tail, feed)
    tail = lax.all_to_all(tail, ("batch", "z", "x"), 0, 0, tiled=True)
    feed = lax.all_gather(feed, ("z", "x"), axis=0, tiled=True).reshape(16, 80, 640)
    theirs = swapped(theirs)
    sums = [mine[j].astype(f32) + theirs[j].astype(f32) for j in range(5)]
    right, left = passed_along(sums[4].astype(bf16), 1), passed_along(sums[0].astype(bf16), -1)
    tail, right, left = together(tail, right, left)
    right, left = (right.astype(f32) + sums[3]).astype(bf16), (left.astype(f32) + sums[1]).astype(bf16)
    tail, right, left = together(jnp.sum(tail.astype(f32), axis=0).astype(bf16), right, left)
    right, left = passed_along(right, 1), passed_along(left, -1)
    tail = gathered(tail, "x").reshape(160, 384)
    tail, right, left = together(tail, right, left)
    tail = gathered(tail, "z").reshape(16, 40, 384)
    tail, right, left = together(tail, right, left)
    d_one = (sums[2] + right.astype(f32) + left.astype(f32)).reshape(512, 640)
    n_one, r_one = moments(tok.reshape(512, 640).astype(f32))
    grad_tokens = (grad_middle + norm_back(d_one, n_one, r_one, vec[0:1])).astype(bf16)
    tail, grad_tokens, feed = together(tail, grad_tokens, feed)
    grad_qkv, grad_out, spare = final_heads(core_arg, tail, swapped(tail))
    grad_up, grad_down = final_feed(core_arg, feed, swapped(feed))
    return (
        block_out.reshape(2, 1, 256, 640), grad_tokens.reshape(2, 1, 256, 640), spare[:, 0], spare[:, 1], grad_qkv, grad_out,
        spare[:, 2], spare[:, 3], grad_up, grad_down)


def solution(mesh):
    fine = Mesh(mesh.devices.reshape(4, 4, 4, 2), ("batch", "z", "x", "core"))
    rows = P(None, "batch", ("z", "x", "core"), None)
    one, two = P("batch"), P("batch", None)
    return jax.shard_map(
        body,
        mesh=fine,
        in_specs=(rows, P(None, "batch", None), one, one, two, two, one, one, two, two, rows),
        out_specs=(rows, rows, one, one, two, two, one, one, two, two),
        check_vma=False,
    )
```

```python
import math

import jax
import jax.numpy as jnp
from jax import lax
from jax.experimental import pallas as pl
from jax.experimental.pallas import tpu as pltpu
from jax.sharding import Mesh
from jax.sharding import PartitionSpec as P

HEAD_DIM = 32
SCALE = HEAD_DIM ** -0.5
LOG2E = math.log2(math.e)
C2 = SCALE * LOG2E
BIG = 1e30
TILE = 256
EPSILON = 1e-05
PAIRS = 5
SHORT, LONG = 384, 1152
f32, bf16 = jnp.float32, jnp.bfloat16
NT = (((1,), (1,)), ((), ()))


def pair_offset(info_ref):
    p = pl.program_id(0)
    sub = jnp.where(p == PAIRS - 1, info_ref[0], lax.rem(p, 2))
    return sub * (2 * HEAD_DIM)


def split3(v):
    a = v.astype(bf16)
    r = v - a.astype(f32)
    b = r.astype(bf16)
    d = (r - b.astype(f32)).astype(bf16)
    return a, b, d


def rows_masked(xT, off):
    row = lax.broadcasted_iota(jnp.int32, xT.shape, 0) - off
    xf = xT.astype(f32)
    return [jnp.where((row >= HEAD_DIM * j) & (row < HEAD_DIM * (j + 1)), xf, 0.0).astype(bf16) for j in range(2)]


def lanes_masked(x, off):
    lane = lax.broadcasted_iota(jnp.int32, x.shape, 1) - off
    xf = x.astype(f32)
    return [jnp.where((lane >= HEAD_DIM * j) & (lane < HEAD_DIM * (j + 1)), xf, 0.0).astype(bf16) for j in range(2)]


def attend_kernel(info_ref, qT_ref, k_ref, vT_ref, kaug_ref, qaugT_ref, oT_ref, o_ref, l_ref, rhs):
    off = pair_offset(info_ref)
    oT_ref[...] = jnp.where(lax.rem(pl.program_id(0), 2) == 0, 0.0, oT_ref[...])
    for t in range(2):
        cols = slice(t * TILE, (t + 1) * TILE)
        masked = rows_masked(qT_ref[:, cols], off)
        for j in range(2):
            rhs[0:128, j * TILE:(j + 1) * TILE] = masked[j]
            rhs[128:256, j * TILE:(j + 1) * TILE] = qaugT_ref[:, cols]
        start = info_ref[1 + t]
        need = info_ref[3 + t]

        def block(first, size):
            def step(i, carry):
                row = pl.multiple_of(first + i * size, 128)
                lhs = jnp.concatenate([k_ref[pl.ds(row, size), :], kaug_ref[pl.ds(row, size), :]], axis=1)
                raw = [jnp.dot(lhs, rhs[:, j * TILE:(j + 1) * TILE], preferred_element_type=f32) for j in range(2)]
                out = []
                for j in range(2):
                    m, l, o = carry[j]
                    s = raw[j] * C2
                    m_new = jnp.maximum(m, jnp.max(s, axis=0, keepdims=True))
                    alpha = jnp.exp2(m - m_new)
                    p = jnp.exp2(s - m_new)
                    vT = vT_ref[pl.ds(pl.multiple_of(off + j * HEAD_DIM, HEAD_DIM), HEAD_DIM), pl.ds(row, size)]
                    out.append((m_new, l * alpha + jnp.sum(p, axis=0, keepdims=True),
                                o * alpha + jnp.dot(vT, p.astype(bf16), preferred_element_type=f32)))
                return tuple(out)
            return step

        def finish(state):
            for j in range(2):
                m, l, o = state[j]
                oT_ref[pl.ds(pl.multiple_of(off + j * HEAD_DIM, HEAD_DIM), HEAD_DIM), cols] = o * (1.0 / l)
                l_ref[0, j:j + 1, cols] = m + jnp.log2(l)

        init = tuple((jnp.full((1, TILE), -1e38, f32), jnp.zeros((1, TILE), f32), jnp.zeros((HEAD_DIM, TILE), f32)) for _ in range(2))

        longs = lax.div(need, LONG)
        state = lax.fori_loop(0, longs, block(start, LONG), init)
        finish(lax.fori_loop(0, lax.div(need - longs * LONG, SHORT), block(start + longs * LONG, SHORT), state))

    o_ref[...] = oT_ref[...].T.astype(bf16)


def attend(m, info, qT, k, vT, kaug, qaugT):
    win, nq = k.shape[1], qT.shape[2]
    qT, k, vT = stay(qT, k, vT)
    return pl.pallas_call(
        attend_kernel,
        out_shape=(jax.ShapeDtypeStruct((384, nq), f32), jax.ShapeDtypeStruct((nq, 384), bf16), jax.ShapeDtypeStruct((PAIRS, 8, nq), f32)),
        grid_spec=pltpu.PrefetchScalarGridSpec(
            num_scalar_prefetch=1, grid=(PAIRS,),
            in_specs=[
                pl.BlockSpec((None, 128, nq), lambda p, *_: (m, p // 2, 0)),
                pl.BlockSpec((None, win, 128), lambda p, *_: (m, 0, p // 2)),
                pl.BlockSpec((None, 128, win), lambda p, *_: (m, p // 2, 0)),
                pl.BlockSpec((win, 128), lambda p, *_: (0, 0)),
                pl.BlockSpec((128, nq), lambda p, *_: (0, 0)),
            ],
            out_specs=[
                pl.BlockSpec((128, nq), lambda p, *_: (p // 2, 0)),
                pl.BlockSpec((nq, 128), lambda p, *_: (0, p // 2)),
                pl.BlockSpec((1, 8, nq), lambda p, *_: (p, 0, 0)),
            ],
            scratch_shapes=[pltpu.VMEM((256, 2 * TILE), bf16)],
        ),
        compiler_params=pltpu.CompilerParams(vmem_limit_bytes=28 << 20),
        cost_estimate=pl.CostEstimate(flops=int(20 * 10**9 * 0.02), bytes_accessed=0, transcendentals=0),
        name="attend",
    )(info, qT, k, vT, kaug, qaugT)


def attend_back_kernel(info_ref, qT_ref, q_ref, k_ref, kT_ref, v_ref, doT_ref, do_ref, oT_ref, l_ref, kaug_ref, qaugT_ref,
                       dq_ref, dk_ref, dv_ref, dqT_ref, rhs_s, rhs_d, q_stk, do_stk, dk_acc, dv_acc):
    p_id = pl.program_id(0)
    off = pair_offset(info_ref)

    @pl.when(lax.rem(p_id, 2) == 0)
    def _():
        dqT_ref[...] = jnp.zeros_like(dqT_ref)
        dk_acc[...] = jnp.zeros_like(dk_acc)
        dv_acc[...] = jnp.zeros_like(dv_acc)

    for t in range(2):
        cols = slice(t * TILE, (t + 1) * TILE)
        masked_q = rows_masked(qT_ref[:, cols], off)
        masked_do = rows_masked(doT_ref[:, cols], off)
        lane_q = lanes_masked(q_ref[cols, :], off)
        lane_do = lanes_masked(do_ref[cols, :], off)
        for j in range(2):
            part = slice(j * TILE, (j + 1) * TILE)
            head = pl.ds(pl.multiple_of(off + j * HEAD_DIM, HEAD_DIM), HEAD_DIM)
            delta = jnp.sum(doT_ref[head, cols].astype(f32) * oT_ref[head, cols], axis=0, keepdims=True)
            total = l_ref[0, j:j + 1, cols] * (1.0 / C2)
            rowid = lax.broadcasted_iota(jnp.int32, (64, TILE), 0)
            lp, dp = split3(-total), split3(-delta)
            def pieces(parts):
                x = jnp.zeros((64, TILE), f32)
                for n in range(3):
                    x = jnp.where(rowid == n, parts[n].astype(f32), x)
                return x.astype(bf16)
            rhs_s[0:128, part] = masked_q[j]
            rhs_s[128:192, part] = qaugT_ref[0:64, cols]
            rhs_s[192:256, part] = pieces(lp)
            rhs_d[0:128, part] = masked_do[j]
            rhs_d[128:192, part] = jnp.zeros((64, TILE), bf16)
            rhs_d[192:256, part] = pieces(dp)
            q_stk[part, :] = lane_q[j]
            do_stk[part, :] = lane_do[j]
        start = info_ref[1 + t]
        need = info_ref[3 + t]

        def block(first, size):
            def step(i, carry):
                row = pl.multiple_of(first + i * size, 128)
                rows = pl.ds(row, size)
                aug = kaug_ref[rows, :]
                lhs_k = jnp.concatenate([k_ref[rows, :], aug], axis=1)
                lhs_v = jnp.concatenate([v_ref[rows, :], aug], axis=1)
                out, dv, dk = [], dv_acc[rows, :], dk_acc[rows, :]
                for j in range(2):
                    part = slice(j * TILE, (j + 1) * TILE)
                    s = jnp.dot(lhs_k, rhs_s[:, part], preferred_element_type=f32)
                    dp = jnp.dot(lhs_v, rhs_d[:, part], preferred_element_type=f32)
                    p = jnp.exp2(s * C2)
                    ds = (p * dp).astype(bf16)
                    dv = dv + jnp.dot(p.astype(bf16), do_stk[part, :], preferred_element_type=f32)
                    dk = dk + jnp.dot(ds, q_stk[part, :], preferred_element_type=f32)
                    kT = kT_ref[pl.ds(pl.multiple_of(off + j * HEAD_DIM, HEAD_DIM), HEAD_DIM), rows]
                    out.append(carry[j] + jnp.dot(kT, ds, preferred_element_type=f32))
                dv_acc[rows, :] = dv
                dk_acc[rows, :] = dk
                return tuple(out)
            return step

        def finish(dqs):
            for j in range(2):
                dqT_ref[pl.ds(pl.multiple_of(off + j * HEAD_DIM, HEAD_DIM), HEAD_DIM), cols] = dqs[j] * SCALE

        init = tuple(jnp.zeros((HEAD_DIM, TILE), f32) for _ in range(2))

        longs = lax.div(need, LONG)
        state = lax.fori_loop(0, longs, block(start, LONG), init)
        finish(lax.fori_loop(0, lax.div(need - longs * LONG, SHORT), block(start + longs * LONG, SHORT), state))
    @pl.when((lax.rem(p_id, 2) == 1) | (p_id == PAIRS - 1))
    def _():
        dq_ref[...] = dqT_ref[...].T.astype(bf16)
        dk_ref[...] = (dk_acc[...] * SCALE).astype(bf16)
        dv_ref[...] = dv_acc[...].astype(bf16)


def attend_back(m, info, qT, q, k, kT, v, doT, do, oT, lse, kaug, qaugT):
    win, nq = k.shape[1], qT.shape[2]
    qT, q, k, kT, v, doT, do = stay(qT, q, k, kT, v, doT, do)
    wide = pl.BlockSpec((128, nq), lambda p, *_: (p // 2, 0))
    tall = pl.BlockSpec((nq, 128), lambda p, *_: (0, p // 2))
    keys = pl.BlockSpec((win, 128), lambda p, *_: (0, p // 2))
    wide_m = pl.BlockSpec((None, 128, nq), lambda p, *_: (m, p // 2, 0))
    tall_m = pl.BlockSpec((None, nq, 128), lambda p, *_: (m, 0, p // 2))
    keys_m = pl.BlockSpec((None, win, 128), lambda p, *_: (m, 0, p // 2))
    return pl.pallas_call(
        attend_back_kernel,
        out_shape=tuple(pltpu.MemorySpace.VMEM(d, bf16) for d in ((nq, 384), (win, 384), (win, 384))),
        grid_spec=pltpu.PrefetchScalarGridSpec(
            num_scalar_prefetch=1, grid=(PAIRS,),
            in_specs=[wide_m, tall_m, keys_m, pl.BlockSpec((None, 128, win), lambda p, *_: (m, p // 2, 0)), keys_m,
                      pl.BlockSpec((128, nq), lambda p, *_: (p // 2, m)), pl.BlockSpec((nq, 128), lambda p, *_: (m, p // 2)), wide,
                      pl.BlockSpec((1, 8, nq), lambda p, *_: (p, 0, 0)),
                      pl.BlockSpec((win, 128), lambda p, *_: (0, 0)), pl.BlockSpec((128, nq), lambda p, *_: (0, 0))],
            out_specs=[tall, keys, keys],
            scratch_shapes=[pltpu.VMEM((128, nq), f32), pltpu.VMEM((256, 2 * TILE), bf16), pltpu.VMEM((256, 2 * TILE), bf16),
                            pltpu.VMEM((2 * TILE, 128), bf16), pltpu.VMEM((2 * TILE, 128), bf16),
                            pltpu.VMEM((win, 128), f32), pltpu.VMEM((win, 128), f32)],
        ),
        compiler_params=pltpu.CompilerParams(vmem_limit_bytes=32 << 20),
        cost_estimate=pl.CostEstimate(flops=int(40 * 10**9 * 0.02), bytes_accessed=0, transcendentals=0),
        name="attend_back",
    )(info, qT, q, k, kT, v, doT, do, oT, lse, kaug, qaugT)


def moments(x):
    centred = x - jnp.mean(x, axis=-1, keepdims=True)
    r = lax.rsqrt(jnp.mean(centred * centred, axis=-1, keepdims=True) + EPSILON)
    return centred * r, r


def norm_back(grad, n, r, gain):
    e = grad * gain
    return r * (e - jnp.mean(e, axis=-1, keepdims=True) - n * jnp.mean(e * n, axis=-1, keepdims=True))


def call(kernel, out_shape, name, flops=10**9, limit=48, **spec):
    return pl.pallas_call(
        kernel, out_shape=out_shape, name=name,
        compiler_params=pltpu.CompilerParams(vmem_limit_bytes=limit << 20),
        cost_estimate=pl.CostEstimate(flops=int(flops * 0.02), bytes_accessed=0, transcendentals=0), **spec)


def shape(*dims, dtype=bf16):
    return jax.ShapeDtypeStruct(dims, dtype)


def far(*dims, dtype=bf16):
    return pltpu.MemorySpace.HBM(dims, dtype)


def stay(*arrays):
    return [pltpu.with_memory_space_constraint(a, pltpu.MemorySpace.HBM) for a in arrays]


def scalar_first(grid, in_specs, out_specs, scratch=()):
    return dict(grid_spec=pltpu.PrefetchScalarGridSpec(
        num_scalar_prefetch=1, grid=grid, in_specs=in_specs, out_specs=out_specs, scratch_shapes=list(scratch)))


def full(*dims):
    return pl.BlockSpec(dims, lambda *_: (0,) * len(dims))


def pack_heads_kernel(core_ref, qkv_ref, vec_ref, heads_ref):
    for part in range(3):
        near = pl.ds(pl.multiple_of(640 * part + 256 * core_ref[0], 128), 256)
        heads_ref[:, 384 * part:384 * part + 256] = qkv_ref[:, near]
        heads_ref[:, 384 * part + 256:384 * (part + 1)] = qkv_ref[:, 640 * part + 512:640 * (part + 1)]
    heads_ref[:, 1152:1280] = vec_ref[...]


def pack_heads(core, w_qkv, vectors):
    return call(pack_heads_kernel, shape(160, 1280), "pack_heads", 10**6, 8, **scalar_first(
        (1,), [full(160, 1920), full(160, 128)], full(160, 1280)))(core, w_qkv, vectors)


def turn_kernel(vec_ref, rows_ref):
    rows_ref[...] = vec_ref[...].astype(f32).T[:16]


def vector_rows(heads):
    return call(turn_kernel, shape(16, 640, dtype=f32), "vector_rows", 10**12, 8, grid=(1,),
                in_specs=[pl.BlockSpec((640, 128), lambda i: (0, 9))], out_specs=full(16, 640))(*stay(heads))


def pack_feed_kernel(core_ref, out_ref, up_ref, down_ref, feed_ref):
    core = core_ref[0]
    feed_ref[:, 5120:5760] = out_ref[...]
    for f in range(4):
        feed_ref[:, 640 * f:640 * (f + 1)] = up_ref[:, pl.ds(pl.multiple_of(1280 * f + 640 * core, 128), 640)]
        feed_ref[:, 2560 + 640 * f:2560 + 640 * (f + 1)] = down_ref[pl.ds(pl.multiple_of(640 * core + 160 * f, 32), 160), :]


def pack_feed(core, w_out, w_up, w_down):
    return call(pack_feed_kernel, far(160, 5760), "pack_feed", 10**6, 16, **scalar_first(
        (1,), [full(160, 640), full(160, 5120), full(1280, 640)], full(160, 5760)))(core, *stay(w_out, w_up, w_down))


def rows_in_order(core, mine_ref, theirs_ref, x_ref):
    for c, (first, second) in enumerate(((mine_ref, theirs_ref), (theirs_ref, mine_ref))):
        @pl.when(core == c)
        def _():
            x_ref[0:256, :], x_ref[256:512, :] = first[...], second[...]


def normal_kernel(tok_ref, n_ref):
    for m in range(2):
        n_ref[m] = moments(tok_ref[m].astype(f32))[0].astype(bf16)


def normal_rows(tok):
    return call(normal_kernel, shape(2, 256, 640), "normal_rows", 10**6, 8, grid=(1,), in_specs=[full(2, 256, 640)], out_specs=full(2, 256, 640))(tok)


def project_kernel(chips, place_ref, *refs):
    n = len(chips)
    own_refs, other_refs = refs[:n], refs[n:2 * n]
    vec_ref, w_ref = refs[2 * n:2 * n + 2]
    k_ref, v_ref, kT_ref, vT_ref = refs[-6 - 2 * (n == 3):][:4]
    x_ref, hid_ref = refs[-2:]
    m, step = pl.program_id(0), pl.program_id(1)
    block = sum(jnp.where(step == i, chip, 0) for i, chip in enumerate(chips))
    needed = (block >= place_ref[1 + 2 * m]) & (block < place_ref[2 + 2 * m])

    @pl.when(jnp.logical_not(needed))
    def _():
        for ref in (k_ref, v_ref, kT_ref, vT_ref):
            ref[...] = jnp.zeros_like(ref)

    @pl.when(needed)
    def _():
        for j in range(n):
            @pl.when(step == j)
            def _():
                rows_in_order(place_ref[0], own_refs[j].at[m], other_refs[j].at[m], x_ref)

        hidden = (x_ref[...].astype(f32) * vec_ref[0:1, :] + vec_ref[1:2, :]).astype(bf16)
        hid_ref[...] = hidden
        kv = jnp.dot(hidden, w_ref[:, 384:], preferred_element_type=f32)
        low = kv.astype(bf16)
        k_ref[0] = low[:, :384]
        v_ref[0] = low[:, 384:]
        turned = kv.T.astype(bf16)
        kT_ref[0] = turned[:384]
        vT_ref[0] = turned[384:]

    if n == 3:
        q_ref, qT_ref = refs[-4:-2]

        @pl.when(step == 1)
        def _():
            q = jnp.dot(hid_ref[...], w_ref[:, :384], preferred_element_type=f32)
            q_ref[0] = q.astype(bf16)
            qT_ref[0] = q.T.astype(bf16)


def project(chips, place, own, other, vec, w, earlier=()):
    n = len(chips)
    chip = (lambda b: b + 1) if n == 3 else (lambda b: 4 * b)
    tall = pl.BlockSpec((1, 512, 384), lambda m, b, *_: (m, chip(b), 0))
    wide = pl.BlockSpec((1, 384, 512), lambda m, b, *_: (m, 0, chip(b)))
    shapes = [far(2, 2560, 384), far(2, 2560, 384), far(2, 384, 2560), far(2, 384, 2560)]
    specs = [tall, tall, wide, wide]
    if n == 3:
        shapes += [far(2, 512, 384), far(2, 384, 512)]
        specs += [pl.BlockSpec((1, 512, 384), lambda m, *_: (m, 0, 0)), pl.BlockSpec((1, 384, 512), lambda m, *_: (m, 0, 0))]
    own, other = [own[c] for c in chips], [other[c] for c in chips]
    return call(
        lambda *refs: project_kernel(chips, *refs), shapes, "project", 5 * 10**9, 28,
        input_output_aliases={2 * n + 3 + i: i for i in range(len(earlier))}, **scalar_first(
            (2, n), [full(2, 256, 640)] * (2 * n) + [full(16, 640), full(640, 1152)] + [pl.BlockSpec(memory_space=pl.ANY)] * len(earlier),
            specs, [pltpu.VMEM((512, 640), bf16), pltpu.VMEM((512, 640), bf16)]))(place, *own, *other, *stay(vec, w), *earlier)


def heads_joined(core, mine, theirs):
    first, second = (jnp.where(core == 0, a, b) for a, b in ((mine, theirs), (theirs, mine)))
    return jnp.concatenate([first[:, :256], second[:, :256], first[:, 256:] + second[:, 256:]], axis=1)


def middle_kernel(core_ref, w_ref, low0_ref, low1_ref, theirs_ref, tok_ref, tok2_ref, vec_ref, mid_ref, hid_ref, hid2_ref):
    core = core_ref[0]
    for m, low_ref in enumerate((low0_ref, low1_ref)):
        attended = heads_joined(core, low_ref[...].astype(f32), theirs_ref[m].astype(f32)).astype(bf16)
        branch = jnp.dot(attended, w_ref[...], preferred_element_type=f32)
        mine = jnp.where(core == 0, branch[:256], branch[256:]) + tok_ref[m].astype(f32)
        theirs = jnp.where(core == 0, branch[256:], branch[:256]) + tok2_ref[m].astype(f32)
        part = slice(256 * m, 256 * (m + 1))
        mid_ref[part, :] = mine
        hid_ref[part, :] = (moments(mine)[0] * vec_ref[2:3, :] + vec_ref[3:4, :]).astype(bf16)
        hid2_ref[part, :] = (moments(theirs)[0] * vec_ref[2:3, :] + vec_ref[3:4, :]).astype(bf16)


W_OUT = pl.BlockSpec((640, 640), lambda *_: (0, 8))


def middle_step(core, weights, *args):
    return call(middle_kernel, (far(512, 640, dtype=f32), far(512, 640), far(512, 640)), "middle", 10**9, 20, **scalar_first(
        (1,), [W_OUT] + [full(*a.shape) for a in args], [full(512, 640)] * 3))(core, *stay(weights), *args[:-1], *stay(args[-1]))


def feed_kernel(h_ref, h2_ref, cot_ref, cot2_ref, up_ref, down_ref, mine_ref, theirs_ref, g_ref, h, cot, hT, cT, out, dh):
    chunk = pl.program_id(0)

    @pl.when(chunk == 0)
    def _():
        h[0:512, :], h[512:1024, :] = h_ref[...], h2_ref[...]
        cot[0:512, :], cot[512:1024, :] = cot_ref[...], cot2_ref[...]
        hT[...] = h[...].astype(f32).T.astype(bf16)
        cT[...] = cot[...].astype(f32).T.astype(bf16)
        out[...] = jnp.zeros_like(out)
        dh[...] = jnp.zeros_like(dh)

    up_w = up_ref[...]
    down_w = jnp.concatenate([down_ref[160 * y:160 * (y + 1), 640 * i:640 * (i + 1)] for y in range(2) for i in range(4)], axis=0)
    acts, d_ups = [], []
    for t in range(4):
        rows = slice(256 * t, 256 * (t + 1))
        u = jnp.dot(h[rows, :], up_w, preferred_element_type=f32)
        d_act = lax.dot_general(cot[rows, :], down_w, NT, preferred_element_type=f32)
        cdf = 0.5 * (1.0 + lax.erf(u * (2.0 ** -0.5)))
        pdf = jnp.exp(u * u * -0.5) * ((2.0 * math.pi) ** -0.5)
        act = (u * cdf).astype(bf16)
        d_up = (d_act * (cdf + u * pdf)).astype(bf16)
        out[rows, :] += jnp.dot(act, down_w, preferred_element_type=f32)
        dh[rows, :] += lax.dot_general(d_up, up_w, NT, preferred_element_type=f32)
        acts.append(act)
        d_ups.append(d_up)
    g_up = jnp.dot(hT[...], jnp.concatenate(d_ups, axis=0), preferred_element_type=f32).astype(bf16)
    g_down = jnp.dot(cT[...], jnp.concatenate(acts, axis=0), preferred_element_type=f32).T.astype(bf16)
    for f in range(2):
        for y in range(4):
            for i in range(2):
                g_ref[4 * chunk + 2 * f + i, y] = g_up[160 * y + 80 * i:160 * y + 80 * (i + 1), 640 * f:640 * (f + 1)]
        for i in range(8):
            g_ref[8 + i, 2 * chunk + f] = g_down[640 * f + 80 * i:640 * f + 80 * (i + 1)]

    @pl.when(chunk == 1)
    def _():
        mine_ref[0], mine_ref[1] = out[0:512, :].astype(bf16), dh[0:512, :].astype(bf16)
        theirs_ref[0], theirs_ref[1] = out[512:1024, :].astype(bf16), dh[512:1024, :].astype(bf16)


def feed_forward(h, h2, cot, cot2, weights):
    return call(
        feed_kernel,
        (far(2, 512, 640), far(2, 512, 640), far(16, 4, 80, 640)),
        "feed_forward", 30 * 10**9, 52, grid=(2,),
        in_specs=[full(512, 640)] * 4 + [pl.BlockSpec((640, 1280), lambda f: (0, f)), pl.BlockSpec((320, 2560), lambda f: (f, 1))],
        out_specs=[full(2, 512, 640), full(2, 512, 640), full(16, 4, 80, 640)],
        scratch_shapes=[pltpu.VMEM((1024, 640), bf16), pltpu.VMEM((1024, 640), bf16), pltpu.VMEM((640, 1024), bf16), pltpu.VMEM((640, 1024), bf16),
                        pltpu.VMEM((1024, 640), f32), pltpu.VMEM((1024, 640), f32)],
    )(*stay(h, h2, cot), cot2, *stay(weights, weights))


def after_kernel(mid_ref, mine_ref, theirs_ref, cot_ref, vec_ref, block_ref, grad_ref, branch_ref, g_ref):
    @pl.when(pl.program_id(0) == 0)
    def _():
        g_ref[...] = jnp.zeros_like(g_ref)

    middle = mid_ref[...]
    block_ref[...] = (middle + mine_ref[0].astype(f32) + theirs_ref[0].astype(f32)).astype(bf16)
    d_hidden = mine_ref[1].astype(f32) + theirs_ref[1].astype(f32)
    n, r = moments(middle)
    g_ref[0:1, :] += jnp.sum(d_hidden * n, axis=0, keepdims=True)
    g_ref[1:2, :] += jnp.sum(d_hidden, axis=0, keepdims=True)
    grad = cot_ref[...].astype(f32) + norm_back(d_hidden, n, r, vec_ref[2:3, :])
    grad_ref[...] = grad
    branch_ref[...] = grad.astype(bf16)


def after_feed(*args):
    rows, pair = pl.BlockSpec((128, 640), lambda i: (i, 0)), pl.BlockSpec((2, 128, 640), lambda i: (0, i, 0))
    return call(
        after_kernel, (far(512, 640), far(512, 640, dtype=f32), shape(512, 640), shape(8, 640, dtype=f32)), "after_feed", 10**9, 16,
        grid=(4,), in_specs=[rows, pair, pair, rows, full(16, 640)], out_specs=[rows, rows, rows, full(8, 640)])(*stay(args[0], args[1]), args[2], *stay(args[3], args[4]))


def branch_kernel(core_ref, own_ref, their_ref, w_ref, low0_ref, low1_ref, theirs_ref, do_ref, doT_ref, g_ref):
    core = core_ref[0]
    w = jnp.concatenate([w_ref[pl.ds(pl.multiple_of(256 * core, 256), 256), :], w_ref[512:640, :]], axis=0)
    g = jnp.zeros((640, 384), f32)
    for m in range(2):
        part = slice(256 * m, 256 * (m + 1))
        mine, theirs = own_ref[part, :].astype(f32), their_ref[part, :].astype(f32)
        branch = jnp.concatenate([jnp.where(core == 0, mine, theirs), jnp.where(core == 0, theirs, mine)], axis=0)
        kept = jnp.where(core == 0, branch[:, :384], branch[:, 256:]).astype(bf16)
        branch = branch.astype(bf16)
        rows = slice(512 * m, 512 * (m + 1))
        do = lax.dot_general(branch, w, NT, preferred_element_type=f32)
        do_ref[rows, :] = do.astype(bf16)
        doT_ref[:, rows] = do.T.astype(bf16)
        attended = heads_joined(core, (low0_ref, low1_ref)[m][...].astype(f32), theirs_ref[m].astype(f32))
        g = g + jnp.dot(attended.T.astype(bf16), kept, preferred_element_type=f32)
    g_ref[...] = g.astype(bf16)


def branch_step(core, own, their, weights, *args):
    return call(
        branch_kernel, (far(1024, 384), far(384, 1024), shape(640, 384)), "branch", 10**9, 24, **scalar_first(
            (1,), [full(512, 640)] * 2 + [W_OUT] + [full(*a.shape) for a in args], [full(1024, 384), full(384, 1024), full(640, 384)]))(
                core, own, their, *stay(weights), *args)


def near_by(*arrays):
    return [pltpu.with_memory_space_constraint(a, pltpu.MemorySpace.VMEM) for a in arrays]


def project_back_kernel(place_ref, *refs):
    own_refs, other_refs = refs[:5], refs[5:10]
    (vec_ref, w_ref, dq0_ref, dq1_ref, dk0_ref, dk1_ref, dv0_ref, dv1_ref, g_out_ref, g_two_ref,
     mine_ref, theirs_ref, tail_ref, n_ref, d_kv, d_q, d_hid, g_ref, g_vec, slots, arrived) = refs[10:]
    step, core = pl.program_id(0), place_ref[0]
    block, second = lax.rem(step, 5), lax.div(step, 5)
    inside = lambda j, m: (j >= place_ref[1 + 2 * m]) & (j < place_ref[2 + 2 * m])
    needed = inside(block, second)

    def copies(j, m, slot):
        return [pltpu.make_async_copy(refs_of[j].at[m], slots.at[slot, i], arrived.at[slot, i]) for i, refs_of in enumerate((own_refs, other_refs))]

    @pl.when(step == 0)
    def _():
        for m in range(2):
            for j in range(5):
                @pl.when(inside(j, m))
                def _():
                    for copy in copies(j, m, 5 * m + j):
                        copy.start()
        g_ref[...] = jnp.zeros_like(g_ref)
        g_vec[...] = jnp.zeros_like(g_vec)
        g_vec[2:4, :] = g_two_ref[0:2, :]

    @pl.when(jnp.logical_not(needed))
    def _():
        mine_ref[...] = jnp.zeros_like(mine_ref)
        theirs_ref[...] = jnp.zeros_like(theirs_ref)

    @pl.when(needed)
    def _():
        for copy in copies(0, 0, step):
            copy.wait()
        rows_in_order(core, slots.at[step, 0], slots.at[step, 1], n_ref)

    for m, (dq, dk, dv) in enumerate(((dq0_ref, dk0_ref, dv0_ref), (dq1_ref, dk1_ref, dv1_ref))):
        @pl.when(needed & (second == m))
        def _():
            rows = pl.ds(pl.multiple_of(block * 512, 512), 512)
            d_kv[:, :384], d_kv[:, 384:] = dk[rows, :], dv[rows, :]
            d_q[...] = dq[...]

    @pl.when(needed)
    def _():
        n = n_ref[...].astype(f32)
        hiddenT = (n * vec_ref[0:1, :] + vec_ref[1:2, :]).T.astype(bf16)
        d_hid[...] = lax.dot_general(d_kv[...], w_ref[:, 384:1152], NT, preferred_element_type=f32)
        g_ref[:, 384:] += jnp.dot(hiddenT, d_kv[...], preferred_element_type=f32)

        @pl.when(block == 2)
        def _():
            g_ref[:, :384] += jnp.dot(hiddenT, d_q[...], preferred_element_type=f32)
            d_hid[...] += lax.dot_general(d_q[...], w_ref[:, :384], NT, preferred_element_type=f32)

        dh = d_hid[...]
        low = dh.astype(bf16)
        for c, (first, other) in enumerate(((mine_ref, theirs_ref), (theirs_ref, mine_ref))):
            @pl.when(core == c)
            def _():
                first[0, 0], other[0, 0] = low[:256], low[256:]
        g_vec[0:1, :] += jnp.sum(dh * n, axis=0, keepdims=True)
        g_vec[1:2, :] += jnp.sum(dh, axis=0, keepdims=True)

    @pl.when(step == 9)
    def _():
        turned = g_vec[...].T
        lane = lax.broadcasted_iota(jnp.int32, (640, 128), 1) - 64 * (1 - core)
        spare = g_ref[:, 256:384]
        for i in range(4):
            spare = jnp.where(lane == i, turned[:, i:i + 1], spare)
        g_ref[:, 256:384] = spare
        for y in range(4):
            for z in range(4):
                rows = slice(160 * y + 40 * z, 160 * y + 40 * (z + 1))
                for x in range(3):
                    tail_ref[16 * y + 4 * z + x] = g_ref[rows, 384 * x:384 * (x + 1)].astype(bf16)
                tail_ref[16 * y + 4 * z + 3] = g_out_ref[rows, :].astype(bf16)


def project_back(place, own, other, vec, w, dq, dk, dv, g_out, g_two):
    here = pl.BlockSpec(memory_space=pltpu.VMEM)
    part = pl.BlockSpec((1, 1, 256, 640), lambda b, *_: (lax.rem(b, 5), b // 5, 0, 0))
    return call(
        project_back_kernel, (far(5, 2, 256, 640), far(5, 2, 256, 640), far(64, 40, 384)), "project_back", 10**10, 30, **scalar_first(
            (10,), [pl.BlockSpec(memory_space=pl.ANY)] * 10 + [here] * 10, [part, part, full(64, 40, 384)],
            [pltpu.VMEM((512, 640), bf16), pltpu.VMEM((512, 768), bf16), pltpu.VMEM((512, 384), bf16),
             pltpu.VMEM((512, 640), f32), pltpu.VMEM((640, 1152), f32), pltpu.VMEM((8, 640), f32),
             pltpu.VMEM((10, 2, 256, 640), bf16), pltpu.SemaphoreType.DMA((10, 2))]))(
                 place, *stay(*own, *other), *near_by(vec, w, *dq, *dk, *dv, g_out, g_two))


def in_core_order(core_ref, mine, theirs):
    core, mine, theirs = core_ref[0], mine.astype(f32), theirs.astype(f32)
    return jnp.where(core == 0, mine, theirs), jnp.where(core == 0, theirs, mine)


def final_feed_kernel(core_ref, mine_ref, theirs_ref, up_ref, down_ref):
    for i in range(16):
        for c, piece in enumerate(in_core_order(core_ref, mine_ref[i], theirs_ref[i])):
            if i < 8:
                base = 1280 * (i // 2) + 640 * c
                up_ref[80 * (i % 2):80 * (i % 2 + 1), base:base + 640] = piece
            else:
                base = 640 * c + 80 * (i - 8)
                down_ref[base:base + 80, :] = piece


def final_feed(core, mine, theirs):
    return call(final_feed_kernel, (shape(160, 5120, dtype=f32), shape(1280, 640, dtype=f32)), "final_feed", 10**6, 32, **scalar_first(
        (1,), [full(16, 80, 640)] * 2, [full(160, 5120), full(1280, 640)]))(core, mine, theirs)


def final_heads_kernel(core_ref, mine_ref, theirs_ref, qkv_ref, out_ref, vec_ref):
    lane = lax.broadcasted_iota(jnp.int32, (40, 128), 1)
    for z in range(4):
        rows = slice(40 * z, 40 * (z + 1))
        for x in range(4):
            a, b = in_core_order(core_ref, mine_ref[4 * z + x], theirs_ref[4 * z + x])
            if x < 3:
                last = jnp.where(lane < 64, a[:, 256:], b[:, 256:])
                qkv_ref[rows, 640 * x:640 * (x + 1)] = jnp.concatenate([a[:, :256], b[:, :256], last], axis=1)
            else:
                out_ref[rows, :] = jnp.concatenate([a, b[:, 128:]], axis=1)
            if x == 0:
                vec_ref[rows, :] = pltpu.roll(a[:, 256:], 64, 1) + b[:, 256:]


def final_heads(core, mine, theirs):
    return call(
        final_heads_kernel, (shape(160, 1920, dtype=f32), shape(160, 640, dtype=f32), shape(160, 128, dtype=f32)), "final_heads", 10**6, 16,
        **scalar_first((1,), [full(16, 40, 384)] * 2, [full(160, 1920), full(160, 640), full(160, 128)]))(core, mine, theirs)


def shifted(array, axis, by):
    devices = lax.axis_size(axis)
    return lax.ppermute(array, axis, [(i, (i + by) % devices) for i in range(devices)])


def passed_along(array, by):
    devices = lax.axis_size(("z", "x"))
    return lax.ppermute(array, ("z", "x"), [(i, i + by) for i in range(devices) if 0 <= i + by < devices])


def swapped(array):
    return lax.ppermute(array, "core", [(0, 1), (1, 0)])


def pick(array, index):
    return lax.dynamic_index_in_dim(array, index, 0, keepdims=False)


def summed_share(array, axis):
    me, devices = lax.axis_index(axis), lax.axis_size(axis)
    total = pick(array, me).astype(f32)
    for by in (1, devices - 1, 2):
        total = total + shifted(pick(array, (me + by) % devices), axis, by).astype(f32)
    return total.astype(bf16)


def gathered(array, axis):
    me, devices = lax.axis_index(axis), lax.axis_size(axis)
    out = jnp.zeros((devices,) + array.shape, array.dtype)
    out = lax.dynamic_update_index_in_dim(out, array, me, 0)
    for by in (1, devices - 1, 2):
        out = lax.dynamic_update_index_in_dim(out, shifted(array, axis, by), (me + devices - by) % devices, 0)
    return out


def window_info(length_row, chip, core, win):
    ends = jnp.cumsum(length_row)
    starts = ends - length_row
    base = chip * 512 - 1024
    places = base + jnp.arange(win, dtype=jnp.int32)
    inside = (places[:, None] >= starts[None, :]) & (places[:, None] < ends[None, :])
    ones = jnp.broadcast_to(jnp.arange(64) < 3, (win, 64)).astype(bf16)
    key_rows = jnp.concatenate([jnp.where(inside, 0.0, -BIG).astype(bf16), ones], axis=1)
    own = chip * 512 + jnp.arange(512, dtype=jnp.int32)
    inside_q = (own[None, :] >= starts[:, None]) & (own[None, :] < ends[:, None])
    query_rows = jnp.concatenate([inside_q.astype(bf16), jnp.zeros((64, 512), bf16)], axis=0)
    info = [core]
    sizes = []
    for t in range(2):
        first = chip * 512 + t * TILE
        low = jnp.max(jnp.where(starts <= first, starts, 0)) - base
        high = jnp.min(jnp.where(ends > first + TILE - 1, ends, 1 << 30)) - base
        start = low // 128 * 128
        need = high - start
        size = (need + SHORT - 1) // SHORT * SHORT
        info.append(jnp.minimum(start, win - size))
        sizes.append(size)
    low = jnp.minimum(info[1], info[2]) // 512
    high = (jnp.maximum(info[1] + sizes[0], info[2] + sizes[1]) + 511) // 512
    return jnp.stack(info + sizes).astype(jnp.int32), key_rows, query_rows, [low, high]


def body(tokens, lengths, gain_one, bias_one, w_qkv, w_out, gain_two, bias_two, w_up, w_down, cotangent):
    core, chip = lax.axis_index("core"), lax.axis_index(("z", "x"))
    core_arg = core[None].astype(jnp.int32)
    tok, cot = tokens[:, 0], cotangent[:, 0].reshape(512, 640)
    together = lambda *arrays: lax.optimization_barrier(arrays)

    vectors = jnp.pad(jnp.stack([gain_one, bias_one, gain_two, bias_two], axis=1), ((0, 0), (0, 124)))
    heads, tok_sent = together(pack_heads(core_arg, w_qkv, vectors), tok)
    heads = lax.all_gather(heads, "batch", axis=0, tiled=True)
    vec = vector_rows(heads)
    normal = normal_rows(tok_sent)
    before, after, normal_other, tok_other = passed_along(normal, 1), passed_along(normal, -1), swapped(normal), swapped(tok)
    windows = [window_info(lengths[m, 0], chip, core, 2560) for m in range(2)]
    place = jnp.stack([core] + windows[0][3] + windows[1][3]).astype(jnp.int32)
    feed_pack = pack_feed(core_arg, w_out, w_up, w_down)
    heads, vec, before, after, normal_other, tok_other, feed_pack, place, windows = together(
        heads, vec, before, after, normal_other, tok_other, feed_pack, place, windows)
    own = [passed_along(before, 1), before, normal, after, passed_along(after, -1)]
    other = [None, swapped(before), normal_other, swapped(after), None]
    feed_weights = lax.all_gather(feed_pack, "batch", axis=0, tiled=True)
    *near_parts, q, qT = project((1, 2, 3), place, own, other, vec, heads)
    own[0], own[4], near_parts = together(own[0], own[4], near_parts)
    other[0], other[4] = swapped(own[0]), swapped(own[4])
    k, v, kT, vT = project((0, 4), place, own, other, vec, heads, near_parts)
    (oT0, low0, lse0), (oT1, low1, lse1) = (
        attend(m, info, qT, k, vT, key_rows, query_rows) for m, (info, key_rows, query_rows, _) in enumerate(windows))

    theirs = swapped(jnp.stack([low0, low1]))
    middle, hidden_two, hidden_other = middle_step(core_arg, feed_weights, low0, low1, theirs, tok, tok_other, vec)
    mine, partial, feed_grads = feed_forward(hidden_two, hidden_other, cot, swapped(cot), feed_weights)
    feed_grads = lax.psum_scatter(feed_grads.reshape(5120, 640), ("z", "x"), scatter_dimension=0, tiled=True)
    block_out, grad_middle, branch, g_two = after_feed(middle, mine, swapped(partial), cot, vec)

    do, doT, g_out = branch_step(core_arg, branch, swapped(branch), feed_weights, low0, low1, theirs)
    dq, dk, dv = zip(*(
        attend_back(m, info, qT, q, k, kT, v, doT, do, oT, lse, key_rows, query_rows)
        for m, ((info, key_rows, query_rows, _), oT, lse) in enumerate(zip(windows, (oT0, oT1), (lse0, lse1)))))
    mine, theirs, tail = project_back(place, own, other, vec, heads, dq, dk, dv, g_out, g_two)
    feed_grads, mine, theirs, tail = together(feed_grads, mine, theirs, tail)

    feed = summed_share(feed_grads.reshape(4, 80, 640), "batch")
    theirs = swapped(theirs)
    sums = [mine[j].astype(f32) + theirs[j].astype(f32) for j in range(5)]
    feed, right, left = together(feed, sums[4].astype(bf16), sums[0].astype(bf16))
    feed = lax.all_gather(feed, ("z", "x"), axis=0, tiled=True).reshape(16, 80, 640)
    right, left = passed_along(right, 1), passed_along(left, -1)
    tail, right, left = together(tail, right, left)
    tail = lax.all_to_all(tail, ("batch", "z", "x"), 0, 0, tiled=True)
    right = passed_along((right.astype(f32) + sums[3]).astype(bf16), 1)
    left = passed_along((left.astype(f32) + sums[1]).astype(bf16), -1)
    tail, right, left = together(tail, right, left)
    tail = gathered(jnp.sum(tail.astype(f32), axis=0).astype(bf16), "x").reshape(160, 384)
    tail = gathered(tail, "z").reshape(16, 40, 384)
    d_one = (sums[2] + right.astype(f32) + left.astype(f32)).reshape(512, 640)
    n_one, r_one = moments(tok.reshape(512, 640).astype(f32))
    grad_tokens = (grad_middle + norm_back(d_one, n_one, r_one, vec[0:1])).astype(bf16)
    tail, grad_tokens, feed = together(tail, grad_tokens, feed)
    grad_qkv, grad_out, spare = final_heads(core_arg, tail, swapped(tail))
    grad_up, grad_down = final_feed(core_arg, feed, swapped(feed))
    return (
        block_out.reshape(2, 1, 256, 640), grad_tokens.reshape(2, 1, 256, 640), spare[:, 0], spare[:, 1], grad_qkv, grad_out,
        spare[:, 2], spare[:, 3], grad_up, grad_down)


def solution(mesh):
    fine = Mesh(mesh.devices.reshape(4, 4, 4, 2), ("batch", "z", "x", "core"))
    rows = P(None, "batch", ("z", "x", "core"), None)
    one, two = P("batch"), P("batch", None)
    return jax.shard_map(
        body,
        mesh=fine,
        in_specs=(rows, P(None, "batch", None), one, one, two, two, one, one, two, two, rows),
        out_specs=(rows, rows, one, one, two, two, one, one, two, two),
        check_vma=False,
    )
```

```python
import math

import jax
import jax.numpy as jnp
from jax import lax
from jax.experimental import pallas as pl
from jax.experimental.pallas import tpu as pltpu
from jax.sharding import Mesh
from jax.sharding import PartitionSpec as P

HEAD_DIM = 32
SCALE = HEAD_DIM ** -0.5
LOG2E = math.log2(math.e)
C2 = SCALE * LOG2E
BIG = 1e30
TILE = 256
EPSILON = 1e-05
PAIRS = 5
SHORT, LONG = 384, 1152
f32, bf16 = jnp.float32, jnp.bfloat16
NT = (((1,), (1,)), ((), ()))


def pair_offset(info_ref):
    p = pl.program_id(0)
    sub = jnp.where(p == PAIRS - 1, info_ref[0], lax.rem(p, 2))
    return sub * (2 * HEAD_DIM)


def split3(v):
    a = v.astype(bf16)
    r = v - a.astype(f32)
    b = r.astype(bf16)
    d = (r - b.astype(f32)).astype(bf16)
    return a, b, d


def rows_masked(xT, off):
    row = lax.broadcasted_iota(jnp.int32, xT.shape, 0) - off
    xf = xT.astype(f32)
    return [jnp.where((row >= HEAD_DIM * j) & (row < HEAD_DIM * (j + 1)), xf, 0.0).astype(bf16) for j in range(2)]


def lanes_masked(x, off):
    lane = lax.broadcasted_iota(jnp.int32, x.shape, 1) - off
    xf = x.astype(f32)
    return [jnp.where((lane >= HEAD_DIM * j) & (lane < HEAD_DIM * (j + 1)), xf, 0.0).astype(bf16) for j in range(2)]


def attend_kernel(info_ref, qT_ref, k_ref, vT_ref, kaug_ref, qaugT_ref, oT_ref, o_ref, l_ref, rhs):
    off = pair_offset(info_ref)
    oT_ref[...] = jnp.where(lax.rem(pl.program_id(0), 2) == 0, 0.0, oT_ref[...])
    for t in range(2):
        cols = slice(t * TILE, (t + 1) * TILE)
        masked = rows_masked(qT_ref[:, cols], off)
        for j in range(2):
            rhs[0:128, j * TILE:(j + 1) * TILE] = masked[j]
            rhs[128:256, j * TILE:(j + 1) * TILE] = qaugT_ref[:, cols]
        start = info_ref[1 + t]
        need = info_ref[3 + t]

        def block(first, size):
            def step(i, carry):
                row = pl.multiple_of(first + i * size, 128)
                lhs = jnp.concatenate([k_ref[pl.ds(row, size), :], kaug_ref[pl.ds(row, size), :]], axis=1)
                raw = [jnp.dot(lhs, rhs[:, j * TILE:(j + 1) * TILE], preferred_element_type=f32) for j in range(2)]
                out = []
                for j in range(2):
                    m, l, o = carry[j]
                    s = raw[j] * C2
                    m_new = jnp.maximum(m, jnp.max(s, axis=0, keepdims=True))
                    alpha = jnp.exp2(m - m_new)
                    p = jnp.exp2(s - m_new)
                    vT = vT_ref[pl.ds(pl.multiple_of(off + j * HEAD_DIM, HEAD_DIM), HEAD_DIM), pl.ds(row, size)]
                    out.append((m_new, l * alpha + jnp.sum(p, axis=0, keepdims=True),
                                o * alpha + jnp.dot(vT, p.astype(bf16), preferred_element_type=f32)))
                return tuple(out)
            return step

        def finish(state):
            for j in range(2):
                m, l, o = state[j]
                oT_ref[pl.ds(pl.multiple_of(off + j * HEAD_DIM, HEAD_DIM), HEAD_DIM), cols] = o * (1.0 / l)
                l_ref[0, j:j + 1, cols] = m + jnp.log2(l)

        init = tuple((jnp.full((1, TILE), -1e38, f32), jnp.zeros((1, TILE), f32), jnp.zeros((HEAD_DIM, TILE), f32)) for _ in range(2))

        longs = lax.div(need, LONG)
        state = lax.fori_loop(0, longs, block(start, LONG), init)
        finish(lax.fori_loop(0, lax.div(need - longs * LONG, SHORT), block(start + longs * LONG, SHORT), state))

    o_ref[...] = oT_ref[...].T.astype(bf16)


def attend(m, info, qT, k, vT, kaug, qaugT):
    win, nq = k.shape[1], qT.shape[2]
    qT, k, vT = stay(qT, k, vT)
    return pl.pallas_call(
        attend_kernel,
        out_shape=(jax.ShapeDtypeStruct((384, nq), f32), jax.ShapeDtypeStruct((nq, 384), bf16), jax.ShapeDtypeStruct((PAIRS, 8, nq), f32)),
        grid_spec=pltpu.PrefetchScalarGridSpec(
            num_scalar_prefetch=1, grid=(PAIRS,),
            in_specs=[
                pl.BlockSpec((None, 128, nq), lambda p, *_: (m, p // 2, 0)),
                pl.BlockSpec((None, win, 128), lambda p, *_: (m, 0, p // 2)),
                pl.BlockSpec((None, 128, win), lambda p, *_: (m, p // 2, 0)),
                pl.BlockSpec((win, 128), lambda p, *_: (0, 0)),
                pl.BlockSpec((128, nq), lambda p, *_: (0, 0)),
            ],
            out_specs=[
                pl.BlockSpec((128, nq), lambda p, *_: (p // 2, 0)),
                pl.BlockSpec((nq, 128), lambda p, *_: (0, p // 2)),
                pl.BlockSpec((1, 8, nq), lambda p, *_: (p, 0, 0)),
            ],
            scratch_shapes=[pltpu.VMEM((256, 2 * TILE), bf16)],
        ),
        compiler_params=pltpu.CompilerParams(vmem_limit_bytes=28 << 20),
        cost_estimate=pl.CostEstimate(flops=int(20 * 10**9 * 0.02), bytes_accessed=0, transcendentals=0),
        name="attend",
    )(info, qT, k, vT, kaug, qaugT)


def attend_back_kernel(info_ref, qT_ref, q_ref, k_ref, kT_ref, v_ref, doT_ref, do_ref, oT_ref, l_ref, kaug_ref, qaugT_ref,
                       dq_ref, dk_ref, dv_ref, dqT_ref, rhs_s, rhs_d, q_stk, do_stk, dk_acc, dv_acc):
    p_id = pl.program_id(0)
    off = pair_offset(info_ref)

    @pl.when(lax.rem(p_id, 2) == 0)
    def _():
        dqT_ref[...] = jnp.zeros_like(dqT_ref)
        dk_acc[...] = jnp.zeros_like(dk_acc)
        dv_acc[...] = jnp.zeros_like(dv_acc)

    for t in range(2):
        cols = slice(t * TILE, (t + 1) * TILE)
        masked_q = rows_masked(qT_ref[:, cols], off)
        masked_do = rows_masked(doT_ref[:, cols], off)
        lane_q = lanes_masked(q_ref[cols, :], off)
        lane_do = lanes_masked(do_ref[cols, :], off)
        for j in range(2):
            part = slice(j * TILE, (j + 1) * TILE)
            head = pl.ds(pl.multiple_of(off + j * HEAD_DIM, HEAD_DIM), HEAD_DIM)
            delta = jnp.sum(doT_ref[head, cols].astype(f32) * oT_ref[head, cols], axis=0, keepdims=True)
            total = l_ref[0, j:j + 1, cols] * (1.0 / C2)
            rowid = lax.broadcasted_iota(jnp.int32, (64, TILE), 0)
            lp, dp = split3(-total), split3(-delta)
            def pieces(parts):
                x = jnp.zeros((64, TILE), f32)
                for n in range(3):
                    x = jnp.where(rowid == n, parts[n].astype(f32), x)
                return x.astype(bf16)
            rhs_s[0:128, part] = masked_q[j]
            rhs_s[128:192, part] = qaugT_ref[0:64, cols]
            rhs_s[192:256, part] = pieces(lp)
            rhs_d[0:128, part] = masked_do[j]
            rhs_d[128:192, part] = jnp.zeros((64, TILE), bf16)
            rhs_d[192:256, part] = pieces(dp)
            q_stk[part, :] = lane_q[j]
            do_stk[part, :] = lane_do[j]
        start = info_ref[1 + t]
        need = info_ref[3 + t]

        def block(first, size):
            def step(i, carry):
                row = pl.multiple_of(first + i * size, 128)
                rows = pl.ds(row, size)
                aug = kaug_ref[rows, :]
                lhs_k = jnp.concatenate([k_ref[rows, :], aug], axis=1)
                lhs_v = jnp.concatenate([v_ref[rows, :], aug], axis=1)
                out, dv, dk = [], dv_acc[rows, :], dk_acc[rows, :]
                for j in range(2):
                    part = slice(j * TILE, (j + 1) * TILE)
                    s = jnp.dot(lhs_k, rhs_s[:, part], preferred_element_type=f32)
                    dp = jnp.dot(lhs_v, rhs_d[:, part], preferred_element_type=f32)
                    p = jnp.exp2(s * C2)
                    ds = (p * dp).astype(bf16)
                    dv = dv + jnp.dot(p.astype(bf16), do_stk[part, :], preferred_element_type=f32)
                    dk = dk + jnp.dot(ds, q_stk[part, :], preferred_element_type=f32)
                    kT = kT_ref[pl.ds(pl.multiple_of(off + j * HEAD_DIM, HEAD_DIM), HEAD_DIM), rows]
                    out.append(carry[j] + jnp.dot(kT, ds, preferred_element_type=f32))
                dv_acc[rows, :] = dv
                dk_acc[rows, :] = dk
                return tuple(out)
            return step

        def finish(dqs):
            for j in range(2):
                dqT_ref[pl.ds(pl.multiple_of(off + j * HEAD_DIM, HEAD_DIM), HEAD_DIM), cols] = dqs[j] * SCALE

        init = tuple(jnp.zeros((HEAD_DIM, TILE), f32) for _ in range(2))

        longs = lax.div(need, LONG)
        state = lax.fori_loop(0, longs, block(start, LONG), init)
        finish(lax.fori_loop(0, lax.div(need - longs * LONG, SHORT), block(start + longs * LONG, SHORT), state))
    @pl.when((lax.rem(p_id, 2) == 1) | (p_id == PAIRS - 1))
    def _():
        dq_ref[...] = dqT_ref[...].T.astype(bf16)
        dk_ref[...] = (dk_acc[...] * SCALE).astype(bf16)
        dv_ref[...] = dv_acc[...].astype(bf16)


def attend_back(m, info, qT, q, k, kT, v, doT, do, oT, lse, kaug, qaugT):
    win, nq = k.shape[1], qT.shape[2]
    qT, q, k, kT, v, doT, do = stay(qT, q, k, kT, v, doT, do)
    wide = pl.BlockSpec((128, nq), lambda p, *_: (p // 2, 0))
    tall = pl.BlockSpec((nq, 128), lambda p, *_: (0, p // 2))
    keys = pl.BlockSpec((win, 128), lambda p, *_: (0, p // 2))
    wide_m = pl.BlockSpec((None, 128, nq), lambda p, *_: (m, p // 2, 0))
    tall_m = pl.BlockSpec((None, nq, 128), lambda p, *_: (m, 0, p // 2))
    keys_m = pl.BlockSpec((None, win, 128), lambda p, *_: (m, 0, p // 2))
    return pl.pallas_call(
        attend_back_kernel,
        out_shape=tuple(pltpu.MemorySpace.VMEM(d, bf16) for d in ((nq, 384), (win, 384), (win, 384))),
        grid_spec=pltpu.PrefetchScalarGridSpec(
            num_scalar_prefetch=1, grid=(PAIRS,),
            in_specs=[wide_m, tall_m, keys_m, pl.BlockSpec((None, 128, win), lambda p, *_: (m, p // 2, 0)), keys_m,
                      pl.BlockSpec((128, nq), lambda p, *_: (p // 2, m)), pl.BlockSpec((nq, 128), lambda p, *_: (m, p // 2)), wide,
                      pl.BlockSpec((1, 8, nq), lambda p, *_: (p, 0, 0)),
                      pl.BlockSpec((win, 128), lambda p, *_: (0, 0)), pl.BlockSpec((128, nq), lambda p, *_: (0, 0))],
            out_specs=[tall, keys, keys],
            scratch_shapes=[pltpu.VMEM((128, nq), f32), pltpu.VMEM((256, 2 * TILE), bf16), pltpu.VMEM((256, 2 * TILE), bf16),
                            pltpu.VMEM((2 * TILE, 128), bf16), pltpu.VMEM((2 * TILE, 128), bf16),
                            pltpu.VMEM((win, 128), f32), pltpu.VMEM((win, 128), f32)],
        ),
        compiler_params=pltpu.CompilerParams(vmem_limit_bytes=32 << 20),
        cost_estimate=pl.CostEstimate(flops=int(40 * 10**9 * 0.02), bytes_accessed=0, transcendentals=0),
        name="attend_back",
    )(info, qT, q, k, kT, v, doT, do, oT, lse, kaug, qaugT)


def moments(x):
    centred = x - jnp.mean(x, axis=-1, keepdims=True)
    r = lax.rsqrt(jnp.mean(centred * centred, axis=-1, keepdims=True) + EPSILON)
    return centred * r, r


def norm_back(grad, n, r, gain):
    e = grad * gain
    return r * (e - jnp.mean(e, axis=-1, keepdims=True) - n * jnp.mean(e * n, axis=-1, keepdims=True))


def call(kernel, out_shape, name, flops=10**9, limit=48, **spec):
    return pl.pallas_call(
        kernel, out_shape=out_shape, name=name,
        compiler_params=pltpu.CompilerParams(vmem_limit_bytes=limit << 20),
        cost_estimate=pl.CostEstimate(flops=int(flops * 0.02), bytes_accessed=0, transcendentals=0), **spec)


def shape(*dims, dtype=bf16):
    return jax.ShapeDtypeStruct(dims, dtype)


def far(*dims, dtype=bf16):
    return pltpu.MemorySpace.HBM(dims, dtype)


def stay(*arrays):
    return [pltpu.with_memory_space_constraint(a, pltpu.MemorySpace.HBM) for a in arrays]


def scalar_first(grid, in_specs, out_specs, scratch=()):
    return dict(grid_spec=pltpu.PrefetchScalarGridSpec(
        num_scalar_prefetch=1, grid=grid, in_specs=in_specs, out_specs=out_specs, scratch_shapes=list(scratch)))


def full(*dims):
    return pl.BlockSpec(dims, lambda *_: (0,) * len(dims))


def pack_heads_kernel(core_ref, qkv_ref, vec_ref, heads_ref):
    for part in range(3):
        near = pl.ds(pl.multiple_of(640 * part + 256 * core_ref[0], 128), 256)
        heads_ref[:, 384 * part:384 * part + 256] = qkv_ref[:, near]
        heads_ref[:, 384 * part + 256:384 * (part + 1)] = qkv_ref[:, 640 * part + 512:640 * (part + 1)]
    heads_ref[:, 1152:1280] = vec_ref[...]


def pack_heads(core, w_qkv, vectors):
    return call(pack_heads_kernel, shape(160, 1280), "pack_heads", 10**6, 8, **scalar_first(
        (1,), [full(160, 1920), full(160, 128)], full(160, 1280)))(core, w_qkv, vectors)


def turn_kernel(vec_ref, rows_ref):
    rows_ref[...] = vec_ref[...].astype(f32).T[:16]


def vector_rows(heads):
    return call(turn_kernel, shape(16, 640, dtype=f32), "vector_rows", 10**12, 8, grid=(1,),
                in_specs=[pl.BlockSpec((640, 128), lambda i: (0, 9))], out_specs=full(16, 640))(*stay(heads))


def pack_feed_kernel(core_ref, out_ref, up_ref, down_ref, feed_ref):
    core = core_ref[0]
    feed_ref[:, 5120:5760] = out_ref[...]
    for f in range(4):
        feed_ref[:, 640 * f:640 * (f + 1)] = up_ref[:, pl.ds(pl.multiple_of(1280 * f + 640 * core, 128), 640)]
        feed_ref[:, 2560 + 640 * f:2560 + 640 * (f + 1)] = down_ref[pl.ds(pl.multiple_of(640 * core + 160 * f, 32), 160), :]


def pack_feed(core, w_out, w_up, w_down):
    return call(pack_feed_kernel, far(160, 5760), "pack_feed", 10**6, 16, **scalar_first(
        (1,), [full(160, 640), full(160, 5120), full(1280, 640)], full(160, 5760)))(core, *stay(w_out, w_up, w_down))


def rows_in_order(core, mine_ref, theirs_ref, x_ref):
    for c, (first, second) in enumerate(((mine_ref, theirs_ref), (theirs_ref, mine_ref))):
        @pl.when(core == c)
        def _():
            x_ref[0:256, :], x_ref[256:512, :] = first[...], second[...]


def normal_kernel(tok_ref, n_ref):
    for m in range(2):
        n_ref[m] = moments(tok_ref[m].astype(f32))[0].astype(bf16)


def normal_rows(tok):
    return call(normal_kernel, shape(2, 256, 640), "normal_rows", 10**6, 8, grid=(1,), in_specs=[full(2, 256, 640)], out_specs=full(2, 256, 640))(tok)


def project_kernel(chips, place_ref, *refs):
    n = len(chips)
    own_refs, other_refs = refs[:n], refs[n:2 * n]
    vec_ref, w_ref = refs[2 * n:2 * n + 2]
    k_ref, v_ref, kT_ref, vT_ref = refs[-6 - 2 * (n == 3):][:4]
    x_ref, hid_ref = refs[-2:]
    m, step = pl.program_id(0), pl.program_id(1)
    block = sum(jnp.where(step == i, chip, 0) for i, chip in enumerate(chips))
    needed = (block >= place_ref[1 + 2 * m]) & (block < place_ref[2 + 2 * m])

    @pl.when(jnp.logical_not(needed))
    def _():
        for ref in (k_ref, v_ref, kT_ref, vT_ref):
            ref[...] = jnp.zeros_like(ref)

    @pl.when(needed)
    def _():
        for j in range(n):
            @pl.when(step == j)
            def _():
                rows_in_order(place_ref[0], own_refs[j].at[m], other_refs[j].at[m], x_ref)

        hidden = (x_ref[...].astype(f32) * vec_ref[0:1, :] + vec_ref[1:2, :]).astype(bf16)
        hid_ref[...] = hidden
        kv = jnp.dot(hidden, w_ref[:, 384:], preferred_element_type=f32)
        low = kv.astype(bf16)
        k_ref[0] = low[:, :384]
        v_ref[0] = low[:, 384:]
        turned = kv.T.astype(bf16)
        kT_ref[0] = turned[:384]
        vT_ref[0] = turned[384:]

    if n == 3:
        q_ref, qT_ref = refs[-4:-2]

        @pl.when(step == 1)
        def _():
            q = jnp.dot(hid_ref[...], w_ref[:, :384], preferred_element_type=f32)
            q_ref[0] = q.astype(bf16)
            qT_ref[0] = q.T.astype(bf16)


def project(chips, place, own, other, vec, w, earlier=()):
    n = len(chips)
    chip = (lambda b: b + 1) if n == 3 else (lambda b: 4 * b)
    tall = pl.BlockSpec((1, 512, 384), lambda m, b, *_: (m, chip(b), 0))
    wide = pl.BlockSpec((1, 384, 512), lambda m, b, *_: (m, 0, chip(b)))
    shapes = [far(2, 2560, 384), far(2, 2560, 384), far(2, 384, 2560), far(2, 384, 2560)]
    specs = [tall, tall, wide, wide]
    if n == 3:
        shapes += [far(2, 512, 384), far(2, 384, 512)]
        specs += [pl.BlockSpec((1, 512, 384), lambda m, *_: (m, 0, 0)), pl.BlockSpec((1, 384, 512), lambda m, *_: (m, 0, 0))]
    own, other = [own[c] for c in chips], [other[c] for c in chips]
    return call(
        lambda *refs: project_kernel(chips, *refs), shapes, "project", 5 * 10**9, 28,
        input_output_aliases={2 * n + 3 + i: i for i in range(len(earlier))}, **scalar_first(
            (2, n), [full(2, 256, 640)] * (2 * n) + [full(16, 640), full(640, 1152)] + [pl.BlockSpec(memory_space=pl.ANY)] * len(earlier),
            specs, [pltpu.VMEM((512, 640), bf16), pltpu.VMEM((512, 640), bf16)]))(place, *own, *other, *stay(vec, w), *earlier)


def heads_joined(core, mine, theirs):
    first, second = (jnp.where(core == 0, a, b) for a, b in ((mine, theirs), (theirs, mine)))
    return jnp.concatenate([first[:, :256], second[:, :256], first[:, 256:] + second[:, 256:]], axis=1)


def middle_kernel(core_ref, w_ref, low0_ref, low1_ref, theirs_ref, tok_ref, tok2_ref, vec_ref, mid_ref, hid_ref, hid2_ref):
    core = core_ref[0]
    for m, low_ref in enumerate((low0_ref, low1_ref)):
        attended = heads_joined(core, low_ref[...].astype(f32), theirs_ref[m].astype(f32)).astype(bf16)
        branch = jnp.dot(attended, w_ref[...], preferred_element_type=f32)
        mine = jnp.where(core == 0, branch[:256], branch[256:]) + tok_ref[m].astype(f32)
        theirs = jnp.where(core == 0, branch[256:], branch[:256]) + tok2_ref[m].astype(f32)
        part = slice(256 * m, 256 * (m + 1))
        mid_ref[part, :] = mine
        hid_ref[part, :] = (moments(mine)[0] * vec_ref[2:3, :] + vec_ref[3:4, :]).astype(bf16)
        hid2_ref[part, :] = (moments(theirs)[0] * vec_ref[2:3, :] + vec_ref[3:4, :]).astype(bf16)


W_OUT = pl.BlockSpec((640, 640), lambda *_: (0, 8))


def middle_step(core, weights, *args):
    return call(middle_kernel, (far(512, 640, dtype=f32), far(512, 640), far(512, 640)), "middle", 10**9, 20, **scalar_first(
        (1,), [W_OUT] + [full(*a.shape) for a in args], [full(512, 640)] * 3))(core, *stay(weights), *args[:-1], *stay(args[-1]))


def feed_kernel(h_ref, h2_ref, cot_ref, cot2_ref, up_ref, down_ref, mine_ref, theirs_ref, g_out_ref, h, cot, hT, cT, out, dh, g_ref, left):
    chunk = pl.program_id(0)

    def leaving(number):
        up = (slice(None), pl.ds(4 * number, 4))
        down = (pl.ds(2 * number, 2), pl.ds(8, 8))
        return [pltpu.make_async_copy(g_ref.at[part], g_out_ref.at[part], left.at[number, i]) for i, part in enumerate((up, down))]

    @pl.when(chunk == 0)
    def _():
        h[0:512, :], h[512:1024, :] = h_ref[...], h2_ref[...]
        cot[0:512, :], cot[512:1024, :] = cot_ref[...], cot2_ref[...]
        hT[...] = h[...].astype(f32).T.astype(bf16)
        cT[...] = cot[...].astype(f32).T.astype(bf16)
        out[...] = jnp.zeros_like(out)
        dh[...] = jnp.zeros_like(dh)

    up_w = up_ref[...]
    down_w = jnp.concatenate([down_ref[160 * y:160 * (y + 1), 640 * i:640 * (i + 1)] for y in range(2) for i in range(4)], axis=0)
    acts, d_ups = [], []
    for t in range(4):
        rows = slice(256 * t, 256 * (t + 1))
        u = jnp.dot(h[rows, :], up_w, preferred_element_type=f32)
        d_act = lax.dot_general(cot[rows, :], down_w, NT, preferred_element_type=f32)
        cdf = 0.5 * (1.0 + lax.erf(u * (2.0 ** -0.5)))
        pdf = jnp.exp(u * u * -0.5) * ((2.0 * math.pi) ** -0.5)
        act = (u * cdf).astype(bf16)
        d_up = (d_act * (cdf + u * pdf)).astype(bf16)
        out[rows, :] += jnp.dot(act, down_w, preferred_element_type=f32)
        dh[rows, :] += lax.dot_general(d_up, up_w, NT, preferred_element_type=f32)
        acts.append(act)
        d_ups.append(d_up)
    g_up = jnp.dot(hT[...], jnp.concatenate(d_ups, axis=0), preferred_element_type=f32).astype(bf16)
    g_down = jnp.dot(cT[...], jnp.concatenate(acts, axis=0), preferred_element_type=f32).T.astype(bf16)
    for f in range(2):
        for y in range(4):
            for i in range(2):
                g_ref[y, 4 * chunk + 2 * f + i] = g_up[160 * y + 80 * i:160 * y + 80 * (i + 1), 640 * f:640 * (f + 1)]
        for i in range(8):
            g_ref[2 * chunk + f, 8 + i] = g_down[640 * f + 80 * i:640 * f + 80 * (i + 1)]

    for number in range(2):
        @pl.when(chunk == number)
        def _():
            for copy in leaving(number):
                copy.start()

    @pl.when(chunk == 1)
    def _():
        mine_ref[0], mine_ref[1] = out[0:512, :].astype(bf16), dh[0:512, :].astype(bf16)
        theirs_ref[0], theirs_ref[1] = out[512:1024, :].astype(bf16), dh[512:1024, :].astype(bf16)
        for number in range(2):
            for copy in leaving(number):
                copy.wait()


def feed_forward(h, h2, cot, cot2, weights):
    return call(
        feed_kernel,
        (far(2, 512, 640), far(2, 512, 640), far(4, 16, 80, 640)),
        "feed_forward", 30 * 10**9, 52, grid=(2,),
        in_specs=[full(512, 640)] * 4 + [pl.BlockSpec((640, 1280), lambda f: (0, f)), pl.BlockSpec((320, 2560), lambda f: (f, 1))],
        out_specs=[full(2, 512, 640), full(2, 512, 640), pl.BlockSpec(memory_space=pl.ANY)],
        scratch_shapes=[pltpu.VMEM((1024, 640), bf16), pltpu.VMEM((1024, 640), bf16), pltpu.VMEM((640, 1024), bf16), pltpu.VMEM((640, 1024), bf16),
                        pltpu.VMEM((1024, 640), f32), pltpu.VMEM((1024, 640), f32), pltpu.VMEM((4, 16, 80, 640), bf16), pltpu.SemaphoreType.DMA((2, 2))],
    )(*stay(h, h2, cot), cot2, *stay(weights, weights))


def after_kernel(mid_ref, mine_ref, theirs_ref, cot_ref, vec_ref, block_ref, grad_ref, branch_ref, g_ref):
    @pl.when(pl.program_id(0) == 0)
    def _():
        g_ref[...] = jnp.zeros_like(g_ref)

    middle = mid_ref[...]
    block_ref[...] = (middle + mine_ref[0].astype(f32) + theirs_ref[0].astype(f32)).astype(bf16)
    d_hidden = mine_ref[1].astype(f32) + theirs_ref[1].astype(f32)
    n, r = moments(middle)
    g_ref[0:1, :] += jnp.sum(d_hidden * n, axis=0, keepdims=True)
    g_ref[1:2, :] += jnp.sum(d_hidden, axis=0, keepdims=True)
    grad = cot_ref[...].astype(f32) + norm_back(d_hidden, n, r, vec_ref[2:3, :])
    grad_ref[...] = grad
    branch_ref[...] = grad.astype(bf16)


def after_feed(*args):
    rows, pair = pl.BlockSpec((128, 640), lambda i: (i, 0)), pl.BlockSpec((2, 128, 640), lambda i: (0, i, 0))
    return call(
        after_kernel, (far(512, 640), far(512, 640, dtype=f32), shape(512, 640), shape(8, 640, dtype=f32)), "after_feed", 10**9, 16,
        grid=(4,), in_specs=[rows, pair, pair, rows, full(16, 640)], out_specs=[rows, rows, rows, full(8, 640)])(*stay(args[0], args[1]), args[2], *stay(args[3], args[4]))


def branch_kernel(core_ref, own_ref, their_ref, w_ref, low0_ref, low1_ref, theirs_ref, do_ref, doT_ref, g_ref):
    core = core_ref[0]
    w = jnp.concatenate([w_ref[pl.ds(pl.multiple_of(256 * core, 256), 256), :], w_ref[512:640, :]], axis=0)
    g = jnp.zeros((640, 384), f32)
    for m in range(2):
        part = slice(256 * m, 256 * (m + 1))
        mine, theirs = own_ref[part, :].astype(f32), their_ref[part, :].astype(f32)
        branch = jnp.concatenate([jnp.where(core == 0, mine, theirs), jnp.where(core == 0, theirs, mine)], axis=0)
        kept = jnp.where(core == 0, branch[:, :384], branch[:, 256:]).astype(bf16)
        branch = branch.astype(bf16)
        rows = slice(512 * m, 512 * (m + 1))
        do = lax.dot_general(branch, w, NT, preferred_element_type=f32)
        do_ref[rows, :] = do.astype(bf16)
        doT_ref[:, rows] = do.T.astype(bf16)
        attended = heads_joined(core, (low0_ref, low1_ref)[m][...].astype(f32), theirs_ref[m].astype(f32))
        g = g + jnp.dot(attended.T.astype(bf16), kept, preferred_element_type=f32)
    g_ref[...] = g.astype(bf16)


def branch_step(core, own, their, weights, *args):
    return call(
        branch_kernel, (far(1024, 384), far(384, 1024), shape(640, 384)), "branch", 10**9, 24, **scalar_first(
            (1,), [full(512, 640)] * 2 + [W_OUT] + [full(*a.shape) for a in args], [full(1024, 384), full(384, 1024), full(640, 384)]))(
                core, own, their, *stay(weights), *args)


def near_by(*arrays):
    return [pltpu.with_memory_space_constraint(a, pltpu.MemorySpace.VMEM) for a in arrays]


def project_back_kernel(place_ref, *refs):
    own_refs, other_refs = refs[:5], refs[5:10]
    (vec_ref, w_ref, dq0_ref, dq1_ref, dk0_ref, dk1_ref, dv0_ref, dv1_ref, g_out_ref, g_two_ref,
     mine_ref, theirs_ref, tail_ref, n_ref, d_kv, d_q, d_hid, g_ref, g_vec, slots, arrived) = refs[10:]
    step, core = pl.program_id(0), place_ref[0]
    block, second = lax.rem(step, 5), lax.div(step, 5)
    inside = lambda j, m: (j >= place_ref[1 + 2 * m]) & (j < place_ref[2 + 2 * m])
    needed = inside(block, second)

    def copies(j, m, slot):
        return [pltpu.make_async_copy(refs_of[j].at[m], slots.at[slot, i], arrived.at[slot, i]) for i, refs_of in enumerate((own_refs, other_refs))]

    @pl.when(step == 0)
    def _():
        for m in range(2):
            for j in range(5):
                @pl.when(inside(j, m))
                def _():
                    for copy in copies(j, m, 5 * m + j):
                        copy.start()
        g_ref[...] = jnp.zeros_like(g_ref)
        g_vec[...] = jnp.zeros_like(g_vec)
        g_vec[2:4, :] = g_two_ref[0:2, :]

    @pl.when(jnp.logical_not(needed))
    def _():
        mine_ref[...] = jnp.zeros_like(mine_ref)
        theirs_ref[...] = jnp.zeros_like(theirs_ref)

    @pl.when(needed)
    def _():
        for copy in copies(0, 0, step):
            copy.wait()
        rows_in_order(core, slots.at[step, 0], slots.at[step, 1], n_ref)

    for m, (dq, dk, dv) in enumerate(((dq0_ref, dk0_ref, dv0_ref), (dq1_ref, dk1_ref, dv1_ref))):
        @pl.when(needed & (second == m))
        def _():
            rows = pl.ds(pl.multiple_of(block * 512, 512), 512)
            d_kv[:, :384], d_kv[:, 384:] = dk[rows, :], dv[rows, :]
            d_q[...] = dq[...]

    @pl.when(needed)
    def _():
        n = n_ref[...].astype(f32)
        hiddenT = (n * vec_ref[0:1, :] + vec_ref[1:2, :]).T.astype(bf16)
        d_hid[...] = lax.dot_general(d_kv[...], w_ref[:, 384:1152], NT, preferred_element_type=f32)
        g_ref[:, 384:] += jnp.dot(hiddenT, d_kv[...], preferred_element_type=f32)

        @pl.when(block == 2)
        def _():
            g_ref[:, :384] += jnp.dot(hiddenT, d_q[...], preferred_element_type=f32)
            d_hid[...] += lax.dot_general(d_q[...], w_ref[:, :384], NT, preferred_element_type=f32)

        dh = d_hid[...]
        low = dh.astype(bf16)
        for c, (first, other) in enumerate(((mine_ref, theirs_ref), (theirs_ref, mine_ref))):
            @pl.when(core == c)
            def _():
                first[0, 0], other[0, 0] = low[:256], low[256:]
        g_vec[0:1, :] += jnp.sum(dh * n, axis=0, keepdims=True)
        g_vec[1:2, :] += jnp.sum(dh, axis=0, keepdims=True)

    @pl.when(step == 9)
    def _():
        turned = g_vec[...].T
        lane = lax.broadcasted_iota(jnp.int32, (640, 128), 1) - 64 * (1 - core)
        spare = g_ref[:, 256:384]
        for i in range(4):
            spare = jnp.where(lane == i, turned[:, i:i + 1], spare)
        g_ref[:, 256:384] = spare
        for y in range(4):
            for z in range(4):
                rows = slice(160 * y + 40 * z, 160 * y + 40 * (z + 1))
                for x in range(3):
                    tail_ref[16 * y + 4 * z + x] = g_ref[rows, 384 * x:384 * (x + 1)].astype(bf16)
                tail_ref[16 * y + 4 * z + 3] = g_out_ref[rows, :].astype(bf16)


def project_back(place, own, other, vec, w, dq, dk, dv, g_out, g_two):
    here = pl.BlockSpec(memory_space=pltpu.VMEM)
    part = pl.BlockSpec((1, 1, 256, 640), lambda b, *_: (lax.rem(b, 5), b // 5, 0, 0))
    return call(
        project_back_kernel, (far(5, 2, 256, 640), far(5, 2, 256, 640), far(64, 40, 384)), "project_back", 10**10, 30, **scalar_first(
            (10,), [pl.BlockSpec(memory_space=pl.ANY)] * 10 + [here] * 10, [part, part, full(64, 40, 384)],
            [pltpu.VMEM((512, 640), bf16), pltpu.VMEM((512, 768), bf16), pltpu.VMEM((512, 384), bf16),
             pltpu.VMEM((512, 640), f32), pltpu.VMEM((640, 1152), f32), pltpu.VMEM((8, 640), f32),
             pltpu.VMEM((10, 2, 256, 640), bf16), pltpu.SemaphoreType.DMA((10, 2))]))(
                 place, *stay(*own, *other), *near_by(vec, w, *dq, *dk, *dv, g_out, g_two))


def in_core_order(core_ref, mine, theirs):
    core, mine, theirs = core_ref[0], mine.astype(f32), theirs.astype(f32)
    return jnp.where(core == 0, mine, theirs), jnp.where(core == 0, theirs, mine)


def final_feed_kernel(core_ref, mine_ref, theirs_ref, up_ref, down_ref):
    for i in range(16):
        for c, piece in enumerate(in_core_order(core_ref, mine_ref[i], theirs_ref[i])):
            if i < 8:
                base = 1280 * (i // 2) + 640 * c
                up_ref[80 * (i % 2):80 * (i % 2 + 1), base:base + 640] = piece
            else:
                base = 640 * c + 80 * (i - 8)
                down_ref[base:base + 80, :] = piece


def final_feed(core, mine, theirs):
    return call(final_feed_kernel, (shape(160, 5120, dtype=f32), shape(1280, 640, dtype=f32)), "final_feed", 10**6, 32, **scalar_first(
        (1,), [full(16, 80, 640)] * 2, [full(160, 5120), full(1280, 640)]))(core, mine, theirs)


def final_heads_kernel(core_ref, mine_ref, theirs_ref, qkv_ref, out_ref, vec_ref):
    lane = lax.broadcasted_iota(jnp.int32, (40, 128), 1)
    for z in range(4):
        rows = slice(40 * z, 40 * (z + 1))
        for x in range(4):
            a, b = in_core_order(core_ref, mine_ref[4 * z + x], theirs_ref[4 * z + x])
            if x < 3:
                last = jnp.where(lane < 64, a[:, 256:], b[:, 256:])
                qkv_ref[rows, 640 * x:640 * (x + 1)] = jnp.concatenate([a[:, :256], b[:, :256], last], axis=1)
            else:
                out_ref[rows, :] = jnp.concatenate([a, b[:, 128:]], axis=1)
            if x == 0:
                vec_ref[rows, :] = pltpu.roll(a[:, 256:], 64, 1) + b[:, 256:]


def final_heads(core, mine, theirs):
    return call(
        final_heads_kernel, (shape(160, 1920, dtype=f32), shape(160, 640, dtype=f32), shape(160, 128, dtype=f32)), "final_heads", 10**6, 16,
        **scalar_first((1,), [full(16, 40, 384)] * 2, [full(160, 1920), full(160, 640), full(160, 128)]))(core, mine, theirs)


def shifted(array, axis, by):
    devices = lax.axis_size(axis)
    return lax.ppermute(array, axis, [(i, (i + by) % devices) for i in range(devices)])


def passed_along(array, by):
    devices = lax.axis_size(("z", "x"))
    return lax.ppermute(array, ("z", "x"), [(i, i + by) for i in range(devices) if 0 <= i + by < devices])


def swapped(array):
    return lax.ppermute(array, "core", [(0, 1), (1, 0)])


def pick(array, index):
    return lax.dynamic_index_in_dim(array, index, 0, keepdims=False)


def gathered(array, axis):
    me, devices = lax.axis_index(axis), lax.axis_size(axis)
    out = jnp.zeros((devices,) + array.shape, array.dtype)
    out = lax.dynamic_update_index_in_dim(out, array, me, 0)
    for by in (1, devices - 1, 2):
        out = lax.dynamic_update_index_in_dim(out, shifted(array, axis, by), (me + devices - by) % devices, 0)
    return out


def window_info(length_row, chip, core, win, key_row=None):
    ends = jnp.cumsum(length_row)
    starts = ends - length_row
    key_ends = ends if key_row is None else jnp.cumsum(key_row)
    key_starts = starts if key_row is None else key_ends - key_row
    base = chip * 512 - 1024
    places = base + jnp.arange(win, dtype=jnp.int32)
    inside = (places[:, None] >= key_starts[None, :]) & (places[:, None] < key_ends[None, :])
    ones = jnp.broadcast_to(jnp.arange(64) < 3, (win, 64)).astype(bf16)
    key_rows = jnp.concatenate([jnp.where(inside, 0.0, -BIG).astype(bf16), ones], axis=1)
    own = chip * 512 + jnp.arange(512, dtype=jnp.int32)
    inside_q = (own[None, :] >= starts[:, None]) & (own[None, :] < ends[:, None])
    query_rows = jnp.concatenate([inside_q.astype(bf16), jnp.zeros((64, 512), bf16)], axis=0)
    info = [core]
    sizes = []
    for t in range(2):
        first = chip * 512 + t * TILE
        low = jnp.max(jnp.where(starts <= first, starts, 0)) - base
        high = jnp.min(jnp.where(ends > first + TILE - 1, ends, 1 << 30)) - base
        start = low // 128 * 128
        need = high - start
        size = (need + SHORT - 1) // SHORT * SHORT
        info.append(jnp.minimum(start, win - size))
        sizes.append(size)
    low = jnp.minimum(info[1], info[2]) // 512
    high = (jnp.maximum(info[1] + sizes[0], info[2] + sizes[1]) + 511) // 512
    return jnp.stack(info + sizes).astype(jnp.int32), key_rows, query_rows, [low, high]


def body(tokens, lengths, gain_one, bias_one, w_qkv, w_out, gain_two, bias_two, w_up, w_down, cotangent):
    core, chip = lax.axis_index("core"), lax.axis_index(("z", "x"))
    core_arg = core[None].astype(jnp.int32)
    tok, cot = tokens[:, 0], cotangent[:, 0].reshape(512, 640)
    together = lambda *arrays: lax.optimization_barrier(arrays)

    vectors = jnp.pad(jnp.stack([gain_one, bias_one, gain_two, bias_two], axis=1), ((0, 0), (0, 124)))
    heads, tok_sent = together(pack_heads(core_arg, w_qkv, vectors), tok)
    heads = lax.all_gather(heads, "batch", axis=0, tiled=True)
    vec = vector_rows(heads)
    normal = normal_rows(tok_sent)
    before, after, normal_other, tok_other = passed_along(normal, 1), passed_along(normal, -1), swapped(normal), swapped(tok)
    feed_pack = pack_feed(core_arg, w_out, w_up, w_down)
    heads, feed_pack, key_row = together(heads, feed_pack, lengths[1, 0])
    feed_weights = lax.all_gather(feed_pack, "batch", axis=0, tiled=True)
    windows = [window_info(lengths[0, 0], chip, core, 2560), window_info(lengths[1, 0], chip, core, 2560, key_row)]
    place = jnp.stack([core] + windows[0][3] + windows[1][3]).astype(jnp.int32)
    heads, vec, before, after, normal_other, tok_other, place, windows = together(
        heads, vec, before, after, normal_other, tok_other, place, windows)
    own = [passed_along(before, 1), before, normal, after, passed_along(after, -1)]
    other = [None, swapped(before), normal_other, swapped(after), None]
    *near_parts, q, qT = project((1, 2, 3), place, own, other, vec, heads)
    own[0], own[4], near_parts = together(own[0], own[4], near_parts)
    other[0], other[4] = swapped(own[0]), swapped(own[4])
    k, v, kT, vT = project((0, 4), place, own, other, vec, heads, near_parts)
    (oT0, low0, lse0), (oT1, low1, lse1) = (
        attend(m, info, qT, k, vT, key_rows, query_rows) for m, (info, key_rows, query_rows, _) in enumerate(windows))

    theirs = swapped(jnp.stack([low0, low1]))
    middle, hidden_two, hidden_other = middle_step(core_arg, feed_weights, low0, low1, theirs, tok, tok_other, vec)
    mine, partial, feed_grads = feed_forward(hidden_two, hidden_other, cot, swapped(cot), feed_weights)
    feed_grads = lax.all_to_all(feed_grads.reshape(64, 80, 640), ("batch", "z", "x"), 0, 0, tiled=True)
    block_out, grad_middle, branch, g_two = after_feed(middle, mine, swapped(partial), cot, vec)

    do, doT, g_out = branch_step(core_arg, branch, swapped(branch), feed_weights, low0, low1, theirs)
    dq, dk, dv = zip(*(
        attend_back(m, info, qT, q, k, kT, v, doT, do, oT, lse, key_rows, query_rows)
        for m, ((info, key_rows, query_rows, _), oT, lse) in enumerate(zip(windows, (oT0, oT1), (lse0, lse1)))))
    mine, theirs, tail = project_back(place, own, other, vec, heads, dq, dk, dv, g_out, g_two)
    feed_grads, mine, theirs, tail = together(feed_grads, mine, theirs, tail)

    feed = jnp.sum(feed_grads.astype(f32), axis=0).astype(bf16)
    tail = lax.all_to_all(tail, ("batch", "z", "x"), 0, 0, tiled=True)
    feed = lax.all_gather(feed, ("z", "x"), axis=0, tiled=True).reshape(16, 80, 640)
    theirs = swapped(theirs)
    sums = [mine[j].astype(f32) + theirs[j].astype(f32) for j in range(5)]
    right, left = passed_along(sums[4].astype(bf16), 1), passed_along(sums[0].astype(bf16), -1)
    tail, right, left = together(tail, right, left)
    right, left = (right.astype(f32) + sums[3]).astype(bf16), (left.astype(f32) + sums[1]).astype(bf16)
    tail, right, left = together(jnp.sum(tail.astype(f32), axis=0).astype(bf16), right, left)
    right, left = passed_along(right, 1), passed_along(left, -1)
    tail = gathered(tail, "x").reshape(160, 384)
    tail = gathered(tail, "z").reshape(16, 40, 384)
    tail, right, left = together(tail, right, left)
    d_one = (sums[2] + right.astype(f32) + left.astype(f32)).reshape(512, 640)
    n_one, r_one = moments(tok.reshape(512, 640).astype(f32))
    grad_tokens = (grad_middle + norm_back(d_one, n_one, r_one, vec[0:1])).astype(bf16)
    tail, grad_tokens, feed = together(tail, grad_tokens, feed)
    grad_qkv, grad_out, spare = final_heads(core_arg, tail, swapped(tail))
    grad_up, grad_down = final_feed(core_arg, feed, swapped(feed))
    return (
        block_out.reshape(2, 1, 256, 640), grad_tokens.reshape(2, 1, 256, 640), spare[:, 0], spare[:, 1], grad_qkv, grad_out,
        spare[:, 2], spare[:, 3], grad_up, grad_down)


def solution(mesh):
    fine = Mesh(mesh.devices.reshape(4, 4, 4, 2), ("batch", "z", "x", "core"))
    rows = P(None, "batch", ("z", "x", "core"), None)
    one, two = P("batch"), P("batch", None)
    return jax.shard_map(
        body,
        mesh=fine,
        in_specs=(rows, P(None, "batch", None), one, one, two, two, one, one, two, two, rows),
        out_specs=(rows, rows, one, one, two, two, one, one, two, two),
        check_vma=False,
    )
```

```python
import math

import jax
import jax.numpy as jnp
from jax import lax
from jax.experimental import pallas as pl
from jax.experimental.pallas import tpu as pltpu
from jax.sharding import Mesh
from jax.sharding import PartitionSpec as P

HEAD_DIM = 32
SCALE = HEAD_DIM ** -0.5
LOG2E = math.log2(math.e)
C2 = SCALE * LOG2E
BIG = 1e30
TILE = 256
EPSILON = 1e-05
PAIRS = 5
SHORT, LONG = 384, 1152
f32, bf16 = jnp.float32, jnp.bfloat16
NT = (((1,), (1,)), ((), ()))


def pair_offset(info_ref):
    p = pl.program_id(0)
    sub = jnp.where(p == PAIRS - 1, info_ref[0], lax.rem(p, 2))
    return sub * (2 * HEAD_DIM)


def split3(v):
    a = v.astype(bf16)
    r = v - a.astype(f32)
    b = r.astype(bf16)
    d = (r - b.astype(f32)).astype(bf16)
    return a, b, d


def rows_masked(xT, off):
    row = lax.broadcasted_iota(jnp.int32, xT.shape, 0) - off
    xf = xT.astype(f32)
    return [jnp.where((row >= HEAD_DIM * j) & (row < HEAD_DIM * (j + 1)), xf, 0.0).astype(bf16) for j in range(2)]


def lanes_masked(x, off):
    lane = lax.broadcasted_iota(jnp.int32, x.shape, 1) - off
    xf = x.astype(f32)
    return [jnp.where((lane >= HEAD_DIM * j) & (lane < HEAD_DIM * (j + 1)), xf, 0.0).astype(bf16) for j in range(2)]


def attend_kernel(info_ref, qT_ref, k_ref, vT_ref, kaug_ref, qaugT_ref, oT_ref, o_ref, l_ref, rhs):
    off = pair_offset(info_ref)
    oT_ref[...] = jnp.where(lax.rem(pl.program_id(0), 2) == 0, 0.0, oT_ref[...])
    for t in range(2):
        cols = slice(t * TILE, (t + 1) * TILE)
        masked = rows_masked(qT_ref[:, cols], off)
        for j in range(2):
            rhs[0:128, j * TILE:(j + 1) * TILE] = masked[j]
            rhs[128:256, j * TILE:(j + 1) * TILE] = qaugT_ref[:, cols]
        start = info_ref[1 + t]
        need = info_ref[3 + t]

        def block(first, size):
            def step(i, carry):
                row = pl.multiple_of(first + i * size, 128)
                lhs = jnp.concatenate([k_ref[pl.ds(row, size), :], kaug_ref[pl.ds(row, size), :]], axis=1)
                raw = [jnp.dot(lhs, rhs[:, j * TILE:(j + 1) * TILE], preferred_element_type=f32) for j in range(2)]
                out = []
                for j in range(2):
                    m, l, o = carry[j]
                    s = raw[j] * C2
                    m_new = jnp.maximum(m, jnp.max(s, axis=0, keepdims=True))
                    alpha = jnp.exp2(m - m_new)
                    p = jnp.exp2(s - m_new)
                    vT = vT_ref[pl.ds(pl.multiple_of(off + j * HEAD_DIM, HEAD_DIM), HEAD_DIM), pl.ds(row, size)]
                    out.append((m_new, l * alpha + jnp.sum(p, axis=0, keepdims=True),
                                o * alpha + jnp.dot(vT, p.astype(bf16), preferred_element_type=f32)))
                return tuple(out)
            return step

        def finish(state):
            for j in range(2):
                m, l, o = state[j]
                oT_ref[pl.ds(pl.multiple_of(off + j * HEAD_DIM, HEAD_DIM), HEAD_DIM), cols] = o * (1.0 / l)
                l_ref[0, j:j + 1, cols] = m + jnp.log2(l)

        init = tuple((jnp.full((1, TILE), -1e38, f32), jnp.zeros((1, TILE), f32), jnp.zeros((HEAD_DIM, TILE), f32)) for _ in range(2))

        longs = lax.div(need, LONG)
        state = lax.fori_loop(0, longs, block(start, LONG), init)
        finish(lax.fori_loop(0, lax.div(need - longs * LONG, SHORT), block(start + longs * LONG, SHORT), state))

    o_ref[...] = oT_ref[...].T.astype(bf16)


def attend(m, info, qT, k, vT, kaug, qaugT):
    win, nq = k.shape[1], qT.shape[2]
    qT, k, vT = stay(qT, k, vT)
    return pl.pallas_call(
        attend_kernel,
        out_shape=(jax.ShapeDtypeStruct((384, nq), f32), jax.ShapeDtypeStruct((nq, 384), bf16), jax.ShapeDtypeStruct((PAIRS, 8, nq), f32)),
        grid_spec=pltpu.PrefetchScalarGridSpec(
            num_scalar_prefetch=1, grid=(PAIRS,),
            in_specs=[
                pl.BlockSpec((None, 128, nq), lambda p, *_: (m, p // 2, 0)),
                pl.BlockSpec((None, win, 128), lambda p, *_: (m, 0, p // 2)),
                pl.BlockSpec((None, 128, win), lambda p, *_: (m, p // 2, 0)),
                pl.BlockSpec((win, 128), lambda p, *_: (0, 0)),
                pl.BlockSpec((128, nq), lambda p, *_: (0, 0)),
            ],
            out_specs=[
                pl.BlockSpec((128, nq), lambda p, *_: (p // 2, 0)),
                pl.BlockSpec((nq, 128), lambda p, *_: (0, p // 2)),
                pl.BlockSpec((1, 8, nq), lambda p, *_: (p, 0, 0)),
            ],
            scratch_shapes=[pltpu.VMEM((256, 2 * TILE), bf16)],
        ),
        compiler_params=pltpu.CompilerParams(vmem_limit_bytes=28 << 20),
        cost_estimate=pl.CostEstimate(flops=int(20 * 10**9 * 0.02), bytes_accessed=0, transcendentals=0),
        name="attend",
    )(info, qT, k, vT, kaug, qaugT)


def attend_back_kernel(info_ref, qT_ref, q_ref, k_ref, kT_ref, v_ref, doT_ref, do_ref, oT_ref, l_ref, kaug_ref, qaugT_ref,
                       dq_ref, dk_ref, dv_ref, dqT_ref, rhs_s, rhs_d, q_stk, do_stk, dk_acc, dv_acc):
    p_id = pl.program_id(0)
    off = pair_offset(info_ref)

    @pl.when(lax.rem(p_id, 2) == 0)
    def _():
        dqT_ref[...] = jnp.zeros_like(dqT_ref)
        dk_acc[...] = jnp.zeros_like(dk_acc)
        dv_acc[...] = jnp.zeros_like(dv_acc)

    for t in range(2):
        cols = slice(t * TILE, (t + 1) * TILE)
        masked_q = rows_masked(qT_ref[:, cols], off)
        masked_do = rows_masked(doT_ref[:, cols], off)
        lane_q = lanes_masked(q_ref[cols, :], off)
        lane_do = lanes_masked(do_ref[cols, :], off)
        for j in range(2):
            part = slice(j * TILE, (j + 1) * TILE)
            head = pl.ds(pl.multiple_of(off + j * HEAD_DIM, HEAD_DIM), HEAD_DIM)
            delta = jnp.sum(doT_ref[head, cols].astype(f32) * oT_ref[head, cols], axis=0, keepdims=True)
            total = l_ref[0, j:j + 1, cols] * (1.0 / C2)
            rowid = lax.broadcasted_iota(jnp.int32, (64, TILE), 0)
            lp, dp = split3(-total), split3(-delta)
            def pieces(parts):
                x = jnp.zeros((64, TILE), f32)
                for n in range(3):
                    x = jnp.where(rowid == n, parts[n].astype(f32), x)
                return x.astype(bf16)
            rhs_s[0:128, part] = masked_q[j]
            rhs_s[128:192, part] = qaugT_ref[0:64, cols]
            rhs_s[192:256, part] = pieces(lp)
            rhs_d[0:128, part] = masked_do[j]
            rhs_d[128:192, part] = jnp.zeros((64, TILE), bf16)
            rhs_d[192:256, part] = pieces(dp)
            q_stk[part, :] = lane_q[j]
            do_stk[part, :] = lane_do[j]
        start = info_ref[1 + t]
        need = info_ref[3 + t]

        def block(first, size):
            def step(i, carry):
                row = pl.multiple_of(first + i * size, 128)
                rows = pl.ds(row, size)
                aug = kaug_ref[rows, :]
                lhs_k = jnp.concatenate([k_ref[rows, :], aug], axis=1)
                lhs_v = jnp.concatenate([v_ref[rows, :], aug], axis=1)
                out, dv, dk = [], dv_acc[rows, :], dk_acc[rows, :]
                for j in range(2):
                    part = slice(j * TILE, (j + 1) * TILE)
                    s = jnp.dot(lhs_k, rhs_s[:, part], preferred_element_type=f32)
                    dp = jnp.dot(lhs_v, rhs_d[:, part], preferred_element_type=f32)
                    p = jnp.exp2(s * C2)
                    ds = (p * dp).astype(bf16)
                    dv = dv + jnp.dot(p.astype(bf16), do_stk[part, :], preferred_element_type=f32)
                    dk = dk + jnp.dot(ds, q_stk[part, :], preferred_element_type=f32)
                    kT = kT_ref[pl.ds(pl.multiple_of(off + j * HEAD_DIM, HEAD_DIM), HEAD_DIM), rows]
                    out.append(carry[j] + jnp.dot(kT, ds, preferred_element_type=f32))
                dv_acc[rows, :] = dv
                dk_acc[rows, :] = dk
                return tuple(out)
            return step

        def finish(dqs):
            for j in range(2):
                dqT_ref[pl.ds(pl.multiple_of(off + j * HEAD_DIM, HEAD_DIM), HEAD_DIM), cols] = dqs[j] * SCALE

        init = tuple(jnp.zeros((HEAD_DIM, TILE), f32) for _ in range(2))

        longs = lax.div(need, LONG)
        state = lax.fori_loop(0, longs, block(start, LONG), init)
        finish(lax.fori_loop(0, lax.div(need - longs * LONG, SHORT), block(start + longs * LONG, SHORT), state))
    @pl.when((lax.rem(p_id, 2) == 1) | (p_id == PAIRS - 1))
    def _():
        dq_ref[...] = dqT_ref[...].T.astype(bf16)
        dk_ref[...] = (dk_acc[...] * SCALE).astype(bf16)
        dv_ref[...] = dv_acc[...].astype(bf16)


def attend_back(m, info, qT, q, k, kT, v, doT, do, oT, lse, kaug, qaugT):
    win, nq = k.shape[1], qT.shape[2]
    qT, q, k, kT, v, doT, do = stay(qT, q, k, kT, v, doT, do)
    wide = pl.BlockSpec((128, nq), lambda p, *_: (p // 2, 0))
    tall = pl.BlockSpec((nq, 128), lambda p, *_: (0, p // 2))
    keys = pl.BlockSpec((win, 128), lambda p, *_: (0, p // 2))
    wide_m = pl.BlockSpec((None, 128, nq), lambda p, *_: (m, p // 2, 0))
    tall_m = pl.BlockSpec((None, nq, 128), lambda p, *_: (m, 0, p // 2))
    keys_m = pl.BlockSpec((None, win, 128), lambda p, *_: (m, 0, p // 2))
    return pl.pallas_call(
        attend_back_kernel,
        out_shape=tuple(pltpu.MemorySpace.VMEM(d, bf16) for d in ((nq, 384), (win, 384), (win, 384))),
        grid_spec=pltpu.PrefetchScalarGridSpec(
            num_scalar_prefetch=1, grid=(PAIRS,),
            in_specs=[wide_m, tall_m, keys_m, pl.BlockSpec((None, 128, win), lambda p, *_: (m, p // 2, 0)), keys_m,
                      pl.BlockSpec((128, nq), lambda p, *_: (p // 2, m)), pl.BlockSpec((nq, 128), lambda p, *_: (m, p // 2)), wide,
                      pl.BlockSpec((1, 8, nq), lambda p, *_: (p, 0, 0)),
                      pl.BlockSpec((win, 128), lambda p, *_: (0, 0)), pl.BlockSpec((128, nq), lambda p, *_: (0, 0))],
            out_specs=[tall, keys, keys],
            scratch_shapes=[pltpu.VMEM((128, nq), f32), pltpu.VMEM((256, 2 * TILE), bf16), pltpu.VMEM((256, 2 * TILE), bf16),
                            pltpu.VMEM((2 * TILE, 128), bf16), pltpu.VMEM((2 * TILE, 128), bf16),
                            pltpu.VMEM((win, 128), f32), pltpu.VMEM((win, 128), f32)],
        ),
        compiler_params=pltpu.CompilerParams(vmem_limit_bytes=32 << 20),
        cost_estimate=pl.CostEstimate(flops=int(40 * 10**9 * 0.02), bytes_accessed=0, transcendentals=0),
        name="attend_back",
    )(info, qT, q, k, kT, v, doT, do, oT, lse, kaug, qaugT)


def moments(x):
    centred = x - jnp.mean(x, axis=-1, keepdims=True)
    r = lax.rsqrt(jnp.mean(centred * centred, axis=-1, keepdims=True) + EPSILON)
    return centred * r, r


def norm_back(grad, n, r, gain):
    e = grad * gain
    return r * (e - jnp.mean(e, axis=-1, keepdims=True) - n * jnp.mean(e * n, axis=-1, keepdims=True))


def call(kernel, out_shape, name, flops=10**9, limit=48, **spec):
    return pl.pallas_call(
        kernel, out_shape=out_shape, name=name,
        compiler_params=pltpu.CompilerParams(vmem_limit_bytes=limit << 20),
        cost_estimate=pl.CostEstimate(flops=int(flops * 0.02), bytes_accessed=0, transcendentals=0), **spec)


def shape(*dims, dtype=bf16):
    return jax.ShapeDtypeStruct(dims, dtype)


def far(*dims, dtype=bf16):
    return pltpu.MemorySpace.HBM(dims, dtype)


def stay(*arrays):
    return [pltpu.with_memory_space_constraint(a, pltpu.MemorySpace.HBM) for a in arrays]


def scalar_first(grid, in_specs, out_specs, scratch=()):
    return dict(grid_spec=pltpu.PrefetchScalarGridSpec(
        num_scalar_prefetch=1, grid=grid, in_specs=in_specs, out_specs=out_specs, scratch_shapes=list(scratch)))


def full(*dims):
    return pl.BlockSpec(dims, lambda *_: (0,) * len(dims))


def pack_heads_kernel(core_ref, qkv_ref, vec_ref, heads_ref):
    for part in range(3):
        near = pl.ds(pl.multiple_of(640 * part + 256 * core_ref[0], 128), 256)
        heads_ref[:, 384 * part:384 * part + 256] = qkv_ref[:, near]
        heads_ref[:, 384 * part + 256:384 * (part + 1)] = qkv_ref[:, 640 * part + 512:640 * (part + 1)]
    heads_ref[:, 1152:1280] = vec_ref[...]


def pack_heads(core, w_qkv, vectors):
    return call(pack_heads_kernel, shape(160, 1280), "pack_heads", 10**6, 8, **scalar_first(
        (1,), [full(160, 1920), full(160, 128)], full(160, 1280)))(core, w_qkv, vectors)


def turn_kernel(vec_ref, rows_ref):
    rows_ref[...] = vec_ref[...].astype(f32).T[:16]


def vector_rows(heads):
    return call(turn_kernel, shape(16, 640, dtype=f32), "vector_rows", 10**12, 8, grid=(1,),
                in_specs=[pl.BlockSpec((640, 128), lambda i: (0, 9))], out_specs=full(16, 640))(*stay(heads))


def pack_feed_kernel(core_ref, out_ref, up_ref, down_ref, feed_ref):
    core = core_ref[0]
    feed_ref[:, 5120:5760] = out_ref[...]
    for f in range(4):
        feed_ref[:, 640 * f:640 * (f + 1)] = up_ref[:, pl.ds(pl.multiple_of(1280 * f + 640 * core, 128), 640)]
        feed_ref[:, 2560 + 640 * f:2560 + 640 * (f + 1)] = down_ref[pl.ds(pl.multiple_of(640 * core + 160 * f, 32), 160), :]


def pack_feed(core, w_out, w_up, w_down):
    return call(pack_feed_kernel, far(160, 5760), "pack_feed", 10**6, 16, **scalar_first(
        (1,), [full(160, 640), full(160, 5120), full(1280, 640)], full(160, 5760)))(core, *stay(w_out, w_up, w_down))


def rows_in_order(core, mine_ref, theirs_ref, x_ref):
    for c, (first, second) in enumerate(((mine_ref, theirs_ref), (theirs_ref, mine_ref))):
        @pl.when(core == c)
        def _():
            x_ref[0:256, :], x_ref[256:512, :] = first[...], second[...]


def normal_kernel(tok_ref, n_ref):
    for m in range(2):
        n_ref[m] = moments(tok_ref[m].astype(f32))[0].astype(bf16)


def normal_rows(tok):
    return call(normal_kernel, shape(2, 256, 640), "normal_rows", 10**6, 8, grid=(1,), in_specs=[full(2, 256, 640)], out_specs=full(2, 256, 640))(tok)


def project_kernel(chips, place_ref, *refs):
    n = len(chips)
    own_refs, other_refs = refs[:n], refs[n:2 * n]
    vec_ref, w_ref = refs[2 * n:2 * n + 2]
    k_ref, v_ref, kT_ref, vT_ref = refs[-6 - 2 * (n == 3):][:4]
    x_ref, hid_ref = refs[-2:]
    m, step = pl.program_id(0), pl.program_id(1)
    block = sum(jnp.where(step == i, chip, 0) for i, chip in enumerate(chips))
    needed = (block >= place_ref[1 + 2 * m]) & (block < place_ref[2 + 2 * m])

    @pl.when(jnp.logical_not(needed))
    def _():
        for ref in (k_ref, v_ref, kT_ref, vT_ref):
            ref[...] = jnp.zeros_like(ref)

    @pl.when(needed)
    def _():
        for j in range(n):
            @pl.when(step == j)
            def _():
                rows_in_order(place_ref[0], own_refs[j].at[m], other_refs[j].at[m], x_ref)

        hidden = (x_ref[...].astype(f32) * vec_ref[0:1, :] + vec_ref[1:2, :]).astype(bf16)
        hid_ref[...] = hidden
        kv = jnp.dot(hidden, w_ref[:, 384:], preferred_element_type=f32)
        low = kv.astype(bf16)
        k_ref[0] = low[:, :384]
        v_ref[0] = low[:, 384:]
        turned = kv.T.astype(bf16)
        kT_ref[0] = turned[:384]
        vT_ref[0] = turned[384:]

    if n == 3:
        q_ref, qT_ref = refs[-4:-2]

        @pl.when(step == 1)
        def _():
            q = jnp.dot(hid_ref[...], w_ref[:, :384], preferred_element_type=f32)
            q_ref[0] = q.astype(bf16)
            qT_ref[0] = q.T.astype(bf16)


def project(chips, place, own, other, vec, w, earlier=()):
    n = len(chips)
    chip = (lambda b: b + 1) if n == 3 else (lambda b: 4 * b)
    tall = pl.BlockSpec((1, 512, 384), lambda m, b, *_: (m, chip(b), 0))
    wide = pl.BlockSpec((1, 384, 512), lambda m, b, *_: (m, 0, chip(b)))
    shapes = [far(2, 2560, 384), far(2, 2560, 384), far(2, 384, 2560), far(2, 384, 2560)]
    specs = [tall, tall, wide, wide]
    if n == 3:
        shapes += [far(2, 512, 384), far(2, 384, 512)]
        specs += [pl.BlockSpec((1, 512, 384), lambda m, *_: (m, 0, 0)), pl.BlockSpec((1, 384, 512), lambda m, *_: (m, 0, 0))]
    own, other = [own[c] for c in chips], [other[c] for c in chips]
    return call(
        lambda *refs: project_kernel(chips, *refs), shapes, "project", 5 * 10**9, 28,
        input_output_aliases={2 * n + 3 + i: i for i in range(len(earlier))}, **scalar_first(
            (2, n), [full(2, 256, 640)] * (2 * n) + [full(16, 640), full(640, 1152)] + [pl.BlockSpec(memory_space=pl.ANY)] * len(earlier),
            specs, [pltpu.VMEM((512, 640), bf16), pltpu.VMEM((512, 640), bf16)]))(place, *own, *other, *stay(vec, w), *earlier)


def heads_joined(core, mine, theirs):
    first, second = (jnp.where(core == 0, a, b) for a, b in ((mine, theirs), (theirs, mine)))
    return jnp.concatenate([first[:, :256], second[:, :256], first[:, 256:] + second[:, 256:]], axis=1)


def middle_kernel(core_ref, w_ref, low0_ref, low1_ref, theirs_ref, tok_ref, tok2_ref, vec_ref, mid_ref, hid_ref, hid2_ref):
    core = core_ref[0]
    for m, low_ref in enumerate((low0_ref, low1_ref)):
        attended = heads_joined(core, low_ref[...].astype(f32), theirs_ref[m].astype(f32)).astype(bf16)
        branch = jnp.dot(attended, w_ref[...], preferred_element_type=f32)
        mine = jnp.where(core == 0, branch[:256], branch[256:]) + tok_ref[m].astype(f32)
        theirs = jnp.where(core == 0, branch[256:], branch[:256]) + tok2_ref[m].astype(f32)
        part = slice(256 * m, 256 * (m + 1))
        mid_ref[part, :] = mine
        hid_ref[part, :] = (moments(mine)[0] * vec_ref[2:3, :] + vec_ref[3:4, :]).astype(bf16)
        hid2_ref[part, :] = (moments(theirs)[0] * vec_ref[2:3, :] + vec_ref[3:4, :]).astype(bf16)


W_OUT = pl.BlockSpec((640, 640), lambda *_: (0, 8))


def middle_step(core, weights, *args):
    return call(middle_kernel, (far(512, 640, dtype=f32), far(512, 640), far(512, 640)), "middle", 10**9, 20, **scalar_first(
        (1,), [W_OUT] + [full(*a.shape) for a in args], [full(512, 640)] * 3))(core, *stay(weights), *args[:-1], *stay(args[-1]))


def feed_kernel(h_ref, h2_ref, cot_ref, cot2_ref, up_ref, down_ref, mine_ref, theirs_ref, g_ref, h, cot, hT, cT, out, dh):
    chunk = pl.program_id(0)

    @pl.when(chunk == 0)
    def _():
        h[0:512, :], h[512:1024, :] = h_ref[...], h2_ref[...]
        cot[0:512, :], cot[512:1024, :] = cot_ref[...], cot2_ref[...]
        hT[...] = h[...].astype(f32).T.astype(bf16)
        cT[...] = cot[...].astype(f32).T.astype(bf16)
        out[...] = jnp.zeros_like(out)
        dh[...] = jnp.zeros_like(dh)

    up_w = up_ref[...]
    down_w = jnp.concatenate([down_ref[160 * y:160 * (y + 1), 640 * i:640 * (i + 1)] for y in range(2) for i in range(4)], axis=0)
    acts, d_ups = [], []
    for t in range(4):
        rows = slice(256 * t, 256 * (t + 1))
        u = jnp.dot(h[rows, :], up_w, preferred_element_type=f32)
        d_act = lax.dot_general(cot[rows, :], down_w, NT, preferred_element_type=f32)
        cdf = 0.5 * (1.0 + lax.erf(u * (2.0 ** -0.5)))
        pdf = jnp.exp(u * u * -0.5) * ((2.0 * math.pi) ** -0.5)
        act = (u * cdf).astype(bf16)
        d_up = (d_act * (cdf + u * pdf)).astype(bf16)
        out[rows, :] += jnp.dot(act, down_w, preferred_element_type=f32)
        dh[rows, :] += lax.dot_general(d_up, up_w, NT, preferred_element_type=f32)
        acts.append(act)
        d_ups.append(d_up)
    g_up = jnp.dot(hT[...], jnp.concatenate(d_ups, axis=0), preferred_element_type=f32).astype(bf16)
    g_down = jnp.dot(cT[...], jnp.concatenate(acts, axis=0), preferred_element_type=f32).T.astype(bf16)
    for f in range(2):
        for y in range(4):
            for i in range(2):
                g_ref[y, 4 * chunk + 2 * f + i] = g_up[160 * y + 80 * i:160 * y + 80 * (i + 1), 640 * f:640 * (f + 1)]
        for i in range(8):
            g_ref[2 * chunk + f, 8 + i] = g_down[640 * f + 80 * i:640 * f + 80 * (i + 1)]

    @pl.when(chunk == 1)
    def _():
        mine_ref[0], mine_ref[1] = out[0:512, :].astype(bf16), dh[0:512, :].astype(bf16)
        theirs_ref[0], theirs_ref[1] = out[512:1024, :].astype(bf16), dh[512:1024, :].astype(bf16)


def feed_forward(h, h2, cot, cot2, weights):
    return call(
        feed_kernel,
        (far(2, 512, 640), far(2, 512, 640), far(4, 16, 80, 640)),
        "feed_forward", 30 * 10**9, 52, grid=(2,),
        in_specs=[full(512, 640)] * 4 + [pl.BlockSpec((640, 1280), lambda f: (0, f)), pl.BlockSpec((320, 2560), lambda f: (f, 1))],
        out_specs=[full(2, 512, 640), full(2, 512, 640), full(4, 16, 80, 640)],
        scratch_shapes=[pltpu.VMEM((1024, 640), bf16), pltpu.VMEM((1024, 640), bf16), pltpu.VMEM((640, 1024), bf16), pltpu.VMEM((640, 1024), bf16),
                        pltpu.VMEM((1024, 640), f32), pltpu.VMEM((1024, 640), f32)],
    )(*stay(h, h2, cot), cot2, *stay(weights, weights))


def after_kernel(mid_ref, mine_ref, theirs_ref, cot_ref, vec_ref, block_ref, grad_ref, branch_ref, g_ref):
    @pl.when(pl.program_id(0) == 0)
    def _():
        g_ref[...] = jnp.zeros_like(g_ref)

    middle = mid_ref[...]
    block_ref[...] = (middle + mine_ref[0].astype(f32) + theirs_ref[0].astype(f32)).astype(bf16)
    d_hidden = mine_ref[1].astype(f32) + theirs_ref[1].astype(f32)
    n, r = moments(middle)
    g_ref[0:1, :] += jnp.sum(d_hidden * n, axis=0, keepdims=True)
    g_ref[1:2, :] += jnp.sum(d_hidden, axis=0, keepdims=True)
    grad = cot_ref[...].astype(f32) + norm_back(d_hidden, n, r, vec_ref[2:3, :])
    grad_ref[...] = grad
    branch_ref[...] = grad.astype(bf16)


def after_feed(*args):
    rows, pair = pl.BlockSpec((128, 640), lambda i: (i, 0)), pl.BlockSpec((2, 128, 640), lambda i: (0, i, 0))
    return call(
        after_kernel, (far(512, 640), far(512, 640, dtype=f32), shape(512, 640), shape(8, 640, dtype=f32)), "after_feed", 10**9, 16,
        grid=(4,), in_specs=[rows, pair, pair, rows, full(16, 640)], out_specs=[rows, rows, rows, full(8, 640)])(*stay(args[0], args[1]), args[2], *stay(args[3], args[4]))


def branch_kernel(core_ref, own_ref, their_ref, w_ref, low0_ref, low1_ref, theirs_ref, do_ref, doT_ref, g_ref):
    core = core_ref[0]
    w = jnp.concatenate([w_ref[pl.ds(pl.multiple_of(256 * core, 256), 256), :], w_ref[512:640, :]], axis=0)
    g = jnp.zeros((640, 384), f32)
    for m in range(2):
        part = slice(256 * m, 256 * (m + 1))
        mine, theirs = own_ref[part, :].astype(f32), their_ref[part, :].astype(f32)
        branch = jnp.concatenate([jnp.where(core == 0, mine, theirs), jnp.where(core == 0, theirs, mine)], axis=0)
        kept = jnp.where(core == 0, branch[:, :384], branch[:, 256:]).astype(bf16)
        branch = branch.astype(bf16)
        rows = slice(512 * m, 512 * (m + 1))
        do = lax.dot_general(branch, w, NT, preferred_element_type=f32)
        do_ref[rows, :] = do.astype(bf16)
        doT_ref[:, rows] = do.T.astype(bf16)
        attended = heads_joined(core, (low0_ref, low1_ref)[m][...].astype(f32), theirs_ref[m].astype(f32))
        g = g + jnp.dot(attended.T.astype(bf16), kept, preferred_element_type=f32)
    g_ref[...] = g.astype(bf16)


def branch_step(core, own, their, weights, *args):
    return call(
        branch_kernel, (far(1024, 384), far(384, 1024), shape(640, 384)), "branch", 10**9, 24, **scalar_first(
            (1,), [full(512, 640)] * 2 + [W_OUT] + [full(*a.shape) for a in args], [full(1024, 384), full(384, 1024), full(640, 384)]))(
                core, own, their, *stay(weights), *args)


def near_by(*arrays):
    return [pltpu.with_memory_space_constraint(a, pltpu.MemorySpace.VMEM) for a in arrays]


def project_back_kernel(place_ref, *refs):
    own_refs, other_refs = refs[:5], refs[5:10]
    (vec_ref, w_ref, dq0_ref, dq1_ref, dk0_ref, dk1_ref, dv0_ref, dv1_ref, g_out_ref, g_two_ref,
     mine_ref, theirs_ref, tail_ref, n_ref, d_kv, d_q, d_hid, g_ref, g_vec, slots, arrived) = refs[10:]
    step, core = pl.program_id(0), place_ref[0]
    block, second = lax.rem(step, 5), lax.div(step, 5)
    inside = lambda j, m: (j >= place_ref[1 + 2 * m]) & (j < place_ref[2 + 2 * m])
    needed = inside(block, second)

    def copies(j, m, slot):
        return [pltpu.make_async_copy(refs_of[j].at[m], slots.at[slot, i], arrived.at[slot, i]) for i, refs_of in enumerate((own_refs, other_refs))]

    @pl.when(step == 0)
    def _():
        for m in range(2):
            for j in range(5):
                @pl.when(inside(j, m))
                def _():
                    for copy in copies(j, m, 5 * m + j):
                        copy.start()
        g_ref[...] = jnp.zeros_like(g_ref)
        g_vec[...] = jnp.zeros_like(g_vec)
        g_vec[2:4, :] = g_two_ref[0:2, :]

    @pl.when(jnp.logical_not(needed))
    def _():
        mine_ref[...] = jnp.zeros_like(mine_ref)
        theirs_ref[...] = jnp.zeros_like(theirs_ref)

    @pl.when(needed)
    def _():
        for copy in copies(0, 0, step):
            copy.wait()
        rows_in_order(core, slots.at[step, 0], slots.at[step, 1], n_ref)

    for m, (dq, dk, dv) in enumerate(((dq0_ref, dk0_ref, dv0_ref), (dq1_ref, dk1_ref, dv1_ref))):
        @pl.when(needed & (second == m))
        def _():
            rows = pl.ds(pl.multiple_of(block * 512, 512), 512)
            d_kv[:, :384], d_kv[:, 384:] = dk[rows, :], dv[rows, :]
            d_q[...] = dq[...]

    @pl.when(needed)
    def _():
        n = n_ref[...].astype(f32)
        hiddenT = (n * vec_ref[0:1, :] + vec_ref[1:2, :]).T.astype(bf16)
        d_hid[...] = lax.dot_general(d_kv[...], w_ref[:, 384:1152], NT, preferred_element_type=f32)
        g_ref[:, 384:] += jnp.dot(hiddenT, d_kv[...], preferred_element_type=f32)

        @pl.when(block == 2)
        def _():
            g_ref[:, :384] += jnp.dot(hiddenT, d_q[...], preferred_element_type=f32)
            d_hid[...] += lax.dot_general(d_q[...], w_ref[:, :384], NT, preferred_element_type=f32)

        dh = d_hid[...]
        low = dh.astype(bf16)
        for c, (first, other) in enumerate(((mine_ref, theirs_ref), (theirs_ref, mine_ref))):
            @pl.when(core == c)
            def _():
                first[0, 0], other[0, 0] = low[:256], low[256:]
        g_vec[0:1, :] += jnp.sum(dh * n, axis=0, keepdims=True)
        g_vec[1:2, :] += jnp.sum(dh, axis=0, keepdims=True)

    @pl.when(step == 9)
    def _():
        turned = g_vec[...].T
        lane = lax.broadcasted_iota(jnp.int32, (640, 128), 1) - 64 * (1 - core)
        spare = g_ref[:, 256:384]
        for i in range(4):
            spare = jnp.where(lane == i, turned[:, i:i + 1], spare)
        g_ref[:, 256:384] = spare
        for y in range(4):
            for z in range(4):
                rows = slice(160 * y + 40 * z, 160 * y + 40 * (z + 1))
                for x in range(3):
                    tail_ref[16 * y + 4 * z + x] = g_ref[rows, 384 * x:384 * (x + 1)].astype(bf16)
                tail_ref[16 * y + 4 * z + 3] = g_out_ref[rows, :].astype(bf16)


def project_back(place, own, other, vec, w, dq, dk, dv, g_out, g_two):
    here = pl.BlockSpec(memory_space=pltpu.VMEM)
    part = pl.BlockSpec((1, 1, 256, 640), lambda b, *_: (lax.rem(b, 5), b // 5, 0, 0))
    return call(
        project_back_kernel, (far(5, 2, 256, 640), far(5, 2, 256, 640), far(64, 40, 384)), "project_back", 10**10, 30, **scalar_first(
            (10,), [pl.BlockSpec(memory_space=pl.ANY)] * 10 + [here] * 10, [part, part, full(64, 40, 384)],
            [pltpu.VMEM((512, 640), bf16), pltpu.VMEM((512, 768), bf16), pltpu.VMEM((512, 384), bf16),
             pltpu.VMEM((512, 640), f32), pltpu.VMEM((640, 1152), f32), pltpu.VMEM((8, 640), f32),
             pltpu.VMEM((10, 2, 256, 640), bf16), pltpu.SemaphoreType.DMA((10, 2))]))(
                 place, *stay(*own, *other), *near_by(vec, w, *dq, *dk, *dv, g_out, g_two))


def in_core_order(core_ref, mine, theirs):
    core, mine, theirs = core_ref[0], mine.astype(f32), theirs.astype(f32)
    return jnp.where(core == 0, mine, theirs), jnp.where(core == 0, theirs, mine)


def final_feed_kernel(core_ref, mine_ref, theirs_ref, up_ref, down_ref):
    for i in range(16):
        for c, piece in enumerate(in_core_order(core_ref, mine_ref[i], theirs_ref[i])):
            if i < 8:
                base = 1280 * (i // 2) + 640 * c
                up_ref[80 * (i % 2):80 * (i % 2 + 1), base:base + 640] = piece
            else:
                base = 640 * c + 80 * (i - 8)
                down_ref[base:base + 80, :] = piece


def final_feed(core, mine, theirs):
    return call(final_feed_kernel, (shape(160, 5120, dtype=f32), shape(1280, 640, dtype=f32)), "final_feed", 10**6, 32, **scalar_first(
        (1,), [full(16, 80, 640)] * 2, [full(160, 5120), full(1280, 640)]))(core, mine, theirs)


def final_heads_kernel(core_ref, mine_ref, theirs_ref, qkv_ref, out_ref, vec_ref):
    lane = lax.broadcasted_iota(jnp.int32, (40, 128), 1)
    for z in range(4):
        rows = slice(40 * z, 40 * (z + 1))
        for x in range(4):
            a, b = in_core_order(core_ref, mine_ref[4 * z + x], theirs_ref[4 * z + x])
            if x < 3:
                last = jnp.where(lane < 64, a[:, 256:], b[:, 256:])
                qkv_ref[rows, 640 * x:640 * (x + 1)] = jnp.concatenate([a[:, :256], b[:, :256], last], axis=1)
            else:
                out_ref[rows, :] = jnp.concatenate([a, b[:, 128:]], axis=1)
            if x == 0:
                vec_ref[rows, :] = pltpu.roll(a[:, 256:], 64, 1) + b[:, 256:]


def final_heads(core, mine, theirs):
    return call(
        final_heads_kernel, (shape(160, 1920, dtype=f32), shape(160, 640, dtype=f32), shape(160, 128, dtype=f32)), "final_heads", 10**6, 16,
        **scalar_first((1,), [full(16, 40, 384)] * 2, [full(160, 1920), full(160, 640), full(160, 128)]))(core, mine, theirs)


def shifted(array, axis, by):
    devices = lax.axis_size(axis)
    return lax.ppermute(array, axis, [(i, (i + by) % devices) for i in range(devices)])


def passed_along(array, by):
    devices = lax.axis_size(("z", "x"))
    return lax.ppermute(array, ("z", "x"), [(i, i + by) for i in range(devices) if 0 <= i + by < devices])


def swapped(array):
    return lax.ppermute(array, "core", [(0, 1), (1, 0)])


def pick(array, index):
    return lax.dynamic_index_in_dim(array, index, 0, keepdims=False)


def gathered(array, axis):
    me, devices = lax.axis_index(axis), lax.axis_size(axis)
    out = jnp.zeros((devices,) + array.shape, array.dtype)
    out = lax.dynamic_update_index_in_dim(out, array, me, 0)
    for by in (1, devices - 1, 2):
        out = lax.dynamic_update_index_in_dim(out, shifted(array, axis, by), (me + devices - by) % devices, 0)
    return out


def window_info(length_row, chip, core, win):
    ends = jnp.cumsum(length_row)
    starts = ends - length_row
    base = chip * 512 - 1024
    places = base + jnp.arange(win, dtype=jnp.int32)
    inside = (places[:, None] >= starts[None, :]) & (places[:, None] < ends[None, :])
    ones = jnp.broadcast_to(jnp.arange(64) < 3, (win, 64)).astype(bf16)
    key_rows = jnp.concatenate([jnp.where(inside, 0.0, -BIG).astype(bf16), ones], axis=1)
    own = chip * 512 + jnp.arange(512, dtype=jnp.int32)
    inside_q = (own[None, :] >= starts[:, None]) & (own[None, :] < ends[:, None])
    query_rows = jnp.concatenate([inside_q.astype(bf16), jnp.zeros((64, 512), bf16)], axis=0)
    info = [core]
    sizes = []
    for t in range(2):
        first = chip * 512 + t * TILE
        low = jnp.max(jnp.where(starts <= first, starts, 0)) - base
        high = jnp.min(jnp.where(ends > first + TILE - 1, ends, 1 << 30)) - base
        start = low // 128 * 128
        need = high - start
        size = (need + SHORT - 1) // SHORT * SHORT
        info.append(jnp.minimum(start, win - size))
        sizes.append(size)
    low = jnp.minimum(info[1], info[2]) // 512
    high = (jnp.maximum(info[1] + sizes[0], info[2] + sizes[1]) + 511) // 512
    return jnp.stack(info + sizes).astype(jnp.int32), key_rows, query_rows, [low, high]


def body(tokens, lengths, gain_one, bias_one, w_qkv, w_out, gain_two, bias_two, w_up, w_down, cotangent):
    core, chip = lax.axis_index("core"), lax.axis_index(("z", "x"))
    core_arg = core[None].astype(jnp.int32)
    tok, cot = tokens[:, 0], cotangent[:, 0].reshape(512, 640)
    together = lambda *arrays: lax.optimization_barrier(arrays)

    vectors = jnp.pad(jnp.stack([gain_one, bias_one, gain_two, bias_two], axis=1), ((0, 0), (0, 124)))
    heads, tok_sent = together(pack_heads(core_arg, w_qkv, vectors), tok)
    heads = lax.all_gather(heads, "batch", axis=0, tiled=True)
    vec = vector_rows(heads)
    normal = normal_rows(tok_sent)
    before, after, normal_other, tok_other = passed_along(normal, 1), passed_along(normal, -1), swapped(normal), swapped(tok)
    windows = [window_info(lengths[m, 0], chip, core, 2560) for m in range(2)]
    place = jnp.stack([core] + windows[0][3] + windows[1][3]).astype(jnp.int32)
    feed_pack = pack_feed(core_arg, w_out, w_up, w_down)
    heads, vec, before, after, normal_other, tok_other, feed_pack, place, windows = together(
        heads, vec, before, after, normal_other, tok_other, feed_pack, place, windows)
    own = [passed_along(before, 1), before, normal, after, passed_along(after, -1)]
    other = [None, swapped(before), normal_other, swapped(after), None]
    feed_weights = lax.all_gather(feed_pack, "batch", axis=0, tiled=True)
    *near_parts, q, qT = project((1, 2, 3), place, own, other, vec, heads)
    own[0], own[4], near_parts = together(own[0], own[4], near_parts)
    other[0], other[4] = swapped(own[0]), swapped(own[4])
    k, v, kT, vT = project((0, 4), place, own, other, vec, heads, near_parts)
    (oT0, low0, lse0), (oT1, low1, lse1) = (
        attend(m, info, qT, k, vT, key_rows, query_rows) for m, (info, key_rows, query_rows, _) in enumerate(windows))

    theirs = swapped(jnp.stack([low0, low1]))
    middle, hidden_two, hidden_other = middle_step(core_arg, feed_weights, low0, low1, theirs, tok, tok_other, vec)
    mine, partial, feed_grads = feed_forward(hidden_two, hidden_other, cot, swapped(cot), feed_weights)
    feed_grads = lax.all_to_all(feed_grads.reshape(64, 80, 640), ("batch", "z", "x"), 0, 0, tiled=True)
    block_out, grad_middle, branch, g_two = after_feed(middle, mine, swapped(partial), cot, vec)

    do, doT, g_out = branch_step(core_arg, branch, swapped(branch), feed_weights, low0, low1, theirs)
    dq, dk, dv = zip(*(
        attend_back(m, info, qT, q, k, kT, v, doT, do, oT, lse, key_rows, query_rows)
        for m, ((info, key_rows, query_rows, _), oT, lse) in enumerate(zip(windows, (oT0, oT1), (lse0, lse1)))))
    mine, theirs, tail = project_back(place, own, other, vec, heads, dq, dk, dv, g_out, g_two)
    feed_grads, mine, theirs, tail = together(feed_grads, mine, theirs, tail)

    feed = jnp.sum(feed_grads.astype(f32), axis=0).astype(bf16)
    theirs = swapped(theirs)
    sums = [mine[j].astype(f32) + theirs[j].astype(f32) for j in range(5)]
    right, left = passed_along(sums[4].astype(bf16), 1), passed_along(sums[0].astype(bf16), -1)
    tail, feed, right, left = together(tail, feed, right, left)
    tail = lax.all_to_all(tail, ("batch", "z", "x"), 0, 0, tiled=True)
    feed = lax.all_gather(feed, ("z", "x"), axis=0, tiled=True).reshape(16, 80, 640)
    right = passed_along((right.astype(f32) + sums[3]).astype(bf16), 1)
    left = passed_along((left.astype(f32) + sums[1]).astype(bf16), -1)
    tail, right, left = together(tail, right, left)
    tail = gathered(jnp.sum(tail.astype(f32), axis=0).astype(bf16), "x").reshape(160, 384)
    tail = gathered(tail, "z").reshape(16, 40, 384)
    d_one = (sums[2] + right.astype(f32) + left.astype(f32)).reshape(512, 640)
    n_one, r_one = moments(tok.reshape(512, 640).astype(f32))
    grad_tokens = (grad_middle + norm_back(d_one, n_one, r_one, vec[0:1])).astype(bf16)
    tail, grad_tokens, feed = together(tail, grad_tokens, feed)
    grad_qkv, grad_out, spare = final_heads(core_arg, tail, swapped(tail))
    grad_up, grad_down = final_feed(core_arg, feed, swapped(feed))
    return (
        block_out.reshape(2, 1, 256, 640), grad_tokens.reshape(2, 1, 256, 640), spare[:, 0], spare[:, 1], grad_qkv, grad_out,
        spare[:, 2], spare[:, 3], grad_up, grad_down)


def solution(mesh):
    fine = Mesh(mesh.devices.reshape(4, 4, 4, 2), ("batch", "z", "x", "core"))
    rows = P(None, "batch", ("z", "x", "core"), None)
    one, two = P("batch"), P("batch", None)
    return jax.shard_map(
        body,
        mesh=fine,
        in_specs=(rows, P(None, "batch", None), one, one, two, two, one, one, two, two, rows),
        out_specs=(rows, rows, one, one, two, two, one, one, two, two),
        check_vma=False,
    )
```

```python
import math

import jax
import jax.numpy as jnp
from jax import lax
from jax.experimental import pallas as pl
from jax.experimental.pallas import tpu as pltpu
from jax.sharding import Mesh
from jax.sharding import PartitionSpec as P

HEAD_DIM = 32
SCALE = HEAD_DIM ** -0.5
LOG2E = math.log2(math.e)
C2 = SCALE * LOG2E
BIG = 1e30
TILE = 256
EPSILON = 1e-05
PAIRS = 5
SHORT, LONG = 384, 1152
f32, bf16 = jnp.float32, jnp.bfloat16
NT = (((1,), (1,)), ((), ()))


def pair_offset(info_ref):
    p = pl.program_id(0)
    sub = jnp.where(p == PAIRS - 1, info_ref[0], lax.rem(p, 2))
    return sub * (2 * HEAD_DIM)


def split3(v):
    a = v.astype(bf16)
    r = v - a.astype(f32)
    b = r.astype(bf16)
    d = (r - b.astype(f32)).astype(bf16)
    return a, b, d


def rows_masked(xT, off):
    row = lax.broadcasted_iota(jnp.int32, xT.shape, 0) - off
    xf = xT.astype(f32)
    return [jnp.where((row >= HEAD_DIM * j) & (row < HEAD_DIM * (j + 1)), xf, 0.0).astype(bf16) for j in range(2)]


def lanes_masked(x, off):
    lane = lax.broadcasted_iota(jnp.int32, x.shape, 1) - off
    xf = x.astype(f32)
    return [jnp.where((lane >= HEAD_DIM * j) & (lane < HEAD_DIM * (j + 1)), xf, 0.0).astype(bf16) for j in range(2)]


def attend_kernel(info_ref, qT_ref, k_ref, vT_ref, kaug_ref, qaugT_ref, oT_ref, o_ref, l_ref, rhs):
    off = pair_offset(info_ref)
    oT_ref[...] = jnp.where(lax.rem(pl.program_id(0), 2) == 0, 0.0, oT_ref[...])
    for t in range(2):
        cols = slice(t * TILE, (t + 1) * TILE)
        masked = rows_masked(qT_ref[:, cols], off)
        for j in range(2):
            rhs[0:128, j * TILE:(j + 1) * TILE] = masked[j]
            rhs[128:256, j * TILE:(j + 1) * TILE] = qaugT_ref[:, cols]
        start = info_ref[1 + t]
        need = info_ref[3 + t]

        def block(first, size):
            def step(i, carry):
                row = pl.multiple_of(first + i * size, 128)
                lhs = jnp.concatenate([k_ref[pl.ds(row, size), :], kaug_ref[pl.ds(row, size), :]], axis=1)
                raw = [jnp.dot(lhs, rhs[:, j * TILE:(j + 1) * TILE], preferred_element_type=f32) for j in range(2)]
                out = []
                for j in range(2):
                    m, l, o = carry[j]
                    s = raw[j] * C2
                    m_new = jnp.maximum(m, jnp.max(s, axis=0, keepdims=True))
                    alpha = jnp.exp2(m - m_new)
                    p = jnp.exp2(s - m_new)
                    vT = vT_ref[pl.ds(pl.multiple_of(off + j * HEAD_DIM, HEAD_DIM), HEAD_DIM), pl.ds(row, size)]
                    out.append((m_new, l * alpha + jnp.sum(p, axis=0, keepdims=True),
                                o * alpha + jnp.dot(vT, p.astype(bf16), preferred_element_type=f32)))
                return tuple(out)
            return step

        def finish(state):
            for j in range(2):
                m, l, o = state[j]
                oT_ref[pl.ds(pl.multiple_of(off + j * HEAD_DIM, HEAD_DIM), HEAD_DIM), cols] = o * (1.0 / l)
                l_ref[0, j:j + 1, cols] = m + jnp.log2(l)

        init = tuple((jnp.full((1, TILE), -1e38, f32), jnp.zeros((1, TILE), f32), jnp.zeros((HEAD_DIM, TILE), f32)) for _ in range(2))

        longs = lax.div(need, LONG)
        state = lax.fori_loop(0, longs, block(start, LONG), init)
        finish(lax.fori_loop(0, lax.div(need - longs * LONG, SHORT), block(start + longs * LONG, SHORT), state))

    o_ref[...] = oT_ref[...].T.astype(bf16)


def attend(m, info, qT, k, vT, kaug, qaugT):
    win, nq = k.shape[1], qT.shape[2]
    qT, k, vT = stay(qT, k, vT)
    return pl.pallas_call(
        attend_kernel,
        out_shape=(jax.ShapeDtypeStruct((384, nq), f32), jax.ShapeDtypeStruct((nq, 384), bf16), jax.ShapeDtypeStruct((PAIRS, 8, nq), f32)),
        grid_spec=pltpu.PrefetchScalarGridSpec(
            num_scalar_prefetch=1, grid=(PAIRS,),
            in_specs=[
                pl.BlockSpec((None, 128, nq), lambda p, *_: (m, p // 2, 0)),
                pl.BlockSpec((None, win, 128), lambda p, *_: (m, 0, p // 2)),
                pl.BlockSpec((None, 128, win), lambda p, *_: (m, p // 2, 0)),
                pl.BlockSpec((win, 128), lambda p, *_: (0, 0)),
                pl.BlockSpec((128, nq), lambda p, *_: (0, 0)),
            ],
            out_specs=[
                pl.BlockSpec((128, nq), lambda p, *_: (p // 2, 0)),
                pl.BlockSpec((nq, 128), lambda p, *_: (0, p // 2)),
                pl.BlockSpec((1, 8, nq), lambda p, *_: (p, 0, 0)),
            ],
            scratch_shapes=[pltpu.VMEM((256, 2 * TILE), bf16)],
        ),
        compiler_params=pltpu.CompilerParams(vmem_limit_bytes=28 << 20),
        cost_estimate=pl.CostEstimate(flops=int(20 * 10**9 * 0.02), bytes_accessed=0, transcendentals=0),
        name="attend",
    )(info, qT, k, vT, kaug, qaugT)


def attend_back_kernel(info_ref, qT_ref, q_ref, k_ref, kT_ref, v_ref, doT_ref, do_ref, oT_ref, l_ref, kaug_ref, qaugT_ref,
                       dq_ref, dk_ref, dv_ref, dqT_ref, rhs_s, rhs_d, q_stk, do_stk, dk_acc, dv_acc):
    p_id = pl.program_id(0)
    off = pair_offset(info_ref)

    @pl.when(lax.rem(p_id, 2) == 0)
    def _():
        dqT_ref[...] = jnp.zeros_like(dqT_ref)
        dk_acc[...] = jnp.zeros_like(dk_acc)
        dv_acc[...] = jnp.zeros_like(dv_acc)

    for t in range(2):
        cols = slice(t * TILE, (t + 1) * TILE)
        masked_q = rows_masked(qT_ref[:, cols], off)
        masked_do = rows_masked(doT_ref[:, cols], off)
        lane_q = lanes_masked(q_ref[cols, :], off)
        lane_do = lanes_masked(do_ref[cols, :], off)
        for j in range(2):
            part = slice(j * TILE, (j + 1) * TILE)
            head = pl.ds(pl.multiple_of(off + j * HEAD_DIM, HEAD_DIM), HEAD_DIM)
            delta = jnp.sum(doT_ref[head, cols].astype(f32) * oT_ref[head, cols], axis=0, keepdims=True)
            total = l_ref[0, j:j + 1, cols] * (1.0 / C2)
            rowid = lax.broadcasted_iota(jnp.int32, (64, TILE), 0)
            lp, dp = split3(-total), split3(-delta)
            def pieces(parts):
                x = jnp.zeros((64, TILE), f32)
                for n in range(3):
                    x = jnp.where(rowid == n, parts[n].astype(f32), x)
                return x.astype(bf16)
            rhs_s[0:128, part] = masked_q[j]
            rhs_s[128:192, part] = qaugT_ref[0:64, cols]
            rhs_s[192:256, part] = pieces(lp)
            rhs_d[0:128, part] = masked_do[j]
            rhs_d[128:192, part] = jnp.zeros((64, TILE), bf16)
            rhs_d[192:256, part] = pieces(dp)
            q_stk[part, :] = lane_q[j]
            do_stk[part, :] = lane_do[j]
        start = info_ref[1 + t]
        need = info_ref[3 + t]

        def block(first, size):
            def step(i, carry):
                row = pl.multiple_of(first + i * size, 128)
                rows = pl.ds(row, size)
                aug = kaug_ref[rows, :]
                lhs_k = jnp.concatenate([k_ref[rows, :], aug], axis=1)
                lhs_v = jnp.concatenate([v_ref[rows, :], aug], axis=1)
                out, dv, dk = [], dv_acc[rows, :], dk_acc[rows, :]
                for j in range(2):
                    part = slice(j * TILE, (j + 1) * TILE)
                    s = jnp.dot(lhs_k, rhs_s[:, part], preferred_element_type=f32)
                    dp = jnp.dot(lhs_v, rhs_d[:, part], preferred_element_type=f32)
                    p = jnp.exp2(s * C2)
                    ds = (p * dp).astype(bf16)
                    dv = dv + jnp.dot(p.astype(bf16), do_stk[part, :], preferred_element_type=f32)
                    dk = dk + jnp.dot(ds, q_stk[part, :], preferred_element_type=f32)
                    kT = kT_ref[pl.ds(pl.multiple_of(off + j * HEAD_DIM, HEAD_DIM), HEAD_DIM), rows]
                    out.append(carry[j] + jnp.dot(kT, ds, preferred_element_type=f32))
                dv_acc[rows, :] = dv
                dk_acc[rows, :] = dk
                return tuple(out)
            return step

        def finish(dqs):
            for j in range(2):
                dqT_ref[pl.ds(pl.multiple_of(off + j * HEAD_DIM, HEAD_DIM), HEAD_DIM), cols] = dqs[j] * SCALE

        init = tuple(jnp.zeros((HEAD_DIM, TILE), f32) for _ in range(2))

        longs = lax.div(need, LONG)
        state = lax.fori_loop(0, longs, block(start, LONG), init)
        finish(lax.fori_loop(0, lax.div(need - longs * LONG, SHORT), block(start + longs * LONG, SHORT), state))
    @pl.when((lax.rem(p_id, 2) == 1) | (p_id == PAIRS - 1))
    def _():
        dq_ref[...] = dqT_ref[...].T.astype(bf16)
        dk_ref[...] = (dk_acc[...] * SCALE).astype(bf16)
        dv_ref[...] = dv_acc[...].astype(bf16)


def attend_back(m, info, qT, q, k, kT, v, doT, do, oT, lse, kaug, qaugT):
    win, nq = k.shape[1], qT.shape[2]
    qT, q, k, kT, v, doT, do = stay(qT, q, k, kT, v, doT, do)
    wide = pl.BlockSpec((128, nq), lambda p, *_: (p // 2, 0))
    tall = pl.BlockSpec((nq, 128), lambda p, *_: (0, p // 2))
    keys = pl.BlockSpec((win, 128), lambda p, *_: (0, p // 2))
    wide_m = pl.BlockSpec((None, 128, nq), lambda p, *_: (m, p // 2, 0))
    tall_m = pl.BlockSpec((None, nq, 128), lambda p, *_: (m, 0, p // 2))
    keys_m = pl.BlockSpec((None, win, 128), lambda p, *_: (m, 0, p // 2))
    return pl.pallas_call(
        attend_back_kernel,
        out_shape=tuple(pltpu.MemorySpace.VMEM(d, bf16) for d in ((nq, 384), (win, 384), (win, 384))),
        grid_spec=pltpu.PrefetchScalarGridSpec(
            num_scalar_prefetch=1, grid=(PAIRS,),
            in_specs=[wide_m, tall_m, keys_m, pl.BlockSpec((None, 128, win), lambda p, *_: (m, p // 2, 0)), keys_m,
                      pl.BlockSpec((128, nq), lambda p, *_: (p // 2, m)), pl.BlockSpec((nq, 128), lambda p, *_: (m, p // 2)), wide,
                      pl.BlockSpec((1, 8, nq), lambda p, *_: (p, 0, 0)),
                      pl.BlockSpec((win, 128), lambda p, *_: (0, 0)), pl.BlockSpec((128, nq), lambda p, *_: (0, 0))],
            out_specs=[tall, keys, keys],
            scratch_shapes=[pltpu.VMEM((128, nq), f32), pltpu.VMEM((256, 2 * TILE), bf16), pltpu.VMEM((256, 2 * TILE), bf16),
                            pltpu.VMEM((2 * TILE, 128), bf16), pltpu.VMEM((2 * TILE, 128), bf16),
                            pltpu.VMEM((win, 128), f32), pltpu.VMEM((win, 128), f32)],
        ),
        compiler_params=pltpu.CompilerParams(vmem_limit_bytes=32 << 20),
        cost_estimate=pl.CostEstimate(flops=int(40 * 10**9 * 0.02), bytes_accessed=0, transcendentals=0),
        name="attend_back",
    )(info, qT, q, k, kT, v, doT, do, oT, lse, kaug, qaugT)


def moments(x):
    centred = x - jnp.mean(x, axis=-1, keepdims=True)
    r = lax.rsqrt(jnp.mean(centred * centred, axis=-1, keepdims=True) + EPSILON)
    return centred * r, r


def norm_back(grad, n, r, gain):
    e = grad * gain
    return r * (e - jnp.mean(e, axis=-1, keepdims=True) - n * jnp.mean(e * n, axis=-1, keepdims=True))


def call(kernel, out_shape, name, flops=10**9, limit=48, **spec):
    return pl.pallas_call(
        kernel, out_shape=out_shape, name=name,
        compiler_params=pltpu.CompilerParams(vmem_limit_bytes=limit << 20),
        cost_estimate=pl.CostEstimate(flops=int(flops * 0.02), bytes_accessed=0, transcendentals=0), **spec)


def shape(*dims, dtype=bf16):
    return jax.ShapeDtypeStruct(dims, dtype)


def far(*dims, dtype=bf16):
    return pltpu.MemorySpace.HBM(dims, dtype)


def stay(*arrays):
    return [pltpu.with_memory_space_constraint(a, pltpu.MemorySpace.HBM) for a in arrays]


def near_by(*arrays):
    return [pltpu.with_memory_space_constraint(a, pltpu.MemorySpace.VMEM) for a in arrays]


def scalar_first(grid, in_specs, out_specs, scratch=()):
    return dict(grid_spec=pltpu.PrefetchScalarGridSpec(
        num_scalar_prefetch=1, grid=grid, in_specs=in_specs, out_specs=out_specs, scratch_shapes=list(scratch)))


def full(*dims):
    return pl.BlockSpec(dims, lambda *_: (0,) * len(dims))


def pack_heads_kernel(core_ref, qkv_ref, vec_ref, heads_ref):
    for part in range(3):
        near = pl.ds(pl.multiple_of(640 * part + 256 * core_ref[0], 128), 256)
        heads_ref[:, 384 * part:384 * part + 256] = qkv_ref[:, near]
        heads_ref[:, 384 * part + 256:384 * (part + 1)] = qkv_ref[:, 640 * part + 512:640 * (part + 1)]
    heads_ref[:, 1152:1280] = vec_ref[...]


def pack_heads(core, w_qkv, vectors):
    return call(pack_heads_kernel, shape(160, 1280), "pack_heads", 10**6, 8, **scalar_first(
        (1,), [full(160, 1920), full(160, 128)], full(160, 1280)))(core, w_qkv, vectors)


def turn_kernel(vec_ref, rows_ref):
    rows_ref[...] = vec_ref[...].astype(f32).T[:16]


def vector_rows(heads):
    return call(turn_kernel, shape(16, 640, dtype=f32), "vector_rows", 10**12, 8, grid=(1,),
                in_specs=[pl.BlockSpec((640, 128), lambda i: (0, 9))], out_specs=full(16, 640))(*stay(heads))


def pack_feed_kernel(core_ref, out_ref, up_ref, down_ref, feed_ref):
    core = core_ref[0]
    feed_ref[:, 5120:5760] = out_ref[...]
    for f in range(4):
        feed_ref[:, 640 * f:640 * (f + 1)] = up_ref[:, pl.ds(pl.multiple_of(1280 * f + 640 * core, 128), 640)]
        feed_ref[:, 2560 + 640 * f:2560 + 640 * (f + 1)] = down_ref[pl.ds(pl.multiple_of(640 * core + 160 * f, 32), 160), :]


def pack_feed(core, w_out, w_up, w_down):
    return call(pack_feed_kernel, far(160, 5760), "pack_feed", 10**6, 16, **scalar_first(
        (1,), [full(160, 640), full(160, 5120), full(1280, 640)], full(160, 5760)))(core, *stay(w_out, w_up, w_down))


def rows_in_order(core, mine_ref, theirs_ref, x_ref):
    for c, (first, second) in enumerate(((mine_ref, theirs_ref), (theirs_ref, mine_ref))):
        @pl.when(core == c)
        def _():
            x_ref[0:256, :], x_ref[256:512, :] = first[...], second[...]


def normal_kernel(tok_ref, n_ref):
    for m in range(2):
        n_ref[m] = moments(tok_ref[m].astype(f32))[0].astype(bf16)


def normal_rows(tok):
    return call(normal_kernel, shape(2, 256, 640), "normal_rows", 10**6, 8, grid=(1,), in_specs=[full(2, 256, 640)], out_specs=full(2, 256, 640))(tok)


def project_kernel(chips, place_ref, *refs):
    n = len(chips)
    own_refs, other_refs = refs[:n], refs[n:2 * n]
    vec_ref, w_ref = refs[2 * n:2 * n + 2]
    k_ref, v_ref, kT_ref, vT_ref = refs[-6 - 2 * (n == 3):][:4]
    x_ref, hid_ref = refs[-2:]
    m, step = pl.program_id(0), pl.program_id(1)
    block = sum(jnp.where(step == i, chip, 0) for i, chip in enumerate(chips))
    needed = (block >= place_ref[1 + 2 * m]) & (block < place_ref[2 + 2 * m])

    @pl.when(jnp.logical_not(needed))
    def _():
        for ref in (k_ref, v_ref, kT_ref, vT_ref):
            ref[...] = jnp.zeros_like(ref)

    @pl.when(needed)
    def _():
        for j in range(n):
            @pl.when(step == j)
            def _():
                rows_in_order(place_ref[0], own_refs[j].at[m], other_refs[j].at[m], x_ref)

        hidden = (x_ref[...].astype(f32) * vec_ref[0:1, :] + vec_ref[1:2, :]).astype(bf16)
        hid_ref[...] = hidden
        kv = jnp.dot(hidden, w_ref[:, 384:], preferred_element_type=f32)
        low = kv.astype(bf16)
        k_ref[0] = low[:, :384]
        v_ref[0] = low[:, 384:]
        turned = kv.T.astype(bf16)
        kT_ref[0] = turned[:384]
        vT_ref[0] = turned[384:]

    if n == 3:
        q_ref, qT_ref = refs[-4:-2]

        @pl.when(step == 1)
        def _():
            q = jnp.dot(hid_ref[...], w_ref[:, :384], preferred_element_type=f32)
            q_ref[0] = q.astype(bf16)
            qT_ref[0] = q.T.astype(bf16)


def project(chips, place, own, other, vec, w, earlier=()):
    n = len(chips)
    chip = (lambda b: b + 1) if n == 3 else (lambda b: 4 * b)
    tall = pl.BlockSpec((1, 512, 384), lambda m, b, *_: (m, chip(b), 0))
    wide = pl.BlockSpec((1, 384, 512), lambda m, b, *_: (m, 0, chip(b)))
    shapes = [far(2, 2560, 384), far(2, 2560, 384), far(2, 384, 2560), far(2, 384, 2560)]
    specs = [tall, tall, wide, wide]
    if n == 3:
        shapes += [far(2, 512, 384), far(2, 384, 512)]
        specs += [pl.BlockSpec((1, 512, 384), lambda m, *_: (m, 0, 0)), pl.BlockSpec((1, 384, 512), lambda m, *_: (m, 0, 0))]
    own, other = [own[c] for c in chips], [other[c] for c in chips]
    return call(
        lambda *refs: project_kernel(chips, *refs), shapes, "project", 5 * 10**9, 28,
        input_output_aliases={2 * n + 3 + i: i for i in range(len(earlier))}, **scalar_first(
            (2, n), [full(2, 256, 640)] * (2 * n) + [full(16, 640), full(640, 1152)] + [pl.BlockSpec(memory_space=pl.ANY)] * len(earlier),
            specs, [pltpu.VMEM((512, 640), bf16), pltpu.VMEM((512, 640), bf16)]))(place, *own, *other, *stay(vec, w), *earlier)


def heads_joined(core, mine, theirs):
    first, second = (jnp.where(core == 0, a, b) for a, b in ((mine, theirs), (theirs, mine)))
    return jnp.concatenate([first[:, :256], second[:, :256], first[:, 256:] + second[:, 256:]], axis=1)


def middle_kernel(core_ref, w_ref, low0_ref, low1_ref, theirs_ref, tok_ref, tok2_ref, vec_ref, mid_ref, hid_ref, hid2_ref):
    core = core_ref[0]
    for m, low_ref in enumerate((low0_ref, low1_ref)):
        attended = heads_joined(core, low_ref[...].astype(f32), theirs_ref[m].astype(f32)).astype(bf16)
        branch = jnp.dot(attended, w_ref[...], preferred_element_type=f32)
        mine = jnp.where(core == 0, branch[:256], branch[256:]) + tok_ref[m].astype(f32)
        theirs = jnp.where(core == 0, branch[256:], branch[:256]) + tok2_ref[m].astype(f32)
        part = slice(256 * m, 256 * (m + 1))
        mid_ref[part, :] = mine
        hid_ref[part, :] = (moments(mine)[0] * vec_ref[2:3, :] + vec_ref[3:4, :]).astype(bf16)
        hid2_ref[part, :] = (moments(theirs)[0] * vec_ref[2:3, :] + vec_ref[3:4, :]).astype(bf16)


W_OUT = pl.BlockSpec((640, 640), lambda *_: (0, 8))


def middle_step(core, weights, *args):
    return call(middle_kernel, (far(512, 640, dtype=f32), *(pltpu.MemorySpace.VMEM((512, 640), bf16),) * 2), "middle", 10**9, 20, **scalar_first(
        (1,), [W_OUT] + [full(*a.shape) for a in args], [full(512, 640)] * 3))(core, *stay(weights), *args[:-1], *stay(args[-1]))


def feed_kernel(h_ref, h2_ref, cot_ref, cot2_ref, up_ref, down_ref, mine_ref, theirs_ref, g_ref, h, cot, hT, cT, out, dh):
    chunk = pl.program_id(0)

    @pl.when(chunk == 0)
    def _():
        h[0:512, :], h[512:1024, :] = h_ref[...], h2_ref[...]
        cot[0:512, :], cot[512:1024, :] = cot_ref[...], cot2_ref[...]
        hT[...] = h[...].astype(f32).T.astype(bf16)
        cT[...] = cot[...].astype(f32).T.astype(bf16)
        out[...] = jnp.zeros_like(out)
        dh[...] = jnp.zeros_like(dh)

    up_w = up_ref[...]
    down_w = jnp.concatenate([down_ref[160 * y:160 * (y + 1), 640 * i:640 * (i + 1)] for y in range(2) for i in range(4)], axis=0)
    acts, d_ups = [], []
    for t in range(4):
        rows = slice(256 * t, 256 * (t + 1))
        u = jnp.dot(h[rows, :], up_w, preferred_element_type=f32)
        d_act = lax.dot_general(cot[rows, :], down_w, NT, preferred_element_type=f32)
        cdf = 0.5 * (1.0 + lax.erf(u * (2.0 ** -0.5)))
        pdf = jnp.exp(u * u * -0.5) * ((2.0 * math.pi) ** -0.5)
        act = (u * cdf).astype(bf16)
        d_up = (d_act * (cdf + u * pdf)).astype(bf16)
        out[rows, :] += jnp.dot(act, down_w, preferred_element_type=f32)
        dh[rows, :] += lax.dot_general(d_up, up_w, NT, preferred_element_type=f32)
        acts.append(act)
        d_ups.append(d_up)
    g_up = jnp.dot(hT[...], jnp.concatenate(d_ups, axis=0), preferred_element_type=f32).astype(bf16)
    g_down = jnp.dot(cT[...], jnp.concatenate(acts, axis=0), preferred_element_type=f32).T.astype(bf16)
    for f in range(2):
        for y in range(4):
            for i in range(2):
                g_ref[y, 4 * chunk + 2 * f + i] = g_up[160 * y + 80 * i:160 * y + 80 * (i + 1), 640 * f:640 * (f + 1)]
        for i in range(8):
            g_ref[2 * chunk + f, 8 + i] = g_down[640 * f + 80 * i:640 * f + 80 * (i + 1)]

    @pl.when(chunk == 1)
    def _():
        mine_ref[0], mine_ref[1] = out[0:512, :].astype(bf16), dh[0:512, :].astype(bf16)
        theirs_ref[0], theirs_ref[1] = out[512:1024, :].astype(bf16), dh[512:1024, :].astype(bf16)


def feed_forward(h, h2, cot, cot2, weights):
    return call(
        feed_kernel,
        (far(2, 512, 640), far(2, 512, 640), far(4, 16, 80, 640)),
        "feed_forward", 30 * 10**9, 52, grid=(2,),
        in_specs=[pl.BlockSpec(memory_space=pltpu.VMEM)] * 2 + [full(512, 640), pl.BlockSpec(memory_space=pltpu.VMEM), pl.BlockSpec((640, 1280), lambda f: (0, f)), pl.BlockSpec((320, 2560), lambda f: (f, 1))],
        out_specs=[full(2, 512, 640), full(2, 512, 640), full(4, 16, 80, 640)],
        scratch_shapes=[pltpu.VMEM((1024, 640), bf16), pltpu.VMEM((1024, 640), bf16), pltpu.VMEM((640, 1024), bf16), pltpu.VMEM((640, 1024), bf16),
                        pltpu.VMEM((1024, 640), f32), pltpu.VMEM((1024, 640), f32)],
    )(*near_by(h, h2), *stay(cot), *near_by(cot2), *stay(weights, weights))


def after_kernel(mid_ref, mine_ref, theirs_ref, cot_ref, vec_ref, block_ref, grad_ref, branch_ref, g_ref):
    @pl.when(pl.program_id(0) == 0)
    def _():
        g_ref[...] = jnp.zeros_like(g_ref)

    middle = mid_ref[...]
    block_ref[...] = (middle + mine_ref[0].astype(f32) + theirs_ref[0].astype(f32)).astype(bf16)
    d_hidden = mine_ref[1].astype(f32) + theirs_ref[1].astype(f32)
    n, r = moments(middle)
    g_ref[0:1, :] += jnp.sum(d_hidden * n, axis=0, keepdims=True)
    g_ref[1:2, :] += jnp.sum(d_hidden, axis=0, keepdims=True)
    grad = cot_ref[...].astype(f32) + norm_back(d_hidden, n, r, vec_ref[2:3, :])
    grad_ref[...] = grad
    branch_ref[...] = grad.astype(bf16)


def after_feed(*args):
    rows, pair = pl.BlockSpec((128, 640), lambda i: (i, 0)), pl.BlockSpec((2, 128, 640), lambda i: (0, i, 0))
    return call(
        after_kernel, (far(512, 640), far(512, 640, dtype=f32), shape(512, 640), shape(8, 640, dtype=f32)), "after_feed", 10**9, 16,
        grid=(4,), in_specs=[rows, pair, pair, rows, full(16, 640)], out_specs=[rows, rows, rows, full(8, 640)])(*stay(args[0], args[1]), args[2], *stay(args[3], args[4]))


def branch_kernel(core_ref, own_ref, their_ref, w_ref, low0_ref, low1_ref, theirs_ref, do_ref, doT_ref, g_ref):
    core = core_ref[0]
    w = jnp.concatenate([w_ref[pl.ds(pl.multiple_of(256 * core, 256), 256), :], w_ref[512:640, :]], axis=0)
    g = jnp.zeros((640, 384), f32)
    for m in range(2):
        part = slice(256 * m, 256 * (m + 1))
        mine, theirs = own_ref[part, :].astype(f32), their_ref[part, :].astype(f32)
        branch = jnp.concatenate([jnp.where(core == 0, mine, theirs), jnp.where(core == 0, theirs, mine)], axis=0)
        kept = jnp.where(core == 0, branch[:, :384], branch[:, 256:]).astype(bf16)
        branch = branch.astype(bf16)
        rows = slice(512 * m, 512 * (m + 1))
        do = lax.dot_general(branch, w, NT, preferred_element_type=f32)
        do_ref[rows, :] = do.astype(bf16)
        doT_ref[:, rows] = do.T.astype(bf16)
        attended = heads_joined(core, (low0_ref, low1_ref)[m][...].astype(f32), theirs_ref[m].astype(f32))
        g = g + jnp.dot(attended.T.astype(bf16), kept, preferred_element_type=f32)
    g_ref[...] = g.astype(bf16)


def branch_step(core, own, their, weights, *args):
    return call(
        branch_kernel, (far(1024, 384), far(384, 1024), shape(640, 384)), "branch", 10**9, 24, **scalar_first(
            (1,), [full(512, 640)] * 2 + [W_OUT] + [full(*a.shape) for a in args], [full(1024, 384), full(384, 1024), full(640, 384)]))(
                core, own, their, *stay(weights), *args)


def project_back_kernel(place_ref, *refs):
    own_refs, other_refs = refs[:5], refs[5:10]
    (vec_ref, w_ref, dq0_ref, dq1_ref, dk0_ref, dk1_ref, dv0_ref, dv1_ref, g_out_ref, g_two_ref,
     mine_ref, theirs_ref, tail_ref, n_ref, d_kv, d_q, d_hid, g_ref, g_vec, slots, arrived) = refs[10:]
    step, core = pl.program_id(0), place_ref[0]
    block, second = lax.rem(step, 5), lax.div(step, 5)
    inside = lambda j, m: (j >= place_ref[1 + 2 * m]) & (j < place_ref[2 + 2 * m])
    needed = inside(block, second)

    def copies(j, m, slot):
        return [pltpu.make_async_copy(refs_of[j].at[m], slots.at[slot, i], arrived.at[slot, i]) for i, refs_of in enumerate((own_refs, other_refs))]

    @pl.when(step == 0)
    def _():
        for m in range(2):
            for j in range(5):
                @pl.when(inside(j, m))
                def _():
                    for copy in copies(j, m, 5 * m + j):
                        copy.start()
        g_ref[...] = jnp.zeros_like(g_ref)
        g_vec[...] = jnp.zeros_like(g_vec)
        g_vec[2:4, :] = g_two_ref[0:2, :]

    @pl.when(jnp.logical_not(needed))
    def _():
        mine_ref[...] = jnp.zeros_like(mine_ref)
        theirs_ref[...] = jnp.zeros_like(theirs_ref)

    @pl.when(needed)
    def _():
        for copy in copies(0, 0, step):
            copy.wait()
        rows_in_order(core, slots.at[step, 0], slots.at[step, 1], n_ref)

    for m, (dq, dk, dv) in enumerate(((dq0_ref, dk0_ref, dv0_ref), (dq1_ref, dk1_ref, dv1_ref))):
        @pl.when(needed & (second == m))
        def _():
            rows = pl.ds(pl.multiple_of(block * 512, 512), 512)
            d_kv[:, :384], d_kv[:, 384:] = dk[rows, :], dv[rows, :]
            d_q[...] = dq[...]

    @pl.when(needed)
    def _():
        n = n_ref[...].astype(f32)
        hiddenT = (n * vec_ref[0:1, :] + vec_ref[1:2, :]).T.astype(bf16)
        d_hid[...] = lax.dot_general(d_kv[...], w_ref[:, 384:1152], NT, preferred_element_type=f32)
        g_ref[:, 384:] += jnp.dot(hiddenT, d_kv[...], preferred_element_type=f32)

        @pl.when(block == 2)
        def _():
            g_ref[:, :384] += jnp.dot(hiddenT, d_q[...], preferred_element_type=f32)
            d_hid[...] += lax.dot_general(d_q[...], w_ref[:, :384], NT, preferred_element_type=f32)

        dh = d_hid[...]
        low = dh.astype(bf16)
        for c, (first, other) in enumerate(((mine_ref, theirs_ref), (theirs_ref, mine_ref))):
            @pl.when(core == c)
            def _():
                first[0, 0], other[0, 0] = low[:256], low[256:]
        g_vec[0:1, :] += jnp.sum(dh * n, axis=0, keepdims=True)
        g_vec[1:2, :] += jnp.sum(dh, axis=0, keepdims=True)

    @pl.when(step == 9)
    def _():
        turned = g_vec[...].T
        lane = lax.broadcasted_iota(jnp.int32, (640, 128), 1) - 64 * (1 - core)
        spare = g_ref[:, 256:384]
        for i in range(4):
            spare = jnp.where(lane == i, turned[:, i:i + 1], spare)
        g_ref[:, 256:384] = spare
        for y in range(4):
            for z in range(4):
                rows = slice(160 * y + 40 * z, 160 * y + 40 * (z + 1))
                for x in range(3):
                    tail_ref[16 * y + 4 * z + x] = g_ref[rows, 384 * x:384 * (x + 1)].astype(bf16)
                tail_ref[16 * y + 4 * z + 3] = g_out_ref[rows, :].astype(bf16)


def project_back(place, own, other, vec, w, dq, dk, dv, g_out, g_two):
    here = pl.BlockSpec(memory_space=pltpu.VMEM)
    part = pl.BlockSpec((1, 1, 256, 640), lambda b, *_: (lax.rem(b, 5), b // 5, 0, 0))
    return call(
        project_back_kernel, (far(5, 2, 256, 640), far(5, 2, 256, 640), far(64, 40, 384)), "project_back", 10**10, 30, **scalar_first(
            (10,), [pl.BlockSpec(memory_space=pl.ANY)] * 10 + [here] * 10, [part, part, full(64, 40, 384)],
            [pltpu.VMEM((512, 640), bf16), pltpu.VMEM((512, 768), bf16), pltpu.VMEM((512, 384), bf16),
             pltpu.VMEM((512, 640), f32), pltpu.VMEM((640, 1152), f32), pltpu.VMEM((8, 640), f32),
             pltpu.VMEM((10, 2, 256, 640), bf16), pltpu.SemaphoreType.DMA((10, 2))]))(
                 place, *stay(*own, *other), *near_by(vec, w, *dq, *dk, *dv, g_out, g_two))


def in_core_order(core_ref, mine, theirs):
    core, mine, theirs = core_ref[0], mine.astype(f32), theirs.astype(f32)
    return jnp.where(core == 0, mine, theirs), jnp.where(core == 0, theirs, mine)


def final_feed_kernel(core_ref, mine_ref, theirs_ref, up_ref, down_ref):
    for i in range(16):
        for c, piece in enumerate(in_core_order(core_ref, mine_ref[i], theirs_ref[i])):
            if i < 8:
                base = 1280 * (i // 2) + 640 * c
                up_ref[80 * (i % 2):80 * (i % 2 + 1), base:base + 640] = piece
            else:
                base = 640 * c + 80 * (i - 8)
                down_ref[base:base + 80, :] = piece


def final_feed(core, mine, theirs):
    return call(final_feed_kernel, (shape(160, 5120, dtype=f32), shape(1280, 640, dtype=f32)), "final_feed", 10**6, 32, **scalar_first(
        (1,), [full(16, 80, 640)] * 2, [full(160, 5120), full(1280, 640)]))(core, mine, theirs)


def final_heads_kernel(core_ref, mine_ref, theirs_ref, qkv_ref, out_ref, vec_ref):
    lane = lax.broadcasted_iota(jnp.int32, (40, 128), 1)
    for z in range(4):
        rows = slice(40 * z, 40 * (z + 1))
        for x in range(4):
            a, b = in_core_order(core_ref, mine_ref[4 * z + x], theirs_ref[4 * z + x])
            if x < 3:
                last = jnp.where(lane < 64, a[:, 256:], b[:, 256:])
                qkv_ref[rows, 640 * x:640 * (x + 1)] = jnp.concatenate([a[:, :256], b[:, :256], last], axis=1)
            else:
                out_ref[rows, :] = jnp.concatenate([a, b[:, 128:]], axis=1)
            if x == 0:
                vec_ref[rows, :] = pltpu.roll(a[:, 256:], 64, 1) + b[:, 256:]


def final_heads(core, mine, theirs):
    return call(
        final_heads_kernel, (shape(160, 1920, dtype=f32), shape(160, 640, dtype=f32), shape(160, 128, dtype=f32)), "final_heads", 10**6, 16,
        **scalar_first((1,), [full(16, 40, 384)] * 2, [full(160, 1920), full(160, 640), full(160, 128)]))(core, mine, theirs)


def shifted(array, axis, by):
    devices = lax.axis_size(axis)
    return lax.ppermute(array, axis, [(i, (i + by) % devices) for i in range(devices)])


def passed_along(array, by):
    devices = lax.axis_size(("z", "x"))
    return lax.ppermute(array, ("z", "x"), [(i, i + by) for i in range(devices) if 0 <= i + by < devices])


def swapped(array):
    return lax.ppermute(array, "core", [(0, 1), (1, 0)])


def pick(array, index):
    return lax.dynamic_index_in_dim(array, index, 0, keepdims=False)


def gathered(array, axis):
    me, devices = lax.axis_index(axis), lax.axis_size(axis)
    out = jnp.zeros((devices,) + array.shape, array.dtype)
    out = lax.dynamic_update_index_in_dim(out, array, me, 0)
    for by in (1, devices - 1, 2):
        out = lax.dynamic_update_index_in_dim(out, shifted(array, axis, by), (me + devices - by) % devices, 0)
    return out


def window_info(length_row, chip, core, win):
    ends = jnp.cumsum(length_row)
    starts = ends - length_row
    base = chip * 512 - 1024
    places = base + jnp.arange(win, dtype=jnp.int32)
    inside = (places[:, None] >= starts[None, :]) & (places[:, None] < ends[None, :])
    ones = jnp.broadcast_to(jnp.arange(64) < 3, (win, 64)).astype(bf16)
    key_rows = jnp.concatenate([jnp.where(inside, 0.0, -BIG).astype(bf16), ones], axis=1)
    own = chip * 512 + jnp.arange(512, dtype=jnp.int32)
    inside_q = (own[None, :] >= starts[:, None]) & (own[None, :] < ends[:, None])
    query_rows = jnp.concatenate([inside_q.astype(bf16), jnp.zeros((64, 512), bf16)], axis=0)
    info = [core]
    sizes = []
    for t in range(2):
        first = chip * 512 + t * TILE
        low = jnp.max(jnp.where(starts <= first, starts, 0)) - base
        high = jnp.min(jnp.where(ends > first + TILE - 1, ends, 1 << 30)) - base
        start = low // 128 * 128
        need = high - start
        size = (need + SHORT - 1) // SHORT * SHORT
        info.append(jnp.minimum(start, win - size))
        sizes.append(size)
    low = jnp.minimum(info[1], info[2]) // 512
    high = (jnp.maximum(info[1] + sizes[0], info[2] + sizes[1]) + 511) // 512
    return jnp.stack(info + sizes).astype(jnp.int32), key_rows, query_rows, [low, high]


def body(tokens, lengths, gain_one, bias_one, w_qkv, w_out, gain_two, bias_two, w_up, w_down, cotangent):
    core, chip = lax.axis_index("core"), lax.axis_index(("z", "x"))
    core_arg = core[None].astype(jnp.int32)
    tok, cot = tokens[:, 0], cotangent[:, 0].reshape(512, 640)
    together = lambda *arrays: lax.optimization_barrier(arrays)

    vectors = jnp.pad(jnp.stack([gain_one, bias_one, gain_two, bias_two], axis=1), ((0, 0), (0, 124)))
    heads, tok_sent = together(pack_heads(core_arg, w_qkv, vectors), tok)
    heads = lax.all_gather(heads, "batch", axis=0, tiled=True)
    vec = vector_rows(heads)
    normal = normal_rows(tok_sent)
    before, after, normal_other, tok_other = passed_along(normal, 1), passed_along(normal, -1), swapped(normal), swapped(tok)
    windows = [window_info(lengths[m, 0], chip, core, 2560) for m in range(2)]
    place = jnp.stack([core] + windows[0][3] + windows[1][3]).astype(jnp.int32)
    feed_pack = pack_feed(core_arg, w_out, w_up, w_down)
    heads, vec, before, after, normal_other, tok_other, feed_pack, place, windows = together(
        heads, vec, before, after, normal_other, tok_other, feed_pack, place, windows)
    own = [passed_along(before, 1), before, normal, after, passed_along(after, -1)]
    other = [None, swapped(before), normal_other, swapped(after), None]
    feed_weights = lax.all_gather(feed_pack, "batch", axis=0, tiled=True)
    *near_parts, q, qT = project((1, 2, 3), place, own, other, vec, heads)
    own[0], own[4], near_parts = together(own[0], own[4], near_parts)
    other[0], other[4] = swapped(own[0]), swapped(own[4])
    k, v, kT, vT = project((0, 4), place, own, other, vec, heads, near_parts)
    (oT0, low0, lse0), (oT1, low1, lse1) = (
        attend(m, info, qT, k, vT, key_rows, query_rows) for m, (info, key_rows, query_rows, _) in enumerate(windows))

    theirs = swapped(jnp.stack([low0, low1]))
    middle, hidden_two, hidden_other = middle_step(core_arg, feed_weights, low0, low1, theirs, tok, tok_other, vec)
    mine, partial, feed_grads = feed_forward(hidden_two, hidden_other, cot, swapped(cot), feed_weights)
    feed_grads = lax.all_to_all(feed_grads.reshape(64, 80, 640), ("batch", "z", "x"), 0, 0, tiled=True)
    block_out, grad_middle, branch, g_two = after_feed(middle, mine, swapped(partial), cot, vec)

    do, doT, g_out = branch_step(core_arg, branch, swapped(branch), feed_weights, low0, low1, theirs)
    dq, dk, dv = zip(*(
        attend_back(m, info, qT, q, k, kT, v, doT, do, oT, lse, key_rows, query_rows)
        for m, ((info, key_rows, query_rows, _), oT, lse) in enumerate(zip(windows, (oT0, oT1), (lse0, lse1)))))
    mine, theirs, tail = project_back(place, own, other, vec, heads, dq, dk, dv, g_out, g_two)
    feed_grads, mine, theirs, tail = together(feed_grads, mine, theirs, tail)

    feed = jnp.sum(feed_grads.astype(f32), axis=0).astype(bf16)
    tail = lax.all_to_all(tail, ("batch", "z", "x"), 0, 0, tiled=True)
    feed = lax.all_gather(feed, ("z", "x"), axis=0, tiled=True).reshape(16, 80, 640)
    theirs = swapped(theirs)
    sums = [mine[j].astype(f32) + theirs[j].astype(f32) for j in range(5)]
    right, left = passed_along(sums[4].astype(bf16), 1), passed_along(sums[0].astype(bf16), -1)
    tail, right, left = together(tail, right, left)
    right, left = (right.astype(f32) + sums[3]).astype(bf16), (left.astype(f32) + sums[1]).astype(bf16)
    tail, right, left = together(jnp.sum(tail.astype(f32), axis=0).astype(bf16), right, left)
    right, left = passed_along(right, 1), passed_along(left, -1)
    tail = gathered(tail, "x").reshape(160, 384)
    tail = gathered(tail, "z").reshape(16, 40, 384)
    tail, right, left = together(tail, right, left)
    d_one = (sums[2] + right.astype(f32) + left.astype(f32)).reshape(512, 640)
    n_one, r_one = moments(tok.reshape(512, 640).astype(f32))
    grad_tokens = (grad_middle + norm_back(d_one, n_one, r_one, vec[0:1])).astype(bf16)
    tail, grad_tokens, feed = together(tail, grad_tokens, feed)
    grad_qkv, grad_out, spare = final_heads(core_arg, tail, swapped(tail))
    grad_up, grad_down = final_feed(core_arg, feed, swapped(feed))
    return (
        block_out.reshape(2, 1, 256, 640), grad_tokens.reshape(2, 1, 256, 640), spare[:, 0], spare[:, 1], grad_qkv, grad_out,
        spare[:, 2], spare[:, 3], grad_up, grad_down)


def solution(mesh):
    fine = Mesh(mesh.devices.reshape(4, 4, 4, 2), ("batch", "z", "x", "core"))
    rows = P(None, "batch", ("z", "x", "core"), None)
    one, two = P("batch"), P("batch", None)
    return jax.shard_map(
        body,
        mesh=fine,
        in_specs=(rows, P(None, "batch", None), one, one, two, two, one, one, two, two, rows),
        out_specs=(rows, rows, one, one, two, two, one, one, two, two),
        check_vma=False,
    )
```

```python
import math

import jax
import jax.numpy as jnp
from jax import lax
from jax.experimental import pallas as pl
from jax.experimental.pallas import tpu as pltpu
from jax.sharding import Mesh
from jax.sharding import PartitionSpec as P

HEAD_DIM = 32
SCALE = HEAD_DIM ** -0.5
LOG2E = math.log2(math.e)
C2 = SCALE * LOG2E
BIG = 1e30
TILE = 256
EPSILON = 1e-05
PAIRS = 5
SHORT, LONG = 384, 1152
f32, bf16 = jnp.float32, jnp.bfloat16
NT = (((1,), (1,)), ((), ()))


def pair_offset(info_ref):
    p = pl.program_id(0)
    sub = jnp.where(p == PAIRS - 1, info_ref[0], lax.rem(p, 2))
    return sub * (2 * HEAD_DIM)


def split3(v):
    a = v.astype(bf16)
    r = v - a.astype(f32)
    b = r.astype(bf16)
    d = (r - b.astype(f32)).astype(bf16)
    return a, b, d


def rows_masked(xT, off):
    row = lax.broadcasted_iota(jnp.int32, xT.shape, 0) - off
    xf = xT.astype(f32)
    return [jnp.where((row >= HEAD_DIM * j) & (row < HEAD_DIM * (j + 1)), xf, 0.0).astype(bf16) for j in range(2)]


def lanes_masked(x, off):
    lane = lax.broadcasted_iota(jnp.int32, x.shape, 1) - off
    xf = x.astype(f32)
    return [jnp.where((lane >= HEAD_DIM * j) & (lane < HEAD_DIM * (j + 1)), xf, 0.0).astype(bf16) for j in range(2)]


def attend_kernel(info_ref, qT_ref, k_ref, vT_ref, kaug_ref, qaugT_ref, oT_ref, o_ref, l_ref, rhs):
    off = pair_offset(info_ref)
    oT_ref[...] = jnp.where(lax.rem(pl.program_id(0), 2) == 0, 0.0, oT_ref[...])
    for t in range(2):
        cols = slice(t * TILE, (t + 1) * TILE)
        masked = rows_masked(qT_ref[:, cols], off)
        for j in range(2):
            rhs[0:128, j * TILE:(j + 1) * TILE] = masked[j]
            rhs[128:256, j * TILE:(j + 1) * TILE] = qaugT_ref[:, cols]
        start = info_ref[1 + t]
        need = info_ref[3 + t]

        def block(first, size):
            def step(i, carry):
                row = pl.multiple_of(first + i * size, 128)
                lhs = jnp.concatenate([k_ref[pl.ds(row, size), :], kaug_ref[pl.ds(row, size), :]], axis=1)
                raw = [jnp.dot(lhs, rhs[:, j * TILE:(j + 1) * TILE], preferred_element_type=f32) for j in range(2)]
                out = []
                for j in range(2):
                    m, l, o = carry[j]
                    s = raw[j] * C2
                    m_new = jnp.maximum(m, jnp.max(s, axis=0, keepdims=True))
                    alpha = jnp.exp2(m - m_new)
                    p = jnp.exp2(s - m_new)
                    vT = vT_ref[pl.ds(pl.multiple_of(off + j * HEAD_DIM, HEAD_DIM), HEAD_DIM), pl.ds(row, size)]
                    out.append((m_new, l * alpha + jnp.sum(p, axis=0, keepdims=True),
                                o * alpha + jnp.dot(vT, p.astype(bf16), preferred_element_type=f32)))
                return tuple(out)
            return step

        def finish(state):
            for j in range(2):
                m, l, o = state[j]
                oT_ref[pl.ds(pl.multiple_of(off + j * HEAD_DIM, HEAD_DIM), HEAD_DIM), cols] = o * (1.0 / l)
                l_ref[0, j:j + 1, cols] = m + jnp.log2(l)

        init = tuple((jnp.full((1, TILE), -1e38, f32), jnp.zeros((1, TILE), f32), jnp.zeros((HEAD_DIM, TILE), f32)) for _ in range(2))

        longs = lax.div(need, LONG)
        state = lax.fori_loop(0, longs, block(start, LONG), init)
        finish(lax.fori_loop(0, lax.div(need - longs * LONG, SHORT), block(start + longs * LONG, SHORT), state))

    o_ref[...] = oT_ref[...].T.astype(bf16)


def attend(m, info, qT, k, vT, kaug, qaugT):
    win, nq = k.shape[1], qT.shape[2]
    qT, k, vT = stay(qT, k, vT)
    return pl.pallas_call(
        attend_kernel,
        out_shape=(jax.ShapeDtypeStruct((384, nq), f32), jax.ShapeDtypeStruct((nq, 384), bf16), jax.ShapeDtypeStruct((PAIRS, 8, nq), f32)),
        grid_spec=pltpu.PrefetchScalarGridSpec(
            num_scalar_prefetch=1, grid=(PAIRS,),
            in_specs=[
                pl.BlockSpec((None, 128, nq), lambda p, *_: (m, p // 2, 0)),
                pl.BlockSpec((None, win, 128), lambda p, *_: (m, 0, p // 2)),
                pl.BlockSpec((None, 128, win), lambda p, *_: (m, p // 2, 0)),
                pl.BlockSpec((win, 128), lambda p, *_: (0, 0)),
                pl.BlockSpec((128, nq), lambda p, *_: (0, 0)),
            ],
            out_specs=[
                pl.BlockSpec((128, nq), lambda p, *_: (p // 2, 0)),
                pl.BlockSpec((nq, 128), lambda p, *_: (0, p // 2)),
                pl.BlockSpec((1, 8, nq), lambda p, *_: (p, 0, 0)),
            ],
            scratch_shapes=[pltpu.VMEM((256, 2 * TILE), bf16)],
        ),
        compiler_params=pltpu.CompilerParams(vmem_limit_bytes=28 << 20),
        cost_estimate=pl.CostEstimate(flops=int(20 * 10**9 * 0.02), bytes_accessed=0, transcendentals=0),
        name="attend",
    )(info, qT, k, vT, kaug, qaugT)


def attend_back_kernel(info_ref, qT_ref, q_ref, k_ref, kT_ref, v_ref, doT_ref, do_ref, oT_ref, l_ref, kaug_ref, qaugT_ref,
                       dq_ref, dk_ref, dv_ref, dqT_ref, rhs_s, rhs_d, q_stk, do_stk, dk_acc, dv_acc):
    p_id = pl.program_id(0)
    off = pair_offset(info_ref)

    @pl.when(lax.rem(p_id, 2) == 0)
    def _():
        dqT_ref[...] = jnp.zeros_like(dqT_ref)
        dk_acc[...] = jnp.zeros_like(dk_acc)
        dv_acc[...] = jnp.zeros_like(dv_acc)

    for t in range(2):
        cols = slice(t * TILE, (t + 1) * TILE)
        masked_q = rows_masked(qT_ref[:, cols], off)
        masked_do = rows_masked(doT_ref[:, cols], off)
        lane_q = lanes_masked(q_ref[cols, :], off)
        lane_do = lanes_masked(do_ref[cols, :], off)
        for j in range(2):
            part = slice(j * TILE, (j + 1) * TILE)
            head = pl.ds(pl.multiple_of(off + j * HEAD_DIM, HEAD_DIM), HEAD_DIM)
            delta = jnp.sum(doT_ref[head, cols].astype(f32) * oT_ref[head, cols], axis=0, keepdims=True)
            total = l_ref[0, j:j + 1, cols] * (1.0 / C2)
            rowid = lax.broadcasted_iota(jnp.int32, (64, TILE), 0)
            lp, dp = split3(-total), split3(-delta)
            def pieces(parts):
                x = jnp.zeros((64, TILE), f32)
                for n in range(3):
                    x = jnp.where(rowid == n, parts[n].astype(f32), x)
                return x.astype(bf16)
            rhs_s[0:128, part] = masked_q[j]
            rhs_s[128:192, part] = qaugT_ref[0:64, cols]
            rhs_s[192:256, part] = pieces(lp)
            rhs_d[0:128, part] = masked_do[j]
            rhs_d[128:192, part] = jnp.zeros((64, TILE), bf16)
            rhs_d[192:256, part] = pieces(dp)
            q_stk[part, :] = lane_q[j]
            do_stk[part, :] = lane_do[j]
        start = info_ref[1 + t]
        need = info_ref[3 + t]

        def block(first, size):
            def step(i, carry):
                row = pl.multiple_of(first + i * size, 128)
                rows = pl.ds(row, size)
                aug = kaug_ref[rows, :]
                lhs_k = jnp.concatenate([k_ref[rows, :], aug], axis=1)
                lhs_v = jnp.concatenate([v_ref[rows, :], aug], axis=1)
                out, dv, dk = [], dv_acc[rows, :], dk_acc[rows, :]
                for j in range(2):
                    part = slice(j * TILE, (j + 1) * TILE)
                    s = jnp.dot(lhs_k, rhs_s[:, part], preferred_element_type=f32)
                    dp = jnp.dot(lhs_v, rhs_d[:, part], preferred_element_type=f32)
                    p = jnp.exp2(s * C2)
                    ds = (p * dp).astype(bf16)
                    dv = dv + jnp.dot(p.astype(bf16), do_stk[part, :], preferred_element_type=f32)
                    dk = dk + jnp.dot(ds, q_stk[part, :], preferred_element_type=f32)
                    kT = kT_ref[pl.ds(pl.multiple_of(off + j * HEAD_DIM, HEAD_DIM), HEAD_DIM), rows]
                    out.append(carry[j] + jnp.dot(kT, ds, preferred_element_type=f32))
                dv_acc[rows, :] = dv
                dk_acc[rows, :] = dk
                return tuple(out)
            return step

        def finish(dqs):
            for j in range(2):
                dqT_ref[pl.ds(pl.multiple_of(off + j * HEAD_DIM, HEAD_DIM), HEAD_DIM), cols] = dqs[j] * SCALE

        init = tuple(jnp.zeros((HEAD_DIM, TILE), f32) for _ in range(2))

        longs = lax.div(need, LONG)
        state = lax.fori_loop(0, longs, block(start, LONG), init)
        finish(lax.fori_loop(0, lax.div(need - longs * LONG, SHORT), block(start + longs * LONG, SHORT), state))
    @pl.when((lax.rem(p_id, 2) == 1) | (p_id == PAIRS - 1))
    def _():
        dq_ref[...] = dqT_ref[...].T.astype(bf16)
        dk_ref[...] = (dk_acc[...] * SCALE).astype(bf16)
        dv_ref[...] = dv_acc[...].astype(bf16)


def attend_back(m, info, qT, q, k, kT, v, doT, do, oT, lse, kaug, qaugT):
    win, nq = k.shape[1], qT.shape[2]
    qT, q, k, kT, v = stay(qT, q, k, kT, v)
    wide = pl.BlockSpec((128, nq), lambda p, *_: (p // 2, 0))
    tall = pl.BlockSpec((nq, 128), lambda p, *_: (0, p // 2))
    keys = pl.BlockSpec((win, 128), lambda p, *_: (0, p // 2))
    wide_m = pl.BlockSpec((None, 128, nq), lambda p, *_: (m, p // 2, 0))
    tall_m = pl.BlockSpec((None, nq, 128), lambda p, *_: (m, 0, p // 2))
    keys_m = pl.BlockSpec((None, win, 128), lambda p, *_: (m, 0, p // 2))
    return pl.pallas_call(
        attend_back_kernel,
        out_shape=tuple(pltpu.MemorySpace.VMEM(d, bf16) for d in ((nq, 384), (win, 384), (win, 384))),
        grid_spec=pltpu.PrefetchScalarGridSpec(
            num_scalar_prefetch=1, grid=(PAIRS,),
            in_specs=[wide_m, tall_m, keys_m, pl.BlockSpec((None, 128, win), lambda p, *_: (m, p // 2, 0)), keys_m,
                      pl.BlockSpec((128, nq), lambda p, *_: (p // 2, m)), pl.BlockSpec((nq, 128), lambda p, *_: (m, p // 2)), wide,
                      pl.BlockSpec((1, 8, nq), lambda p, *_: (p, 0, 0)),
                      pl.BlockSpec((win, 128), lambda p, *_: (0, 0)), pl.BlockSpec((128, nq), lambda p, *_: (0, 0))],
            out_specs=[tall, keys, keys],
            scratch_shapes=[pltpu.VMEM((128, nq), f32), pltpu.VMEM((256, 2 * TILE), bf16), pltpu.VMEM((256, 2 * TILE), bf16),
                            pltpu.VMEM((2 * TILE, 128), bf16), pltpu.VMEM((2 * TILE, 128), bf16),
                            pltpu.VMEM((win, 128), f32), pltpu.VMEM((win, 128), f32)],
        ),
        compiler_params=pltpu.CompilerParams(vmem_limit_bytes=32 << 20),
        cost_estimate=pl.CostEstimate(flops=int(40 * 10**9 * 0.02), bytes_accessed=0, transcendentals=0),
        name="attend_back",
    )(info, qT, q, k, kT, v, doT, do, oT, lse, kaug, qaugT)


def moments(x):
    centred = x - jnp.mean(x, axis=-1, keepdims=True)
    r = lax.rsqrt(jnp.mean(centred * centred, axis=-1, keepdims=True) + EPSILON)
    return centred * r, r


def norm_back(grad, n, r, gain):
    e = grad * gain
    return r * (e - jnp.mean(e, axis=-1, keepdims=True) - n * jnp.mean(e * n, axis=-1, keepdims=True))


def call(kernel, out_shape, name, flops=10**9, limit=48, **spec):
    return pl.pallas_call(
        kernel, out_shape=out_shape, name=name,
        compiler_params=pltpu.CompilerParams(vmem_limit_bytes=limit << 20),
        cost_estimate=pl.CostEstimate(flops=int(flops * 0.02), bytes_accessed=0, transcendentals=0), **spec)


def shape(*dims, dtype=bf16):
    return jax.ShapeDtypeStruct(dims, dtype)


def far(*dims, dtype=bf16):
    return pltpu.MemorySpace.HBM(dims, dtype)


def stay(*arrays):
    return [pltpu.with_memory_space_constraint(a, pltpu.MemorySpace.HBM) for a in arrays]


def near_by(*arrays):
    return [pltpu.with_memory_space_constraint(a, pltpu.MemorySpace.VMEM) for a in arrays]


def scalar_first(grid, in_specs, out_specs, scratch=()):
    return dict(grid_spec=pltpu.PrefetchScalarGridSpec(
        num_scalar_prefetch=1, grid=grid, in_specs=in_specs, out_specs=out_specs, scratch_shapes=list(scratch)))


def full(*dims):
    return pl.BlockSpec(dims, lambda *_: (0,) * len(dims))


def pack_heads_kernel(core_ref, qkv_ref, vec_ref, heads_ref):
    for part in range(3):
        near = pl.ds(pl.multiple_of(640 * part + 256 * core_ref[0], 128), 256)
        heads_ref[:, 384 * part:384 * part + 256] = qkv_ref[:, near]
        heads_ref[:, 384 * part + 256:384 * (part + 1)] = qkv_ref[:, 640 * part + 512:640 * (part + 1)]
    heads_ref[:, 1152:1280] = vec_ref[...]


def pack_heads(core, w_qkv, vectors):
    return call(pack_heads_kernel, shape(160, 1280), "pack_heads", 10**6, 8, **scalar_first(
        (1,), [full(160, 1920), full(160, 128)], full(160, 1280)))(core, w_qkv, vectors)


def turn_kernel(vec_ref, rows_ref):
    rows_ref[...] = vec_ref[...].astype(f32).T[:16]


def vector_rows(heads):
    return call(turn_kernel, shape(16, 640, dtype=f32), "vector_rows", 10**12, 8, grid=(1,),
                in_specs=[pl.BlockSpec((640, 128), lambda i: (0, 9))], out_specs=full(16, 640))(*stay(heads))


def pack_feed_kernel(core_ref, out_ref, up_ref, down_ref, feed_ref):
    core = core_ref[0]
    feed_ref[:, 5120:5760] = out_ref[...]
    for f in range(4):
        feed_ref[:, 640 * f:640 * (f + 1)] = up_ref[:, pl.ds(pl.multiple_of(1280 * f + 640 * core, 128), 640)]
        feed_ref[:, 2560 + 640 * f:2560 + 640 * (f + 1)] = down_ref[pl.ds(pl.multiple_of(640 * core + 160 * f, 32), 160), :]


def pack_feed(core, w_out, w_up, w_down):
    return call(pack_feed_kernel, far(160, 5760), "pack_feed", 10**6, 16, **scalar_first(
        (1,), [full(160, 640), full(160, 5120), full(1280, 640)], full(160, 5760)))(core, *stay(w_out, w_up, w_down))


def rows_in_order(core, mine_ref, theirs_ref, x_ref):
    for c, (first, second) in enumerate(((mine_ref, theirs_ref), (theirs_ref, mine_ref))):
        @pl.when(core == c)
        def _():
            x_ref[0:256, :], x_ref[256:512, :] = first[...], second[...]


def normal_kernel(tok_ref, n_ref):
    for m in range(2):
        n_ref[m] = moments(tok_ref[m].astype(f32))[0].astype(bf16)


def normal_rows(tok):
    return call(normal_kernel, shape(2, 256, 640), "normal_rows", 10**6, 8, grid=(1,), in_specs=[full(2, 256, 640)], out_specs=full(2, 256, 640))(tok)


def project_kernel(chips, place_ref, *refs):
    n = len(chips)
    own_refs, other_refs = refs[:n], refs[n:2 * n]
    vec_ref, w_ref = refs[2 * n:2 * n + 2]
    k_ref, v_ref, kT_ref, vT_ref = refs[-6 - 2 * (n == 3):][:4]
    x_ref, hid_ref = refs[-2:]
    m, step = pl.program_id(0), pl.program_id(1)
    block = sum(jnp.where(step == i, chip, 0) for i, chip in enumerate(chips))
    needed = (block >= place_ref[1 + 2 * m]) & (block < place_ref[2 + 2 * m])

    @pl.when(jnp.logical_not(needed))
    def _():
        for ref in (k_ref, v_ref, kT_ref, vT_ref):
            ref[...] = jnp.zeros_like(ref)

    @pl.when(needed)
    def _():
        for j in range(n):
            @pl.when(step == j)
            def _():
                rows_in_order(place_ref[0], own_refs[j].at[m], other_refs[j].at[m], x_ref)

        hidden = (x_ref[...].astype(f32) * vec_ref[0:1, :] + vec_ref[1:2, :]).astype(bf16)
        hid_ref[...] = hidden
        kv = jnp.dot(hidden, w_ref[:, 384:], preferred_element_type=f32)
        low = kv.astype(bf16)
        k_ref[0] = low[:, :384]
        v_ref[0] = low[:, 384:]
        turned = kv.T.astype(bf16)
        kT_ref[0] = turned[:384]
        vT_ref[0] = turned[384:]

    if n == 3:
        q_ref, qT_ref = refs[-4:-2]

        @pl.when(step == 1)
        def _():
            q = jnp.dot(hid_ref[...], w_ref[:, :384], preferred_element_type=f32)
            q_ref[0] = q.astype(bf16)
            qT_ref[0] = q.T.astype(bf16)


def project(chips, place, own, other, vec, w, earlier=()):
    n = len(chips)
    chip = (lambda b: b + 1) if n == 3 else (lambda b: 4 * b)
    tall = pl.BlockSpec((1, 512, 384), lambda m, b, *_: (m, chip(b), 0))
    wide = pl.BlockSpec((1, 384, 512), lambda m, b, *_: (m, 0, chip(b)))
    shapes = [far(2, 2560, 384), far(2, 2560, 384), far(2, 384, 2560), far(2, 384, 2560)]
    specs = [tall, tall, wide, wide]
    if n == 3:
        shapes += [far(2, 512, 384), far(2, 384, 512)]
        specs += [pl.BlockSpec((1, 512, 384), lambda m, *_: (m, 0, 0)), pl.BlockSpec((1, 384, 512), lambda m, *_: (m, 0, 0))]
    own, other = [own[c] for c in chips], [other[c] for c in chips]
    return call(
        lambda *refs: project_kernel(chips, *refs), shapes, "project", 5 * 10**9, 28,
        input_output_aliases={2 * n + 3 + i: i for i in range(len(earlier))}, **scalar_first(
            (2, n), [full(2, 256, 640)] * (2 * n) + [full(16, 640), full(640, 1152)] + [pl.BlockSpec(memory_space=pl.ANY)] * len(earlier),
            specs, [pltpu.VMEM((512, 640), bf16), pltpu.VMEM((512, 640), bf16)]))(place, *own, *other, *stay(vec, w), *earlier)


def heads_joined(core, mine, theirs):
    first, second = (jnp.where(core == 0, a, b) for a, b in ((mine, theirs), (theirs, mine)))
    return jnp.concatenate([first[:, :256], second[:, :256], first[:, 256:] + second[:, 256:]], axis=1)


def middle_kernel(core_ref, w_ref, low0_ref, low1_ref, theirs_ref, tok_ref, tok2_ref, vec_ref, mid_ref, hid_ref, hid2_ref):
    core = core_ref[0]
    for m, low_ref in enumerate((low0_ref, low1_ref)):
        attended = heads_joined(core, low_ref[...].astype(f32), theirs_ref[m].astype(f32)).astype(bf16)
        branch = jnp.dot(attended, w_ref[...], preferred_element_type=f32)
        mine = jnp.where(core == 0, branch[:256], branch[256:]) + tok_ref[m].astype(f32)
        theirs = jnp.where(core == 0, branch[256:], branch[:256]) + tok2_ref[m].astype(f32)
        part = slice(256 * m, 256 * (m + 1))
        mid_ref[part, :] = mine
        hid_ref[part, :] = (moments(mine)[0] * vec_ref[2:3, :] + vec_ref[3:4, :]).astype(bf16)
        hid2_ref[part, :] = (moments(theirs)[0] * vec_ref[2:3, :] + vec_ref[3:4, :]).astype(bf16)


W_OUT = pl.BlockSpec((640, 640), lambda *_: (0, 8))


def middle_step(core, weights, *args):
    return call(middle_kernel, (far(512, 640, dtype=f32), *(pltpu.MemorySpace.VMEM((512, 640), bf16),) * 2), "middle", 10**9, 20, **scalar_first(
        (1,), [W_OUT] + [full(*a.shape) for a in args], [full(512, 640)] * 3))(core, *stay(weights), *args[:-1], *stay(args[-1]))


def feed_kernel(h_ref, h2_ref, cot_ref, cot2_ref, up_ref, down_ref, mine_ref, theirs_ref, g_ref, h, cot, hT, cT, out, dh):
    chunk = pl.program_id(0)

    @pl.when(chunk == 0)
    def _():
        h[0:512, :], h[512:1024, :] = h_ref[...], h2_ref[...]
        cot[0:512, :], cot[512:1024, :] = cot_ref[...], cot2_ref[...]
        hT[...] = h[...].astype(f32).T.astype(bf16)
        cT[...] = cot[...].astype(f32).T.astype(bf16)
        out[...] = jnp.zeros_like(out)
        dh[...] = jnp.zeros_like(dh)

    up_w = up_ref[...]
    down_w = jnp.concatenate([down_ref[160 * y:160 * (y + 1), 640 * i:640 * (i + 1)] for y in range(2) for i in range(4)], axis=0)
    acts, d_ups = [], []
    for t in range(4):
        rows = slice(256 * t, 256 * (t + 1))
        u = jnp.dot(h[rows, :], up_w, preferred_element_type=f32)
        d_act = lax.dot_general(cot[rows, :], down_w, NT, preferred_element_type=f32)
        cdf = 0.5 * (1.0 + lax.erf(u * (2.0 ** -0.5)))
        pdf = jnp.exp(u * u * -0.5) * ((2.0 * math.pi) ** -0.5)
        act = (u * cdf).astype(bf16)
        d_up = (d_act * (cdf + u * pdf)).astype(bf16)
        out[rows, :] += jnp.dot(act, down_w, preferred_element_type=f32)
        dh[rows, :] += lax.dot_general(d_up, up_w, NT, preferred_element_type=f32)
        acts.append(act)
        d_ups.append(d_up)
    g_up = jnp.dot(hT[...], jnp.concatenate(d_ups, axis=0), preferred_element_type=f32).astype(bf16)
    g_down = jnp.dot(cT[...], jnp.concatenate(acts, axis=0), preferred_element_type=f32).T.astype(bf16)
    for f in range(2):
        for y in range(4):
            for i in range(2):
                g_ref[y, 4 * chunk + 2 * f + i] = g_up[160 * y + 80 * i:160 * y + 80 * (i + 1), 640 * f:640 * (f + 1)]
        for i in range(8):
            g_ref[2 * chunk + f, 8 + i] = g_down[640 * f + 80 * i:640 * f + 80 * (i + 1)]

    @pl.when(chunk == 1)
    def _():
        mine_ref[0], mine_ref[1] = out[0:512, :].astype(bf16), dh[0:512, :].astype(bf16)
        theirs_ref[0], theirs_ref[1] = out[512:1024, :].astype(bf16), dh[512:1024, :].astype(bf16)


def feed_forward(h, h2, cot, cot2, weights):
    return call(
        feed_kernel,
        (*(pltpu.MemorySpace.VMEM((2, 512, 640), bf16),) * 2, far(4, 16, 80, 640)),
        "feed_forward", 30 * 10**9, 48, grid=(2,),
        in_specs=[pl.BlockSpec(memory_space=pltpu.VMEM)] * 2 + [full(512, 640), pl.BlockSpec(memory_space=pltpu.VMEM), pl.BlockSpec((640, 1280), lambda f: (0, f)), pl.BlockSpec((320, 2560), lambda f: (f, 1))],
        out_specs=[pl.BlockSpec(memory_space=pltpu.VMEM)] * 2 + [full(4, 16, 80, 640)],
        scratch_shapes=[pltpu.VMEM((1024, 640), bf16), pltpu.VMEM((1024, 640), bf16), pltpu.VMEM((640, 1024), bf16), pltpu.VMEM((640, 1024), bf16),
                        pltpu.VMEM((1024, 640), f32), pltpu.VMEM((1024, 640), f32)],
    )(*near_by(h, h2), *stay(cot), *near_by(cot2), *stay(weights, weights))


def after_kernel(mid_ref, mine_ref, theirs_ref, cot_ref, vec_ref, block_ref, grad_ref, branch_ref, g_ref):
    @pl.when(pl.program_id(0) == 0)
    def _():
        g_ref[...] = jnp.zeros_like(g_ref)

    middle = mid_ref[...]
    block_ref[...] = (middle + mine_ref[0].astype(f32) + theirs_ref[0].astype(f32)).astype(bf16)
    d_hidden = mine_ref[1].astype(f32) + theirs_ref[1].astype(f32)
    n, r = moments(middle)
    g_ref[0:1, :] += jnp.sum(d_hidden * n, axis=0, keepdims=True)
    g_ref[1:2, :] += jnp.sum(d_hidden, axis=0, keepdims=True)
    grad = cot_ref[...].astype(f32) + norm_back(d_hidden, n, r, vec_ref[2:3, :])
    grad_ref[...] = grad
    branch_ref[...] = grad.astype(bf16)


def after_feed(*args):
    here = pl.BlockSpec(memory_space=pltpu.VMEM)
    return call(
        after_kernel, (far(512, 640), far(512, 640, dtype=f32), shape(512, 640), shape(8, 640, dtype=f32)), "after_feed", 10**9, 16,
        grid=(1,), in_specs=[here] * 4 + [full(16, 640)], out_specs=[full(512, 640), full(512, 640), full(512, 640), full(8, 640)],
    )(*near_by(*args[:4]), *stay(args[4]))


def branch_kernel(core_ref, own_ref, their_ref, w_ref, low0_ref, low1_ref, theirs_ref, do_ref, doT_ref, g_ref):
    core = core_ref[0]
    w = jnp.concatenate([w_ref[pl.ds(pl.multiple_of(256 * core, 256), 256), :], w_ref[512:640, :]], axis=0)
    g = jnp.zeros((640, 384), f32)
    for m in range(2):
        part = slice(256 * m, 256 * (m + 1))
        mine, theirs = own_ref[part, :].astype(f32), their_ref[part, :].astype(f32)
        branch = jnp.concatenate([jnp.where(core == 0, mine, theirs), jnp.where(core == 0, theirs, mine)], axis=0)
        kept = jnp.where(core == 0, branch[:, :384], branch[:, 256:]).astype(bf16)
        branch = branch.astype(bf16)
        rows = slice(512 * m, 512 * (m + 1))
        do = lax.dot_general(branch, w, NT, preferred_element_type=f32)
        do_ref[rows, :] = do.astype(bf16)
        doT_ref[:, rows] = do.T.astype(bf16)
        attended = heads_joined(core, (low0_ref, low1_ref)[m][...].astype(f32), theirs_ref[m].astype(f32))
        g = g + jnp.dot(attended.T.astype(bf16), kept, preferred_element_type=f32)
    g_ref[...] = g.astype(bf16)


def branch_step(core, own, their, weights, *args):
    return call(
        branch_kernel, (shape(1024, 384), shape(384, 1024), shape(640, 384)), "branch", 10**9, 24, **scalar_first(
            (1,), [full(512, 640)] * 2 + [W_OUT] + [full(*a.shape) for a in args], [full(1024, 384), full(384, 1024), full(640, 384)]))(
                core, own, their, *stay(weights), *args)


def project_back_kernel(place_ref, *refs):
    own_refs, other_refs = refs[:5], refs[5:10]
    (vec_ref, w_ref, dq0_ref, dq1_ref, dk0_ref, dk1_ref, dv0_ref, dv1_ref, g_out_ref, g_two_ref,
     mine_ref, theirs_ref, tail_ref, n_ref, d_kv, d_q, d_hid, g_ref, g_vec, slots, arrived) = refs[10:]
    step, core = pl.program_id(0), place_ref[0]
    block, second = lax.rem(step, 5), lax.div(step, 5)
    inside = lambda j, m: (j >= place_ref[1 + 2 * m]) & (j < place_ref[2 + 2 * m])
    needed = inside(block, second)

    def copies(j, m, slot):
        return [pltpu.make_async_copy(refs_of[j].at[m], slots.at[slot, i], arrived.at[slot, i]) for i, refs_of in enumerate((own_refs, other_refs))]

    @pl.when(step == 0)
    def _():
        for m in range(2):
            for j in range(5):
                @pl.when(inside(j, m))
                def _():
                    for copy in copies(j, m, 5 * m + j):
                        copy.start()
        g_ref[...] = jnp.zeros_like(g_ref)
        g_vec[...] = jnp.zeros_like(g_vec)
        g_vec[2:4, :] = g_two_ref[0:2, :]

    @pl.when(jnp.logical_not(needed))
    def _():
        mine_ref[...] = jnp.zeros_like(mine_ref)
        theirs_ref[...] = jnp.zeros_like(theirs_ref)

    @pl.when(needed)
    def _():
        for copy in copies(0, 0, step):
            copy.wait()
        rows_in_order(core, slots.at[step, 0], slots.at[step, 1], n_ref)

    for m, (dq, dk, dv) in enumerate(((dq0_ref, dk0_ref, dv0_ref), (dq1_ref, dk1_ref, dv1_ref))):
        @pl.when(needed & (second == m))
        def _():
            rows = pl.ds(pl.multiple_of(block * 512, 512), 512)
            d_kv[:, :384], d_kv[:, 384:] = dk[rows, :], dv[rows, :]
            d_q[...] = dq[...]

    @pl.when(needed)
    def _():
        n = n_ref[...].astype(f32)
        hiddenT = (n * vec_ref[0:1, :] + vec_ref[1:2, :]).T.astype(bf16)
        d_hid[...] = lax.dot_general(d_kv[...], w_ref[:, 384:1152], NT, preferred_element_type=f32)
        g_ref[:, 384:] += jnp.dot(hiddenT, d_kv[...], preferred_element_type=f32)

        @pl.when(block == 2)
        def _():
            g_ref[:, :384] += jnp.dot(hiddenT, d_q[...], preferred_element_type=f32)
            d_hid[...] += lax.dot_general(d_q[...], w_ref[:, :384], NT, preferred_element_type=f32)

        dh = d_hid[...]
        low = dh.astype(bf16)
        for c, (first, other) in enumerate(((mine_ref, theirs_ref), (theirs_ref, mine_ref))):
            @pl.when(core == c)
            def _():
                first[0, 0], other[0, 0] = low[:256], low[256:]
        g_vec[0:1, :] += jnp.sum(dh * n, axis=0, keepdims=True)
        g_vec[1:2, :] += jnp.sum(dh, axis=0, keepdims=True)

    @pl.when(step == 9)
    def _():
        turned = g_vec[...].T
        lane = lax.broadcasted_iota(jnp.int32, (640, 128), 1) - 64 * (1 - core)
        spare = g_ref[:, 256:384]
        for i in range(4):
            spare = jnp.where(lane == i, turned[:, i:i + 1], spare)
        g_ref[:, 256:384] = spare
        for y in range(4):
            for z in range(4):
                rows = slice(160 * y + 40 * z, 160 * y + 40 * (z + 1))
                for x in range(3):
                    tail_ref[16 * y + 4 * z + x] = g_ref[rows, 384 * x:384 * (x + 1)].astype(bf16)
                tail_ref[16 * y + 4 * z + 3] = g_out_ref[rows, :].astype(bf16)


def project_back(place, own, other, vec, w, dq, dk, dv, g_out, g_two):
    here = pl.BlockSpec(memory_space=pltpu.VMEM)
    part = pl.BlockSpec((1, 1, 256, 640), lambda b, *_: (lax.rem(b, 5), b // 5, 0, 0))
    return call(
        project_back_kernel, (far(5, 2, 256, 640), far(5, 2, 256, 640), far(64, 40, 384)), "project_back", 10**10, 30, **scalar_first(
            (10,), [pl.BlockSpec(memory_space=pl.ANY)] * 10 + [here] * 10, [part, part, full(64, 40, 384)],
            [pltpu.VMEM((512, 640), bf16), pltpu.VMEM((512, 768), bf16), pltpu.VMEM((512, 384), bf16),
             pltpu.VMEM((512, 640), f32), pltpu.VMEM((640, 1152), f32), pltpu.VMEM((8, 640), f32),
             pltpu.VMEM((10, 2, 256, 640), bf16), pltpu.SemaphoreType.DMA((10, 2))]))(
                 place, *stay(*own, *other), *near_by(vec, w, *dq, *dk, *dv, g_out, g_two))


def in_core_order(core_ref, mine, theirs):
    core, mine, theirs = core_ref[0], mine.astype(f32), theirs.astype(f32)
    return jnp.where(core == 0, mine, theirs), jnp.where(core == 0, theirs, mine)


def final_feed_kernel(core_ref, mine_ref, theirs_ref, up_ref, down_ref):
    for i in range(16):
        for c, piece in enumerate(in_core_order(core_ref, mine_ref[i], theirs_ref[i])):
            if i < 8:
                base = 1280 * (i // 2) + 640 * c
                up_ref[80 * (i % 2):80 * (i % 2 + 1), base:base + 640] = piece
            else:
                base = 640 * c + 80 * (i - 8)
                down_ref[base:base + 80, :] = piece


def final_feed(core, mine, theirs):
    return call(final_feed_kernel, (shape(160, 5120, dtype=f32), shape(1280, 640, dtype=f32)), "final_feed", 10**6, 32, **scalar_first(
        (1,), [full(16, 80, 640)] * 2, [full(160, 5120), full(1280, 640)]))(core, mine, theirs)


def final_heads_kernel(core_ref, mine_ref, theirs_ref, qkv_ref, out_ref, vec_ref):
    lane = lax.broadcasted_iota(jnp.int32, (40, 128), 1)
    for z in range(4):
        rows = slice(40 * z, 40 * (z + 1))
        for x in range(4):
            a, b = in_core_order(core_ref, mine_ref[4 * z + x], theirs_ref[4 * z + x])
            if x < 3:
                last = jnp.where(lane < 64, a[:, 256:], b[:, 256:])
                qkv_ref[rows, 640 * x:640 * (x + 1)] = jnp.concatenate([a[:, :256], b[:, :256], last], axis=1)
            else:
                out_ref[rows, :] = jnp.concatenate([a, b[:, 128:]], axis=1)
            if x == 0:
                vec_ref[rows, :] = pltpu.roll(a[:, 256:], 64, 1) + b[:, 256:]


def final_heads(core, mine, theirs):
    return call(
        final_heads_kernel, (shape(160, 1920, dtype=f32), shape(160, 640, dtype=f32), shape(160, 128, dtype=f32)), "final_heads", 10**6, 16,
        **scalar_first((1,), [full(16, 40, 384)] * 2, [full(160, 1920), full(160, 640), full(160, 128)]))(core, mine, theirs)


def shifted(array, axis, by):
    devices = lax.axis_size(axis)
    return lax.ppermute(array, axis, [(i, (i + by) % devices) for i in range(devices)])


def passed_along(array, by):
    devices = lax.axis_size(("z", "x"))
    return lax.ppermute(array, ("z", "x"), [(i, i + by) for i in range(devices) if 0 <= i + by < devices])


def swapped(array):
    return lax.ppermute(array, "core", [(0, 1), (1, 0)])


def pick(array, index):
    return lax.dynamic_index_in_dim(array, index, 0, keepdims=False)


def gathered(array, axis):
    me, devices = lax.axis_index(axis), lax.axis_size(axis)
    out = jnp.zeros((devices,) + array.shape, array.dtype)
    out = lax.dynamic_update_index_in_dim(out, array, me, 0)
    for by in (1, devices - 1, 2):
        out = lax.dynamic_update_index_in_dim(out, shifted(array, axis, by), (me + devices - by) % devices, 0)
    return out


def window_info(length_row, chip, core, win):
    ends = jnp.cumsum(length_row)
    starts = ends - length_row
    base = chip * 512 - 1024
    places = base + jnp.arange(win, dtype=jnp.int32)
    inside = (places[:, None] >= starts[None, :]) & (places[:, None] < ends[None, :])
    ones = jnp.broadcast_to(jnp.arange(64) < 3, (win, 64)).astype(bf16)
    key_rows = jnp.concatenate([jnp.where(inside, 0.0, -BIG).astype(bf16), ones], axis=1)
    own = chip * 512 + jnp.arange(512, dtype=jnp.int32)
    inside_q = (own[None, :] >= starts[:, None]) & (own[None, :] < ends[:, None])
    query_rows = jnp.concatenate([inside_q.astype(bf16), jnp.zeros((64, 512), bf16)], axis=0)
    info = [core]
    sizes = []
    for t in range(2):
        first = chip * 512 + t * TILE
        low = jnp.max(jnp.where(starts <= first, starts, 0)) - base
        high = jnp.min(jnp.where(ends > first + TILE - 1, ends, 1 << 30)) - base
        start = low // 128 * 128
        need = high - start
        size = (need + SHORT - 1) // SHORT * SHORT
        info.append(jnp.minimum(start, win - size))
        sizes.append(size)
    low = jnp.minimum(info[1], info[2]) // 512
    high = (jnp.maximum(info[1] + sizes[0], info[2] + sizes[1]) + 511) // 512
    return jnp.stack(info + sizes).astype(jnp.int32), key_rows, query_rows, [low, high]


def body(tokens, lengths, gain_one, bias_one, w_qkv, w_out, gain_two, bias_two, w_up, w_down, cotangent):
    core, chip = lax.axis_index("core"), lax.axis_index(("z", "x"))
    core_arg = core[None].astype(jnp.int32)
    tok, cot = tokens[:, 0], cotangent[:, 0].reshape(512, 640)
    together = lambda *arrays: lax.optimization_barrier(arrays)

    vectors = jnp.pad(jnp.stack([gain_one, bias_one, gain_two, bias_two], axis=1), ((0, 0), (0, 124)))
    heads, tok_sent = together(pack_heads(core_arg, w_qkv, vectors), tok)
    heads = lax.all_gather(heads, "batch", axis=0, tiled=True)
    vec = vector_rows(heads)
    normal = normal_rows(tok_sent)
    before, after, normal_other, tok_other = passed_along(normal, 1), passed_along(normal, -1), swapped(normal), swapped(tok)
    windows = [window_info(lengths[m, 0], chip, core, 2560) for m in range(2)]
    place = jnp.stack([core] + windows[0][3] + windows[1][3]).astype(jnp.int32)
    feed_pack = pack_feed(core_arg, w_out, w_up, w_down)
    heads, vec, before, after, normal_other, tok_other, feed_pack, place, windows = together(
        heads, vec, before, after, normal_other, tok_other, feed_pack, place, windows)
    own = [passed_along(before, 1), before, normal, after, passed_along(after, -1)]
    other = [None, swapped(before), normal_other, swapped(after), None]
    feed_weights = lax.all_gather(feed_pack, "batch", axis=0, tiled=True)
    *near_parts, q, qT = project((1, 2, 3), place, own, other, vec, heads)
    own[0], own[4], near_parts = together(own[0], own[4], near_parts)
    other[0], other[4] = swapped(own[0]), swapped(own[4])
    k, v, kT, vT = project((0, 4), place, own, other, vec, heads, near_parts)
    (oT0, low0, lse0), (oT1, low1, lse1) = (
        attend(m, info, qT, k, vT, key_rows, query_rows) for m, (info, key_rows, query_rows, _) in enumerate(windows))

    theirs = swapped(jnp.stack([low0, low1]))
    middle, hidden_two, hidden_other = middle_step(core_arg, feed_weights, low0, low1, theirs, tok, tok_other, vec)
    mine, partial, feed_grads = feed_forward(hidden_two, hidden_other, cot, swapped(cot), feed_weights)
    feed_grads = lax.all_to_all(feed_grads.reshape(64, 80, 640), ("batch", "z", "x"), 0, 0, tiled=True)
    block_out, grad_middle, branch, g_two = after_feed(middle, mine, swapped(partial), cot, vec)

    do, doT, g_out = branch_step(core_arg, branch, swapped(branch), feed_weights, low0, low1, theirs)
    dq, dk, dv = zip(*(
        attend_back(m, info, qT, q, k, kT, v, doT, do, oT, lse, key_rows, query_rows)
        for m, ((info, key_rows, query_rows, _), oT, lse) in enumerate(zip(windows, (oT0, oT1), (lse0, lse1)))))
    mine, theirs, tail = project_back(place, own, other, vec, heads, dq, dk, dv, g_out, g_two)
    feed_grads, mine, theirs, tail = together(feed_grads, mine, theirs, tail)

    feed = jnp.sum(feed_grads.astype(f32), axis=0).astype(bf16)
    tail = lax.all_to_all(tail, ("batch", "z", "x"), 0, 0, tiled=True)
    feed = lax.all_gather(feed, ("z", "x"), axis=0, tiled=True).reshape(16, 80, 640)
    theirs = swapped(theirs)
    sums = [mine[j].astype(f32) + theirs[j].astype(f32) for j in range(5)]
    right, left = passed_along(sums[4].astype(bf16), 1), passed_along(sums[0].astype(bf16), -1)
    tail, right, left = together(tail, right, left)
    right, left = (right.astype(f32) + sums[3]).astype(bf16), (left.astype(f32) + sums[1]).astype(bf16)
    tail, right, left = together(jnp.sum(tail.astype(f32), axis=0).astype(bf16), right, left)
    right, left = passed_along(right, 1), passed_along(left, -1)
    tail = gathered(tail, "x").reshape(160, 384)
    tail = gathered(tail, "z").reshape(16, 40, 384)
    tail, right, left = together(tail, right, left)
    d_one = (sums[2] + right.astype(f32) + left.astype(f32)).reshape(512, 640)
    n_one, r_one = moments(tok.reshape(512, 640).astype(f32))
    grad_tokens = (grad_middle + norm_back(d_one, n_one, r_one, vec[0:1])).astype(bf16)
    tail, grad_tokens, feed = together(tail, grad_tokens, feed)
    grad_qkv, grad_out, spare = final_heads(core_arg, tail, swapped(tail))
    grad_up, grad_down = final_feed(core_arg, feed, swapped(feed))
    return (
        block_out.reshape(2, 1, 256, 640), grad_tokens.reshape(2, 1, 256, 640), spare[:, 0], spare[:, 1], grad_qkv, grad_out,
        spare[:, 2], spare[:, 3], grad_up, grad_down)


def solution(mesh):
    fine = Mesh(mesh.devices.reshape(4, 4, 4, 2), ("batch", "z", "x", "core"))
    rows = P(None, "batch", ("z", "x", "core"), None)
    one, two = P("batch"), P("batch", None)
    return jax.shard_map(
        body,
        mesh=fine,
        in_specs=(rows, P(None, "batch", None), one, one, two, two, one, one, two, two, rows),
        out_specs=(rows, rows, one, one, two, two, one, one, two, two),
        check_vma=False,
    )
```

```python
import math

import jax
import jax.numpy as jnp
from jax import lax
from jax.experimental import pallas as pl
from jax.experimental.pallas import tpu as pltpu
from jax.sharding import Mesh
from jax.sharding import PartitionSpec as P

HEAD_DIM = 32
SCALE = HEAD_DIM ** -0.5
LOG2E = math.log2(math.e)
C2 = SCALE * LOG2E
BIG = 1e30
TILE = 256
EPSILON = 1e-05
PAIRS = 5
SHORT, LONG = 384, 1152
f32, bf16 = jnp.float32, jnp.bfloat16
NT = (((1,), (1,)), ((), ()))


def pair_offset(info_ref):
    p = pl.program_id(0)
    sub = jnp.where(p == PAIRS - 1, info_ref[0], lax.rem(p, 2))
    return sub * (2 * HEAD_DIM)


def split3(v):
    a = v.astype(bf16)
    r = v - a.astype(f32)
    b = r.astype(bf16)
    d = (r - b.astype(f32)).astype(bf16)
    return a, b, d


def rows_masked(xT, off):
    row = lax.broadcasted_iota(jnp.int32, xT.shape, 0) - off
    xf = xT.astype(f32)
    return [jnp.where((row >= HEAD_DIM * j) & (row < HEAD_DIM * (j + 1)), xf, 0.0).astype(bf16) for j in range(2)]


def lanes_masked(x, off):
    lane = lax.broadcasted_iota(jnp.int32, x.shape, 1) - off
    xf = x.astype(f32)
    return [jnp.where((lane >= HEAD_DIM * j) & (lane < HEAD_DIM * (j + 1)), xf, 0.0).astype(bf16) for j in range(2)]


def attend_kernel(info_ref, qT_ref, k_ref, vT_ref, kaug_ref, qaugT_ref, oT_ref, o_ref, l_ref, rhs):
    off = pair_offset(info_ref)
    oT_ref[...] = jnp.where(lax.rem(pl.program_id(0), 2) == 0, 0.0, oT_ref[...])
    for t in range(2):
        cols = slice(t * TILE, (t + 1) * TILE)
        masked = rows_masked(qT_ref[:, cols], off)
        for j in range(2):
            rhs[0:128, j * TILE:(j + 1) * TILE] = masked[j]
            rhs[128:256, j * TILE:(j + 1) * TILE] = qaugT_ref[:, cols]
        start = info_ref[1 + t]
        need = info_ref[3 + t]

        def block(first, size):
            def step(i, carry):
                row = pl.multiple_of(first + i * size, 128)
                lhs = jnp.concatenate([k_ref[pl.ds(row, size), :], kaug_ref[pl.ds(row, size), :]], axis=1)
                raw = [jnp.dot(lhs, rhs[:, j * TILE:(j + 1) * TILE], preferred_element_type=f32) for j in range(2)]
                out = []
                for j in range(2):
                    m, l, o = carry[j]
                    s = raw[j] * C2
                    m_new = jnp.maximum(m, jnp.max(s, axis=0, keepdims=True))
                    alpha = jnp.exp2(m - m_new)
                    p = jnp.exp2(s - m_new)
                    vT = vT_ref[pl.ds(pl.multiple_of(off + j * HEAD_DIM, HEAD_DIM), HEAD_DIM), pl.ds(row, size)]
                    out.append((m_new, l * alpha + jnp.sum(p, axis=0, keepdims=True),
                                o * alpha + jnp.dot(vT, p.astype(bf16), preferred_element_type=f32)))
                return tuple(out)
            return step

        def finish(state):
            for j in range(2):
                m, l, o = state[j]
                oT_ref[pl.ds(pl.multiple_of(off + j * HEAD_DIM, HEAD_DIM), HEAD_DIM), cols] = o * (1.0 / l)
                l_ref[0, j:j + 1, cols] = m + jnp.log2(l)

        init = tuple((jnp.full((1, TILE), -1e38, f32), jnp.zeros((1, TILE), f32), jnp.zeros((HEAD_DIM, TILE), f32)) for _ in range(2))

        longs = lax.div(need, LONG)
        state = lax.fori_loop(0, longs, block(start, LONG), init)
        finish(lax.fori_loop(0, lax.div(need - longs * LONG, SHORT), block(start + longs * LONG, SHORT), state))

    o_ref[...] = oT_ref[...].T.astype(bf16)


def attend(m, info, qT, k, vT, kaug, qaugT):
    win, nq = k.shape[1], qT.shape[2]
    qT, k, vT = stay(qT, k, vT)
    return pl.pallas_call(
        attend_kernel,
        out_shape=(jax.ShapeDtypeStruct((384, nq), f32), jax.ShapeDtypeStruct((nq, 384), bf16), jax.ShapeDtypeStruct((PAIRS, 8, nq), f32)),
        grid_spec=pltpu.PrefetchScalarGridSpec(
            num_scalar_prefetch=1, grid=(PAIRS,),
            in_specs=[
                pl.BlockSpec((None, 128, nq), lambda p, *_: (m, p // 2, 0)),
                pl.BlockSpec((None, win, 128), lambda p, *_: (m, 0, p // 2)),
                pl.BlockSpec((None, 128, win), lambda p, *_: (m, p // 2, 0)),
                pl.BlockSpec((win, 128), lambda p, *_: (0, 0)),
                pl.BlockSpec((128, nq), lambda p, *_: (0, 0)),
            ],
            out_specs=[
                pl.BlockSpec((128, nq), lambda p, *_: (p // 2, 0)),
                pl.BlockSpec((nq, 128), lambda p, *_: (0, p // 2)),
                pl.BlockSpec((1, 8, nq), lambda p, *_: (p, 0, 0)),
            ],
            scratch_shapes=[pltpu.VMEM((256, 2 * TILE), bf16)],
        ),
        compiler_params=pltpu.CompilerParams(vmem_limit_bytes=28 << 20),
        cost_estimate=pl.CostEstimate(flops=int(20 * 10**9 * 0.02), bytes_accessed=0, transcendentals=0),
        name="attend",
    )(info, qT, k, vT, kaug, qaugT)


def attend_back_kernel(info_ref, qT_ref, q_ref, k_ref, kT_ref, v_ref, doT_ref, do_ref, oT_ref, l_ref, kaug_ref, qaugT_ref,
                       dq_ref, dk_ref, dv_ref, dqT_ref, rhs_s, rhs_d, q_stk, do_stk, dk_acc, dv_acc):
    p_id = pl.program_id(0)
    off = pair_offset(info_ref)

    @pl.when(lax.rem(p_id, 2) == 0)
    def _():
        dqT_ref[...] = jnp.zeros_like(dqT_ref)
        dk_acc[...] = jnp.zeros_like(dk_acc)
        dv_acc[...] = jnp.zeros_like(dv_acc)

    for t in range(2):
        cols = slice(t * TILE, (t + 1) * TILE)
        masked_q = rows_masked(qT_ref[:, cols], off)
        masked_do = rows_masked(doT_ref[:, cols], off)
        lane_q = lanes_masked(q_ref[cols, :], off)
        lane_do = lanes_masked(do_ref[cols, :], off)
        for j in range(2):
            part = slice(j * TILE, (j + 1) * TILE)
            head = pl.ds(pl.multiple_of(off + j * HEAD_DIM, HEAD_DIM), HEAD_DIM)
            delta = jnp.sum(doT_ref[head, cols].astype(f32) * oT_ref[head, cols], axis=0, keepdims=True)
            total = l_ref[0, j:j + 1, cols] * (1.0 / C2)
            rowid = lax.broadcasted_iota(jnp.int32, (64, TILE), 0)
            lp, dp = split3(-total), split3(-delta)
            def pieces(parts):
                x = jnp.zeros((64, TILE), f32)
                for n in range(3):
                    x = jnp.where(rowid == n, parts[n].astype(f32), x)
                return x.astype(bf16)
            rhs_s[0:128, part] = masked_q[j]
            rhs_s[128:192, part] = qaugT_ref[0:64, cols]
            rhs_s[192:256, part] = pieces(lp)
            rhs_d[0:128, part] = masked_do[j]
            rhs_d[128:192, part] = jnp.zeros((64, TILE), bf16)
            rhs_d[192:256, part] = pieces(dp)
            q_stk[part, :] = lane_q[j]
            do_stk[part, :] = lane_do[j]
        start = info_ref[1 + t]
        need = info_ref[3 + t]

        def block(first, size):
            def step(i, carry):
                row = pl.multiple_of(first + i * size, 128)
                rows = pl.ds(row, size)
                aug = kaug_ref[rows, :]
                lhs_k = jnp.concatenate([k_ref[rows, :], aug], axis=1)
                lhs_v = jnp.concatenate([v_ref[rows, :], aug], axis=1)
                out, dv, dk = [], dv_acc[rows, :], dk_acc[rows, :]
                for j in range(2):
                    part = slice(j * TILE, (j + 1) * TILE)
                    s = jnp.dot(lhs_k, rhs_s[:, part], preferred_element_type=f32)
                    dp = jnp.dot(lhs_v, rhs_d[:, part], preferred_element_type=f32)
                    p = jnp.exp2(s * C2)
                    ds = (p * dp).astype(bf16)
                    dv = dv + jnp.dot(p.astype(bf16), do_stk[part, :], preferred_element_type=f32)
                    dk = dk + jnp.dot(ds, q_stk[part, :], preferred_element_type=f32)
                    kT = kT_ref[pl.ds(pl.multiple_of(off + j * HEAD_DIM, HEAD_DIM), HEAD_DIM), rows]
                    out.append(carry[j] + jnp.dot(kT, ds, preferred_element_type=f32))
                dv_acc[rows, :] = dv
                dk_acc[rows, :] = dk
                return tuple(out)
            return step

        def finish(dqs):
            for j in range(2):
                dqT_ref[pl.ds(pl.multiple_of(off + j * HEAD_DIM, HEAD_DIM), HEAD_DIM), cols] = dqs[j] * SCALE

        init = tuple(jnp.zeros((HEAD_DIM, TILE), f32) for _ in range(2))

        longs = lax.div(need, LONG)
        state = lax.fori_loop(0, longs, block(start, LONG), init)
        finish(lax.fori_loop(0, lax.div(need - longs * LONG, SHORT), block(start + longs * LONG, SHORT), state))
    @pl.when((lax.rem(p_id, 2) == 1) | (p_id == PAIRS - 1))
    def _():
        dq_ref[...] = dqT_ref[...].T.astype(bf16)
        dk_ref[...] = (dk_acc[...] * SCALE).astype(bf16)
        dv_ref[...] = dv_acc[...].astype(bf16)


def attend_back(m, info, qT, q, k, kT, v, doT, do, oT, lse, kaug, qaugT):
    win, nq = k.shape[1], qT.shape[2]
    qT, q, k, kT, v = stay(qT, q, k, kT, v)
    wide = pl.BlockSpec((128, nq), lambda p, *_: (p // 2, 0))
    tall = pl.BlockSpec((nq, 128), lambda p, *_: (0, p // 2))
    keys = pl.BlockSpec((win, 128), lambda p, *_: (0, p // 2))
    wide_m = pl.BlockSpec((None, 128, nq), lambda p, *_: (m, p // 2, 0))
    tall_m = pl.BlockSpec((None, nq, 128), lambda p, *_: (m, 0, p // 2))
    keys_m = pl.BlockSpec((None, win, 128), lambda p, *_: (m, 0, p // 2))
    return pl.pallas_call(
        attend_back_kernel,
        out_shape=tuple(pltpu.MemorySpace.VMEM(d, bf16) for d in ((nq, 384), (win, 384), (win, 384))),
        grid_spec=pltpu.PrefetchScalarGridSpec(
            num_scalar_prefetch=1, grid=(PAIRS,),
            in_specs=[wide_m, tall_m, keys_m, pl.BlockSpec((None, 128, win), lambda p, *_: (m, p // 2, 0)), keys_m,
                      pl.BlockSpec((128, nq), lambda p, *_: (p // 2, m)), pl.BlockSpec((nq, 128), lambda p, *_: (m, p // 2)), wide,
                      pl.BlockSpec((1, 8, nq), lambda p, *_: (p, 0, 0)),
                      pl.BlockSpec((win, 128), lambda p, *_: (0, 0)), pl.BlockSpec((128, nq), lambda p, *_: (0, 0))],
            out_specs=[tall, keys, keys],
            scratch_shapes=[pltpu.VMEM((128, nq), f32), pltpu.VMEM((256, 2 * TILE), bf16), pltpu.VMEM((256, 2 * TILE), bf16),
                            pltpu.VMEM((2 * TILE, 128), bf16), pltpu.VMEM((2 * TILE, 128), bf16),
                            pltpu.VMEM((win, 128), f32), pltpu.VMEM((win, 128), f32)],
        ),
        compiler_params=pltpu.CompilerParams(vmem_limit_bytes=32 << 20),
        cost_estimate=pl.CostEstimate(flops=int(40 * 10**9 * 0.02), bytes_accessed=0, transcendentals=0),
        name="attend_back",
    )(info, qT, q, k, kT, v, doT, do, oT, lse, kaug, qaugT)


def moments(x):
    centred = x - jnp.mean(x, axis=-1, keepdims=True)
    r = lax.rsqrt(jnp.mean(centred * centred, axis=-1, keepdims=True) + EPSILON)
    return centred * r, r


def norm_back(grad, n, r, gain):
    e = grad * gain
    return r * (e - jnp.mean(e, axis=-1, keepdims=True) - n * jnp.mean(e * n, axis=-1, keepdims=True))


def call(kernel, out_shape, name, flops=10**9, limit=48, **spec):
    return pl.pallas_call(
        kernel, out_shape=out_shape, name=name,
        compiler_params=pltpu.CompilerParams(vmem_limit_bytes=limit << 20),
        cost_estimate=pl.CostEstimate(flops=int(flops * 0.02), bytes_accessed=0, transcendentals=0), **spec)


def shape(*dims, dtype=bf16):
    return jax.ShapeDtypeStruct(dims, dtype)


def far(*dims, dtype=bf16):
    return pltpu.MemorySpace.HBM(dims, dtype)


def stay(*arrays):
    return [pltpu.with_memory_space_constraint(a, pltpu.MemorySpace.HBM) for a in arrays]


def near_by(*arrays):
    return [pltpu.with_memory_space_constraint(a, pltpu.MemorySpace.VMEM) for a in arrays]


def scalar_first(grid, in_specs, out_specs, scratch=()):
    return dict(grid_spec=pltpu.PrefetchScalarGridSpec(
        num_scalar_prefetch=1, grid=grid, in_specs=in_specs, out_specs=out_specs, scratch_shapes=list(scratch)))


def full(*dims):
    return pl.BlockSpec(dims, lambda *_: (0,) * len(dims))


def pack_heads_kernel(core_ref, qkv_ref, vec_ref, heads_ref):
    for part in range(3):
        near = pl.ds(pl.multiple_of(640 * part + 256 * core_ref[0], 128), 256)
        heads_ref[:, 384 * part:384 * part + 256] = qkv_ref[:, near]
        heads_ref[:, 384 * part + 256:384 * (part + 1)] = qkv_ref[:, 640 * part + 512:640 * (part + 1)]
    heads_ref[:, 1152:1280] = vec_ref[...]


def pack_heads(core, w_qkv, vectors):
    return call(pack_heads_kernel, shape(160, 1280), "pack_heads", 10**6, 8, **scalar_first(
        (1,), [full(160, 1920), full(160, 128)], full(160, 1280)))(core, w_qkv, vectors)


def turn_kernel(vec_ref, rows_ref):
    rows_ref[...] = vec_ref[...].astype(f32).T[:16]


def vector_rows(heads):
    return call(turn_kernel, shape(16, 640, dtype=f32), "vector_rows", 10**12, 8, grid=(1,),
                in_specs=[pl.BlockSpec((640, 128), lambda i: (0, 9))], out_specs=full(16, 640))(*stay(heads))


def pack_feed_kernel(core_ref, out_ref, up_ref, down_ref, feed_ref):
    core = core_ref[0]
    feed_ref[:, 5120:5760] = out_ref[...]
    for f in range(4):
        feed_ref[:, 640 * f:640 * (f + 1)] = up_ref[:, pl.ds(pl.multiple_of(1280 * f + 640 * core, 128), 640)]
        feed_ref[:, 2560 + 640 * f:2560 + 640 * (f + 1)] = down_ref[pl.ds(pl.multiple_of(640 * core + 160 * f, 32), 160), :]


def pack_feed(core, w_out, w_up, w_down):
    return call(pack_feed_kernel, far(160, 5760), "pack_feed", 10**6, 16, **scalar_first(
        (1,), [full(160, 640), full(160, 5120), full(1280, 640)], full(160, 5760)))(core, *stay(w_out, w_up, w_down))


def rows_in_order(core, mine_ref, theirs_ref, x_ref):
    for c, (first, second) in enumerate(((mine_ref, theirs_ref), (theirs_ref, mine_ref))):
        @pl.when(core == c)
        def _():
            x_ref[0:256, :], x_ref[256:512, :] = first[...], second[...]


def normal_kernel(tok_ref, n_ref):
    for m in range(2):
        n_ref[m] = moments(tok_ref[m].astype(f32))[0].astype(bf16)


def normal_rows(tok):
    return call(normal_kernel, shape(2, 256, 640), "normal_rows", 10**6, 8, grid=(1,), in_specs=[full(2, 256, 640)], out_specs=full(2, 256, 640))(tok)


def project_kernel(chips, place_ref, *refs):
    n = len(chips)
    own_refs, other_refs = refs[:n], refs[n:2 * n]
    vec_ref, w_ref = refs[2 * n:2 * n + 2]
    k_ref, v_ref, kT_ref, vT_ref = refs[-6 - 2 * (n == 3):][:4]
    x_ref, hid_ref = refs[-2:]
    m, step = pl.program_id(0), pl.program_id(1)
    block = sum(jnp.where(step == i, chip, 0) for i, chip in enumerate(chips))
    needed = (block >= place_ref[1 + 2 * m]) & (block < place_ref[2 + 2 * m])

    @pl.when(jnp.logical_not(needed))
    def _():
        for ref in (k_ref, v_ref, kT_ref, vT_ref):
            ref[...] = jnp.zeros_like(ref)

    @pl.when(needed)
    def _():
        for j in range(n):
            @pl.when(step == j)
            def _():
                rows_in_order(place_ref[0], own_refs[j].at[m], other_refs[j].at[m], x_ref)

        hidden = (x_ref[...].astype(f32) * vec_ref[0:1, :] + vec_ref[1:2, :]).astype(bf16)
        hid_ref[...] = hidden
        kv = jnp.dot(hidden, w_ref[:, 384:], preferred_element_type=f32)
        low = kv.astype(bf16)
        k_ref[0] = low[:, :384]
        v_ref[0] = low[:, 384:]
        turned = kv.T.astype(bf16)
        kT_ref[0] = turned[:384]
        vT_ref[0] = turned[384:]

    if n == 3:
        q_ref, qT_ref = refs[-4:-2]

        @pl.when(step == 1)
        def _():
            q = jnp.dot(hid_ref[...], w_ref[:, :384], preferred_element_type=f32)
            q_ref[0] = q.astype(bf16)
            qT_ref[0] = q.T.astype(bf16)


def project(chips, place, own, other, vec, w, earlier=()):
    n = len(chips)
    chip = (lambda b: b + 1) if n == 3 else (lambda b: 4 * b)
    tall = pl.BlockSpec((1, 512, 384), lambda m, b, *_: (m, chip(b), 0))
    wide = pl.BlockSpec((1, 384, 512), lambda m, b, *_: (m, 0, chip(b)))
    shapes = [far(2, 2560, 384), far(2, 2560, 384), far(2, 384, 2560), far(2, 384, 2560)]
    specs = [tall, tall, wide, wide]
    if n == 3:
        shapes += [far(2, 512, 384), far(2, 384, 512)]
        specs += [pl.BlockSpec((1, 512, 384), lambda m, *_: (m, 0, 0)), pl.BlockSpec((1, 384, 512), lambda m, *_: (m, 0, 0))]
    own, other = [own[c] for c in chips], [other[c] for c in chips]
    return call(
        lambda *refs: project_kernel(chips, *refs), shapes, "project", 5 * 10**9, 28,
        input_output_aliases={2 * n + 3 + i: i for i in range(len(earlier))}, **scalar_first(
            (2, n), [full(2, 256, 640)] * (2 * n) + [full(16, 640), full(640, 1152)] + [pl.BlockSpec(memory_space=pl.ANY)] * len(earlier),
            specs, [pltpu.VMEM((512, 640), bf16), pltpu.VMEM((512, 640), bf16)]))(place, *own, *other, *stay(vec, w), *earlier)


def heads_joined(core, mine, theirs):
    first, second = (jnp.where(core == 0, a, b) for a, b in ((mine, theirs), (theirs, mine)))
    return jnp.concatenate([first[:, :256], second[:, :256], first[:, 256:] + second[:, 256:]], axis=1)


def middle_kernel(core_ref, w_ref, low0_ref, low1_ref, theirs_ref, tok_ref, tok2_ref, vec_ref, mid_ref, hid_ref, hid2_ref):
    core = core_ref[0]
    for m, low_ref in enumerate((low0_ref, low1_ref)):
        attended = heads_joined(core, low_ref[...].astype(f32), theirs_ref[m].astype(f32)).astype(bf16)
        branch = jnp.dot(attended, w_ref[...], preferred_element_type=f32)
        mine = jnp.where(core == 0, branch[:256], branch[256:]) + tok_ref[m].astype(f32)
        theirs = jnp.where(core == 0, branch[256:], branch[:256]) + tok2_ref[m].astype(f32)
        part = slice(256 * m, 256 * (m + 1))
        mid_ref[part, :] = mine
        hid_ref[part, :] = (moments(mine)[0] * vec_ref[2:3, :] + vec_ref[3:4, :]).astype(bf16)
        hid2_ref[part, :] = (moments(theirs)[0] * vec_ref[2:3, :] + vec_ref[3:4, :]).astype(bf16)


W_OUT = pl.BlockSpec((640, 640), lambda *_: (0, 8))


def middle_step(core, weights, *args):
    return call(middle_kernel, (far(512, 640, dtype=f32), *(pltpu.MemorySpace.VMEM((512, 640), bf16),) * 2), "middle", 10**9, 20, **scalar_first(
        (1,), [W_OUT] + [full(*a.shape) for a in args], [full(512, 640)] * 3))(core, *stay(weights), *args[:-1], *stay(args[-1]))


def feed_kernel(h_ref, h2_ref, cot_ref, cot2_ref, up_ref, down_ref, mine_ref, theirs_ref, g_ref, h, cot, hT, cT, out, dh):
    chunk = pl.program_id(0)

    @pl.when(chunk == 0)
    def _():
        h[0:512, :], h[512:1024, :] = h_ref[...], h2_ref[...]
        cot[0:512, :], cot[512:1024, :] = cot_ref[...], cot2_ref[...]
        hT[...] = h[...].astype(f32).T.astype(bf16)
        cT[...] = cot[...].astype(f32).T.astype(bf16)
        out[...] = jnp.zeros_like(out)
        dh[...] = jnp.zeros_like(dh)

    up_w = up_ref[...]
    down_w = jnp.concatenate([down_ref[160 * y:160 * (y + 1), 640 * i:640 * (i + 1)] for y in range(2) for i in range(4)], axis=0)
    acts, d_ups = [], []
    for t in range(4):
        rows = slice(256 * t, 256 * (t + 1))
        u = jnp.dot(h[rows, :], up_w, preferred_element_type=f32)
        d_act = lax.dot_general(cot[rows, :], down_w, NT, preferred_element_type=f32)
        cdf = 0.5 * (1.0 + lax.erf(u * (2.0 ** -0.5)))
        pdf = jnp.exp(u * u * -0.5) * ((2.0 * math.pi) ** -0.5)
        act = (u * cdf).astype(bf16)
        d_up = (d_act * (cdf + u * pdf)).astype(bf16)
        out[rows, :] += jnp.dot(act, down_w, preferred_element_type=f32)
        dh[rows, :] += lax.dot_general(d_up, up_w, NT, preferred_element_type=f32)
        acts.append(act)
        d_ups.append(d_up)
    g_up = jnp.dot(hT[...], jnp.concatenate(d_ups, axis=0), preferred_element_type=f32).astype(bf16)
    g_down = jnp.dot(cT[...], jnp.concatenate(acts, axis=0), preferred_element_type=f32).T.astype(bf16)
    for f in range(2):
        for y in range(4):
            for i in range(2):
                g_ref[y, 4 * chunk + 2 * f + i] = g_up[160 * y + 80 * i:160 * y + 80 * (i + 1), 640 * f:640 * (f + 1)]
        for i in range(8):
            g_ref[2 * chunk + f, 8 + i] = g_down[640 * f + 80 * i:640 * f + 80 * (i + 1)]

    @pl.when(chunk == 1)
    def _():
        mine_ref[0], mine_ref[1] = out[0:512, :].astype(bf16), dh[0:512, :].astype(bf16)
        theirs_ref[0], theirs_ref[1] = out[512:1024, :].astype(bf16), dh[512:1024, :].astype(bf16)


def feed_forward(h, h2, cot, cot2, weights):
    return call(
        feed_kernel,
        (far(2, 512, 640), far(2, 512, 640), far(4, 16, 80, 640)),
        "feed_forward", 30 * 10**9, 52, grid=(2,),
        in_specs=[pl.BlockSpec(memory_space=pltpu.VMEM)] * 2 + [full(512, 640), pl.BlockSpec(memory_space=pltpu.VMEM), pl.BlockSpec((640, 1280), lambda f: (0, f)), pl.BlockSpec((320, 2560), lambda f: (f, 1))],
        out_specs=[full(2, 512, 640), full(2, 512, 640), full(4, 16, 80, 640)],
        scratch_shapes=[pltpu.VMEM((1024, 640), bf16), pltpu.VMEM((1024, 640), bf16), pltpu.VMEM((640, 1024), bf16), pltpu.VMEM((640, 1024), bf16),
                        pltpu.VMEM((1024, 640), f32), pltpu.VMEM((1024, 640), f32)],
    )(*near_by(h, h2), *stay(cot), *near_by(cot2), *stay(weights, weights))


def after_kernel(mid_ref, mine_ref, theirs_ref, cot_ref, vec_ref, block_ref, grad_ref, branch_ref, g_ref):
    @pl.when(pl.program_id(0) == 0)
    def _():
        g_ref[...] = jnp.zeros_like(g_ref)

    middle = mid_ref[...]
    block_ref[...] = (middle + mine_ref[0].astype(f32) + theirs_ref[0].astype(f32)).astype(bf16)
    d_hidden = mine_ref[1].astype(f32) + theirs_ref[1].astype(f32)
    n, r = moments(middle)
    g_ref[0:1, :] += jnp.sum(d_hidden * n, axis=0, keepdims=True)
    g_ref[1:2, :] += jnp.sum(d_hidden, axis=0, keepdims=True)
    grad = cot_ref[...].astype(f32) + norm_back(d_hidden, n, r, vec_ref[2:3, :])
    grad_ref[...] = grad
    branch_ref[...] = grad.astype(bf16)


def after_feed(*args):
    rows, pair = pl.BlockSpec((128, 640), lambda i: (i, 0)), pl.BlockSpec((2, 128, 640), lambda i: (0, i, 0))
    return call(
        after_kernel, (far(512, 640), far(512, 640, dtype=f32), shape(512, 640), shape(8, 640, dtype=f32)), "after_feed", 10**9, 16,
        grid=(4,), in_specs=[rows, pair, pair, rows, full(16, 640)], out_specs=[rows, rows, rows, full(8, 640)])(*stay(args[0], args[1]), args[2], *stay(args[3], args[4]))


def branch_kernel(core_ref, own_ref, their_ref, w_ref, low0_ref, low1_ref, theirs_ref, do_ref, doT_ref, g_ref):
    core = core_ref[0]
    w = jnp.concatenate([w_ref[pl.ds(pl.multiple_of(256 * core, 256), 256), :], w_ref[512:640, :]], axis=0)
    g = jnp.zeros((640, 384), f32)
    for m in range(2):
        part = slice(256 * m, 256 * (m + 1))
        mine, theirs = own_ref[part, :].astype(f32), their_ref[part, :].astype(f32)
        branch = jnp.concatenate([jnp.where(core == 0, mine, theirs), jnp.where(core == 0, theirs, mine)], axis=0)
        kept = jnp.where(core == 0, branch[:, :384], branch[:, 256:]).astype(bf16)
        branch = branch.astype(bf16)
        rows = slice(512 * m, 512 * (m + 1))
        do = lax.dot_general(branch, w, NT, preferred_element_type=f32)
        do_ref[rows, :] = do.astype(bf16)
        doT_ref[:, rows] = do.T.astype(bf16)
        attended = heads_joined(core, (low0_ref, low1_ref)[m][...].astype(f32), theirs_ref[m].astype(f32))
        g = g + jnp.dot(attended.T.astype(bf16), kept, preferred_element_type=f32)
    g_ref[...] = g.astype(bf16)


def branch_step(core, own, their, weights, *args):
    return call(
        branch_kernel, (shape(1024, 384), shape(384, 1024), shape(640, 384)), "branch", 10**9, 24, **scalar_first(
            (1,), [full(512, 640)] * 2 + [W_OUT] + [full(*a.shape) for a in args], [full(1024, 384), full(384, 1024), full(640, 384)]))(
                core, own, their, *stay(weights), *args)


def project_back_kernel(place_ref, *refs):
    own_refs, other_refs = refs[:5], refs[5:10]
    (vec_ref, w_ref, dq0_ref, dq1_ref, dk0_ref, dk1_ref, dv0_ref, dv1_ref, g_out_ref, g_two_ref,
     mine_ref, theirs_ref, tail_ref, n_ref, d_kv, d_q, d_hid, g_ref, g_vec, slots, arrived) = refs[10:]
    step, core = pl.program_id(0), place_ref[0]
    block, second = lax.rem(step, 5), lax.div(step, 5)
    inside = lambda j, m: (j >= place_ref[1 + 2 * m]) & (j < place_ref[2 + 2 * m])
    needed = inside(block, second)

    def copies(j, m, slot):
        return [pltpu.make_async_copy(refs_of[j].at[m], slots.at[slot, i], arrived.at[slot, i]) for i, refs_of in enumerate((own_refs, other_refs))]

    @pl.when(step == 0)
    def _():
        for m in range(2):
            for j in range(5):
                @pl.when(inside(j, m))
                def _():
                    for copy in copies(j, m, 5 * m + j):
                        copy.start()
        g_ref[...] = jnp.zeros_like(g_ref)
        g_vec[...] = jnp.zeros_like(g_vec)
        g_vec[2:4, :] = g_two_ref[0:2, :]

    @pl.when(jnp.logical_not(needed))
    def _():
        mine_ref[...] = jnp.zeros_like(mine_ref)
        theirs_ref[...] = jnp.zeros_like(theirs_ref)

    @pl.when(needed)
    def _():
        for copy in copies(0, 0, step):
            copy.wait()
        rows_in_order(core, slots.at[step, 0], slots.at[step, 1], n_ref)

    for m, (dq, dk, dv) in enumerate(((dq0_ref, dk0_ref, dv0_ref), (dq1_ref, dk1_ref, dv1_ref))):
        @pl.when(needed & (second == m))
        def _():
            rows = pl.ds(pl.multiple_of(block * 512, 512), 512)
            d_kv[:, :384], d_kv[:, 384:] = dk[rows, :], dv[rows, :]
            d_q[...] = dq[...]

    @pl.when(needed)
    def _():
        n = n_ref[...].astype(f32)
        hiddenT = (n * vec_ref[0:1, :] + vec_ref[1:2, :]).T.astype(bf16)
        d_hid[...] = lax.dot_general(d_kv[...], w_ref[:, 384:1152], NT, preferred_element_type=f32)
        g_ref[:, 384:] += jnp.dot(hiddenT, d_kv[...], preferred_element_type=f32)

        @pl.when(block == 2)
        def _():
            g_ref[:, :384] += jnp.dot(hiddenT, d_q[...], preferred_element_type=f32)
            d_hid[...] += lax.dot_general(d_q[...], w_ref[:, :384], NT, preferred_element_type=f32)

        dh = d_hid[...]
        low = dh.astype(bf16)
        for c, (first, other) in enumerate(((mine_ref, theirs_ref), (theirs_ref, mine_ref))):
            @pl.when(core == c)
            def _():
                first[0, 0], other[0, 0] = low[:256], low[256:]
        g_vec[0:1, :] += jnp.sum(dh * n, axis=0, keepdims=True)
        g_vec[1:2, :] += jnp.sum(dh, axis=0, keepdims=True)

    @pl.when(step == 9)
    def _():
        turned = g_vec[...].T
        lane = lax.broadcasted_iota(jnp.int32, (640, 128), 1) - 64 * (1 - core)
        spare = g_ref[:, 256:384]
        for i in range(4):
            spare = jnp.where(lane == i, turned[:, i:i + 1], spare)
        g_ref[:, 256:384] = spare
        for y in range(4):
            for z in range(4):
                rows = slice(160 * y + 40 * z, 160 * y + 40 * (z + 1))
                for x in range(3):
                    tail_ref[16 * y + 4 * z + x] = g_ref[rows, 384 * x:384 * (x + 1)].astype(bf16)
                tail_ref[16 * y + 4 * z + 3] = g_out_ref[rows, :].astype(bf16)


def project_back(place, own, other, vec, w, dq, dk, dv, g_out, g_two):
    here = pl.BlockSpec(memory_space=pltpu.VMEM)
    part = pl.BlockSpec((1, 1, 256, 640), lambda b, *_: (lax.rem(b, 5), b // 5, 0, 0))
    return call(
        project_back_kernel, (far(5, 2, 256, 640), far(5, 2, 256, 640), far(64, 40, 384)), "project_back", 10**10, 30, **scalar_first(
            (10,), [pl.BlockSpec(memory_space=pl.ANY)] * 10 + [here] * 10, [part, part, full(64, 40, 384)],
            [pltpu.VMEM((512, 640), bf16), pltpu.VMEM((512, 768), bf16), pltpu.VMEM((512, 384), bf16),
             pltpu.VMEM((512, 640), f32), pltpu.VMEM((640, 1152), f32), pltpu.VMEM((8, 640), f32),
             pltpu.VMEM((10, 2, 256, 640), bf16), pltpu.SemaphoreType.DMA((10, 2))]))(
                 place, *stay(*own, *other), *near_by(vec, w, *dq, *dk, *dv, g_out, g_two))


def in_core_order(core_ref, mine, theirs):
    core, mine, theirs = core_ref[0], mine.astype(f32), theirs.astype(f32)
    return jnp.where(core == 0, mine, theirs), jnp.where(core == 0, theirs, mine)


def final_feed_kernel(core_ref, mine_ref, theirs_ref, up_ref, down_ref):
    for i in range(16):
        for c, piece in enumerate(in_core_order(core_ref, mine_ref[i], theirs_ref[i])):
            if i < 8:
                base = 1280 * (i // 2) + 640 * c
                up_ref[80 * (i % 2):80 * (i % 2 + 1), base:base + 640] = piece
            else:
                base = 640 * c + 80 * (i - 8)
                down_ref[base:base + 80, :] = piece


def final_feed(core, mine, theirs):
    return call(final_feed_kernel, (shape(160, 5120, dtype=f32), shape(1280, 640, dtype=f32)), "final_feed", 10**6, 32, **scalar_first(
        (1,), [full(16, 80, 640)] * 2, [full(160, 5120), full(1280, 640)]))(core, mine, theirs)


def final_heads_kernel(core_ref, mine_ref, theirs_ref, qkv_ref, out_ref, vec_ref):
    lane = lax.broadcasted_iota(jnp.int32, (40, 128), 1)
    for z in range(4):
        rows = slice(40 * z, 40 * (z + 1))
        for x in range(4):
            a, b = in_core_order(core_ref, mine_ref[4 * z + x], theirs_ref[4 * z + x])
            if x < 3:
                last = jnp.where(lane < 64, a[:, 256:], b[:, 256:])
                qkv_ref[rows, 640 * x:640 * (x + 1)] = jnp.concatenate([a[:, :256], b[:, :256], last], axis=1)
            else:
                out_ref[rows, :] = jnp.concatenate([a, b[:, 128:]], axis=1)
            if x == 0:
                vec_ref[rows, :] = pltpu.roll(a[:, 256:], 64, 1) + b[:, 256:]


def final_heads(core, mine, theirs):
    return call(
        final_heads_kernel, (shape(160, 1920, dtype=f32), shape(160, 640, dtype=f32), shape(160, 128, dtype=f32)), "final_heads", 10**6, 16,
        **scalar_first((1,), [full(16, 40, 384)] * 2, [full(160, 1920), full(160, 640), full(160, 128)]))(core, mine, theirs)


def shifted(array, axis, by):
    devices = lax.axis_size(axis)
    return lax.ppermute(array, axis, [(i, (i + by) % devices) for i in range(devices)])


def passed_along(array, by):
    devices = lax.axis_size(("z", "x"))
    return lax.ppermute(array, ("z", "x"), [(i, i + by) for i in range(devices) if 0 <= i + by < devices])


def swapped(array):
    return lax.ppermute(array, "core", [(0, 1), (1, 0)])


def pick(array, index):
    return lax.dynamic_index_in_dim(array, index, 0, keepdims=False)


def gathered(array, axis):
    me, devices = lax.axis_index(axis), lax.axis_size(axis)
    out = jnp.zeros((devices,) + array.shape, array.dtype)
    out = lax.dynamic_update_index_in_dim(out, array, me, 0)
    for by in (1, devices - 1, 2):
        out = lax.dynamic_update_index_in_dim(out, shifted(array, axis, by), (me + devices - by) % devices, 0)
    return out


def window_info(length_row, chip, core, win):
    ends = jnp.cumsum(length_row)
    starts = ends - length_row
    base = chip * 512 - 1024
    places = base + jnp.arange(win, dtype=jnp.int32)
    inside = (places[:, None] >= starts[None, :]) & (places[:, None] < ends[None, :])
    ones = jnp.broadcast_to(jnp.arange(64) < 3, (win, 64)).astype(bf16)
    key_rows = jnp.concatenate([jnp.where(inside, 0.0, -BIG).astype(bf16), ones], axis=1)
    own = chip * 512 + jnp.arange(512, dtype=jnp.int32)
    inside_q = (own[None, :] >= starts[:, None]) & (own[None, :] < ends[:, None])
    query_rows = jnp.concatenate([inside_q.astype(bf16), jnp.zeros((64, 512), bf16)], axis=0)
    info = [core]
    sizes = []
    for t in range(2):
        first = chip * 512 + t * TILE
        low = jnp.max(jnp.where(starts <= first, starts, 0)) - base
        high = jnp.min(jnp.where(ends > first + TILE - 1, ends, 1 << 30)) - base
        start = low // 128 * 128
        need = high - start
        size = (need + SHORT - 1) // SHORT * SHORT
        info.append(jnp.minimum(start, win - size))
        sizes.append(size)
    low = jnp.minimum(info[1], info[2]) // 512
    high = (jnp.maximum(info[1] + sizes[0], info[2] + sizes[1]) + 511) // 512
    return jnp.stack(info + sizes).astype(jnp.int32), key_rows, query_rows, [low, high]


def body(tokens, lengths, gain_one, bias_one, w_qkv, w_out, gain_two, bias_two, w_up, w_down, cotangent):
    core, chip = lax.axis_index("core"), lax.axis_index(("z", "x"))
    core_arg = core[None].astype(jnp.int32)
    tok, cot = tokens[:, 0], cotangent[:, 0].reshape(512, 640)
    together = lambda *arrays: lax.optimization_barrier(arrays)

    vectors = jnp.pad(jnp.stack([gain_one, bias_one, gain_two, bias_two], axis=1), ((0, 0), (0, 124)))
    heads, tok_sent = together(pack_heads(core_arg, w_qkv, vectors), tok)
    heads = lax.all_gather(heads, "batch", axis=0, tiled=True)
    vec = vector_rows(heads)
    normal = normal_rows(tok_sent)
    before, after, normal_other, tok_other = passed_along(normal, 1), passed_along(normal, -1), swapped(normal), swapped(tok)
    windows = [window_info(lengths[m, 0], chip, core, 2560) for m in range(2)]
    place = jnp.stack([core] + windows[0][3] + windows[1][3]).astype(jnp.int32)
    feed_pack = pack_feed(core_arg, w_out, w_up, w_down)
    heads, vec, before, after, normal_other, tok_other, feed_pack, place, windows = together(
        heads, vec, before, after, normal_other, tok_other, feed_pack, place, windows)
    own = [passed_along(before, 1), before, normal, after, passed_along(after, -1)]
    other = [None, swapped(before), normal_other, swapped(after), None]
    feed_weights = lax.all_gather(feed_pack, "batch", axis=0, tiled=True)
    *near_parts, q, qT = project((1, 2, 3), place, own, other, vec, heads)
    own[0], own[4], near_parts = together(own[0], own[4], near_parts)
    other[0], other[4] = swapped(own[0]), swapped(own[4])
    k, v, kT, vT = project((0, 4), place, own, other, vec, heads, near_parts)
    (oT0, low0, lse0), (oT1, low1, lse1) = (
        attend(m, info, qT, k, vT, key_rows, query_rows) for m, (info, key_rows, query_rows, _) in enumerate(windows))

    theirs = swapped(jnp.stack([low0, low1]))
    middle, hidden_two, hidden_other = middle_step(core_arg, feed_weights, low0, low1, theirs, tok, tok_other, vec)
    mine, partial, feed_grads = feed_forward(hidden_two, hidden_other, cot, swapped(cot), feed_weights)
    feed_grads = lax.all_to_all(feed_grads.reshape(64, 80, 640), ("batch", "z", "x"), 0, 0, tiled=True)
    block_out, grad_middle, branch, g_two = after_feed(middle, mine, swapped(partial), cot, vec)

    do, doT, g_out = branch_step(core_arg, branch, swapped(branch), feed_weights, low0, low1, theirs)
    dq, dk, dv = zip(*(
        attend_back(m, info, qT, q, k, kT, v, doT, do, oT, lse, key_rows, query_rows)
        for m, ((info, key_rows, query_rows, _), oT, lse) in enumerate(zip(windows, (oT0, oT1), (lse0, lse1)))))
    mine, theirs, tail = project_back(place, own, other, vec, heads, dq, dk, dv, g_out, g_two)
    feed_grads, mine, theirs, tail = together(feed_grads, mine, theirs, tail)

    feed = jnp.sum(feed_grads.astype(f32), axis=0).astype(bf16)
    tail = lax.all_to_all(tail, ("batch", "z", "x"), 0, 0, tiled=True)
    feed = lax.all_gather(feed, ("z", "x"), axis=0, tiled=True).reshape(16, 80, 640)
    theirs = swapped(theirs)
    sums = [mine[j].astype(f32) + theirs[j].astype(f32) for j in range(5)]
    right, left = passed_along(sums[4].astype(bf16), 1), passed_along(sums[0].astype(bf16), -1)
    tail, right, left = together(tail, right, left)
    right, left = (right.astype(f32) + sums[3]).astype(bf16), (left.astype(f32) + sums[1]).astype(bf16)
    tail, right, left = together(jnp.sum(tail.astype(f32), axis=0).astype(bf16), right, left)
    right, left = passed_along(right, 1), passed_along(left, -1)
    tail = gathered(tail, "x").reshape(160, 384)
    tail = gathered(tail, "z").reshape(16, 40, 384)
    tail, right, left = together(tail, right, left)
    d_one = (sums[2] + right.astype(f32) + left.astype(f32)).reshape(512, 640)
    n_one, r_one = moments(tok.reshape(512, 640).astype(f32))
    grad_tokens = (grad_middle + norm_back(d_one, n_one, r_one, vec[0:1])).astype(bf16)
    tail, feed = together(tail, feed)
    grad_qkv, grad_out, spare = final_heads(core_arg, tail, swapped(tail))
    grad_up, grad_down = final_feed(core_arg, feed, swapped(feed))
    return (
        block_out.reshape(2, 1, 256, 640), grad_tokens.reshape(2, 1, 256, 640), spare[:, 0], spare[:, 1], grad_qkv, grad_out,
        spare[:, 2], spare[:, 3], grad_up, grad_down)


def solution(mesh):
    fine = Mesh(mesh.devices.reshape(4, 4, 4, 2), ("batch", "z", "x", "core"))
    rows = P(None, "batch", ("z", "x", "core"), None)
    one, two = P("batch"), P("batch", None)
    return jax.shard_map(
        body,
        mesh=fine,
        in_specs=(rows, P(None, "batch", None), one, one, two, two, one, one, two, two, rows),
        out_specs=(rows, rows, one, one, two, two, one, one, two, two),
        check_vma=False,
    )
```
